32 devices in a mesh: seq: 8 (over y, x, core), dp: 4 (over z).
Axes of the slice: x: 2, y: 2, z: 4, core: 2. Of those that a mesh axis runs over, the one named last changes fastest.
Arguments:
- inputs: bfloat16 [16, 1024, 768], P('dp', 'seq'), may hold values from -6 to 6
- cotangent: bfloat16 [16, 1024, 768], P('dp', 'seq'), may hold values from -6 to 6
- neighbours: bfloat16 [16, 16, 2, 128, 768], P('dp', 'seq'), may hold values from -6 to 6
- presence: int32 [16, 16, 2], P('dp', 'seq'), may hold values 0 or 1
- row_order: int32 [768], replicated, may hold values from 0 to 767, each once
- w_master: float32 [768, 12288], P('dp', 'seq')
- w_first: float32 [768, 12288], P('dp', 'seq'), may hold values from -80 to 80
- w_second: float32 [768, 12288], P('dp', 'seq'), may hold values from 819.2 to 3276.8
- w_average: float32 [768, 12288], P('dp', 'seq'), may hold values from -0.21875 to 0.21875
- n_master: float32 [6, 768], P(None, 'dp')
- n_first: float32 [6, 768], P(None, 'dp'), may hold values from -80 to 80
- n_second: float32 [6, 768], P(None, 'dp'), may hold values from 819.2 to 3276.8
- n_average: float32 [6, 768], P(None, 'dp'), may hold values from 0.5 to 1.5
Outputs:
- outputs: bfloat16 [16, 1024, 768], P('dp', 'seq')
- grad_inputs: float32 [16, 1024, 768], P('dp', 'seq')
- w_first_new: float32 [768, 12288], P('dp', 'seq')
- w_second_new: float32 [768, 12288], P('dp', 'seq')
- w_new: float32 [768, 12288], P('dp', 'seq')
- w_average_new: float32 [768, 12288], P('dp', 'seq')
- n_first_new: float32 [6, 768], P(None, 'dp')
- n_second_new: float32 [6, 768], P(None, 'dp')
- n_new: float32 [6, 768], P(None, 'dp')
- n_average_new: float32 [6, 768], P(None, 'dp')
The draws below stay inside these ranges and needn't reach their ends.
Inputs may be any that keep to these rules, and one draw needn't show every extreme that they name: A permutation of the weight rows: state row j holds weight row row_order[j]. `presence`: 1 where the neighbour exists; a span may have none.
All inputs are finite; a program needn't handle non-finite values. No bound on the sum of `presence` on one device may be relied on, other than what follows from the above.
Results may differ from the reference program's by a relative error of at most 0.025.
Values may be sent and summed in bfloat16 or wider, within the bound.
A program may use at most 320 MiB of HBM per device.

```python
import math
import jax
import jax.numpy as jnp
from jax import lax

D = 768
HEAD = 64
FF = 3072
SPAN = 64
NB = 2
RET = 128
STEP = 5
LENGTH = 1024
NSEQ = 16
SPANS = 16
WCOLS = 12288


def draw_w_master(key, part):
    key = jax.random.fold_in(key, 11)
    column = jnp.arange(8 * D + 2 * FF)
    factor = jnp.where(column < 3 * D, 1.0, jnp.where(column < 4 * D, 4.0, jnp.where(column < 7 * D, 1.0, jnp.where(column < 8 * D, 3.0, 1.0))))
    scale = factor * D ** (-0.5)
    scale = jnp.where(column >= 8 * D + FF, 2.0 * FF ** (-0.5), scale)
    base = jax.random.normal(key, (D, 8 * D + 2 * FF), jnp.float32)
    return base * scale[None, :]


def draw_n_master(key, part):
    key = jax.random.fold_in(key, 12)
    noise = jnp.clip(jax.random.normal(key, (6, D), jnp.float32), -4.0, 4.0)
    parity = jnp.arange(6)[:, None] % 2
    return jnp.where(parity == 0, 1.0 + 0.15 * noise, 0.3 * noise)


def with_ends(entries, own_key, least, largest):
    longest = entries.shape.index(max(entries.shape))
    spots = []
    for shift in (0, 1):
        where = [jax.random.randint(jax.random.fold_in(own_key, axis), (), 0, length) for axis, length in enumerate(entries.shape)]
        where[longest] = (where[longest] + shift) % entries.shape[longest]
        spots.append(tuple(where))
    return entries.at[spots[0]].set(least).at[spots[1]].set(largest)


def level_of(rng, extent, pieces, least, top_value):
    def one(dim, parts):
        heights = jax.random.uniform(jax.random.fold_in(jax.random.fold_in(rng, 6), dim), (parts,), jnp.float32, least / len(pieces), top_value / len(pieces))
        return jnp.repeat(jnp.exp(heights), extent[dim] // parts).reshape((-1,) + (1,) * (len(extent) - dim - 1))

    factor_of = one(*pieces[0])
    for cut in pieces[1:]:
        factor_of = factor_of * one(*cut)
    return factor_of


def normal_values(own_key, extent, scale, reach, split=(), held_as=jnp.bfloat16):
    values = scale * jax.random.normal(own_key, extent, jnp.float32)
    if split:
        values = values * level_of(own_key, extent, split, -0.22, 0.18)
    return jnp.clip(values, -reach, reach).astype(held_as)


def setup_inputs(seed: int = 0) -> dict:
    splits = jax.random.split(jax.random.key(seed), 14)
    return {
        "inputs": normal_values(splits[0], (NSEQ, LENGTH, D), 1.0, 6.0, ((0, 4), (1, 8))),
        "cotangent": normal_values(splits[1], (NSEQ, LENGTH, D), 1.0, 6.0, ((0, 4), (1, 8))),
        "neighbours": normal_values(splits[2], (NSEQ, SPANS, NB, RET, D), 1.0, 6.0, ((0, 4), (1, 8))),
        "presence": with_ends((jax.random.randint(splits[3], (NSEQ, SPANS, NB), 0, 4) < 3).astype(jnp.int32), jax.random.fold_in(splits[3], 1), 0, 1),
        "row_order": jax.random.permutation(splits[4], D).astype(jnp.int32),
        "w_master": draw_w_master(jax.random.fold_in(splits[13], 71), 0),
        "w_first": normal_values(splits[6], (D, WCOLS), (0.1 * (NSEQ * LENGTH) ** 0.5), 80.0, ((0, 4), (1, 8)), jnp.float32),
        "w_second": jnp.clip(jnp.exp(math.log(3276.8) - 1.3862944 * jax.random.uniform(splits[7], (D, WCOLS), jnp.float32) ** level_of(splits[7], (D, WCOLS), ((0, 4), (1, 8)), -0.2, 0.2)), 819.2, 3276.8),
        "w_average": normal_values(splits[8], (D, WCOLS), D ** -0.5, 0.21875, ((0, 4), (1, 8)), jnp.float32),
        "n_master": draw_n_master(jax.random.fold_in(splits[13], 71), 0),
        "n_first": normal_values(splits[10], (6, D), (0.1 * (NSEQ * LENGTH) ** 0.5), 80.0, ((1, 4),), jnp.float32),
        "n_second": jnp.clip(jnp.exp(math.log(3276.8) - 1.3862944 * jax.random.uniform(splits[11], (6, D), jnp.float32) ** level_of(splits[11], (6, D), ((1, 4),), -0.2, 0.2)), 819.2, 3276.8),
        "n_average": jnp.clip(1.0 + 0.1 * jax.random.normal(splits[12], (6, D), jnp.float32), 0.5, 1.5),
    }


@jax.custom_vjp
def low(v):
    return lax.optimization_barrier(v.astype(jnp.bfloat16)).astype(jnp.float32)

@jax.custom_vjp
def low_back(v):
    return v

def low_keep(v):
    return (low(v), None)

def low_pass(kept, grad):
    return (grad,)

def back_keep(v):
    return (v, None)

def back_low(kept, grad):
    return (low(grad),)
low.defvjp(low_keep, low_pass)
low_back.defvjp(back_keep, back_low)
beta_first = 0.9
beta_second = 0.95
adam_eps = 1e-08
learn_rate = 0.04
norm_rate = 0.6
weight_decay = 0.1
ema_decay = 0.5
norm_eps = 1e-05
masked_score = -1e+30
highest = lax.Precision.HIGHEST

def matmul(left, right):
    return jnp.dot(left, right, precision=highest, preferred_element_type=jnp.float32)

def layer_norm(values, gain, shift):
    centre = lax.optimization_barrier(jnp.mean(values, axis=-1, keepdims=True))
    centred = values - centre
    spread = lax.optimization_barrier(jnp.mean(centred * centred, axis=-1, keepdims=True))
    return centred * lax.rsqrt(spread + norm_eps) * gain + shift

def layer(inputs, weights, norms, neighbours, presence):
    length, dim = inputs.shape
    heads = dim // HEAD
    ffw = (weights.shape[1] - 8 * dim) // 2
    scale = HEAD ** (-0.5)
    w_qkv = weights[:, :3 * dim]
    w_out = weights[:, 3 * dim:4 * dim]
    w_cq = weights[:, 4 * dim:5 * dim]
    w_ckv = weights[:, 5 * dim:7 * dim]
    w_co = weights[:, 7 * dim:8 * dim]
    w_up = weights[:, 8 * dim:8 * dim + ffw]
    w_down = weights[:, 8 * dim + ffw:]
    hidden_a = low(layer_norm(inputs, norms[0], norms[1]))
    triple = low(low_back(matmul(hidden_a, w_qkv)))
    query = triple[:, :dim].reshape(length, heads, HEAD)
    keys = triple[:, dim:2 * dim].reshape(length, heads, HEAD)
    values = triple[:, 2 * dim:].reshape(length, heads, HEAD)
    scores = low_back(jnp.einsum('qhe,khe->hqk', query, keys, precision=highest) * scale)
    position = jnp.arange(length)
    causal = position[None, :] <= position[:, None]
    scores = jnp.where(causal[None], scores, masked_score)
    peak = lax.optimization_barrier(jnp.max(scores, axis=-1, keepdims=True))
    expon = jnp.exp(scores - peak)
    probs = low(expon / lax.optimization_barrier(jnp.sum(expon, axis=-1, keepdims=True)))
    attended = low(low_back(jnp.einsum('hqk,khe->qhe', probs, values, precision=highest).reshape(length, dim)))
    first = inputs + low_back(matmul(attended, w_out))
    hidden_c = low(layer_norm(first, norms[2], norms[3]))
    spans = length // SPAN
    cross_q = low(low_back(matmul(hidden_c, w_cq))).reshape(spans, SPAN, heads, HEAD)
    near_kv = low(low_back(matmul(neighbours.reshape(-1, dim), w_ckv))).reshape(spans, NB * RET, 2 * dim)
    cross_k = near_kv[:, :, :dim].reshape(spans, NB * RET, heads, HEAD)
    cross_v = near_kv[:, :, dim:].reshape(spans, NB * RET, heads, HEAD)
    cscores = low_back(jnp.einsum('cqhe,ckhe->chqk', cross_q, cross_k, precision=highest) * scale)
    live = jnp.repeat(presence, RET, axis=1) > 0
    livemask = live[:, None, None, :]
    cscores = jnp.where(livemask, cscores, masked_score)
    cpeak = lax.optimization_barrier(jnp.max(cscores, axis=-1, keepdims=True))
    cexpon = jnp.exp(cscores - cpeak) * livemask.astype(jnp.float32)
    anyone = lax.optimization_barrier(jnp.max(presence, axis=1)).astype(jnp.float32)[:, None, None, None]
    cprobs = low(cexpon / (lax.optimization_barrier(jnp.sum(cexpon, axis=-1, keepdims=True)) + 1.0 - anyone))
    cross_out = low(low_back(jnp.einsum('chqk,ckhe->cqhe', cprobs, cross_v, precision=highest).reshape(length, dim)))
    second = first + low_back(matmul(cross_out, w_co))
    hidden_e = low(layer_norm(second, norms[4], norms[5]))
    upward = low_back(matmul(hidden_e, w_up))
    active = low(jax.nn.gelu(upward, approximate=True))
    downward = lax.dot_general(active, w_down, (((1,), (1,)), ((), ())), precision=highest, preferred_element_type=jnp.float32)
    return second + low_back(downward)

def adam_update(grad, weight, first, second, average, rate, decay):
    first = beta_first * first + (1.0 - beta_first) * grad
    second = beta_second * second + (1.0 - beta_second) * grad * grad
    stepped = first / (1.0 - beta_first ** STEP) / (jnp.sqrt(second / (1.0 - beta_second ** STEP)) + adam_eps)
    weight = weight - rate * (stepped + decay * weight)
    average = ema_decay * average + (1.0 - ema_decay) * weight
    return (first, second, weight, average)

def reference(inputs, cotangent, neighbours, presence, row_order, w_master, w_first, w_second, w_average, n_master, n_first, n_second, n_average):
    order_back = jnp.argsort(row_order).astype(jnp.int32)
    weights = w_master.astype(jnp.bfloat16).astype(jnp.float32)[order_back]
    norms = n_master.astype(jnp.bfloat16).astype(jnp.float32)

    def one_sequence(carry, item):
        seq_in, seq_cot, seq_near, seq_pres = item

        def forward(acts, wts, nrm):
            return layer(acts, wts, nrm, seq_near.astype(jnp.float32), seq_pres)
        result, pull = jax.vjp(forward, seq_in.astype(jnp.float32), weights, norms)
        grad_in, grad_w, grad_n = pull(seq_cot.astype(jnp.float32))
        return ((carry[0] + grad_w, carry[1] + grad_n), (result.astype(jnp.bfloat16), grad_in))
    start = (jnp.zeros(weights.shape, jnp.float32), jnp.zeros(norms.shape, jnp.float32))
    (grad_w, grad_n), (outputs, grad_inputs) = lax.scan(one_sequence, start, (inputs, cotangent, neighbours, presence))
    grad_slots = grad_w[row_order.astype(jnp.int32)]
    w_first_new, w_second_new, w_new, w_average_new = adam_update(grad_slots, w_master, w_first, w_second, w_average, learn_rate, weight_decay)
    n_first_new, n_second_new, n_new, n_average_new = adam_update(grad_n, n_master, n_first, n_second, n_average, norm_rate, 0.0)
    return (outputs, grad_inputs, w_first_new, w_second_new, w_new, w_average_new, n_first_new, n_second_new, n_new, n_average_new)
```

```python
from functools import partial

import jax
import jax.numpy as jnp
from jax import lax
from jax.experimental import pallas as pl
from jax.experimental.pallas import tpu as pltpu
from jax.sharding import PartitionSpec as P

HEAD = 64
STEP = 5
LANES = 128
SCALE = HEAD ** (-0.5)

beta_first = 0.9
beta_second = 0.95
adam_eps = 1e-08
learn_rate = 0.04
norm_rate = 0.6
weight_decay = 0.1
ema_decay = 0.5
norm_eps = 1e-05
masked_score = -1e30
VMEM_BYTES = 60 * 1024 * 1024
bf16 = jnp.bfloat16
f32 = jnp.float32


def mm(left, right):
    return lax.dot_general(left, right, (((1,), (0,)), ((), ())), preferred_element_type=f32)


def nt(left, right):
    return lax.dot_general(left, right, (((1,), (1,)), ((), ())), preferred_element_type=f32)


def tn(left, right):
    return lax.dot_general(left, right, (((0,), (0,)), ((), ())), preferred_element_type=f32)


def params():
    return pltpu.CompilerParams(vmem_limit_bytes=VMEM_BYTES)


def rows_of(index, size):
    return pl.ds(pl.multiple_of(index * size, size), size)


def centre_scale(values):
    centre = jnp.mean(values, axis=-1, keepdims=True)
    centred = values - centre
    spread = jnp.mean(centred * centred, axis=-1, keepdims=True)
    recip = lax.rsqrt(spread + norm_eps)
    return centred * recip, recip


def norm_back(upstream, normed, recip, gain):
    scaled = upstream * gain
    inner = (
        scaled
        - jnp.mean(scaled, axis=-1, keepdims=True)
        - normed * jnp.mean(scaled * normed, axis=-1, keepdims=True)
    )
    return (
        recip * inner,
        jnp.sum(upstream * normed, axis=0, keepdims=True),
        jnp.sum(upstream, axis=0, keepdims=True),
    )


def gelu_parts(value):
    const = 0.7978845608028654
    square = value * value
    bend = jnp.tanh(const * value * (1.0 + 0.044715 * square))
    half = 0.5 * (1.0 + bend)
    slope = half + 0.5 * value * (1.0 - bend * bend) * (const * (1.0 + 3 * 0.044715 * square))
    return value * half, slope


def head_mask(rows, half):
    lane = lax.broadcasted_iota(jnp.int32, (rows, LANES), 1)
    return (lane < HEAD) if half == 0 else (lane >= HEAD)


def pick(mask, value):
    return jnp.where(mask, value, jnp.zeros_like(value))


def self_forward_kernel(pairs, x_ref, norms_ref, perm_ref, w_ref, hid_ref, qkv_ref, att_ref, lse_ref):
    length, dim = x_ref.shape
    width = pairs * LANES
    tile = 256
    tiles = length // tile

    @pl.loop(0, tiles)
    def _(step):
        rows = rows_of(step, tile)
        normed, _ = centre_scale(x_ref[rows, :].astype(f32))
        hidden = (normed * norms_ref[0:1, :] + norms_ref[1:2, :]).astype(bf16)
        hid_ref[rows, :] = mm(hidden, perm_ref[...]).astype(bf16)

    for part in range(3):
        triple = mm(hid_ref[...], w_ref[:, part * width : (part + 1) * width]).astype(bf16)
        for pair in range(pairs):
            qkv_ref[part * pairs + pair] = triple[:, pair * LANES : (pair + 1) * LANES]

    below = lax.broadcasted_iota(jnp.int32, (tile, tile), 1) <= lax.broadcasted_iota(
        jnp.int32, (tile, tile), 0
    )
    masks = [head_mask(tile, 0), head_mask(tile, 1)]

    @pl.loop(0, pairs)
    def _(pair):
        for step in range(tiles):
            rows = slice(step * tile, (step + 1) * tile)
            query = qkv_ref[pair, rows, :] * SCALE
            keys_here = qkv_ref[pairs + pair, rows, :]
            values_here = qkv_ref[2 * pairs + pair, rows, :]
            outs = []
            for half in range(2):
                mine = pick(masks[half], query)
                here = jnp.where(below, nt(mine, keys_here), masked_score)
                peak = jnp.max(here, axis=-1, keepdims=True)
                if step:
                    past = nt(mine, qkv_ref[pairs + pair, : step * tile, :])
                    peak = jnp.maximum(peak, jnp.max(past, axis=-1, keepdims=True))
                    past = jnp.exp(past - peak)
                here = jnp.exp(here - peak)
                total = jnp.sum(here, axis=-1, keepdims=True)
                out = mm(here.astype(bf16), values_here)
                if step:
                    total = total + jnp.sum(past, axis=-1, keepdims=True)
                    out = out + mm(past.astype(bf16), qkv_ref[2 * pairs + pair, : step * tile, :])
                outs.append(out / total)
                lse_ref[pair, rows, half : half + 1] = peak + jnp.log(total)
            att_ref[rows, pl.ds(pl.multiple_of(pair * LANES, LANES), LANES)] = jnp.where(
                masks[0], outs[0], outs[1]
            ).astype(bf16)


def self_forward(pairs, x, norms, perm, w):
    length, dim = x.shape
    return pl.pallas_call(
        partial(self_forward_kernel, pairs),
        out_shape=(
            jax.ShapeDtypeStruct((length, dim), bf16),
            jax.ShapeDtypeStruct((3 * pairs, length, LANES), bf16),
            jax.ShapeDtypeStruct((length, pairs * LANES), bf16),
            jax.ShapeDtypeStruct((pairs, length, 2), f32),
        ),
        compiler_params=params(),
        name="self_forward",
    )(x, norms, perm, w)


def self_backward_kernel(
    pairs, qkv_ref, att_ref, gatt_ref, lse_ref, hid_ref, w_ref, gw_ref, ghid_ref, grad_ref, acc_ref
):
    length = att_ref.shape[0]
    dim = hid_ref.shape[1]
    width = pairs * LANES
    tile = 256
    tiles = length // tile
    above = lax.broadcasted_iota(jnp.int32, (tile, tile), 0) <= lax.broadcasted_iota(
        jnp.int32, (tile, tile), 1
    )
    masks = [head_mask(tile, 0), head_mask(tile, 1)]
    ones = jnp.ones((8, LANES), bf16)

    @pl.loop(0, pairs)
    def _(pair):
        lanes = pl.ds(pl.multiple_of(pair * LANES, LANES), LANES)
        key_acc = [None] * tiles
        for step in range(tiles):
            rows = slice(step * tile, (step + 1) * tile)
            query = qkv_ref[pair, rows, :] * SCALE
            grad_out = gatt_ref[rows, lanes]
            product = grad_out.astype(f32) * att_ref[rows, lanes].astype(f32)
            queries = [pick(masks[half], query) for half in range(2)]
            grads = [pick(masks[half], grad_out) for half in range(2)]
            deltas = [
                jnp.sum(pick(masks[half], product).T, axis=0, keepdims=True) for half in range(2)
            ]
            grad_query = [None, None]
            for other in range(step + 1):
                cols = slice(other * tile, (other + 1) * tile)
                keys = qkv_ref[pairs + pair, cols, :]
                values = qkv_ref[2 * pairs + pair, cols, :]
                key_part = value_part = None
                for half in range(2):
                    scores = nt(keys, queries[half])
                    if other == step:
                        scores = jnp.where(above, scores, masked_score)
                    probs = jnp.exp(scores - lse_ref[pair, half : half + 1, rows])
                    grad_scores = (probs * (nt(values, grads[half]) - deltas[half])).astype(bf16)
                    query_term = tn(grad_scores, keys)
                    grad_query[half] = (
                        query_term if grad_query[half] is None else grad_query[half] + query_term
                    )
                    key_term = mm(grad_scores, queries[half])
                    value_term = mm(probs.astype(bf16), grads[half])
                    key_part = key_term if key_part is None else key_part + key_term
                    value_part = value_term if value_part is None else value_part + value_term
                if other == step:
                    acc_ref[0, cols, :] = key_part
                    acc_ref[1, cols, :] = value_part
                else:
                    acc_ref[0, cols, :] += key_part
                    acc_ref[1, cols, :] += value_part
            grad_ref[rows, lanes] = (
                jnp.where(masks[0], grad_query[0], grad_query[1]) * SCALE
            ).astype(bf16)
        for part in range(2):
            lanes_to = pl.ds(pl.multiple_of((part + 1) * width + pair * LANES, LANES), LANES)
            grad_ref[:, lanes_to] = acc_ref[part].astype(bf16)

    hidden_t = hid_ref[...].T
    for begin in range(0, 3 * width, width):
        cols = slice(begin, begin + width)
        gw_ref[:, cols] = mm(hidden_t, grad_ref[:, cols]).astype(bf16)
    for begin in range(0, length, tile):
        rows = slice(begin, begin + tile)
        ghid_ref[rows, :] = nt(grad_ref[rows, :], w_ref[...]).astype(bf16)


def self_backward(pairs, qkv, att, gatt, lse, hid, w):
    length, dim = hid.shape
    width = pairs * LANES
    return pl.pallas_call(
        partial(self_backward_kernel, pairs),
        out_shape=(
            jax.ShapeDtypeStruct((dim, 3 * width), bf16),
            jax.ShapeDtypeStruct((length, dim), bf16),
        ),
        scratch_shapes=[
            pltpu.VMEM((length, 3 * width), bf16),
            pltpu.VMEM((2, length, LANES), f32),
        ],
        compiler_params=params(),
        name="self_backward",
    )(qkv, att, gatt, lse, hid, w)


def spread_heads(block, rows, group):
    lane = lax.broadcasted_iota(jnp.int32, block.shape, 1) // HEAD
    return jnp.concatenate([pick(lane == head, block) for head in range(group)], axis=0)


def gather_heads(stacked, rows, group):
    lane = lax.broadcasted_iota(jnp.int32, (rows, stacked.shape[1]), 1) // HEAD
    out = None
    for head in range(group):
        part = pick(lane == head, stacked[head * rows : (head + 1) * rows])
        out = part if out is None else out + part
    return out


def live_keys(presence_ref, span, shape, axis, neighbours, each):
    index = lax.broadcasted_iota(jnp.int32, shape, axis) // each
    live = jnp.zeros(shape, f32)
    anyone = None
    for which in range(neighbours):
        here = presence_ref[span * neighbours + which]
        there = jnp.where(here > 0, 1.0, 0.0).astype(f32)
        live = jnp.where(index == which, there, live)
        anyone = here if anyone is None else jnp.maximum(anyone, here)
    return live, anyone.astype(f32)


def cross_forward_kernel(
    spans,
    neighbours,
    presence_ref,
    att_ref,
    x_ref,
    norms_ref,
    perm_ref,
    perm_att_ref,
    near_ref,
    w_out_ref,
    w_cq_ref,
    w_ck_ref,
    w_cv_ref,
    w_co_ref,
    att_p_ref,
    first_ref,
    hid_p_ref,
    cross_q_ref,
    near_p_ref,
    near_kv_ref,
    co_p_ref,
    second_ref,
    cross_ref,
):
    count, dim = x_ref.shape
    rows_near = near_ref.shape[0]
    span_len = count // spans
    near = rows_near // spans
    group = 256 // HEAD
    tile = 512

    att_p_ref[...] = mm(att_ref[...], perm_att_ref[...]).astype(bf16)
    first_ref[...] = x_ref[...].astype(f32) + mm(att_p_ref[...], w_out_ref[...])

    normed, _ = centre_scale(first_ref[...])
    hidden = (normed * norms_ref[2:3, :] + norms_ref[3:4, :]).astype(bf16)
    hid_p_ref[...] = mm(hidden, perm_ref[...]).astype(bf16)
    cross_q_ref[...] = mm(hid_p_ref[...], w_cq_ref[...]).astype(bf16)

    @pl.loop(0, rows_near // tile)
    def _(step):
        rows = rows_of(step, tile)
        near_p_ref[rows, :] = mm(near_ref[rows, :], perm_ref[...]).astype(bf16)
        near_kv_ref[rows, :dim] = mm(near_p_ref[rows, :], w_ck_ref[...]).astype(bf16)
        near_kv_ref[rows, dim:] = mm(near_p_ref[rows, :], w_cv_ref[...]).astype(bf16)

    @pl.loop(0, spans)
    def _(span):
        rows = rows_of(span, span_len)
        keys = rows_of(span, near)
        live, anyone = live_keys(presence_ref, span, (1, near), 1, neighbours, near // neighbours)
        for begin in range(0, dim, group * HEAD):
            lanes = slice(begin, begin + group * HEAD)
            lanes_v = slice(dim + begin, dim + begin + group * HEAD)
            query = spread_heads(cross_q_ref[rows, lanes] * SCALE, span_len, group)
            scores = jnp.where(live > 0, nt(query, near_kv_ref[keys, lanes]), masked_score)
            peak = jnp.max(scores, axis=-1, keepdims=True)
            expon = jnp.exp(scores - peak) * live
            total = jnp.sum(expon, axis=-1, keepdims=True) + 1.0 - anyone
            out = mm(expon.astype(bf16), near_kv_ref[keys, lanes_v]) / total
            cross_ref[rows, lanes] = gather_heads(out, span_len, group).astype(bf16)

    co_p_ref[...] = mm(cross_ref[...], perm_ref[...]).astype(bf16)
    second_ref[...] = first_ref[...] + mm(co_p_ref[...], w_co_ref[...])


def column_block(rows, width, index):
    return pl.BlockSpec((rows, width), lambda *_: (0, index), pipeline_mode=pl.Buffered(1))


def whole(array):
    return pl.BlockSpec(array.shape, lambda *_: (0,) * array.ndim, pipeline_mode=pl.Buffered(1))


def whole_shape(shape):
    return pl.BlockSpec(shape, lambda *_: (0,) * len(shape), pipeline_mode=pl.Buffered(1))


def cross_forward(spans, neighbours, presence, att, x, norms, perm, perm_att, near, weights):
    count, dim = x.shape
    rows_near = near.shape[0]
    out_shape = (
        jax.ShapeDtypeStruct((count, dim), bf16),
        jax.ShapeDtypeStruct((count, dim), f32),
        jax.ShapeDtypeStruct((count, dim), bf16),
        jax.ShapeDtypeStruct((count, dim), bf16),
        jax.ShapeDtypeStruct((rows_near, dim), bf16),
        jax.ShapeDtypeStruct((rows_near, 2 * dim), bf16),
        jax.ShapeDtypeStruct((count, dim), bf16),
        jax.ShapeDtypeStruct((count, dim), f32),
    )
    operands = (att, x, norms, perm, perm_att, near)
    return pl.pallas_call(
        partial(cross_forward_kernel, spans, neighbours),
        out_shape=out_shape,
        grid=(1,),
        in_specs=[pl.BlockSpec(memory_space=pltpu.SMEM)]
        + [whole(op) for op in operands]
        + [column_block(dim, dim, index) for index in (3, 4, 5, 6, 7)],
        out_specs=tuple(whole_shape(shape.shape) for shape in out_shape),
        scratch_shapes=[pltpu.VMEM((count, dim), bf16)],
        compiler_params=params(),
        name="cross_forward",
    )(presence, *operands, *([weights] * 5))


def feed_kernel(
    second_ref,
    cot_ref,
    norms_ref,
    perm_ref,
    w_up_ref,
    w_down_ref,
    out_ref,
    gsecond_ref,
    gup_ref,
    gdown_ref,
    gnorm_ref,
    hid_p_ref,
    hid_t_ref,
    cot_p_ref,
    cot_t_ref,
    result_ref,
    back_ref,
):
    step = pl.program_id(0)

    @pl.when(step == 0)
    def _():
        normed, _ = centre_scale(second_ref[...])
        hidden = (normed * norms_ref[4:5, :] + norms_ref[5:6, :]).astype(bf16)
        hid_p_ref[...] = mm(hidden, perm_ref[...]).astype(bf16)
        hid_t_ref[...] = hid_p_ref[...].T
        cot_p_ref[...] = mm(cot_ref[...], perm_ref[...]).astype(bf16)
        cot_t_ref[...] = cot_p_ref[...].T
        result_ref[...] = jnp.zeros_like(result_ref)
        back_ref[...] = jnp.zeros_like(back_ref)

    upward = mm(hid_p_ref[...], w_up_ref[...])
    active, slope = gelu_parts(upward)
    active = active.astype(bf16)
    result_ref[...] += nt(active, w_down_ref[...])
    gdown_ref[...] = mm(cot_t_ref[...], active).astype(bf16)
    grad_up = (mm(cot_p_ref[...], w_down_ref[...]) * slope).astype(bf16)
    gup_ref[...] = mm(hid_t_ref[...], grad_up).astype(bf16)
    back_ref[...] += nt(grad_up, w_up_ref[...])

    @pl.when(step == pl.num_programs(0) - 1)
    def _():
        out_ref[...] = (
            second_ref[...] + nt(result_ref[...].astype(bf16), perm_ref[...])
        ).astype(bf16)
        upstream = nt(back_ref[...].astype(bf16), perm_ref[...])
        normed, recip = centre_scale(second_ref[...])
        back, gain, shift = norm_back(upstream, normed, recip, norms_ref[4:5, :])
        gsecond_ref[...] = cot_ref[...].astype(f32) + back
        gnorm_ref[0:1, :] = gain
        gnorm_ref[1:2, :] = shift


def feed(second, cot, norms, perm, weights):
    count, dim = second.shape
    ffw = (weights.shape[1] - 8 * dim) // 2
    tile = 512
    first_up = 8 * dim // tile
    first_down = (8 * dim + ffw) // tile
    out_shape = (
        jax.ShapeDtypeStruct((count, dim), bf16),
        jax.ShapeDtypeStruct((count, dim), f32),
        jax.ShapeDtypeStruct((dim, ffw), bf16),
        jax.ShapeDtypeStruct((dim, ffw), bf16),
        jax.ShapeDtypeStruct((2, dim), f32),
    )
    operands = (second, cot, norms, perm)
    moving = pl.BlockSpec((dim, tile), lambda i: (0, i))
    return pl.pallas_call(
        feed_kernel,
        out_shape=out_shape,
        grid=(ffw // tile,),
        in_specs=[whole(op) for op in operands]
        + [
            pl.BlockSpec((dim, tile), lambda i: (0, first_up + i)),
            pl.BlockSpec((dim, tile), lambda i: (0, first_down + i)),
        ],
        out_specs=(
            whole_shape((count, dim)),
            whole_shape((count, dim)),
            moving,
            moving,
            whole_shape((2, dim)),
        ),
        scratch_shapes=[
            pltpu.VMEM((count, dim), bf16),
            pltpu.VMEM((dim, count), bf16),
            pltpu.VMEM((count, dim), bf16),
            pltpu.VMEM((dim, count), bf16),
            pltpu.VMEM((count, dim), f32),
            pltpu.VMEM((count, dim), f32),
        ],
        compiler_params=params(),
        name="feed",
    )(*operands, weights, weights)


def cross_backward_kernel(
    spans,
    neighbours,
    presence_ref,
    gsecond_ref,
    first_ref,
    norms_ref,
    perm_ref,
    perm_att_ref,
    att_p_ref,
    hid_p_ref,
    cross_q_ref,
    near_p_ref,
    near_kv_ref,
    co_p_ref,
    w_out_ref,
    w_cq_ref,
    w_co_ref,
    gfirst_ref,
    gatt_ref,
    gw_ref,
    gnorm_ref,
    gco_ref,
    gcq_ref,
    gnear_ref,
):
    count, dim = first_ref.shape
    rows_near = near_p_ref.shape[0]
    span_len = count // spans
    near = rows_near // spans
    group = 256 // HEAD

    upper = gsecond_ref[...].astype(bf16)
    gw_ref[:, 4 * dim : 5 * dim] = mm(co_p_ref[...].T, upper).astype(bf16)
    gco_ref[...] = nt(nt(upper, w_co_ref[...]).astype(bf16), perm_ref[...]).astype(bf16)

    @pl.loop(0, spans)
    def _(span):
        rows = rows_of(span, span_len)
        keys = rows_of(span, near)
        live, anyone = live_keys(presence_ref, span, (near, 1), 0, neighbours, near // neighbours)
        for begin in range(0, dim, group * HEAD):
            lanes = slice(begin, begin + group * HEAD)
            lanes_v = slice(dim + begin, dim + begin + group * HEAD)
            query = spread_heads(cross_q_ref[rows, lanes] * SCALE, span_len, group)
            grad_out = spread_heads(gco_ref[rows, lanes], span_len, group)
            key = near_kv_ref[keys, lanes]
            scores = jnp.where(live > 0, nt(key, query), masked_score)
            peak = jnp.max(scores, axis=0, keepdims=True)
            expon = jnp.exp(scores - peak) * live
            total = jnp.sum(expon, axis=0, keepdims=True) + 1.0 - anyone
            probs = expon * (1.0 / total)
            grad_probs = nt(near_kv_ref[keys, lanes_v], grad_out)
            inner = jnp.sum(probs * grad_probs, axis=0, keepdims=True)
            grad_scores = (probs * (grad_probs - inner)).astype(bf16)
            gcq_ref[rows, lanes] = (
                gather_heads(tn(grad_scores, key), span_len, group) * SCALE
            ).astype(bf16)
            gnear_ref[keys, lanes] = mm(grad_scores, query).astype(bf16)
            gnear_ref[keys, lanes_v] = mm(probs.astype(bf16), grad_out).astype(bf16)

    near_t = near_p_ref[...].T
    for part in range(2):
        gw_ref[:, (2 + part) * dim : (3 + part) * dim] = mm(
            near_t, gnear_ref[:, part * dim : (part + 1) * dim]
        ).astype(bf16)
    gw_ref[:, dim : 2 * dim] = mm(hid_p_ref[...].T, gcq_ref[...]).astype(bf16)
    upstream = nt(nt(gcq_ref[...], w_cq_ref[...]).astype(bf16), perm_ref[...])
    normed, recip = centre_scale(first_ref[...])
    back, gain, shift = norm_back(upstream, normed, recip, norms_ref[2:3, :])
    gnorm_ref[0:1, :] = gain
    gnorm_ref[1:2, :] = shift
    gfirst_ref[...] = gsecond_ref[...] + back
    lower = gfirst_ref[...].astype(bf16)
    gw_ref[:, :dim] = mm(att_p_ref[...].T, lower).astype(bf16)
    gatt_ref[...] = nt(nt(lower, w_out_ref[...]).astype(bf16), perm_att_ref[...]).astype(bf16)


def cross_backward(
    spans,
    neighbours,
    presence,
    gsecond,
    first,
    norms,
    perm,
    perm_att,
    att_p,
    hid_p,
    cross_q,
    near_p,
    near_kv,
    co_p,
    weights,
):
    count, dim = first.shape
    rows_near = near_p.shape[0]
    out_shape = (
        jax.ShapeDtypeStruct((count, dim), f32),
        jax.ShapeDtypeStruct((count, perm_att.shape[0]), bf16),
        jax.ShapeDtypeStruct((dim, 5 * dim), bf16),
        jax.ShapeDtypeStruct((2, dim), f32),
    )
    operands = (
        gsecond,
        first,
        norms,
        perm,
        perm_att,
        att_p,
        hid_p,
        cross_q,
        near_p,
        near_kv,
        co_p,
    )
    return pl.pallas_call(
        partial(cross_backward_kernel, spans, neighbours),
        out_shape=out_shape,
        grid=(1,),
        in_specs=[pl.BlockSpec(memory_space=pltpu.SMEM)]
        + [whole(op) for op in operands]
        + [column_block(dim, dim, index) for index in (3, 4, 7)],
        out_specs=tuple(whole_shape(shape.shape) for shape in out_shape),
        scratch_shapes=[
            pltpu.VMEM((count, dim), bf16),
            pltpu.VMEM((count, dim), bf16),
            pltpu.VMEM((rows_near, 2 * dim), bf16),
        ],
        compiler_params=params(),
        name="cross_backward",
    )(presence, *operands, *([weights] * 3))


def last_norm_kernel(parts_ref, x_ref, gfirst_ref, norms_ref, perm_ref, out_ref, gnorm_ref):
    total = parts_ref[0].astype(f32)
    for part in range(1, parts_ref.shape[0]):
        total = total + parts_ref[part].astype(f32)
    upstream = nt(total.astype(bf16), perm_ref[...])
    normed, recip = centre_scale(x_ref[...].astype(f32))
    back, gain, shift = norm_back(upstream, normed, recip, norms_ref[0:1, :])
    out_ref[...] = gfirst_ref[...] + back
    gnorm_ref[0:1, :] = gain
    gnorm_ref[1:2, :] = shift


def last_norm(parts, x, gfirst, norms, perm):
    count, dim = x.shape
    return pl.pallas_call(
        last_norm_kernel,
        out_shape=(
            jax.ShapeDtypeStruct((count, dim), f32),
            jax.ShapeDtypeStruct((2, dim), f32),
        ),
        compiler_params=params(),
        name="last_norm",
    )(parts, x, gfirst, norms, perm)


def adam_update(grad, weight, first, second, average, rate, decay):
    first = beta_first * first + (1.0 - beta_first) * grad
    second = beta_second * second + (1.0 - beta_second) * grad * grad
    stepped = (
        first / (1.0 - beta_first**STEP) / (jnp.sqrt(second / (1.0 - beta_second**STEP)) + adam_eps)
    )
    weight = weight - rate * (stepped + decay * weight)
    average = ema_decay * average + (1.0 - ema_decay) * weight
    return (first, second, weight, average)


def on_device(
    inputs,
    cotangent,
    neighbours,
    presence,
    row_order,
    w_master,
    w_first,
    w_second,
    w_average,
    n_master,
    n_first,
    n_second,
    n_average,
):
    seqs, tokens, dim = inputs.shape
    heads = dim // HEAD
    devices = lax.axis_size("seq")
    count = seqs * tokens
    length = devices * tokens
    me = lax.axis_index("seq")
    shares = devices // seqs
    held = heads // shares
    pairs = (held + 1) // 2
    width = pairs * LANES
    spare = width - held * HEAD
    sequence, share = me // shares, me % shares

    weights = lax.all_gather(w_master.astype(bf16), "dp", axis=0, tiled=True)
    weights = lax.all_gather(weights, "seq", axis=1, tiled=True)
    norms = lax.all_gather(n_master.astype(bf16), "dp", axis=1, tiled=True).astype(f32)

    perm = (jnp.arange(dim)[:, None] == row_order[None, :]).astype(bf16)
    perm_att = jnp.pad(perm.reshape(shares, held * HEAD, dim), ((0, 0), (0, spare), (0, 0)))
    perm_att = perm_att.reshape(shares * width, dim)
    w_qkv = weights[:, : 3 * dim].reshape(dim, 3, shares, held * HEAD)
    w_qkv = lax.dynamic_index_in_dim(w_qkv, share, axis=2, keepdims=False)
    w_qkv = jnp.pad(w_qkv, ((0, 0), (0, 0), (0, spare))).reshape(dim, 3 * width)

    x = inputs.reshape(count, dim)
    rows = lax.all_to_all(jnp.repeat(inputs, shares, axis=0), "seq", 0, 0).reshape(length, dim)
    hid, qkv, att, lse = self_forward(pairs, rows, norms, perm, w_qkv)
    att_tok = (
        lax.all_to_all(att.reshape(devices, tokens, width), "seq", 0, 0)
        .reshape(seqs, shares, tokens, width)
        .transpose(0, 2, 1, 3)
        .reshape(count, shares * width)
    )
    spans = seqs * neighbours.shape[1]
    each = neighbours.shape[2]
    near = neighbours.reshape(-1, dim)
    live = presence.reshape(-1)
    att_p, first, hid_p, cross_q, near_p, near_kv, co_p, second = cross_forward(
        spans, each, live, att_tok, x, norms, perm, perm_att, near, weights
    )
    outputs, gsecond, gup, gdown, gnorm_e = feed(
        second, cotangent.reshape(count, dim), norms, perm, weights
    )
    gfirst, gatt_tok, gmiddle, gnorm_c = cross_backward(
        spans,
        each,
        live,
        gsecond,
        first,
        norms,
        perm,
        perm_att,
        att_p,
        hid_p,
        cross_q,
        near_p,
        near_kv,
        co_p,
        weights,
    )
    gatt = lax.all_to_all(
        gatt_tok.reshape(seqs, tokens, shares, width)
        .transpose(0, 2, 1, 3)
        .reshape(devices, tokens, width),
        "seq",
        0,
        0,
    ).reshape(length, width)
    gqkv, ghid = self_backward(pairs, qkv, att, gatt, lse.transpose(0, 2, 1), hid, w_qkv)
    parts = (
        lax.all_to_all(ghid.reshape(devices, tokens, dim), "seq", 0, 0)
        .reshape(seqs, shares, tokens, dim)
        .transpose(1, 0, 2, 3)
        .reshape(shares, count, dim)
    )
    grad_inputs, gnorm_a = last_norm(parts, x, gfirst, norms, perm)

    gqkv = gqkv.reshape(dim, 3, 1, width)[..., : held * HEAD]
    gqkv = jnp.where(jnp.arange(shares)[:, None] == share, gqkv, jnp.zeros_like(gqkv))
    grads = jnp.concatenate([gqkv.reshape(dim, 3 * dim), gmiddle, gup, gdown], axis=1)
    norm_grads = lax.psum(jnp.concatenate([gnorm_a, gnorm_c, gnorm_e], axis=0), "seq")
    partial_sum = lax.psum_scatter(grads, "seq", scatter_dimension=1, tiled=True)
    grad_shard = lax.psum_scatter(partial_sum, "dp", scatter_dimension=0, tiled=True).astype(f32)
    norm_shard = lax.psum_scatter(
        norm_grads.astype(bf16), "dp", scatter_dimension=1, tiled=True
    ).astype(f32)
    w_first_new, w_second_new, w_new, w_average_new = adam_update(
        grad_shard, w_master, w_first, w_second, w_average, learn_rate, weight_decay
    )
    n_first_new, n_second_new, n_new, n_average_new = adam_update(
        norm_shard, n_master, n_first, n_second, n_average, norm_rate, 0.0
    )
    return (
        outputs.reshape(seqs, tokens, dim),
        grad_inputs.reshape(seqs, tokens, dim),
        w_first_new,
        w_second_new,
        w_new,
        w_average_new,
        n_first_new,
        n_second_new,
        n_new,
        n_average_new,
    )


def solution(mesh):
    in_specs = (
        P("dp", "seq", None),
        P("dp", "seq", None),
        P("dp", "seq", None, None, None),
        P("dp", "seq", None),
        P(),
        P("dp", "seq"),
        P("dp", "seq"),
        P("dp", "seq"),
        P("dp", "seq"),
        P(None, "dp"),
        P(None, "dp"),
        P(None, "dp"),
        P(None, "dp"),
    )
    out_specs = (
        P("dp", "seq", None),
        P("dp", "seq", None),
        P("dp", "seq"),
        P("dp", "seq"),
        P("dp", "seq"),
        P("dp", "seq"),
        P(None, "dp"),
        P(None, "dp"),
        P(None, "dp"),
        P(None, "dp"),
    )
    return jax.shard_map(
        on_device, mesh=mesh, in_specs=in_specs, out_specs=out_specs, check_vma=False
    )
```

```python
from functools import partial

import jax
import jax.numpy as jnp
from jax import lax
from jax.experimental import pallas as pl
from jax.experimental.pallas import tpu as pltpu
from jax.sharding import PartitionSpec as P

HEAD = 64
STEP = 5
LANES = 128
SCALE = HEAD ** (-0.5)

beta_first = 0.9
beta_second = 0.95
adam_eps = 1e-08
learn_rate = 0.04
norm_rate = 0.6
weight_decay = 0.1
ema_decay = 0.5
norm_eps = 1e-05
masked_score = -1e30
VMEM_BYTES = 60 * 1024 * 1024
bf16 = jnp.bfloat16
f32 = jnp.float32


def mm(left, right):
    return lax.dot_general(left, right, (((1,), (0,)), ((), ())), preferred_element_type=f32)


def nt(left, right):
    return lax.dot_general(left, right, (((1,), (1,)), ((), ())), preferred_element_type=f32)


def tn(left, right):
    return lax.dot_general(left, right, (((0,), (0,)), ((), ())), preferred_element_type=f32)


def params():
    return pltpu.CompilerParams(vmem_limit_bytes=VMEM_BYTES)


def rows_of(index, size):
    return pl.ds(pl.multiple_of(index * size, size), size)


def centre_scale(values):
    centre = jnp.mean(values, axis=-1, keepdims=True)
    centred = values - centre
    spread = jnp.mean(centred * centred, axis=-1, keepdims=True)
    recip = lax.rsqrt(spread + norm_eps)
    return centred * recip, recip


def norm_back(upstream, normed, recip, gain):
    scaled = upstream * gain
    inner = (
        scaled
        - jnp.mean(scaled, axis=-1, keepdims=True)
        - normed * jnp.mean(scaled * normed, axis=-1, keepdims=True)
    )
    return (
        recip * inner,
        jnp.sum(upstream * normed, axis=0, keepdims=True),
        jnp.sum(upstream, axis=0, keepdims=True),
    )


def gelu_parts(value):
    const = 0.7978845608028654
    square = value * value
    bend = jnp.tanh(const * value * (1.0 + 0.044715 * square))
    half = 0.5 * (1.0 + bend)
    slope = half + 0.5 * value * (1.0 - bend * bend) * (const * (1.0 + 3 * 0.044715 * square))
    return value * half, slope


def head_mask(rows, half):
    lane = lax.broadcasted_iota(jnp.int32, (rows, LANES), 1)
    return (lane < HEAD) if half == 0 else (lane >= HEAD)


def pick(mask, value):
    return jnp.where(mask, value, jnp.zeros_like(value))


def columns_of(pairs, share_columns, dim):
    width = pairs * LANES
    if not share_columns:
        return 0, width
    return lax.rem(lax.axis_index("seq"), dim // width) * width, dim


def weight_copies(pairs, direct, dim, wts_ref, w_ref, sems):
    width = pairs * LANES
    first, step = columns_of(pairs, direct, dim)
    return [
        pltpu.make_async_copy(
            wts_ref.at[:, pl.ds(pl.multiple_of(first + part * step, LANES), width)],
            w_ref.at[:, pl.ds(part * width, width)],
            sems.at[part],
        )
        for part in range(3)
    ]


def self_forward_kernel(
    pairs, direct, x_ref, norms_ref, perm_ref, wts_ref, hid_ref, qkv_ref, att_ref, lse_ref, w_ref, sems
):
    length, dim = x_ref.shape
    width = pairs * LANES
    tile = 256
    tiles = length // tile
    copies = weight_copies(pairs, direct, dim, wts_ref, w_ref, sems)
    for copy in copies:
        copy.start()

    @pl.loop(0, tiles)
    def _(step):
        rows = rows_of(step, tile)
        normed, _ = centre_scale(x_ref[rows, :].astype(f32))
        hidden = (normed * norms_ref[0:1, :] + norms_ref[1:2, :]).astype(bf16)
        hid_ref[rows, :] = mm(hidden, perm_ref[...]).astype(bf16)

    for part in range(3):
        copies[part].wait()
        triple = mm(hid_ref[...], w_ref[:, part * width : (part + 1) * width]).astype(bf16)
        for pair in range(pairs):
            qkv_ref[part * pairs + pair] = triple[:, pair * LANES : (pair + 1) * LANES]

    below = lax.broadcasted_iota(jnp.int32, (tile, tile), 1) <= lax.broadcasted_iota(
        jnp.int32, (tile, tile), 0
    )
    masks = [head_mask(tile, 0), head_mask(tile, 1)]

    @pl.loop(0, pairs)
    def _(pair):
        for step in range(tiles):
            rows = slice(step * tile, (step + 1) * tile)
            query = qkv_ref[pair, rows, :] * SCALE
            keys_here = qkv_ref[pairs + pair, rows, :]
            values_here = qkv_ref[2 * pairs + pair, rows, :]
            outs = []
            for half in range(2):
                mine = pick(masks[half], query)
                here = jnp.where(below, nt(mine, keys_here), masked_score)
                peak = jnp.max(here, axis=-1, keepdims=True)
                if step:
                    past = nt(mine, qkv_ref[pairs + pair, : step * tile, :])
                    peak = jnp.maximum(peak, jnp.max(past, axis=-1, keepdims=True))
                    past = jnp.exp(past - peak)
                here = jnp.exp(here - peak)
                total = jnp.sum(here, axis=-1, keepdims=True)
                out = mm(here.astype(bf16), values_here)
                if step:
                    total = total + jnp.sum(past, axis=-1, keepdims=True)
                    out = out + mm(past.astype(bf16), qkv_ref[2 * pairs + pair, : step * tile, :])
                outs.append(out / total)
                lse_ref[pair, rows, half : half + 1] = peak + jnp.log(total)
            att_ref[rows, pl.ds(pl.multiple_of(pair * LANES, LANES), LANES)] = jnp.where(
                masks[0], outs[0], outs[1]
            ).astype(bf16)


def self_forward(pairs, direct, x, norms, perm, w):
    length, dim = x.shape
    vmem = pl.BlockSpec(memory_space=pltpu.VMEM)
    return pl.pallas_call(
        partial(self_forward_kernel, pairs, direct),
        in_specs=[vmem] * 3 + [pl.BlockSpec(memory_space=pl.ANY)],
        scratch_shapes=[
            pltpu.VMEM((dim, 3 * pairs * LANES), bf16),
            pltpu.SemaphoreType.DMA((3,)),
        ],
        out_shape=(
            jax.ShapeDtypeStruct((length, dim), bf16),
            jax.ShapeDtypeStruct((3 * pairs, length, LANES), bf16),
            jax.ShapeDtypeStruct((length, pairs * LANES), bf16),
            jax.ShapeDtypeStruct((pairs, length, 2), f32),
        ),
        compiler_params=params(),
        name="self_forward",
    )(x, norms, perm, w)


def self_backward_kernel(
    pairs,
    direct,
    qkv_ref,
    att_ref,
    gatt_ref,
    lse_ref,
    hid_ref,
    wts_ref,
    _,
    all_ref,
    ghid_ref,
    grad_ref,
    acc_ref,
    gw_ref,
    w_ref,
    sems,
):
    length = att_ref.shape[0]
    dim = hid_ref.shape[1]
    width = pairs * LANES
    copies = weight_copies(pairs, direct, dim, wts_ref, w_ref, sems)
    for copy in copies:
        copy.start()
    tile = 256
    tiles = length // tile
    above = lax.broadcasted_iota(jnp.int32, (tile, tile), 0) <= lax.broadcasted_iota(
        jnp.int32, (tile, tile), 1
    )
    masks = [head_mask(tile, 0), head_mask(tile, 1)]

    @pl.loop(0, pairs)
    def _(pair):
        lanes = pl.ds(pl.multiple_of(pair * LANES, LANES), LANES)
        for step in range(tiles):
            rows = slice(step * tile, (step + 1) * tile)
            query = qkv_ref[pair, rows, :] * SCALE
            grad_out = gatt_ref[rows, lanes]
            product = grad_out.astype(f32) * att_ref[rows, lanes].astype(f32)
            queries = [pick(masks[half], query) for half in range(2)]
            grads = [pick(masks[half], grad_out) for half in range(2)]
            deltas = [
                jnp.sum(pick(masks[half], product).T, axis=0, keepdims=True) for half in range(2)
            ]
            grad_query = [None, None]
            for other in range(step + 1):
                cols = slice(other * tile, (other + 1) * tile)
                keys = qkv_ref[pairs + pair, cols, :]
                values = qkv_ref[2 * pairs + pair, cols, :]
                key_part = value_part = None
                for half in range(2):
                    scores = nt(keys, queries[half])
                    if other == step:
                        scores = jnp.where(above, scores, masked_score)
                    probs = jnp.exp(scores - lse_ref[pair, half : half + 1, rows])
                    grad_scores = (probs * (nt(values, grads[half]) - deltas[half])).astype(bf16)
                    query_term = tn(grad_scores, keys)
                    grad_query[half] = (
                        query_term if grad_query[half] is None else grad_query[half] + query_term
                    )
                    key_term = mm(grad_scores, queries[half])
                    value_term = mm(probs.astype(bf16), grads[half])
                    key_part = key_term if key_part is None else key_part + key_term
                    value_part = value_term if value_part is None else value_part + value_term
                if other == step:
                    acc_ref[0, cols, :] = key_part
                    acc_ref[1, cols, :] = value_part
                else:
                    acc_ref[0, cols, :] += key_part
                    acc_ref[1, cols, :] += value_part
            grad_ref[rows, lanes] = (
                jnp.where(masks[0], grad_query[0], grad_query[1]) * SCALE
            ).astype(bf16)
        for part in range(2):
            lanes_to = pl.ds(pl.multiple_of((part + 1) * width + pair * LANES, LANES), LANES)
            grad_ref[:, lanes_to] = acc_ref[part].astype(bf16)

    hidden_t = hid_ref[...].T
    for copy in copies:
        copy.wait()
    outs = []
    if direct:
        share_count = dim // width
        share = lax.rem(lax.axis_index("seq"), share_count)
        gw_ref[3] = jnp.zeros_like(gw_ref[3])
        for part in range(3):
            for other in range(1, share_count):
                first = part * dim + lax.rem(share + other, share_count) * width
                outs.append(
                    pltpu.make_async_copy(
                        gw_ref.at[3],
                        all_ref.at[:, pl.ds(pl.multiple_of(first, LANES), width)],
                        sems.at[6 + part * (share_count - 1) + other - 1],
                    )
                )
                outs[-1].start()
    first, step = columns_of(pairs, direct, dim)
    for part in range(3):
        gw_ref[part] = mm(hidden_t, grad_ref[:, part * width : (part + 1) * width]).astype(bf16)
        outs.append(
            pltpu.make_async_copy(
                gw_ref.at[part],
                all_ref.at[:, pl.ds(pl.multiple_of(first + part * step, LANES), width)],
                sems.at[3 + part],
            )
        )
        outs[-1].start()
    for begin in range(0, length, tile):
        rows = slice(begin, begin + tile)
        ghid_ref[rows, :] = nt(grad_ref[rows, :], w_ref[...]).astype(bf16)
    for copy in outs:
        copy.wait()


def self_backward(pairs, direct, qkv, att, gatt, lse, hid, w, grads):
    length, dim = hid.shape
    width = pairs * LANES
    any_space = pl.BlockSpec(memory_space=pl.ANY)
    vmem = pl.BlockSpec(memory_space=pltpu.VMEM)
    return pl.pallas_call(
        partial(self_backward_kernel, pairs, direct),
        out_shape=(
            jax.ShapeDtypeStruct(grads.shape, bf16),
            jax.ShapeDtypeStruct((length, dim), bf16),
        ),
        in_specs=[vmem] * 5 + [any_space] * 2,
        out_specs=(any_space, vmem),
        scratch_shapes=[
            pltpu.VMEM((length, 3 * width), bf16),
            pltpu.VMEM((2, length, LANES), f32),
            pltpu.VMEM((4, dim, width), bf16),
            pltpu.VMEM((dim, 3 * width), bf16),
            pltpu.SemaphoreType.DMA((6 + 3 * (dim // width),)),
        ],
        input_output_aliases={6: 0} if direct else {},
        compiler_params=params(),
        name="self_backward",
    )(qkv, att, gatt, lse, hid, w, grads)


def spread_heads(block, rows, group):
    lane = lax.broadcasted_iota(jnp.int32, block.shape, 1) // HEAD
    return jnp.concatenate([pick(lane == head, block) for head in range(group)], axis=0)


def gather_heads(stacked, rows, group):
    lane = lax.broadcasted_iota(jnp.int32, (rows, stacked.shape[1]), 1) // HEAD
    out = None
    for head in range(group):
        part = pick(lane == head, stacked[head * rows : (head + 1) * rows])
        out = part if out is None else out + part
    return out


def live_keys(presence_ref, span, shape, axis, neighbours, each):
    index = lax.broadcasted_iota(jnp.int32, shape, axis) // each
    live = jnp.zeros(shape, f32)
    anyone = None
    for which in range(neighbours):
        here = presence_ref[span * neighbours + which]
        there = jnp.where(here > 0, 1.0, 0.0).astype(f32)
        live = jnp.where(index == which, there, live)
        anyone = here if anyone is None else jnp.maximum(anyone, here)
    return live, anyone.astype(f32)


def cross_forward_kernel(
    spans,
    neighbours,
    presence_ref,
    att_ref,
    x_ref,
    norms_ref,
    perm_ref,
    perm_att_ref,
    near_ref,
    w_out_ref,
    w_cq_ref,
    w_ck_ref,
    w_cv_ref,
    w_co_ref,
    att_p_ref,
    first_ref,
    hid_p_ref,
    cross_q_ref,
    near_p_ref,
    near_kv_ref,
    co_p_ref,
    second_ref,
    cross_ref,
):
    count, dim = x_ref.shape
    rows_near = near_ref.shape[0]
    span_len = count // spans
    near = rows_near // spans
    group = 256 // HEAD
    tile = 512

    att_p_ref[...] = mm(att_ref[...], perm_att_ref[...]).astype(bf16)
    first_ref[...] = x_ref[...].astype(f32) + mm(att_p_ref[...], w_out_ref[...])

    normed, _ = centre_scale(first_ref[...])
    hidden = (normed * norms_ref[2:3, :] + norms_ref[3:4, :]).astype(bf16)
    hid_p_ref[...] = mm(hidden, perm_ref[...]).astype(bf16)
    cross_q_ref[...] = mm(hid_p_ref[...], w_cq_ref[...]).astype(bf16)

    @pl.loop(0, rows_near // tile)
    def _(step):
        rows = rows_of(step, tile)
        near_p_ref[rows, :] = mm(near_ref[rows, :], perm_ref[...]).astype(bf16)
        near_kv_ref[rows, :dim] = mm(near_p_ref[rows, :], w_ck_ref[...]).astype(bf16)
        near_kv_ref[rows, dim:] = mm(near_p_ref[rows, :], w_cv_ref[...]).astype(bf16)

    @pl.loop(0, spans)
    def _(span):
        rows = rows_of(span, span_len)
        keys = rows_of(span, near)
        live, anyone = live_keys(presence_ref, span, (1, near), 1, neighbours, near // neighbours)
        for begin in range(0, dim, group * HEAD):
            lanes = slice(begin, begin + group * HEAD)
            lanes_v = slice(dim + begin, dim + begin + group * HEAD)
            query = spread_heads(cross_q_ref[rows, lanes] * SCALE, span_len, group)
            scores = jnp.where(live > 0, nt(query, near_kv_ref[keys, lanes]), masked_score)
            peak = jnp.max(scores, axis=-1, keepdims=True)
            expon = jnp.exp(scores - peak) * live
            total = jnp.sum(expon, axis=-1, keepdims=True) + 1.0 - anyone
            out = mm(expon.astype(bf16), near_kv_ref[keys, lanes_v]) / total
            cross_ref[rows, lanes] = gather_heads(out, span_len, group).astype(bf16)

    co_p_ref[...] = mm(cross_ref[...], perm_ref[...]).astype(bf16)
    second_ref[...] = first_ref[...] + mm(co_p_ref[...], w_co_ref[...])


def column_block(rows, width, index):
    return pl.BlockSpec((rows, width), lambda *_: (0, index), pipeline_mode=pl.Buffered(1))


def whole(array):
    return pl.BlockSpec(array.shape, lambda *_: (0,) * array.ndim, pipeline_mode=pl.Buffered(1))


def whole_shape(shape):
    return pl.BlockSpec(shape, lambda *_: (0,) * len(shape), pipeline_mode=pl.Buffered(1))


def cross_forward(spans, neighbours, presence, att, x, norms, perm, perm_att, near, weights):
    count, dim = x.shape
    rows_near = near.shape[0]
    out_shape = (
        jax.ShapeDtypeStruct((count, dim), bf16),
        jax.ShapeDtypeStruct((count, dim), f32),
        jax.ShapeDtypeStruct((count, dim), bf16),
        jax.ShapeDtypeStruct((count, dim), bf16),
        jax.ShapeDtypeStruct((rows_near, dim), bf16),
        jax.ShapeDtypeStruct((rows_near, 2 * dim), bf16),
        jax.ShapeDtypeStruct((count, dim), bf16),
        jax.ShapeDtypeStruct((count, dim), f32),
    )
    operands = (att, x, norms, perm, perm_att, near)
    return pl.pallas_call(
        partial(cross_forward_kernel, spans, neighbours),
        out_shape=out_shape,
        grid=(1,),
        in_specs=[pl.BlockSpec(memory_space=pltpu.SMEM)]
        + [whole(op) for op in operands]
        + [column_block(dim, dim, index) for index in (3, 4, 5, 6, 7)],
        out_specs=tuple(whole_shape(shape.shape) for shape in out_shape),
        scratch_shapes=[pltpu.VMEM((count, dim), bf16)],
        compiler_params=params(),
        name="cross_forward",
    )(presence, *operands, *([weights] * 5))


def feed_kernel(
    second_ref,
    cot_ref,
    norms_ref,
    perm_ref,
    w_up_ref,
    w_down_ref,
    out_ref,
    gsecond_ref,
    all_ref,
    gnorm_ref,
    hid_p_ref,
    hid_t_ref,
    cot_p_ref,
    cot_t_ref,
    result_ref,
    back_ref,
    gup_ref,
    gdown_ref,
    sems,
):
    step = pl.program_id(0)
    last = pl.num_programs(0) - 1
    slot = lax.rem(step, 2)
    dim, tile = w_up_ref.shape

    def copies(step, slot):
        up = pl.multiple_of(8 * dim + step * tile, tile)
        down = pl.multiple_of(8 * dim + (last + 1 + step) * tile, tile)
        return (
            pltpu.make_async_copy(gup_ref.at[slot], all_ref.at[:, pl.ds(up, tile)], sems.at[0, slot]),
            pltpu.make_async_copy(
                gdown_ref.at[slot], all_ref.at[:, pl.ds(down, tile)], sems.at[1, slot]
            ),
        )

    @pl.when(step >= 2)
    def _():
        for copy in copies(step - 2, slot):
            copy.wait()

    @pl.when(step == 0)
    def _():
        normed, _ = centre_scale(second_ref[...])
        hidden = (normed * norms_ref[4:5, :] + norms_ref[5:6, :]).astype(bf16)
        hid_p_ref[...] = mm(hidden, perm_ref[...]).astype(bf16)
        hid_t_ref[...] = hid_p_ref[...].T
        cot_p_ref[...] = mm(cot_ref[...], perm_ref[...]).astype(bf16)
        cot_t_ref[...] = cot_p_ref[...].T
        result_ref[...] = jnp.zeros_like(result_ref)
        back_ref[...] = jnp.zeros_like(back_ref)

    upward = mm(hid_p_ref[...], w_up_ref[...])
    active, slope = gelu_parts(upward)
    active = active.astype(bf16)
    result_ref[...] += nt(active, w_down_ref[...])
    gdown_ref[slot] = mm(cot_t_ref[...], active).astype(bf16)
    grad_up = (mm(cot_p_ref[...], w_down_ref[...]) * slope).astype(bf16)
    gup_ref[slot] = mm(hid_t_ref[...], grad_up).astype(bf16)
    for copy in copies(step, slot):
        copy.start()
    back_ref[...] += nt(grad_up, w_up_ref[...])

    @pl.when(step == last)
    def _():
        out_ref[...] = (
            second_ref[...] + nt(result_ref[...].astype(bf16), perm_ref[...])
        ).astype(bf16)
        upstream = nt(back_ref[...].astype(bf16), perm_ref[...])
        normed, recip = centre_scale(second_ref[...])
        back, gain, shift = norm_back(upstream, normed, recip, norms_ref[4:5, :])
        gsecond_ref[...] = cot_ref[...].astype(f32) + back
        gnorm_ref[0:1, :] = gain
        gnorm_ref[1:2, :] = shift
        for which in (step - 1, step):
            for copy in copies(which, lax.rem(which, 2)):
                copy.wait()


def feed(second, cot, norms, perm, weights):
    count, dim = second.shape
    ffw = (weights.shape[1] - 8 * dim) // 2
    tile = 512
    first_up = 8 * dim // tile
    first_down = (8 * dim + ffw) // tile
    out_shape = (
        jax.ShapeDtypeStruct((count, dim), bf16),
        jax.ShapeDtypeStruct((count, dim), f32),
        jax.ShapeDtypeStruct(weights.shape, bf16),
        jax.ShapeDtypeStruct((2, dim), f32),
    )
    operands = (second, cot, norms, perm)
    return pl.pallas_call(
        feed_kernel,
        out_shape=out_shape,
        grid=(ffw // tile,),
        in_specs=[whole(op) for op in operands]
        + [
            pl.BlockSpec((dim, tile), lambda i: (0, first_up + i)),
            pl.BlockSpec((dim, tile), lambda i: (0, first_down + i)),
        ],
        out_specs=(
            whole_shape((count, dim)),
            whole_shape((count, dim)),
            pl.BlockSpec(memory_space=pl.ANY),
            whole_shape((2, dim)),
        ),
        scratch_shapes=[
            pltpu.VMEM((count, dim), bf16),
            pltpu.VMEM((dim, count), bf16),
            pltpu.VMEM((count, dim), bf16),
            pltpu.VMEM((dim, count), bf16),
            pltpu.VMEM((count, dim), f32),
            pltpu.VMEM((count, dim), f32),
            pltpu.VMEM((2, dim, tile), bf16),
            pltpu.VMEM((2, dim, tile), bf16),
            pltpu.SemaphoreType.DMA((2, 2)),
        ],
        compiler_params=params(),
        name="feed",
    )(*operands, weights, weights)


def cross_backward_kernel(
    spans,
    neighbours,
    presence_ref,
    gsecond_ref,
    first_ref,
    norms_ref,
    perm_ref,
    perm_att_ref,
    att_p_ref,
    hid_p_ref,
    cross_q_ref,
    near_p_ref,
    near_kv_ref,
    co_p_ref,
    w_out_ref,
    w_cq_ref,
    w_co_ref,
    _,
    gfirst_ref,
    gatt_ref,
    all_ref,
    gnorm_ref,
    gco_ref,
    gcq_ref,
    gnear_ref,
    gw_ref,
    sems,
):
    count, dim = first_ref.shape
    rows_near = near_p_ref.shape[0]
    span_len = count // spans
    near = rows_near // spans
    group = 256 // HEAD
    outs = []

    def keep(index, value):
        gw_ref[index] = value.astype(bf16)
        outs.append(
            pltpu.make_async_copy(
                gw_ref.at[index],
                all_ref.at[:, pl.ds((3 + index) * dim, dim)],
                sems.at[index],
            )
        )
        outs[-1].start()

    upper = gsecond_ref[...].astype(bf16)
    keep(4, mm(co_p_ref[...].T, upper))
    gco_ref[...] = nt(nt(upper, w_co_ref[...]).astype(bf16), perm_ref[...]).astype(bf16)

    @pl.loop(0, spans)
    def _(span):
        rows = rows_of(span, span_len)
        keys = rows_of(span, near)
        live, anyone = live_keys(presence_ref, span, (near, 1), 0, neighbours, near // neighbours)
        for begin in range(0, dim, group * HEAD):
            lanes = slice(begin, begin + group * HEAD)
            lanes_v = slice(dim + begin, dim + begin + group * HEAD)
            query = spread_heads(cross_q_ref[rows, lanes] * SCALE, span_len, group)
            grad_out = spread_heads(gco_ref[rows, lanes], span_len, group)
            key = near_kv_ref[keys, lanes]
            scores = jnp.where(live > 0, nt(key, query), masked_score)
            peak = jnp.max(scores, axis=0, keepdims=True)
            expon = jnp.exp(scores - peak) * live
            total = jnp.sum(expon, axis=0, keepdims=True) + 1.0 - anyone
            probs = expon * (1.0 / total)
            grad_probs = nt(near_kv_ref[keys, lanes_v], grad_out)
            inner = jnp.sum(probs * grad_probs, axis=0, keepdims=True)
            grad_scores = (probs * (grad_probs - inner)).astype(bf16)
            gcq_ref[rows, lanes] = (
                gather_heads(tn(grad_scores, key), span_len, group) * SCALE
            ).astype(bf16)
            gnear_ref[keys, lanes] = mm(grad_scores, query).astype(bf16)
            gnear_ref[keys, lanes_v] = mm(probs.astype(bf16), grad_out).astype(bf16)

    near_t = near_p_ref[...].T
    for part in range(2):
        keep(2 + part, mm(near_t, gnear_ref[:, part * dim : (part + 1) * dim]))
    keep(1, mm(hid_p_ref[...].T, gcq_ref[...]))
    upstream = nt(nt(gcq_ref[...], w_cq_ref[...]).astype(bf16), perm_ref[...])
    normed, recip = centre_scale(first_ref[...])
    back, gain, shift = norm_back(upstream, normed, recip, norms_ref[2:3, :])
    gnorm_ref[0:1, :] = gain
    gnorm_ref[1:2, :] = shift
    gfirst_ref[...] = gsecond_ref[...] + back
    lower = gfirst_ref[...].astype(bf16)
    keep(0, mm(att_p_ref[...].T, lower))
    gatt_ref[...] = nt(nt(lower, w_out_ref[...]).astype(bf16), perm_att_ref[...]).astype(bf16)
    for copy in outs:
        copy.wait()


def cross_backward(
    spans,
    neighbours,
    presence,
    gsecond,
    first,
    norms,
    perm,
    perm_att,
    att_p,
    hid_p,
    cross_q,
    near_p,
    near_kv,
    co_p,
    weights,
    grads,
):
    count, dim = first.shape
    rows_near = near_p.shape[0]
    out_shape = (
        jax.ShapeDtypeStruct((count, dim), f32),
        jax.ShapeDtypeStruct((count, perm_att.shape[0]), bf16),
        jax.ShapeDtypeStruct(grads.shape, bf16),
        jax.ShapeDtypeStruct((2, dim), f32),
    )
    operands = (
        gsecond,
        first,
        norms,
        perm,
        perm_att,
        att_p,
        hid_p,
        cross_q,
        near_p,
        near_kv,
        co_p,
    )
    return pl.pallas_call(
        partial(cross_backward_kernel, spans, neighbours),
        out_shape=out_shape,
        grid=(1,),
        in_specs=[pl.BlockSpec(memory_space=pltpu.SMEM)]
        + [whole(op) for op in operands]
        + [column_block(dim, dim, index) for index in (3, 4, 7)]
        + [pl.BlockSpec(memory_space=pl.ANY)],
        out_specs=tuple(
            pl.BlockSpec(memory_space=pl.ANY) if index == 2 else whole_shape(shape.shape)
            for index, shape in enumerate(out_shape)
        ),
        scratch_shapes=[
            pltpu.VMEM((count, dim), bf16),
            pltpu.VMEM((count, dim), bf16),
            pltpu.VMEM((rows_near, 2 * dim), bf16),
            pltpu.VMEM((5, dim, dim), bf16),
            pltpu.SemaphoreType.DMA((5,)),
        ],
        input_output_aliases={len(operands) + 4: 2},
        compiler_params=params(),
        name="cross_backward",
    )(presence, *operands, *([weights] * 3), grads)


def last_norm_kernel(parts_ref, x_ref, gfirst_ref, norms_ref, perm_ref, out_ref, gnorm_ref):
    total = parts_ref[0].astype(f32)
    for part in range(1, parts_ref.shape[0]):
        total = total + parts_ref[part].astype(f32)
    upstream = nt(total.astype(bf16), perm_ref[...])
    normed, recip = centre_scale(x_ref[...].astype(f32))
    back, gain, shift = norm_back(upstream, normed, recip, norms_ref[0:1, :])
    out_ref[...] = gfirst_ref[...] + back
    gnorm_ref[0:1, :] = gain
    gnorm_ref[1:2, :] = shift


def last_norm(parts, x, gfirst, norms, perm):
    count, dim = x.shape
    return pl.pallas_call(
        last_norm_kernel,
        out_shape=(
            jax.ShapeDtypeStruct((count, dim), f32),
            jax.ShapeDtypeStruct((2, dim), f32),
        ),
        compiler_params=params(),
        name="last_norm",
    )(parts, x, gfirst, norms, perm)


MESH = pl.DeviceIdType.MESH


class Place:
    def __init__(self, lines):
        self.lines = lines
        self.z = lax.axis_index("dp")
        self.me = lax.axis_index("seq")
        core, x, y = self.me % 2, (self.me // 2) % 2, self.me // 4
        self.core, self.chip = core, self.me // 2
        self.sib = self.me + 1 - 2 * core
        self.xn = self.me + 2 - 4 * x
        self.yn = self.me + 4 - 8 * y
        self.dg = self.xn + 4 - 8 * y

    def events(self):
        found = [(None, self.z, 0, 0)]
        for far in range(1, self.lines):
            found.append((self.z >= far, self.z - far, far, -1))
            found.append((self.z + far < self.lines, self.z + far, far, 1))
        return found

    def plane(self):
        return [lax.rem(self.me + step, 8) for step in range(1, 8)]

    def line(self):
        return [lax.rem(self.z + step, self.lines) for step in range(1, self.lines)]

    def meet(self):
        barrier = pltpu.get_barrier_semaphore()
        for other in self.plane():
            pl.semaphore_signal(
                barrier, inc=1, device_id={"dp": self.z, "seq": other}, device_id_type=MESH
            )
        for other in self.line():
            pl.semaphore_signal(
                barrier, inc=1, device_id={"dp": other, "seq": self.me}, device_id_type=MESH
            )
        pl.semaphore_wait(barrier, 7 + self.lines - 1)


def when(condition, body):
    if condition is None:
        body()
    else:
        pl.when(condition)(body)


def both(first, second):
    return second if first is None else jnp.logical_and(first, second)


class Sender:
    def __init__(self, place, send_sems):
        self.place, self.sems, self.open = place, send_sems, []

    def start(self, condition, src, dst, recv_sem, z=None, seq=None):
        place = self.place
        target = {"dp": place.z if z is None else z, "seq": place.me if seq is None else seq}
        copy = pltpu.make_async_remote_copy(
            src_ref=src,
            dst_ref=dst,
            send_sem=self.sems.at[len(self.open)],
            recv_sem=recv_sem,
            device_id=target,
            device_id_type=MESH,
        )
        self.open.append((condition, copy))
        when(condition, copy.start)

    def arrived(self, condition, ref, recv_sem):
        copy = pltpu.make_async_remote_copy(
            src_ref=ref,
            dst_ref=ref,
            send_sem=self.sems.at[0],
            recv_sem=recv_sem,
            device_id={"dp": self.place.z, "seq": self.place.sib},
            device_id_type=MESH,
        )
        when(condition, copy.wait_recv)

    def finish(self):
        for condition, copy in self.open:
            when(condition, copy.wait_send)


def gather_kernel(
    lines,
    w_ref,
    small_ref,
    x_ref,
    wts_ref,
    norms_ref,
    rows_ref,
    own_ref,
    send_sems,
    z_sems,
    x_sems,
    y_sems,
    a_sems,
    b_sems,
    sib_sems,
    norm_sems,
    row_sems,
    local_sems,
):
    place = Place(lines)
    z, me = place.z, place.me
    unit_rows, unit_cols = own_ref.shape
    half = unit_rows // 2
    tokens = x_ref.shape[1]
    own_ref[...] = w_ref[...].astype(bf16)
    place.meet()
    send = Sender(place, send_sems)

    def unit(line, seq, begin=0, size=unit_rows):
        return wts_ref.at[
            pl.ds(pl.multiple_of(line * unit_rows + begin, 16), size),
            pl.ds(pl.multiple_of(seq * unit_cols, unit_cols), unit_cols),
        ]

    keep = pltpu.make_async_copy(own_ref, unit(z, me), local_sems.at[0])
    keep.start()

    events = place.events()

    def obtain(index):
        condition, line, far, side = events[index]
        mine = unit(line, me)
        src = own_ref if far == 0 else mine
        if far:
            send.arrived(condition, mine, z_sems.at[line])
        if side >= 0:
            send.start(both(condition, z > 0), src, mine, z_sems.at[line], z=z - 1)
        if side <= 0:
            send.start(both(condition, z < lines - 1), src, mine, z_sems.at[line], z=z + 1)
        send.start(condition, src, mine, x_sems.at[line], seq=place.xn)
        send.start(condition, src, mine, y_sems.at[line], seq=place.yn)
        send.start(condition, src, mine, sib_sems.at[0, line], seq=place.sib)

    def pass_on(index):
        condition, line, _, _ = events[index]
        from_x, from_y = unit(line, place.xn), unit(line, place.yn)
        send.arrived(condition, from_x, x_sems.at[line])
        part = unit(line, place.xn, half, half)
        send.start(condition, part, part, b_sems.at[line], seq=place.yn)
        send.start(condition, from_x, from_x, sib_sems.at[1, line], seq=place.sib)
        send.arrived(condition, from_y, y_sems.at[line])
        part = unit(line, place.yn, 0, half)
        send.start(condition, part, part, a_sems.at[line], seq=place.xn)
        send.start(condition, from_y, from_y, sib_sems.at[2, line], seq=place.sib)

    def corner(index):
        condition, line, _, _ = events[index]
        part = unit(line, place.dg, 0, half)
        send.arrived(condition, part, a_sems.at[line])
        send.start(condition, part, part, sib_sems.at[3, line], seq=place.sib)
        part = unit(line, place.dg, half, half)
        send.arrived(condition, part, b_sems.at[line])
        send.start(condition, part, part, sib_sems.at[4, line], seq=place.sib)

    def row_block(seq):
        return rows_ref.at[pl.ds(pl.multiple_of(seq * tokens, tokens), tokens)]

    obtain(0)
    own_rows = pltpu.make_async_copy(x_ref.at[place.chip], row_block(me), local_sems.at[1])
    own_rows.start()
    send.start(None, x_ref.at[place.chip], row_block(me), row_sems.at[me], seq=place.sib)
    others = (place.xn, place.yn, place.dg)
    for other in others:
        send.start(None, x_ref.at[other // 2], row_block(me), row_sems.at[me], seq=other)
    for other in place.line():
        send.start(None, small_ref, norms_ref.at[z], norm_sems.at[z], z=other)
    norms_ref[z] = small_ref[...]

    last = len(events)
    order = [obtain, 1, obtain, 2, pass_on, 0]
    far = 3
    while far < last:
        order += [obtain, far, obtain, far + 1, pass_on, far - 2, pass_on, far - 1]
        order += [corner, 0] if far == 3 else [corner, far - 4, corner, far - 3]
        far += 2
    done_pass = far - 2
    order += [pass_on, done_pass, pass_on, done_pass + 1]
    done_corner = max(far - 4, 1)
    for index in range(done_corner, last):
        order += [corner, index]
    for position in range(0, len(order), 2):
        order[position](order[position + 1])
        if position == 4:
            for other in others:
                send.arrived(None, row_block(other), row_sems.at[other])
                send.start(
                    None, row_block(other), row_block(other), row_sems.at[other], seq=place.sib
                )

    for other in others:
        theirs = other + 1 - 2 * place.core
        send.arrived(None, row_block(theirs), row_sems.at[theirs])
    send.arrived(None, row_block(place.sib), row_sems.at[place.sib])
    for other in place.line():
        send.arrived(None, norms_ref.at[other], norm_sems.at[other])
    for line in range(lines):
        for index, first in enumerate((me, place.xn, place.yn)):
            theirs = first + 1 - 2 * place.core
            send.arrived(None, unit(line, theirs), sib_sems.at[index, line])
        theirs = place.dg + 1 - 2 * place.core
        send.arrived(None, unit(line, theirs, 0, half), sib_sems.at[3, line])
        send.arrived(None, unit(line, theirs, half, half), sib_sems.at[4, line])
    own_rows.wait()
    keep.wait()
    send.finish()


def gather(lines, w_shard, small, inputs):
    unit_rows, unit_cols = w_shard.shape
    seqs, tokens, dim = inputs.shape
    any_space = pl.BlockSpec(memory_space=pl.ANY)
    vmem = pl.BlockSpec(memory_space=pltpu.VMEM)
    dma = pltpu.SemaphoreType.DMA
    return pl.pallas_call(
        partial(gather_kernel, lines),
        out_shape=(
            jax.ShapeDtypeStruct((unit_rows * lines, unit_cols * 8), bf16),
            jax.ShapeDtypeStruct((lines,) + small.shape, bf16),
            jax.ShapeDtypeStruct((8 * tokens, dim), bf16),
        ),
        in_specs=[vmem, vmem, any_space],
        out_specs=(any_space, vmem, any_space),
        scratch_shapes=[
            pltpu.VMEM((unit_rows, unit_cols), bf16),
            dma((11 * (2 * lines - 1) + 7 + lines,)),
            dma((lines,)),
            dma((lines,)),
            dma((lines,)),
            dma((lines,)),
            dma((lines,)),
            dma((5, lines)),
            dma((lines,)),
            dma((8,)),
            dma((2,)),
        ],
        compiler_params=pltpu.CompilerParams(
            vmem_limit_bytes=VMEM_BYTES, collective_id=1, has_side_effects=True
        ),
        name="gather_weights",
    )(w_shard, small, inputs)


def reduce_kernel(
    lines,
    grads_ref,
    small_ref,
    shard_ref,
    norms_ref,
    mine_ref,
    sib_ref,
    corner_a_ref,
    corner_b_ref,
    from_x_ref,
    from_y_ref,
    below_ref,
    above_ref,
    plane_ref,
    plane_sum_ref,
    line_ref,
    send_sems,
    load_sems,
    sib_sems,
    a_sems,
    b_sems,
    x_sems,
    y_sems,
    below_sems,
    above_sems,
    plane_sems,
    line_sems,
):
    place = Place(lines)
    z, me = place.z, place.me
    unit_rows, unit_cols = shard_ref.shape
    half = unit_rows // 2
    tile = 32
    place.meet()
    send = Sender(place, send_sems)
    chips = (place.dg, place.yn, place.xn, me)
    corner, over_y, over_x, here = range(4)

    def unit(line, seq):
        return grads_ref.at[
            pl.ds(pl.multiple_of(line * unit_rows, unit_rows), unit_rows),
            pl.ds(pl.multiple_of(seq * unit_cols, unit_cols), unit_cols),
        ]

    def load(which, line):
        return pltpu.make_async_copy(
            unit(line, chips[which]), mine_ref.at[which, line], load_sems.at[which, line]
        )

    for other in place.plane():
        send.start(None, small_ref, plane_ref.at[me], plane_sems.at[me], seq=other)
    plane_ref[me] = small_ref[...]

    events = place.events()[::-1]
    for condition, line, _, _ in events:
        for which in range(4):
            theirs = chips[which] + 1 - 2 * place.core
            send.start(
                condition,
                unit(line, theirs),
                sib_ref.at[which, line],
                sib_sems.at[which, line],
                seq=place.sib,
            )
            when(condition, load(which, line).start)

    def add(target, *terms, begin=0, size=unit_rows):
        @pl.loop(0, size // tile)
        def _(step):
            rows = pl.ds(pl.multiple_of(begin + step * tile, tile), tile)
            if len(terms) == 1:
                ref, first = terms[0]
                at = pl.ds(pl.multiple_of(begin - first + step * tile, tile), tile)
                target[rows, :] = target[rows, :] + ref[at, :]
            else:
                total = target[rows, :].astype(f32)
                for ref, first in terms:
                    at = pl.ds(pl.multiple_of(begin - first + step * tile, tile), tile)
                    total = total + ref[at, :].astype(f32)
                target[rows, :] = total.astype(target.dtype)

    def own(which, index):
        condition, line, _, _ = events[index]
        send.arrived(condition, sib_ref.at[which, line], sib_sems.at[which, line])
        when(condition, load(which, line).wait)

    def first(index):
        condition, line, _, _ = events[index]
        own(corner, index)
        target = mine_ref.at[corner, line]
        when(condition, lambda: add(target, (sib_ref.at[corner, line], 0)))
        send.start(
            condition,
            target.at[pl.ds(0, half)],
            corner_a_ref.at[line],
            a_sems.at[line],
            seq=place.xn,
        )
        send.start(
            condition,
            target.at[pl.ds(half, half)],
            corner_b_ref.at[line],
            b_sems.at[line],
            seq=place.yn,
        )

    def second(index):
        condition, line, _, _ = events[index]
        for which, part, sems, begin, to, landing, landing_sems in (
            (over_y, corner_a_ref, a_sems, 0, place.yn, from_y_ref, y_sems),
            (over_x, corner_b_ref, b_sems, half, place.xn, from_x_ref, x_sems),
        ):
            own(which, index)
            send.arrived(condition, part.at[line], sems.at[line])
            target = mine_ref.at[which, line]

            def body(which=which, part=part, begin=begin, target=target):
                add(
                    target,
                    (sib_ref.at[which, line], 0),
                    (part.at[line], begin),
                    begin=begin,
                    size=half,
                )
                add(target, (sib_ref.at[which, line], 0), begin=half - begin, size=half)

            when(condition, body)
            send.start(condition, target, landing.at[line], landing_sems.at[line], seq=to)

    def third(index):
        condition, line, far, side = events[index]
        own(here, index)
        send.arrived(condition, from_x_ref.at[line], x_sems.at[line])
        send.arrived(condition, from_y_ref.at[line], y_sems.at[line])
        target = mine_ref.at[here, line]
        terms = [(ref.at[line], 0) for ref in (sib_ref.at[here], from_x_ref, from_y_ref)]
        if side == 0:
            has_below, has_above = z > 0, z < lines - 1
            add(target, *terms)
            send.arrived(has_below, below_ref.at[line], below_sems.at[line])
            send.arrived(has_above, above_ref.at[line], above_sems.at[line])

            @pl.loop(0, unit_rows // tile)
            def _(step):
                rows = rows_of(step, tile)
                shard_ref[rows, :] = target[rows, :].astype(f32)

            when(has_below, lambda: add(shard_ref, (below_ref.at[line], 0)))
            when(has_above, lambda: add(shard_ref, (above_ref.at[line], 0)))
            return
        landing, sems = (below_ref, below_sems) if side > 0 else (above_ref, above_sems)
        more = both(condition, z > 0) if side > 0 else both(condition, z < lines - 1)
        none = both(condition, z == 0) if side > 0 else both(condition, z == lines - 1)
        send.arrived(more, landing.at[line], sems.at[line])
        when(more, lambda: add(target, *terms, (landing.at[line], 0)))
        when(none, lambda: add(target, *terms))
        send.start(condition, target, landing.at[line], sems.at[line], z=z + side)

    count = len(events)
    first(0)
    first(1)
    for index in range(2, count + 4):
        if index < count:
            first(index)
        if 0 <= index - 2 < count:
            second(index - 2)
        if index == 3:
            for other in place.plane():
                send.arrived(None, plane_ref.at[other], plane_sems.at[other])
            total = plane_ref[0]
            for other in range(1, 8):
                total = total + plane_ref[other]
            plane_sum_ref[...] = total
            line_ref[z] = total
            for other in place.line():
                send.start(None, plane_sum_ref, line_ref.at[z], line_sems.at[z], z=other)
        if 0 <= index - 4 < count:
            third(index - 4)

    for other in place.line():
        send.arrived(None, line_ref.at[other], line_sems.at[other])
    total = line_ref[0]
    for other in range(1, lines):
        total = total + line_ref[other]
    norms_ref[...] = total
    send.finish()


def reduce_grads(lines, grads, small):
    rows, cols = grads.shape
    unit_rows, unit_cols = rows // lines, cols // 8
    half = unit_rows // 2
    any_space = pl.BlockSpec(memory_space=pl.ANY)
    vmem = pl.BlockSpec(memory_space=pltpu.VMEM)
    dma = pltpu.SemaphoreType.DMA
    return pl.pallas_call(
        partial(reduce_kernel, lines),
        out_shape=(
            jax.ShapeDtypeStruct((unit_rows, unit_cols), f32),
            jax.ShapeDtypeStruct(small.shape, f32),
        ),
        in_specs=[any_space, vmem],
        out_specs=(vmem, vmem),
        scratch_shapes=[
            pltpu.VMEM((4, lines, unit_rows, unit_cols), bf16),
            pltpu.VMEM((4, lines, unit_rows, unit_cols), bf16),
            pltpu.VMEM((lines, half, unit_cols), bf16),
            pltpu.VMEM((lines, half, unit_cols), bf16),
            pltpu.VMEM((lines, unit_rows, unit_cols), bf16),
            pltpu.VMEM((lines, unit_rows, unit_cols), bf16),
            pltpu.VMEM((lines, unit_rows, unit_cols), bf16),
            pltpu.VMEM((lines, unit_rows, unit_cols), bf16),
            pltpu.VMEM((8,) + small.shape, f32),
            pltpu.VMEM(small.shape, f32),
            pltpu.VMEM((lines,) + small.shape, f32),
            dma((9 * (2 * lines - 1) + 7 + lines,)),
            dma((4, lines)),
            dma((4, lines)),
            dma((lines,)),
            dma((lines,)),
            dma((lines,)),
            dma((lines,)),
            dma((lines,)),
            dma((lines,)),
            dma((8,)),
            dma((lines,)),
        ],
        compiler_params=pltpu.CompilerParams(
            vmem_limit_bytes=VMEM_BYTES, collective_id=2, has_side_effects=True
        ),
        name="reduce_grads",
    )(grads, small)


def adam_update(grad, weight, first, second, average, rate, decay):
    first = beta_first * first + (1.0 - beta_first) * grad
    second = beta_second * second + (1.0 - beta_second) * grad * grad
    stepped = (
        first / (1.0 - beta_first**STEP) / (jnp.sqrt(second / (1.0 - beta_second**STEP)) + adam_eps)
    )
    weight = weight - rate * (stepped + decay * weight)
    average = ema_decay * average + (1.0 - ema_decay) * weight
    return (first, second, weight, average)


def on_device(
    inputs,
    cotangent,
    neighbours,
    presence,
    row_order,
    w_master,
    w_first,
    w_second,
    w_average,
    n_master,
    n_first,
    n_second,
    n_average,
):
    seqs, tokens, dim = inputs.shape
    heads = dim // HEAD
    devices = lax.axis_size("seq")
    count = seqs * tokens
    length = devices * tokens
    me = lax.axis_index("seq")
    shares = devices // seqs
    held = heads // shares
    pairs = (held + 1) // 2
    width = pairs * LANES
    spare = width - held * HEAD
    sequence, share = me // shares, me % shares

    lines = lax.axis_size("dp")
    planar = devices == 8 and seqs == 4
    direct = spare == 0
    if planar:
        part = n_master.shape[1]
        small = jnp.pad(n_master.astype(bf16), ((0, 16 - 6), (0, -part % LANES)))
        weights, norms, rows = gather(lines, w_master, small, inputs)
        norms = norms[:, :6, :part].transpose(1, 0, 2).reshape(6, dim).astype(f32)
    else:
        weights = lax.all_gather(w_master.astype(bf16), "dp", axis=0, tiled=True)
        weights = lax.all_gather(weights, "seq", axis=1, tiled=True)
        norms = lax.all_gather(n_master.astype(bf16), "dp", axis=1, tiled=True).astype(f32)
        rows = lax.all_to_all(jnp.repeat(inputs, shares, axis=0), "seq", 0, 0)
        rows = rows.reshape(length, dim)

    perm = (jnp.arange(dim)[:, None] == row_order[None, :]).astype(bf16)
    perm_att = jnp.pad(perm.reshape(shares, held * HEAD, dim), ((0, 0), (0, spare), (0, 0)))
    perm_att = perm_att.reshape(shares * width, dim)
    if direct:
        w_qkv = weights
    else:
        w_qkv = weights[:, : 3 * dim].reshape(dim, 3, shares, held * HEAD)
        w_qkv = lax.dynamic_index_in_dim(w_qkv, share, axis=2, keepdims=False)
        w_qkv = jnp.pad(w_qkv, ((0, 0), (0, 0), (0, spare))).reshape(dim, 3 * width)

    x = inputs.reshape(count, dim)
    hid, qkv, att, lse = self_forward(pairs, direct, rows, norms, perm, w_qkv)
    att_tok = (
        lax.all_to_all(att.reshape(devices, tokens, width), "seq", 0, 0)
        .reshape(seqs, shares, tokens, width)
        .transpose(0, 2, 1, 3)
        .reshape(count, shares * width)
    )
    spans = seqs * neighbours.shape[1]
    each = neighbours.shape[2]
    near = neighbours.reshape(-1, dim)
    live = presence.reshape(-1)
    att_p, first, hid_p, cross_q, near_p, near_kv, co_p, second = cross_forward(
        spans, each, live, att_tok, x, norms, perm, perm_att, near, weights
    )
    outputs, gsecond, grads, gnorm_e = feed(
        second, cotangent.reshape(count, dim), norms, perm, weights
    )
    gfirst, gatt_tok, grads, gnorm_c = cross_backward(
        spans,
        each,
        live,
        gsecond,
        first,
        norms,
        perm,
        perm_att,
        att_p,
        hid_p,
        cross_q,
        near_p,
        near_kv,
        co_p,
        weights,
        grads,
    )
    gatt = lax.all_to_all(
        gatt_tok.reshape(seqs, tokens, shares, width)
        .transpose(0, 2, 1, 3)
        .reshape(devices, tokens, width),
        "seq",
        0,
        0,
    ).reshape(length, width)
    gqkv, ghid = self_backward(
        pairs,
        direct,
        qkv,
        att,
        gatt,
        lse.transpose(0, 2, 1),
        hid,
        w_qkv,
        grads if direct else jnp.zeros((dim, 3 * width), bf16),
    )
    parts = (
        lax.all_to_all(ghid.reshape(devices, tokens, dim), "seq", 0, 0)
        .reshape(seqs, shares, tokens, dim)
        .transpose(1, 0, 2, 3)
        .reshape(shares, count, dim)
    )
    grad_inputs, gnorm_a = last_norm(parts, x, gfirst, norms, perm)

    if direct:
        grads = gqkv
    else:
        gqkv = gqkv.reshape(dim, 3, 1, width)[..., : held * HEAD]
        gqkv = jnp.where(jnp.arange(shares)[:, None] == share, gqkv, jnp.zeros_like(gqkv))
        grads = lax.dynamic_update_slice(grads, gqkv.reshape(dim, 3 * dim), (0, 0))
    norm_grads = jnp.concatenate([gnorm_a, gnorm_c, gnorm_e], axis=0)
    if planar:
        grad_shard, norm_sums = reduce_grads(lines, grads, jnp.pad(norm_grads, ((0, 2), (0, 0))))
        part = n_master.shape[1]
        norm_shard = lax.dynamic_slice(
            norm_sums, (0, lax.axis_index("dp") * part), (6, part)
        )
    else:
        norm_grads = lax.psum(norm_grads, "seq")
        partial_sum = lax.psum_scatter(grads, "seq", scatter_dimension=1, tiled=True)
        grad_shard = lax.psum_scatter(partial_sum, "dp", scatter_dimension=0, tiled=True)
        grad_shard = grad_shard.astype(f32)
        norm_shard = lax.psum_scatter(
            norm_grads.astype(bf16), "dp", scatter_dimension=1, tiled=True
        ).astype(f32)
    w_first_new, w_second_new, w_new, w_average_new = adam_update(
        grad_shard, w_master, w_first, w_second, w_average, learn_rate, weight_decay
    )
    n_first_new, n_second_new, n_new, n_average_new = adam_update(
        norm_shard, n_master, n_first, n_second, n_average, norm_rate, 0.0
    )
    return (
        outputs.reshape(seqs, tokens, dim),
        grad_inputs.reshape(seqs, tokens, dim),
        w_first_new,
        w_second_new,
        w_new,
        w_average_new,
        n_first_new,
        n_second_new,
        n_new,
        n_average_new,
    )


def solution(mesh):
    in_specs = (
        P("dp", "seq", None),
        P("dp", "seq", None),
        P("dp", "seq", None, None, None),
        P("dp", "seq", None),
        P(),
        P("dp", "seq"),
        P("dp", "seq"),
        P("dp", "seq"),
        P("dp", "seq"),
        P(None, "dp"),
        P(None, "dp"),
        P(None, "dp"),
        P(None, "dp"),
    )
    out_specs = (
        P("dp", "seq", None),
        P("dp", "seq", None),
        P("dp", "seq"),
        P("dp", "seq"),
        P("dp", "seq"),
        P("dp", "seq"),
        P(None, "dp"),
        P(None, "dp"),
        P(None, "dp"),
        P(None, "dp"),
    )
    return jax.shard_map(
        on_device, mesh=mesh, in_specs=in_specs, out_specs=out_specs, check_vma=False
    )
```

```python
from functools import partial

import jax
import jax.numpy as jnp
from jax import lax
from jax.experimental import pallas as pl
from jax.experimental.pallas import tpu as pltpu
from jax.sharding import PartitionSpec as P

HEAD = 64
STEP = 5
LANES = 128
SCALE = HEAD ** (-0.5)

beta_first = 0.9
beta_second = 0.95
adam_eps = 1e-08
learn_rate = 0.04
norm_rate = 0.6
weight_decay = 0.1
ema_decay = 0.5
norm_eps = 1e-05
masked_score = -1e30
VMEM_BYTES = 60 * 1024 * 1024
bf16 = jnp.bfloat16
f32 = jnp.float32


def mm(left, right):
    return lax.dot_general(left, right, (((1,), (0,)), ((), ())), preferred_element_type=f32)


def nt(left, right):
    return lax.dot_general(left, right, (((1,), (1,)), ((), ())), preferred_element_type=f32)


def tn(left, right):
    return lax.dot_general(left, right, (((0,), (0,)), ((), ())), preferred_element_type=f32)


def params():
    return pltpu.CompilerParams(vmem_limit_bytes=VMEM_BYTES)


def rows_of(index, size):
    return pl.ds(pl.multiple_of(index * size, size), size)


def centre_scale(values):
    centre = jnp.mean(values, axis=-1, keepdims=True)
    centred = values - centre
    spread = jnp.mean(centred * centred, axis=-1, keepdims=True)
    recip = lax.rsqrt(spread + norm_eps)
    return centred * recip, recip


def norm_back(upstream, normed, recip, gain):
    scaled = upstream * gain
    inner = (
        scaled
        - jnp.mean(scaled, axis=-1, keepdims=True)
        - normed * jnp.mean(scaled * normed, axis=-1, keepdims=True)
    )
    return (
        recip * inner,
        jnp.sum(upstream * normed, axis=0, keepdims=True),
        jnp.sum(upstream, axis=0, keepdims=True),
    )


def gelu_parts(value):
    const = 0.7978845608028654
    square = value * value
    bend = jnp.tanh(const * value * (1.0 + 0.044715 * square))
    half = 0.5 * (1.0 + bend)
    slope = half + 0.5 * value * (1.0 - bend * bend) * (const * (1.0 + 3 * 0.044715 * square))
    return value * half, slope


def head_mask(rows, half):
    lane = lax.broadcasted_iota(jnp.int32, (rows, LANES), 1)
    return (lane < HEAD) if half == 0 else (lane >= HEAD)


def pick(mask, value):
    return jnp.where(mask, value, jnp.zeros_like(value))


MESH = pl.DeviceIdType.MESH


class Place:
    def __init__(self, lines):
        self.lines = lines
        self.z = lax.axis_index("dp")
        self.me = lax.axis_index("seq")
        core, x, y = self.me % 2, (self.me // 2) % 2, self.me // 4
        self.core, self.x, self.y, self.chip = core, x, y, self.me // 2
        self.sib = self.me + 1 - 2 * core
        self.xn = self.me + 2 - 4 * x
        self.yn = self.me + 4 - 8 * y
        self.dg = self.xn + 4 - 8 * y

    def events(self):
        found = [(None, self.z, 0, 0)]
        for far in range(1, self.lines):
            found.append((self.z >= far, self.z - far, far, -1))
            found.append((self.z + far < self.lines, self.z + far, far, 1))
        return found

    def plane(self):
        return [lax.rem(self.me + step, 8) for step in range(1, 8)]

    def line(self):
        return [lax.rem(self.z + step, self.lines) for step in range(1, self.lines)]

    def meet(self):
        barrier = pltpu.get_barrier_semaphore()
        for other in self.plane():
            pl.semaphore_signal(
                barrier, inc=1, device_id={"dp": self.z, "seq": other}, device_id_type=MESH
            )
        for other in self.line():
            pl.semaphore_signal(
                barrier, inc=1, device_id={"dp": other, "seq": self.me}, device_id_type=MESH
            )
        pl.semaphore_wait(barrier, 7 + self.lines - 1)


def when(condition, body):
    if condition is None:
        body()
    else:
        pl.when(condition)(body)


def both(first, second):
    if first is None or second is None:
        return second if first is None else first
    return jnp.logical_and(first, second)


class Sender:
    def __init__(self, place, send_sems):
        self.place, self.sems, self.open = place, send_sems, []

    def start(self, condition, src, dst, recv_sem, z=None, seq=None):
        place = self.place
        target = {"dp": place.z if z is None else z, "seq": place.me if seq is None else seq}
        copy = pltpu.make_async_remote_copy(
            src_ref=src,
            dst_ref=dst,
            send_sem=self.sems.at[len(self.open)],
            recv_sem=recv_sem,
            device_id=target,
            device_id_type=MESH,
        )
        self.open.append((condition, copy))
        when(condition, copy.start)

    def arrived(self, condition, ref, recv_sem):
        copy = pltpu.make_async_remote_copy(
            src_ref=ref,
            dst_ref=ref,
            send_sem=self.sems.at[0],
            recv_sem=recv_sem,
            device_id={"dp": self.place.z, "seq": self.place.sib},
            device_id_type=MESH,
        )
        when(condition, copy.wait_recv)

    def finish(self):
        for condition, copy in self.open:
            when(condition, copy.wait_send)


class Weave:
    def __init__(self, steps):
        self.steps = list(steps)

    def some(self, count):
        for _ in range(min(count, len(self.steps))):
            self.steps.pop(0)()

    def rest(self):
        self.some(len(self.steps))


def unit_of(ref, lines, line, seq, begin=0, size=None):
    rows, cols = ref.shape[0] // lines, ref.shape[1] // 8
    size = rows if size is None else size
    return ref.at[
        pl.ds(pl.multiple_of(line * rows + begin, 16), size),
        pl.ds(pl.multiple_of(seq * cols, cols), cols),
    ]


class RowReduce:
    def __init__(self, place, send, grads, shard, row, refs):
        self.place, self.send, self.grads, self.shard, self.row = place, send, grads, shard, row
        self.mine, self.sib, self.rx, self.ry, self.below, self.above = refs[:6]
        self.load_sems, self.sib_sems, self.rx_sems, self.ry_sems = refs[6:10]
        self.below_sems, self.above_sems = refs[10:12]
        self.events = place.events()[::-1]

    @staticmethod
    def scratch(lines, rows, cols):
        dma = pltpu.SemaphoreType.DMA
        return [
            pltpu.VMEM((2, lines, rows, cols), bf16),
            pltpu.VMEM((2, lines, rows, cols), bf16),
        ] + [pltpu.VMEM((lines, rows, cols), bf16)] * 4 + [
            dma((2, lines)),
            dma((2, lines)),
        ] + [dma((lines,))] * 4

    def load(self, column, line):
        place = self.place
        seq = self.row * 4 + column * 2 + place.core
        return pltpu.make_async_copy(
            unit_of(self.grads, place.lines, line, seq),
            self.mine.at[column, line],
            self.load_sems.at[column, line],
        )

    def begin(self, columns):
        place = self.place
        for condition, line, _, _ in self.events:
            for column in columns:
                seq = self.row * 4 + column * 2 + 1 - place.core
                self.send.start(
                    condition,
                    unit_of(self.grads, place.lines, line, seq),
                    self.sib.at[column, line],
                    self.sib_sems.at[column, line],
                    seq=place.sib,
                )
                when(condition, self.load(column, line).start)

    def add(self, target, *terms):
        tile = 32

        @pl.loop(0, target.shape[0] // tile)
        def _(step):
            rows = rows_of(step, tile)
            if len(terms) == 1:
                target[rows, :] = target[rows, :] + terms[0][rows, :]
            else:
                total = target[rows, :].astype(f32)
                for term in terms:
                    total = total + term[rows, :].astype(f32)
                target[rows, :] = total.astype(target.dtype)

    def chip_sum(self, column, index):
        condition, line, _, _ = self.events[index]
        self.send.arrived(condition, self.sib.at[column, line], self.sib_sems.at[column, line])

        def body():
            self.load(column, line).wait()
            self.add(self.sib.at[column, line], self.mine.at[column, line])

        when(condition, body)

    def to_x(self, column, index, own):
        condition, line, _, _ = self.events[index]
        self.send.start(
            both(own, condition),
            self.sib.at[column, line],
            self.rx.at[line],
            self.rx_sems.at[line],
            seq=self.place.xn,
        )

    def x_sum(self, column, index, own):
        condition, line, _, _ = self.events[index]
        condition = both(own, condition)
        self.send.arrived(condition, self.rx.at[line], self.rx_sems.at[line])
        when(condition, lambda: self.add(self.sib.at[column, line], self.rx.at[line]))
        self.send.start(
            both(self.place.y != self.row, condition),
            self.sib.at[column, line],
            self.ry.at[line],
            self.ry_sems.at[line],
            seq=self.place.yn,
        )

    def y_sum(self, column, index, own):
        place, send = self.place, self.send
        condition, line, _, side = self.events[index]
        condition = both(both(own, condition), place.y == self.row)
        z, last = place.z, place.lines - 1
        target = self.sib.at[column, line]
        send.arrived(condition, self.ry.at[line], self.ry_sems.at[line])
        if side == 0:
            has_below, has_above = both(condition, z > 0), both(condition, z < last)
            send.arrived(has_below, self.below.at[line], self.below_sems.at[line])
            send.arrived(has_above, self.above.at[line], self.above_sems.at[line])
            tile = 32

            def total(*terms):
                @pl.loop(0, target.shape[0] // tile)
                def _(step):
                    rows = rows_of(step, tile)
                    value = target[rows, :].astype(f32)
                    for term in terms:
                        value = value + term[line, rows, :].astype(f32)
                    self.shard[rows, :] = value

            if last == 0:
                when(condition, lambda: total(self.ry))
                return
            when(both(condition, z == 0), lambda: total(self.ry, self.above))
            when(both(condition, z == last), lambda: total(self.ry, self.below))
            middle = both(both(condition, z > 0), z < last)
            when(middle, lambda: total(self.ry, self.below, self.above))
            return
        landing, sems = (self.below, self.below_sems) if side > 0 else (self.above, self.above_sems)
        more = both(condition, z > 0) if side > 0 else both(condition, z < last)
        none = both(condition, z == 0) if side > 0 else both(condition, z == last)
        send.arrived(more, landing.at[line], sems.at[line])
        when(more, lambda: self.add(target, self.ry.at[line], landing.at[line]))
        when(none, lambda: self.add(target, self.ry.at[line]))
        send.start(condition, target, landing.at[line], sems.at[line], z=z + side)

    def steps(self, column=None):
        place, count = self.place, len(self.events)
        found = []
        for index in range(count + 2):
            if index < count:
                if column is None:
                    found.append(partial(self.chip_sum, 1 - place.x, index))
                    found.append(partial(self.to_x, 1 - place.x, index, None))
                    found.append(partial(self.chip_sum, place.x, index))
                else:
                    found.append(partial(self.chip_sum, column, index))
                    found.append(partial(self.to_x, column, index, place.x != column))
            here, own = (place.x, None) if column is None else (column, place.x == column)
            if 0 <= index - 1 < count:
                found.append(partial(self.x_sum, here, index - 1, own))
            if 0 <= index - 2 < count:
                found.append(partial(self.y_sum, here, index - 2, own))
        return found


def columns_of(pairs, share_columns, dim):
    width = pairs * LANES
    if not share_columns:
        return 0, width
    return lax.rem(lax.axis_index("seq"), dim // width) * width, dim


def weight_copies(pairs, direct, dim, wts_ref, w_ref, sems):
    width = pairs * LANES
    first, step = columns_of(pairs, direct, dim)
    return [
        pltpu.make_async_copy(
            wts_ref.at[:, pl.ds(pl.multiple_of(first + part * step, LANES), width)],
            w_ref.at[:, pl.ds(part * width, width)],
            sems.at[part],
        )
        for part in range(3)
    ]


def self_forward_kernel(
    pairs, direct, x_ref, norms_ref, perm_ref, wts_ref, hid_ref, qkv_ref, att_ref, lse_ref, w_ref, sems
):
    length, dim = x_ref.shape
    width = pairs * LANES
    tile = 256
    tiles = length // tile
    copies = weight_copies(pairs, direct, dim, wts_ref, w_ref, sems)
    for copy in copies:
        copy.start()

    @pl.loop(0, tiles)
    def _(step):
        rows = rows_of(step, tile)
        normed, _ = centre_scale(x_ref[rows, :].astype(f32))
        hidden = (normed * norms_ref[0:1, :] + norms_ref[1:2, :]).astype(bf16)
        hid_ref[rows, :] = mm(hidden, perm_ref[...]).astype(bf16)

    for part in range(3):
        copies[part].wait()
        triple = mm(hid_ref[...], w_ref[:, part * width : (part + 1) * width]).astype(bf16)
        for pair in range(pairs):
            qkv_ref[part * pairs + pair] = triple[:, pair * LANES : (pair + 1) * LANES]

    below = lax.broadcasted_iota(jnp.int32, (tile, tile), 1) <= lax.broadcasted_iota(
        jnp.int32, (tile, tile), 0
    )
    masks = [head_mask(tile, 0), head_mask(tile, 1)]

    @pl.loop(0, pairs)
    def _(pair):
        for step in range(tiles):
            rows = slice(step * tile, (step + 1) * tile)
            query = qkv_ref[pair, rows, :] * SCALE
            keys_here = qkv_ref[pairs + pair, rows, :]
            values_here = qkv_ref[2 * pairs + pair, rows, :]
            outs = []
            for half in range(2):
                mine = pick(masks[half], query)
                here = jnp.where(below, nt(mine, keys_here), masked_score)
                peak = jnp.max(here, axis=-1, keepdims=True)
                if step:
                    past = nt(mine, qkv_ref[pairs + pair, : step * tile, :])
                    peak = jnp.maximum(peak, jnp.max(past, axis=-1, keepdims=True))
                    past = jnp.exp(past - peak)
                here = jnp.exp(here - peak)
                total = jnp.sum(here, axis=-1, keepdims=True)
                out = mm(here.astype(bf16), values_here)
                if step:
                    total = total + jnp.sum(past, axis=-1, keepdims=True)
                    out = out + mm(past.astype(bf16), qkv_ref[2 * pairs + pair, : step * tile, :])
                outs.append(out / total)
                lse_ref[pair, rows, half : half + 1] = peak + jnp.log(total)
            att_ref[rows, pl.ds(pl.multiple_of(pair * LANES, LANES), LANES)] = jnp.where(
                masks[0], outs[0], outs[1]
            ).astype(bf16)


def self_forward(pairs, direct, x, norms, perm, w):
    length, dim = x.shape
    vmem = pl.BlockSpec(memory_space=pltpu.VMEM)
    return pl.pallas_call(
        partial(self_forward_kernel, pairs, direct),
        in_specs=[vmem] * 3 + [pl.BlockSpec(memory_space=pl.ANY)],
        scratch_shapes=[
            pltpu.VMEM((dim, 3 * pairs * LANES), bf16),
            pltpu.SemaphoreType.DMA((3,)),
        ],
        out_shape=(
            jax.ShapeDtypeStruct((length, dim), bf16),
            jax.ShapeDtypeStruct((3 * pairs, length, LANES), bf16),
            jax.ShapeDtypeStruct((length, pairs * LANES), bf16),
            jax.ShapeDtypeStruct((pairs, length, 2), f32),
        ),
        compiler_params=params(),
        name="self_forward",
    )(x, norms, perm, w)


def pair_backward(pair, pairs, qkv_ref, att_ref, gatt_ref, lse_ref, grad_ref, acc_ref, between):
    length = att_ref.shape[0]
    width = pairs * LANES
    tile = 256
    above = lax.broadcasted_iota(jnp.int32, (tile, tile), 0) <= lax.broadcasted_iota(
        jnp.int32, (tile, tile), 1
    )
    masks = [head_mask(tile, 0), head_mask(tile, 1)]
    lanes = pl.ds(pl.multiple_of(pair * LANES, LANES), LANES)
    for step in range(length // tile):
        rows = slice(step * tile, (step + 1) * tile)
        query = qkv_ref[pair, rows, :] * SCALE
        grad_out = gatt_ref[rows, lanes]
        product = grad_out.astype(f32) * att_ref[rows, lanes].astype(f32)
        queries = [pick(masks[half], query) for half in range(2)]
        grads = [pick(masks[half], grad_out) for half in range(2)]
        deltas = [jnp.sum(pick(masks[half], product).T, axis=0, keepdims=True) for half in range(2)]
        grad_query = [None, None]
        for other in range(step + 1):
            cols = slice(other * tile, (other + 1) * tile)
            keys = qkv_ref[pairs + pair, cols, :]
            values = qkv_ref[2 * pairs + pair, cols, :]
            key_part = value_part = None
            for half in range(2):
                scores = nt(keys, queries[half])
                if other == step:
                    scores = jnp.where(above, scores, masked_score)
                probs = jnp.exp(scores - lse_ref[pair, half : half + 1, rows])
                grad_scores = (probs * (nt(values, grads[half]) - deltas[half])).astype(bf16)
                query_term = tn(grad_scores, keys)
                grad_query[half] = (
                    query_term if grad_query[half] is None else grad_query[half] + query_term
                )
                key_term = mm(grad_scores, queries[half])
                value_term = mm(probs.astype(bf16), grads[half])
                key_part = key_term if key_part is None else key_part + key_term
                value_part = value_term if value_part is None else value_part + value_term
            if other == step:
                acc_ref[0, cols, :] = key_part
                acc_ref[1, cols, :] = value_part
            else:
                acc_ref[0, cols, :] += key_part
                acc_ref[1, cols, :] += value_part
        grad_ref[rows, lanes] = (jnp.where(masks[0], grad_query[0], grad_query[1]) * SCALE).astype(
            bf16
        )
        between()
    for part in range(2):
        lanes_to = pl.ds(pl.multiple_of((part + 1) * width + pair * LANES, LANES), LANES)
        grad_ref[:, lanes_to] = acc_ref[part].astype(bf16)


def self_backward_kernel(
    pairs,
    direct,
    qkv_ref,
    att_ref,
    gatt_ref,
    lse_ref,
    hid_ref,
    wts_ref,
    gw_ref,
    ghid_ref,
    grad_ref,
    acc_ref,
    w_ref,
    sems,
):
    length = att_ref.shape[0]
    dim = hid_ref.shape[1]
    width = pairs * LANES
    copies = weight_copies(pairs, direct, dim, wts_ref, w_ref, sems)
    for copy in copies:
        copy.start()
    attention = (qkv_ref, att_ref, gatt_ref, lse_ref, grad_ref, acc_ref)

    @pl.loop(0, pairs)
    def _(pair):
        pair_backward(pair, pairs, *attention, lambda: None)

    for copy in copies:
        copy.wait()
    hidden_t = hid_ref[...].T
    for part in range(3):
        cols = slice(part * width, (part + 1) * width)
        gw_ref[:, cols] = mm(hidden_t, grad_ref[:, cols]).astype(bf16)
    for begin in range(0, length, 256):
        rows = slice(begin, begin + 256)
        ghid_ref[rows, :] = nt(grad_ref[rows, :], w_ref[...]).astype(bf16)


def self_backward(pairs, direct, qkv, att, gatt, lse, hid, w):
    length, dim = hid.shape
    width = pairs * LANES
    vmem = pl.BlockSpec(memory_space=pltpu.VMEM)
    return pl.pallas_call(
        partial(self_backward_kernel, pairs, direct),
        out_shape=(
            jax.ShapeDtypeStruct((dim, 3 * width), bf16),
            jax.ShapeDtypeStruct((length, dim), bf16),
        ),
        in_specs=[vmem] * 5 + [pl.BlockSpec(memory_space=pl.ANY)],
        scratch_shapes=[
            pltpu.VMEM((length, 3 * width), bf16),
            pltpu.VMEM((2, length, LANES), f32),
            pltpu.VMEM((dim, 3 * width), bf16),
            pltpu.SemaphoreType.DMA((3,)),
        ],
        compiler_params=params(),
        name="self_backward",
    )(qkv, att, gatt, lse, hid, w)


def finish_kernel(
    pairs,
    lines,
    qkv_ref,
    att_ref,
    gatt_ref,
    lse_ref,
    hid_ref,
    x_ref,
    gfirst_ref,
    norms_ref,
    perm_ref,
    others_ref,
    wts_ref,
    _,
    all_ref,
    gin_ref,
    shard_ref,
    sums_ref,
    grad_ref,
    acc_ref,
    gw_ref,
    w_ref,
    sems,
    ghid_ref,
    gsib_ref,
    parts_ref,
    small_ref,
    plane_ref,
    plane_sum_ref,
    line_ref,
    gsib_sems,
    part_sems,
    plane_sems,
    line_sems,
    send_sems,
    *rest,
):
    length, dim = hid_ref.shape
    width = pairs * LANES
    tokens = length // 8
    place = Place(lines)
    me, core = place.me, place.core
    place.meet()
    send = Sender(place, send_sems)
    sums = RowReduce(place, send, all_ref, shard_ref, 0, rest)
    sums.begin((1,))
    copies = weight_copies(pairs, True, dim, wts_ref, w_ref, sems)
    for copy in copies:
        copy.start()

    share_count = dim // width
    share = lax.rem(me, share_count)
    gw_ref[3] = jnp.zeros_like(gw_ref[3])
    outs = []
    for part in range(3):
        for other in range(1, share_count):
            first = part * dim + lax.rem(share + other, share_count) * width
            outs.append(
                pltpu.make_async_copy(
                    gw_ref.at[3],
                    all_ref.at[:, pl.ds(pl.multiple_of(first, LANES), width)],
                    sems.at[6 + part * (share_count - 1) + other - 1],
                )
            )
            outs[-1].start()
    shard_ref[...] = jnp.zeros_like(shard_ref)

    attention = (qkv_ref, att_ref, gatt_ref, lse_ref, grad_ref, acc_ref)
    weave = Weave(sums.steps(1))
    for pair in range(pairs):
        pair_backward(pair, pairs, *attention, lambda: weave.some(2))

    hidden_t = hid_ref[...].T
    first, step = columns_of(pairs, True, dim)
    for part in range(3):
        gw_ref[part] = mm(hidden_t, grad_ref[:, part * width : (part + 1) * width]).astype(bf16)
        outs.append(
            pltpu.make_async_copy(
                gw_ref.at[part],
                all_ref.at[:, pl.ds(pl.multiple_of(first + part * step, LANES), width)],
                sems.at[3 + part],
            )
        )
        outs[-1].start()
    for copy in outs + copies:
        copy.wait()
    sums.begin((0,))
    weave.rest()
    weave = Weave(sums.steps(0))

    def token_rows(device):
        return pl.ds(pl.multiple_of(device * tokens, tokens), tokens)

    for begin in range(0, length, 256):
        rows = slice(begin, begin + 256)
        ghid_ref[rows, :] = nt(grad_ref[rows, :], w_ref[...]).astype(bf16)
    chips = (place.xn // 2, place.yn // 2, place.dg // 2, place.chip)
    for chip in chips:
        theirs = chip * 2 + 1 - core
        send.start(
            None, ghid_ref.at[token_rows(theirs)], gsib_ref.at[chip], gsib_sems.at[chip], seq=place.sib
        )
    for chip in chips:
        send.arrived(None, gsib_ref.at[chip], gsib_sems.at[chip])
        rows = token_rows(chip * 2 + core)
        total = (ghid_ref[rows, :].astype(f32) + gsib_ref[chip].astype(f32)).astype(bf16)
        if chip is place.chip:
            parts_ref[chip] = total
        else:
            ghid_ref[rows, :] = total
            send.start(
                None,
                ghid_ref.at[rows],
                parts_ref.at[place.chip],
                part_sems.at[place.chip],
                seq=chip * 2 + core,
            )
    weave.some(6)
    for chip in chips[:3]:
        send.arrived(None, parts_ref.at[chip], part_sems.at[chip])
    gain_sum = shift_sum = None
    for chip in range(4):
        rows = slice(chip * tokens, (chip + 1) * tokens)
        upstream = nt(parts_ref[chip], perm_ref[...])
        normed, recip = centre_scale(x_ref[rows, :].astype(f32))
        back, gain, shift = norm_back(upstream, normed, recip, norms_ref[0:1, :])
        gin_ref[rows, :] = gfirst_ref[rows, :] + back
        gain_sum = gain if gain_sum is None else gain_sum + gain
        shift_sum = shift if shift_sum is None else shift_sum + shift
    small_ref[...] = others_ref[...]
    small_ref[0:1, :] = gain_sum
    small_ref[1:2, :] = shift_sum
    for other in place.plane():
        send.start(None, small_ref, plane_ref.at[me], plane_sems.at[me], seq=other)
    plane_ref[me] = small_ref[...]
    weave.some(8)
    for other in place.plane():
        send.arrived(None, plane_ref.at[other], plane_sems.at[other])
    total = plane_ref[0]
    for other in range(1, 8):
        total = total + plane_ref[other]
    plane_sum_ref[...] = total
    line_ref[place.z] = total
    for other in place.line():
        send.start(None, plane_sum_ref, line_ref.at[place.z], line_sems.at[place.z], z=other)
    weave.rest()
    for other in place.line():
        send.arrived(None, line_ref.at[other], line_sems.at[other])
    total = line_ref[0]
    for other in range(1, lines):
        total = total + line_ref[other]
    sums_ref[...] = total
    send.finish()


def finish(pairs, lines, qkv, att, gatt, lse, hid, x, gfirst, norms, perm, others, weights, grads):
    length, dim = hid.shape
    width = pairs * LANES
    count = x.shape[0]
    tokens = length // 8
    shard = (grads.shape[0] // lines, grads.shape[1] // 8)
    any_space = pl.BlockSpec(memory_space=pl.ANY)
    vmem = pl.BlockSpec(memory_space=pltpu.VMEM)
    dma = pltpu.SemaphoreType.DMA
    return pl.pallas_call(
        partial(finish_kernel, pairs, lines),
        out_shape=(
            jax.ShapeDtypeStruct(grads.shape, bf16),
            jax.ShapeDtypeStruct((count, dim), f32),
            jax.ShapeDtypeStruct(shard, f32),
            jax.ShapeDtypeStruct((8, dim), f32),
        ),
        in_specs=[vmem] * 10 + [any_space] * 2,
        out_specs=(any_space, vmem, vmem, vmem),
        scratch_shapes=[
            pltpu.VMEM((length, 3 * width), bf16),
            pltpu.VMEM((2, length, LANES), f32),
            pltpu.VMEM((4, dim, width), bf16),
            pltpu.VMEM((dim, 3 * width), bf16),
            dma((6 + 3 * (dim // width),)),
            pltpu.VMEM((length, dim), bf16),
            pltpu.VMEM((4, tokens, dim), bf16),
            pltpu.VMEM((4, tokens, dim), bf16),
            pltpu.VMEM((8, dim), f32),
            pltpu.VMEM((8, 8, dim), f32),
            pltpu.VMEM((8, dim), f32),
            pltpu.VMEM((lines, 8, dim), f32),
            dma((4,)),
            dma((4,)),
            dma((8,)),
            dma((lines,)),
            dma((16 * lines + 24,)),
        ]
        + RowReduce.scratch(lines, *shard),
        input_output_aliases={11: 0},
        compiler_params=pltpu.CompilerParams(
            vmem_limit_bytes=VMEM_BYTES, collective_id=3, has_side_effects=True
        ),
        name="finish",
    )(qkv, att, gatt, lse, hid, x, gfirst, norms, perm, others, weights, grads)


def spread_heads(block, rows, group):
    lane = lax.broadcasted_iota(jnp.int32, block.shape, 1) // HEAD
    return jnp.concatenate([pick(lane == head, block) for head in range(group)], axis=0)


def gather_heads(stacked, rows, group):
    lane = lax.broadcasted_iota(jnp.int32, (rows, stacked.shape[1]), 1) // HEAD
    out = None
    for head in range(group):
        part = pick(lane == head, stacked[head * rows : (head + 1) * rows])
        out = part if out is None else out + part
    return out


def live_keys(presence_ref, span, shape, axis, neighbours, each):
    index = lax.broadcasted_iota(jnp.int32, shape, axis) // each
    live = jnp.zeros(shape, f32)
    anyone = None
    for which in range(neighbours):
        here = presence_ref[span * neighbours + which]
        there = jnp.where(here > 0, 1.0, 0.0).astype(f32)
        live = jnp.where(index == which, there, live)
        anyone = here if anyone is None else jnp.maximum(anyone, here)
    return live, anyone.astype(f32)


def cross_forward_kernel(
    spans,
    neighbours,
    presence_ref,
    att_ref,
    x_ref,
    norms_ref,
    perm_ref,
    perm_att_ref,
    near_ref,
    w_out_ref,
    w_cq_ref,
    w_ck_ref,
    w_cv_ref,
    w_co_ref,
    att_p_ref,
    first_ref,
    hid_p_ref,
    cross_q_ref,
    near_p_ref,
    near_kv_ref,
    co_p_ref,
    second_ref,
    cross_ref,
):
    count, dim = x_ref.shape
    rows_near = near_ref.shape[0]
    span_len = count // spans
    near = rows_near // spans
    group = 256 // HEAD
    tile = 512

    att_p_ref[...] = mm(att_ref[...], perm_att_ref[...]).astype(bf16)
    first_ref[...] = x_ref[...].astype(f32) + mm(att_p_ref[...], w_out_ref[...])

    normed, _ = centre_scale(first_ref[...])
    hidden = (normed * norms_ref[2:3, :] + norms_ref[3:4, :]).astype(bf16)
    hid_p_ref[...] = mm(hidden, perm_ref[...]).astype(bf16)
    cross_q_ref[...] = mm(hid_p_ref[...], w_cq_ref[...]).astype(bf16)

    @pl.loop(0, rows_near // tile)
    def _(step):
        rows = rows_of(step, tile)
        near_p_ref[rows, :] = mm(near_ref[rows, :], perm_ref[...]).astype(bf16)
        near_kv_ref[rows, :dim] = mm(near_p_ref[rows, :], w_ck_ref[...]).astype(bf16)
        near_kv_ref[rows, dim:] = mm(near_p_ref[rows, :], w_cv_ref[...]).astype(bf16)

    @pl.loop(0, spans)
    def _(span):
        rows = rows_of(span, span_len)
        keys = rows_of(span, near)
        live, anyone = live_keys(presence_ref, span, (1, near), 1, neighbours, near // neighbours)
        for begin in range(0, dim, group * HEAD):
            lanes = slice(begin, begin + group * HEAD)
            lanes_v = slice(dim + begin, dim + begin + group * HEAD)
            query = spread_heads(cross_q_ref[rows, lanes] * SCALE, span_len, group)
            scores = jnp.where(live > 0, nt(query, near_kv_ref[keys, lanes]), masked_score)
            peak = jnp.max(scores, axis=-1, keepdims=True)
            expon = jnp.exp(scores - peak) * live
            total = jnp.sum(expon, axis=-1, keepdims=True) + 1.0 - anyone
            out = mm(expon.astype(bf16), near_kv_ref[keys, lanes_v]) / total
            cross_ref[rows, lanes] = gather_heads(out, span_len, group).astype(bf16)

    co_p_ref[...] = mm(cross_ref[...], perm_ref[...]).astype(bf16)
    second_ref[...] = first_ref[...] + mm(co_p_ref[...], w_co_ref[...])


def column_block(rows, width, index):
    return pl.BlockSpec((rows, width), lambda *_: (0, index), pipeline_mode=pl.Buffered(1))


def whole(array):
    return pl.BlockSpec(array.shape, lambda *_: (0,) * array.ndim, pipeline_mode=pl.Buffered(1))


def whole_shape(shape):
    return pl.BlockSpec(shape, lambda *_: (0,) * len(shape), pipeline_mode=pl.Buffered(1))


def cross_forward(spans, neighbours, presence, att, x, norms, perm, perm_att, near, weights):
    count, dim = x.shape
    rows_near = near.shape[0]
    out_shape = (
        jax.ShapeDtypeStruct((count, dim), bf16),
        jax.ShapeDtypeStruct((count, dim), f32),
        jax.ShapeDtypeStruct((count, dim), bf16),
        jax.ShapeDtypeStruct((count, dim), bf16),
        jax.ShapeDtypeStruct((rows_near, dim), bf16),
        jax.ShapeDtypeStruct((rows_near, 2 * dim), bf16),
        jax.ShapeDtypeStruct((count, dim), bf16),
        jax.ShapeDtypeStruct((count, dim), f32),
    )
    operands = (att, x, norms, perm, perm_att, near)
    return pl.pallas_call(
        partial(cross_forward_kernel, spans, neighbours),
        out_shape=out_shape,
        grid=(1,),
        in_specs=[pl.BlockSpec(memory_space=pltpu.SMEM)]
        + [whole(op) for op in operands]
        + [column_block(dim, dim, index) for index in (3, 4, 5, 6, 7)],
        out_specs=tuple(whole_shape(shape.shape) for shape in out_shape),
        scratch_shapes=[pltpu.VMEM((count, dim), bf16)],
        compiler_params=params(),
        name="cross_forward",
    )(presence, *operands, *([weights] * 5))


def feed_kernel(
    second_ref,
    cot_ref,
    norms_ref,
    perm_ref,
    w_up_ref,
    w_down_ref,
    out_ref,
    gsecond_ref,
    all_ref,
    gnorm_ref,
    hid_p_ref,
    hid_t_ref,
    cot_p_ref,
    cot_t_ref,
    result_ref,
    back_ref,
    gup_ref,
    gdown_ref,
    sems,
):
    step = pl.program_id(0)
    last = pl.num_programs(0) - 1
    slot = lax.rem(step, 2)
    dim, tile = w_up_ref.shape

    def copies(step, slot):
        up = pl.multiple_of(8 * dim + step * tile, tile)
        down = pl.multiple_of(8 * dim + (last + 1 + step) * tile, tile)
        return (
            pltpu.make_async_copy(gup_ref.at[slot], all_ref.at[:, pl.ds(up, tile)], sems.at[0, slot]),
            pltpu.make_async_copy(
                gdown_ref.at[slot], all_ref.at[:, pl.ds(down, tile)], sems.at[1, slot]
            ),
        )

    @pl.when(step >= 2)
    def _():
        for copy in copies(step - 2, slot):
            copy.wait()

    @pl.when(step == 0)
    def _():
        normed, _ = centre_scale(second_ref[...])
        hidden = (normed * norms_ref[4:5, :] + norms_ref[5:6, :]).astype(bf16)
        hid_p_ref[...] = mm(hidden, perm_ref[...]).astype(bf16)
        hid_t_ref[...] = hid_p_ref[...].T
        cot_p_ref[...] = mm(cot_ref[...], perm_ref[...]).astype(bf16)
        cot_t_ref[...] = cot_p_ref[...].T
        result_ref[...] = jnp.zeros_like(result_ref)
        back_ref[...] = jnp.zeros_like(back_ref)

    upward = mm(hid_p_ref[...], w_up_ref[...])
    active, slope = gelu_parts(upward)
    active = active.astype(bf16)
    result_ref[...] += nt(active, w_down_ref[...])
    gdown_ref[slot] = mm(cot_t_ref[...], active).astype(bf16)
    grad_up = (mm(cot_p_ref[...], w_down_ref[...]) * slope).astype(bf16)
    gup_ref[slot] = mm(hid_t_ref[...], grad_up).astype(bf16)
    for copy in copies(step, slot):
        copy.start()
    back_ref[...] += nt(grad_up, w_up_ref[...])

    @pl.when(step == last)
    def _():
        out_ref[...] = (
            second_ref[...] + nt(result_ref[...].astype(bf16), perm_ref[...])
        ).astype(bf16)
        upstream = nt(back_ref[...].astype(bf16), perm_ref[...])
        normed, recip = centre_scale(second_ref[...])
        back, gain, shift = norm_back(upstream, normed, recip, norms_ref[4:5, :])
        gsecond_ref[...] = cot_ref[...].astype(f32) + back
        gnorm_ref[0:1, :] = gain
        gnorm_ref[1:2, :] = shift
        for which in (step - 1, step):
            for copy in copies(which, lax.rem(which, 2)):
                copy.wait()


def feed(second, cot, norms, perm, weights):
    count, dim = second.shape
    ffw = (weights.shape[1] - 8 * dim) // 2
    tile = 512
    first_up = 8 * dim // tile
    first_down = (8 * dim + ffw) // tile
    out_shape = (
        jax.ShapeDtypeStruct((count, dim), bf16),
        jax.ShapeDtypeStruct((count, dim), f32),
        jax.ShapeDtypeStruct(weights.shape, bf16),
        jax.ShapeDtypeStruct((2, dim), f32),
    )
    operands = (second, cot, norms, perm)
    return pl.pallas_call(
        feed_kernel,
        out_shape=out_shape,
        grid=(ffw // tile,),
        in_specs=[whole(op) for op in operands]
        + [
            pl.BlockSpec((dim, tile), lambda i: (0, first_up + i)),
            pl.BlockSpec((dim, tile), lambda i: (0, first_down + i)),
        ],
        out_specs=(
            whole_shape((count, dim)),
            whole_shape((count, dim)),
            pl.BlockSpec(memory_space=pl.ANY),
            whole_shape((2, dim)),
        ),
        scratch_shapes=[
            pltpu.VMEM((count, dim), bf16),
            pltpu.VMEM((dim, count), bf16),
            pltpu.VMEM((count, dim), bf16),
            pltpu.VMEM((dim, count), bf16),
            pltpu.VMEM((count, dim), f32),
            pltpu.VMEM((count, dim), f32),
            pltpu.VMEM((2, dim, tile), bf16),
            pltpu.VMEM((2, dim, tile), bf16),
            pltpu.SemaphoreType.DMA((2, 2)),
        ],
        compiler_params=params(),
        name="feed",
    )(*operands, weights, weights)


def cross_backward_kernel(
    spans,
    neighbours,
    lines,
    presence_ref,
    gsecond_ref,
    first_ref,
    norms_ref,
    perm_ref,
    perm_att_ref,
    att_p_ref,
    hid_p_ref,
    cross_q_ref,
    near_p_ref,
    near_kv_ref,
    co_p_ref,
    w_out_ref,
    w_cq_ref,
    w_co_ref,
    _,
    gfirst_ref,
    gatt_ref,
    all_ref,
    gnorm_ref,
    *rest,
):
    count, dim = first_ref.shape
    rows_near = near_p_ref.shape[0]
    span_len = count // spans
    near = rows_near // spans
    group = 256 // HEAD
    outs = []
    if lines:
        shard_ref, gco_ref, gcq_ref, gnear_ref, gw_ref, sems = rest[:6]
        gatt_tok_ref, row_sems, send_sems = rest[6:9]
        place = Place(lines)
        place.meet()
        send = Sender(place, send_sems)
        sums = RowReduce(place, send, all_ref, shard_ref, 1, rest[9:])
        sums.begin((1 - place.x, place.x))
        shard_ref[...] = jnp.zeros_like(shard_ref)
        weave = Weave(sums.steps())
    else:
        gco_ref, gcq_ref, gnear_ref, gw_ref, sems = rest
        weave = Weave([])

    def keep(index, value):
        slot = len(outs) % 3
        if len(outs) >= 3:
            outs[-3].wait()
        gw_ref[slot] = value.astype(bf16)
        outs.append(
            pltpu.make_async_copy(
                gw_ref.at[slot],
                all_ref.at[:, pl.ds((3 + index) * dim, dim)],
                sems.at[index],
            )
        )
        outs[-1].start()

    upper = gsecond_ref[...].astype(bf16)
    gco_ref[...] = nt(nt(upper, w_co_ref[...]).astype(bf16), perm_ref[...]).astype(bf16)

    def one_span(span):
        rows = rows_of(span, span_len)
        keys = rows_of(span, near)
        live, anyone = live_keys(presence_ref, span, (near, 1), 0, neighbours, near // neighbours)
        for begin in range(0, dim, group * HEAD):
            lanes = slice(begin, begin + group * HEAD)
            lanes_v = slice(dim + begin, dim + begin + group * HEAD)
            query = spread_heads(cross_q_ref[rows, lanes] * SCALE, span_len, group)
            grad_out = spread_heads(gco_ref[rows, lanes], span_len, group)
            key = near_kv_ref[keys, lanes]
            scores = jnp.where(live > 0, nt(key, query), masked_score)
            peak = jnp.max(scores, axis=0, keepdims=True)
            expon = jnp.exp(scores - peak) * live
            total = jnp.sum(expon, axis=0, keepdims=True) + 1.0 - anyone
            probs = expon * (1.0 / total)
            grad_probs = nt(near_kv_ref[keys, lanes_v], grad_out)
            inner = jnp.sum(probs * grad_probs, axis=0, keepdims=True)
            grad_scores = (probs * (grad_probs - inner)).astype(bf16)
            gcq_ref[rows, lanes] = (
                gather_heads(tn(grad_scores, key), span_len, group) * SCALE
            ).astype(bf16)
            gnear_ref[keys, lanes] = mm(grad_scores, query).astype(bf16)
            gnear_ref[keys, lanes_v] = mm(probs.astype(bf16), grad_out).astype(bf16)

    pieces = 4 if lines and spans % 4 == 0 else 1
    for piece in range(pieces):
        size = spans // pieces
        pl.loop(piece * size, (piece + 1) * size)(one_span)
        weave.some(5)

    upstream = nt(nt(gcq_ref[...], w_cq_ref[...]).astype(bf16), perm_ref[...])
    normed, recip = centre_scale(first_ref[...])
    back, gain, shift = norm_back(upstream, normed, recip, norms_ref[2:3, :])
    gnorm_ref[0:1, :] = gain
    gnorm_ref[1:2, :] = shift
    gfirst_ref[...] = gsecond_ref[...] + back
    lower = gfirst_ref[...].astype(bf16)
    gatt = nt(nt(lower, w_out_ref[...]).astype(bf16), perm_att_ref[...]).astype(bf16)
    if lines:
        width = gatt_ref.shape[1]
        tokens = gatt_ref.shape[0] // 8
        shares = gatt.shape[1] // width
        gatt_tok_ref[...] = gatt

        def block(device):
            return gatt_tok_ref.at[
                pl.ds(pl.multiple_of(device // shares * tokens, tokens), tokens),
                pl.ds(pl.multiple_of(device % shares * width, width), width),
            ]

        def landing(device):
            return gatt_ref.at[pl.ds(pl.multiple_of(device * tokens, tokens), tokens)]

        for other in place.plane():
            send.start(None, block(other), landing(place.me), row_sems.at[place.me], seq=other)
        own = pltpu.make_async_copy(block(place.me), landing(place.me), row_sems.at[place.me])
        own.start()
    else:
        gatt_ref[...] = gatt
    weave.some(3)
    keep(4, mm(co_p_ref[...].T, upper))
    weave.some(3)
    near_t = near_p_ref[...].T
    for part in range(2):
        keep(2 + part, mm(near_t, gnear_ref[:, part * dim : (part + 1) * dim]))
        weave.some(4)
    keep(1, mm(hid_p_ref[...].T, gcq_ref[...]))
    keep(0, mm(att_p_ref[...].T, lower))
    weave.rest()
    if lines:
        for other in place.plane():
            send.arrived(None, landing(other), row_sems.at[other])
        own.wait()
        send.finish()
    for copy in outs[-3:]:
        copy.wait()


def cross_backward(
    spans,
    neighbours,
    lines,
    presence,
    gsecond,
    first,
    norms,
    perm,
    perm_att,
    att_p,
    hid_p,
    cross_q,
    near_p,
    near_kv,
    co_p,
    weights,
    grads,
):
    count, dim = first.shape
    rows_near = near_p.shape[0]
    all_rows, all_cols = grads.shape
    gatt_shape = (count, perm_att.shape[0])
    out_shape = [
        jax.ShapeDtypeStruct((count, dim), f32),
        jax.ShapeDtypeStruct(gatt_shape, bf16),
        jax.ShapeDtypeStruct(grads.shape, bf16),
        jax.ShapeDtypeStruct((2, dim), f32),
    ]
    scratch = [
        pltpu.VMEM((count, dim), bf16),
        pltpu.VMEM((count, dim), bf16),
        pltpu.VMEM((rows_near, 2 * dim), bf16),
        pltpu.VMEM((3, dim, dim), bf16),
        pltpu.SemaphoreType.DMA((5,)),
    ]
    compiler_params = params()
    if lines:
        shard = (all_rows // lines, all_cols // 8)
        out_shape[1] = jax.ShapeDtypeStruct((2 * count, gatt_shape[1] // 2), bf16)
        out_shape.append(jax.ShapeDtypeStruct(shard, f32))
        scratch += [
            pltpu.VMEM(gatt_shape, bf16),
            pltpu.SemaphoreType.DMA((8,)),
            pltpu.SemaphoreType.DMA((16 * lines + 8,)),
        ] + RowReduce.scratch(lines, *shard)
        compiler_params = pltpu.CompilerParams(
            vmem_limit_bytes=VMEM_BYTES, collective_id=2, has_side_effects=True
        )
    operands = (
        gsecond,
        first,
        norms,
        perm,
        perm_att,
        att_p,
        hid_p,
        cross_q,
        near_p,
        near_kv,
        co_p,
    )
    return pl.pallas_call(
        partial(cross_backward_kernel, spans, neighbours, lines),
        out_shape=out_shape,
        grid=(1,),
        in_specs=[pl.BlockSpec(memory_space=pltpu.SMEM)]
        + [whole(op) for op in operands]
        + [column_block(dim, dim, index) for index in (3, 4, 7)]
        + [pl.BlockSpec(memory_space=pl.ANY)],
        out_specs=tuple(
            pl.BlockSpec(memory_space=pl.ANY) if index == 2 else whole_shape(shape.shape)
            for index, shape in enumerate(out_shape)
        ),
        scratch_shapes=scratch,
        input_output_aliases={len(operands) + 4: 2},
        compiler_params=compiler_params,
        name="cross_backward",
    )(presence, *operands, *([weights] * 3), grads)


def last_norm_kernel(parts_ref, x_ref, gfirst_ref, norms_ref, perm_ref, out_ref, gnorm_ref):
    total = parts_ref[0].astype(f32)
    for part in range(1, parts_ref.shape[0]):
        total = total + parts_ref[part].astype(f32)
    upstream = nt(total.astype(bf16), perm_ref[...])
    normed, recip = centre_scale(x_ref[...].astype(f32))
    back, gain, shift = norm_back(upstream, normed, recip, norms_ref[0:1, :])
    out_ref[...] = gfirst_ref[...] + back
    gnorm_ref[0:1, :] = gain
    gnorm_ref[1:2, :] = shift


def last_norm(parts, x, gfirst, norms, perm):
    count, dim = x.shape
    return pl.pallas_call(
        last_norm_kernel,
        out_shape=(
            jax.ShapeDtypeStruct((count, dim), f32),
            jax.ShapeDtypeStruct((2, dim), f32),
        ),
        compiler_params=params(),
        name="last_norm",
    )(parts, x, gfirst, norms, perm)


def gather_kernel(
    lines,
    w_ref,
    small_ref,
    x_ref,
    wts_ref,
    norms_ref,
    rows_ref,
    own_ref,
    send_sems,
    z_sems,
    x_sems,
    y_sems,
    a_sems,
    b_sems,
    sib_sems,
    norm_sems,
    row_sems,
    local_sems,
):
    place = Place(lines)
    z, me = place.z, place.me
    unit_rows, unit_cols = own_ref.shape
    half = unit_rows // 2
    tokens = x_ref.shape[1]
    own_ref[...] = w_ref[...].astype(bf16)
    place.meet()
    send = Sender(place, send_sems)

    unit = partial(unit_of, wts_ref, lines)

    keep = pltpu.make_async_copy(own_ref, unit(z, me), local_sems.at[0])
    keep.start()

    events = place.events()

    def obtain(index):
        condition, line, far, side = events[index]
        mine = unit(line, me)
        src = own_ref if far == 0 else mine
        if far:
            send.arrived(condition, mine, z_sems.at[line])
        if side >= 0:
            send.start(both(condition, z > 0), src, mine, z_sems.at[line], z=z - 1)
        if side <= 0:
            send.start(both(condition, z < lines - 1), src, mine, z_sems.at[line], z=z + 1)
        send.start(condition, src, mine, x_sems.at[line], seq=place.xn)
        send.start(condition, src, mine, y_sems.at[line], seq=place.yn)
        send.start(condition, src, mine, sib_sems.at[0, line], seq=place.sib)

    def pass_on(index):
        condition, line, _, _ = events[index]
        from_x, from_y = unit(line, place.xn), unit(line, place.yn)
        send.arrived(condition, from_x, x_sems.at[line])
        part = unit(line, place.xn, half, half)
        send.start(condition, part, part, b_sems.at[line], seq=place.yn)
        send.start(condition, from_x, from_x, sib_sems.at[1, line], seq=place.sib)
        send.arrived(condition, from_y, y_sems.at[line])
        part = unit(line, place.yn, 0, half)
        send.start(condition, part, part, a_sems.at[line], seq=place.xn)
        send.start(condition, from_y, from_y, sib_sems.at[2, line], seq=place.sib)

    def corner(index):
        condition, line, _, _ = events[index]
        part = unit(line, place.dg, 0, half)
        send.arrived(condition, part, a_sems.at[line])
        send.start(condition, part, part, sib_sems.at[3, line], seq=place.sib)
        part = unit(line, place.dg, half, half)
        send.arrived(condition, part, b_sems.at[line])
        send.start(condition, part, part, sib_sems.at[4, line], seq=place.sib)

    def row_block(seq):
        return rows_ref.at[pl.ds(pl.multiple_of(seq * tokens, tokens), tokens)]

    obtain(0)
    own_rows = pltpu.make_async_copy(x_ref.at[place.chip], row_block(me), local_sems.at[1])
    own_rows.start()
    send.start(None, x_ref.at[place.chip], row_block(me), row_sems.at[me], seq=place.sib)
    others = (place.xn, place.yn, place.dg)
    for other in others:
        send.start(None, x_ref.at[other // 2], row_block(me), row_sems.at[me], seq=other)
    for other in place.line():
        send.start(None, small_ref, norms_ref.at[z], norm_sems.at[z], z=other)
    norms_ref[z] = small_ref[...]

    last = len(events)
    order = [obtain, 1, obtain, 2, pass_on, 0]
    far = 3
    while far < last:
        order += [obtain, far, obtain, far + 1, pass_on, far - 2, pass_on, far - 1]
        order += [corner, 0] if far == 3 else [corner, far - 4, corner, far - 3]
        far += 2
    done_pass = far - 2
    order += [pass_on, done_pass, pass_on, done_pass + 1]
    done_corner = max(far - 4, 1)
    for index in range(done_corner, last):
        order += [corner, index]
    for position in range(0, len(order), 2):
        order[position](order[position + 1])
        if position == 4:
            for other in others:
                send.arrived(None, row_block(other), row_sems.at[other])
                send.start(
                    None, row_block(other), row_block(other), row_sems.at[other], seq=place.sib
                )

    for other in others:
        theirs = other + 1 - 2 * place.core
        send.arrived(None, row_block(theirs), row_sems.at[theirs])
    send.arrived(None, row_block(place.sib), row_sems.at[place.sib])
    for other in place.line():
        send.arrived(None, norms_ref.at[other], norm_sems.at[other])
    for line in range(lines):
        for index, first in enumerate((me, place.xn, place.yn)):
            theirs = first + 1 - 2 * place.core
            send.arrived(None, unit(line, theirs), sib_sems.at[index, line])
        theirs = place.dg + 1 - 2 * place.core
        send.arrived(None, unit(line, theirs, 0, half), sib_sems.at[3, line])
        send.arrived(None, unit(line, theirs, half, half), sib_sems.at[4, line])
    own_rows.wait()
    keep.wait()
    send.finish()


def gather(lines, w_shard, small, inputs):
    unit_rows, unit_cols = w_shard.shape
    seqs, tokens, dim = inputs.shape
    any_space = pl.BlockSpec(memory_space=pl.ANY)
    vmem = pl.BlockSpec(memory_space=pltpu.VMEM)
    dma = pltpu.SemaphoreType.DMA
    return pl.pallas_call(
        partial(gather_kernel, lines),
        out_shape=(
            jax.ShapeDtypeStruct((unit_rows * lines, unit_cols * 8), bf16),
            jax.ShapeDtypeStruct((lines,) + small.shape, bf16),
            jax.ShapeDtypeStruct((8 * tokens, dim), bf16),
        ),
        in_specs=[vmem, vmem, any_space],
        out_specs=(any_space, vmem, any_space),
        scratch_shapes=[
            pltpu.VMEM((unit_rows, unit_cols), bf16),
            dma((11 * (2 * lines - 1) + 7 + lines,)),
            dma((lines,)),
            dma((lines,)),
            dma((lines,)),
            dma((lines,)),
            dma((lines,)),
            dma((5, lines)),
            dma((lines,)),
            dma((8,)),
            dma((2,)),
        ],
        compiler_params=pltpu.CompilerParams(
            vmem_limit_bytes=VMEM_BYTES, collective_id=1, has_side_effects=True
        ),
        name="gather_weights",
    )(w_shard, small, inputs)


def adam_update(grad, weight, first, second, average, rate, decay):
    first = beta_first * first + (1.0 - beta_first) * grad
    second = beta_second * second + (1.0 - beta_second) * grad * grad
    stepped = (
        first / (1.0 - beta_first**STEP) / (jnp.sqrt(second / (1.0 - beta_second**STEP)) + adam_eps)
    )
    weight = weight - rate * (stepped + decay * weight)
    average = ema_decay * average + (1.0 - ema_decay) * weight
    return (first, second, weight, average)


def on_device(
    inputs,
    cotangent,
    neighbours,
    presence,
    row_order,
    w_master,
    w_first,
    w_second,
    w_average,
    n_master,
    n_first,
    n_second,
    n_average,
):
    seqs, tokens, dim = inputs.shape
    heads = dim // HEAD
    devices = lax.axis_size("seq")
    count = seqs * tokens
    length = devices * tokens
    me = lax.axis_index("seq")
    shares = devices // seqs
    held = heads // shares
    pairs = (held + 1) // 2
    width = pairs * LANES
    spare = width - held * HEAD
    sequence, share = me // shares, me % shares

    lines = lax.axis_size("dp")
    direct = spare == 0
    planar = devices == 8 and seqs == 4 and direct
    if planar:
        part = n_master.shape[1]
        small = jnp.pad(n_master.astype(bf16), ((0, 16 - 6), (0, -part % LANES)))
        weights, norms, rows = gather(lines, w_master, small, inputs)
        norms = norms[:, :6, :part].transpose(1, 0, 2).reshape(6, dim).astype(f32)
    else:
        weights = lax.all_gather(w_master.astype(bf16), "dp", axis=0, tiled=True)
        weights = lax.all_gather(weights, "seq", axis=1, tiled=True)
        norms = lax.all_gather(n_master.astype(bf16), "dp", axis=1, tiled=True).astype(f32)
        rows = lax.all_to_all(jnp.repeat(inputs, shares, axis=0), "seq", 0, 0)
        rows = rows.reshape(length, dim)

    perm = (jnp.arange(dim)[:, None] == row_order[None, :]).astype(bf16)
    perm_att = jnp.pad(perm.reshape(shares, held * HEAD, dim), ((0, 0), (0, spare), (0, 0)))
    perm_att = perm_att.reshape(shares * width, dim)
    if direct:
        w_qkv = weights
    else:
        w_qkv = weights[:, : 3 * dim].reshape(dim, 3, shares, held * HEAD)
        w_qkv = lax.dynamic_index_in_dim(w_qkv, share, axis=2, keepdims=False)
        w_qkv = jnp.pad(w_qkv, ((0, 0), (0, 0), (0, spare))).reshape(dim, 3 * width)

    x = inputs.reshape(count, dim)
    hid, qkv, att, lse = self_forward(pairs, direct, rows, norms, perm, w_qkv)
    att_tok = (
        lax.all_to_all(att.reshape(devices, tokens, width), "seq", 0, 0)
        .reshape(seqs, shares, tokens, width)
        .transpose(0, 2, 1, 3)
        .reshape(count, shares * width)
    )
    spans = seqs * neighbours.shape[1]
    each = neighbours.shape[2]
    near = neighbours.reshape(-1, dim)
    live = presence.reshape(-1)
    att_p, first, hid_p, cross_q, near_p, near_kv, co_p, second = cross_forward(
        spans, each, live, att_tok, x, norms, perm, perm_att, near, weights
    )
    outputs, gsecond, grads, gnorm_e = feed(
        second, cotangent.reshape(count, dim), norms, perm, weights
    )
    gfirst, gatt_tok, grads, gnorm_c, *late_shard = cross_backward(
        spans,
        each,
        lines if planar else 0,
        live,
        gsecond,
        first,
        norms,
        perm,
        perm_att,
        att_p,
        hid_p,
        cross_q,
        near_p,
        near_kv,
        co_p,
        weights,
        grads,
    )
    if planar:
        others = jnp.concatenate(
            [jnp.zeros((2, dim), f32), gnorm_c, gnorm_e, jnp.zeros((2, dim), f32)], axis=0
        )
        _, grad_inputs, grad_shard, norm_sums = finish(
            pairs,
            lines,
            qkv,
            att,
            gatt_tok,
            lse.transpose(0, 2, 1),
            hid,
            x,
            gfirst,
            norms,
            perm,
            others,
            weights,
            grads,
        )
        grad_shard = grad_shard + late_shard[0]
        part = n_master.shape[1]
        norm_shard = lax.dynamic_slice(norm_sums, (0, lax.axis_index("dp") * part), (6, part))
    else:
        gatt = lax.all_to_all(
            gatt_tok.reshape(seqs, tokens, shares, width)
            .transpose(0, 2, 1, 3)
            .reshape(devices, tokens, width),
            "seq",
            0,
            0,
        ).reshape(length, width)
        gqkv, ghid = self_backward(
            pairs, direct, qkv, att, gatt, lse.transpose(0, 2, 1), hid, w_qkv
        )
        parts = (
            lax.all_to_all(ghid.reshape(devices, tokens, dim), "seq", 0, 0)
            .reshape(seqs, shares, tokens, dim)
            .transpose(1, 0, 2, 3)
            .reshape(shares, count, dim)
        )
        grad_inputs, gnorm_a = last_norm(parts, x, gfirst, norms, perm)
        gqkv = gqkv.reshape(dim, 3, 1, width)[..., : held * HEAD]
        gqkv = jnp.where(jnp.arange(shares)[:, None] == share, gqkv, jnp.zeros_like(gqkv))
        grads = lax.dynamic_update_slice(grads, gqkv.reshape(dim, 3 * dim), (0, 0))
        norm_grads = lax.psum(jnp.concatenate([gnorm_a, gnorm_c, gnorm_e], axis=0), "seq")
        partial_sum = lax.psum_scatter(grads, "seq", scatter_dimension=1, tiled=True)
        grad_shard = lax.psum_scatter(partial_sum, "dp", scatter_dimension=0, tiled=True)
        grad_shard = grad_shard.astype(f32)
        norm_shard = lax.psum_scatter(
            norm_grads.astype(bf16), "dp", scatter_dimension=1, tiled=True
        ).astype(f32)
    w_first_new, w_second_new, w_new, w_average_new = adam_update(
        grad_shard, w_master, w_first, w_second, w_average, learn_rate, weight_decay
    )
    n_first_new, n_second_new, n_new, n_average_new = adam_update(
        norm_shard, n_master, n_first, n_second, n_average, norm_rate, 0.0
    )
    return (
        outputs.reshape(seqs, tokens, dim),
        grad_inputs.reshape(seqs, tokens, dim),
        w_first_new,
        w_second_new,
        w_new,
        w_average_new,
        n_first_new,
        n_second_new,
        n_new,
        n_average_new,
    )


def solution(mesh):
    in_specs = (
        P("dp", "seq", None),
        P("dp", "seq", None),
        P("dp", "seq", None, None, None),
        P("dp", "seq", None),
        P(),
        P("dp", "seq"),
        P("dp", "seq"),
        P("dp", "seq"),
        P("dp", "seq"),
        P(None, "dp"),
        P(None, "dp"),
        P(None, "dp"),
        P(None, "dp"),
    )
    out_specs = (
        P("dp", "seq", None),
        P("dp", "seq", None),
        P("dp", "seq"),
        P("dp", "seq"),
        P("dp", "seq"),
        P("dp", "seq"),
        P(None, "dp"),
        P(None, "dp"),
        P(None, "dp"),
        P(None, "dp"),
    )
    return jax.shard_map(
        on_device, mesh=mesh, in_specs=in_specs, out_specs=out_specs, check_vma=False
    )
```

```python
from functools import partial

import jax
import jax.numpy as jnp
from jax import lax
from jax.experimental import pallas as pl
from jax.experimental.pallas import tpu as pltpu
from jax.sharding import PartitionSpec as P

HEAD = 64
STEP = 5
LANES = 128
SCALE = HEAD ** (-0.5)

beta_first = 0.9
beta_second = 0.95
adam_eps = 1e-08
learn_rate = 0.04
norm_rate = 0.6
weight_decay = 0.1
ema_decay = 0.5
norm_eps = 1e-05
masked_score = -1e30
VMEM_BYTES = 60 * 1024 * 1024
bf16 = jnp.bfloat16
f32 = jnp.float32


def mm(left, right):
    return lax.dot_general(left, right, (((1,), (0,)), ((), ())), preferred_element_type=f32)


def nt(left, right):
    return lax.dot_general(left, right, (((1,), (1,)), ((), ())), preferred_element_type=f32)


def tn(left, right):
    return lax.dot_general(left, right, (((0,), (0,)), ((), ())), preferred_element_type=f32)


def params():
    return pltpu.CompilerParams(vmem_limit_bytes=VMEM_BYTES)


def rows_of(index, size):
    return pl.ds(pl.multiple_of(index * size, size), size)


def centre_scale(values):
    centre = jnp.mean(values, axis=-1, keepdims=True)
    centred = values - centre
    spread = jnp.mean(centred * centred, axis=-1, keepdims=True)
    recip = lax.rsqrt(spread + norm_eps)
    return centred * recip, recip


def norm_back(upstream, normed, recip, gain):
    scaled = upstream * gain
    inner = (
        scaled
        - jnp.mean(scaled, axis=-1, keepdims=True)
        - normed * jnp.mean(scaled * normed, axis=-1, keepdims=True)
    )
    return (
        recip * inner,
        jnp.sum(upstream * normed, axis=0, keepdims=True),
        jnp.sum(upstream, axis=0, keepdims=True),
    )


def gelu_parts(value):
    const = 0.7978845608028654
    square = value * value
    bend = jnp.tanh(const * value * (1.0 + 0.044715 * square))
    half = 0.5 * (1.0 + bend)
    slope = half + 0.5 * value * (1.0 - bend * bend) * (const * (1.0 + 3 * 0.044715 * square))
    return value * half, slope


def head_mask(rows, half):
    lane = lax.broadcasted_iota(jnp.int32, (rows, LANES), 1)
    return (lane < HEAD) if half == 0 else (lane >= HEAD)


def pick(mask, value):
    return jnp.where(mask, value, jnp.zeros_like(value))


MESH = pl.DeviceIdType.MESH


class Place:
    def __init__(self, lines):
        self.lines = lines
        self.z = lax.axis_index("dp")
        self.me = lax.axis_index("seq")
        core, x, y = self.me % 2, (self.me // 2) % 2, self.me // 4
        self.core, self.x, self.y, self.chip = core, x, y, self.me // 2
        self.sib = self.me + 1 - 2 * core
        self.xn = self.me + 2 - 4 * x
        self.yn = self.me + 4 - 8 * y
        self.dg = self.xn + 4 - 8 * y

    def events(self):
        found = [(None, self.z, 0, 0)]
        for far in range(1, self.lines):
            found.append((self.z >= far, self.z - far, far, -1))
            found.append((self.z + far < self.lines, self.z + far, far, 1))
        return found

    def plane(self):
        return [lax.rem(self.me + step, 8) for step in range(1, 8)]

    def line(self):
        return [lax.rem(self.z + step, self.lines) for step in range(1, self.lines)]

    def meet(self):
        barrier = pltpu.get_barrier_semaphore()
        for other in self.plane():
            pl.semaphore_signal(
                barrier, inc=1, device_id={"dp": self.z, "seq": other}, device_id_type=MESH
            )
        for other in self.line():
            pl.semaphore_signal(
                barrier, inc=1, device_id={"dp": other, "seq": self.me}, device_id_type=MESH
            )
        pl.semaphore_wait(barrier, 7 + self.lines - 1)


def when(condition, body):
    if condition is None:
        body()
    else:
        pl.when(condition)(body)


def both(first, second):
    if first is None or second is None:
        return second if first is None else first
    return jnp.logical_and(first, second)


class Sender:
    def __init__(self, place, send_sems):
        self.place, self.sems, self.open = place, send_sems, []

    def start(self, condition, src, dst, recv_sem, z=None, seq=None):
        place = self.place
        target = {"dp": place.z if z is None else z, "seq": place.me if seq is None else seq}
        copy = pltpu.make_async_remote_copy(
            src_ref=src,
            dst_ref=dst,
            send_sem=self.sems.at[len(self.open)],
            recv_sem=recv_sem,
            device_id=target,
            device_id_type=MESH,
        )
        self.open.append((condition, copy))
        when(condition, copy.start)

    def arrived(self, condition, ref, recv_sem):
        copy = pltpu.make_async_remote_copy(
            src_ref=ref,
            dst_ref=ref,
            send_sem=self.sems.at[0],
            recv_sem=recv_sem,
            device_id={"dp": self.place.z, "seq": self.place.sib},
            device_id_type=MESH,
        )
        when(condition, copy.wait_recv)

    def finish(self):
        for condition, copy in self.open:
            when(condition, copy.wait_send)


class Weave:
    def __init__(self, steps):
        self.steps = list(steps)

    def some(self, count):
        for _ in range(min(count, len(self.steps))):
            self.steps.pop(0)()

    def rest(self):
        self.some(len(self.steps))


def unit_of(ref, lines, line, seq, begin=0, size=None):
    rows, cols = ref.shape[0] // lines, ref.shape[1] // 8
    size = rows if size is None else size
    return ref.at[
        pl.ds(pl.multiple_of(line * rows + begin, 16), size),
        pl.ds(pl.multiple_of(seq * cols, cols), cols),
    ]


def weight_copies(pairs, dim, wts_ref, w_ref, sems):
    width = pairs * LANES
    first = lax.rem(lax.axis_index("seq"), dim // width) * width
    return [
        pltpu.make_async_copy(
            wts_ref.at[:, pl.ds(pl.multiple_of(first + part * dim, LANES), width)],
            w_ref.at[:, pl.ds(part * width, width)],
            sems.at[part],
        )
        for part in range(3)
    ]


def pair_forward(pair, pairs, qkv_ref, att_ref, lse_ref, between):
    length = att_ref.shape[0]
    tile = 256
    below = lax.broadcasted_iota(jnp.int32, (tile, tile), 1) <= lax.broadcasted_iota(
        jnp.int32, (tile, tile), 0
    )
    masks = [head_mask(tile, 0), head_mask(tile, 1)]
    lane = lax.broadcasted_iota(jnp.int32, (tile, LANES), 1)
    for step in range(length // tile):
        rows = slice(step * tile, (step + 1) * tile)
        query = qkv_ref[pair, rows, :] * SCALE
        keys_here = qkv_ref[pairs + pair, rows, :]
        values_here = qkv_ref[2 * pairs + pair, rows, :]
        outs, logs = [], []
        for half in range(2):
            mine = pick(masks[half], query)
            here = jnp.where(below, nt(mine, keys_here), masked_score)
            peak = jnp.max(here, axis=-1, keepdims=True)
            if step:
                past = nt(mine, qkv_ref[pairs + pair, : step * tile, :])
                peak = jnp.maximum(peak, jnp.max(past, axis=-1, keepdims=True))
                past = jnp.exp(past - peak)
            here = jnp.exp(here - peak)
            total = jnp.sum(here, axis=-1, keepdims=True)
            out = mm(here.astype(bf16), values_here)
            if step:
                total = total + jnp.sum(past, axis=-1, keepdims=True)
                out = out + mm(past.astype(bf16), qkv_ref[2 * pairs + pair, : step * tile, :])
            outs.append(out / total)
            logs.append(peak + jnp.log(total))
        lse_ref[pair, :, rows] = jnp.where(lane == 0, logs[0], logs[1]).T[0:2, :]
        att_ref[rows, pl.ds(pl.multiple_of(pair * LANES, LANES), LANES)] = jnp.where(
            masks[0], outs[0], outs[1]
        ).astype(bf16)
        between()


def norm_rows(x_ref, norms, perm_ref, hid_ref):
    tile = 256

    @pl.loop(0, x_ref.shape[0] // tile)
    def _(step):
        rows = rows_of(step, tile)
        normed, _ = centre_scale(x_ref[rows, :].astype(f32))
        hidden = (normed * norms[0:1, :] + norms[1:2, :]).astype(bf16)
        hid_ref[rows, :] = mm(hidden, perm_ref[...]).astype(bf16)


def triple_part(part, pairs, hid_ref, w_ref, qkv_ref):
    width = pairs * LANES
    triple = mm(hid_ref[...], w_ref[:, part * width : (part + 1) * width]).astype(bf16)
    for pair in range(pairs):
        qkv_ref[part * pairs + pair] = triple[:, pair * LANES : (pair + 1) * LANES]


def self_forward_kernel(
    pairs, x_ref, norms_ref, perm_ref, w_ref, hid_ref, qkv_ref, att_ref, lse_ref
):
    norm_rows(x_ref, norms_ref, perm_ref, hid_ref)
    for part in range(3):
        triple_part(part, pairs, hid_ref, w_ref, qkv_ref)

    @pl.loop(0, pairs)
    def _(pair):
        pair_forward(pair, pairs, qkv_ref, att_ref, lse_ref, lambda: None)


def self_forward(pairs, x, norms, perm, w):
    length, dim = x.shape
    return pl.pallas_call(
        partial(self_forward_kernel, pairs),
        out_shape=(
            jax.ShapeDtypeStruct((length, dim), bf16),
            jax.ShapeDtypeStruct((3 * pairs, length, LANES), bf16),
            jax.ShapeDtypeStruct((length, pairs * LANES), bf16),
            jax.ShapeDtypeStruct((pairs, 2, length), f32),
        ),
        compiler_params=params(),
        name="self_forward",
    )(x, norms, perm, w)


def pair_backward(pair, pairs, qkv_ref, att_ref, gatt_ref, lse_ref, grad_ref, acc_ref, between):
    length = att_ref.shape[0]
    width = pairs * LANES
    tile = 256
    above = lax.broadcasted_iota(jnp.int32, (tile, tile), 0) <= lax.broadcasted_iota(
        jnp.int32, (tile, tile), 1
    )
    masks = [head_mask(tile, 0), head_mask(tile, 1)]
    lanes = pl.ds(pl.multiple_of(pair * LANES, LANES), LANES)
    for step in range(length // tile):
        rows = slice(step * tile, (step + 1) * tile)
        query = qkv_ref[pair, rows, :] * SCALE
        grad_out = gatt_ref[rows, lanes]
        product = grad_out.astype(f32) * att_ref[rows, lanes].astype(f32)
        queries = [pick(masks[half], query) for half in range(2)]
        grads = [pick(masks[half], grad_out) for half in range(2)]
        deltas = [jnp.sum(pick(masks[half], product).T, axis=0, keepdims=True) for half in range(2)]
        grad_query = [None, None]
        for other in range(step + 1):
            cols = slice(other * tile, (other + 1) * tile)
            keys = qkv_ref[pairs + pair, cols, :]
            values = qkv_ref[2 * pairs + pair, cols, :]
            key_part = value_part = None
            for half in range(2):
                scores = nt(keys, queries[half])
                if other == step:
                    scores = jnp.where(above, scores, masked_score)
                probs = jnp.exp(scores - lse_ref[pair, half : half + 1, rows])
                grad_scores = (probs * (nt(values, grads[half]) - deltas[half])).astype(bf16)
                query_term = tn(grad_scores, keys)
                grad_query[half] = (
                    query_term if grad_query[half] is None else grad_query[half] + query_term
                )
                key_term = mm(grad_scores, queries[half])
                value_term = mm(probs.astype(bf16), grads[half])
                key_part = key_term if key_part is None else key_part + key_term
                value_part = value_term if value_part is None else value_part + value_term
            if other == step:
                acc_ref[0, cols, :] = key_part
                acc_ref[1, cols, :] = value_part
            else:
                acc_ref[0, cols, :] += key_part
                acc_ref[1, cols, :] += value_part
        grad_ref[rows, lanes] = (jnp.where(masks[0], grad_query[0], grad_query[1]) * SCALE).astype(
            bf16
        )
        between()
    for part in range(2):
        lanes_to = pl.ds(pl.multiple_of((part + 1) * width + pair * LANES, LANES), LANES)
        grad_ref[:, lanes_to] = acc_ref[part].astype(bf16)


def self_backward_kernel(
    pairs,
    qkv_ref,
    att_ref,
    gatt_ref,
    lse_ref,
    hid_ref,
    w_ref,
    gw_ref,
    ghid_ref,
    grad_ref,
    acc_ref,
):
    length = att_ref.shape[0]
    width = pairs * LANES
    attention = (qkv_ref, att_ref, gatt_ref, lse_ref, grad_ref, acc_ref)

    @pl.loop(0, pairs)
    def _(pair):
        pair_backward(pair, pairs, *attention, lambda: None)

    hidden_t = hid_ref[...].T
    for part in range(3):
        cols = slice(part * width, (part + 1) * width)
        gw_ref[:, cols] = mm(hidden_t, grad_ref[:, cols]).astype(bf16)
    for begin in range(0, length, 256):
        rows = slice(begin, begin + 256)
        ghid_ref[rows, :] = nt(grad_ref[rows, :], w_ref[...]).astype(bf16)


def self_backward(pairs, qkv, att, gatt, lse, hid, w):
    length, dim = hid.shape
    width = pairs * LANES
    return pl.pallas_call(
        partial(self_backward_kernel, pairs),
        out_shape=(
            jax.ShapeDtypeStruct((dim, 3 * width), bf16),
            jax.ShapeDtypeStruct((length, dim), bf16),
        ),
        scratch_shapes=[
            pltpu.VMEM((length, 3 * width), bf16),
            pltpu.VMEM((2, length, LANES), f32),
        ],
        compiler_params=params(),
        name="self_backward",
    )(qkv, att, gatt, lse, hid, w)


def finish_kernel(
    pairs,
    lines,
    qkv_ref,
    att_ref,
    gatt_ref,
    lse_ref,
    hid_ref,
    x_ref,
    gfirst_ref,
    norms_ref,
    perm_ref,
    others_ref,
    wts_ref,
    _,
    all_ref,
    gin_ref,
    small_ref,
    grad_ref,
    acc_ref,
    gw_ref,
    w_ref,
    sems,
    ghid_ref,
    gsib_ref,
    parts_ref,
    gsib_sems,
    part_sems,
    send_sems,
):
    length, dim = hid_ref.shape
    width = pairs * LANES
    tokens = length // 8
    place = Place(lines)
    me, core = place.me, place.core
    place.meet()
    send = Sender(place, send_sems)
    copies = weight_copies(pairs, dim, wts_ref, w_ref, sems)
    for copy in copies:
        copy.start()

    share_count = dim // width
    share = lax.rem(me, share_count)
    gw_ref[3] = jnp.zeros_like(gw_ref[3])
    outs = []
    for part in range(3):
        for other in range(1, share_count):
            first = part * dim + lax.rem(share + other, share_count) * width
            outs.append(
                pltpu.make_async_copy(
                    gw_ref.at[3],
                    all_ref.at[:, pl.ds(pl.multiple_of(first, LANES), width)],
                    sems.at[6 + part * (share_count - 1) + other - 1],
                )
            )
            outs[-1].start()

    attention = (qkv_ref, att_ref, gatt_ref, lse_ref, grad_ref, acc_ref)

    @pl.loop(0, pairs)
    def _(pair):
        pair_backward(pair, pairs, *attention, lambda: None)

    def token_rows(device):
        return pl.ds(pl.multiple_of(device * tokens, tokens), tokens)

    for copy in copies:
        copy.wait()
    for begin in range(0, length, 256):
        rows = slice(begin, begin + 256)
        ghid_ref[rows, :] = nt(grad_ref[rows, :], w_ref[...]).astype(bf16)
    chips = (place.xn // 2, place.yn // 2, place.dg // 2, place.chip)
    for chip in chips:
        theirs = chip * 2 + 1 - core
        send.start(
            None, ghid_ref.at[token_rows(theirs)], gsib_ref.at[chip], gsib_sems.at[chip], seq=place.sib
        )
    for chip in chips:
        send.arrived(None, gsib_ref.at[chip], gsib_sems.at[chip])
        rows = token_rows(chip * 2 + core)
        total = (ghid_ref[rows, :].astype(f32) + gsib_ref[chip].astype(f32)).astype(bf16)
        if chip is place.chip:
            parts_ref[chip] = total
        else:
            ghid_ref[rows, :] = total
            send.start(
                None,
                ghid_ref.at[rows],
                parts_ref.at[place.chip],
                part_sems.at[place.chip],
                seq=chip * 2 + core,
            )

    hidden_t = hid_ref[...].T
    for part in range(3):
        gw_ref[part] = mm(hidden_t, grad_ref[:, part * width : (part + 1) * width]).astype(bf16)
        first = part * dim + share * width
        outs.append(
            pltpu.make_async_copy(
                gw_ref.at[part],
                all_ref.at[:, pl.ds(pl.multiple_of(first, LANES), width)],
                sems.at[3 + part],
            )
        )
        outs[-1].start()

    for chip in chips[:3]:
        send.arrived(None, parts_ref.at[chip], part_sems.at[chip])
    gain_sum = shift_sum = None
    for chip in range(4):
        rows = slice(chip * tokens, (chip + 1) * tokens)
        upstream = nt(parts_ref[chip], perm_ref[...])
        normed, recip = centre_scale(x_ref[rows, :].astype(f32))
        back, gain, shift = norm_back(upstream, normed, recip, norms_ref[0:1, :])
        gin_ref[rows, :] = gfirst_ref[rows, :] + back
        gain_sum = gain if gain_sum is None else gain_sum + gain
        shift_sum = shift if shift_sum is None else shift_sum + shift
    small_ref[...] = others_ref[...]
    small_ref[0:1, :] = gain_sum
    small_ref[1:2, :] = shift_sum
    for copy in outs:
        copy.wait()
    send.finish()


def finish(pairs, lines, qkv, att, gatt, lse, hid, x, gfirst, norms, perm, others, weights, grads):
    length, dim = hid.shape
    width = pairs * LANES
    count = x.shape[0]
    tokens = length // 8
    any_space = pl.BlockSpec(memory_space=pl.ANY)
    vmem = pl.BlockSpec(memory_space=pltpu.VMEM)
    dma = pltpu.SemaphoreType.DMA
    return pl.pallas_call(
        partial(finish_kernel, pairs, lines),
        out_shape=(
            jax.ShapeDtypeStruct(grads.shape, bf16),
            jax.ShapeDtypeStruct((count, dim), f32),
            jax.ShapeDtypeStruct((8, dim), f32),
        ),
        in_specs=[vmem] * 10 + [any_space] * 2,
        out_specs=(any_space, vmem, vmem),
        scratch_shapes=[
            pltpu.VMEM((length, 3 * width), bf16),
            pltpu.VMEM((2, length, LANES), f32),
            pltpu.VMEM((4, dim, width), bf16),
            pltpu.VMEM((dim, 3 * width), bf16),
            dma((6 + 3 * (dim // width),)),
            pltpu.VMEM((length, dim), bf16),
            pltpu.VMEM((4, tokens, dim), bf16),
            pltpu.VMEM((4, tokens, dim), bf16),
            dma((4,)),
            dma((4,)),
            dma((8,)),
        ],
        input_output_aliases={11: 0},
        compiler_params=pltpu.CompilerParams(
            vmem_limit_bytes=VMEM_BYTES, collective_id=3, has_side_effects=True
        ),
        name="finish",
    )(qkv, att, gatt, lse, hid, x, gfirst, norms, perm, others, weights, grads)


def spread_heads(block, rows, group):
    lane = lax.broadcasted_iota(jnp.int32, block.shape, 1) // HEAD
    return jnp.concatenate([pick(lane == head, block) for head in range(group)], axis=0)


def gather_heads(stacked, rows, group):
    lane = lax.broadcasted_iota(jnp.int32, (rows, stacked.shape[1]), 1) // HEAD
    out = None
    for head in range(group):
        part = pick(lane == head, stacked[head * rows : (head + 1) * rows])
        out = part if out is None else out + part
    return out


def live_keys(presence_ref, span, shape, axis, neighbours, each):
    index = lax.broadcasted_iota(jnp.int32, shape, axis) // each
    live = jnp.zeros(shape, f32)
    anyone = None
    for which in range(neighbours):
        here = presence_ref[span * neighbours + which]
        there = jnp.where(here > 0, 1.0, 0.0).astype(f32)
        live = jnp.where(index == which, there, live)
        anyone = here if anyone is None else jnp.maximum(anyone, here)
    return live, anyone.astype(f32)


def span_forward(span, spans, neighbours, presence_ref, cross_q_ref, near_kv_ref, cross_ref):
    count, dim = cross_q_ref.shape
    span_len = count // spans
    near = near_kv_ref.shape[0] // spans
    group = 256 // HEAD
    rows = rows_of(span, span_len)
    keys = rows_of(span, near)
    live, anyone = live_keys(presence_ref, span, (1, near), 1, neighbours, near // neighbours)
    for begin in range(0, dim, group * HEAD):
        lanes = slice(begin, begin + group * HEAD)
        lanes_v = slice(dim + begin, dim + begin + group * HEAD)
        query = spread_heads(cross_q_ref[rows, lanes] * SCALE, span_len, group)
        scores = jnp.where(live > 0, nt(query, near_kv_ref[keys, lanes]), masked_score)
        peak = jnp.max(scores, axis=-1, keepdims=True)
        expon = jnp.exp(scores - peak) * live
        total = jnp.sum(expon, axis=-1, keepdims=True) + 1.0 - anyone
        out = mm(expon.astype(bf16), near_kv_ref[keys, lanes_v]) / total
        cross_ref[rows, lanes] = gather_heads(out, span_len, group).astype(bf16)


def cross_forward_kernel(
    spans,
    neighbours,
    presence_ref,
    att_ref,
    x_ref,
    norms_ref,
    perm_ref,
    perm_att_ref,
    near_ref,
    w_out_ref,
    w_cq_ref,
    w_ck_ref,
    w_cv_ref,
    w_co_ref,
    att_p_ref,
    first_ref,
    hid_p_ref,
    cross_q_ref,
    near_p_ref,
    near_kv_ref,
    co_p_ref,
    second_ref,
    cross_ref,
):
    count, dim = x_ref.shape
    rows_near = near_ref.shape[0]
    tile = 512

    att_p_ref[...] = mm(att_ref[...], perm_att_ref[...]).astype(bf16)
    first_ref[...] = x_ref[...].astype(f32) + mm(att_p_ref[...], w_out_ref[...])

    normed, _ = centre_scale(first_ref[...])
    hidden = (normed * norms_ref[2:3, :] + norms_ref[3:4, :]).astype(bf16)
    hid_p_ref[...] = mm(hidden, perm_ref[...]).astype(bf16)
    cross_q_ref[...] = mm(hid_p_ref[...], w_cq_ref[...]).astype(bf16)

    @pl.loop(0, rows_near // tile)
    def _(step):
        rows = rows_of(step, tile)
        near_p_ref[rows, :] = mm(near_ref[rows, :], perm_ref[...]).astype(bf16)
        near_kv_ref[rows, :dim] = mm(near_p_ref[rows, :], w_ck_ref[...]).astype(bf16)
        near_kv_ref[rows, dim:] = mm(near_p_ref[rows, :], w_cv_ref[...]).astype(bf16)

    @pl.loop(0, spans)
    def _(span):
        span_forward(span, spans, neighbours, presence_ref, cross_q_ref, near_kv_ref, cross_ref)

    co_p_ref[...] = mm(cross_ref[...], perm_ref[...]).astype(bf16)
    second_ref[...] = first_ref[...] + mm(co_p_ref[...], w_co_ref[...])


def column_block(rows, width, index):
    return pl.BlockSpec((rows, width), lambda *_: (0, index), pipeline_mode=pl.Buffered(1))


def whole(array):
    return pl.BlockSpec(array.shape, lambda *_: (0,) * array.ndim, pipeline_mode=pl.Buffered(1))


def whole_shape(shape):
    return pl.BlockSpec(shape, lambda *_: (0,) * len(shape), pipeline_mode=pl.Buffered(1))


def cross_forward(spans, neighbours, presence, att, x, norms, perm, perm_att, near, weights):
    count, dim = x.shape
    rows_near = near.shape[0]
    out_shape = (
        jax.ShapeDtypeStruct((count, dim), bf16),
        jax.ShapeDtypeStruct((count, dim), f32),
        jax.ShapeDtypeStruct((count, dim), bf16),
        jax.ShapeDtypeStruct((count, dim), bf16),
        jax.ShapeDtypeStruct((rows_near, dim), bf16),
        jax.ShapeDtypeStruct((rows_near, 2 * dim), bf16),
        jax.ShapeDtypeStruct((count, dim), bf16),
        jax.ShapeDtypeStruct((count, dim), f32),
    )
    operands = (att, x, norms, perm, perm_att, near)
    return pl.pallas_call(
        partial(cross_forward_kernel, spans, neighbours),
        out_shape=out_shape,
        grid=(1,),
        in_specs=[pl.BlockSpec(memory_space=pltpu.SMEM)]
        + [whole(op) for op in operands]
        + [column_block(dim, dim, index) for index in (3, 4, 5, 6, 7)],
        out_specs=tuple(whole_shape(shape.shape) for shape in out_shape),
        scratch_shapes=[pltpu.VMEM((count, dim), bf16)],
        compiler_params=params(),
        name="cross_forward",
    )(presence, *operands, *([weights] * 5))


def feed_kernel(
    second_ref,
    cot_ref,
    norms_ref,
    perm_ref,
    w_up_ref,
    w_down_ref,
    out_ref,
    gsecond_ref,
    all_ref,
    gnorm_ref,
    hid_p_ref,
    hid_t_ref,
    cot_p_ref,
    cot_t_ref,
    result_ref,
    back_ref,
    gup_ref,
    gdown_ref,
    sems,
):
    step = pl.program_id(0)
    last = pl.num_programs(0) - 1
    slot = lax.rem(step, 2)
    dim, tile = w_up_ref.shape

    def copies(step, slot):
        up = pl.multiple_of(8 * dim + step * tile, tile)
        down = pl.multiple_of(8 * dim + (last + 1 + step) * tile, tile)
        return (
            pltpu.make_async_copy(gup_ref.at[slot], all_ref.at[:, pl.ds(up, tile)], sems.at[0, slot]),
            pltpu.make_async_copy(
                gdown_ref.at[slot], all_ref.at[:, pl.ds(down, tile)], sems.at[1, slot]
            ),
        )

    @pl.when(step >= 2)
    def _():
        for copy in copies(step - 2, slot):
            copy.wait()

    @pl.when(step == 0)
    def _():
        normed, _ = centre_scale(second_ref[...])
        hidden = (normed * norms_ref[4:5, :] + norms_ref[5:6, :]).astype(bf16)
        hid_p_ref[...] = mm(hidden, perm_ref[...]).astype(bf16)
        hid_t_ref[...] = hid_p_ref[...].T
        cot_p_ref[...] = mm(cot_ref[...], perm_ref[...]).astype(bf16)
        cot_t_ref[...] = cot_p_ref[...].T
        result_ref[...] = jnp.zeros_like(result_ref)
        back_ref[...] = jnp.zeros_like(back_ref)

    upward = mm(hid_p_ref[...], w_up_ref[...])
    active, slope = gelu_parts(upward)
    active = active.astype(bf16)
    result_ref[...] += nt(active, w_down_ref[...])
    gdown_ref[slot] = mm(cot_t_ref[...], active).astype(bf16)
    grad_up = (mm(cot_p_ref[...], w_down_ref[...]) * slope).astype(bf16)
    gup_ref[slot] = mm(hid_t_ref[...], grad_up).astype(bf16)
    for copy in copies(step, slot):
        copy.start()
    back_ref[...] += nt(grad_up, w_up_ref[...])

    @pl.when(step == last)
    def _():
        out_ref[...] = (
            second_ref[...] + nt(result_ref[...].astype(bf16), perm_ref[...])
        ).astype(bf16)
        upstream = nt(back_ref[...].astype(bf16), perm_ref[...])
        normed, recip = centre_scale(second_ref[...])
        back, gain, shift = norm_back(upstream, normed, recip, norms_ref[4:5, :])
        gsecond_ref[...] = cot_ref[...].astype(f32) + back
        gnorm_ref[0:1, :] = gain
        gnorm_ref[1:2, :] = shift
        for which in (step - 1, step):
            for copy in copies(which, lax.rem(which, 2)):
                copy.wait()


def feed(second, cot, norms, perm, weights):
    count, dim = second.shape
    ffw = (weights.shape[1] - 8 * dim) // 2
    tile = 512
    first_up = 8 * dim // tile
    first_down = (8 * dim + ffw) // tile
    out_shape = (
        jax.ShapeDtypeStruct((count, dim), bf16),
        jax.ShapeDtypeStruct((count, dim), f32),
        jax.ShapeDtypeStruct(weights.shape, bf16),
        jax.ShapeDtypeStruct((2, dim), f32),
    )
    operands = (second, cot, norms, perm)
    return pl.pallas_call(
        feed_kernel,
        out_shape=out_shape,
        grid=(ffw // tile,),
        in_specs=[whole(op) for op in operands]
        + [
            pl.BlockSpec((dim, tile), lambda i: (0, first_up + i)),
            pl.BlockSpec((dim, tile), lambda i: (0, first_down + i)),
        ],
        out_specs=(
            whole_shape((count, dim)),
            whole_shape((count, dim)),
            pl.BlockSpec(memory_space=pl.ANY),
            whole_shape((2, dim)),
        ),
        scratch_shapes=[
            pltpu.VMEM((count, dim), bf16),
            pltpu.VMEM((dim, count), bf16),
            pltpu.VMEM((count, dim), bf16),
            pltpu.VMEM((dim, count), bf16),
            pltpu.VMEM((count, dim), f32),
            pltpu.VMEM((count, dim), f32),
            pltpu.VMEM((2, dim, tile), bf16),
            pltpu.VMEM((2, dim, tile), bf16),
            pltpu.SemaphoreType.DMA((2, 2)),
        ],
        compiler_params=params(),
        name="feed",
    )(*operands, weights, weights)


def cross_backward_kernel(
    spans,
    neighbours,
    lines,
    presence_ref,
    gsecond_ref,
    first_ref,
    norms_ref,
    perm_ref,
    perm_att_ref,
    att_p_ref,
    hid_p_ref,
    cross_q_ref,
    near_p_ref,
    near_kv_ref,
    co_p_ref,
    w_out_ref,
    w_cq_ref,
    w_co_ref,
    _,
    gfirst_ref,
    gatt_ref,
    all_ref,
    gnorm_ref,
    *rest,
):
    count, dim = first_ref.shape
    rows_near = near_p_ref.shape[0]
    span_len = count // spans
    near = rows_near // spans
    group = 256 // HEAD
    outs = []
    if lines:
        gatt_tok_ref, row_sems, send_sems = rest[5:]
        place = Place(lines)
        place.meet()
        send = Sender(place, send_sems)
    gco_ref, gcq_ref, gnear_ref, gw_ref, sems = rest[:5]

    def keep(index, value):
        slot = len(outs) % 3
        if len(outs) >= 3:
            outs[-3].wait()
        gw_ref[slot] = value.astype(bf16)
        outs.append(
            pltpu.make_async_copy(
                gw_ref.at[slot],
                all_ref.at[:, pl.ds((3 + index) * dim, dim)],
                sems.at[index],
            )
        )
        outs[-1].start()

    upper = gsecond_ref[...].astype(bf16)
    gco_ref[...] = nt(nt(upper, w_co_ref[...]).astype(bf16), perm_ref[...]).astype(bf16)

    def one_span(span):
        rows = rows_of(span, span_len)
        keys = rows_of(span, near)
        live, anyone = live_keys(presence_ref, span, (near, 1), 0, neighbours, near // neighbours)
        for begin in range(0, dim, group * HEAD):
            lanes = slice(begin, begin + group * HEAD)
            lanes_v = slice(dim + begin, dim + begin + group * HEAD)
            query = spread_heads(cross_q_ref[rows, lanes] * SCALE, span_len, group)
            grad_out = spread_heads(gco_ref[rows, lanes], span_len, group)
            key = near_kv_ref[keys, lanes]
            scores = jnp.where(live > 0, nt(key, query), masked_score)
            peak = jnp.max(scores, axis=0, keepdims=True)
            expon = jnp.exp(scores - peak) * live
            total = jnp.sum(expon, axis=0, keepdims=True) + 1.0 - anyone
            probs = expon * (1.0 / total)
            grad_probs = nt(near_kv_ref[keys, lanes_v], grad_out)
            inner = jnp.sum(probs * grad_probs, axis=0, keepdims=True)
            grad_scores = (probs * (grad_probs - inner)).astype(bf16)
            gcq_ref[rows, lanes] = (
                gather_heads(tn(grad_scores, key), span_len, group) * SCALE
            ).astype(bf16)
            gnear_ref[keys, lanes] = mm(grad_scores, query).astype(bf16)
            gnear_ref[keys, lanes_v] = mm(probs.astype(bf16), grad_out).astype(bf16)

    pl.loop(0, spans)(one_span)

    upstream = nt(nt(gcq_ref[...], w_cq_ref[...]).astype(bf16), perm_ref[...])
    normed, recip = centre_scale(first_ref[...])
    back, gain, shift = norm_back(upstream, normed, recip, norms_ref[2:3, :])
    gnorm_ref[0:1, :] = gain
    gnorm_ref[1:2, :] = shift
    gfirst_ref[...] = gsecond_ref[...] + back
    lower = gfirst_ref[...].astype(bf16)
    gatt = nt(nt(lower, w_out_ref[...]).astype(bf16), perm_att_ref[...]).astype(bf16)
    if lines:
        width = gatt_ref.shape[1]
        tokens = gatt_ref.shape[0] // 8
        shares = gatt.shape[1] // width
        gatt_tok_ref[...] = gatt

        def block(device):
            return gatt_tok_ref.at[
                pl.ds(pl.multiple_of(device // shares * tokens, tokens), tokens),
                pl.ds(pl.multiple_of(device % shares * width, width), width),
            ]

        def landing(device):
            return gatt_ref.at[pl.ds(pl.multiple_of(device * tokens, tokens), tokens)]

        for other in place.plane():
            send.start(None, block(other), landing(place.me), row_sems.at[place.me], seq=other)
        own = pltpu.make_async_copy(block(place.me), landing(place.me), row_sems.at[place.me])
        own.start()
    else:
        gatt_ref[...] = gatt
    keep(4, mm(co_p_ref[...].T, upper))
    near_t = near_p_ref[...].T
    for part in range(2):
        keep(2 + part, mm(near_t, gnear_ref[:, part * dim : (part + 1) * dim]))
    keep(1, mm(hid_p_ref[...].T, gcq_ref[...]))
    keep(0, mm(att_p_ref[...].T, lower))
    if lines:
        for other in place.plane():
            send.arrived(None, landing(other), row_sems.at[other])
        own.wait()
        send.finish()
    for copy in outs[-3:]:
        copy.wait()


def cross_backward(
    spans,
    neighbours,
    lines,
    presence,
    gsecond,
    first,
    norms,
    perm,
    perm_att,
    att_p,
    hid_p,
    cross_q,
    near_p,
    near_kv,
    co_p,
    weights,
    grads,
):
    count, dim = first.shape
    rows_near = near_p.shape[0]
    gatt_shape = (count, perm_att.shape[0])
    out_shape = [
        jax.ShapeDtypeStruct((count, dim), f32),
        jax.ShapeDtypeStruct(gatt_shape, bf16),
        jax.ShapeDtypeStruct(grads.shape, bf16),
        jax.ShapeDtypeStruct((2, dim), f32),
    ]
    scratch = [
        pltpu.VMEM((count, dim), bf16),
        pltpu.VMEM((count, dim), bf16),
        pltpu.VMEM((rows_near, 2 * dim), bf16),
        pltpu.VMEM((3, dim, dim), bf16),
        pltpu.SemaphoreType.DMA((5,)),
    ]
    compiler_params = params()
    if lines:
        out_shape[1] = jax.ShapeDtypeStruct((2 * count, gatt_shape[1] // 2), bf16)
        scratch += [
            pltpu.VMEM(gatt_shape, bf16),
            pltpu.SemaphoreType.DMA((8,)),
            pltpu.SemaphoreType.DMA((8,)),
        ]
        compiler_params = pltpu.CompilerParams(
            vmem_limit_bytes=VMEM_BYTES, collective_id=2, has_side_effects=True
        )
    operands = (
        gsecond,
        first,
        norms,
        perm,
        perm_att,
        att_p,
        hid_p,
        cross_q,
        near_p,
        near_kv,
        co_p,
    )
    return pl.pallas_call(
        partial(cross_backward_kernel, spans, neighbours, lines),
        out_shape=out_shape,
        grid=(1,),
        in_specs=[pl.BlockSpec(memory_space=pltpu.SMEM)]
        + [whole(op) for op in operands]
        + [column_block(dim, dim, index) for index in (3, 4, 7)]
        + [pl.BlockSpec(memory_space=pl.ANY)],
        out_specs=tuple(
            pl.BlockSpec(memory_space=pl.ANY) if index == 2 else whole_shape(shape.shape)
            for index, shape in enumerate(out_shape)
        ),
        scratch_shapes=scratch,
        input_output_aliases={len(operands) + 4: 2},
        compiler_params=compiler_params,
        name="cross_backward",
    )(presence, *operands, *([weights] * 3), grads)


def last_norm_kernel(parts_ref, x_ref, gfirst_ref, norms_ref, perm_ref, out_ref, gnorm_ref):
    total = parts_ref[0].astype(f32)
    for part in range(1, parts_ref.shape[0]):
        total = total + parts_ref[part].astype(f32)
    upstream = nt(total.astype(bf16), perm_ref[...])
    normed, recip = centre_scale(x_ref[...].astype(f32))
    back, gain, shift = norm_back(upstream, normed, recip, norms_ref[0:1, :])
    out_ref[...] = gfirst_ref[...] + back
    gnorm_ref[0:1, :] = gain
    gnorm_ref[1:2, :] = shift


def last_norm(parts, x, gfirst, norms, perm):
    count, dim = x.shape
    return pl.pallas_call(
        last_norm_kernel,
        out_shape=(
            jax.ShapeDtypeStruct((count, dim), f32),
            jax.ShapeDtypeStruct((2, dim), f32),
        ),
        compiler_params=params(),
        name="last_norm",
    )(parts, x, gfirst, norms, perm)


def forward_kernel(
    lines,
    pairs,
    spans,
    neighbours,
    presence_ref,
    w_ref,
    norm_ref,
    x_ref,
    perm_ref,
    near_ref,
    wts_ref,
    norms_ref,
    hid_ref,
    qkv_ref,
    att_ref,
    lse_ref,
    att_p_ref,
    first_ref,
    hid_p_ref,
    cross_q_ref,
    near_p_ref,
    near_kv_ref,
    co_p_ref,
    second_ref,
    own_ref,
    small_ref,
    rows_ref,
    w_qkv_ref,
    w_mid_ref,
    att_tok_ref,
    cross_ref,
    send_sems,
    z_sems,
    y_sems,
    x_sems,
    sib_sems,
    norm_sems,
    row_sems,
    att_sems,
    local_sems,
    qkv_sems,
    mid_sems,
):
    place = Place(lines)
    z, me, core = place.z, place.me, place.core
    length, dim = hid_ref.shape
    width = pairs * LANES
    tokens = length // 8
    own_ref[...] = w_ref[...].astype(bf16)
    place.meet()
    send = Sender(place, send_sems)
    unit = partial(unit_of, wts_ref, lines)
    low, high = place.y == 0, place.y == 1
    events = place.events()
    keep = pltpu.make_async_copy(own_ref, unit(z, me), local_sems.at[0])
    keep.start()

    def crossing(row, of=core):
        return row * 4 + (1 - place.x) * 2 + of

    def own_unit(index):
        condition, line, far, side = events[index]
        mine = unit(line, me)
        src = own_ref if far == 0 else mine
        if far:
            send.arrived(condition, mine, z_sems.at[line])
        if side >= 0:
            send.start(both(condition, z > 0), src, mine, z_sems.at[line], z=z - 1)
        if side <= 0:
            send.start(both(condition, z < lines - 1), src, mine, z_sems.at[line], z=z + 1)
        send.start(condition, src, mine, y_sems.at[line], seq=place.yn)
        send.start(both(condition, low), src, mine, x_sems.at[0, line], seq=place.xn)
        send.start(condition, src, mine, sib_sems.at[0, line], seq=place.sib)

    def from_y(index):
        condition, line, _, _ = events[index]
        theirs = unit(line, place.yn)
        send.arrived(condition, theirs, y_sems.at[line])
        send.start(both(condition, high), theirs, theirs, x_sems.at[0, line], seq=place.xn)
        send.start(condition, theirs, theirs, sib_sems.at[1, line], seq=place.sib)

    def from_x(row, index):
        condition, line, _, _ = events[index]
        theirs = unit(line, crossing(row))
        send.arrived(condition, theirs, x_sems.at[row, line])
        send.start(condition, theirs, theirs, sib_sems.at[2 + row, line], seq=place.sib)

    def late_x(index):
        condition, line, far, _ = events[index]
        mine, theirs = unit(line, me), unit(line, place.yn)
        src = own_ref if far == 0 else mine
        send.start(both(condition, high), src, mine, x_sems.at[1, line], seq=place.xn)
        send.start(both(condition, low), theirs, theirs, x_sems.at[1, line], seq=place.xn)

    def row_block(seq):
        return rows_ref.at[pl.ds(pl.multiple_of(seq * tokens, tokens), tokens)]

    own_unit(0)
    own_rows = pltpu.make_async_copy(x_ref.at[place.chip], row_block(me), local_sems.at[1])
    own_rows.start()
    send.start(None, x_ref.at[place.chip], row_block(me), row_sems.at[me], seq=place.sib)
    others = (place.xn, place.yn, place.dg)
    for other in others:
        send.start(None, x_ref.at[other // 2], row_block(me), row_sems.at[me], seq=other)
    for other in place.line():
        send.start(None, norm_ref, small_ref.at[z], norm_sems.at[z], z=other)
    small_ref[z] = norm_ref[...]

    @pl.loop(0, near_ref.shape[0] // 512)
    def _(step):
        rows = rows_of(step, 512)
        near_p_ref[rows, :] = mm(near_ref[rows, :], perm_ref[...]).astype(bf16)

    own_unit(1)
    own_unit(2)
    from_y(0)
    for other in others:
        send.arrived(None, row_block(other), row_sems.at[other])
        send.start(None, row_block(other), row_block(other), row_sems.at[other], seq=place.sib)
    own_unit(3)
    own_unit(4)
    from_x(0, 0)
    from_y(1)
    from_y(2)

    for other in place.line():
        send.arrived(None, small_ref.at[other], norm_sems.at[other])
    piece = small_ref.shape[2]
    total = None
    for line in range(lines):
        row = lax.broadcasted_iota(jnp.int32, (piece, dim), 0)
        column = lax.broadcasted_iota(jnp.int32, (piece, dim), 1)
        part = dim // lines
        place_of = jnp.logical_and(row < part, column == row + line * part).astype(bf16)
        term = mm(small_ref[line], place_of)
        total = term if total is None else total + term
    norms_ref[...] = total[: norms_ref.shape[0]]

    own_unit(5)
    own_unit(6)
    from_x(0, 1)
    from_x(0, 2)
    from_y(3)
    from_y(4)
    for other in others:
        theirs = other + 1 - 2 * core
        send.arrived(None, row_block(theirs), row_sems.at[theirs])
    send.arrived(None, row_block(place.sib), row_sems.at[place.sib])
    own_rows.wait()
    norm_rows(rows_ref, norms_ref[...], perm_ref, hid_ref)
    from_x(0, 3)
    from_x(0, 4)
    from_y(5)
    from_y(6)
    late_x(0)
    late_x(1)
    late_x(2)
    from_x(0, 5)
    from_x(0, 6)
    for index in range(3, len(events)):
        late_x(index)
    keep.wait()
    for line in range(lines):
        theirs = unit(line, place.sib)
        send.arrived(low, theirs, sib_sems.at[0, line])
        theirs = unit(line, place.yn + 1 - 2 * core)
        send.arrived(high, theirs, sib_sems.at[1, line])
        theirs = unit(line, crossing(0, 1 - core))
        send.arrived(None, theirs, sib_sems.at[2, line])
    weave = Weave([partial(from_x, 1, index) for index in range(len(events))])

    copies = weight_copies(pairs, dim, wts_ref, w_qkv_ref, qkv_sems)
    middle = [
        pltpu.make_async_copy(
            wts_ref.at[:, pl.ds((3 + index) * dim, dim)], w_mid_ref.at[index], mid_sems.at[index]
        )
        for index in range(5)
    ]
    for copy in copies + middle:
        copy.start()
    for part in range(3):
        copies[part].wait()
        triple_part(part, pairs, hid_ref, w_qkv_ref, qkv_ref)

    share = lax.rem(me, dim // width)
    seq_rows = pl.ds(pl.multiple_of(place.chip * tokens, tokens), tokens)

    def landing(pair, chip_rows, share):
        lanes = pl.ds(pl.multiple_of(share * width + pair * LANES, LANES), LANES)
        return att_tok_ref.at[chip_rows, lanes]

    for pair in range(pairs):
        lanes = slice(pair * LANES, (pair + 1) * LANES)
        pair_forward(pair, pairs, qkv_ref, att_ref, lse_ref, lambda: None)
        for other in place.plane():
            block = att_ref.at[pl.ds(pl.multiple_of(other * tokens, tokens), tokens), lanes]
            to = landing(pair, seq_rows, share)
            send.start(None, block, to, att_sems.at[pair, me], seq=other)
        own_block = att_ref[pl.ds(pl.multiple_of(me * tokens, tokens), tokens), lanes]
        landing(pair, seq_rows, share)[...] = own_block
        weave.some(1)

    for copy in middle:
        copy.wait()
    w_out_ref, w_cq_ref, w_ck_ref, w_cv_ref, w_co_ref = (w_mid_ref.at[index] for index in range(5))

    @pl.loop(0, near_ref.shape[0] // 512)
    def _(step):
        rows = rows_of(step, 512)
        near_kv_ref[rows, :dim] = mm(near_p_ref[rows, :], w_ck_ref[...]).astype(bf16)
        near_kv_ref[rows, dim:] = mm(near_p_ref[rows, :], w_cv_ref[...]).astype(bf16)

    weave.some(2)
    for pair in range(pairs):
        for other in place.plane():
            rows = pl.ds(pl.multiple_of(other // 2 * tokens, tokens), tokens)
            send.arrived(
                None, landing(pair, rows, lax.rem(other, 2)), att_sems.at[pair, other]
            )
    att_p_ref[...] = mm(att_tok_ref[...], perm_ref[...]).astype(bf16)
    own_x = x_ref[...].reshape(first_ref.shape).astype(f32)
    first_ref[...] = own_x + mm(att_p_ref[...], w_out_ref[...])
    normed, _ = centre_scale(first_ref[...])
    hidden = (normed * norms_ref[2:3, :] + norms_ref[3:4, :]).astype(bf16)
    hid_p_ref[...] = mm(hidden, perm_ref[...]).astype(bf16)
    cross_q_ref[...] = mm(hid_p_ref[...], w_cq_ref[...]).astype(bf16)
    weave.rest()

    @pl.loop(0, spans)
    def _(span):
        span_forward(span, spans, neighbours, presence_ref, cross_q_ref, near_kv_ref, cross_ref)

    co_p_ref[...] = mm(cross_ref[...], perm_ref[...]).astype(bf16)
    second_ref[...] = first_ref[...] + mm(co_p_ref[...], w_co_ref[...])

    for line in range(lines):
        theirs = unit(line, place.sib)
        send.arrived(high, theirs, sib_sems.at[0, line])
        theirs = unit(line, place.yn + 1 - 2 * core)
        send.arrived(low, theirs, sib_sems.at[1, line])
        theirs = unit(line, crossing(1, 1 - core))
        send.arrived(None, theirs, sib_sems.at[3, line])
    send.finish()


def forward(lines, pairs, spans, neighbours, presence, w_shard, n_shard, inputs, perm, near):
    unit_rows, unit_cols = w_shard.shape
    seqs, tokens, dim = inputs.shape
    count, length, width = seqs * tokens, 8 * tokens, pairs * LANES
    rows_near = near.shape[0]
    events = 2 * lines - 1
    any_space = pl.BlockSpec(memory_space=pl.ANY)
    vmem = pl.BlockSpec(memory_space=pltpu.VMEM)
    dma = pltpu.SemaphoreType.DMA
    out_shape = (
        jax.ShapeDtypeStruct((unit_rows * lines, unit_cols * 8), bf16),
        jax.ShapeDtypeStruct((8, dim), f32),
        jax.ShapeDtypeStruct((length, dim), bf16),
        jax.ShapeDtypeStruct((3 * pairs, length, LANES), bf16),
        jax.ShapeDtypeStruct((length, width), bf16),
        jax.ShapeDtypeStruct((pairs, 2, length), f32),
        jax.ShapeDtypeStruct((count, dim), bf16),
        jax.ShapeDtypeStruct((count, dim), f32),
        jax.ShapeDtypeStruct((count, dim), bf16),
        jax.ShapeDtypeStruct((count, dim), bf16),
        jax.ShapeDtypeStruct((rows_near, dim), bf16),
        jax.ShapeDtypeStruct((rows_near, 2 * dim), bf16),
        jax.ShapeDtypeStruct((count, dim), bf16),
        jax.ShapeDtypeStruct((count, dim), f32),
    )
    return pl.pallas_call(
        partial(forward_kernel, lines, pairs, spans, neighbours),
        out_shape=out_shape,
        in_specs=[pl.BlockSpec(memory_space=pltpu.SMEM)] + [vmem] * 5,
        out_specs=(any_space,) + (vmem,) * (len(out_shape) - 1),
        scratch_shapes=[
            pltpu.VMEM((unit_rows, unit_cols), bf16),
            pltpu.VMEM((lines,) + n_shard.shape, bf16),
            pltpu.VMEM((length, dim), bf16),
            pltpu.VMEM((dim, 3 * width), bf16),
            pltpu.VMEM((5, dim, dim), bf16),
            pltpu.VMEM((count, dim), bf16),
            pltpu.VMEM((count, dim), bf16),
            dma((11 * events + 7 + lines + 7 * pairs,)),
            dma((lines,)),
            dma((lines,)),
            dma((2, lines)),
            dma((4, lines)),
            dma((lines,)),
            dma((8,)),
            dma((pairs, 8)),
            dma((2,)),
            dma((3,)),
            dma((5,)),
        ],
        compiler_params=pltpu.CompilerParams(
            vmem_limit_bytes=VMEM_BYTES, collective_id=1, has_side_effects=True
        ),
        name="forward",
    )(presence, w_shard, n_shard, inputs, perm, near)


def reduce_kernel(
    lines,
    grads_ref,
    small_ref,
    shard_ref,
    norms_ref,
    mine_ref,
    sib_ref,
    corner_a_ref,
    corner_b_ref,
    from_x_ref,
    from_y_ref,
    below_ref,
    above_ref,
    plane_ref,
    plane_sum_ref,
    line_ref,
    send_sems,
    load_sems,
    sib_sems,
    a_sems,
    b_sems,
    x_sems,
    y_sems,
    below_sems,
    above_sems,
    plane_sems,
    line_sems,
):
    place = Place(lines)
    z, me = place.z, place.me
    unit_rows, unit_cols = shard_ref.shape
    half = unit_rows // 2
    tile = 32
    place.meet()
    send = Sender(place, send_sems)
    chips = (place.dg, place.yn, place.xn, me)
    corner, over_y, over_x, here = range(4)

    unit = partial(unit_of, grads_ref, lines)

    def load(which, line):
        return pltpu.make_async_copy(
            unit(line, chips[which]), mine_ref.at[which, line], load_sems.at[which, line]
        )

    for other in place.plane():
        send.start(None, small_ref, plane_ref.at[me], plane_sems.at[me], seq=other)
    plane_ref[me] = small_ref[...]

    events = place.events()[::-1]
    for condition, line, _, _ in events:
        for which in range(4):
            theirs = chips[which] + 1 - 2 * place.core
            send.start(
                condition,
                unit(line, theirs),
                sib_ref.at[which, line],
                sib_sems.at[which, line],
                seq=place.sib,
            )
            when(condition, load(which, line).start)

    def add(target, *terms, begin=0, size=unit_rows):
        @pl.loop(0, size // tile)
        def _(step):
            rows = pl.ds(pl.multiple_of(begin + step * tile, tile), tile)
            if len(terms) == 1:
                ref, first = terms[0]
                at = pl.ds(pl.multiple_of(begin - first + step * tile, tile), tile)
                target[rows, :] = target[rows, :] + ref[at, :]
            else:
                total = target[rows, :].astype(f32)
                for ref, first in terms:
                    at = pl.ds(pl.multiple_of(begin - first + step * tile, tile), tile)
                    total = total + ref[at, :].astype(f32)
                target[rows, :] = total.astype(target.dtype)

    def own(which, index):
        condition, line, _, _ = events[index]
        send.arrived(condition, sib_ref.at[which, line], sib_sems.at[which, line])
        when(condition, load(which, line).wait)

    def first(index):
        condition, line, _, _ = events[index]
        own(corner, index)
        target = mine_ref.at[corner, line]
        when(condition, lambda: add(target, (sib_ref.at[corner, line], 0)))
        send.start(
            condition,
            target.at[pl.ds(0, half)],
            corner_a_ref.at[line],
            a_sems.at[line],
            seq=place.xn,
        )
        send.start(
            condition,
            target.at[pl.ds(half, half)],
            corner_b_ref.at[line],
            b_sems.at[line],
            seq=place.yn,
        )

    def second(index):
        condition, line, _, _ = events[index]
        for which, part, sems, begin, to, landing, landing_sems in (
            (over_y, corner_a_ref, a_sems, 0, place.yn, from_y_ref, y_sems),
            (over_x, corner_b_ref, b_sems, half, place.xn, from_x_ref, x_sems),
        ):
            own(which, index)
            send.arrived(condition, part.at[line], sems.at[line])
            target = mine_ref.at[which, line]

            def body(which=which, part=part, begin=begin, target=target):
                add(
                    target,
                    (sib_ref.at[which, line], 0),
                    (part.at[line], begin),
                    begin=begin,
                    size=half,
                )
                add(target, (sib_ref.at[which, line], 0), begin=half - begin, size=half)

            when(condition, body)
            send.start(condition, target, landing.at[line], landing_sems.at[line], seq=to)

    def third(index):
        condition, line, far, side = events[index]
        own(here, index)
        send.arrived(condition, from_x_ref.at[line], x_sems.at[line])
        send.arrived(condition, from_y_ref.at[line], y_sems.at[line])
        target = mine_ref.at[here, line]
        terms = [(ref.at[line], 0) for ref in (sib_ref.at[here], from_x_ref, from_y_ref)]
        if side == 0:
            has_below, has_above = z > 0, z < lines - 1
            add(target, *terms)
            send.arrived(has_below, below_ref.at[line], below_sems.at[line])
            send.arrived(has_above, above_ref.at[line], above_sems.at[line])

            @pl.loop(0, unit_rows // tile)
            def _(step):
                rows = rows_of(step, tile)
                shard_ref[rows, :] = target[rows, :].astype(f32)

            when(has_below, lambda: add(shard_ref, (below_ref.at[line], 0)))
            when(has_above, lambda: add(shard_ref, (above_ref.at[line], 0)))
            return
        landing, sems = (below_ref, below_sems) if side > 0 else (above_ref, above_sems)
        more = both(condition, z > 0) if side > 0 else both(condition, z < lines - 1)
        none = both(condition, z == 0) if side > 0 else both(condition, z == lines - 1)
        send.arrived(more, landing.at[line], sems.at[line])
        when(more, lambda: add(target, *terms, (landing.at[line], 0)))
        when(none, lambda: add(target, *terms))
        send.start(condition, target, landing.at[line], sems.at[line], z=z + side)

    count = len(events)
    first(0)
    first(1)
    for index in range(2, count + 4):
        if index < count:
            first(index)
        if 0 <= index - 2 < count:
            second(index - 2)
        if index == 3:
            for other in place.plane():
                send.arrived(None, plane_ref.at[other], plane_sems.at[other])
            total = plane_ref[0]
            for other in range(1, 8):
                total = total + plane_ref[other]
            plane_sum_ref[...] = total
            line_ref[z] = total
            for other in place.line():
                send.start(None, plane_sum_ref, line_ref.at[z], line_sems.at[z], z=other)
        if 0 <= index - 4 < count:
            third(index - 4)

    for other in place.line():
        send.arrived(None, line_ref.at[other], line_sems.at[other])
    total = line_ref[0]
    for other in range(1, lines):
        total = total + line_ref[other]
    norms_ref[...] = total
    send.finish()


def reduce_grads(lines, grads, small):
    rows, cols = grads.shape
    unit_rows, unit_cols = rows // lines, cols // 8
    half = unit_rows // 2
    any_space = pl.BlockSpec(memory_space=pl.ANY)
    vmem = pl.BlockSpec(memory_space=pltpu.VMEM)
    dma = pltpu.SemaphoreType.DMA
    return pl.pallas_call(
        partial(reduce_kernel, lines),
        out_shape=(
            jax.ShapeDtypeStruct((unit_rows, unit_cols), f32),
            jax.ShapeDtypeStruct(small.shape, f32),
        ),
        in_specs=[any_space, vmem],
        out_specs=(vmem, vmem),
        scratch_shapes=[
            pltpu.VMEM((4, lines, unit_rows, unit_cols), bf16),
            pltpu.VMEM((4, lines, unit_rows, unit_cols), bf16),
            pltpu.VMEM((lines, half, unit_cols), bf16),
            pltpu.VMEM((lines, half, unit_cols), bf16),
            pltpu.VMEM((lines, unit_rows, unit_cols), bf16),
            pltpu.VMEM((lines, unit_rows, unit_cols), bf16),
            pltpu.VMEM((lines, unit_rows, unit_cols), bf16),
            pltpu.VMEM((lines, unit_rows, unit_cols), bf16),
            pltpu.VMEM((8,) + small.shape, f32),
            pltpu.VMEM(small.shape, f32),
            pltpu.VMEM((lines,) + small.shape, f32),
            dma((9 * (2 * lines - 1) + 7 + lines,)),
            dma((4, lines)),
            dma((4, lines)),
            dma((lines,)),
            dma((lines,)),
            dma((lines,)),
            dma((lines,)),
            dma((lines,)),
            dma((lines,)),
            dma((8,)),
            dma((lines,)),
        ],
        compiler_params=pltpu.CompilerParams(
            vmem_limit_bytes=VMEM_BYTES, collective_id=4, has_side_effects=True
        ),
        name="reduce_grads",
    )(grads, small)


def adam_update(grad, weight, first, second, average, rate, decay):
    first = beta_first * first + (1.0 - beta_first) * grad
    second = beta_second * second + (1.0 - beta_second) * grad * grad
    stepped = (
        first / (1.0 - beta_first**STEP) / (jnp.sqrt(second / (1.0 - beta_second**STEP)) + adam_eps)
    )
    weight = weight - rate * (stepped + decay * weight)
    average = ema_decay * average + (1.0 - ema_decay) * weight
    return (first, second, weight, average)


def on_device(
    inputs,
    cotangent,
    neighbours,
    presence,
    row_order,
    w_master,
    w_first,
    w_second,
    w_average,
    n_master,
    n_first,
    n_second,
    n_average,
):
    seqs, tokens, dim = inputs.shape
    heads = dim // HEAD
    devices = lax.axis_size("seq")
    count = seqs * tokens
    length = devices * tokens
    me = lax.axis_index("seq")
    shares = devices // seqs
    held = heads // shares
    pairs = (held + 1) // 2
    width = pairs * LANES
    spare = width - held * HEAD
    sequence, share = me // shares, me % shares

    lines = lax.axis_size("dp")
    planar = devices == 8 and seqs == 4 and spare == 0
    perm = (jnp.arange(dim)[:, None] == row_order[None, :]).astype(bf16)
    perm_att = perm
    if spare:
        perm_att = jnp.pad(perm.reshape(shares, held * HEAD, dim), ((0, 0), (0, spare), (0, 0)))
        perm_att = perm_att.reshape(shares * width, dim)
    x = inputs.reshape(count, dim)
    spans = seqs * neighbours.shape[1]
    each = neighbours.shape[2]
    near = neighbours.reshape(-1, dim)
    live = presence.reshape(-1)
    part = n_master.shape[1]
    if planar:
        small = jnp.pad(n_master.astype(bf16), ((0, 16 - 6), (0, -part % LANES)))
        (
            weights,
            norms,
            hid,
            qkv,
            att,
            lse,
            att_p,
            first,
            hid_p,
            cross_q,
            near_p,
            near_kv,
            co_p,
            second,
        ) = forward(lines, pairs, spans, each, live, w_master, small, inputs, perm, near)
    else:
        weights = lax.all_gather(w_master.astype(bf16), "dp", axis=0, tiled=True)
        weights = lax.all_gather(weights, "seq", axis=1, tiled=True)
        norms = lax.all_gather(n_master.astype(bf16), "dp", axis=1, tiled=True).astype(f32)
        rows = lax.all_to_all(jnp.repeat(inputs, shares, axis=0), "seq", 0, 0)
        rows = rows.reshape(length, dim)
        w_qkv = weights[:, : 3 * dim].reshape(dim, 3, shares, held * HEAD)
        w_qkv = lax.dynamic_index_in_dim(w_qkv, share, axis=2, keepdims=False)
        w_qkv = jnp.pad(w_qkv, ((0, 0), (0, 0), (0, spare))).reshape(dim, 3 * width)
        hid, qkv, att, lse = self_forward(pairs, rows, norms, perm, w_qkv)
        att_tok = (
            lax.all_to_all(att.reshape(devices, tokens, width), "seq", 0, 0)
            .reshape(seqs, shares, tokens, width)
            .transpose(0, 2, 1, 3)
            .reshape(count, shares * width)
        )
        att_p, first, hid_p, cross_q, near_p, near_kv, co_p, second = cross_forward(
            spans, each, live, att_tok, x, norms, perm, perm_att, near, weights
        )
    outputs, gsecond, grads, gnorm_e = feed(
        second, cotangent.reshape(count, dim), norms, perm, weights
    )
    gfirst, gatt_tok, grads, gnorm_c = cross_backward(
        spans,
        each,
        lines if planar else 0,
        live,
        gsecond,
        first,
        norms,
        perm,
        perm_att,
        att_p,
        hid_p,
        cross_q,
        near_p,
        near_kv,
        co_p,
        weights,
        grads,
    )
    if planar:
        others = jnp.concatenate(
            [jnp.zeros((2, dim), f32), gnorm_c, gnorm_e, jnp.zeros((2, dim), f32)], axis=0
        )
        grads, grad_inputs, norm_grads = finish(
            pairs,
            lines,
            qkv,
            att,
            gatt_tok,
            lse,
            hid,
            x,
            gfirst,
            norms,
            perm,
            others,
            weights,
            grads,
        )
        grad_shard, norm_sums = reduce_grads(lines, grads, norm_grads)
        norm_shard = lax.dynamic_slice(norm_sums, (0, lax.axis_index("dp") * part), (6, part))
    else:
        gatt = lax.all_to_all(
            gatt_tok.reshape(seqs, tokens, shares, width)
            .transpose(0, 2, 1, 3)
            .reshape(devices, tokens, width),
            "seq",
            0,
            0,
        ).reshape(length, width)
        gqkv, ghid = self_backward(pairs, qkv, att, gatt, lse, hid, w_qkv)
        parts = (
            lax.all_to_all(ghid.reshape(devices, tokens, dim), "seq", 0, 0)
            .reshape(seqs, shares, tokens, dim)
            .transpose(1, 0, 2, 3)
            .reshape(shares, count, dim)
        )
        grad_inputs, gnorm_a = last_norm(parts, x, gfirst, norms, perm)
        gqkv = gqkv.reshape(dim, 3, 1, width)[..., : held * HEAD]
        gqkv = jnp.where(jnp.arange(shares)[:, None] == share, gqkv, jnp.zeros_like(gqkv))
        grads = lax.dynamic_update_slice(grads, gqkv.reshape(dim, 3 * dim), (0, 0))
        norm_grads = lax.psum(jnp.concatenate([gnorm_a, gnorm_c, gnorm_e], axis=0), "seq")
        partial_sum = lax.psum_scatter(grads, "seq", scatter_dimension=1, tiled=True)
        grad_shard = lax.psum_scatter(partial_sum, "dp", scatter_dimension=0, tiled=True)
        grad_shard = grad_shard.astype(f32)
        norm_shard = lax.psum_scatter(
            norm_grads.astype(bf16), "dp", scatter_dimension=1, tiled=True
        ).astype(f32)
    w_first_new, w_second_new, w_new, w_average_new = adam_update(
        grad_shard, w_master, w_first, w_second, w_average, learn_rate, weight_decay
    )
    n_first_new, n_second_new, n_new, n_average_new = adam_update(
        norm_shard, n_master, n_first, n_second, n_average, norm_rate, 0.0
    )
    return (
        outputs.reshape(seqs, tokens, dim),
        grad_inputs.reshape(seqs, tokens, dim),
        w_first_new,
        w_second_new,
        w_new,
        w_average_new,
        n_first_new,
        n_second_new,
        n_new,
        n_average_new,
    )


def solution(mesh):
    in_specs = (
        P("dp", "seq", None),
        P("dp", "seq", None),
        P("dp", "seq", None, None, None),
        P("dp", "seq", None),
        P(),
        P("dp", "seq"),
        P("dp", "seq"),
        P("dp", "seq"),
        P("dp", "seq"),
        P(None, "dp"),
        P(None, "dp"),
        P(None, "dp"),
        P(None, "dp"),
    )
    out_specs = (
        P("dp", "seq", None),
        P("dp", "seq", None),
        P("dp", "seq"),
        P("dp", "seq"),
        P("dp", "seq"),
        P("dp", "seq"),
        P(None, "dp"),
        P(None, "dp"),
        P(None, "dp"),
        P(None, "dp"),
    )
    return jax.shard_map(
        on_device, mesh=mesh, in_specs=in_specs, out_specs=out_specs, check_vma=False
    )
```

```python
from functools import partial

import jax
import jax.numpy as jnp
from jax import lax
from jax.experimental import pallas as pl
from jax.experimental.pallas import tpu as pltpu
from jax.sharding import PartitionSpec as P

HEAD = 64
STEP = 5
LANES = 128
SCALE = HEAD ** (-0.5)

beta_first = 0.9
beta_second = 0.95
adam_eps = 1e-08
learn_rate = 0.04
norm_rate = 0.6
weight_decay = 0.1
ema_decay = 0.5
norm_eps = 1e-05
masked_score = -1e30
VMEM_BYTES = 60 * 1024 * 1024
bf16 = jnp.bfloat16
f32 = jnp.float32


def mm(left, right):
    return lax.dot_general(left, right, (((1,), (0,)), ((), ())), preferred_element_type=f32)


def nt(left, right):
    return lax.dot_general(left, right, (((1,), (1,)), ((), ())), preferred_element_type=f32)


def tn(left, right):
    return lax.dot_general(left, right, (((0,), (0,)), ((), ())), preferred_element_type=f32)


def params():
    return pltpu.CompilerParams(vmem_limit_bytes=VMEM_BYTES)


def rows_of(index, size):
    return pl.ds(pl.multiple_of(index * size, size), size)


def centre_scale(values):
    centre = jnp.mean(values, axis=-1, keepdims=True)
    centred = values - centre
    spread = jnp.mean(centred * centred, axis=-1, keepdims=True)
    recip = lax.rsqrt(spread + norm_eps)
    return centred * recip, recip


def norm_back(upstream, normed, recip, gain):
    scaled = upstream * gain
    inner = (
        scaled
        - jnp.mean(scaled, axis=-1, keepdims=True)
        - normed * jnp.mean(scaled * normed, axis=-1, keepdims=True)
    )
    return (
        recip * inner,
        jnp.sum(upstream * normed, axis=0, keepdims=True),
        jnp.sum(upstream, axis=0, keepdims=True),
    )


def gelu_parts(value):
    const = 0.7978845608028654
    square = value * value
    bend = jnp.tanh(const * value * (1.0 + 0.044715 * square))
    half = 0.5 * (1.0 + bend)
    slope = half + 0.5 * value * (1.0 - bend * bend) * (const * (1.0 + 3 * 0.044715 * square))
    return value * half, slope


def head_mask(rows, half):
    lane = lax.broadcasted_iota(jnp.int32, (rows, LANES), 1)
    return (lane < HEAD) if half == 0 else (lane >= HEAD)


def pick(mask, value):
    return jnp.where(mask, value, jnp.zeros_like(value))


MESH = pl.DeviceIdType.MESH


class Place:
    def __init__(self, lines):
        self.lines = lines
        self.z = lax.axis_index("dp")
        self.me = lax.axis_index("seq")
        core, x, y = self.me % 2, (self.me // 2) % 2, self.me // 4
        self.core, self.x, self.y, self.chip = core, x, y, self.me // 2
        self.sib = self.me + 1 - 2 * core
        self.xn = self.me + 2 - 4 * x
        self.yn = self.me + 4 - 8 * y
        self.dg = self.xn + 4 - 8 * y

    def events(self):
        found = [(None, self.z, 0, 0)]
        for far in range(1, self.lines):
            found.append((self.z >= far, self.z - far, far, -1))
            found.append((self.z + far < self.lines, self.z + far, far, 1))
        return found

    def plane(self):
        return [lax.rem(self.me + step, 8) for step in range(1, 8)]

    def line(self):
        return [lax.rem(self.z + step, self.lines) for step in range(1, self.lines)]

    def meet(self):
        barrier = pltpu.get_barrier_semaphore()
        for other in self.plane():
            pl.semaphore_signal(
                barrier, inc=1, device_id={"dp": self.z, "seq": other}, device_id_type=MESH
            )
        for other in self.line():
            pl.semaphore_signal(
                barrier, inc=1, device_id={"dp": other, "seq": self.me}, device_id_type=MESH
            )
        pl.semaphore_wait(barrier, 7 + self.lines - 1)


def when(condition, body):
    if condition is None:
        body()
    else:
        pl.when(condition)(body)


def both(first, second):
    if first is None or second is None:
        return second if first is None else first
    return jnp.logical_and(first, second)


class Sender:
    def __init__(self, place, send_sems):
        self.place, self.sems, self.open = place, send_sems, []

    def start(self, condition, src, dst, recv_sem, z=None, seq=None):
        place = self.place
        target = {"dp": place.z if z is None else z, "seq": place.me if seq is None else seq}
        copy = pltpu.make_async_remote_copy(
            src_ref=src,
            dst_ref=dst,
            send_sem=self.sems.at[len(self.open)],
            recv_sem=recv_sem,
            device_id=target,
            device_id_type=MESH,
        )
        self.open.append((condition, copy))
        when(condition, copy.start)

    def arrived(self, condition, ref, recv_sem):
        copy = pltpu.make_async_remote_copy(
            src_ref=ref,
            dst_ref=ref,
            send_sem=self.sems.at[0],
            recv_sem=recv_sem,
            device_id={"dp": self.place.z, "seq": self.place.sib},
            device_id_type=MESH,
        )
        when(condition, copy.wait_recv)

    def finish(self):
        for condition, copy in self.open:
            when(condition, copy.wait_send)


class Weave:
    def __init__(self, steps):
        self.steps = list(steps)

    def some(self, count):
        for _ in range(min(count, len(self.steps))):
            self.steps.pop(0)()

    def rest(self):
        self.some(len(self.steps))


def unit_of(ref, lines, line, seq, begin=0, size=None):
    rows, cols = ref.shape[0] // lines, ref.shape[1] // 8
    size = rows if size is None else size
    return ref.at[
        pl.ds(pl.multiple_of(line * rows + begin, 16), size),
        pl.ds(pl.multiple_of(seq * cols, cols), cols),
    ]


def weight_copies(pairs, dim, wts_ref, w_ref, sems):
    width = pairs * LANES
    first = lax.rem(lax.axis_index("seq"), dim // width) * width
    return [
        pltpu.make_async_copy(
            wts_ref.at[:, pl.ds(pl.multiple_of(first + part * dim, LANES), width)],
            w_ref.at[:, pl.ds(part * width, width)],
            sems.at[part],
        )
        for part in range(3)
    ]


def pair_forward(pair, pairs, qkv_ref, att_ref, lse_ref, between):
    length = att_ref.shape[0]
    tile = 256
    below = lax.broadcasted_iota(jnp.int32, (tile, tile), 1) <= lax.broadcasted_iota(
        jnp.int32, (tile, tile), 0
    )
    masks = [head_mask(tile, 0), head_mask(tile, 1)]
    lane = lax.broadcasted_iota(jnp.int32, (tile, LANES), 1)
    for step in range(length // tile):
        rows = slice(step * tile, (step + 1) * tile)
        query = qkv_ref[pair, rows, :] * SCALE
        keys_here = qkv_ref[pairs + pair, rows, :]
        values_here = qkv_ref[2 * pairs + pair, rows, :]
        outs, logs = [], []
        for half in range(2):
            mine = pick(masks[half], query)
            here = jnp.where(below, nt(mine, keys_here), masked_score)
            peak = jnp.max(here, axis=-1, keepdims=True)
            if step:
                past = nt(mine, qkv_ref[pairs + pair, : step * tile, :])
                peak = jnp.maximum(peak, jnp.max(past, axis=-1, keepdims=True))
                past = jnp.exp(past - peak)
            here = jnp.exp(here - peak)
            total = jnp.sum(here, axis=-1, keepdims=True)
            out = mm(here.astype(bf16), values_here)
            if step:
                total = total + jnp.sum(past, axis=-1, keepdims=True)
                out = out + mm(past.astype(bf16), qkv_ref[2 * pairs + pair, : step * tile, :])
            outs.append(out / total)
            logs.append(peak + jnp.log(total))
        lse_ref[pair, :, rows] = jnp.where(lane == 0, logs[0], logs[1]).T[0:2, :]
        att_ref[rows, pl.ds(pl.multiple_of(pair * LANES, LANES), LANES)] = jnp.where(
            masks[0], outs[0], outs[1]
        ).astype(bf16)
        between()


def norm_rows(x_ref, norms, perm_ref, hid_ref):
    tile = 256

    @pl.loop(0, x_ref.shape[0] // tile)
    def _(step):
        rows = rows_of(step, tile)
        normed, _ = centre_scale(x_ref[rows, :].astype(f32))
        hidden = (normed * norms[0:1, :] + norms[1:2, :]).astype(bf16)
        hid_ref[rows, :] = mm(hidden, perm_ref[...]).astype(bf16)


def triple_part(part, pairs, hid_ref, w_ref, qkv_ref):
    width = pairs * LANES
    triple = mm(hid_ref[...], w_ref[:, part * width : (part + 1) * width]).astype(bf16)
    for pair in range(pairs):
        qkv_ref[part * pairs + pair] = triple[:, pair * LANES : (pair + 1) * LANES]


def self_forward_kernel(
    pairs, x_ref, norms_ref, perm_ref, w_ref, hid_ref, qkv_ref, att_ref, lse_ref
):
    norm_rows(x_ref, norms_ref, perm_ref, hid_ref)
    for part in range(3):
        triple_part(part, pairs, hid_ref, w_ref, qkv_ref)

    @pl.loop(0, pairs)
    def _(pair):
        pair_forward(pair, pairs, qkv_ref, att_ref, lse_ref, lambda: None)


def self_forward(pairs, x, norms, perm, w):
    length, dim = x.shape
    return pl.pallas_call(
        partial(self_forward_kernel, pairs),
        out_shape=(
            jax.ShapeDtypeStruct((length, dim), bf16),
            jax.ShapeDtypeStruct((3 * pairs, length, LANES), bf16),
            jax.ShapeDtypeStruct((length, pairs * LANES), bf16),
            jax.ShapeDtypeStruct((pairs, 2, length), f32),
        ),
        compiler_params=params(),
        name="self_forward",
    )(x, norms, perm, w)


def pair_backward(pair, pairs, qkv_ref, att_ref, gatt_ref, lse_ref, grad_ref, acc_ref, between):
    length = att_ref.shape[0]
    width = pairs * LANES
    tile = 256
    above = lax.broadcasted_iota(jnp.int32, (tile, tile), 0) <= lax.broadcasted_iota(
        jnp.int32, (tile, tile), 1
    )
    masks = [head_mask(tile, 0), head_mask(tile, 1)]
    lanes = pl.ds(pl.multiple_of(pair * LANES, LANES), LANES)
    for step in range(length // tile):
        rows = slice(step * tile, (step + 1) * tile)
        query = qkv_ref[pair, rows, :] * SCALE
        grad_out = gatt_ref[rows, lanes]
        product = grad_out.astype(f32) * att_ref[rows, lanes].astype(f32)
        queries = [pick(masks[half], query) for half in range(2)]
        grads = [pick(masks[half], grad_out) for half in range(2)]
        deltas = [jnp.sum(pick(masks[half], product).T, axis=0, keepdims=True) for half in range(2)]
        grad_query = [None, None]
        for other in range(step + 1):
            cols = slice(other * tile, (other + 1) * tile)
            keys = qkv_ref[pairs + pair, cols, :]
            values = qkv_ref[2 * pairs + pair, cols, :]
            key_part = value_part = None
            for half in range(2):
                scores = nt(keys, queries[half])
                if other == step:
                    scores = jnp.where(above, scores, masked_score)
                probs = jnp.exp(scores - lse_ref[pair, half : half + 1, rows])
                grad_scores = (probs * (nt(values, grads[half]) - deltas[half])).astype(bf16)
                query_term = tn(grad_scores, keys)
                grad_query[half] = (
                    query_term if grad_query[half] is None else grad_query[half] + query_term
                )
                key_term = mm(grad_scores, queries[half])
                value_term = mm(probs.astype(bf16), grads[half])
                key_part = key_term if key_part is None else key_part + key_term
                value_part = value_term if value_part is None else value_part + value_term
            if other == step:
                acc_ref[0, cols, :] = key_part
                acc_ref[1, cols, :] = value_part
            else:
                acc_ref[0, cols, :] += key_part
                acc_ref[1, cols, :] += value_part
        grad_ref[rows, lanes] = (jnp.where(masks[0], grad_query[0], grad_query[1]) * SCALE).astype(
            bf16
        )
        between()
    for part in range(2):
        lanes_to = pl.ds(pl.multiple_of((part + 1) * width + pair * LANES, LANES), LANES)
        grad_ref[:, lanes_to] = acc_ref[part].astype(bf16)


def self_backward_kernel(
    pairs,
    qkv_ref,
    att_ref,
    gatt_ref,
    lse_ref,
    hid_ref,
    w_ref,
    gw_ref,
    ghid_ref,
    grad_ref,
    acc_ref,
):
    length = att_ref.shape[0]
    width = pairs * LANES
    attention = (qkv_ref, att_ref, gatt_ref, lse_ref, grad_ref, acc_ref)

    @pl.loop(0, pairs)
    def _(pair):
        pair_backward(pair, pairs, *attention, lambda: None)

    hidden_t = hid_ref[...].T
    for part in range(3):
        cols = slice(part * width, (part + 1) * width)
        gw_ref[:, cols] = mm(hidden_t, grad_ref[:, cols]).astype(bf16)
    for begin in range(0, length, 256):
        rows = slice(begin, begin + 256)
        ghid_ref[rows, :] = nt(grad_ref[rows, :], w_ref[...]).astype(bf16)


def self_backward(pairs, qkv, att, gatt, lse, hid, w):
    length, dim = hid.shape
    width = pairs * LANES
    return pl.pallas_call(
        partial(self_backward_kernel, pairs),
        out_shape=(
            jax.ShapeDtypeStruct((dim, 3 * width), bf16),
            jax.ShapeDtypeStruct((length, dim), bf16),
        ),
        scratch_shapes=[
            pltpu.VMEM((length, 3 * width), bf16),
            pltpu.VMEM((2, length, LANES), f32),
        ],
        compiler_params=params(),
        name="self_backward",
    )(qkv, att, gatt, lse, hid, w)


def finish_kernel(
    pairs,
    lines,
    qkv_ref,
    att_ref,
    gatt_ref,
    lse_ref,
    hid_ref,
    x_ref,
    gfirst_ref,
    norms_ref,
    perm_ref,
    others_ref,
    wts_ref,
    _,
    all_ref,
    gin_ref,
    small_ref,
    grad_ref,
    acc_ref,
    gw_ref,
    w_ref,
    sems,
    ghid_ref,
    gsib_ref,
    parts_ref,
    gsib_sems,
    part_sems,
    send_sems,
):
    length, dim = hid_ref.shape
    width = pairs * LANES
    tokens = length // 8
    place = Place(lines)
    me, core = place.me, place.core
    place.meet()
    send = Sender(place, send_sems)
    copies = weight_copies(pairs, dim, wts_ref, w_ref, sems)
    for copy in copies:
        copy.start()

    share_count = dim // width
    share = lax.rem(me, share_count)
    gw_ref[3] = jnp.zeros_like(gw_ref[3])
    outs = []
    for part in range(3):
        for other in range(1, share_count):
            first = part * dim + lax.rem(share + other, share_count) * width
            outs.append(
                pltpu.make_async_copy(
                    gw_ref.at[3],
                    all_ref.at[:, pl.ds(pl.multiple_of(first, LANES), width)],
                    sems.at[6 + part * (share_count - 1) + other - 1],
                )
            )
            outs[-1].start()

    attention = (qkv_ref, att_ref, gatt_ref, lse_ref, grad_ref, acc_ref)

    @pl.loop(0, pairs)
    def _(pair):
        pair_backward(pair, pairs, *attention, lambda: None)

    def token_rows(device):
        return pl.ds(pl.multiple_of(device * tokens, tokens), tokens)

    for copy in copies:
        copy.wait()
    for begin in range(0, length, 256):
        rows = slice(begin, begin + 256)
        ghid_ref[rows, :] = nt(grad_ref[rows, :], w_ref[...]).astype(bf16)
    chips = (place.xn // 2, place.yn // 2, place.dg // 2, place.chip)
    for chip in chips:
        theirs = chip * 2 + 1 - core
        send.start(
            None, ghid_ref.at[token_rows(theirs)], gsib_ref.at[chip], gsib_sems.at[chip], seq=place.sib
        )
    for chip in chips:
        send.arrived(None, gsib_ref.at[chip], gsib_sems.at[chip])
        rows = token_rows(chip * 2 + core)
        total = (ghid_ref[rows, :].astype(f32) + gsib_ref[chip].astype(f32)).astype(bf16)
        if chip is place.chip:
            parts_ref[chip] = total
        else:
            ghid_ref[rows, :] = total
            send.start(
                None,
                ghid_ref.at[rows],
                parts_ref.at[place.chip],
                part_sems.at[place.chip],
                seq=chip * 2 + core,
            )

    hidden_t = hid_ref[...].T
    for part in range(3):
        gw_ref[part] = mm(hidden_t, grad_ref[:, part * width : (part + 1) * width]).astype(bf16)
        first = part * dim + share * width
        outs.append(
            pltpu.make_async_copy(
                gw_ref.at[part],
                all_ref.at[:, pl.ds(pl.multiple_of(first, LANES), width)],
                sems.at[3 + part],
            )
        )
        outs[-1].start()

    for chip in chips[:3]:
        send.arrived(None, parts_ref.at[chip], part_sems.at[chip])
    gain_sum = shift_sum = None
    for chip in range(4):
        rows = slice(chip * tokens, (chip + 1) * tokens)
        upstream = nt(parts_ref[chip], perm_ref[...])
        normed, recip = centre_scale(x_ref[rows, :].astype(f32))
        back, gain, shift = norm_back(upstream, normed, recip, norms_ref[0:1, :])
        gin_ref[rows, :] = gfirst_ref[rows, :] + back
        gain_sum = gain if gain_sum is None else gain_sum + gain
        shift_sum = shift if shift_sum is None else shift_sum + shift
    small_ref[...] = others_ref[...]
    small_ref[0:1, :] = gain_sum
    small_ref[1:2, :] = shift_sum
    for copy in outs:
        copy.wait()
    send.finish()


def finish(pairs, lines, qkv, att, gatt, lse, hid, x, gfirst, norms, perm, others, weights, grads):
    length, dim = hid.shape
    width = pairs * LANES
    count = x.shape[0]
    tokens = length // 8
    any_space = pl.BlockSpec(memory_space=pl.ANY)
    vmem = pl.BlockSpec(memory_space=pltpu.VMEM)
    dma = pltpu.SemaphoreType.DMA
    return pl.pallas_call(
        partial(finish_kernel, pairs, lines),
        out_shape=(
            jax.ShapeDtypeStruct(grads.shape, bf16),
            jax.ShapeDtypeStruct((count, dim), f32),
            jax.ShapeDtypeStruct((8, dim), f32),
        ),
        in_specs=[vmem] * 10 + [any_space] * 2,
        out_specs=(any_space, vmem, vmem),
        scratch_shapes=[
            pltpu.VMEM((length, 3 * width), bf16),
            pltpu.VMEM((2, length, LANES), f32),
            pltpu.VMEM((4, dim, width), bf16),
            pltpu.VMEM((dim, 3 * width), bf16),
            dma((6 + 3 * (dim // width),)),
            pltpu.VMEM((length, dim), bf16),
            pltpu.VMEM((4, tokens, dim), bf16),
            pltpu.VMEM((4, tokens, dim), bf16),
            dma((4,)),
            dma((4,)),
            dma((8,)),
        ],
        input_output_aliases={11: 0},
        compiler_params=pltpu.CompilerParams(
            vmem_limit_bytes=VMEM_BYTES, collective_id=3, has_side_effects=True
        ),
        name="finish",
    )(qkv, att, gatt, lse, hid, x, gfirst, norms, perm, others, weights, grads)


def spread_heads(block, rows, group):
    lane = lax.broadcasted_iota(jnp.int32, block.shape, 1) // HEAD
    return jnp.concatenate([pick(lane == head, block) for head in range(group)], axis=0)


def gather_heads(stacked, rows, group):
    lane = lax.broadcasted_iota(jnp.int32, (rows, stacked.shape[1]), 1) // HEAD
    out = None
    for head in range(group):
        part = pick(lane == head, stacked[head * rows : (head + 1) * rows])
        out = part if out is None else out + part
    return out


def live_keys(presence_ref, span, shape, axis, neighbours, each):
    index = lax.broadcasted_iota(jnp.int32, shape, axis) // each
    live = jnp.zeros(shape, f32)
    anyone = None
    for which in range(neighbours):
        here = presence_ref[span * neighbours + which]
        there = jnp.where(here > 0, 1.0, 0.0).astype(f32)
        live = jnp.where(index == which, there, live)
        anyone = here if anyone is None else jnp.maximum(anyone, here)
    return live, anyone.astype(f32)


def span_forward(span, spans, neighbours, presence_ref, cross_q_ref, near_kv_ref, cross_ref):
    count, dim = cross_q_ref.shape
    span_len = count // spans
    near = near_kv_ref.shape[0] // spans
    group = 256 // HEAD
    rows = rows_of(span, span_len)
    keys = rows_of(span, near)
    live, anyone = live_keys(presence_ref, span, (1, near), 1, neighbours, near // neighbours)
    for begin in range(0, dim, group * HEAD):
        lanes = slice(begin, begin + group * HEAD)
        lanes_v = slice(dim + begin, dim + begin + group * HEAD)
        query = spread_heads(cross_q_ref[rows, lanes] * SCALE, span_len, group)
        scores = jnp.where(live > 0, nt(query, near_kv_ref[keys, lanes]), masked_score)
        peak = jnp.max(scores, axis=-1, keepdims=True)
        expon = jnp.exp(scores - peak) * live
        total = jnp.sum(expon, axis=-1, keepdims=True) + 1.0 - anyone
        out = mm(expon.astype(bf16), near_kv_ref[keys, lanes_v]) / total
        cross_ref[rows, lanes] = gather_heads(out, span_len, group).astype(bf16)


def cross_forward_kernel(
    spans,
    neighbours,
    presence_ref,
    att_ref,
    x_ref,
    norms_ref,
    perm_ref,
    perm_att_ref,
    near_ref,
    w_out_ref,
    w_cq_ref,
    w_ck_ref,
    w_cv_ref,
    w_co_ref,
    att_p_ref,
    first_ref,
    hid_p_ref,
    cross_q_ref,
    near_p_ref,
    near_kv_ref,
    co_p_ref,
    second_ref,
    cross_ref,
):
    count, dim = x_ref.shape
    rows_near = near_ref.shape[0]
    tile = 512

    att_p_ref[...] = mm(att_ref[...], perm_att_ref[...]).astype(bf16)
    first_ref[...] = x_ref[...].astype(f32) + mm(att_p_ref[...], w_out_ref[...])

    normed, _ = centre_scale(first_ref[...])
    hidden = (normed * norms_ref[2:3, :] + norms_ref[3:4, :]).astype(bf16)
    hid_p_ref[...] = mm(hidden, perm_ref[...]).astype(bf16)
    cross_q_ref[...] = mm(hid_p_ref[...], w_cq_ref[...]).astype(bf16)

    @pl.loop(0, rows_near // tile)
    def _(step):
        rows = rows_of(step, tile)
        near_p_ref[rows, :] = mm(near_ref[rows, :], perm_ref[...]).astype(bf16)
        near_kv_ref[rows, :dim] = mm(near_p_ref[rows, :], w_ck_ref[...]).astype(bf16)
        near_kv_ref[rows, dim:] = mm(near_p_ref[rows, :], w_cv_ref[...]).astype(bf16)

    @pl.loop(0, spans)
    def _(span):
        span_forward(span, spans, neighbours, presence_ref, cross_q_ref, near_kv_ref, cross_ref)

    co_p_ref[...] = mm(cross_ref[...], perm_ref[...]).astype(bf16)
    second_ref[...] = first_ref[...] + mm(co_p_ref[...], w_co_ref[...])


def column_block(rows, width, index):
    return pl.BlockSpec((rows, width), lambda *_: (0, index), pipeline_mode=pl.Buffered(1))


def whole(array):
    return pl.BlockSpec(array.shape, lambda *_: (0,) * array.ndim, pipeline_mode=pl.Buffered(1))


def whole_shape(shape):
    return pl.BlockSpec(shape, lambda *_: (0,) * len(shape), pipeline_mode=pl.Buffered(1))


def cross_forward(spans, neighbours, presence, att, x, norms, perm, perm_att, near, weights):
    count, dim = x.shape
    rows_near = near.shape[0]
    out_shape = (
        jax.ShapeDtypeStruct((count, dim), bf16),
        jax.ShapeDtypeStruct((count, dim), f32),
        jax.ShapeDtypeStruct((count, dim), bf16),
        jax.ShapeDtypeStruct((count, dim), bf16),
        jax.ShapeDtypeStruct((rows_near, dim), bf16),
        jax.ShapeDtypeStruct((rows_near, 2 * dim), bf16),
        jax.ShapeDtypeStruct((count, dim), bf16),
        jax.ShapeDtypeStruct((count, dim), f32),
    )
    operands = (att, x, norms, perm, perm_att, near)
    return pl.pallas_call(
        partial(cross_forward_kernel, spans, neighbours),
        out_shape=out_shape,
        grid=(1,),
        in_specs=[pl.BlockSpec(memory_space=pltpu.SMEM)]
        + [whole(op) for op in operands]
        + [column_block(dim, dim, index) for index in (3, 4, 5, 6, 7)],
        out_specs=tuple(whole_shape(shape.shape) for shape in out_shape),
        scratch_shapes=[pltpu.VMEM((count, dim), bf16)],
        compiler_params=params(),
        name="cross_forward",
    )(presence, *operands, *([weights] * 5))


def feed_kernel(
    second_ref,
    cot_ref,
    norms_ref,
    perm_ref,
    w_up_ref,
    w_down_ref,
    out_ref,
    gsecond_ref,
    all_ref,
    gnorm_ref,
    hid_p_ref,
    hid_t_ref,
    cot_p_ref,
    cot_t_ref,
    result_ref,
    back_ref,
    gup_ref,
    gdown_ref,
    sems,
):
    step = pl.program_id(0)
    last = pl.num_programs(0) - 1
    slot = lax.rem(step, 2)
    dim, tile = w_up_ref.shape

    def copies(step, slot):
        up = pl.multiple_of(8 * dim + step * tile, tile)
        down = pl.multiple_of(8 * dim + (last + 1 + step) * tile, tile)
        return (
            pltpu.make_async_copy(gup_ref.at[slot], all_ref.at[:, pl.ds(up, tile)], sems.at[0, slot]),
            pltpu.make_async_copy(
                gdown_ref.at[slot], all_ref.at[:, pl.ds(down, tile)], sems.at[1, slot]
            ),
        )

    @pl.when(step >= 2)
    def _():
        for copy in copies(step - 2, slot):
            copy.wait()

    @pl.when(step == 0)
    def _():
        normed, _ = centre_scale(second_ref[...])
        hidden = (normed * norms_ref[4:5, :] + norms_ref[5:6, :]).astype(bf16)
        hid_p_ref[...] = mm(hidden, perm_ref[...]).astype(bf16)
        hid_t_ref[...] = hid_p_ref[...].T
        cot_p_ref[...] = mm(cot_ref[...], perm_ref[...]).astype(bf16)
        cot_t_ref[...] = cot_p_ref[...].T
        result_ref[...] = jnp.zeros_like(result_ref)
        back_ref[...] = jnp.zeros_like(back_ref)

    upward = mm(hid_p_ref[...], w_up_ref[...])
    active, slope = gelu_parts(upward)
    active = active.astype(bf16)
    result_ref[...] += nt(active, w_down_ref[...])
    gdown_ref[slot] = mm(cot_t_ref[...], active).astype(bf16)
    grad_up = (mm(cot_p_ref[...], w_down_ref[...]) * slope).astype(bf16)
    gup_ref[slot] = mm(hid_t_ref[...], grad_up).astype(bf16)
    for copy in copies(step, slot):
        copy.start()
    back_ref[...] += nt(grad_up, w_up_ref[...])

    @pl.when(step == last)
    def _():
        out_ref[...] = (
            second_ref[...] + nt(result_ref[...].astype(bf16), perm_ref[...])
        ).astype(bf16)
        upstream = nt(back_ref[...].astype(bf16), perm_ref[...])
        normed, recip = centre_scale(second_ref[...])
        back, gain, shift = norm_back(upstream, normed, recip, norms_ref[4:5, :])
        gsecond_ref[...] = cot_ref[...].astype(f32) + back
        gnorm_ref[0:1, :] = gain
        gnorm_ref[1:2, :] = shift
        for which in (step - 1, step):
            for copy in copies(which, lax.rem(which, 2)):
                copy.wait()


def feed(second, cot, norms, perm, weights):
    count, dim = second.shape
    ffw = (weights.shape[1] - 8 * dim) // 2
    tile = 512
    first_up = 8 * dim // tile
    first_down = (8 * dim + ffw) // tile
    out_shape = (
        jax.ShapeDtypeStruct((count, dim), bf16),
        jax.ShapeDtypeStruct((count, dim), f32),
        jax.ShapeDtypeStruct(weights.shape, bf16),
        jax.ShapeDtypeStruct((2, dim), f32),
    )
    operands = (second, cot, norms, perm)
    return pl.pallas_call(
        feed_kernel,
        out_shape=out_shape,
        grid=(ffw // tile,),
        in_specs=[whole(op) for op in operands]
        + [
            pl.BlockSpec((dim, tile), lambda i: (0, first_up + i)),
            pl.BlockSpec((dim, tile), lambda i: (0, first_down + i)),
        ],
        out_specs=(
            whole_shape((count, dim)),
            whole_shape((count, dim)),
            pl.BlockSpec(memory_space=pl.ANY),
            whole_shape((2, dim)),
        ),
        scratch_shapes=[
            pltpu.VMEM((count, dim), bf16),
            pltpu.VMEM((dim, count), bf16),
            pltpu.VMEM((count, dim), bf16),
            pltpu.VMEM((dim, count), bf16),
            pltpu.VMEM((count, dim), f32),
            pltpu.VMEM((count, dim), f32),
            pltpu.VMEM((2, dim, tile), bf16),
            pltpu.VMEM((2, dim, tile), bf16),
            pltpu.SemaphoreType.DMA((2, 2)),
        ],
        compiler_params=params(),
        name="feed",
    )(*operands, weights, weights)


def cross_backward_kernel(
    spans,
    neighbours,
    lines,
    presence_ref,
    gsecond_ref,
    first_ref,
    norms_ref,
    perm_ref,
    perm_att_ref,
    att_p_ref,
    hid_p_ref,
    cross_q_ref,
    near_p_ref,
    near_kv_ref,
    co_p_ref,
    w_out_ref,
    w_cq_ref,
    w_co_ref,
    _,
    gfirst_ref,
    gatt_ref,
    all_ref,
    gnorm_ref,
    *rest,
):
    count, dim = first_ref.shape
    rows_near = near_p_ref.shape[0]
    span_len = count // spans
    near = rows_near // spans
    group = 256 // HEAD
    outs = []
    if lines:
        gatt_tok_ref, row_sems, send_sems = rest[5:]
        place = Place(lines)
        place.meet()
        send = Sender(place, send_sems)
    gco_ref, gcq_ref, gnear_ref, gw_ref, sems = rest[:5]

    def keep(index, value):
        slot = len(outs) % 3
        if len(outs) >= 3:
            outs[-3].wait()
        gw_ref[slot] = value.astype(bf16)
        outs.append(
            pltpu.make_async_copy(
                gw_ref.at[slot],
                all_ref.at[:, pl.ds((3 + index) * dim, dim)],
                sems.at[index],
            )
        )
        outs[-1].start()

    upper = gsecond_ref[...].astype(bf16)
    gco_ref[...] = nt(nt(upper, w_co_ref[...]).astype(bf16), perm_ref[...]).astype(bf16)

    def one_span(span):
        rows = rows_of(span, span_len)
        keys = rows_of(span, near)
        live, anyone = live_keys(presence_ref, span, (near, 1), 0, neighbours, near // neighbours)
        for begin in range(0, dim, group * HEAD):
            lanes = slice(begin, begin + group * HEAD)
            lanes_v = slice(dim + begin, dim + begin + group * HEAD)
            query = spread_heads(cross_q_ref[rows, lanes] * SCALE, span_len, group)
            grad_out = spread_heads(gco_ref[rows, lanes], span_len, group)
            key = near_kv_ref[keys, lanes]
            scores = jnp.where(live > 0, nt(key, query), masked_score)
            peak = jnp.max(scores, axis=0, keepdims=True)
            expon = jnp.exp(scores - peak) * live
            total = jnp.sum(expon, axis=0, keepdims=True) + 1.0 - anyone
            probs = expon * (1.0 / total)
            grad_probs = nt(near_kv_ref[keys, lanes_v], grad_out)
            inner = jnp.sum(probs * grad_probs, axis=0, keepdims=True)
            grad_scores = (probs * (grad_probs - inner)).astype(bf16)
            gcq_ref[rows, lanes] = (
                gather_heads(tn(grad_scores, key), span_len, group) * SCALE
            ).astype(bf16)
            gnear_ref[keys, lanes] = mm(grad_scores, query).astype(bf16)
            gnear_ref[keys, lanes_v] = mm(probs.astype(bf16), grad_out).astype(bf16)

    pl.loop(0, spans)(one_span)

    upstream = nt(nt(gcq_ref[...], w_cq_ref[...]).astype(bf16), perm_ref[...])
    normed, recip = centre_scale(first_ref[...])
    back, gain, shift = norm_back(upstream, normed, recip, norms_ref[2:3, :])
    gnorm_ref[0:1, :] = gain
    gnorm_ref[1:2, :] = shift
    gfirst_ref[...] = gsecond_ref[...] + back
    lower = gfirst_ref[...].astype(bf16)
    gatt = nt(nt(lower, w_out_ref[...]).astype(bf16), perm_att_ref[...]).astype(bf16)
    if lines:
        width = gatt_ref.shape[1]
        tokens = gatt_ref.shape[0] // 8
        shares = gatt.shape[1] // width
        gatt_tok_ref[...] = gatt

        def block(device):
            return gatt_tok_ref.at[
                pl.ds(pl.multiple_of(device // shares * tokens, tokens), tokens),
                pl.ds(pl.multiple_of(device % shares * width, width), width),
            ]

        def landing(device):
            return gatt_ref.at[pl.ds(pl.multiple_of(device * tokens, tokens), tokens)]

        for other in place.plane():
            send.start(None, block(other), landing(place.me), row_sems.at[place.me], seq=other)
        own = pltpu.make_async_copy(block(place.me), landing(place.me), row_sems.at[place.me])
        own.start()
    else:
        gatt_ref[...] = gatt
    keep(4, mm(co_p_ref[...].T, upper))
    near_t = near_p_ref[...].T
    for part in range(2):
        keep(2 + part, mm(near_t, gnear_ref[:, part * dim : (part + 1) * dim]))
    keep(1, mm(hid_p_ref[...].T, gcq_ref[...]))
    keep(0, mm(att_p_ref[...].T, lower))
    if lines:
        for other in place.plane():
            send.arrived(None, landing(other), row_sems.at[other])
        own.wait()
        send.finish()
    for copy in outs[-3:]:
        copy.wait()


def cross_backward(
    spans,
    neighbours,
    lines,
    presence,
    gsecond,
    first,
    norms,
    perm,
    perm_att,
    att_p,
    hid_p,
    cross_q,
    near_p,
    near_kv,
    co_p,
    weights,
    grads,
):
    count, dim = first.shape
    rows_near = near_p.shape[0]
    gatt_shape = (count, perm_att.shape[0])
    out_shape = [
        jax.ShapeDtypeStruct((count, dim), f32),
        jax.ShapeDtypeStruct(gatt_shape, bf16),
        jax.ShapeDtypeStruct(grads.shape, bf16),
        jax.ShapeDtypeStruct((2, dim), f32),
    ]
    scratch = [
        pltpu.VMEM((count, dim), bf16),
        pltpu.VMEM((count, dim), bf16),
        pltpu.VMEM((rows_near, 2 * dim), bf16),
        pltpu.VMEM((3, dim, dim), bf16),
        pltpu.SemaphoreType.DMA((5,)),
    ]
    compiler_params = params()
    if lines:
        out_shape[1] = jax.ShapeDtypeStruct((2 * count, gatt_shape[1] // 2), bf16)
        scratch += [
            pltpu.VMEM(gatt_shape, bf16),
            pltpu.SemaphoreType.DMA((8,)),
            pltpu.SemaphoreType.DMA((8,)),
        ]
        compiler_params = pltpu.CompilerParams(
            vmem_limit_bytes=VMEM_BYTES, collective_id=2, has_side_effects=True
        )
    operands = (
        gsecond,
        first,
        norms,
        perm,
        perm_att,
        att_p,
        hid_p,
        cross_q,
        near_p,
        near_kv,
        co_p,
    )
    return pl.pallas_call(
        partial(cross_backward_kernel, spans, neighbours, lines),
        out_shape=out_shape,
        grid=(1,),
        in_specs=[pl.BlockSpec(memory_space=pltpu.SMEM)]
        + [whole(op) for op in operands]
        + [column_block(dim, dim, index) for index in (3, 4, 7)]
        + [pl.BlockSpec(memory_space=pl.ANY)],
        out_specs=tuple(
            pl.BlockSpec(memory_space=pl.ANY) if index == 2 else whole_shape(shape.shape)
            for index, shape in enumerate(out_shape)
        ),
        scratch_shapes=scratch,
        input_output_aliases={len(operands) + 4: 2},
        compiler_params=compiler_params,
        name="cross_backward",
    )(presence, *operands, *([weights] * 3), grads)


def last_norm_kernel(parts_ref, x_ref, gfirst_ref, norms_ref, perm_ref, out_ref, gnorm_ref):
    total = parts_ref[0].astype(f32)
    for part in range(1, parts_ref.shape[0]):
        total = total + parts_ref[part].astype(f32)
    upstream = nt(total.astype(bf16), perm_ref[...])
    normed, recip = centre_scale(x_ref[...].astype(f32))
    back, gain, shift = norm_back(upstream, normed, recip, norms_ref[0:1, :])
    out_ref[...] = gfirst_ref[...] + back
    gnorm_ref[0:1, :] = gain
    gnorm_ref[1:2, :] = shift


def last_norm(parts, x, gfirst, norms, perm):
    count, dim = x.shape
    return pl.pallas_call(
        last_norm_kernel,
        out_shape=(
            jax.ShapeDtypeStruct((count, dim), f32),
            jax.ShapeDtypeStruct((2, dim), f32),
        ),
        compiler_params=params(),
        name="last_norm",
    )(parts, x, gfirst, norms, perm)


def forward_kernel(
    lines,
    pairs,
    spans,
    neighbours,
    presence_ref,
    w_ref,
    norm_ref,
    x_ref,
    perm_ref,
    near_ref,
    wts_ref,
    norms_ref,
    hid_ref,
    qkv_ref,
    att_ref,
    lse_ref,
    att_p_ref,
    first_ref,
    hid_p_ref,
    cross_q_ref,
    near_p_ref,
    near_kv_ref,
    co_p_ref,
    second_ref,
    own_ref,
    small_ref,
    rows_ref,
    w_qkv_ref,
    w_mid_ref,
    att_tok_ref,
    cross_ref,
    send_sems,
    z_sems,
    y_sems,
    x_sems,
    sib_sems,
    norm_sems,
    row_sems,
    att_sems,
    local_sems,
    qkv_sems,
    mid_sems,
):
    place = Place(lines)
    z, me, core = place.z, place.me, place.core
    length, dim = hid_ref.shape
    width = pairs * LANES
    tokens = length // 8
    own_ref[...] = w_ref[...].astype(bf16)
    place.meet()
    send = Sender(place, send_sems)
    cols = own_ref.shape[1] // 2

    def unit(line, seq, half):
        rows = own_ref.shape[0]
        return wts_ref.at[
            pl.ds(pl.multiple_of(line * rows, rows), rows),
            pl.ds(pl.multiple_of((seq * 2 + half) * cols, cols), cols),
        ]

    low, high = place.y == 0, place.y == 1
    events = place.events()
    keep = pltpu.make_async_copy(own_ref, unit_of(wts_ref, lines, z, me), local_sems.at[0])
    keep.start()

    def crossing(row, of=core):
        return row * 4 + (1 - place.x) * 2 + of

    def pieces(slot):
        far, half = slot // 2, slot % 2
        found = events[:1] if far == 0 else events[2 * far - 1 : 2 * far + 1]
        return [(*event, half) for event in found]

    def source(line, far, half):
        return own_ref.at[:, pl.ds(half * cols, cols)] if far == 0 else unit(line, me, half)

    def own_unit(slot):
        for condition, line, far, side, half in pieces(slot):
            mine, src = unit(line, me, half), source(line, far, half)
            if far:
                send.arrived(condition, mine, z_sems.at[line, half])
            below, above = both(condition, z > 0), both(condition, z < lines - 1)
            if side >= 0:
                send.start(below, src, mine, z_sems.at[line, half], z=z - 1)
            if side <= 0:
                send.start(above, src, mine, z_sems.at[line, half], z=z + 1)
            send.start(condition, src, mine, y_sems.at[line, half], seq=place.yn)
            send.start(both(condition, low), src, mine, x_sems.at[0, line, half], seq=place.xn)
            send.start(condition, src, mine, sib_sems.at[0, line, half], seq=place.sib)

    def from_y(slot):
        for condition, line, _, _, half in pieces(slot):
            theirs = unit(line, place.yn, half)
            send.arrived(condition, theirs, y_sems.at[line, half])
            on = both(condition, high)
            send.start(on, theirs, theirs, x_sems.at[0, line, half], seq=place.xn)
            send.start(condition, theirs, theirs, sib_sems.at[1, line, half], seq=place.sib)

    def from_x(row, slot):
        for condition, line, _, _, half in pieces(slot):
            theirs = unit(line, crossing(row), half)
            send.arrived(condition, theirs, x_sems.at[row, line, half])
            sem = sib_sems.at[2 + row, line, half]
            send.start(condition, theirs, theirs, sem, seq=place.sib)

    def late_x(slot):
        for condition, line, far, _, half in pieces(slot):
            mine, theirs = unit(line, me, half), unit(line, place.yn, half)
            src, sem = source(line, far, half), x_sems.at[1, line, half]
            send.start(both(condition, high), src, mine, sem, seq=place.xn)
            send.start(both(condition, low), theirs, theirs, sem, seq=place.xn)

    def from_sib(line, group, condition, seq):
        for half in range(2):
            theirs = unit(line, seq, half)
            send.arrived(condition, theirs, sib_sems.at[group, line, half])

    def row_block(seq):
        return rows_ref.at[pl.ds(pl.multiple_of(seq * tokens, tokens), tokens)]

    own_unit(0)
    own_unit(1)
    own_rows = pltpu.make_async_copy(x_ref.at[place.chip], row_block(me), local_sems.at[1])
    own_rows.start()
    send.start(None, x_ref.at[place.chip], row_block(me), row_sems.at[me], seq=place.sib)
    others = (place.xn, place.yn, place.dg)
    for other in others:
        send.start(None, x_ref.at[other // 2], row_block(me), row_sems.at[me], seq=other)
    for other in place.line():
        send.start(None, norm_ref, small_ref.at[z], norm_sems.at[z], z=other)
    small_ref[z] = norm_ref[...]

    @pl.loop(0, near_ref.shape[0] // 512)
    def _(step):
        rows = rows_of(step, 512)
        near_p_ref[rows, :] = mm(near_ref[rows, :], perm_ref[...]).astype(bf16)

    slots = 2 * lines

    def advance(slot):
        if slot < slots:
            own_unit(slot)
        if slot - 1 < slots:
            from_y(slot - 1)
        from_x(0, slot - 2)

    from_y(0)
    advance(2)
    advance(3)
    for other in others:
        send.arrived(None, row_block(other), row_sems.at[other])
        send.start(None, row_block(other), row_block(other), row_sems.at[other], seq=place.sib)

    for other in place.line():
        send.arrived(None, small_ref.at[other], norm_sems.at[other])
    piece = small_ref.shape[2]
    total = None
    for line in range(lines):
        row = lax.broadcasted_iota(jnp.int32, (piece, dim), 0)
        column = lax.broadcasted_iota(jnp.int32, (piece, dim), 1)
        part = dim // lines
        place_of = jnp.logical_and(row < part, column == row + line * part).astype(bf16)
        term = mm(small_ref[line], place_of)
        total = term if total is None else total + term
    norms_ref[...] = total[: norms_ref.shape[0]]

    advance(4)
    advance(5)
    for other in others:
        theirs = other + 1 - 2 * core
        send.arrived(None, row_block(theirs), row_sems.at[theirs])
    send.arrived(None, row_block(place.sib), row_sems.at[place.sib])
    own_rows.wait()
    norm_rows(rows_ref, norms_ref[...], perm_ref, hid_ref)
    for slot in range(6, slots + 2):
        advance(slot)
        if slot == slots:
            late_x(0)
            late_x(1)
    for slot in range(2, slots):
        late_x(slot)
    keep.wait()
    for line in range(lines):
        from_sib(line, 0, low, place.sib)
        from_sib(line, 1, high, place.yn + 1 - 2 * core)
        from_sib(line, 2, None, crossing(0, 1 - core))
    weave = Weave([partial(from_x, 1, slot) for slot in range(slots)])

    copies = weight_copies(pairs, dim, wts_ref, w_qkv_ref, qkv_sems)
    middle = [
        pltpu.make_async_copy(
            wts_ref.at[:, pl.ds((3 + index) * dim, dim)], w_mid_ref.at[index], mid_sems.at[index]
        )
        for index in range(5)
    ]
    for copy in copies + middle:
        copy.start()
    for part in range(3):
        copies[part].wait()
        triple_part(part, pairs, hid_ref, w_qkv_ref, qkv_ref)

    share = lax.rem(me, dim // width)
    seq_rows = pl.ds(pl.multiple_of(place.chip * tokens, tokens), tokens)

    def landing(pair, chip_rows, share):
        lanes = pl.ds(pl.multiple_of(share * width + pair * LANES, LANES), LANES)
        return att_tok_ref.at[chip_rows, lanes]

    for pair in range(pairs):
        lanes = slice(pair * LANES, (pair + 1) * LANES)
        pair_forward(pair, pairs, qkv_ref, att_ref, lse_ref, lambda: None)
        for other in place.plane():
            block = att_ref.at[pl.ds(pl.multiple_of(other * tokens, tokens), tokens), lanes]
            to = landing(pair, seq_rows, share)
            send.start(None, block, to, att_sems.at[pair, me], seq=other)
        own_block = att_ref[pl.ds(pl.multiple_of(me * tokens, tokens), tokens), lanes]
        landing(pair, seq_rows, share)[...] = own_block
        weave.some(1)

    for copy in middle:
        copy.wait()
    w_out_ref, w_cq_ref, w_ck_ref, w_cv_ref, w_co_ref = (w_mid_ref.at[index] for index in range(5))

    @pl.loop(0, near_ref.shape[0] // 512)
    def _(step):
        rows = rows_of(step, 512)
        near_kv_ref[rows, :dim] = mm(near_p_ref[rows, :], w_ck_ref[...]).astype(bf16)
        near_kv_ref[rows, dim:] = mm(near_p_ref[rows, :], w_cv_ref[...]).astype(bf16)

    weave.some(1)
    for pair in range(pairs):
        for other in place.plane():
            rows = pl.ds(pl.multiple_of(other // 2 * tokens, tokens), tokens)
            send.arrived(
                None, landing(pair, rows, lax.rem(other, 2)), att_sems.at[pair, other]
            )
    att_p_ref[...] = mm(att_tok_ref[...], perm_ref[...]).astype(bf16)
    own_x = x_ref[...].reshape(first_ref.shape).astype(f32)
    first_ref[...] = own_x + mm(att_p_ref[...], w_out_ref[...])
    normed, _ = centre_scale(first_ref[...])
    hidden = (normed * norms_ref[2:3, :] + norms_ref[3:4, :]).astype(bf16)
    hid_p_ref[...] = mm(hidden, perm_ref[...]).astype(bf16)
    cross_q_ref[...] = mm(hid_p_ref[...], w_cq_ref[...]).astype(bf16)
    weave.some(1)

    def one_span(span):
        span_forward(span, spans, neighbours, presence_ref, cross_q_ref, near_kv_ref, cross_ref)

    pl.loop(0, spans // 2)(one_span)
    weave.some(1)
    pl.loop(spans // 2, spans)(one_span)
    co_p_ref[...] = mm(cross_ref[...], perm_ref[...]).astype(bf16)
    second_ref[...] = first_ref[...] + mm(co_p_ref[...], w_co_ref[...])

    weave.rest()
    for line in range(lines):
        from_sib(line, 0, high, place.sib)
        from_sib(line, 1, low, place.yn + 1 - 2 * core)
        from_sib(line, 3, None, crossing(1, 1 - core))
    send.finish()


def forward(lines, pairs, spans, neighbours, presence, w_shard, n_shard, inputs, perm, near):
    unit_rows, unit_cols = w_shard.shape
    seqs, tokens, dim = inputs.shape
    count, length, width = seqs * tokens, 8 * tokens, pairs * LANES
    rows_near = near.shape[0]
    events = 2 * lines - 1
    any_space = pl.BlockSpec(memory_space=pl.ANY)
    vmem = pl.BlockSpec(memory_space=pltpu.VMEM)
    dma = pltpu.SemaphoreType.DMA
    out_shape = (
        jax.ShapeDtypeStruct((unit_rows * lines, unit_cols * 8), bf16),
        jax.ShapeDtypeStruct((8, dim), f32),
        jax.ShapeDtypeStruct((length, dim), bf16),
        jax.ShapeDtypeStruct((3 * pairs, length, LANES), bf16),
        jax.ShapeDtypeStruct((length, width), bf16),
        jax.ShapeDtypeStruct((pairs, 2, length), f32),
        jax.ShapeDtypeStruct((count, dim), bf16),
        jax.ShapeDtypeStruct((count, dim), f32),
        jax.ShapeDtypeStruct((count, dim), bf16),
        jax.ShapeDtypeStruct((count, dim), bf16),
        jax.ShapeDtypeStruct((rows_near, dim), bf16),
        jax.ShapeDtypeStruct((rows_near, 2 * dim), bf16),
        jax.ShapeDtypeStruct((count, dim), bf16),
        jax.ShapeDtypeStruct((count, dim), f32),
    )
    return pl.pallas_call(
        partial(forward_kernel, lines, pairs, spans, neighbours),
        out_shape=out_shape,
        in_specs=[pl.BlockSpec(memory_space=pltpu.SMEM)] + [vmem] * 5,
        out_specs=(any_space,) + (vmem,) * (len(out_shape) - 1),
        scratch_shapes=[
            pltpu.VMEM((unit_rows, unit_cols), bf16),
            pltpu.VMEM((lines,) + n_shard.shape, bf16),
            pltpu.VMEM((length, dim), bf16),
            pltpu.VMEM((dim, 3 * width), bf16),
            pltpu.VMEM((5, dim, dim), bf16),
            pltpu.VMEM((count, dim), bf16),
            pltpu.VMEM((count, dim), bf16),
            dma((22 * events + 7 + lines + 7 * pairs,)),
            dma((lines, 2)),
            dma((lines, 2)),
            dma((2, lines, 2)),
            dma((4, lines, 2)),
            dma((lines,)),
            dma((8,)),
            dma((pairs, 8)),
            dma((2,)),
            dma((3,)),
            dma((5,)),
        ],
        compiler_params=pltpu.CompilerParams(
            vmem_limit_bytes=VMEM_BYTES, collective_id=1, has_side_effects=True
        ),
        name="forward",
    )(presence, w_shard, n_shard, inputs, perm, near)


def reduce_kernel(
    lines,
    grads_ref,
    small_ref,
    shard_ref,
    norms_ref,
    mine_ref,
    sib_ref,
    corner_a_ref,
    corner_b_ref,
    from_x_ref,
    from_y_ref,
    below_ref,
    above_ref,
    plane_ref,
    plane_sum_ref,
    line_ref,
    send_sems,
    load_sems,
    sib_sems,
    a_sems,
    b_sems,
    x_sems,
    y_sems,
    below_sems,
    above_sems,
    plane_sems,
    line_sems,
):
    place = Place(lines)
    z, me = place.z, place.me
    unit_rows, unit_cols = shard_ref.shape
    half = unit_rows // 2
    tile = 32
    place.meet()
    send = Sender(place, send_sems)
    chips = (place.dg, place.yn, place.xn, me)
    corner, over_y, over_x, here = range(4)

    unit = partial(unit_of, grads_ref, lines)

    def load(which, line):
        return pltpu.make_async_copy(
            unit(line, chips[which]), mine_ref.at[which, line], load_sems.at[which, line]
        )

    for other in place.plane():
        send.start(None, small_ref, plane_ref.at[me], plane_sems.at[me], seq=other)
    plane_ref[me] = small_ref[...]

    events = place.events()[::-1]
    for condition, line, _, _ in events:
        for which in range(4):
            theirs = chips[which] + 1 - 2 * place.core
            send.start(
                condition,
                unit(line, theirs),
                sib_ref.at[which, line],
                sib_sems.at[which, line],
                seq=place.sib,
            )
            when(condition, load(which, line).start)

    def add(target, *terms, begin=0, size=unit_rows):
        @pl.loop(0, size // tile)
        def _(step):
            rows = pl.ds(pl.multiple_of(begin + step * tile, tile), tile)
            if len(terms) == 1:
                ref, first = terms[0]
                at = pl.ds(pl.multiple_of(begin - first + step * tile, tile), tile)
                target[rows, :] = target[rows, :] + ref[at, :]
            else:
                total = target[rows, :].astype(f32)
                for ref, first in terms:
                    at = pl.ds(pl.multiple_of(begin - first + step * tile, tile), tile)
                    total = total + ref[at, :].astype(f32)
                target[rows, :] = total.astype(target.dtype)

    def own(which, index):
        condition, line, _, _ = events[index]
        send.arrived(condition, sib_ref.at[which, line], sib_sems.at[which, line])
        when(condition, load(which, line).wait)

    def first(index):
        condition, line, _, _ = events[index]
        own(corner, index)
        target = mine_ref.at[corner, line]
        when(condition, lambda: add(target, (sib_ref.at[corner, line], 0)))
        send.start(
            condition,
            target.at[pl.ds(0, half)],
            corner_a_ref.at[line],
            a_sems.at[line],
            seq=place.xn,
        )
        send.start(
            condition,
            target.at[pl.ds(half, half)],
            corner_b_ref.at[line],
            b_sems.at[line],
            seq=place.yn,
        )

    def second(index):
        condition, line, _, _ = events[index]
        for which, part, sems, begin, to, landing, landing_sems in (
            (over_y, corner_a_ref, a_sems, 0, place.yn, from_y_ref, y_sems),
            (over_x, corner_b_ref, b_sems, half, place.xn, from_x_ref, x_sems),
        ):
            own(which, index)
            send.arrived(condition, part.at[line], sems.at[line])
            target = mine_ref.at[which, line]

            def body(which=which, part=part, begin=begin, target=target):
                add(
                    target,
                    (sib_ref.at[which, line], 0),
                    (part.at[line], begin),
                    begin=begin,
                    size=half,
                )
                add(target, (sib_ref.at[which, line], 0), begin=half - begin, size=half)

            when(condition, body)
            send.start(condition, target, landing.at[line], landing_sems.at[line], seq=to)

    def third(index):
        condition, line, far, side = events[index]
        own(here, index)
        send.arrived(condition, from_x_ref.at[line], x_sems.at[line])
        send.arrived(condition, from_y_ref.at[line], y_sems.at[line])
        target = mine_ref.at[here, line]
        terms = [(ref.at[line], 0) for ref in (sib_ref.at[here], from_x_ref, from_y_ref)]
        if side == 0:
            has_below, has_above = z > 0, z < lines - 1
            add(target, *terms)
            send.arrived(has_below, below_ref.at[line], below_sems.at[line])
            send.arrived(has_above, above_ref.at[line], above_sems.at[line])

            @pl.loop(0, unit_rows // tile)
            def _(step):
                rows = rows_of(step, tile)
                shard_ref[rows, :] = target[rows, :].astype(f32)

            when(has_below, lambda: add(shard_ref, (below_ref.at[line], 0)))
            when(has_above, lambda: add(shard_ref, (above_ref.at[line], 0)))
            return
        landing, sems = (below_ref, below_sems) if side > 0 else (above_ref, above_sems)
        more = both(condition, z > 0) if side > 0 else both(condition, z < lines - 1)
        none = both(condition, z == 0) if side > 0 else both(condition, z == lines - 1)
        send.arrived(more, landing.at[line], sems.at[line])
        when(more, lambda: add(target, *terms, (landing.at[line], 0)))
        when(none, lambda: add(target, *terms))
        send.start(condition, target, landing.at[line], sems.at[line], z=z + side)

    count = len(events)
    first(0)
    first(1)
    for index in range(2, count + 4):
        if index < count:
            first(index)
        if 0 <= index - 2 < count:
            second(index - 2)
        if index == 3:
            for other in place.plane():
                send.arrived(None, plane_ref.at[other], plane_sems.at[other])
            total = plane_ref[0]
            for other in range(1, 8):
                total = total + plane_ref[other]
            plane_sum_ref[...] = total
            line_ref[z] = total
            for other in place.line():
                send.start(None, plane_sum_ref, line_ref.at[z], line_sems.at[z], z=other)
        if 0 <= index - 4 < count:
            third(index - 4)

    for other in place.line():
        send.arrived(None, line_ref.at[other], line_sems.at[other])
    total = line_ref[0]
    for other in range(1, lines):
        total = total + line_ref[other]
    norms_ref[...] = total
    send.finish()


def reduce_grads(lines, grads, small):
    rows, cols = grads.shape
    unit_rows, unit_cols = rows // lines, cols // 8
    half = unit_rows // 2
    any_space = pl.BlockSpec(memory_space=pl.ANY)
    vmem = pl.BlockSpec(memory_space=pltpu.VMEM)
    dma = pltpu.SemaphoreType.DMA
    return pl.pallas_call(
        partial(reduce_kernel, lines),
        out_shape=(
            jax.ShapeDtypeStruct((unit_rows, unit_cols), f32),
            jax.ShapeDtypeStruct(small.shape, f32),
        ),
        in_specs=[any_space, vmem],
        out_specs=(vmem, vmem),
        scratch_shapes=[
            pltpu.VMEM((4, lines, unit_rows, unit_cols), bf16),
            pltpu.VMEM((4, lines, unit_rows, unit_cols), bf16),
            pltpu.VMEM((lines, half, unit_cols), bf16),
            pltpu.VMEM((lines, half, unit_cols), bf16),
            pltpu.VMEM((lines, unit_rows, unit_cols), bf16),
            pltpu.VMEM((lines, unit_rows, unit_cols), bf16),
            pltpu.VMEM((lines, unit_rows, unit_cols), bf16),
            pltpu.VMEM((lines, unit_rows, unit_cols), bf16),
            pltpu.VMEM((8,) + small.shape, f32),
            pltpu.VMEM(small.shape, f32),
            pltpu.VMEM((lines,) + small.shape, f32),
            dma((9 * (2 * lines - 1) + 7 + lines,)),
            dma((4, lines)),
            dma((4, lines)),
            dma((lines,)),
            dma((lines,)),
            dma((lines,)),
            dma((lines,)),
            dma((lines,)),
            dma((lines,)),
            dma((8,)),
            dma((lines,)),
        ],
        compiler_params=pltpu.CompilerParams(
            vmem_limit_bytes=VMEM_BYTES, collective_id=4, has_side_effects=True
        ),
        name="reduce_grads",
    )(grads, small)


def adam_update(grad, weight, first, second, average, rate, decay):
    first = beta_first * first + (1.0 - beta_first) * grad
    second = beta_second * second + (1.0 - beta_second) * grad * grad
    stepped = (
        first / (1.0 - beta_first**STEP) / (jnp.sqrt(second / (1.0 - beta_second**STEP)) + adam_eps)
    )
    weight = weight - rate * (stepped + decay * weight)
    average = ema_decay * average + (1.0 - ema_decay) * weight
    return (first, second, weight, average)


def on_device(
    inputs,
    cotangent,
    neighbours,
    presence,
    row_order,
    w_master,
    w_first,
    w_second,
    w_average,
    n_master,
    n_first,
    n_second,
    n_average,
):
    seqs, tokens, dim = inputs.shape
    heads = dim // HEAD
    devices = lax.axis_size("seq")
    count = seqs * tokens
    length = devices * tokens
    me = lax.axis_index("seq")
    shares = devices // seqs
    held = heads // shares
    pairs = (held + 1) // 2
    width = pairs * LANES
    spare = width - held * HEAD
    sequence, share = me // shares, me % shares

    lines = lax.axis_size("dp")
    planar = devices == 8 and seqs == 4 and spare == 0
    perm = (jnp.arange(dim)[:, None] == row_order[None, :]).astype(bf16)
    perm_att = perm
    if spare:
        perm_att = jnp.pad(perm.reshape(shares, held * HEAD, dim), ((0, 0), (0, spare), (0, 0)))
        perm_att = perm_att.reshape(shares * width, dim)
    x = inputs.reshape(count, dim)
    spans = seqs * neighbours.shape[1]
    each = neighbours.shape[2]
    near = neighbours.reshape(-1, dim)
    live = presence.reshape(-1)
    part = n_master.shape[1]
    if planar:
        small = jnp.pad(n_master.astype(bf16), ((0, 16 - 6), (0, -part % LANES)))
        (
            weights,
            norms,
            hid,
            qkv,
            att,
            lse,
            att_p,
            first,
            hid_p,
            cross_q,
            near_p,
            near_kv,
            co_p,
            second,
        ) = forward(lines, pairs, spans, each, live, w_master, small, inputs, perm, near)
    else:
        weights = lax.all_gather(w_master.astype(bf16), "dp", axis=0, tiled=True)
        weights = lax.all_gather(weights, "seq", axis=1, tiled=True)
        norms = lax.all_gather(n_master.astype(bf16), "dp", axis=1, tiled=True).astype(f32)
        rows = lax.all_to_all(jnp.repeat(inputs, shares, axis=0), "seq", 0, 0)
        rows = rows.reshape(length, dim)
        w_qkv = weights[:, : 3 * dim].reshape(dim, 3, shares, held * HEAD)
        w_qkv = lax.dynamic_index_in_dim(w_qkv, share, axis=2, keepdims=False)
        w_qkv = jnp.pad(w_qkv, ((0, 0), (0, 0), (0, spare))).reshape(dim, 3 * width)
        hid, qkv, att, lse = self_forward(pairs, rows, norms, perm, w_qkv)
        att_tok = (
            lax.all_to_all(att.reshape(devices, tokens, width), "seq", 0, 0)
            .reshape(seqs, shares, tokens, width)
            .transpose(0, 2, 1, 3)
            .reshape(count, shares * width)
        )
        att_p, first, hid_p, cross_q, near_p, near_kv, co_p, second = cross_forward(
            spans, each, live, att_tok, x, norms, perm, perm_att, near, weights
        )
    outputs, gsecond, grads, gnorm_e = feed(
        second, cotangent.reshape(count, dim), norms, perm, weights
    )
    gfirst, gatt_tok, grads, gnorm_c = cross_backward(
        spans,
        each,
        lines if planar else 0,
        live,
        gsecond,
        first,
        norms,
        perm,
        perm_att,
        att_p,
        hid_p,
        cross_q,
        near_p,
        near_kv,
        co_p,
        weights,
        grads,
    )
    if planar:
        others = jnp.concatenate(
            [jnp.zeros((2, dim), f32), gnorm_c, gnorm_e, jnp.zeros((2, dim), f32)], axis=0
        )
        grads, grad_inputs, norm_grads = finish(
            pairs,
            lines,
            qkv,
            att,
            gatt_tok,
            lse,
            hid,
            x,
            gfirst,
            norms,
            perm,
            others,
            weights,
            grads,
        )
        grad_shard, norm_sums = reduce_grads(lines, grads, norm_grads)
        norm_shard = lax.dynamic_slice(norm_sums, (0, lax.axis_index("dp") * part), (6, part))
    else:
        gatt = lax.all_to_all(
            gatt_tok.reshape(seqs, tokens, shares, width)
            .transpose(0, 2, 1, 3)
            .reshape(devices, tokens, width),
            "seq",
            0,
            0,
        ).reshape(length, width)
        gqkv, ghid = self_backward(pairs, qkv, att, gatt, lse, hid, w_qkv)
        parts = (
            lax.all_to_all(ghid.reshape(devices, tokens, dim), "seq", 0, 0)
            .reshape(seqs, shares, tokens, dim)
            .transpose(1, 0, 2, 3)
            .reshape(shares, count, dim)
        )
        grad_inputs, gnorm_a = last_norm(parts, x, gfirst, norms, perm)
        gqkv = gqkv.reshape(dim, 3, 1, width)[..., : held * HEAD]
        gqkv = jnp.where(jnp.arange(shares)[:, None] == share, gqkv, jnp.zeros_like(gqkv))
        grads = lax.dynamic_update_slice(grads, gqkv.reshape(dim, 3 * dim), (0, 0))
        norm_grads = lax.psum(jnp.concatenate([gnorm_a, gnorm_c, gnorm_e], axis=0), "seq")
        partial_sum = lax.psum_scatter(grads, "seq", scatter_dimension=1, tiled=True)
        grad_shard = lax.psum_scatter(partial_sum, "dp", scatter_dimension=0, tiled=True)
        grad_shard = grad_shard.astype(f32)
        norm_shard = lax.psum_scatter(
            norm_grads.astype(bf16), "dp", scatter_dimension=1, tiled=True
        ).astype(f32)
    w_first_new, w_second_new, w_new, w_average_new = adam_update(
        grad_shard, w_master, w_first, w_second, w_average, learn_rate, weight_decay
    )
    n_first_new, n_second_new, n_new, n_average_new = adam_update(
        norm_shard, n_master, n_first, n_second, n_average, norm_rate, 0.0
    )
    return (
        outputs.reshape(seqs, tokens, dim),
        grad_inputs.reshape(seqs, tokens, dim),
        w_first_new,
        w_second_new,
        w_new,
        w_average_new,
        n_first_new,
        n_second_new,
        n_new,
        n_average_new,
    )


def solution(mesh):
    in_specs = (
        P("dp", "seq", None),
        P("dp", "seq", None),
        P("dp", "seq", None, None, None),
        P("dp", "seq", None),
        P(),
        P("dp", "seq"),
        P("dp", "seq"),
        P("dp", "seq"),
        P("dp", "seq"),
        P(None, "dp"),
        P(None, "dp"),
        P(None, "dp"),
        P(None, "dp"),
    )
    out_specs = (
        P("dp", "seq", None),
        P("dp", "seq", None),
        P("dp", "seq"),
        P("dp", "seq"),
        P("dp", "seq"),
        P("dp", "seq"),
        P(None, "dp"),
        P(None, "dp"),
        P(None, "dp"),
        P(None, "dp"),
    )
    return jax.shard_map(
        on_device, mesh=mesh, in_specs=in_specs, out_specs=out_specs, check_vma=False
    )
```

```python
from functools import partial

import jax
import jax.numpy as jnp
from jax import lax
from jax.experimental import pallas as pl
from jax.experimental.pallas import tpu as pltpu
from jax.sharding import PartitionSpec as P

HEAD = 64
STEP = 5
LANES = 128
SCALE = HEAD ** (-0.5)

beta_first = 0.9
beta_second = 0.95
adam_eps = 1e-08
learn_rate = 0.04
norm_rate = 0.6
weight_decay = 0.1
ema_decay = 0.5
norm_eps = 1e-05
masked_score = -1e30
VMEM_BYTES = 60 * 1024 * 1024
bf16 = jnp.bfloat16
f32 = jnp.float32


def mm(left, right):
    return lax.dot_general(left, right, (((1,), (0,)), ((), ())), preferred_element_type=f32)


def nt(left, right):
    return lax.dot_general(left, right, (((1,), (1,)), ((), ())), preferred_element_type=f32)


def tn(left, right):
    return lax.dot_general(left, right, (((0,), (0,)), ((), ())), preferred_element_type=f32)


def params():
    return pltpu.CompilerParams(vmem_limit_bytes=VMEM_BYTES)


def rows_of(index, size):
    return pl.ds(pl.multiple_of(index * size, size), size)


def centre_scale(values):
    centre = jnp.mean(values, axis=-1, keepdims=True)
    centred = values - centre
    spread = jnp.mean(centred * centred, axis=-1, keepdims=True)
    recip = lax.rsqrt(spread + norm_eps)
    return centred * recip, recip


def norm_back(upstream, normed, recip, gain):
    scaled = upstream * gain
    inner = (
        scaled
        - jnp.mean(scaled, axis=-1, keepdims=True)
        - normed * jnp.mean(scaled * normed, axis=-1, keepdims=True)
    )
    return (
        recip * inner,
        jnp.sum(upstream * normed, axis=0, keepdims=True),
        jnp.sum(upstream, axis=0, keepdims=True),
    )


def gelu_parts(value):
    const = 0.7978845608028654
    square = value * value
    bend = jnp.tanh(const * value * (1.0 + 0.044715 * square))
    half = 0.5 * (1.0 + bend)
    slope = half + 0.5 * value * (1.0 - bend * bend) * (const * (1.0 + 3 * 0.044715 * square))
    return value * half, slope


def head_mask(rows, half):
    lane = lax.broadcasted_iota(jnp.int32, (rows, LANES), 1)
    return (lane < HEAD) if half == 0 else (lane >= HEAD)


def pick(mask, value):
    return jnp.where(mask, value, jnp.zeros_like(value))


MESH = pl.DeviceIdType.MESH


class Place:
    def __init__(self, lines):
        self.lines = lines
        self.z = lax.axis_index("dp")
        self.me = lax.axis_index("seq")
        core, x, y = self.me % 2, (self.me // 2) % 2, self.me // 4
        self.core, self.x, self.y, self.chip = core, x, y, self.me // 2
        self.sib = self.me + 1 - 2 * core
        self.xn = self.me + 2 - 4 * x
        self.yn = self.me + 4 - 8 * y
        self.dg = self.xn + 4 - 8 * y

    def events(self):
        found = [(None, self.z, 0, 0)]
        for far in range(1, self.lines):
            found.append((self.z >= far, self.z - far, far, -1))
            found.append((self.z + far < self.lines, self.z + far, far, 1))
        return found

    def plane(self):
        return [lax.rem(self.me + step, 8) for step in range(1, 8)]

    def line(self):
        return [lax.rem(self.z + step, self.lines) for step in range(1, self.lines)]

    def meet(self):
        barrier = pltpu.get_barrier_semaphore()
        for other in self.plane():
            pl.semaphore_signal(
                barrier, inc=1, device_id={"dp": self.z, "seq": other}, device_id_type=MESH
            )
        for other in self.line():
            pl.semaphore_signal(
                barrier, inc=1, device_id={"dp": other, "seq": self.me}, device_id_type=MESH
            )
        pl.semaphore_wait(barrier, 7 + self.lines - 1)


def when(condition, body):
    if condition is None:
        body()
    else:
        pl.when(condition)(body)


def both(first, second):
    if first is None or second is None:
        return second if first is None else first
    return jnp.logical_and(first, second)


class Sender:
    def __init__(self, place, send_sems):
        self.place, self.sems, self.open = place, send_sems, []

    def start(self, condition, src, dst, recv_sem, z=None, seq=None):
        place = self.place
        target = {"dp": place.z if z is None else z, "seq": place.me if seq is None else seq}
        copy = pltpu.make_async_remote_copy(
            src_ref=src,
            dst_ref=dst,
            send_sem=self.sems.at[len(self.open)],
            recv_sem=recv_sem,
            device_id=target,
            device_id_type=MESH,
        )
        self.open.append((condition, copy))
        when(condition, copy.start)

    def arrived(self, condition, ref, recv_sem):
        copy = pltpu.make_async_remote_copy(
            src_ref=ref,
            dst_ref=ref,
            send_sem=self.sems.at[0],
            recv_sem=recv_sem,
            device_id={"dp": self.place.z, "seq": self.place.sib},
            device_id_type=MESH,
        )
        when(condition, copy.wait_recv)

    def finish(self):
        for condition, copy in self.open:
            when(condition, copy.wait_send)


class Weave:
    def __init__(self, steps):
        self.steps = list(steps)

    def some(self, count):
        for _ in range(min(count, len(self.steps))):
            self.steps.pop(0)()

    def rest(self):
        self.some(len(self.steps))


def unit_of(ref, lines, line, seq, begin=0, size=None):
    rows, cols = ref.shape[0] // lines, ref.shape[1] // 8
    size = rows if size is None else size
    return ref.at[
        pl.ds(pl.multiple_of(line * rows + begin, 16), size),
        pl.ds(pl.multiple_of(seq * cols, cols), cols),
    ]


def weight_copies(pairs, dim, wts_ref, w_ref, sems):
    width = pairs * LANES
    first = lax.rem(lax.axis_index("seq"), dim // width) * width
    return [
        pltpu.make_async_copy(
            wts_ref.at[:, pl.ds(pl.multiple_of(first + part * dim, LANES), width)],
            w_ref.at[:, pl.ds(part * width, width)],
            sems.at[part],
        )
        for part in range(3)
    ]


def pair_forward(pair, pairs, qkv_ref, att_ref, lse_ref, between):
    length = att_ref.shape[0]
    tile = 256
    below = lax.broadcasted_iota(jnp.int32, (tile, tile), 1) <= lax.broadcasted_iota(
        jnp.int32, (tile, tile), 0
    )
    masks = [head_mask(tile, 0), head_mask(tile, 1)]
    lane = lax.broadcasted_iota(jnp.int32, (tile, LANES), 1)
    for step in range(length // tile):
        rows = slice(step * tile, (step + 1) * tile)
        query = qkv_ref[pair, rows, :] * SCALE
        keys_here = qkv_ref[pairs + pair, rows, :]
        values_here = qkv_ref[2 * pairs + pair, rows, :]
        outs, logs = [], []
        for half in range(2):
            mine = pick(masks[half], query)
            here = jnp.where(below, nt(mine, keys_here), masked_score)
            peak = jnp.max(here, axis=-1, keepdims=True)
            if step:
                past = nt(mine, qkv_ref[pairs + pair, : step * tile, :])
                peak = jnp.maximum(peak, jnp.max(past, axis=-1, keepdims=True))
                past = jnp.exp(past - peak)
            here = jnp.exp(here - peak)
            total = jnp.sum(here, axis=-1, keepdims=True)
            out = mm(here.astype(bf16), values_here)
            if step:
                total = total + jnp.sum(past, axis=-1, keepdims=True)
                out = out + mm(past.astype(bf16), qkv_ref[2 * pairs + pair, : step * tile, :])
            outs.append(out / total)
            logs.append(peak + jnp.log(total))
        lse_ref[pair, :, rows] = jnp.where(lane == 0, logs[0], logs[1]).T[0:2, :]
        att_ref[rows, pl.ds(pl.multiple_of(pair * LANES, LANES), LANES)] = jnp.where(
            masks[0], outs[0], outs[1]
        ).astype(bf16)
        between()


def norm_rows(x_ref, norms, perm_ref, hid_ref):
    tile = 256

    @pl.loop(0, x_ref.shape[0] // tile)
    def _(step):
        rows = rows_of(step, tile)
        normed, _ = centre_scale(x_ref[rows, :].astype(f32))
        hidden = (normed * norms[0:1, :] + norms[1:2, :]).astype(bf16)
        hid_ref[rows, :] = mm(hidden, perm_ref[...]).astype(bf16)


def triple_part(part, pairs, hid_ref, w_ref, qkv_ref):
    width = pairs * LANES
    triple = mm(hid_ref[...], w_ref[:, part * width : (part + 1) * width]).astype(bf16)
    for pair in range(pairs):
        qkv_ref[part * pairs + pair] = triple[:, pair * LANES : (pair + 1) * LANES]


def self_forward_kernel(
    pairs, x_ref, norms_ref, perm_ref, w_ref, hid_ref, qkv_ref, att_ref, lse_ref
):
    norm_rows(x_ref, norms_ref, perm_ref, hid_ref)
    for part in range(3):
        triple_part(part, pairs, hid_ref, w_ref, qkv_ref)

    @pl.loop(0, pairs)
    def _(pair):
        pair_forward(pair, pairs, qkv_ref, att_ref, lse_ref, lambda: None)


def self_forward(pairs, x, norms, perm, w):
    length, dim = x.shape
    return pl.pallas_call(
        partial(self_forward_kernel, pairs),
        out_shape=(
            jax.ShapeDtypeStruct((length, dim), bf16),
            jax.ShapeDtypeStruct((3 * pairs, length, LANES), bf16),
            jax.ShapeDtypeStruct((length, pairs * LANES), bf16),
            jax.ShapeDtypeStruct((pairs, 2, length), f32),
        ),
        compiler_params=params(),
        name="self_forward",
    )(x, norms, perm, w)


def pair_backward(pair, pairs, qkv_ref, att_ref, gatt_ref, lse_ref, grad_ref, acc_ref, between):
    length = att_ref.shape[0]
    width = pairs * LANES
    tile = 256
    above = lax.broadcasted_iota(jnp.int32, (tile, tile), 0) <= lax.broadcasted_iota(
        jnp.int32, (tile, tile), 1
    )
    masks = [head_mask(tile, 0), head_mask(tile, 1)]
    lanes = pl.ds(pl.multiple_of(pair * LANES, LANES), LANES)
    for step in range(length // tile):
        rows = slice(step * tile, (step + 1) * tile)
        query = qkv_ref[pair, rows, :] * SCALE
        grad_out = gatt_ref[rows, lanes]
        product = grad_out.astype(f32) * att_ref[rows, lanes].astype(f32)
        queries = [pick(masks[half], query) for half in range(2)]
        grads = [pick(masks[half], grad_out) for half in range(2)]
        deltas = [jnp.sum(pick(masks[half], product).T, axis=0, keepdims=True) for half in range(2)]
        grad_query = [None, None]
        for other in range(step + 1):
            cols = slice(other * tile, (other + 1) * tile)
            keys = qkv_ref[pairs + pair, cols, :]
            values = qkv_ref[2 * pairs + pair, cols, :]
            key_part = value_part = None
            for half in range(2):
                scores = nt(keys, queries[half])
                if other == step:
                    scores = jnp.where(above, scores, masked_score)
                probs = jnp.exp(scores - lse_ref[pair, half : half + 1, rows])
                grad_scores = (probs * (nt(values, grads[half]) - deltas[half])).astype(bf16)
                query_term = tn(grad_scores, keys)
                grad_query[half] = (
                    query_term if grad_query[half] is None else grad_query[half] + query_term
                )
                key_term = mm(grad_scores, queries[half])
                value_term = mm(probs.astype(bf16), grads[half])
                key_part = key_term if key_part is None else key_part + key_term
                value_part = value_term if value_part is None else value_part + value_term
            if other == step:
                acc_ref[0, cols, :] = key_part
                acc_ref[1, cols, :] = value_part
            else:
                acc_ref[0, cols, :] += key_part
                acc_ref[1, cols, :] += value_part
        grad_ref[rows, lanes] = (jnp.where(masks[0], grad_query[0], grad_query[1]) * SCALE).astype(
            bf16
        )
        between()
    for part in range(2):
        lanes_to = pl.ds(pl.multiple_of((part + 1) * width + pair * LANES, LANES), LANES)
        grad_ref[:, lanes_to] = acc_ref[part].astype(bf16)


def self_backward_kernel(
    pairs,
    qkv_ref,
    att_ref,
    gatt_ref,
    lse_ref,
    hid_ref,
    w_ref,
    gw_ref,
    ghid_ref,
    grad_ref,
    acc_ref,
):
    length = att_ref.shape[0]
    width = pairs * LANES
    attention = (qkv_ref, att_ref, gatt_ref, lse_ref, grad_ref, acc_ref)

    @pl.loop(0, pairs)
    def _(pair):
        pair_backward(pair, pairs, *attention, lambda: None)

    hidden_t = hid_ref[...].T
    for part in range(3):
        cols = slice(part * width, (part + 1) * width)
        gw_ref[:, cols] = mm(hidden_t, grad_ref[:, cols]).astype(bf16)
    for begin in range(0, length, 256):
        rows = slice(begin, begin + 256)
        ghid_ref[rows, :] = nt(grad_ref[rows, :], w_ref[...]).astype(bf16)


def self_backward(pairs, qkv, att, gatt, lse, hid, w):
    length, dim = hid.shape
    width = pairs * LANES
    return pl.pallas_call(
        partial(self_backward_kernel, pairs),
        out_shape=(
            jax.ShapeDtypeStruct((dim, 3 * width), bf16),
            jax.ShapeDtypeStruct((length, dim), bf16),
        ),
        scratch_shapes=[
            pltpu.VMEM((length, 3 * width), bf16),
            pltpu.VMEM((2, length, LANES), f32),
        ],
        compiler_params=params(),
        name="self_backward",
    )(qkv, att, gatt, lse, hid, w)


def finish_kernel(
    pairs,
    lines,
    qkv_ref,
    att_ref,
    gatt_ref,
    lse_ref,
    hid_ref,
    x_ref,
    gfirst_ref,
    norms_ref,
    perm_ref,
    others_ref,
    wts_ref,
    _,
    all_ref,
    gin_ref,
    small_ref,
    grad_ref,
    acc_ref,
    gw_ref,
    w_ref,
    sems,
    ghid_ref,
    gsib_ref,
    parts_ref,
    gsib_sems,
    part_sems,
    send_sems,
):
    length, dim = hid_ref.shape
    width = pairs * LANES
    tokens = length // 8
    place = Place(lines)
    me, core = place.me, place.core
    place.meet()
    send = Sender(place, send_sems)
    copies = weight_copies(pairs, dim, wts_ref, w_ref, sems)
    for copy in copies:
        copy.start()

    share_count = dim // width
    share = lax.rem(me, share_count)
    gw_ref[3] = jnp.zeros_like(gw_ref[3])
    outs = []
    for part in range(3):
        for other in range(1, share_count):
            first = part * dim + lax.rem(share + other, share_count) * width
            outs.append(
                pltpu.make_async_copy(
                    gw_ref.at[3],
                    all_ref.at[:, pl.ds(pl.multiple_of(first, LANES), width)],
                    sems.at[6 + part * (share_count - 1) + other - 1],
                )
            )
            outs[-1].start()

    attention = (qkv_ref, att_ref, gatt_ref, lse_ref, grad_ref, acc_ref)

    @pl.loop(0, pairs)
    def _(pair):
        pair_backward(pair, pairs, *attention, lambda: None)

    def token_rows(device):
        return pl.ds(pl.multiple_of(device * tokens, tokens), tokens)

    for copy in copies:
        copy.wait()
    for begin in range(0, length, 256):
        rows = slice(begin, begin + 256)
        ghid_ref[rows, :] = nt(grad_ref[rows, :], w_ref[...]).astype(bf16)
    chips = (place.xn // 2, place.yn // 2, place.dg // 2, place.chip)
    for chip in chips:
        theirs = chip * 2 + 1 - core
        send.start(
            None, ghid_ref.at[token_rows(theirs)], gsib_ref.at[chip], gsib_sems.at[chip], seq=place.sib
        )
    for chip in chips:
        send.arrived(None, gsib_ref.at[chip], gsib_sems.at[chip])
        rows = token_rows(chip * 2 + core)
        total = (ghid_ref[rows, :].astype(f32) + gsib_ref[chip].astype(f32)).astype(bf16)
        if chip is place.chip:
            parts_ref[chip] = total
        else:
            ghid_ref[rows, :] = total
            send.start(
                None,
                ghid_ref.at[rows],
                parts_ref.at[place.chip],
                part_sems.at[place.chip],
                seq=chip * 2 + core,
            )

    hidden_t = hid_ref[...].T
    for part in range(3):
        gw_ref[part] = mm(hidden_t, grad_ref[:, part * width : (part + 1) * width]).astype(bf16)
        first = part * dim + share * width
        outs.append(
            pltpu.make_async_copy(
                gw_ref.at[part],
                all_ref.at[:, pl.ds(pl.multiple_of(first, LANES), width)],
                sems.at[3 + part],
            )
        )
        outs[-1].start()

    for chip in chips[:3]:
        send.arrived(None, parts_ref.at[chip], part_sems.at[chip])
    gain_sum = shift_sum = None
    for chip in range(4):
        rows = slice(chip * tokens, (chip + 1) * tokens)
        upstream = nt(parts_ref[chip], perm_ref[...])
        normed, recip = centre_scale(x_ref[rows, :].astype(f32))
        back, gain, shift = norm_back(upstream, normed, recip, norms_ref[0:1, :])
        gin_ref[rows, :] = gfirst_ref[rows, :] + back
        gain_sum = gain if gain_sum is None else gain_sum + gain
        shift_sum = shift if shift_sum is None else shift_sum + shift
    small_ref[...] = others_ref[...]
    small_ref[0:1, :] = gain_sum
    small_ref[1:2, :] = shift_sum
    for copy in outs:
        copy.wait()
    send.finish()


def finish(pairs, lines, qkv, att, gatt, lse, hid, x, gfirst, norms, perm, others, weights, grads):
    length, dim = hid.shape
    width = pairs * LANES
    count = x.shape[0]
    tokens = length // 8
    any_space = pl.BlockSpec(memory_space=pl.ANY)
    vmem = pl.BlockSpec(memory_space=pltpu.VMEM)
    dma = pltpu.SemaphoreType.DMA
    return pl.pallas_call(
        partial(finish_kernel, pairs, lines),
        out_shape=(
            jax.ShapeDtypeStruct(grads.shape, bf16),
            jax.ShapeDtypeStruct((count, dim), f32),
            jax.ShapeDtypeStruct((8, dim), f32),
        ),
        in_specs=[vmem] * 10 + [any_space] * 2,
        out_specs=(any_space, vmem, vmem),
        scratch_shapes=[
            pltpu.VMEM((length, 3 * width), bf16),
            pltpu.VMEM((2, length, LANES), f32),
            pltpu.VMEM((4, dim, width), bf16),
            pltpu.VMEM((dim, 3 * width), bf16),
            dma((6 + 3 * (dim // width),)),
            pltpu.VMEM((length, dim), bf16),
            pltpu.VMEM((4, tokens, dim), bf16),
            pltpu.VMEM((4, tokens, dim), bf16),
            dma((4,)),
            dma((4,)),
            dma((8,)),
        ],
        input_output_aliases={11: 0},
        compiler_params=pltpu.CompilerParams(
            vmem_limit_bytes=VMEM_BYTES, collective_id=3, has_side_effects=True
        ),
        name="finish",
    )(qkv, att, gatt, lse, hid, x, gfirst, norms, perm, others, weights, grads)


def spread_heads(block, rows, group):
    lane = lax.broadcasted_iota(jnp.int32, block.shape, 1) // HEAD
    return jnp.concatenate([pick(lane == head, block) for head in range(group)], axis=0)


def gather_heads(stacked, rows, group):
    lane = lax.broadcasted_iota(jnp.int32, (rows, stacked.shape[1]), 1) // HEAD
    out = None
    for head in range(group):
        part = pick(lane == head, stacked[head * rows : (head + 1) * rows])
        out = part if out is None else out + part
    return out


def live_keys(presence_ref, span, shape, axis, neighbours, each):
    index = lax.broadcasted_iota(jnp.int32, shape, axis) // each
    live = jnp.zeros(shape, f32)
    anyone = None
    for which in range(neighbours):
        here = presence_ref[span * neighbours + which]
        there = jnp.where(here > 0, 1.0, 0.0).astype(f32)
        live = jnp.where(index == which, there, live)
        anyone = here if anyone is None else jnp.maximum(anyone, here)
    return live, anyone.astype(f32)


def span_forward(span, spans, neighbours, presence_ref, cross_q_ref, near_kv_ref, cross_ref):
    count, dim = cross_q_ref.shape
    span_len = count // spans
    near = near_kv_ref.shape[0] // spans
    group = 256 // HEAD
    rows = rows_of(span, span_len)
    keys = rows_of(span, near)
    live, anyone = live_keys(presence_ref, span, (1, near), 1, neighbours, near // neighbours)
    for begin in range(0, dim, group * HEAD):
        lanes = slice(begin, begin + group * HEAD)
        lanes_v = slice(dim + begin, dim + begin + group * HEAD)
        query = spread_heads(cross_q_ref[rows, lanes] * SCALE, span_len, group)
        scores = jnp.where(live > 0, nt(query, near_kv_ref[keys, lanes]), masked_score)
        peak = jnp.max(scores, axis=-1, keepdims=True)
        expon = jnp.exp(scores - peak) * live
        total = jnp.sum(expon, axis=-1, keepdims=True) + 1.0 - anyone
        out = mm(expon.astype(bf16), near_kv_ref[keys, lanes_v]) / total
        cross_ref[rows, lanes] = gather_heads(out, span_len, group).astype(bf16)


def cross_forward_kernel(
    spans,
    neighbours,
    presence_ref,
    att_ref,
    x_ref,
    norms_ref,
    perm_ref,
    perm_att_ref,
    near_ref,
    w_out_ref,
    w_cq_ref,
    w_ck_ref,
    w_cv_ref,
    w_co_ref,
    att_p_ref,
    first_ref,
    hid_p_ref,
    cross_q_ref,
    near_p_ref,
    near_kv_ref,
    co_p_ref,
    second_ref,
    cross_ref,
):
    count, dim = x_ref.shape
    rows_near = near_ref.shape[0]
    tile = 512

    att_p_ref[...] = mm(att_ref[...], perm_att_ref[...]).astype(bf16)
    first_ref[...] = x_ref[...].astype(f32) + mm(att_p_ref[...], w_out_ref[...])

    normed, _ = centre_scale(first_ref[...])
    hidden = (normed * norms_ref[2:3, :] + norms_ref[3:4, :]).astype(bf16)
    hid_p_ref[...] = mm(hidden, perm_ref[...]).astype(bf16)
    cross_q_ref[...] = mm(hid_p_ref[...], w_cq_ref[...]).astype(bf16)

    @pl.loop(0, rows_near // tile)
    def _(step):
        rows = rows_of(step, tile)
        near_p_ref[rows, :] = mm(near_ref[rows, :], perm_ref[...]).astype(bf16)
        near_kv_ref[rows, :dim] = mm(near_p_ref[rows, :], w_ck_ref[...]).astype(bf16)
        near_kv_ref[rows, dim:] = mm(near_p_ref[rows, :], w_cv_ref[...]).astype(bf16)

    @pl.loop(0, spans)
    def _(span):
        span_forward(span, spans, neighbours, presence_ref, cross_q_ref, near_kv_ref, cross_ref)

    co_p_ref[...] = mm(cross_ref[...], perm_ref[...]).astype(bf16)
    second_ref[...] = first_ref[...] + mm(co_p_ref[...], w_co_ref[...])


def column_block(rows, width, index):
    return pl.BlockSpec((rows, width), lambda *_: (0, index), pipeline_mode=pl.Buffered(1))


def whole(array):
    return pl.BlockSpec(array.shape, lambda *_: (0,) * array.ndim, pipeline_mode=pl.Buffered(1))


def whole_shape(shape):
    return pl.BlockSpec(shape, lambda *_: (0,) * len(shape), pipeline_mode=pl.Buffered(1))


def cross_forward(spans, neighbours, presence, att, x, norms, perm, perm_att, near, weights):
    count, dim = x.shape
    rows_near = near.shape[0]
    out_shape = (
        jax.ShapeDtypeStruct((count, dim), bf16),
        jax.ShapeDtypeStruct((count, dim), f32),
        jax.ShapeDtypeStruct((count, dim), bf16),
        jax.ShapeDtypeStruct((count, dim), bf16),
        jax.ShapeDtypeStruct((rows_near, dim), bf16),
        jax.ShapeDtypeStruct((rows_near, 2 * dim), bf16),
        jax.ShapeDtypeStruct((count, dim), bf16),
        jax.ShapeDtypeStruct((count, dim), f32),
    )
    operands = (att, x, norms, perm, perm_att, near)
    return pl.pallas_call(
        partial(cross_forward_kernel, spans, neighbours),
        out_shape=out_shape,
        grid=(1,),
        in_specs=[pl.BlockSpec(memory_space=pltpu.SMEM)]
        + [whole(op) for op in operands]
        + [column_block(dim, dim, index) for index in (3, 4, 5, 6, 7)],
        out_specs=tuple(whole_shape(shape.shape) for shape in out_shape),
        scratch_shapes=[pltpu.VMEM((count, dim), bf16)],
        compiler_params=params(),
        name="cross_forward",
    )(presence, *operands, *([weights] * 5))


def feed_kernel(
    second_ref,
    cot_ref,
    norms_ref,
    perm_ref,
    w_up_ref,
    w_down_ref,
    out_ref,
    gsecond_ref,
    all_ref,
    gnorm_ref,
    hid_p_ref,
    hid_t_ref,
    cot_p_ref,
    cot_t_ref,
    result_ref,
    back_ref,
    gup_ref,
    gdown_ref,
    sems,
):
    step = pl.program_id(0)
    last = pl.num_programs(0) - 1
    slot = lax.rem(step, 2)
    dim, tile = w_up_ref.shape

    def copies(step, slot):
        up = pl.multiple_of(8 * dim + step * tile, tile)
        down = pl.multiple_of(8 * dim + (last + 1 + step) * tile, tile)
        return (
            pltpu.make_async_copy(gup_ref.at[slot], all_ref.at[:, pl.ds(up, tile)], sems.at[0, slot]),
            pltpu.make_async_copy(
                gdown_ref.at[slot], all_ref.at[:, pl.ds(down, tile)], sems.at[1, slot]
            ),
        )

    @pl.when(step >= 2)
    def _():
        for copy in copies(step - 2, slot):
            copy.wait()

    @pl.when(step == 0)
    def _():
        normed, _ = centre_scale(second_ref[...])
        hidden = (normed * norms_ref[4:5, :] + norms_ref[5:6, :]).astype(bf16)
        hid_p_ref[...] = mm(hidden, perm_ref[...]).astype(bf16)
        hid_t_ref[...] = hid_p_ref[...].T
        cot_p_ref[...] = mm(cot_ref[...], perm_ref[...]).astype(bf16)
        cot_t_ref[...] = cot_p_ref[...].T
        result_ref[...] = jnp.zeros_like(result_ref)
        back_ref[...] = jnp.zeros_like(back_ref)

    upward = mm(hid_p_ref[...], w_up_ref[...])
    active, slope = gelu_parts(upward)
    active = active.astype(bf16)
    result_ref[...] += nt(active, w_down_ref[...])
    gdown_ref[slot] = mm(cot_t_ref[...], active).astype(bf16)
    grad_up = (mm(cot_p_ref[...], w_down_ref[...]) * slope).astype(bf16)
    gup_ref[slot] = mm(hid_t_ref[...], grad_up).astype(bf16)
    for copy in copies(step, slot):
        copy.start()
    back_ref[...] += nt(grad_up, w_up_ref[...])

    @pl.when(step == last)
    def _():
        out_ref[...] = (
            second_ref[...] + nt(result_ref[...].astype(bf16), perm_ref[...])
        ).astype(bf16)
        upstream = nt(back_ref[...].astype(bf16), perm_ref[...])
        normed, recip = centre_scale(second_ref[...])
        back, gain, shift = norm_back(upstream, normed, recip, norms_ref[4:5, :])
        gsecond_ref[...] = cot_ref[...].astype(f32) + back
        gnorm_ref[0:1, :] = gain
        gnorm_ref[1:2, :] = shift
        for which in (step - 1, step):
            for copy in copies(which, lax.rem(which, 2)):
                copy.wait()


def feed(second, cot, norms, perm, weights):
    count, dim = second.shape
    ffw = (weights.shape[1] - 8 * dim) // 2
    tile = 512
    first_up = 8 * dim // tile
    first_down = (8 * dim + ffw) // tile
    out_shape = (
        jax.ShapeDtypeStruct((count, dim), bf16),
        jax.ShapeDtypeStruct((count, dim), f32),
        jax.ShapeDtypeStruct(weights.shape, bf16),
        jax.ShapeDtypeStruct((2, dim), f32),
    )
    operands = (second, cot, norms, perm)
    return pl.pallas_call(
        feed_kernel,
        out_shape=out_shape,
        grid=(ffw // tile,),
        in_specs=[whole(op) for op in operands]
        + [
            pl.BlockSpec((dim, tile), lambda i: (0, first_up + i)),
            pl.BlockSpec((dim, tile), lambda i: (0, first_down + i)),
        ],
        out_specs=(
            whole_shape((count, dim)),
            whole_shape((count, dim)),
            pl.BlockSpec(memory_space=pl.ANY),
            whole_shape((2, dim)),
        ),
        scratch_shapes=[
            pltpu.VMEM((count, dim), bf16),
            pltpu.VMEM((dim, count), bf16),
            pltpu.VMEM((count, dim), bf16),
            pltpu.VMEM((dim, count), bf16),
            pltpu.VMEM((count, dim), f32),
            pltpu.VMEM((count, dim), f32),
            pltpu.VMEM((2, dim, tile), bf16),
            pltpu.VMEM((2, dim, tile), bf16),
            pltpu.SemaphoreType.DMA((2, 2)),
        ],
        compiler_params=params(),
        name="feed",
    )(*operands, weights, weights)


def cross_backward_kernel(
    spans,
    neighbours,
    lines,
    presence_ref,
    gsecond_ref,
    first_ref,
    norms_ref,
    perm_ref,
    perm_att_ref,
    att_p_ref,
    hid_p_ref,
    cross_q_ref,
    near_p_ref,
    near_kv_ref,
    co_p_ref,
    w_out_ref,
    w_cq_ref,
    w_co_ref,
    _,
    gfirst_ref,
    gatt_ref,
    all_ref,
    gnorm_ref,
    *rest,
):
    count, dim = first_ref.shape
    rows_near = near_p_ref.shape[0]
    span_len = count // spans
    near = rows_near // spans
    group = 256 // HEAD
    outs = []
    if lines:
        gatt_tok_ref, row_sems, send_sems = rest[5:]
        place = Place(lines)
        place.meet()
        send = Sender(place, send_sems)
    gco_ref, gcq_ref, gnear_ref, gw_ref, sems = rest[:5]

    def keep(index, value):
        slot = len(outs) % 3
        if len(outs) >= 3:
            outs[-3].wait()
        gw_ref[slot] = value.astype(bf16)
        outs.append(
            pltpu.make_async_copy(
                gw_ref.at[slot],
                all_ref.at[:, pl.ds((3 + index) * dim, dim)],
                sems.at[index],
            )
        )
        outs[-1].start()

    upper = gsecond_ref[...].astype(bf16)
    gco_ref[...] = nt(nt(upper, w_co_ref[...]).astype(bf16), perm_ref[...]).astype(bf16)

    def one_span(span):
        rows = rows_of(span, span_len)
        keys = rows_of(span, near)
        live, anyone = live_keys(presence_ref, span, (near, 1), 0, neighbours, near // neighbours)
        for begin in range(0, dim, group * HEAD):
            lanes = slice(begin, begin + group * HEAD)
            lanes_v = slice(dim + begin, dim + begin + group * HEAD)
            query = spread_heads(cross_q_ref[rows, lanes] * SCALE, span_len, group)
            grad_out = spread_heads(gco_ref[rows, lanes], span_len, group)
            key = near_kv_ref[keys, lanes]
            scores = jnp.where(live > 0, nt(key, query), masked_score)
            peak = jnp.max(scores, axis=0, keepdims=True)
            expon = jnp.exp(scores - peak) * live
            total = jnp.sum(expon, axis=0, keepdims=True) + 1.0 - anyone
            probs = expon * (1.0 / total)
            grad_probs = nt(near_kv_ref[keys, lanes_v], grad_out)
            inner = jnp.sum(probs * grad_probs, axis=0, keepdims=True)
            grad_scores = (probs * (grad_probs - inner)).astype(bf16)
            gcq_ref[rows, lanes] = (
                gather_heads(tn(grad_scores, key), span_len, group) * SCALE
            ).astype(bf16)
            gnear_ref[keys, lanes] = mm(grad_scores, query).astype(bf16)
            gnear_ref[keys, lanes_v] = mm(probs.astype(bf16), grad_out).astype(bf16)

    pl.loop(0, spans)(one_span)

    upstream = nt(nt(gcq_ref[...], w_cq_ref[...]).astype(bf16), perm_ref[...])
    normed, recip = centre_scale(first_ref[...])
    back, gain, shift = norm_back(upstream, normed, recip, norms_ref[2:3, :])
    gnorm_ref[0:1, :] = gain
    gnorm_ref[1:2, :] = shift
    gfirst_ref[...] = gsecond_ref[...] + back
    lower = gfirst_ref[...].astype(bf16)
    gatt = nt(nt(lower, w_out_ref[...]).astype(bf16), perm_att_ref[...]).astype(bf16)
    if lines:
        width = gatt_ref.shape[1]
        tokens = gatt_ref.shape[0] // 8
        shares = gatt.shape[1] // width
        gatt_tok_ref[...] = gatt

        def block(device):
            return gatt_tok_ref.at[
                pl.ds(pl.multiple_of(device // shares * tokens, tokens), tokens),
                pl.ds(pl.multiple_of(device % shares * width, width), width),
            ]

        def landing(device):
            return gatt_ref.at[pl.ds(pl.multiple_of(device * tokens, tokens), tokens)]

        for other in place.plane():
            send.start(None, block(other), landing(place.me), row_sems.at[place.me], seq=other)
        own = pltpu.make_async_copy(block(place.me), landing(place.me), row_sems.at[place.me])
        own.start()
    else:
        gatt_ref[...] = gatt
    keep(4, mm(co_p_ref[...].T, upper))
    near_t = near_p_ref[...].T
    for part in range(2):
        keep(2 + part, mm(near_t, gnear_ref[:, part * dim : (part + 1) * dim]))
    keep(1, mm(hid_p_ref[...].T, gcq_ref[...]))
    keep(0, mm(att_p_ref[...].T, lower))
    if lines:
        for other in place.plane():
            send.arrived(None, landing(other), row_sems.at[other])
        own.wait()
        send.finish()
    for copy in outs[-3:]:
        copy.wait()


def cross_backward(
    spans,
    neighbours,
    lines,
    presence,
    gsecond,
    first,
    norms,
    perm,
    perm_att,
    att_p,
    hid_p,
    cross_q,
    near_p,
    near_kv,
    co_p,
    weights,
    grads,
):
    count, dim = first.shape
    rows_near = near_p.shape[0]
    gatt_shape = (count, perm_att.shape[0])
    out_shape = [
        jax.ShapeDtypeStruct((count, dim), f32),
        jax.ShapeDtypeStruct(gatt_shape, bf16),
        jax.ShapeDtypeStruct(grads.shape, bf16),
        jax.ShapeDtypeStruct((2, dim), f32),
    ]
    scratch = [
        pltpu.VMEM((count, dim), bf16),
        pltpu.VMEM((count, dim), bf16),
        pltpu.VMEM((rows_near, 2 * dim), bf16),
        pltpu.VMEM((3, dim, dim), bf16),
        pltpu.SemaphoreType.DMA((5,)),
    ]
    compiler_params = params()
    if lines:
        out_shape[1] = jax.ShapeDtypeStruct((2 * count, gatt_shape[1] // 2), bf16)
        scratch += [
            pltpu.VMEM(gatt_shape, bf16),
            pltpu.SemaphoreType.DMA((8,)),
            pltpu.SemaphoreType.DMA((8,)),
        ]
        compiler_params = pltpu.CompilerParams(
            vmem_limit_bytes=VMEM_BYTES, collective_id=2, has_side_effects=True
        )
    operands = (
        gsecond,
        first,
        norms,
        perm,
        perm_att,
        att_p,
        hid_p,
        cross_q,
        near_p,
        near_kv,
        co_p,
    )
    return pl.pallas_call(
        partial(cross_backward_kernel, spans, neighbours, lines),
        out_shape=out_shape,
        grid=(1,),
        in_specs=[pl.BlockSpec(memory_space=pltpu.SMEM)]
        + [whole(op) for op in operands]
        + [column_block(dim, dim, index) for index in (3, 4, 7)]
        + [pl.BlockSpec(memory_space=pl.ANY)],
        out_specs=tuple(
            pl.BlockSpec(memory_space=pl.ANY) if index == 2 else whole_shape(shape.shape)
            for index, shape in enumerate(out_shape)
        ),
        scratch_shapes=scratch,
        input_output_aliases={len(operands) + 4: 2},
        compiler_params=compiler_params,
        name="cross_backward",
    )(presence, *operands, *([weights] * 3), grads)


def last_norm_kernel(parts_ref, x_ref, gfirst_ref, norms_ref, perm_ref, out_ref, gnorm_ref):
    total = parts_ref[0].astype(f32)
    for part in range(1, parts_ref.shape[0]):
        total = total + parts_ref[part].astype(f32)
    upstream = nt(total.astype(bf16), perm_ref[...])
    normed, recip = centre_scale(x_ref[...].astype(f32))
    back, gain, shift = norm_back(upstream, normed, recip, norms_ref[0:1, :])
    out_ref[...] = gfirst_ref[...] + back
    gnorm_ref[0:1, :] = gain
    gnorm_ref[1:2, :] = shift


def last_norm(parts, x, gfirst, norms, perm):
    count, dim = x.shape
    return pl.pallas_call(
        last_norm_kernel,
        out_shape=(
            jax.ShapeDtypeStruct((count, dim), f32),
            jax.ShapeDtypeStruct((2, dim), f32),
        ),
        compiler_params=params(),
        name="last_norm",
    )(parts, x, gfirst, norms, perm)


def forward_kernel(
    lines,
    pairs,
    spans,
    neighbours,
    presence_ref,
    w_ref,
    norm_ref,
    x_ref,
    perm_ref,
    cot_ref,
    near_ref,
    wts_ref,
    all_ref,
    hid_out,
    qkv_out,
    att_out,
    lse_out,
    att_p_out,
    first_out,
    hid_p_out,
    cross_q_out,
    near_p_out,
    near_kv_out,
    co_p_out,
    norms_ref,
    out_ref,
    gsecond_ref,
    gnorm_ref,
    *scratch,
):
    results, scratch = scratch[:11], scratch[11:]
    (
        hid_ref,
        qkv_ref,
        att_ref,
        lse_ref,
        att_p_ref,
        first_ref,
        hid_p_ref,
        cross_q_ref,
        near_p_ref,
        near_kv_ref,
        co_p_ref,
    ) = results
    work, scratch = scratch[:15], scratch[15:]
    (
        second_ref,
        own_ref,
        small_ref,
        rows_ref,
        w_qkv_ref,
        w_mid_ref,
        att_tok_ref,
        cross_ref,
        up_p_ref,
        up_t_ref,
        cot_p_ref,
        cot_t_ref,
        result_ref,
        back_ref,
        gfeed_ref,
    ) = work
    (
        send_sems,
        z_sems,
        y_sems,
        x_sems,
        sib_sems,
        norm_sems,
        row_sems,
        att_sems,
        local_sems,
        qkv_sems,
        mid_sems,
        feed_sems,
        out_sems,
    ) = scratch
    place = Place(lines)
    z, me, core = place.z, place.me, place.core
    length, dim = hid_ref.shape
    width = pairs * LANES
    tokens = length // 8
    cols = own_ref.shape[1] // 2
    slots = 2 * lines
    low, high = place.y == 0, place.y == 1
    near_load = pltpu.make_async_copy(near_ref, near_p_ref, local_sems.at[2])
    near_load.start()
    own_ref[...] = w_ref[...].astype(bf16)
    place.meet()
    send = Sender(place, send_sems)

    def unit(line, seq, half):
        rows = own_ref.shape[0]
        half = jnp.where(seq == 2, 1 - half, half)
        return wts_ref.at[
            pl.ds(pl.multiple_of(line * rows, rows), rows),
            pl.ds(pl.multiple_of((seq * 2 + half) * cols, cols), cols),
        ]

    events = place.events()
    keep = pltpu.make_async_copy(own_ref, unit_of(wts_ref, lines, z, me), local_sems.at[0])
    keep.start()

    def crossing(row, of=core):
        return row * 4 + (1 - place.x) * 2 + of

    def pieces(slot):
        far, half = slot % lines, slot // lines
        found = events[:1] if far == 0 else events[2 * far - 1 : 2 * far + 1]
        return [(*event, half) for event in found]

    def source(line, far, half):
        if far:
            return unit(line, me, half)
        half = jnp.where(me == 2, 1 - half, half)
        return own_ref.at[:, pl.ds(pl.multiple_of(half * cols, cols), cols)]

    def own_unit(slot):
        for condition, line, far, side, half in pieces(slot):
            mine, src = unit(line, me, half), source(line, far, half)
            if far:
                send.arrived(condition, mine, z_sems.at[line, half])
            below, above = both(condition, z > 0), both(condition, z < lines - 1)
            if side >= 0:
                send.start(below, src, mine, z_sems.at[line, half], z=z - 1)
            if side <= 0:
                send.start(above, src, mine, z_sems.at[line, half], z=z + 1)
            send.start(condition, src, mine, y_sems.at[line, half], seq=place.yn)
            on = both(condition, low)
            send.start(on, src, mine, x_sems.at[0, line, half], seq=place.xn)
            send.start(on, src, mine, sib_sems.at[0, line, half], seq=place.sib)

    def from_y(slot):
        for condition, line, _, _, half in pieces(slot):
            theirs = unit(line, place.yn, half)
            send.arrived(condition, theirs, y_sems.at[line, half])
            on = both(condition, high)
            send.start(on, theirs, theirs, x_sems.at[0, line, half], seq=place.xn)
            send.start(on, theirs, theirs, sib_sems.at[1, line, half], seq=place.sib)

    def from_x(slot):
        for condition, line, _, _, half in pieces(slot):
            theirs = unit(line, crossing(0), half)
            send.arrived(condition, theirs, x_sems.at[0, line, half])
            send.start(condition, theirs, theirs, sib_sems.at[2, line, half], seq=place.sib)

    def late_start(slot):
        for condition, line, far, _, half in pieces(slot):
            mine, theirs = unit(line, me, half), unit(line, place.yn, half)
            src, sem = source(line, far, half), x_sems.at[1, line, half]
            above, below = both(condition, high), both(condition, low)
            send.start(above, src, mine, sem, seq=place.xn)
            if half == 0:
                send.start(below, theirs, theirs, sem, seq=place.xn)
            send.start(above, src, mine, sib_sems.at[0, line, half], seq=place.sib)
            send.start(below, theirs, theirs, sib_sems.at[1, line, half], seq=place.sib)

    def late_arrive(slot, row=None):
        for condition, line, _, _, half in pieces(slot):
            theirs = unit(line, crossing(1), half)
            on = condition if row is None else both(condition, row)
            send.arrived(on, theirs, x_sems.at[1, line, half])
            send.start(on, theirs, theirs, sib_sems.at[3, line, half], seq=place.sib)
            if half == 1 and row is high:
                send.start(on, theirs, theirs, x_sems.at[1, line, half], seq=place.yn)

    def from_sib(half, group, condition, seq):
        for line in range(lines):
            theirs = unit(line, seq, half)
            send.arrived(condition, theirs, sib_sems.at[group, line, half])

    def attention_half(half):
        from_sib(half, 0, low, place.sib)
        from_sib(half, 1, high, place.yn + 1 - 2 * core)
        from_sib(half, 2, None, crossing(0, 1 - core))

    def feed_half(half):
        from_sib(half, 0, high, place.sib)
        from_sib(half, 1, low, place.yn + 1 - 2 * core)
        from_sib(half, 3, None, crossing(1, 1 - core))

    kept = []

    def emit(index):
        out = (
            hid_out,
            qkv_out,
            att_out,
            lse_out,
            att_p_out,
            first_out,
            hid_p_out,
            cross_q_out,
            near_p_out,
            near_kv_out,
            co_p_out,
        )[index]
        kept.append(pltpu.make_async_copy(results[index], out, out_sems.at[index]))
        kept[-1].start()

    def row_block(seq):
        return rows_ref.at[pl.ds(pl.multiple_of(seq * tokens, tokens), tokens)]

    def middle(index):
        return pltpu.make_async_copy(
            wts_ref.at[:, pl.ds((3 + index) * dim, dim)], w_mid_ref.at[index], mid_sems.at[index]
        )

    def advance(slot):
        if slot < slots:
            own_unit(slot)
        if slot - 1 < slots:
            from_y(slot - 1)
        from_x(slot - 2)

    own_unit(0)
    own_rows = pltpu.make_async_copy(x_ref.at[place.chip], row_block(me), local_sems.at[1])
    own_rows.start()
    others = (place.xn, place.yn, place.dg)
    for other in place.line():
        send.start(None, norm_ref, small_ref.at[z], norm_sems.at[z], z=other)
    small_ref[z] = norm_ref[...]
    send.start(None, x_ref.at[place.chip], row_block(me), row_sems.at[me], seq=place.sib)
    for other in others:
        send.start(None, x_ref.at[other // 2], row_block(me), row_sems.at[me], seq=other)
    near_load.wait()

    @pl.loop(0, near_p_ref.shape[0] // 512)
    def _(step):
        rows = rows_of(step, 512)
        near_p_ref[rows, :] = mm(near_p_ref[rows, :], perm_ref[...]).astype(bf16)

    emit(8)
    own_unit(1)
    from_y(0)
    advance(2)
    cot_p_ref[...] = mm(cot_ref[...], perm_ref[...]).astype(bf16)
    cot_t_ref[...] = cot_p_ref[...].T
    advance(3)
    for other in others:
        send.arrived(None, row_block(other), row_sems.at[other])
        send.start(None, row_block(other), row_block(other), row_sems.at[other], seq=place.sib)

    for other in place.line():
        send.arrived(None, small_ref.at[other], norm_sems.at[other])
    piece = small_ref.shape[2]
    total = None
    for line in range(lines):
        row = lax.broadcasted_iota(jnp.int32, (piece, dim), 0)
        column = lax.broadcasted_iota(jnp.int32, (piece, dim), 1)
        part = dim // lines
        place_of = jnp.logical_and(row < part, column == row + line * part).astype(bf16)
        term = mm(small_ref[line], place_of)
        total = term if total is None else total + term
    norms_ref[...] = total[: norms_ref.shape[0]]

    advance(4)
    for other in others:
        theirs = other + 1 - 2 * core
        send.arrived(None, row_block(theirs), row_sems.at[theirs])
    send.arrived(None, row_block(place.sib), row_sems.at[place.sib])
    own_rows.wait()
    norm_rows(rows_ref, norms_ref[...], perm_ref, hid_ref)
    emit(0)
    advance(5)
    keep.wait()
    attention_half(0)
    middle(2).start()
    middle(3).start()
    middle(2).wait()
    middle(3).wait()
    near_steps = near_p_ref.shape[0] // 512
    for step in range(max(near_steps, slots - 4)):
        if step < near_steps:
            rows = slice(step * 512, (step + 1) * 512)
            near_kv_ref[rows, :dim] = mm(near_p_ref[rows, :], w_mid_ref[2]).astype(bf16)
            near_kv_ref[rows, dim:] = mm(near_p_ref[rows, :], w_mid_ref[3]).astype(bf16)
        if step + 6 < slots + 2:
            advance(step + 6)
    emit(9)
    for slot in range(slots):
        late_start(slot)
    attention_half(1)
    copies = weight_copies(pairs, dim, wts_ref, w_qkv_ref, qkv_sems)
    for copy in copies + [middle(index) for index in (0, 1, 4)]:
        copy.start()
    for part in range(3):
        copies[part].wait()
        triple_part(part, pairs, hid_ref, w_qkv_ref, qkv_ref)
    emit(1)

    share = lax.rem(me, dim // width)
    seq_rows = pl.ds(pl.multiple_of(place.chip * tokens, tokens), tokens)

    def landing(pair, chip_rows, share):
        lanes = pl.ds(pl.multiple_of(share * width + pair * LANES, LANES), LANES)
        return att_tok_ref.at[chip_rows, lanes]

    for pair in range(pairs):
        lanes = slice(pair * LANES, (pair + 1) * LANES)
        pair_forward(pair, pairs, qkv_ref, att_ref, lse_ref, lambda: None)
        for other in place.plane():
            block = att_ref.at[pl.ds(pl.multiple_of(other * tokens, tokens), tokens), lanes]
            to = landing(pair, seq_rows, share)
            send.start(None, block, to, att_sems.at[pair, me], seq=other)
        own_block = att_ref[pl.ds(pl.multiple_of(me * tokens, tokens), tokens), lanes]
        landing(pair, seq_rows, share)[...] = own_block
        late_arrive(pair)
    emit(2)
    emit(3)

    for index in (0, 1, 4):
        middle(index).wait()
    w_out_ref, w_cq_ref, w_co_ref = (w_mid_ref.at[index] for index in (0, 1, 4))
    for pair in range(pairs):
        for other in place.plane():
            rows = pl.ds(pl.multiple_of(other // 2 * tokens, tokens), tokens)
            send.arrived(None, landing(pair, rows, lax.rem(other, 2)), att_sems.at[pair, other])
    att_p_ref[...] = mm(att_tok_ref[...], perm_ref[...]).astype(bf16)
    emit(4)
    own_x = x_ref[...].reshape(first_ref.shape).astype(f32)
    first_ref[...] = own_x + mm(att_p_ref[...], w_out_ref[...])
    emit(5)
    normed, _ = centre_scale(first_ref[...])
    hidden = (normed * norms_ref[2:3, :] + norms_ref[3:4, :]).astype(bf16)
    hid_p_ref[...] = mm(hidden, perm_ref[...]).astype(bf16)
    emit(6)
    cross_q_ref[...] = mm(hid_p_ref[...], w_cq_ref[...]).astype(bf16)
    emit(7)
    for slot in range(pairs, lines):
        late_arrive(slot)

    def one_span(span):
        span_forward(span, spans, neighbours, presence_ref, cross_q_ref, near_kv_ref, cross_ref)

    pl.loop(0, spans // 2)(one_span)
    late_arrive(lines, high)
    pl.loop(spans // 2, spans)(one_span)
    late_arrive(lines + 1, high)

    ffw = (all_ref.shape[1] - 8 * dim) // 2
    tile = cols
    order = [first + half * tile for half in range(2) for first in range(0, ffw, 2 * tile)]

    def tile_load(index):
        return [
            pltpu.make_async_copy(
                wts_ref.at[:, pl.ds(8 * dim + part * ffw + order[index], tile)],
                w_mid_ref.at[(2 * index + part) % 4],
                feed_sems.at[0, (2 * index + part) % 4],
            )
            for part in range(2)
        ]

    def tile_store(index):
        return [
            pltpu.make_async_copy(
                gfeed_ref.at[(2 * index + part) % 4],
                all_ref.at[:, pl.ds(8 * dim + part * ffw + order[index], tile)],
                feed_sems.at[1, (2 * index + part) % 4],
            )
            for part in range(2)
        ]

    feed_half(0)
    for copy in tile_load(0) + tile_load(1):
        copy.start()
    co_p_ref[...] = mm(cross_ref[...], perm_ref[...]).astype(bf16)
    emit(10)
    second_ref[...] = first_ref[...] + mm(co_p_ref[...], w_co_ref[...])
    normed, _ = centre_scale(second_ref[...])
    hidden = (normed * norms_ref[4:5, :] + norms_ref[5:6, :]).astype(bf16)
    up_p_ref[...] = mm(hidden, perm_ref[...]).astype(bf16)
    up_t_ref[...] = up_p_ref[...].T
    late_arrive(lines + 2, high)

    for index in range(len(order)):
        up_ref, down_ref = w_mid_ref.at[2 * index % 4], w_mid_ref.at[2 * index % 4 + 1]
        for copy in tile_load(index):
            copy.wait()
        if index >= 2:
            for copy in tile_store(index - 2):
                copy.wait()
        active, slope = gelu_parts(mm(up_p_ref[...], up_ref[...]))
        active = active.astype(bf16)
        term = nt(active, down_ref[...])
        result_ref[...] = term if index == 0 else result_ref[...] + term
        gfeed_ref[2 * index % 4 + 1] = mm(cot_t_ref[...], active).astype(bf16)
        grad_up = (mm(cot_p_ref[...], down_ref[...]) * slope).astype(bf16)
        gfeed_ref[2 * index % 4] = mm(up_t_ref[...], grad_up).astype(bf16)
        for copy in tile_store(index):
            copy.start()
        term = nt(grad_up, up_ref[...])
        back_ref[...] = term if index == 0 else back_ref[...] + term
        if index == 0:
            for slot in range(lines + 3, slots):
                late_arrive(slot, high)
            late_arrive(lines, low)
            late_arrive(lines + 1, low)
        if index == 1:
            for slot in range(lines + 2, slots):
                late_arrive(slot, low)
            feed_half(1)
            for copy in tile_load(2) + tile_load(3):
                copy.start()

    out_ref[...] = (second_ref[...] + nt(result_ref[...].astype(bf16), perm_ref[...])).astype(bf16)
    upstream = nt(back_ref[...].astype(bf16), perm_ref[...])
    normed, recip = centre_scale(second_ref[...])
    back, gain, shift = norm_back(upstream, normed, recip, norms_ref[4:5, :])
    gsecond_ref[...] = cot_ref[...].astype(f32) + back
    gnorm_ref[0:1, :] = gain
    gnorm_ref[1:2, :] = shift
    for index in (2, 3):
        for copy in tile_store(index):
            copy.wait()
    for copy in kept:
        copy.wait()
    send.finish()


def forward(lines, pairs, spans, neighbours, presence, w_shard, n_shard, inputs, perm, cot, near):
    unit_rows, unit_cols = w_shard.shape
    seqs, tokens, dim = inputs.shape
    count, length, width = seqs * tokens, 8 * tokens, pairs * LANES
    rows_near = near.shape[0]
    events = 2 * lines - 1
    any_space = pl.BlockSpec(memory_space=pl.ANY)
    vmem = pl.BlockSpec(memory_space=pltpu.VMEM)
    dma = pltpu.SemaphoreType.DMA
    packed = jax.ShapeDtypeStruct((unit_rows * lines, unit_cols * 8), bf16)
    kept = (
        ((length, dim), bf16),
        ((3 * pairs, length, LANES), bf16),
        ((length, width), bf16),
        ((pairs, 2, length), f32),
        ((count, dim), bf16),
        ((count, dim), f32),
        ((count, dim), bf16),
        ((count, dim), bf16),
        ((rows_near, dim), bf16),
        ((rows_near, 2 * dim), bf16),
        ((count, dim), bf16),
    )
    tile = unit_cols // 2
    return pl.pallas_call(
        partial(forward_kernel, lines, pairs, spans, neighbours),
        out_shape=(packed, packed)
        + tuple(jax.ShapeDtypeStruct(*entry) for entry in kept)
        + (
            jax.ShapeDtypeStruct((8, dim), f32),
            jax.ShapeDtypeStruct((count, dim), bf16),
            jax.ShapeDtypeStruct((count, dim), f32),
            jax.ShapeDtypeStruct((2, dim), f32),
        ),
        in_specs=[pl.BlockSpec(memory_space=pltpu.SMEM)] + [vmem] * 5 + [any_space],
        out_specs=(any_space,) * (2 + len(kept)) + (vmem,) * 4,
        scratch_shapes=[pltpu.VMEM(*entry) for entry in kept]
        + [
            pltpu.VMEM((count, dim), f32),
            pltpu.VMEM((unit_rows, unit_cols), bf16),
            pltpu.VMEM((lines,) + n_shard.shape, bf16),
            pltpu.VMEM((length, dim), bf16),
            pltpu.VMEM((dim, 3 * width), bf16),
            pltpu.VMEM((5, dim, dim), bf16),
            pltpu.VMEM((count, dim), bf16),
            pltpu.VMEM((count, dim), bf16),
            pltpu.VMEM((count, dim), bf16),
            pltpu.VMEM((dim, count), bf16),
            pltpu.VMEM((count, dim), bf16),
            pltpu.VMEM((dim, count), bf16),
            pltpu.VMEM((count, dim), f32),
            pltpu.VMEM((count, dim), f32),
            pltpu.VMEM((4, dim, tile), bf16),
            dma((28 * events + 7 + lines + 7 * pairs,)),
            dma((lines, 2)),
            dma((lines, 2)),
            dma((2, lines, 2)),
            dma((4, lines, 2)),
            dma((lines,)),
            dma((8,)),
            dma((pairs, 8)),
            dma((3,)),
            dma((3,)),
            dma((5,)),
            dma((2, 4)),
            dma((len(kept),)),
        ],
        compiler_params=pltpu.CompilerParams(
            vmem_limit_bytes=VMEM_BYTES, collective_id=1, has_side_effects=True
        ),
        name="forward",
    )(presence, w_shard, n_shard, inputs, perm, cot, near)


def reduce_kernel(
    lines,
    grads_ref,
    small_ref,
    shard_ref,
    norms_ref,
    mine_ref,
    sib_ref,
    corner_a_ref,
    corner_b_ref,
    from_x_ref,
    from_y_ref,
    below_ref,
    above_ref,
    plane_ref,
    plane_sum_ref,
    line_ref,
    send_sems,
    load_sems,
    sib_sems,
    a_sems,
    b_sems,
    x_sems,
    y_sems,
    below_sems,
    above_sems,
    plane_sems,
    line_sems,
):
    place = Place(lines)
    z, me = place.z, place.me
    unit_rows, unit_cols = shard_ref.shape
    half = unit_rows // 2
    tile = 32
    place.meet()
    send = Sender(place, send_sems)
    chips = (place.dg, place.yn, place.xn, me)
    corner, over_y, over_x, here = range(4)

    unit = partial(unit_of, grads_ref, lines)

    def load(which, line):
        return pltpu.make_async_copy(
            unit(line, chips[which]), mine_ref.at[which, line], load_sems.at[which, line]
        )

    for other in place.plane():
        send.start(None, small_ref, plane_ref.at[me], plane_sems.at[me], seq=other)
    plane_ref[me] = small_ref[...]

    events = place.events()[::-1]
    for condition, line, _, _ in events:
        for which in range(4):
            theirs = chips[which] + 1 - 2 * place.core
            send.start(
                condition,
                unit(line, theirs),
                sib_ref.at[which, line],
                sib_sems.at[which, line],
                seq=place.sib,
            )
            when(condition, load(which, line).start)

    def add(target, *terms, begin=0, size=unit_rows):
        @pl.loop(0, size // tile)
        def _(step):
            rows = pl.ds(pl.multiple_of(begin + step * tile, tile), tile)
            if len(terms) == 1:
                ref, first = terms[0]
                at = pl.ds(pl.multiple_of(begin - first + step * tile, tile), tile)
                target[rows, :] = target[rows, :] + ref[at, :]
            else:
                total = target[rows, :].astype(f32)
                for ref, first in terms:
                    at = pl.ds(pl.multiple_of(begin - first + step * tile, tile), tile)
                    total = total + ref[at, :].astype(f32)
                target[rows, :] = total.astype(target.dtype)

    def own(which, index):
        condition, line, _, _ = events[index]
        send.arrived(condition, sib_ref.at[which, line], sib_sems.at[which, line])
        when(condition, load(which, line).wait)

    def first(index):
        condition, line, _, _ = events[index]
        own(corner, index)
        target = mine_ref.at[corner, line]
        when(condition, lambda: add(target, (sib_ref.at[corner, line], 0)))
        send.start(
            condition,
            target.at[pl.ds(0, half)],
            corner_a_ref.at[line],
            a_sems.at[line],
            seq=place.xn,
        )
        send.start(
            condition,
            target.at[pl.ds(half, half)],
            corner_b_ref.at[line],
            b_sems.at[line],
            seq=place.yn,
        )

    def second(index):
        condition, line, _, _ = events[index]
        for which, part, sems, begin, to, landing, landing_sems in (
            (over_y, corner_a_ref, a_sems, 0, place.yn, from_y_ref, y_sems),
            (over_x, corner_b_ref, b_sems, half, place.xn, from_x_ref, x_sems),
        ):
            own(which, index)
            send.arrived(condition, part.at[line], sems.at[line])
            target = mine_ref.at[which, line]

            def body(which=which, part=part, begin=begin, target=target):
                add(
                    target,
                    (sib_ref.at[which, line], 0),
                    (part.at[line], begin),
                    begin=begin,
                    size=half,
                )
                add(target, (sib_ref.at[which, line], 0), begin=half - begin, size=half)

            when(condition, body)
            send.start(condition, target, landing.at[line], landing_sems.at[line], seq=to)

    def third(index):
        condition, line, far, side = events[index]
        own(here, index)
        send.arrived(condition, from_x_ref.at[line], x_sems.at[line])
        send.arrived(condition, from_y_ref.at[line], y_sems.at[line])
        target = mine_ref.at[here, line]
        terms = [(ref.at[line], 0) for ref in (sib_ref.at[here], from_x_ref, from_y_ref)]
        if side == 0:
            has_below, has_above = z > 0, z < lines - 1
            add(target, *terms)
            send.arrived(has_below, below_ref.at[line], below_sems.at[line])
            send.arrived(has_above, above_ref.at[line], above_sems.at[line])

            @pl.loop(0, unit_rows // tile)
            def _(step):
                rows = rows_of(step, tile)
                shard_ref[rows, :] = target[rows, :].astype(f32)

            when(has_below, lambda: add(shard_ref, (below_ref.at[line], 0)))
            when(has_above, lambda: add(shard_ref, (above_ref.at[line], 0)))
            return
        landing, sems = (below_ref, below_sems) if side > 0 else (above_ref, above_sems)
        more = both(condition, z > 0) if side > 0 else both(condition, z < lines - 1)
        none = both(condition, z == 0) if side > 0 else both(condition, z == lines - 1)
        send.arrived(more, landing.at[line], sems.at[line])
        when(more, lambda: add(target, *terms, (landing.at[line], 0)))
        when(none, lambda: add(target, *terms))
        send.start(condition, target, landing.at[line], sems.at[line], z=z + side)

    count = len(events)
    first(0)
    first(1)
    for index in range(2, count + 4):
        if index < count:
            first(index)
        if 0 <= index - 2 < count:
            second(index - 2)
        if index == 3:
            for other in place.plane():
                send.arrived(None, plane_ref.at[other], plane_sems.at[other])
            total = plane_ref[0]
            for other in range(1, 8):
                total = total + plane_ref[other]
            plane_sum_ref[...] = total
            line_ref[z] = total
            for other in place.line():
                send.start(None, plane_sum_ref, line_ref.at[z], line_sems.at[z], z=other)
        if 0 <= index - 4 < count:
            third(index - 4)

    for other in place.line():
        send.arrived(None, line_ref.at[other], line_sems.at[other])
    total = line_ref[0]
    for other in range(1, lines):
        total = total + line_ref[other]
    norms_ref[...] = total
    send.finish()


def reduce_grads(lines, grads, small):
    rows, cols = grads.shape
    unit_rows, unit_cols = rows // lines, cols // 8
    half = unit_rows // 2
    any_space = pl.BlockSpec(memory_space=pl.ANY)
    vmem = pl.BlockSpec(memory_space=pltpu.VMEM)
    dma = pltpu.SemaphoreType.DMA
    return pl.pallas_call(
        partial(reduce_kernel, lines),
        out_shape=(
            jax.ShapeDtypeStruct((unit_rows, unit_cols), f32),
            jax.ShapeDtypeStruct(small.shape, f32),
        ),
        in_specs=[any_space, vmem],
        out_specs=(vmem, vmem),
        scratch_shapes=[
            pltpu.VMEM((4, lines, unit_rows, unit_cols), bf16),
            pltpu.VMEM((4, lines, unit_rows, unit_cols), bf16),
            pltpu.VMEM((lines, half, unit_cols), bf16),
            pltpu.VMEM((lines, half, unit_cols), bf16),
            pltpu.VMEM((lines, unit_rows, unit_cols), bf16),
            pltpu.VMEM((lines, unit_rows, unit_cols), bf16),
            pltpu.VMEM((lines, unit_rows, unit_cols), bf16),
            pltpu.VMEM((lines, unit_rows, unit_cols), bf16),
            pltpu.VMEM((8,) + small.shape, f32),
            pltpu.VMEM(small.shape, f32),
            pltpu.VMEM((lines,) + small.shape, f32),
            dma((9 * (2 * lines - 1) + 7 + lines,)),
            dma((4, lines)),
            dma((4, lines)),
            dma((lines,)),
            dma((lines,)),
            dma((lines,)),
            dma((lines,)),
            dma((lines,)),
            dma((lines,)),
            dma((8,)),
            dma((lines,)),
        ],
        compiler_params=pltpu.CompilerParams(
            vmem_limit_bytes=VMEM_BYTES, collective_id=4, has_side_effects=True
        ),
        name="reduce_grads",
    )(grads, small)


def adam_update(grad, weight, first, second, average, rate, decay):
    first = beta_first * first + (1.0 - beta_first) * grad
    second = beta_second * second + (1.0 - beta_second) * grad * grad
    stepped = (
        first / (1.0 - beta_first**STEP) / (jnp.sqrt(second / (1.0 - beta_second**STEP)) + adam_eps)
    )
    weight = weight - rate * (stepped + decay * weight)
    average = ema_decay * average + (1.0 - ema_decay) * weight
    return (first, second, weight, average)


def on_device(
    inputs,
    cotangent,
    neighbours,
    presence,
    row_order,
    w_master,
    w_first,
    w_second,
    w_average,
    n_master,
    n_first,
    n_second,
    n_average,
):
    seqs, tokens, dim = inputs.shape
    heads = dim // HEAD
    devices = lax.axis_size("seq")
    count = seqs * tokens
    length = devices * tokens
    me = lax.axis_index("seq")
    shares = devices // seqs
    held = heads // shares
    pairs = (held + 1) // 2
    width = pairs * LANES
    spare = width - held * HEAD
    sequence, share = me // shares, me % shares

    lines = lax.axis_size("dp")
    planar = devices == 8 and seqs == 4 and spare == 0
    perm = (jnp.arange(dim)[:, None] == row_order[None, :]).astype(bf16)
    perm_att = perm
    if spare:
        perm_att = jnp.pad(perm.reshape(shares, held * HEAD, dim), ((0, 0), (0, spare), (0, 0)))
        perm_att = perm_att.reshape(shares * width, dim)
    x = inputs.reshape(count, dim)
    spans = seqs * neighbours.shape[1]
    each = neighbours.shape[2]
    near = neighbours.reshape(-1, dim)
    live = presence.reshape(-1)
    part = n_master.shape[1]
    if planar:
        small = jnp.pad(n_master.astype(bf16), ((0, 16 - 6), (0, -part % LANES)))
        (
            weights,
            grads,
            hid,
            qkv,
            att,
            lse,
            att_p,
            first,
            hid_p,
            cross_q,
            near_p,
            near_kv,
            co_p,
            norms,
            outputs,
            gsecond,
            gnorm_e,
        ) = forward(
            lines,
            pairs,
            spans,
            each,
            live,
            w_master,
            small,
            inputs,
            perm,
            cotangent.reshape(count, dim),
            near,
        )
    else:
        weights = lax.all_gather(w_master.astype(bf16), "dp", axis=0, tiled=True)
        weights = lax.all_gather(weights, "seq", axis=1, tiled=True)
        norms = lax.all_gather(n_master.astype(bf16), "dp", axis=1, tiled=True).astype(f32)
        rows = lax.all_to_all(jnp.repeat(inputs, shares, axis=0), "seq", 0, 0)
        rows = rows.reshape(length, dim)
        w_qkv = weights[:, : 3 * dim].reshape(dim, 3, shares, held * HEAD)
        w_qkv = lax.dynamic_index_in_dim(w_qkv, share, axis=2, keepdims=False)
        w_qkv = jnp.pad(w_qkv, ((0, 0), (0, 0), (0, spare))).reshape(dim, 3 * width)
        hid, qkv, att, lse = self_forward(pairs, rows, norms, perm, w_qkv)
        att_tok = (
            lax.all_to_all(att.reshape(devices, tokens, width), "seq", 0, 0)
            .reshape(seqs, shares, tokens, width)
            .transpose(0, 2, 1, 3)
            .reshape(count, shares * width)
        )
        att_p, first, hid_p, cross_q, near_p, near_kv, co_p, second = cross_forward(
            spans, each, live, att_tok, x, norms, perm, perm_att, near, weights
        )
        outputs, gsecond, grads, gnorm_e = feed(
            second, cotangent.reshape(count, dim), norms, perm, weights
        )
    gfirst, gatt_tok, grads, gnorm_c = cross_backward(
        spans,
        each,
        lines if planar else 0,
        live,
        gsecond,
        first,
        norms,
        perm,
        perm_att,
        att_p,
        hid_p,
        cross_q,
        near_p,
        near_kv,
        co_p,
        weights,
        grads,
    )
    if planar:
        others = jnp.concatenate(
            [jnp.zeros((2, dim), f32), gnorm_c, gnorm_e, jnp.zeros((2, dim), f32)], axis=0
        )
        grads, grad_inputs, norm_grads = finish(
            pairs,
            lines,
            qkv,
            att,
            gatt_tok,
            lse,
            hid,
            x,
            gfirst,
            norms,
            perm,
            others,
            weights,
            grads,
        )
        grad_shard, norm_sums = reduce_grads(lines, grads, norm_grads)
        norm_shard = lax.dynamic_slice(norm_sums, (0, lax.axis_index("dp") * part), (6, part))
    else:
        gatt = lax.all_to_all(
            gatt_tok.reshape(seqs, tokens, shares, width)
            .transpose(0, 2, 1, 3)
            .reshape(devices, tokens, width),
            "seq",
            0,
            0,
        ).reshape(length, width)
        gqkv, ghid = self_backward(pairs, qkv, att, gatt, lse, hid, w_qkv)
        parts = (
            lax.all_to_all(ghid.reshape(devices, tokens, dim), "seq", 0, 0)
            .reshape(seqs, shares, tokens, dim)
            .transpose(1, 0, 2, 3)
            .reshape(shares, count, dim)
        )
        grad_inputs, gnorm_a = last_norm(parts, x, gfirst, norms, perm)
        gqkv = gqkv.reshape(dim, 3, 1, width)[..., : held * HEAD]
        gqkv = jnp.where(jnp.arange(shares)[:, None] == share, gqkv, jnp.zeros_like(gqkv))
        grads = lax.dynamic_update_slice(grads, gqkv.reshape(dim, 3 * dim), (0, 0))
        norm_grads = lax.psum(jnp.concatenate([gnorm_a, gnorm_c, gnorm_e], axis=0), "seq")
        partial_sum = lax.psum_scatter(grads, "seq", scatter_dimension=1, tiled=True)
        grad_shard = lax.psum_scatter(partial_sum, "dp", scatter_dimension=0, tiled=True)
        grad_shard = grad_shard.astype(f32)
        norm_shard = lax.psum_scatter(
            norm_grads.astype(bf16), "dp", scatter_dimension=1, tiled=True
        ).astype(f32)
    w_first_new, w_second_new, w_new, w_average_new = adam_update(
        grad_shard, w_master, w_first, w_second, w_average, learn_rate, weight_decay
    )
    n_first_new, n_second_new, n_new, n_average_new = adam_update(
        norm_shard, n_master, n_first, n_second, n_average, norm_rate, 0.0
    )
    return (
        outputs.reshape(seqs, tokens, dim),
        grad_inputs.reshape(seqs, tokens, dim),
        w_first_new,
        w_second_new,
        w_new,
        w_average_new,
        n_first_new,
        n_second_new,
        n_new,
        n_average_new,
    )


def solution(mesh):
    in_specs = (
        P("dp", "seq", None),
        P("dp", "seq", None),
        P("dp", "seq", None, None, None),
        P("dp", "seq", None),
        P(),
        P("dp", "seq"),
        P("dp", "seq"),
        P("dp", "seq"),
        P("dp", "seq"),
        P(None, "dp"),
        P(None, "dp"),
        P(None, "dp"),
        P(None, "dp"),
    )
    out_specs = (
        P("dp", "seq", None),
        P("dp", "seq", None),
        P("dp", "seq"),
        P("dp", "seq"),
        P("dp", "seq"),
        P("dp", "seq"),
        P(None, "dp"),
        P(None, "dp"),
        P(None, "dp"),
        P(None, "dp"),
    )
    return jax.shard_map(
        on_device, mesh=mesh, in_specs=in_specs, out_specs=out_specs, check_vma=False
    )
```

```python
from functools import partial

import jax
import jax.numpy as jnp
from jax import lax
from jax.experimental import pallas as pl
from jax.experimental.pallas import tpu as pltpu
from jax.sharding import PartitionSpec as P

HEAD = 64
STEP = 5
LANES = 128
SCALE = HEAD ** (-0.5)

beta_first = 0.9
beta_second = 0.95
adam_eps = 1e-08
learn_rate = 0.04
norm_rate = 0.6
weight_decay = 0.1
ema_decay = 0.5
norm_eps = 1e-05
masked_score = -1e30
VMEM_BYTES = 60 * 1024 * 1024
bf16 = jnp.bfloat16
f32 = jnp.float32


def mm(left, right):
    return lax.dot_general(left, right, (((1,), (0,)), ((), ())), preferred_element_type=f32)


def nt(left, right):
    return lax.dot_general(left, right, (((1,), (1,)), ((), ())), preferred_element_type=f32)


def tn(left, right):
    return lax.dot_general(left, right, (((0,), (0,)), ((), ())), preferred_element_type=f32)


def params():
    return pltpu.CompilerParams(vmem_limit_bytes=VMEM_BYTES)


def rows_of(index, size):
    return pl.ds(pl.multiple_of(index * size, size), size)


def centre_scale(values):
    centre = jnp.mean(values, axis=-1, keepdims=True)
    centred = values - centre
    spread = jnp.mean(centred * centred, axis=-1, keepdims=True)
    recip = lax.rsqrt(spread + norm_eps)
    return centred * recip, recip


def norm_back(upstream, normed, recip, gain):
    scaled = upstream * gain
    inner = (
        scaled
        - jnp.mean(scaled, axis=-1, keepdims=True)
        - normed * jnp.mean(scaled * normed, axis=-1, keepdims=True)
    )
    return (
        recip * inner,
        jnp.sum(upstream * normed, axis=0, keepdims=True),
        jnp.sum(upstream, axis=0, keepdims=True),
    )


def gelu_parts(value):
    const = 0.7978845608028654
    square = value * value
    bend = jnp.tanh(const * value * (1.0 + 0.044715 * square))
    half = 0.5 * (1.0 + bend)
    slope = half + 0.5 * value * (1.0 - bend * bend) * (const * (1.0 + 3 * 0.044715 * square))
    return value * half, slope


def head_mask(rows, half):
    lane = lax.broadcasted_iota(jnp.int32, (rows, LANES), 1)
    return (lane < HEAD) if half == 0 else (lane >= HEAD)


def pick(mask, value):
    return jnp.where(mask, value, jnp.zeros_like(value))


MESH = pl.DeviceIdType.MESH


class Place:
    def __init__(self, lines):
        self.lines = lines
        self.z = lax.axis_index("dp")
        self.me = lax.axis_index("seq")
        core, x, y = self.me % 2, (self.me // 2) % 2, self.me // 4
        self.core, self.x, self.y, self.chip = core, x, y, self.me // 2
        self.sib = self.me + 1 - 2 * core
        self.xn = self.me + 2 - 4 * x
        self.yn = self.me + 4 - 8 * y
        self.dg = self.xn + 4 - 8 * y

    def events(self):
        found = [(None, self.z, 0, 0)]
        for far in range(1, self.lines):
            found.append((self.z >= far, self.z - far, far, -1))
            found.append((self.z + far < self.lines, self.z + far, far, 1))
        return found

    def plane(self):
        return [lax.rem(self.me + step, 8) for step in range(1, 8)]

    def line(self):
        return [lax.rem(self.z + step, self.lines) for step in range(1, self.lines)]

    def meet(self):
        barrier = pltpu.get_barrier_semaphore()
        for other in self.plane():
            pl.semaphore_signal(
                barrier, inc=1, device_id={"dp": self.z, "seq": other}, device_id_type=MESH
            )
        for other in self.line():
            pl.semaphore_signal(
                barrier, inc=1, device_id={"dp": other, "seq": self.me}, device_id_type=MESH
            )
        pl.semaphore_wait(barrier, 7 + self.lines - 1)


def when(condition, body):
    if condition is None:
        body()
    else:
        pl.when(condition)(body)


def both(first, second):
    if first is None or second is None:
        return second if first is None else first
    return jnp.logical_and(first, second)


class Sender:
    def __init__(self, place, send_sems):
        self.place, self.sems, self.open = place, send_sems, []

    def start(self, condition, src, dst, recv_sem, z=None, seq=None):
        place = self.place
        target = {"dp": place.z if z is None else z, "seq": place.me if seq is None else seq}
        copy = pltpu.make_async_remote_copy(
            src_ref=src,
            dst_ref=dst,
            send_sem=self.sems.at[len(self.open)],
            recv_sem=recv_sem,
            device_id=target,
            device_id_type=MESH,
        )
        self.open.append((condition, copy))
        when(condition, copy.start)

    def arrived(self, condition, ref, recv_sem):
        copy = pltpu.make_async_remote_copy(
            src_ref=ref,
            dst_ref=ref,
            send_sem=self.sems.at[0],
            recv_sem=recv_sem,
            device_id={"dp": self.place.z, "seq": self.place.sib},
            device_id_type=MESH,
        )
        when(condition, copy.wait_recv)

    def finish(self):
        for condition, copy in self.open:
            when(condition, copy.wait_send)


class Weave:
    def __init__(self, steps):
        self.steps = list(steps)

    def some(self, count):
        for _ in range(min(count, len(self.steps))):
            self.steps.pop(0)()

    def rest(self):
        self.some(len(self.steps))


def unit_of(ref, lines, line, seq, begin=0, size=None):
    rows, cols = ref.shape[0] // lines, ref.shape[1] // 8
    size = rows if size is None else size
    return ref.at[
        pl.ds(pl.multiple_of(line * rows + begin, 16), size),
        pl.ds(pl.multiple_of(seq * cols, cols), cols),
    ]


def weight_copies(pairs, dim, wts_ref, w_ref, sems):
    width = pairs * LANES
    first = lax.rem(lax.axis_index("seq"), dim // width) * width
    return [
        pltpu.make_async_copy(
            wts_ref.at[:, pl.ds(pl.multiple_of(first + part * dim, LANES), width)],
            w_ref.at[:, pl.ds(part * width, width)],
            sems.at[part],
        )
        for part in range(3)
    ]


def pair_forward(pair, pairs, qkv_ref, att_ref, lse_ref, between):
    length = att_ref.shape[0]
    tile = 256
    below = lax.broadcasted_iota(jnp.int32, (tile, tile), 1) <= lax.broadcasted_iota(
        jnp.int32, (tile, tile), 0
    )
    masks = [head_mask(tile, 0), head_mask(tile, 1)]
    lane = lax.broadcasted_iota(jnp.int32, (tile, LANES), 1)
    for step in range(length // tile):
        rows = slice(step * tile, (step + 1) * tile)
        query = qkv_ref[pair, rows, :] * SCALE
        keys_here = qkv_ref[pairs + pair, rows, :]
        values_here = qkv_ref[2 * pairs + pair, rows, :]
        outs, logs = [], []
        for half in range(2):
            mine = pick(masks[half], query)
            here = jnp.where(below, nt(mine, keys_here), masked_score)
            peak = jnp.max(here, axis=-1, keepdims=True)
            if step:
                past = nt(mine, qkv_ref[pairs + pair, : step * tile, :])
                peak = jnp.maximum(peak, jnp.max(past, axis=-1, keepdims=True))
                past = jnp.exp(past - peak)
            here = jnp.exp(here - peak)
            total = jnp.sum(here, axis=-1, keepdims=True)
            out = mm(here.astype(bf16), values_here)
            if step:
                total = total + jnp.sum(past, axis=-1, keepdims=True)
                out = out + mm(past.astype(bf16), qkv_ref[2 * pairs + pair, : step * tile, :])
            outs.append(out / total)
            logs.append(peak + jnp.log(total))
        lse_ref[pair, :, rows] = jnp.where(lane == 0, logs[0], logs[1]).T[0:2, :]
        att_ref[rows, pl.ds(pl.multiple_of(pair * LANES, LANES), LANES)] = jnp.where(
            masks[0], outs[0], outs[1]
        ).astype(bf16)
        between()


def norm_rows(x_ref, norms, perm_ref, hid_ref):
    tile = 256

    @pl.loop(0, x_ref.shape[0] // tile)
    def _(step):
        rows = rows_of(step, tile)
        normed, _ = centre_scale(x_ref[rows, :].astype(f32))
        hidden = (normed * norms[0:1, :] + norms[1:2, :]).astype(bf16)
        hid_ref[rows, :] = mm(hidden, perm_ref[...]).astype(bf16)


def triple_part(part, pairs, hid_ref, w_ref, qkv_ref):
    width = pairs * LANES
    triple = mm(hid_ref[...], w_ref[:, part * width : (part + 1) * width]).astype(bf16)
    for pair in range(pairs):
        qkv_ref[part * pairs + pair] = triple[:, pair * LANES : (pair + 1) * LANES]


def self_forward_kernel(
    pairs, x_ref, norms_ref, perm_ref, w_ref, hid_ref, qkv_ref, att_ref, lse_ref
):
    norm_rows(x_ref, norms_ref, perm_ref, hid_ref)
    for part in range(3):
        triple_part(part, pairs, hid_ref, w_ref, qkv_ref)

    @pl.loop(0, pairs)
    def _(pair):
        pair_forward(pair, pairs, qkv_ref, att_ref, lse_ref, lambda: None)


def self_forward(pairs, x, norms, perm, w):
    length, dim = x.shape
    return pl.pallas_call(
        partial(self_forward_kernel, pairs),
        out_shape=(
            jax.ShapeDtypeStruct((length, dim), bf16),
            jax.ShapeDtypeStruct((3 * pairs, length, LANES), bf16),
            jax.ShapeDtypeStruct((length, pairs * LANES), bf16),
            jax.ShapeDtypeStruct((pairs, 2, length), f32),
        ),
        compiler_params=params(),
        name="self_forward",
    )(x, norms, perm, w)


def pair_backward(pair, pairs, qkv_ref, att_ref, gatt_ref, lse_ref, grad_ref, acc_ref, between):
    length = att_ref.shape[0]
    width = pairs * LANES
    tile = 256
    above = lax.broadcasted_iota(jnp.int32, (tile, tile), 0) <= lax.broadcasted_iota(
        jnp.int32, (tile, tile), 1
    )
    masks = [head_mask(tile, 0), head_mask(tile, 1)]
    lanes = pl.ds(pl.multiple_of(pair * LANES, LANES), LANES)
    for step in range(length // tile):
        rows = slice(step * tile, (step + 1) * tile)
        query = qkv_ref[pair, rows, :] * SCALE
        grad_out = gatt_ref[rows, lanes]
        product = grad_out.astype(f32) * att_ref[rows, lanes].astype(f32)
        queries = [pick(masks[half], query) for half in range(2)]
        grads = [pick(masks[half], grad_out) for half in range(2)]
        deltas = [jnp.sum(pick(masks[half], product).T, axis=0, keepdims=True) for half in range(2)]
        grad_query = [None, None]
        for other in range(step + 1):
            cols = slice(other * tile, (other + 1) * tile)
            keys = qkv_ref[pairs + pair, cols, :]
            values = qkv_ref[2 * pairs + pair, cols, :]
            key_part = value_part = None
            for half in range(2):
                scores = nt(keys, queries[half])
                if other == step:
                    scores = jnp.where(above, scores, masked_score)
                probs = jnp.exp(scores - lse_ref[pair, half : half + 1, rows])
                grad_scores = (probs * (nt(values, grads[half]) - deltas[half])).astype(bf16)
                query_term = tn(grad_scores, keys)
                grad_query[half] = (
                    query_term if grad_query[half] is None else grad_query[half] + query_term
                )
                key_term = mm(grad_scores, queries[half])
                value_term = mm(probs.astype(bf16), grads[half])
                key_part = key_term if key_part is None else key_part + key_term
                value_part = value_term if value_part is None else value_part + value_term
            if other == step:
                acc_ref[0, cols, :] = key_part
                acc_ref[1, cols, :] = value_part
            else:
                acc_ref[0, cols, :] += key_part
                acc_ref[1, cols, :] += value_part
        grad_ref[rows, lanes] = (jnp.where(masks[0], grad_query[0], grad_query[1]) * SCALE).astype(
            bf16
        )
        between()
    for part in range(2):
        lanes_to = pl.ds(pl.multiple_of((part + 1) * width + pair * LANES, LANES), LANES)
        grad_ref[:, lanes_to] = acc_ref[part].astype(bf16)


def self_backward_kernel(
    pairs,
    qkv_ref,
    att_ref,
    gatt_ref,
    lse_ref,
    hid_ref,
    w_ref,
    gw_ref,
    ghid_ref,
    grad_ref,
    acc_ref,
):
    length = att_ref.shape[0]
    width = pairs * LANES
    attention = (qkv_ref, att_ref, gatt_ref, lse_ref, grad_ref, acc_ref)

    @pl.loop(0, pairs)
    def _(pair):
        pair_backward(pair, pairs, *attention, lambda: None)

    hidden_t = hid_ref[...].T
    for part in range(3):
        cols = slice(part * width, (part + 1) * width)
        gw_ref[:, cols] = mm(hidden_t, grad_ref[:, cols]).astype(bf16)
    for begin in range(0, length, 256):
        rows = slice(begin, begin + 256)
        ghid_ref[rows, :] = nt(grad_ref[rows, :], w_ref[...]).astype(bf16)


def self_backward(pairs, qkv, att, gatt, lse, hid, w):
    length, dim = hid.shape
    width = pairs * LANES
    return pl.pallas_call(
        partial(self_backward_kernel, pairs),
        out_shape=(
            jax.ShapeDtypeStruct((dim, 3 * width), bf16),
            jax.ShapeDtypeStruct((length, dim), bf16),
        ),
        scratch_shapes=[
            pltpu.VMEM((length, 3 * width), bf16),
            pltpu.VMEM((2, length, LANES), f32),
        ],
        compiler_params=params(),
        name="self_backward",
    )(qkv, att, gatt, lse, hid, w)


def finish_kernel(
    pairs,
    lines,
    qkv_ref,
    att_ref,
    gatt_ref,
    lse_ref,
    hid_ref,
    x_ref,
    gfirst_ref,
    norms_ref,
    perm_ref,
    others_ref,
    wts_ref,
    _,
    all_ref,
    gin_ref,
    small_ref,
    grad_ref,
    acc_ref,
    gw_ref,
    w_ref,
    sems,
    ghid_ref,
    gsib_ref,
    parts_ref,
    gsib_sems,
    part_sems,
    send_sems,
):
    length, dim = hid_ref.shape
    width = pairs * LANES
    tokens = length // 8
    place = Place(lines)
    me, core = place.me, place.core
    place.meet()
    send = Sender(place, send_sems)
    copies = weight_copies(pairs, dim, wts_ref, w_ref, sems)
    for copy in copies:
        copy.start()

    share_count = dim // width
    share = lax.rem(me, share_count)
    gw_ref[3] = jnp.zeros_like(gw_ref[3])
    outs = []
    for part in range(3):
        for other in range(1, share_count):
            first = part * dim + lax.rem(share + other, share_count) * width
            outs.append(
                pltpu.make_async_copy(
                    gw_ref.at[3],
                    all_ref.at[:, pl.ds(pl.multiple_of(first, LANES), width)],
                    sems.at[6 + part * (share_count - 1) + other - 1],
                )
            )
            outs[-1].start()

    attention = (qkv_ref, att_ref, gatt_ref, lse_ref, grad_ref, acc_ref)

    @pl.loop(0, pairs)
    def _(pair):
        pair_backward(pair, pairs, *attention, lambda: None)

    def token_rows(device):
        return pl.ds(pl.multiple_of(device * tokens, tokens), tokens)

    for copy in copies:
        copy.wait()
    for begin in range(0, length, 256):
        rows = slice(begin, begin + 256)
        ghid_ref[rows, :] = nt(grad_ref[rows, :], w_ref[...]).astype(bf16)
    chips = (place.xn // 2, place.yn // 2, place.dg // 2, place.chip)
    for chip in chips:
        theirs = chip * 2 + 1 - core
        send.start(
            None, ghid_ref.at[token_rows(theirs)], gsib_ref.at[chip], gsib_sems.at[chip], seq=place.sib
        )
    for chip in chips:
        send.arrived(None, gsib_ref.at[chip], gsib_sems.at[chip])
        rows = token_rows(chip * 2 + core)
        total = (ghid_ref[rows, :].astype(f32) + gsib_ref[chip].astype(f32)).astype(bf16)
        if chip is place.chip:
            parts_ref[chip] = total
        else:
            ghid_ref[rows, :] = total
            send.start(
                None,
                ghid_ref.at[rows],
                parts_ref.at[place.chip],
                part_sems.at[place.chip],
                seq=chip * 2 + core,
            )

    hidden_t = hid_ref[...].T
    for part in range(3):
        gw_ref[part] = mm(hidden_t, grad_ref[:, part * width : (part + 1) * width]).astype(bf16)
        first = part * dim + share * width
        outs.append(
            pltpu.make_async_copy(
                gw_ref.at[part],
                all_ref.at[:, pl.ds(pl.multiple_of(first, LANES), width)],
                sems.at[3 + part],
            )
        )
        outs[-1].start()

    for chip in chips[:3]:
        send.arrived(None, parts_ref.at[chip], part_sems.at[chip])
    gain_sum = shift_sum = None
    for chip in range(4):
        rows = slice(chip * tokens, (chip + 1) * tokens)
        upstream = nt(parts_ref[chip], perm_ref[...])
        normed, recip = centre_scale(x_ref[rows, :].astype(f32))
        back, gain, shift = norm_back(upstream, normed, recip, norms_ref[0:1, :])
        gin_ref[rows, :] = gfirst_ref[rows, :] + back
        gain_sum = gain if gain_sum is None else gain_sum + gain
        shift_sum = shift if shift_sum is None else shift_sum + shift
    small_ref[...] = others_ref[...]
    small_ref[0:1, :] = gain_sum
    small_ref[1:2, :] = shift_sum
    for copy in outs:
        copy.wait()
    send.finish()


def finish(pairs, lines, qkv, att, gatt, lse, hid, x, gfirst, norms, perm, others, weights, grads):
    length, dim = hid.shape
    width = pairs * LANES
    count = x.shape[0]
    tokens = length // 8
    any_space = pl.BlockSpec(memory_space=pl.ANY)
    vmem = pl.BlockSpec(memory_space=pltpu.VMEM)
    dma = pltpu.SemaphoreType.DMA
    return pl.pallas_call(
        partial(finish_kernel, pairs, lines),
        out_shape=(
            jax.ShapeDtypeStruct(grads.shape, bf16),
            jax.ShapeDtypeStruct((count, dim), f32),
            jax.ShapeDtypeStruct((8, dim), f32),
        ),
        in_specs=[vmem] * 10 + [any_space] * 2,
        out_specs=(any_space, vmem, vmem),
        scratch_shapes=[
            pltpu.VMEM((length, 3 * width), bf16),
            pltpu.VMEM((2, length, LANES), f32),
            pltpu.VMEM((4, dim, width), bf16),
            pltpu.VMEM((dim, 3 * width), bf16),
            dma((6 + 3 * (dim // width),)),
            pltpu.VMEM((length, dim), bf16),
            pltpu.VMEM((4, tokens, dim), bf16),
            pltpu.VMEM((4, tokens, dim), bf16),
            dma((4,)),
            dma((4,)),
            dma((8,)),
        ],
        input_output_aliases={11: 0},
        compiler_params=pltpu.CompilerParams(
            vmem_limit_bytes=VMEM_BYTES, collective_id=3, has_side_effects=True
        ),
        name="finish",
    )(qkv, att, gatt, lse, hid, x, gfirst, norms, perm, others, weights, grads)


def spread_heads(block, rows, group):
    lane = lax.broadcasted_iota(jnp.int32, block.shape, 1) // HEAD
    return jnp.concatenate([pick(lane == head, block) for head in range(group)], axis=0)


def gather_heads(stacked, rows, group):
    lane = lax.broadcasted_iota(jnp.int32, (rows, stacked.shape[1]), 1) // HEAD
    out = None
    for head in range(group):
        part = pick(lane == head, stacked[head * rows : (head + 1) * rows])
        out = part if out is None else out + part
    return out


def live_keys(presence_ref, span, shape, axis, neighbours, each):
    index = lax.broadcasted_iota(jnp.int32, shape, axis) // each
    live = jnp.zeros(shape, f32)
    anyone = None
    for which in range(neighbours):
        here = presence_ref[span * neighbours + which]
        there = jnp.where(here > 0, 1.0, 0.0).astype(f32)
        live = jnp.where(index == which, there, live)
        anyone = here if anyone is None else jnp.maximum(anyone, here)
    return live, anyone.astype(f32)


def span_forward(span, spans, neighbours, presence_ref, cross_q_ref, near_kv_ref, cross_ref):
    count, dim = cross_q_ref.shape
    span_len = count // spans
    near = near_kv_ref.shape[0] // spans
    group = 256 // HEAD
    rows = rows_of(span, span_len)
    keys = rows_of(span, near)
    live, anyone = live_keys(presence_ref, span, (1, near), 1, neighbours, near // neighbours)
    for begin in range(0, dim, group * HEAD):
        lanes = slice(begin, begin + group * HEAD)
        lanes_v = slice(dim + begin, dim + begin + group * HEAD)
        query = spread_heads(cross_q_ref[rows, lanes] * SCALE, span_len, group)
        scores = jnp.where(live > 0, nt(query, near_kv_ref[keys, lanes]), masked_score)
        peak = jnp.max(scores, axis=-1, keepdims=True)
        expon = jnp.exp(scores - peak) * live
        total = jnp.sum(expon, axis=-1, keepdims=True) + 1.0 - anyone
        out = mm(expon.astype(bf16), near_kv_ref[keys, lanes_v]) / total
        cross_ref[rows, lanes] = gather_heads(out, span_len, group).astype(bf16)


def cross_forward_kernel(
    spans,
    neighbours,
    presence_ref,
    att_ref,
    x_ref,
    norms_ref,
    perm_ref,
    perm_att_ref,
    near_ref,
    w_out_ref,
    w_cq_ref,
    w_ck_ref,
    w_cv_ref,
    w_co_ref,
    att_p_ref,
    first_ref,
    hid_p_ref,
    cross_q_ref,
    near_p_ref,
    near_kv_ref,
    co_p_ref,
    second_ref,
    cross_ref,
):
    count, dim = x_ref.shape
    rows_near = near_ref.shape[0]
    tile = 512

    att_p_ref[...] = mm(att_ref[...], perm_att_ref[...]).astype(bf16)
    first_ref[...] = x_ref[...].astype(f32) + mm(att_p_ref[...], w_out_ref[...])

    normed, _ = centre_scale(first_ref[...])
    hidden = (normed * norms_ref[2:3, :] + norms_ref[3:4, :]).astype(bf16)
    hid_p_ref[...] = mm(hidden, perm_ref[...]).astype(bf16)
    cross_q_ref[...] = mm(hid_p_ref[...], w_cq_ref[...]).astype(bf16)

    @pl.loop(0, rows_near // tile)
    def _(step):
        rows = rows_of(step, tile)
        near_p_ref[rows, :] = mm(near_ref[rows, :], perm_ref[...]).astype(bf16)
        near_kv_ref[rows, :dim] = mm(near_p_ref[rows, :], w_ck_ref[...]).astype(bf16)
        near_kv_ref[rows, dim:] = mm(near_p_ref[rows, :], w_cv_ref[...]).astype(bf16)

    @pl.loop(0, spans)
    def _(span):
        span_forward(span, spans, neighbours, presence_ref, cross_q_ref, near_kv_ref, cross_ref)

    co_p_ref[...] = mm(cross_ref[...], perm_ref[...]).astype(bf16)
    second_ref[...] = first_ref[...] + mm(co_p_ref[...], w_co_ref[...])


def column_block(rows, width, index):
    return pl.BlockSpec((rows, width), lambda *_: (0, index), pipeline_mode=pl.Buffered(1))


def whole(array):
    return pl.BlockSpec(array.shape, lambda *_: (0,) * array.ndim, pipeline_mode=pl.Buffered(1))


def whole_shape(shape):
    return pl.BlockSpec(shape, lambda *_: (0,) * len(shape), pipeline_mode=pl.Buffered(1))


def cross_forward(spans, neighbours, presence, att, x, norms, perm, perm_att, near, weights):
    count, dim = x.shape
    rows_near = near.shape[0]
    out_shape = (
        jax.ShapeDtypeStruct((count, dim), bf16),
        jax.ShapeDtypeStruct((count, dim), f32),
        jax.ShapeDtypeStruct((count, dim), bf16),
        jax.ShapeDtypeStruct((count, dim), bf16),
        jax.ShapeDtypeStruct((rows_near, dim), bf16),
        jax.ShapeDtypeStruct((rows_near, 2 * dim), bf16),
        jax.ShapeDtypeStruct((count, dim), bf16),
        jax.ShapeDtypeStruct((count, dim), f32),
    )
    operands = (att, x, norms, perm, perm_att, near)
    return pl.pallas_call(
        partial(cross_forward_kernel, spans, neighbours),
        out_shape=out_shape,
        grid=(1,),
        in_specs=[pl.BlockSpec(memory_space=pltpu.SMEM)]
        + [whole(op) for op in operands]
        + [column_block(dim, dim, index) for index in (3, 4, 5, 6, 7)],
        out_specs=tuple(whole_shape(shape.shape) for shape in out_shape),
        scratch_shapes=[pltpu.VMEM((count, dim), bf16)],
        compiler_params=params(),
        name="cross_forward",
    )(presence, *operands, *([weights] * 5))


def feed_kernel(
    second_ref,
    cot_ref,
    norms_ref,
    perm_ref,
    w_up_ref,
    w_down_ref,
    out_ref,
    gsecond_ref,
    all_ref,
    gnorm_ref,
    hid_p_ref,
    hid_t_ref,
    cot_p_ref,
    cot_t_ref,
    result_ref,
    back_ref,
    gup_ref,
    gdown_ref,
    sems,
):
    step = pl.program_id(0)
    last = pl.num_programs(0) - 1
    slot = lax.rem(step, 2)
    dim, tile = w_up_ref.shape

    def copies(step, slot):
        up = pl.multiple_of(8 * dim + step * tile, tile)
        down = pl.multiple_of(8 * dim + (last + 1 + step) * tile, tile)
        return (
            pltpu.make_async_copy(gup_ref.at[slot], all_ref.at[:, pl.ds(up, tile)], sems.at[0, slot]),
            pltpu.make_async_copy(
                gdown_ref.at[slot], all_ref.at[:, pl.ds(down, tile)], sems.at[1, slot]
            ),
        )

    @pl.when(step >= 2)
    def _():
        for copy in copies(step - 2, slot):
            copy.wait()

    @pl.when(step == 0)
    def _():
        normed, _ = centre_scale(second_ref[...])
        hidden = (normed * norms_ref[4:5, :] + norms_ref[5:6, :]).astype(bf16)
        hid_p_ref[...] = mm(hidden, perm_ref[...]).astype(bf16)
        hid_t_ref[...] = hid_p_ref[...].T
        cot_p_ref[...] = mm(cot_ref[...], perm_ref[...]).astype(bf16)
        cot_t_ref[...] = cot_p_ref[...].T
        result_ref[...] = jnp.zeros_like(result_ref)
        back_ref[...] = jnp.zeros_like(back_ref)

    upward = mm(hid_p_ref[...], w_up_ref[...])
    active, slope = gelu_parts(upward)
    active = active.astype(bf16)
    result_ref[...] += nt(active, w_down_ref[...])
    gdown_ref[slot] = mm(cot_t_ref[...], active).astype(bf16)
    grad_up = (mm(cot_p_ref[...], w_down_ref[...]) * slope).astype(bf16)
    gup_ref[slot] = mm(hid_t_ref[...], grad_up).astype(bf16)
    for copy in copies(step, slot):
        copy.start()
    back_ref[...] += nt(grad_up, w_up_ref[...])

    @pl.when(step == last)
    def _():
        out_ref[...] = (
            second_ref[...] + nt(result_ref[...].astype(bf16), perm_ref[...])
        ).astype(bf16)
        upstream = nt(back_ref[...].astype(bf16), perm_ref[...])
        normed, recip = centre_scale(second_ref[...])
        back, gain, shift = norm_back(upstream, normed, recip, norms_ref[4:5, :])
        gsecond_ref[...] = cot_ref[...].astype(f32) + back
        gnorm_ref[0:1, :] = gain
        gnorm_ref[1:2, :] = shift
        for which in (step - 1, step):
            for copy in copies(which, lax.rem(which, 2)):
                copy.wait()


def feed(second, cot, norms, perm, weights):
    count, dim = second.shape
    ffw = (weights.shape[1] - 8 * dim) // 2
    tile = 512
    first_up = 8 * dim // tile
    first_down = (8 * dim + ffw) // tile
    out_shape = (
        jax.ShapeDtypeStruct((count, dim), bf16),
        jax.ShapeDtypeStruct((count, dim), f32),
        jax.ShapeDtypeStruct(weights.shape, bf16),
        jax.ShapeDtypeStruct((2, dim), f32),
    )
    operands = (second, cot, norms, perm)
    return pl.pallas_call(
        feed_kernel,
        out_shape=out_shape,
        grid=(ffw // tile,),
        in_specs=[whole(op) for op in operands]
        + [
            pl.BlockSpec((dim, tile), lambda i: (0, first_up + i)),
            pl.BlockSpec((dim, tile), lambda i: (0, first_down + i)),
        ],
        out_specs=(
            whole_shape((count, dim)),
            whole_shape((count, dim)),
            pl.BlockSpec(memory_space=pl.ANY),
            whole_shape((2, dim)),
        ),
        scratch_shapes=[
            pltpu.VMEM((count, dim), bf16),
            pltpu.VMEM((dim, count), bf16),
            pltpu.VMEM((count, dim), bf16),
            pltpu.VMEM((dim, count), bf16),
            pltpu.VMEM((count, dim), f32),
            pltpu.VMEM((count, dim), f32),
            pltpu.VMEM((2, dim, tile), bf16),
            pltpu.VMEM((2, dim, tile), bf16),
            pltpu.SemaphoreType.DMA((2, 2)),
        ],
        compiler_params=params(),
        name="feed",
    )(*operands, weights, weights)


def cross_backward_kernel(
    spans,
    neighbours,
    lines,
    presence_ref,
    gsecond_ref,
    first_ref,
    norms_ref,
    perm_ref,
    perm_att_ref,
    att_p_ref,
    hid_p_ref,
    cross_q_ref,
    near_p_ref,
    near_kv_ref,
    co_p_ref,
    w_out_ref,
    w_cq_ref,
    w_co_ref,
    _,
    gfirst_ref,
    gatt_ref,
    all_ref,
    gnorm_ref,
    *rest,
):
    count, dim = first_ref.shape
    rows_near = near_p_ref.shape[0]
    span_len = count // spans
    near = rows_near // spans
    group = 256 // HEAD
    outs = []
    if lines:
        gatt_tok_ref, row_sems, send_sems = rest[5:]
        place = Place(lines)
        place.meet()
        send = Sender(place, send_sems)
    gco_ref, gcq_ref, gnear_ref, gw_ref, sems = rest[:5]

    def keep(index, value):
        slot = len(outs) % 3
        if len(outs) >= 3:
            outs[-3].wait()
        gw_ref[slot] = value.astype(bf16)
        outs.append(
            pltpu.make_async_copy(
                gw_ref.at[slot],
                all_ref.at[:, pl.ds((3 + index) * dim, dim)],
                sems.at[index],
            )
        )
        outs[-1].start()

    upper = gsecond_ref[...].astype(bf16)
    gco_ref[...] = nt(nt(upper, w_co_ref[...]).astype(bf16), perm_ref[...]).astype(bf16)

    def one_span(span):
        rows = rows_of(span, span_len)
        keys = rows_of(span, near)
        live, anyone = live_keys(presence_ref, span, (near, 1), 0, neighbours, near // neighbours)
        for begin in range(0, dim, group * HEAD):
            lanes = slice(begin, begin + group * HEAD)
            lanes_v = slice(dim + begin, dim + begin + group * HEAD)
            query = spread_heads(cross_q_ref[rows, lanes] * SCALE, span_len, group)
            grad_out = spread_heads(gco_ref[rows, lanes], span_len, group)
            key = near_kv_ref[keys, lanes]
            scores = jnp.where(live > 0, nt(key, query), masked_score)
            peak = jnp.max(scores, axis=0, keepdims=True)
            expon = jnp.exp(scores - peak) * live
            total = jnp.sum(expon, axis=0, keepdims=True) + 1.0 - anyone
            probs = expon * (1.0 / total)
            grad_probs = nt(near_kv_ref[keys, lanes_v], grad_out)
            inner = jnp.sum(probs * grad_probs, axis=0, keepdims=True)
            grad_scores = (probs * (grad_probs - inner)).astype(bf16)
            gcq_ref[rows, lanes] = (
                gather_heads(tn(grad_scores, key), span_len, group) * SCALE
            ).astype(bf16)
            gnear_ref[keys, lanes] = mm(grad_scores, query).astype(bf16)
            gnear_ref[keys, lanes_v] = mm(probs.astype(bf16), grad_out).astype(bf16)

    pl.loop(0, spans)(one_span)

    upstream = nt(nt(gcq_ref[...], w_cq_ref[...]).astype(bf16), perm_ref[...])
    normed, recip = centre_scale(first_ref[...])
    back, gain, shift = norm_back(upstream, normed, recip, norms_ref[2:3, :])
    gnorm_ref[0:1, :] = gain
    gnorm_ref[1:2, :] = shift
    gfirst_ref[...] = gsecond_ref[...] + back
    lower = gfirst_ref[...].astype(bf16)
    gatt = nt(nt(lower, w_out_ref[...]).astype(bf16), perm_att_ref[...]).astype(bf16)
    if lines:
        width = gatt_ref.shape[1]
        tokens = gatt_ref.shape[0] // 8
        shares = gatt.shape[1] // width
        gatt_tok_ref[...] = gatt

        def block(device):
            return gatt_tok_ref.at[
                pl.ds(pl.multiple_of(device // shares * tokens, tokens), tokens),
                pl.ds(pl.multiple_of(device % shares * width, width), width),
            ]

        def landing(device):
            return gatt_ref.at[pl.ds(pl.multiple_of(device * tokens, tokens), tokens)]

        for other in place.plane():
            send.start(None, block(other), landing(place.me), row_sems.at[place.me], seq=other)
        own = pltpu.make_async_copy(block(place.me), landing(place.me), row_sems.at[place.me])
        own.start()
    else:
        gatt_ref[...] = gatt
    keep(4, mm(co_p_ref[...].T, upper))
    near_t = near_p_ref[...].T
    for part in range(2):
        keep(2 + part, mm(near_t, gnear_ref[:, part * dim : (part + 1) * dim]))
    keep(1, mm(hid_p_ref[...].T, gcq_ref[...]))
    keep(0, mm(att_p_ref[...].T, lower))
    if lines:
        for other in place.plane():
            send.arrived(None, landing(other), row_sems.at[other])
        own.wait()
        send.finish()
    for copy in outs[-3:]:
        copy.wait()


def cross_backward(
    spans,
    neighbours,
    lines,
    presence,
    gsecond,
    first,
    norms,
    perm,
    perm_att,
    att_p,
    hid_p,
    cross_q,
    near_p,
    near_kv,
    co_p,
    weights,
    grads,
):
    count, dim = first.shape
    rows_near = near_p.shape[0]
    gatt_shape = (count, perm_att.shape[0])
    out_shape = [
        jax.ShapeDtypeStruct((count, dim), f32),
        jax.ShapeDtypeStruct(gatt_shape, bf16),
        jax.ShapeDtypeStruct(grads.shape, bf16),
        jax.ShapeDtypeStruct((2, dim), f32),
    ]
    scratch = [
        pltpu.VMEM((count, dim), bf16),
        pltpu.VMEM((count, dim), bf16),
        pltpu.VMEM((rows_near, 2 * dim), bf16),
        pltpu.VMEM((3, dim, dim), bf16),
        pltpu.SemaphoreType.DMA((5,)),
    ]
    compiler_params = params()
    if lines:
        out_shape[1] = jax.ShapeDtypeStruct((2 * count, gatt_shape[1] // 2), bf16)
        scratch += [
            pltpu.VMEM(gatt_shape, bf16),
            pltpu.SemaphoreType.DMA((8,)),
            pltpu.SemaphoreType.DMA((8,)),
        ]
        compiler_params = pltpu.CompilerParams(
            vmem_limit_bytes=VMEM_BYTES, collective_id=2, has_side_effects=True
        )
    operands = (
        gsecond,
        first,
        norms,
        perm,
        perm_att,
        att_p,
        hid_p,
        cross_q,
        near_p,
        near_kv,
        co_p,
    )
    return pl.pallas_call(
        partial(cross_backward_kernel, spans, neighbours, lines),
        out_shape=out_shape,
        grid=(1,),
        in_specs=[pl.BlockSpec(memory_space=pltpu.SMEM)]
        + [whole(op) for op in operands]
        + [column_block(dim, dim, index) for index in (3, 4, 7)]
        + [pl.BlockSpec(memory_space=pl.ANY)],
        out_specs=tuple(
            pl.BlockSpec(memory_space=pl.ANY) if index == 2 else whole_shape(shape.shape)
            for index, shape in enumerate(out_shape)
        ),
        scratch_shapes=scratch,
        input_output_aliases={len(operands) + 4: 2},
        compiler_params=compiler_params,
        name="cross_backward",
    )(presence, *operands, *([weights] * 3), grads)


def last_norm_kernel(parts_ref, x_ref, gfirst_ref, norms_ref, perm_ref, out_ref, gnorm_ref):
    total = parts_ref[0].astype(f32)
    for part in range(1, parts_ref.shape[0]):
        total = total + parts_ref[part].astype(f32)
    upstream = nt(total.astype(bf16), perm_ref[...])
    normed, recip = centre_scale(x_ref[...].astype(f32))
    back, gain, shift = norm_back(upstream, normed, recip, norms_ref[0:1, :])
    out_ref[...] = gfirst_ref[...] + back
    gnorm_ref[0:1, :] = gain
    gnorm_ref[1:2, :] = shift


def last_norm(parts, x, gfirst, norms, perm):
    count, dim = x.shape
    return pl.pallas_call(
        last_norm_kernel,
        out_shape=(
            jax.ShapeDtypeStruct((count, dim), f32),
            jax.ShapeDtypeStruct((2, dim), f32),
        ),
        compiler_params=params(),
        name="last_norm",
    )(parts, x, gfirst, norms, perm)


def forward_kernel(
    lines,
    pairs,
    spans,
    neighbours,
    presence_ref,
    w_ref,
    norm_ref,
    x_ref,
    perm_ref,
    cot_ref,
    near_ref,
    wts_ref,
    all_ref,
    hid_out,
    qkv_out,
    att_out,
    lse_out,
    att_p_out,
    first_out,
    hid_p_out,
    cross_q_out,
    near_p_out,
    near_kv_out,
    co_p_out,
    norms_ref,
    out_ref,
    gsecond_ref,
    gnorm_ref,
    *scratch,
):
    results, scratch = scratch[:11], scratch[11:]
    (
        hid_ref,
        qkv_ref,
        att_ref,
        lse_ref,
        att_p_ref,
        first_ref,
        hid_p_ref,
        cross_q_ref,
        near_p_ref,
        near_kv_ref,
        co_p_ref,
    ) = results
    work, scratch = scratch[:15], scratch[15:]
    (
        second_ref,
        own_ref,
        small_ref,
        rows_ref,
        w_qkv_ref,
        w_mid_ref,
        att_tok_ref,
        cross_ref,
        up_p_ref,
        up_t_ref,
        cot_p_ref,
        cot_t_ref,
        result_ref,
        back_ref,
        gfeed_ref,
    ) = work
    (
        send_sems,
        z_sems,
        y_sems,
        x_sems,
        sib_sems,
        norm_sems,
        row_sems,
        att_sems,
        local_sems,
        qkv_sems,
        mid_sems,
        feed_sems,
        out_sems,
    ) = scratch
    place = Place(lines)
    z, me, core = place.z, place.me, place.core
    length, dim = hid_ref.shape
    width = pairs * LANES
    tokens = length // 8
    cols = own_ref.shape[1] // 2
    slots = 2 * lines
    low, high = place.y == 0, place.y == 1
    near_load = pltpu.make_async_copy(near_ref, near_p_ref, local_sems.at[2])
    near_load.start()
    own_ref[...] = w_ref[...].astype(bf16)
    place.meet()
    send = Sender(place, send_sems)

    def unit(line, seq, half):
        rows = own_ref.shape[0]
        half = jnp.where(seq == 2, 1 - half, half)
        return wts_ref.at[
            pl.ds(pl.multiple_of(line * rows, rows), rows),
            pl.ds(pl.multiple_of((seq * 2 + half) * cols, cols), cols),
        ]

    events = place.events()
    keep = pltpu.make_async_copy(own_ref, unit_of(wts_ref, lines, z, me), local_sems.at[0])
    keep.start()

    def crossing(row, of=core):
        return row * 4 + (1 - place.x) * 2 + of

    def pieces(slot):
        far, half = slot % lines, slot // lines
        found = events[:1] if far == 0 else events[2 * far - 1 : 2 * far + 1]
        return [(*event, half) for event in found]

    def source(line, far, half):
        if far:
            return unit(line, me, half)
        half = jnp.where(me == 2, 1 - half, half)
        return own_ref.at[:, pl.ds(pl.multiple_of(half * cols, cols), cols)]

    def along_z(slot):
        for condition, line, far, side, half in pieces(slot):
            mine, src = unit(line, me, half), source(line, far, half)
            if far:
                send.arrived(condition, mine, z_sems.at[line, half])
            below, above = both(condition, z > 0), both(condition, z < lines - 1)
            if side >= 0:
                send.start(below, src, mine, z_sems.at[line, half], z=z - 1)
            if side <= 0:
                send.start(above, src, mine, z_sems.at[line, half], z=z + 1)

    def own_unit(slot):
        if slot % lines:
            along_z(slot)
        for condition, line, far, side, half in pieces(slot):
            mine, src = unit(line, me, half), source(line, far, half)
            send.start(condition, src, mine, y_sems.at[line, half], seq=place.yn)
            on = both(condition, low)
            send.start(on, src, mine, x_sems.at[0, line, half], seq=place.xn)
            send.start(on, src, mine, sib_sems.at[0, line, half], seq=place.sib)

    def from_y(slot):
        for condition, line, far, _, half in pieces(slot):
            theirs = unit(line, place.yn, half)
            send.arrived(condition, theirs, y_sems.at[line, half])
            on = both(condition, high)
            if far:
                send.start(on, theirs, theirs, x_sems.at[0, line, half], seq=place.xn)
            send.start(on, theirs, theirs, sib_sems.at[1, line, half], seq=place.sib)

    def from_x(slot):
        for condition, line, far, _, half in pieces(slot):
            theirs = unit(line, crossing(0), half)
            send.arrived(condition, theirs, x_sems.at[0, line, half])
            if far == 0:
                send.start(low, theirs, theirs, x_sems.at[0, line, half], seq=place.yn)
            send.start(condition, theirs, theirs, sib_sems.at[2, line, half], seq=place.sib)

    def late_row(slot):
        for condition, line, far, _, half in pieces(slot):
            on, src = both(condition, high), source(line, far, half)
            send.start(on, src, unit(line, me, half), x_sems.at[1, line, half], seq=place.xn)

    def late_start(slot):
        for condition, line, far, _, half in pieces(slot):
            mine, theirs = unit(line, me, half), unit(line, place.yn, half)
            src, sem = source(line, far, half), x_sems.at[1, line, half]
            above, below = both(condition, high), both(condition, low)
            if half == 0:
                send.start(below, theirs, theirs, sem, seq=place.xn)
            send.start(above, src, mine, sib_sems.at[0, line, half], seq=place.sib)
            send.start(below, theirs, theirs, sib_sems.at[1, line, half], seq=place.sib)

    def late_arrive(slot, row=None):
        for condition, line, _, _, half in pieces(slot):
            theirs = unit(line, crossing(1), half)
            on = condition if row is None else both(condition, row)
            send.arrived(on, theirs, x_sems.at[1, line, half])
            send.start(on, theirs, theirs, sib_sems.at[3, line, half], seq=place.sib)
            if half == 1 and row is high:
                send.start(on, theirs, theirs, x_sems.at[1, line, half], seq=place.yn)

    def from_sib(half, group, condition, seq):
        for line in range(lines):
            theirs = unit(line, seq, half)
            send.arrived(condition, theirs, sib_sems.at[group, line, half])

    def attention_half(half):
        from_sib(half, 0, low, place.sib)
        from_sib(half, 1, high, place.yn + 1 - 2 * core)
        from_sib(half, 2, None, crossing(0, 1 - core))

    def feed_half(half):
        from_sib(half, 0, high, place.sib)
        from_sib(half, 1, low, place.yn + 1 - 2 * core)
        from_sib(half, 3, None, crossing(1, 1 - core))

    kept = []

    def emit(index):
        out = (
            hid_out,
            qkv_out,
            att_out,
            lse_out,
            att_p_out,
            first_out,
            hid_p_out,
            cross_q_out,
            near_p_out,
            near_kv_out,
            co_p_out,
        )[index]
        kept.append(pltpu.make_async_copy(results[index], out, out_sems.at[index]))
        kept[-1].start()

    def row_block(seq):
        return rows_ref.at[pl.ds(pl.multiple_of(seq * tokens, tokens), tokens)]

    def middle(index):
        return pltpu.make_async_copy(
            wts_ref.at[:, pl.ds((3 + index) * dim, dim)], w_mid_ref.at[index], mid_sems.at[index]
        )

    def advance(slot):
        if slot < slots:
            own_unit(slot)
        if slot - 1 < slots:
            from_y(slot - 1)
        if slot == slots:
            for after in range(slots):
                if after % lines:
                    late_row(after)
        from_x(slot - 2)

    along_z(0)
    along_z(lines)
    own_unit(0)
    late_row(0)
    late_row(lines)
    own_rows = pltpu.make_async_copy(x_ref.at[place.chip], row_block(me), local_sems.at[1])
    own_rows.start()
    others = (place.xn, place.yn, place.dg)
    for other in place.line():
        send.start(None, norm_ref, small_ref.at[z], norm_sems.at[z], z=other)
    small_ref[z] = norm_ref[...]
    send.start(None, x_ref.at[place.chip], row_block(me), row_sems.at[me], seq=place.sib)
    for other in others:
        send.start(None, x_ref.at[other // 2], row_block(me), row_sems.at[me], seq=other)
    near_load.wait()

    @pl.loop(0, near_p_ref.shape[0] // 512)
    def _(step):
        rows = rows_of(step, 512)
        near_p_ref[rows, :] = mm(near_p_ref[rows, :], perm_ref[...]).astype(bf16)

    emit(8)
    own_unit(1)
    from_y(0)
    advance(2)
    cot_p_ref[...] = mm(cot_ref[...], perm_ref[...]).astype(bf16)
    cot_t_ref[...] = cot_p_ref[...].T
    advance(3)
    for other in others:
        send.arrived(None, row_block(other), row_sems.at[other])
        send.start(None, row_block(other), row_block(other), row_sems.at[other], seq=place.sib)

    for other in place.line():
        send.arrived(None, small_ref.at[other], norm_sems.at[other])
    piece = small_ref.shape[2]
    total = None
    for line in range(lines):
        row = lax.broadcasted_iota(jnp.int32, (piece, dim), 0)
        column = lax.broadcasted_iota(jnp.int32, (piece, dim), 1)
        part = dim // lines
        place_of = jnp.logical_and(row < part, column == row + line * part).astype(bf16)
        term = mm(small_ref[line], place_of)
        total = term if total is None else total + term
    norms_ref[...] = total[: norms_ref.shape[0]]

    advance(4)
    for other in others:
        theirs = other + 1 - 2 * core
        send.arrived(None, row_block(theirs), row_sems.at[theirs])
    send.arrived(None, row_block(place.sib), row_sems.at[place.sib])
    own_rows.wait()
    norm_rows(rows_ref, norms_ref[...], perm_ref, hid_ref)
    emit(0)
    advance(5)
    keep.wait()
    attention_half(0)
    middle(2).start()
    middle(3).start()
    middle(2).wait()
    middle(3).wait()
    near_steps = near_p_ref.shape[0] // 512
    for step in range(max(near_steps, slots - 4)):
        if step < near_steps:
            rows = slice(step * 512, (step + 1) * 512)
            near_kv_ref[rows, :dim] = mm(near_p_ref[rows, :], w_mid_ref[2]).astype(bf16)
            near_kv_ref[rows, dim:] = mm(near_p_ref[rows, :], w_mid_ref[3]).astype(bf16)
        if step + 6 < slots + 2:
            advance(step + 6)
    emit(9)
    for slot in range(slots):
        late_start(slot)
    attention_half(1)
    copies = weight_copies(pairs, dim, wts_ref, w_qkv_ref, qkv_sems)
    for copy in copies + [middle(index) for index in (0, 1, 4)]:
        copy.start()
    for part in range(3):
        copies[part].wait()
        triple_part(part, pairs, hid_ref, w_qkv_ref, qkv_ref)
    emit(1)

    share = lax.rem(me, dim // width)
    seq_rows = pl.ds(pl.multiple_of(place.chip * tokens, tokens), tokens)

    def landing(pair, chip_rows, share):
        lanes = pl.ds(pl.multiple_of(share * width + pair * LANES, LANES), LANES)
        return att_tok_ref.at[chip_rows, lanes]

    for pair in range(pairs):
        lanes = slice(pair * LANES, (pair + 1) * LANES)
        pair_forward(pair, pairs, qkv_ref, att_ref, lse_ref, lambda: None)
        for other in place.plane():
            block = att_ref.at[pl.ds(pl.multiple_of(other * tokens, tokens), tokens), lanes]
            to = landing(pair, seq_rows, share)
            send.start(None, block, to, att_sems.at[pair, me], seq=other)
        own_block = att_ref[pl.ds(pl.multiple_of(me * tokens, tokens), tokens), lanes]
        landing(pair, seq_rows, share)[...] = own_block
        late_arrive(pair)
        if pair == 0:
            late_arrive(lines, high)
    emit(2)
    emit(3)

    for index in (0, 1, 4):
        middle(index).wait()
    w_out_ref, w_cq_ref, w_co_ref = (w_mid_ref.at[index] for index in (0, 1, 4))
    for pair in range(pairs):
        for other in place.plane():
            rows = pl.ds(pl.multiple_of(other // 2 * tokens, tokens), tokens)
            send.arrived(None, landing(pair, rows, lax.rem(other, 2)), att_sems.at[pair, other])
    att_p_ref[...] = mm(att_tok_ref[...], perm_ref[...]).astype(bf16)
    emit(4)
    own_x = x_ref[...].reshape(first_ref.shape).astype(f32)
    first_ref[...] = own_x + mm(att_p_ref[...], w_out_ref[...])
    emit(5)
    normed, _ = centre_scale(first_ref[...])
    hidden = (normed * norms_ref[2:3, :] + norms_ref[3:4, :]).astype(bf16)
    hid_p_ref[...] = mm(hidden, perm_ref[...]).astype(bf16)
    emit(6)
    cross_q_ref[...] = mm(hid_p_ref[...], w_cq_ref[...]).astype(bf16)
    emit(7)
    for slot in range(pairs, lines):
        late_arrive(slot)

    def one_span(span):
        span_forward(span, spans, neighbours, presence_ref, cross_q_ref, near_kv_ref, cross_ref)

    late_arrive(lines + 1, high)
    pl.loop(0, spans // 2)(one_span)
    late_arrive(lines + 2, high)
    pl.loop(spans // 2, spans)(one_span)

    ffw = (all_ref.shape[1] - 8 * dim) // 2
    tile = cols
    order = [first + half * tile for half in range(2) for first in range(0, ffw, 2 * tile)]

    def tile_load(index):
        return [
            pltpu.make_async_copy(
                wts_ref.at[:, pl.ds(8 * dim + part * ffw + order[index], tile)],
                w_mid_ref.at[(2 * index + part) % 4],
                feed_sems.at[0, (2 * index + part) % 4],
            )
            for part in range(2)
        ]

    def tile_store(index):
        return [
            pltpu.make_async_copy(
                gfeed_ref.at[(2 * index + part) % 4],
                all_ref.at[:, pl.ds(8 * dim + part * ffw + order[index], tile)],
                feed_sems.at[1, (2 * index + part) % 4],
            )
            for part in range(2)
        ]

    feed_half(0)
    for copy in tile_load(0) + tile_load(1):
        copy.start()
    co_p_ref[...] = mm(cross_ref[...], perm_ref[...]).astype(bf16)
    emit(10)
    second_ref[...] = first_ref[...] + mm(co_p_ref[...], w_co_ref[...])
    normed, _ = centre_scale(second_ref[...])
    hidden = (normed * norms_ref[4:5, :] + norms_ref[5:6, :]).astype(bf16)
    up_p_ref[...] = mm(hidden, perm_ref[...]).astype(bf16)
    up_t_ref[...] = up_p_ref[...].T
    for slot in range(lines + 3, slots):
        late_arrive(slot, high)

    for index in range(len(order)):
        up_ref, down_ref = w_mid_ref.at[2 * index % 4], w_mid_ref.at[2 * index % 4 + 1]
        for copy in tile_load(index):
            copy.wait()
        if index >= 2:
            for copy in tile_store(index - 2):
                copy.wait()
        active, slope = gelu_parts(mm(up_p_ref[...], up_ref[...]))
        active = active.astype(bf16)
        term = nt(active, down_ref[...])
        result_ref[...] = term if index == 0 else result_ref[...] + term
        gfeed_ref[2 * index % 4 + 1] = mm(cot_t_ref[...], active).astype(bf16)
        grad_up = (mm(cot_p_ref[...], down_ref[...]) * slope).astype(bf16)
        gfeed_ref[2 * index % 4] = mm(up_t_ref[...], grad_up).astype(bf16)
        for copy in tile_store(index):
            copy.start()
        term = nt(grad_up, up_ref[...])
        back_ref[...] = term if index == 0 else back_ref[...] + term
        if index == 0:
            late_arrive(lines, low)
            late_arrive(lines + 1, low)
        if index == 1:
            for slot in range(lines + 2, slots):
                late_arrive(slot, low)
            feed_half(1)
            for copy in tile_load(2) + tile_load(3):
                copy.start()

    out_ref[...] = (second_ref[...] + nt(result_ref[...].astype(bf16), perm_ref[...])).astype(bf16)
    upstream = nt(back_ref[...].astype(bf16), perm_ref[...])
    normed, recip = centre_scale(second_ref[...])
    back, gain, shift = norm_back(upstream, normed, recip, norms_ref[4:5, :])
    gsecond_ref[...] = cot_ref[...].astype(f32) + back
    gnorm_ref[0:1, :] = gain
    gnorm_ref[1:2, :] = shift
    for index in (2, 3):
        for copy in tile_store(index):
            copy.wait()
    for copy in kept:
        copy.wait()
    send.finish()


def forward(lines, pairs, spans, neighbours, presence, w_shard, n_shard, inputs, perm, cot, near):
    unit_rows, unit_cols = w_shard.shape
    seqs, tokens, dim = inputs.shape
    count, length, width = seqs * tokens, 8 * tokens, pairs * LANES
    rows_near = near.shape[0]
    events = 2 * lines - 1
    any_space = pl.BlockSpec(memory_space=pl.ANY)
    vmem = pl.BlockSpec(memory_space=pltpu.VMEM)
    dma = pltpu.SemaphoreType.DMA
    packed = jax.ShapeDtypeStruct((unit_rows * lines, unit_cols * 8), bf16)
    kept = (
        ((length, dim), bf16),
        ((3 * pairs, length, LANES), bf16),
        ((length, width), bf16),
        ((pairs, 2, length), f32),
        ((count, dim), bf16),
        ((count, dim), f32),
        ((count, dim), bf16),
        ((count, dim), bf16),
        ((rows_near, dim), bf16),
        ((rows_near, 2 * dim), bf16),
        ((count, dim), bf16),
    )
    tile = unit_cols // 2
    return pl.pallas_call(
        partial(forward_kernel, lines, pairs, spans, neighbours),
        out_shape=(packed, packed)
        + tuple(jax.ShapeDtypeStruct(*entry) for entry in kept)
        + (
            jax.ShapeDtypeStruct((8, dim), f32),
            jax.ShapeDtypeStruct((count, dim), bf16),
            jax.ShapeDtypeStruct((count, dim), f32),
            jax.ShapeDtypeStruct((2, dim), f32),
        ),
        in_specs=[pl.BlockSpec(memory_space=pltpu.SMEM)] + [vmem] * 5 + [any_space],
        out_specs=(any_space,) * (2 + len(kept)) + (vmem,) * 4,
        scratch_shapes=[pltpu.VMEM(*entry) for entry in kept]
        + [
            pltpu.VMEM((count, dim), f32),
            pltpu.VMEM((unit_rows, unit_cols), bf16),
            pltpu.VMEM((lines,) + n_shard.shape, bf16),
            pltpu.VMEM((length, dim), bf16),
            pltpu.VMEM((dim, 3 * width), bf16),
            pltpu.VMEM((5, dim, dim), bf16),
            pltpu.VMEM((count, dim), bf16),
            pltpu.VMEM((count, dim), bf16),
            pltpu.VMEM((count, dim), bf16),
            pltpu.VMEM((dim, count), bf16),
            pltpu.VMEM((count, dim), bf16),
            pltpu.VMEM((dim, count), bf16),
            pltpu.VMEM((count, dim), f32),
            pltpu.VMEM((count, dim), f32),
            pltpu.VMEM((4, dim, tile), bf16),
            dma((28 * events + 7 + lines + 7 * pairs,)),
            dma((lines, 2)),
            dma((lines, 2)),
            dma((2, lines, 2)),
            dma((4, lines, 2)),
            dma((lines,)),
            dma((8,)),
            dma((pairs, 8)),
            dma((3,)),
            dma((3,)),
            dma((5,)),
            dma((2, 4)),
            dma((len(kept),)),
        ],
        compiler_params=pltpu.CompilerParams(
            vmem_limit_bytes=VMEM_BYTES, collective_id=1, has_side_effects=True
        ),
        name="forward",
    )(presence, w_shard, n_shard, inputs, perm, cot, near)


def reduce_kernel(
    lines,
    grads_ref,
    small_ref,
    shard_ref,
    norms_ref,
    mine_ref,
    sib_ref,
    corner_a_ref,
    corner_b_ref,
    from_x_ref,
    from_y_ref,
    below_ref,
    above_ref,
    plane_ref,
    plane_sum_ref,
    line_ref,
    send_sems,
    load_sems,
    sib_sems,
    a_sems,
    b_sems,
    x_sems,
    y_sems,
    below_sems,
    above_sems,
    plane_sems,
    line_sems,
):
    place = Place(lines)
    z, me = place.z, place.me
    unit_rows, unit_cols = shard_ref.shape
    half = unit_rows // 2
    tile = 32
    place.meet()
    send = Sender(place, send_sems)
    chips = (place.dg, place.yn, place.xn, me)
    corner, over_y, over_x, here = range(4)

    unit = partial(unit_of, grads_ref, lines)

    def load(which, line):
        return pltpu.make_async_copy(
            unit(line, chips[which]), mine_ref.at[which, line], load_sems.at[which, line]
        )

    for other in place.plane():
        send.start(None, small_ref, plane_ref.at[me], plane_sems.at[me], seq=other)
    plane_ref[me] = small_ref[...]

    events = place.events()[::-1]
    for condition, line, _, _ in events:
        for which in range(4):
            theirs = chips[which] + 1 - 2 * place.core
            send.start(
                condition,
                unit(line, theirs),
                sib_ref.at[which, line],
                sib_sems.at[which, line],
                seq=place.sib,
            )
            when(condition, load(which, line).start)

    def add(target, *terms, begin=0, size=unit_rows):
        @pl.loop(0, size // tile)
        def _(step):
            rows = pl.ds(pl.multiple_of(begin + step * tile, tile), tile)
            if len(terms) == 1:
                ref, first = terms[0]
                at = pl.ds(pl.multiple_of(begin - first + step * tile, tile), tile)
                target[rows, :] = target[rows, :] + ref[at, :]
            else:
                total = target[rows, :].astype(f32)
                for ref, first in terms:
                    at = pl.ds(pl.multiple_of(begin - first + step * tile, tile), tile)
                    total = total + ref[at, :].astype(f32)
                target[rows, :] = total.astype(target.dtype)

    def own(which, index):
        condition, line, _, _ = events[index]
        send.arrived(condition, sib_ref.at[which, line], sib_sems.at[which, line])
        when(condition, load(which, line).wait)

    def first(index):
        condition, line, _, _ = events[index]
        own(corner, index)
        target = mine_ref.at[corner, line]
        when(condition, lambda: add(target, (sib_ref.at[corner, line], 0)))
        send.start(
            condition,
            target.at[pl.ds(0, half)],
            corner_a_ref.at[line],
            a_sems.at[line],
            seq=place.xn,
        )
        send.start(
            condition,
            target.at[pl.ds(half, half)],
            corner_b_ref.at[line],
            b_sems.at[line],
            seq=place.yn,
        )

    def second(index):
        condition, line, _, _ = events[index]
        for which, part, sems, begin, to, landing, landing_sems in (
            (over_y, corner_a_ref, a_sems, 0, place.yn, from_y_ref, y_sems),
            (over_x, corner_b_ref, b_sems, half, place.xn, from_x_ref, x_sems),
        ):
            own(which, index)
            send.arrived(condition, part.at[line], sems.at[line])
            target = mine_ref.at[which, line]

            def body(which=which, part=part, begin=begin, target=target):
                add(
                    target,
                    (sib_ref.at[which, line], 0),
                    (part.at[line], begin),
                    begin=begin,
                    size=half,
                )
                add(target, (sib_ref.at[which, line], 0), begin=half - begin, size=half)

            when(condition, body)
            send.start(condition, target, landing.at[line], landing_sems.at[line], seq=to)

    def third(index):
        condition, line, far, side = events[index]
        own(here, index)
        send.arrived(condition, from_x_ref.at[line], x_sems.at[line])
        send.arrived(condition, from_y_ref.at[line], y_sems.at[line])
        target = mine_ref.at[here, line]
        terms = [(ref.at[line], 0) for ref in (sib_ref.at[here], from_x_ref, from_y_ref)]
        if side == 0:
            has_below, has_above = z > 0, z < lines - 1
            add(target, *terms)
            send.arrived(has_below, below_ref.at[line], below_sems.at[line])
            send.arrived(has_above, above_ref.at[line], above_sems.at[line])

            @pl.loop(0, unit_rows // tile)
            def _(step):
                rows = rows_of(step, tile)
                shard_ref[rows, :] = target[rows, :].astype(f32)

            when(has_below, lambda: add(shard_ref, (below_ref.at[line], 0)))
            when(has_above, lambda: add(shard_ref, (above_ref.at[line], 0)))
            return
        landing, sems = (below_ref, below_sems) if side > 0 else (above_ref, above_sems)
        more = both(condition, z > 0) if side > 0 else both(condition, z < lines - 1)
        none = both(condition, z == 0) if side > 0 else both(condition, z == lines - 1)
        send.arrived(more, landing.at[line], sems.at[line])
        when(more, lambda: add(target, *terms, (landing.at[line], 0)))
        when(none, lambda: add(target, *terms))
        send.start(condition, target, landing.at[line], sems.at[line], z=z + side)

    count = len(events)
    first(0)
    first(1)
    for index in range(2, count + 4):
        if index < count:
            first(index)
        if 0 <= index - 2 < count:
            second(index - 2)
        if index == 3:
            for other in place.plane():
                send.arrived(None, plane_ref.at[other], plane_sems.at[other])
            total = plane_ref[0]
            for other in range(1, 8):
                total = total + plane_ref[other]
            plane_sum_ref[...] = total
            line_ref[z] = total
            for other in place.line():
                send.start(None, plane_sum_ref, line_ref.at[z], line_sems.at[z], z=other)
        if 0 <= index - 4 < count:
            third(index - 4)

    for other in place.line():
        send.arrived(None, line_ref.at[other], line_sems.at[other])
    total = line_ref[0]
    for other in range(1, lines):
        total = total + line_ref[other]
    norms_ref[...] = total
    send.finish()


def reduce_grads(lines, grads, small):
    rows, cols = grads.shape
    unit_rows, unit_cols = rows // lines, cols // 8
    half = unit_rows // 2
    any_space = pl.BlockSpec(memory_space=pl.ANY)
    vmem = pl.BlockSpec(memory_space=pltpu.VMEM)
    dma = pltpu.SemaphoreType.DMA
    return pl.pallas_call(
        partial(reduce_kernel, lines),
        out_shape=(
            jax.ShapeDtypeStruct((unit_rows, unit_cols), f32),
            jax.ShapeDtypeStruct(small.shape, f32),
        ),
        in_specs=[any_space, vmem],
        out_specs=(vmem, vmem),
        scratch_shapes=[
            pltpu.VMEM((4, lines, unit_rows, unit_cols), bf16),
            pltpu.VMEM((4, lines, unit_rows, unit_cols), bf16),
            pltpu.VMEM((lines, half, unit_cols), bf16),
            pltpu.VMEM((lines, half, unit_cols), bf16),
            pltpu.VMEM((lines, unit_rows, unit_cols), bf16),
            pltpu.VMEM((lines, unit_rows, unit_cols), bf16),
            pltpu.VMEM((lines, unit_rows, unit_cols), bf16),
            pltpu.VMEM((lines, unit_rows, unit_cols), bf16),
            pltpu.VMEM((8,) + small.shape, f32),
            pltpu.VMEM(small.shape, f32),
            pltpu.VMEM((lines,) + small.shape, f32),
            dma((9 * (2 * lines - 1) + 7 + lines,)),
            dma((4, lines)),
            dma((4, lines)),
            dma((lines,)),
            dma((lines,)),
            dma((lines,)),
            dma((lines,)),
            dma((lines,)),
            dma((lines,)),
            dma((8,)),
            dma((lines,)),
        ],
        compiler_params=pltpu.CompilerParams(
            vmem_limit_bytes=VMEM_BYTES, collective_id=4, has_side_effects=True
        ),
        name="reduce_grads",
    )(grads, small)


def adam_update(grad, weight, first, second, average, rate, decay):
    first = beta_first * first + (1.0 - beta_first) * grad
    second = beta_second * second + (1.0 - beta_second) * grad * grad
    stepped = (
        first / (1.0 - beta_first**STEP) / (jnp.sqrt(second / (1.0 - beta_second**STEP)) + adam_eps)
    )
    weight = weight - rate * (stepped + decay * weight)
    average = ema_decay * average + (1.0 - ema_decay) * weight
    return (first, second, weight, average)


def on_device(
    inputs,
    cotangent,
    neighbours,
    presence,
    row_order,
    w_master,
    w_first,
    w_second,
    w_average,
    n_master,
    n_first,
    n_second,
    n_average,
):
    seqs, tokens, dim = inputs.shape
    heads = dim // HEAD
    devices = lax.axis_size("seq")
    count = seqs * tokens
    length = devices * tokens
    me = lax.axis_index("seq")
    shares = devices // seqs
    held = heads // shares
    pairs = (held + 1) // 2
    width = pairs * LANES
    spare = width - held * HEAD
    sequence, share = me // shares, me % shares

    lines = lax.axis_size("dp")
    planar = devices == 8 and seqs == 4 and spare == 0
    perm = (jnp.arange(dim)[:, None] == row_order[None, :]).astype(bf16)
    perm_att = perm
    if spare:
        perm_att = jnp.pad(perm.reshape(shares, held * HEAD, dim), ((0, 0), (0, spare), (0, 0)))
        perm_att = perm_att.reshape(shares * width, dim)
    x = inputs.reshape(count, dim)
    spans = seqs * neighbours.shape[1]
    each = neighbours.shape[2]
    near = neighbours.reshape(-1, dim)
    live = presence.reshape(-1)
    part = n_master.shape[1]
    if planar:
        small = jnp.pad(n_master.astype(bf16), ((0, 16 - 6), (0, -part % LANES)))
        (
            weights,
            grads,
            hid,
            qkv,
            att,
            lse,
            att_p,
            first,
            hid_p,
            cross_q,
            near_p,
            near_kv,
            co_p,
            norms,
            outputs,
            gsecond,
            gnorm_e,
        ) = forward(
            lines,
            pairs,
            spans,
            each,
            live,
            w_master,
            small,
            inputs,
            perm,
            cotangent.reshape(count, dim),
            near,
        )
    else:
        weights = lax.all_gather(w_master.astype(bf16), "dp", axis=0, tiled=True)
        weights = lax.all_gather(weights, "seq", axis=1, tiled=True)
        norms = lax.all_gather(n_master.astype(bf16), "dp", axis=1, tiled=True).astype(f32)
        rows = lax.all_to_all(jnp.repeat(inputs, shares, axis=0), "seq", 0, 0)
        rows = rows.reshape(length, dim)
        w_qkv = weights[:, : 3 * dim].reshape(dim, 3, shares, held * HEAD)
        w_qkv = lax.dynamic_index_in_dim(w_qkv, share, axis=2, keepdims=False)
        w_qkv = jnp.pad(w_qkv, ((0, 0), (0, 0), (0, spare))).reshape(dim, 3 * width)
        hid, qkv, att, lse = self_forward(pairs, rows, norms, perm, w_qkv)
        att_tok = (
            lax.all_to_all(att.reshape(devices, tokens, width), "seq", 0, 0)
            .reshape(seqs, shares, tokens, width)
            .transpose(0, 2, 1, 3)
            .reshape(count, shares * width)
        )
        att_p, first, hid_p, cross_q, near_p, near_kv, co_p, second = cross_forward(
            spans, each, live, att_tok, x, norms, perm, perm_att, near, weights
        )
        outputs, gsecond, grads, gnorm_e = feed(
            second, cotangent.reshape(count, dim), norms, perm, weights
        )
    gfirst, gatt_tok, grads, gnorm_c = cross_backward(
        spans,
        each,
        lines if planar else 0,
        live,
        gsecond,
        first,
        norms,
        perm,
        perm_att,
        att_p,
        hid_p,
        cross_q,
        near_p,
        near_kv,
        co_p,
        weights,
        grads,
    )
    if planar:
        others = jnp.concatenate(
            [jnp.zeros((2, dim), f32), gnorm_c, gnorm_e, jnp.zeros((2, dim), f32)], axis=0
        )
        grads, grad_inputs, norm_grads = finish(
            pairs,
            lines,
            qkv,
            att,
            gatt_tok,
            lse,
            hid,
            x,
            gfirst,
            norms,
            perm,
            others,
            weights,
            grads,
        )
        grad_shard, norm_sums = reduce_grads(lines, grads, norm_grads)
        norm_shard = lax.dynamic_slice(norm_sums, (0, lax.axis_index("dp") * part), (6, part))
    else:
        gatt = lax.all_to_all(
            gatt_tok.reshape(seqs, tokens, shares, width)
            .transpose(0, 2, 1, 3)
            .reshape(devices, tokens, width),
            "seq",
            0,
            0,
        ).reshape(length, width)
        gqkv, ghid = self_backward(pairs, qkv, att, gatt, lse, hid, w_qkv)
        parts = (
            lax.all_to_all(ghid.reshape(devices, tokens, dim), "seq", 0, 0)
            .reshape(seqs, shares, tokens, dim)
            .transpose(1, 0, 2, 3)
            .reshape(shares, count, dim)
        )
        grad_inputs, gnorm_a = last_norm(parts, x, gfirst, norms, perm)
        gqkv = gqkv.reshape(dim, 3, 1, width)[..., : held * HEAD]
        gqkv = jnp.where(jnp.arange(shares)[:, None] == share, gqkv, jnp.zeros_like(gqkv))
        grads = lax.dynamic_update_slice(grads, gqkv.reshape(dim, 3 * dim), (0, 0))
        norm_grads = lax.psum(jnp.concatenate([gnorm_a, gnorm_c, gnorm_e], axis=0), "seq")
        partial_sum = lax.psum_scatter(grads, "seq", scatter_dimension=1, tiled=True)
        grad_shard = lax.psum_scatter(partial_sum, "dp", scatter_dimension=0, tiled=True)
        grad_shard = grad_shard.astype(f32)
        norm_shard = lax.psum_scatter(
            norm_grads.astype(bf16), "dp", scatter_dimension=1, tiled=True
        ).astype(f32)
    w_first_new, w_second_new, w_new, w_average_new = adam_update(
        grad_shard, w_master, w_first, w_second, w_average, learn_rate, weight_decay
    )
    n_first_new, n_second_new, n_new, n_average_new = adam_update(
        norm_shard, n_master, n_first, n_second, n_average, norm_rate, 0.0
    )
    return (
        outputs.reshape(seqs, tokens, dim),
        grad_inputs.reshape(seqs, tokens, dim),
        w_first_new,
        w_second_new,
        w_new,
        w_average_new,
        n_first_new,
        n_second_new,
        n_new,
        n_average_new,
    )


def solution(mesh):
    in_specs = (
        P("dp", "seq", None),
        P("dp", "seq", None),
        P("dp", "seq", None, None, None),
        P("dp", "seq", None),
        P(),
        P("dp", "seq"),
        P("dp", "seq"),
        P("dp", "seq"),
        P("dp", "seq"),
        P(None, "dp"),
        P(None, "dp"),
        P(None, "dp"),
        P(None, "dp"),
    )
    out_specs = (
        P("dp", "seq", None),
        P("dp", "seq", None),
        P("dp", "seq"),
        P("dp", "seq"),
        P("dp", "seq"),
        P("dp", "seq"),
        P(None, "dp"),
        P(None, "dp"),
        P(None, "dp"),
        P(None, "dp"),
    )
    return jax.shard_map(
        on_device, mesh=mesh, in_specs=in_specs, out_specs=out_specs, check_vma=False
    )
```

```python
from functools import partial

import jax
import jax.numpy as jnp
from jax import lax
from jax.experimental import pallas as pl
from jax.experimental.pallas import tpu as pltpu
from jax.sharding import PartitionSpec as P

HEAD = 64
STEP = 5
LANES = 128
SCALE = HEAD ** (-0.5)

beta_first = 0.9
beta_second = 0.95
adam_eps = 1e-08
learn_rate = 0.04
norm_rate = 0.6
weight_decay = 0.1
ema_decay = 0.5
norm_eps = 1e-05
masked_score = -1e30
VMEM_BYTES = 60 * 1024 * 1024
bf16 = jnp.bfloat16
f32 = jnp.float32


def mm(left, right):
    return lax.dot_general(left, right, (((1,), (0,)), ((), ())), preferred_element_type=f32)


def nt(left, right):
    return lax.dot_general(left, right, (((1,), (1,)), ((), ())), preferred_element_type=f32)


def tn(left, right):
    return lax.dot_general(left, right, (((0,), (0,)), ((), ())), preferred_element_type=f32)


def params():
    return pltpu.CompilerParams(vmem_limit_bytes=VMEM_BYTES)


def rows_of(index, size):
    return pl.ds(pl.multiple_of(index * size, size), size)


def centre_scale(values):
    centre = jnp.mean(values, axis=-1, keepdims=True)
    centred = values - centre
    spread = jnp.mean(centred * centred, axis=-1, keepdims=True)
    recip = lax.rsqrt(spread + norm_eps)
    return centred * recip, recip


def norm_back(upstream, normed, recip, gain):
    scaled = upstream * gain
    inner = (
        scaled
        - jnp.mean(scaled, axis=-1, keepdims=True)
        - normed * jnp.mean(scaled * normed, axis=-1, keepdims=True)
    )
    return (
        recip * inner,
        jnp.sum(upstream * normed, axis=0, keepdims=True),
        jnp.sum(upstream, axis=0, keepdims=True),
    )


def gelu_parts(value):
    const = 0.7978845608028654
    square = value * value
    bend = jnp.tanh(const * value * (1.0 + 0.044715 * square))
    half = 0.5 * (1.0 + bend)
    slope = half + 0.5 * value * (1.0 - bend * bend) * (const * (1.0 + 3 * 0.044715 * square))
    return value * half, slope


def head_mask(rows, half):
    lane = lax.broadcasted_iota(jnp.int32, (rows, LANES), 1)
    return (lane < HEAD) if half == 0 else (lane >= HEAD)


def pick(mask, value):
    return jnp.where(mask, value, jnp.zeros_like(value))


MESH = pl.DeviceIdType.MESH


class Place:
    def __init__(self, lines):
        self.lines = lines
        self.z = lax.axis_index("dp")
        self.me = lax.axis_index("seq")
        core, x, y = self.me % 2, (self.me // 2) % 2, self.me // 4
        self.core, self.x, self.y, self.chip = core, x, y, self.me // 2
        self.sib = self.me + 1 - 2 * core
        self.xn = self.me + 2 - 4 * x
        self.yn = self.me + 4 - 8 * y
        self.dg = self.xn + 4 - 8 * y

    def events(self):
        found = [(None, self.z, 0, 0)]
        for far in range(1, self.lines):
            found.append((self.z >= far, self.z - far, far, -1))
            found.append((self.z + far < self.lines, self.z + far, far, 1))
        return found

    def plane(self):
        return [lax.rem(self.me + step, 8) for step in range(1, 8)]

    def line(self):
        return [lax.rem(self.z + step, self.lines) for step in range(1, self.lines)]

    def meet(self):
        barrier = pltpu.get_barrier_semaphore()
        for other in self.plane():
            pl.semaphore_signal(
                barrier, inc=1, device_id={"dp": self.z, "seq": other}, device_id_type=MESH
            )
        for other in self.line():
            pl.semaphore_signal(
                barrier, inc=1, device_id={"dp": other, "seq": self.me}, device_id_type=MESH
            )
        pl.semaphore_wait(barrier, 7 + self.lines - 1)


def when(condition, body):
    if condition is None:
        body()
    else:
        pl.when(condition)(body)


def both(first, second):
    if first is None or second is None:
        return second if first is None else first
    return jnp.logical_and(first, second)


class Sender:
    def __init__(self, place, send_sems):
        self.place, self.sems, self.open = place, send_sems, []

    def start(self, condition, src, dst, recv_sem, z=None, seq=None):
        place = self.place
        target = {"dp": place.z if z is None else z, "seq": place.me if seq is None else seq}
        copy = pltpu.make_async_remote_copy(
            src_ref=src,
            dst_ref=dst,
            send_sem=self.sems.at[len(self.open)],
            recv_sem=recv_sem,
            device_id=target,
            device_id_type=MESH,
        )
        self.open.append((condition, copy))
        when(condition, copy.start)

    def arrived(self, condition, ref, recv_sem):
        copy = pltpu.make_async_remote_copy(
            src_ref=ref,
            dst_ref=ref,
            send_sem=self.sems.at[0],
            recv_sem=recv_sem,
            device_id={"dp": self.place.z, "seq": self.place.sib},
            device_id_type=MESH,
        )
        when(condition, copy.wait_recv)

    def finish(self):
        for condition, copy in self.open:
            when(condition, copy.wait_send)


class Weave:
    def __init__(self, steps):
        self.steps = list(steps)

    def some(self, count):
        for _ in range(min(count, len(self.steps))):
            self.steps.pop(0)()

    def rest(self):
        self.some(len(self.steps))


def unit_of(ref, lines, line, seq, begin=0, size=None):
    rows, cols = ref.shape[0] // lines, ref.shape[1] // 8
    size = rows if size is None else size
    return ref.at[
        pl.ds(pl.multiple_of(line * rows + begin, 16), size),
        pl.ds(pl.multiple_of(seq * cols, cols), cols),
    ]


def weight_copies(pairs, dim, wts_ref, w_ref, sems):
    width = pairs * LANES
    first = lax.rem(lax.axis_index("seq"), dim // width) * width
    return [
        pltpu.make_async_copy(
            wts_ref.at[:, pl.ds(pl.multiple_of(first + part * dim, LANES), width)],
            w_ref.at[:, pl.ds(part * width, width)],
            sems.at[part],
        )
        for part in range(3)
    ]


def pair_forward(pair, pairs, qkv_ref, att_ref, lse_ref, between):
    length = att_ref.shape[0]
    tile = 256
    below = lax.broadcasted_iota(jnp.int32, (tile, tile), 1) <= lax.broadcasted_iota(
        jnp.int32, (tile, tile), 0
    )
    masks = [head_mask(tile, 0), head_mask(tile, 1)]
    lane = lax.broadcasted_iota(jnp.int32, (tile, LANES), 1)
    for step in range(length // tile):
        rows = slice(step * tile, (step + 1) * tile)
        query = qkv_ref[pair, rows, :] * SCALE
        keys_here = qkv_ref[pairs + pair, rows, :]
        values_here = qkv_ref[2 * pairs + pair, rows, :]
        outs, logs = [], []
        for half in range(2):
            mine = pick(masks[half], query)
            here = jnp.where(below, nt(mine, keys_here), masked_score)
            peak = jnp.max(here, axis=-1, keepdims=True)
            if step:
                past = nt(mine, qkv_ref[pairs + pair, : step * tile, :])
                peak = jnp.maximum(peak, jnp.max(past, axis=-1, keepdims=True))
                past = jnp.exp(past - peak)
            here = jnp.exp(here - peak)
            total = jnp.sum(here, axis=-1, keepdims=True)
            out = mm(here.astype(bf16), values_here)
            if step:
                total = total + jnp.sum(past, axis=-1, keepdims=True)
                out = out + mm(past.astype(bf16), qkv_ref[2 * pairs + pair, : step * tile, :])
            outs.append(out / total)
            logs.append(peak + jnp.log(total))
        lse_ref[pair, :, rows] = jnp.where(lane == 0, logs[0], logs[1]).T[0:2, :]
        att_ref[rows, pl.ds(pl.multiple_of(pair * LANES, LANES), LANES)] = jnp.where(
            masks[0], outs[0], outs[1]
        ).astype(bf16)
        between()


def norm_rows(x_ref, norms, perm_ref, hid_ref):
    tile = 256

    @pl.loop(0, x_ref.shape[0] // tile)
    def _(step):
        rows = rows_of(step, tile)
        normed, _ = centre_scale(x_ref[rows, :].astype(f32))
        hidden = (normed * norms[0:1, :] + norms[1:2, :]).astype(bf16)
        hid_ref[rows, :] = mm(hidden, perm_ref[...]).astype(bf16)


def triple_part(part, pairs, hid_ref, w_ref, qkv_ref):
    width = pairs * LANES
    triple = mm(hid_ref[...], w_ref[:, part * width : (part + 1) * width]).astype(bf16)
    for pair in range(pairs):
        qkv_ref[part * pairs + pair] = triple[:, pair * LANES : (pair + 1) * LANES]


def self_forward_kernel(
    pairs, x_ref, norms_ref, perm_ref, w_ref, hid_ref, qkv_ref, att_ref, lse_ref
):
    norm_rows(x_ref, norms_ref, perm_ref, hid_ref)
    for part in range(3):
        triple_part(part, pairs, hid_ref, w_ref, qkv_ref)

    @pl.loop(0, pairs)
    def _(pair):
        pair_forward(pair, pairs, qkv_ref, att_ref, lse_ref, lambda: None)


def self_forward(pairs, x, norms, perm, w):
    length, dim = x.shape
    return pl.pallas_call(
        partial(self_forward_kernel, pairs),
        out_shape=(
            jax.ShapeDtypeStruct((length, dim), bf16),
            jax.ShapeDtypeStruct((3 * pairs, length, LANES), bf16),
            jax.ShapeDtypeStruct((length, pairs * LANES), bf16),
            jax.ShapeDtypeStruct((pairs, 2, length), f32),
        ),
        compiler_params=params(),
        name="self_forward",
    )(x, norms, perm, w)


def pair_backward(pair, pairs, qkv_ref, att_ref, gatt_ref, lse_ref, grad_ref, acc_ref, between):
    length = att_ref.shape[0]
    width = pairs * LANES
    tile = 256
    above = lax.broadcasted_iota(jnp.int32, (tile, tile), 0) <= lax.broadcasted_iota(
        jnp.int32, (tile, tile), 1
    )
    masks = [head_mask(tile, 0), head_mask(tile, 1)]
    lanes = pl.ds(pl.multiple_of(pair * LANES, LANES), LANES)
    for step in range(length // tile):
        rows = slice(step * tile, (step + 1) * tile)
        query = qkv_ref[pair, rows, :] * SCALE
        grad_out = gatt_ref[rows, lanes]
        product = grad_out.astype(f32) * att_ref[rows, lanes].astype(f32)
        queries = [pick(masks[half], query) for half in range(2)]
        grads = [pick(masks[half], grad_out) for half in range(2)]
        deltas = [jnp.sum(pick(masks[half], product).T, axis=0, keepdims=True) for half in range(2)]
        grad_query = [None, None]
        for other in range(step + 1):
            cols = slice(other * tile, (other + 1) * tile)
            keys = qkv_ref[pairs + pair, cols, :]
            values = qkv_ref[2 * pairs + pair, cols, :]
            key_part = value_part = None
            for half in range(2):
                scores = nt(keys, queries[half])
                if other == step:
                    scores = jnp.where(above, scores, masked_score)
                probs = jnp.exp(scores - lse_ref[pair, half : half + 1, rows])
                grad_scores = (probs * (nt(values, grads[half]) - deltas[half])).astype(bf16)
                query_term = tn(grad_scores, keys)
                grad_query[half] = (
                    query_term if grad_query[half] is None else grad_query[half] + query_term
                )
                key_term = mm(grad_scores, queries[half])
                value_term = mm(probs.astype(bf16), grads[half])
                key_part = key_term if key_part is None else key_part + key_term
                value_part = value_term if value_part is None else value_part + value_term
            if other == step:
                acc_ref[0, cols, :] = key_part
                acc_ref[1, cols, :] = value_part
            else:
                acc_ref[0, cols, :] += key_part
                acc_ref[1, cols, :] += value_part
        grad_ref[rows, lanes] = (jnp.where(masks[0], grad_query[0], grad_query[1]) * SCALE).astype(
            bf16
        )
        between()
    for part in range(2):
        lanes_to = pl.ds(pl.multiple_of((part + 1) * width + pair * LANES, LANES), LANES)
        grad_ref[:, lanes_to] = acc_ref[part].astype(bf16)


def self_backward_kernel(
    pairs,
    qkv_ref,
    att_ref,
    gatt_ref,
    lse_ref,
    hid_ref,
    w_ref,
    gw_ref,
    ghid_ref,
    grad_ref,
    acc_ref,
):
    length = att_ref.shape[0]
    width = pairs * LANES
    attention = (qkv_ref, att_ref, gatt_ref, lse_ref, grad_ref, acc_ref)

    @pl.loop(0, pairs)
    def _(pair):
        pair_backward(pair, pairs, *attention, lambda: None)

    hidden_t = hid_ref[...].T
    for part in range(3):
        cols = slice(part * width, (part + 1) * width)
        gw_ref[:, cols] = mm(hidden_t, grad_ref[:, cols]).astype(bf16)
    for begin in range(0, length, 256):
        rows = slice(begin, begin + 256)
        ghid_ref[rows, :] = nt(grad_ref[rows, :], w_ref[...]).astype(bf16)


def self_backward(pairs, qkv, att, gatt, lse, hid, w):
    length, dim = hid.shape
    width = pairs * LANES
    return pl.pallas_call(
        partial(self_backward_kernel, pairs),
        out_shape=(
            jax.ShapeDtypeStruct((dim, 3 * width), bf16),
            jax.ShapeDtypeStruct((length, dim), bf16),
        ),
        scratch_shapes=[
            pltpu.VMEM((length, 3 * width), bf16),
            pltpu.VMEM((2, length, LANES), f32),
        ],
        compiler_params=params(),
        name="self_backward",
    )(qkv, att, gatt, lse, hid, w)


def finish_kernel(
    pairs,
    lines,
    qkv_ref,
    att_ref,
    gatt_ref,
    lse_ref,
    hid_ref,
    x_ref,
    gfirst_ref,
    norms_ref,
    perm_ref,
    others_ref,
    wts_ref,
    _,
    all_ref,
    gin_ref,
    small_ref,
    grad_ref,
    acc_ref,
    gw_ref,
    w_ref,
    sems,
    ghid_ref,
    gsib_ref,
    parts_ref,
    gsib_sems,
    part_sems,
    send_sems,
):
    length, dim = hid_ref.shape
    width = pairs * LANES
    tokens = length // 8
    place = Place(lines)
    me, core = place.me, place.core
    place.meet()
    send = Sender(place, send_sems)
    copies = weight_copies(pairs, dim, wts_ref, w_ref, sems)
    for copy in copies:
        copy.start()

    share_count = dim // width
    share = lax.rem(me, share_count)
    gw_ref[3] = jnp.zeros_like(gw_ref[3])
    outs = []
    for part in range(3):
        for other in range(1, share_count):
            first = part * dim + lax.rem(share + other, share_count) * width
            outs.append(
                pltpu.make_async_copy(
                    gw_ref.at[3],
                    all_ref.at[:, pl.ds(pl.multiple_of(first, LANES), width)],
                    sems.at[6 + part * (share_count - 1) + other - 1],
                )
            )
            outs[-1].start()

    attention = (qkv_ref, att_ref, gatt_ref, lse_ref, grad_ref, acc_ref)

    @pl.loop(0, pairs)
    def _(pair):
        pair_backward(pair, pairs, *attention, lambda: None)

    def token_rows(device):
        return pl.ds(pl.multiple_of(device * tokens, tokens), tokens)

    for copy in copies:
        copy.wait()
    for begin in range(0, length, 256):
        rows = slice(begin, begin + 256)
        ghid_ref[rows, :] = nt(grad_ref[rows, :], w_ref[...]).astype(bf16)
    chips = (place.xn // 2, place.yn // 2, place.dg // 2, place.chip)
    for chip in chips:
        theirs = chip * 2 + 1 - core
        send.start(
            None, ghid_ref.at[token_rows(theirs)], gsib_ref.at[chip], gsib_sems.at[chip], seq=place.sib
        )
    for chip in chips:
        send.arrived(None, gsib_ref.at[chip], gsib_sems.at[chip])
        rows = token_rows(chip * 2 + core)
        total = (ghid_ref[rows, :].astype(f32) + gsib_ref[chip].astype(f32)).astype(bf16)
        if chip is place.chip:
            parts_ref[chip] = total
        else:
            ghid_ref[rows, :] = total
            send.start(
                None,
                ghid_ref.at[rows],
                parts_ref.at[place.chip],
                part_sems.at[place.chip],
                seq=chip * 2 + core,
            )

    hidden_t = hid_ref[...].T
    for part in range(3):
        gw_ref[part] = mm(hidden_t, grad_ref[:, part * width : (part + 1) * width]).astype(bf16)
        first = part * dim + share * width
        outs.append(
            pltpu.make_async_copy(
                gw_ref.at[part],
                all_ref.at[:, pl.ds(pl.multiple_of(first, LANES), width)],
                sems.at[3 + part],
            )
        )
        outs[-1].start()

    for chip in chips[:3]:
        send.arrived(None, parts_ref.at[chip], part_sems.at[chip])
    gain_sum = shift_sum = None
    for chip in range(4):
        rows = slice(chip * tokens, (chip + 1) * tokens)
        upstream = nt(parts_ref[chip], perm_ref[...])
        normed, recip = centre_scale(x_ref[rows, :].astype(f32))
        back, gain, shift = norm_back(upstream, normed, recip, norms_ref[0:1, :])
        gin_ref[rows, :] = gfirst_ref[rows, :] + back
        gain_sum = gain if gain_sum is None else gain_sum + gain
        shift_sum = shift if shift_sum is None else shift_sum + shift
    small_ref[...] = others_ref[...]
    small_ref[0:1, :] = gain_sum
    small_ref[1:2, :] = shift_sum
    for copy in outs:
        copy.wait()
    send.finish()


def finish(pairs, lines, qkv, att, gatt, lse, hid, x, gfirst, norms, perm, others, weights, grads):
    length, dim = hid.shape
    width = pairs * LANES
    count = x.shape[0]
    tokens = length // 8
    any_space = pl.BlockSpec(memory_space=pl.ANY)
    vmem = pl.BlockSpec(memory_space=pltpu.VMEM)
    dma = pltpu.SemaphoreType.DMA
    return pl.pallas_call(
        partial(finish_kernel, pairs, lines),
        out_shape=(
            jax.ShapeDtypeStruct(grads.shape, bf16),
            jax.ShapeDtypeStruct((count, dim), f32),
            jax.ShapeDtypeStruct((8, dim), f32),
        ),
        in_specs=[vmem] * 10 + [any_space] * 2,
        out_specs=(any_space, vmem, vmem),
        scratch_shapes=[
            pltpu.VMEM((length, 3 * width), bf16),
            pltpu.VMEM((2, length, LANES), f32),
            pltpu.VMEM((4, dim, width), bf16),
            pltpu.VMEM((dim, 3 * width), bf16),
            dma((6 + 3 * (dim // width),)),
            pltpu.VMEM((length, dim), bf16),
            pltpu.VMEM((4, tokens, dim), bf16),
            pltpu.VMEM((4, tokens, dim), bf16),
            dma((4,)),
            dma((4,)),
            dma((8,)),
        ],
        input_output_aliases={11: 0},
        compiler_params=pltpu.CompilerParams(
            vmem_limit_bytes=VMEM_BYTES, collective_id=3, has_side_effects=True
        ),
        name="finish",
    )(qkv, att, gatt, lse, hid, x, gfirst, norms, perm, others, weights, grads)


def spread_heads(block, rows, group):
    lane = lax.broadcasted_iota(jnp.int32, block.shape, 1) // HEAD
    return jnp.concatenate([pick(lane == head, block) for head in range(group)], axis=0)


def gather_heads(stacked, rows, group):
    lane = lax.broadcasted_iota(jnp.int32, (rows, stacked.shape[1]), 1) // HEAD
    out = None
    for head in range(group):
        part = pick(lane == head, stacked[head * rows : (head + 1) * rows])
        out = part if out is None else out + part
    return out


def live_keys(presence_ref, span, shape, axis, neighbours, each):
    index = lax.broadcasted_iota(jnp.int32, shape, axis) // each
    live = jnp.zeros(shape, f32)
    anyone = None
    for which in range(neighbours):
        here = presence_ref[span * neighbours + which]
        there = jnp.where(here > 0, 1.0, 0.0).astype(f32)
        live = jnp.where(index == which, there, live)
        anyone = here if anyone is None else jnp.maximum(anyone, here)
    return live, anyone.astype(f32)


def span_forward(span, spans, neighbours, presence_ref, cross_q_ref, near_kv_ref, cross_ref):
    count, dim = cross_q_ref.shape
    span_len = count // spans
    near = near_kv_ref.shape[0] // spans
    group = 256 // HEAD
    rows = rows_of(span, span_len)
    keys = rows_of(span, near)
    live, anyone = live_keys(presence_ref, span, (1, near), 1, neighbours, near // neighbours)
    for begin in range(0, dim, group * HEAD):
        lanes = slice(begin, begin + group * HEAD)
        lanes_v = slice(dim + begin, dim + begin + group * HEAD)
        query = spread_heads(cross_q_ref[rows, lanes] * SCALE, span_len, group)
        scores = jnp.where(live > 0, nt(query, near_kv_ref[keys, lanes]), masked_score)
        peak = jnp.max(scores, axis=-1, keepdims=True)
        expon = jnp.exp(scores - peak) * live
        total = jnp.sum(expon, axis=-1, keepdims=True) + 1.0 - anyone
        out = mm(expon.astype(bf16), near_kv_ref[keys, lanes_v]) / total
        cross_ref[rows, lanes] = gather_heads(out, span_len, group).astype(bf16)


def cross_forward_kernel(
    spans,
    neighbours,
    presence_ref,
    att_ref,
    x_ref,
    norms_ref,
    perm_ref,
    perm_att_ref,
    near_ref,
    w_out_ref,
    w_cq_ref,
    w_ck_ref,
    w_cv_ref,
    w_co_ref,
    att_p_ref,
    first_ref,
    hid_p_ref,
    cross_q_ref,
    near_p_ref,
    near_kv_ref,
    co_p_ref,
    second_ref,
    cross_ref,
):
    count, dim = x_ref.shape
    rows_near = near_ref.shape[0]
    tile = 512

    att_p_ref[...] = mm(att_ref[...], perm_att_ref[...]).astype(bf16)
    first_ref[...] = x_ref[...].astype(f32) + mm(att_p_ref[...], w_out_ref[...])

    normed, _ = centre_scale(first_ref[...])
    hidden = (normed * norms_ref[2:3, :] + norms_ref[3:4, :]).astype(bf16)
    hid_p_ref[...] = mm(hidden, perm_ref[...]).astype(bf16)
    cross_q_ref[...] = mm(hid_p_ref[...], w_cq_ref[...]).astype(bf16)

    @pl.loop(0, rows_near // tile)
    def _(step):
        rows = rows_of(step, tile)
        near_p_ref[rows, :] = mm(near_ref[rows, :], perm_ref[...]).astype(bf16)
        near_kv_ref[rows, :dim] = mm(near_p_ref[rows, :], w_ck_ref[...]).astype(bf16)
        near_kv_ref[rows, dim:] = mm(near_p_ref[rows, :], w_cv_ref[...]).astype(bf16)

    @pl.loop(0, spans)
    def _(span):
        span_forward(span, spans, neighbours, presence_ref, cross_q_ref, near_kv_ref, cross_ref)

    co_p_ref[...] = mm(cross_ref[...], perm_ref[...]).astype(bf16)
    second_ref[...] = first_ref[...] + mm(co_p_ref[...], w_co_ref[...])


def column_block(rows, width, index):
    return pl.BlockSpec((rows, width), lambda *_: (0, index), pipeline_mode=pl.Buffered(1))


def whole(array):
    return pl.BlockSpec(array.shape, lambda *_: (0,) * array.ndim, pipeline_mode=pl.Buffered(1))


def whole_shape(shape):
    return pl.BlockSpec(shape, lambda *_: (0,) * len(shape), pipeline_mode=pl.Buffered(1))


def cross_forward(spans, neighbours, presence, att, x, norms, perm, perm_att, near, weights):
    count, dim = x.shape
    rows_near = near.shape[0]
    out_shape = (
        jax.ShapeDtypeStruct((count, dim), bf16),
        jax.ShapeDtypeStruct((count, dim), f32),
        jax.ShapeDtypeStruct((count, dim), bf16),
        jax.ShapeDtypeStruct((count, dim), bf16),
        jax.ShapeDtypeStruct((rows_near, dim), bf16),
        jax.ShapeDtypeStruct((rows_near, 2 * dim), bf16),
        jax.ShapeDtypeStruct((count, dim), bf16),
        jax.ShapeDtypeStruct((count, dim), f32),
    )
    operands = (att, x, norms, perm, perm_att, near)
    return pl.pallas_call(
        partial(cross_forward_kernel, spans, neighbours),
        out_shape=out_shape,
        grid=(1,),
        in_specs=[pl.BlockSpec(memory_space=pltpu.SMEM)]
        + [whole(op) for op in operands]
        + [column_block(dim, dim, index) for index in (3, 4, 5, 6, 7)],
        out_specs=tuple(whole_shape(shape.shape) for shape in out_shape),
        scratch_shapes=[pltpu.VMEM((count, dim), bf16)],
        compiler_params=params(),
        name="cross_forward",
    )(presence, *operands, *([weights] * 5))


def feed_kernel(
    second_ref,
    cot_ref,
    norms_ref,
    perm_ref,
    w_up_ref,
    w_down_ref,
    out_ref,
    gsecond_ref,
    all_ref,
    gnorm_ref,
    hid_p_ref,
    hid_t_ref,
    cot_p_ref,
    cot_t_ref,
    result_ref,
    back_ref,
    gup_ref,
    gdown_ref,
    sems,
):
    step = pl.program_id(0)
    last = pl.num_programs(0) - 1
    slot = lax.rem(step, 2)
    dim, tile = w_up_ref.shape

    def copies(step, slot):
        up = pl.multiple_of(8 * dim + step * tile, tile)
        down = pl.multiple_of(8 * dim + (last + 1 + step) * tile, tile)
        return (
            pltpu.make_async_copy(gup_ref.at[slot], all_ref.at[:, pl.ds(up, tile)], sems.at[0, slot]),
            pltpu.make_async_copy(
                gdown_ref.at[slot], all_ref.at[:, pl.ds(down, tile)], sems.at[1, slot]
            ),
        )

    @pl.when(step >= 2)
    def _():
        for copy in copies(step - 2, slot):
            copy.wait()

    @pl.when(step == 0)
    def _():
        normed, _ = centre_scale(second_ref[...])
        hidden = (normed * norms_ref[4:5, :] + norms_ref[5:6, :]).astype(bf16)
        hid_p_ref[...] = mm(hidden, perm_ref[...]).astype(bf16)
        hid_t_ref[...] = hid_p_ref[...].T
        cot_p_ref[...] = mm(cot_ref[...], perm_ref[...]).astype(bf16)
        cot_t_ref[...] = cot_p_ref[...].T
        result_ref[...] = jnp.zeros_like(result_ref)
        back_ref[...] = jnp.zeros_like(back_ref)

    upward = mm(hid_p_ref[...], w_up_ref[...])
    active, slope = gelu_parts(upward)
    active = active.astype(bf16)
    result_ref[...] += nt(active, w_down_ref[...])
    gdown_ref[slot] = mm(cot_t_ref[...], active).astype(bf16)
    grad_up = (mm(cot_p_ref[...], w_down_ref[...]) * slope).astype(bf16)
    gup_ref[slot] = mm(hid_t_ref[...], grad_up).astype(bf16)
    for copy in copies(step, slot):
        copy.start()
    back_ref[...] += nt(grad_up, w_up_ref[...])

    @pl.when(step == last)
    def _():
        out_ref[...] = (
            second_ref[...] + nt(result_ref[...].astype(bf16), perm_ref[...])
        ).astype(bf16)
        upstream = nt(back_ref[...].astype(bf16), perm_ref[...])
        normed, recip = centre_scale(second_ref[...])
        back, gain, shift = norm_back(upstream, normed, recip, norms_ref[4:5, :])
        gsecond_ref[...] = cot_ref[...].astype(f32) + back
        gnorm_ref[0:1, :] = gain
        gnorm_ref[1:2, :] = shift
        for which in (step - 1, step):
            for copy in copies(which, lax.rem(which, 2)):
                copy.wait()


def feed(second, cot, norms, perm, weights):
    count, dim = second.shape
    ffw = (weights.shape[1] - 8 * dim) // 2
    tile = 512
    first_up = 8 * dim // tile
    first_down = (8 * dim + ffw) // tile
    out_shape = (
        jax.ShapeDtypeStruct((count, dim), bf16),
        jax.ShapeDtypeStruct((count, dim), f32),
        jax.ShapeDtypeStruct(weights.shape, bf16),
        jax.ShapeDtypeStruct((2, dim), f32),
    )
    operands = (second, cot, norms, perm)
    return pl.pallas_call(
        feed_kernel,
        out_shape=out_shape,
        grid=(ffw // tile,),
        in_specs=[whole(op) for op in operands]
        + [
            pl.BlockSpec((dim, tile), lambda i: (0, first_up + i)),
            pl.BlockSpec((dim, tile), lambda i: (0, first_down + i)),
        ],
        out_specs=(
            whole_shape((count, dim)),
            whole_shape((count, dim)),
            pl.BlockSpec(memory_space=pl.ANY),
            whole_shape((2, dim)),
        ),
        scratch_shapes=[
            pltpu.VMEM((count, dim), bf16),
            pltpu.VMEM((dim, count), bf16),
            pltpu.VMEM((count, dim), bf16),
            pltpu.VMEM((dim, count), bf16),
            pltpu.VMEM((count, dim), f32),
            pltpu.VMEM((count, dim), f32),
            pltpu.VMEM((2, dim, tile), bf16),
            pltpu.VMEM((2, dim, tile), bf16),
            pltpu.SemaphoreType.DMA((2, 2)),
        ],
        compiler_params=params(),
        name="feed",
    )(*operands, weights, weights)


def cross_backward_kernel(
    spans,
    neighbours,
    lines,
    presence_ref,
    gsecond_ref,
    first_ref,
    norms_ref,
    perm_ref,
    perm_att_ref,
    att_p_ref,
    hid_p_ref,
    cross_q_ref,
    near_p_ref,
    near_kv_ref,
    co_p_ref,
    w_out_ref,
    w_cq_ref,
    w_co_ref,
    _,
    gfirst_ref,
    gatt_ref,
    all_ref,
    gnorm_ref,
    *rest,
):
    count, dim = first_ref.shape
    rows_near = near_p_ref.shape[0]
    span_len = count // spans
    near = rows_near // spans
    group = 256 // HEAD
    outs = []
    if lines:
        gatt_tok_ref, row_sems, send_sems = rest[5:]
        place = Place(lines)
        place.meet()
        send = Sender(place, send_sems)
    gco_ref, gcq_ref, gnear_ref, gw_ref, sems = rest[:5]

    def keep(index, value):
        slot = len(outs) % 3
        if len(outs) >= 3:
            outs[-3].wait()
        gw_ref[slot] = value.astype(bf16)
        outs.append(
            pltpu.make_async_copy(
                gw_ref.at[slot],
                all_ref.at[:, pl.ds((3 + index) * dim, dim)],
                sems.at[index],
            )
        )
        outs[-1].start()

    upper = gsecond_ref[...].astype(bf16)
    gco_ref[...] = nt(nt(upper, w_co_ref[...]).astype(bf16), perm_ref[...]).astype(bf16)

    def one_span(span):
        rows = rows_of(span, span_len)
        keys = rows_of(span, near)
        live, anyone = live_keys(presence_ref, span, (near, 1), 0, neighbours, near // neighbours)
        for begin in range(0, dim, group * HEAD):
            lanes = slice(begin, begin + group * HEAD)
            lanes_v = slice(dim + begin, dim + begin + group * HEAD)
            query = spread_heads(cross_q_ref[rows, lanes] * SCALE, span_len, group)
            grad_out = spread_heads(gco_ref[rows, lanes], span_len, group)
            key = near_kv_ref[keys, lanes]
            scores = jnp.where(live > 0, nt(key, query), masked_score)
            peak = jnp.max(scores, axis=0, keepdims=True)
            expon = jnp.exp(scores - peak) * live
            total = jnp.sum(expon, axis=0, keepdims=True) + 1.0 - anyone
            probs = expon * (1.0 / total)
            grad_probs = nt(near_kv_ref[keys, lanes_v], grad_out)
            inner = jnp.sum(probs * grad_probs, axis=0, keepdims=True)
            grad_scores = (probs * (grad_probs - inner)).astype(bf16)
            gcq_ref[rows, lanes] = (
                gather_heads(tn(grad_scores, key), span_len, group) * SCALE
            ).astype(bf16)
            gnear_ref[keys, lanes] = mm(grad_scores, query).astype(bf16)
            gnear_ref[keys, lanes_v] = mm(probs.astype(bf16), grad_out).astype(bf16)

    pl.loop(0, spans)(one_span)

    upstream = nt(nt(gcq_ref[...], w_cq_ref[...]).astype(bf16), perm_ref[...])
    normed, recip = centre_scale(first_ref[...])
    back, gain, shift = norm_back(upstream, normed, recip, norms_ref[2:3, :])
    gnorm_ref[0:1, :] = gain
    gnorm_ref[1:2, :] = shift
    gfirst_ref[...] = gsecond_ref[...] + back
    lower = gfirst_ref[...].astype(bf16)
    gatt = nt(nt(lower, w_out_ref[...]).astype(bf16), perm_att_ref[...]).astype(bf16)
    if lines:
        width = gatt_ref.shape[1]
        tokens = gatt_ref.shape[0] // 8
        shares = gatt.shape[1] // width
        gatt_tok_ref[...] = gatt

        def block(device):
            return gatt_tok_ref.at[
                pl.ds(pl.multiple_of(device // shares * tokens, tokens), tokens),
                pl.ds(pl.multiple_of(device % shares * width, width), width),
            ]

        def landing(device):
            return gatt_ref.at[pl.ds(pl.multiple_of(device * tokens, tokens), tokens)]

        for other in place.plane():
            send.start(None, block(other), landing(place.me), row_sems.at[place.me], seq=other)
        own = pltpu.make_async_copy(block(place.me), landing(place.me), row_sems.at[place.me])
        own.start()
    else:
        gatt_ref[...] = gatt
    keep(4, mm(co_p_ref[...].T, upper))
    near_t = near_p_ref[...].T
    for part in range(2):
        keep(2 + part, mm(near_t, gnear_ref[:, part * dim : (part + 1) * dim]))
    keep(1, mm(hid_p_ref[...].T, gcq_ref[...]))
    keep(0, mm(att_p_ref[...].T, lower))
    if lines:
        for other in place.plane():
            send.arrived(None, landing(other), row_sems.at[other])
        own.wait()
        send.finish()
    for copy in outs[-3:]:
        copy.wait()


def cross_backward(
    spans,
    neighbours,
    lines,
    presence,
    gsecond,
    first,
    norms,
    perm,
    perm_att,
    att_p,
    hid_p,
    cross_q,
    near_p,
    near_kv,
    co_p,
    weights,
    grads,
):
    count, dim = first.shape
    rows_near = near_p.shape[0]
    gatt_shape = (count, perm_att.shape[0])
    out_shape = [
        jax.ShapeDtypeStruct((count, dim), f32),
        jax.ShapeDtypeStruct(gatt_shape, bf16),
        jax.ShapeDtypeStruct(grads.shape, bf16),
        jax.ShapeDtypeStruct((2, dim), f32),
    ]
    scratch = [
        pltpu.VMEM((count, dim), bf16),
        pltpu.VMEM((count, dim), bf16),
        pltpu.VMEM((rows_near, 2 * dim), bf16),
        pltpu.VMEM((3, dim, dim), bf16),
        pltpu.SemaphoreType.DMA((5,)),
    ]
    compiler_params = params()
    if lines:
        out_shape[1] = jax.ShapeDtypeStruct((2 * count, gatt_shape[1] // 2), bf16)
        scratch += [
            pltpu.VMEM(gatt_shape, bf16),
            pltpu.SemaphoreType.DMA((8,)),
            pltpu.SemaphoreType.DMA((8,)),
        ]
        compiler_params = pltpu.CompilerParams(
            vmem_limit_bytes=VMEM_BYTES, collective_id=2, has_side_effects=True
        )
    operands = (
        gsecond,
        first,
        norms,
        perm,
        perm_att,
        att_p,
        hid_p,
        cross_q,
        near_p,
        near_kv,
        co_p,
    )
    return pl.pallas_call(
        partial(cross_backward_kernel, spans, neighbours, lines),
        out_shape=out_shape,
        grid=(1,),
        in_specs=[pl.BlockSpec(memory_space=pltpu.SMEM)]
        + [whole(op) for op in operands]
        + [column_block(dim, dim, index) for index in (3, 4, 7)]
        + [pl.BlockSpec(memory_space=pl.ANY)],
        out_specs=tuple(
            pl.BlockSpec(memory_space=pl.ANY) if index == 2 else whole_shape(shape.shape)
            for index, shape in enumerate(out_shape)
        ),
        scratch_shapes=scratch,
        input_output_aliases={len(operands) + 4: 2},
        compiler_params=compiler_params,
        name="cross_backward",
    )(presence, *operands, *([weights] * 3), grads)


def last_norm_kernel(parts_ref, x_ref, gfirst_ref, norms_ref, perm_ref, out_ref, gnorm_ref):
    total = parts_ref[0].astype(f32)
    for part in range(1, parts_ref.shape[0]):
        total = total + parts_ref[part].astype(f32)
    upstream = nt(total.astype(bf16), perm_ref[...])
    normed, recip = centre_scale(x_ref[...].astype(f32))
    back, gain, shift = norm_back(upstream, normed, recip, norms_ref[0:1, :])
    out_ref[...] = gfirst_ref[...] + back
    gnorm_ref[0:1, :] = gain
    gnorm_ref[1:2, :] = shift


def last_norm(parts, x, gfirst, norms, perm):
    count, dim = x.shape
    return pl.pallas_call(
        last_norm_kernel,
        out_shape=(
            jax.ShapeDtypeStruct((count, dim), f32),
            jax.ShapeDtypeStruct((2, dim), f32),
        ),
        compiler_params=params(),
        name="last_norm",
    )(parts, x, gfirst, norms, perm)


def forward_kernel(
    lines,
    pairs,
    spans,
    neighbours,
    presence_ref,
    w_ref,
    norm_ref,
    x_ref,
    perm_ref,
    cot_ref,
    near_ref,
    wts_ref,
    all_ref,
    hid_out,
    qkv_out,
    att_out,
    lse_out,
    att_p_out,
    first_out,
    hid_p_out,
    cross_q_out,
    near_p_out,
    near_kv_out,
    co_p_out,
    norms_ref,
    out_ref,
    gsecond_ref,
    gnorm_ref,
    *scratch,
):
    results, scratch = scratch[:11], scratch[11:]
    (
        hid_ref,
        qkv_ref,
        att_ref,
        lse_ref,
        att_p_ref,
        first_ref,
        hid_p_ref,
        cross_q_ref,
        near_p_ref,
        near_kv_ref,
        co_p_ref,
    ) = results
    work, scratch = scratch[:15], scratch[15:]
    (
        second_ref,
        own_ref,
        small_ref,
        rows_ref,
        w_qkv_ref,
        w_mid_ref,
        att_tok_ref,
        cross_ref,
        up_p_ref,
        up_t_ref,
        cot_p_ref,
        cot_t_ref,
        result_ref,
        back_ref,
        gfeed_ref,
    ) = work
    (
        send_sems,
        z_sems,
        y_sems,
        x_sems,
        a_sems,
        b_sems,
        sib_sems,
        norm_sems,
        row_sems,
        att_sems,
        local_sems,
        qkv_sems,
        mid_sems,
        feed_sems,
        out_sems,
    ) = scratch
    place = Place(lines)
    z, me, core = place.z, place.me, place.core
    length, dim = hid_ref.shape
    width = pairs * LANES
    tokens = length // 8
    half = own_ref.shape[0] // 2
    near_load = pltpu.make_async_copy(near_ref, near_p_ref, local_sems.at[2])
    near_load.start()
    own_ref[...] = w_ref[...].astype(bf16)
    place.meet()
    send = Sender(place, send_sems)
    unit = partial(unit_of, wts_ref, lines)
    events = place.events()
    keep = pltpu.make_async_copy(own_ref, unit(z, me), local_sems.at[0])
    keep.start()

    def obtain(index):
        condition, line, far, side = events[index]
        mine = unit(line, me)
        src = own_ref if far == 0 else mine
        if far:
            send.arrived(condition, mine, z_sems.at[line])
        if side >= 0:
            send.start(both(condition, z > 0), src, mine, z_sems.at[line], z=z - 1)
        if side <= 0:
            send.start(both(condition, z < lines - 1), src, mine, z_sems.at[line], z=z + 1)
        send.start(condition, src, mine, x_sems.at[line], seq=place.xn)
        send.start(condition, src, mine, y_sems.at[line], seq=place.yn)
        send.start(condition, src, mine, sib_sems.at[0, line], seq=place.sib)

    def pass_on(index):
        condition, line, _, _ = events[index]
        from_x, from_y = unit(line, place.xn), unit(line, place.yn)
        send.arrived(condition, from_x, x_sems.at[line])
        part = unit(line, place.xn, half, half)
        send.start(condition, part, part, b_sems.at[line], seq=place.yn)
        send.start(condition, from_x, from_x, sib_sems.at[1, line], seq=place.sib)
        send.arrived(condition, from_y, y_sems.at[line])
        part = unit(line, place.yn, 0, half)
        send.start(condition, part, part, a_sems.at[line], seq=place.xn)
        send.start(condition, from_y, from_y, sib_sems.at[2, line], seq=place.sib)

    def corner(index):
        condition, line, _, _ = events[index]
        for group, begin, sems in ((3, 0, a_sems), (4, half, b_sems)):
            part = unit(line, place.dg, begin, half)
            send.arrived(condition, part, sems.at[line])
            send.start(condition, part, part, sib_sems.at[group, line], seq=place.sib)

    kept = []

    def emit(index):
        out = (
            hid_out,
            qkv_out,
            att_out,
            lse_out,
            att_p_out,
            first_out,
            hid_p_out,
            cross_q_out,
            near_p_out,
            near_kv_out,
            co_p_out,
        )[index]
        kept.append(pltpu.make_async_copy(results[index], out, out_sems.at[index]))
        kept[-1].start()

    def row_block(seq):
        return rows_ref.at[pl.ds(pl.multiple_of(seq * tokens, tokens), tokens)]

    def middle(index):
        return pltpu.make_async_copy(
            wts_ref.at[:, pl.ds((3 + index) * dim, dim)], w_mid_ref.at[index], mid_sems.at[index]
        )

    obtain(0)
    own_rows = pltpu.make_async_copy(x_ref.at[place.chip], row_block(me), local_sems.at[1])
    own_rows.start()
    others = (place.xn, place.yn, place.dg)
    for other in place.line():
        send.start(None, norm_ref, small_ref.at[z], norm_sems.at[z], z=other)
    small_ref[z] = norm_ref[...]
    send.start(None, x_ref.at[place.chip], row_block(me), row_sems.at[me], seq=place.sib)
    for other in others:
        send.start(None, x_ref.at[other // 2], row_block(me), row_sems.at[me], seq=other)
    near_load.wait()

    @pl.loop(0, near_p_ref.shape[0] // 512)
    def _(step):
        rows = rows_of(step, 512)
        near_p_ref[rows, :] = mm(near_p_ref[rows, :], perm_ref[...]).astype(bf16)

    emit(8)
    obtain(1)
    obtain(2)
    pass_on(0)
    for other in others:
        send.arrived(None, row_block(other), row_sems.at[other])
        send.start(None, row_block(other), row_block(other), row_sems.at[other], seq=place.sib)
    obtain(3)
    obtain(4)
    cot_p_ref[...] = mm(cot_ref[...], perm_ref[...]).astype(bf16)
    cot_t_ref[...] = cot_p_ref[...].T
    pass_on(1)
    pass_on(2)
    corner(0)

    for other in place.line():
        send.arrived(None, small_ref.at[other], norm_sems.at[other])
    piece = small_ref.shape[2]
    total = None
    for line in range(lines):
        row = lax.broadcasted_iota(jnp.int32, (piece, dim), 0)
        column = lax.broadcasted_iota(jnp.int32, (piece, dim), 1)
        part = dim // lines
        place_of = jnp.logical_and(row < part, column == row + line * part).astype(bf16)
        term = mm(small_ref[line], place_of)
        total = term if total is None else total + term
    norms_ref[...] = total[: norms_ref.shape[0]]

    last = len(events)
    for index in range(5, last, 2):
        obtain(index)
        obtain(index + 1)
        if index == 5:
            for other in others:
                theirs = other + 1 - 2 * core
                send.arrived(None, row_block(theirs), row_sems.at[theirs])
            send.arrived(None, row_block(place.sib), row_sems.at[place.sib])
            own_rows.wait()
            norm_rows(rows_ref, norms_ref[...], perm_ref, hid_ref)
            emit(0)
        pass_on(index - 2)
        pass_on(index - 1)
        corner(index - 4)
        corner(index - 3)
    for index in range(last - 2, last):
        pass_on(index)
    for index in range(last - 4, last):
        corner(index)
    keep.wait()
    for line in range(lines):
        for group, first in enumerate((me, place.xn, place.yn)):
            theirs = first + 1 - 2 * core
            send.arrived(None, unit(line, theirs), sib_sems.at[group, line])
        theirs = place.dg + 1 - 2 * core
        send.arrived(None, unit(line, theirs, 0, half), sib_sems.at[3, line])
        send.arrived(None, unit(line, theirs, half, half), sib_sems.at[4, line])
    copies = weight_copies(pairs, dim, wts_ref, w_qkv_ref, qkv_sems)
    for copy in copies + [middle(index) for index in (2, 3, 0, 1, 4)]:
        copy.start()
    for part in range(3):
        copies[part].wait()
        triple_part(part, pairs, hid_ref, w_qkv_ref, qkv_ref)
    emit(1)

    share = lax.rem(me, dim // width)
    seq_rows = pl.ds(pl.multiple_of(place.chip * tokens, tokens), tokens)

    def landing(pair, chip_rows, share):
        lanes = pl.ds(pl.multiple_of(share * width + pair * LANES, LANES), LANES)
        return att_tok_ref.at[chip_rows, lanes]

    for pair in range(pairs):
        lanes = slice(pair * LANES, (pair + 1) * LANES)
        pair_forward(pair, pairs, qkv_ref, att_ref, lse_ref, lambda: None)
        for other in place.plane():
            block = att_ref.at[pl.ds(pl.multiple_of(other * tokens, tokens), tokens), lanes]
            to = landing(pair, seq_rows, share)
            send.start(None, block, to, att_sems.at[pair, me], seq=other)
        own_block = att_ref[pl.ds(pl.multiple_of(me * tokens, tokens), tokens), lanes]
        landing(pair, seq_rows, share)[...] = own_block
    emit(2)
    emit(3)

    for index in (2, 3, 0, 1, 4):
        middle(index).wait()
    for step in range(near_p_ref.shape[0] // 512):
        rows = slice(step * 512, (step + 1) * 512)
        near_kv_ref[rows, :dim] = mm(near_p_ref[rows, :], w_mid_ref[2]).astype(bf16)
        near_kv_ref[rows, dim:] = mm(near_p_ref[rows, :], w_mid_ref[3]).astype(bf16)
    emit(9)
    w_out_ref, w_cq_ref, w_co_ref = (w_mid_ref.at[index] for index in (0, 1, 4))
    for pair in range(pairs):
        for other in place.plane():
            rows = pl.ds(pl.multiple_of(other // 2 * tokens, tokens), tokens)
            send.arrived(None, landing(pair, rows, lax.rem(other, 2)), att_sems.at[pair, other])
    att_p_ref[...] = mm(att_tok_ref[...], perm_ref[...]).astype(bf16)
    emit(4)
    own_x = x_ref[...].reshape(first_ref.shape).astype(f32)
    first_ref[...] = own_x + mm(att_p_ref[...], w_out_ref[...])
    emit(5)
    normed, _ = centre_scale(first_ref[...])
    hidden = (normed * norms_ref[2:3, :] + norms_ref[3:4, :]).astype(bf16)
    hid_p_ref[...] = mm(hidden, perm_ref[...]).astype(bf16)
    emit(6)
    cross_q_ref[...] = mm(hid_p_ref[...], w_cq_ref[...]).astype(bf16)
    emit(7)
    pl.loop(0, spans)(
        lambda span: span_forward(
            span, spans, neighbours, presence_ref, cross_q_ref, near_kv_ref, cross_ref
        )
    )

    ffw = (all_ref.shape[1] - 8 * dim) // 2
    tile = gfeed_ref.shape[2]
    order = range(0, ffw, tile)

    def tile_load(index):
        return [
            pltpu.make_async_copy(
                wts_ref.at[:, pl.ds(8 * dim + part * ffw + order[index], tile)],
                w_mid_ref.at[(2 * index + part) % 4],
                feed_sems.at[0, (2 * index + part) % 4],
            )
            for part in range(2)
        ]

    def tile_store(index):
        return [
            pltpu.make_async_copy(
                gfeed_ref.at[(2 * index + part) % 4],
                all_ref.at[:, pl.ds(8 * dim + part * ffw + order[index], tile)],
                feed_sems.at[1, (2 * index + part) % 4],
            )
            for part in range(2)
        ]

    for copy in tile_load(0) + tile_load(1):
        copy.start()
    co_p_ref[...] = mm(cross_ref[...], perm_ref[...]).astype(bf16)
    emit(10)
    second_ref[...] = first_ref[...] + mm(co_p_ref[...], w_co_ref[...])
    normed, _ = centre_scale(second_ref[...])
    hidden = (normed * norms_ref[4:5, :] + norms_ref[5:6, :]).astype(bf16)
    up_p_ref[...] = mm(hidden, perm_ref[...]).astype(bf16)
    up_t_ref[...] = up_p_ref[...].T

    for index in range(len(order)):
        up_ref, down_ref = w_mid_ref.at[2 * index % 4], w_mid_ref.at[2 * index % 4 + 1]
        for copy in tile_load(index):
            copy.wait()
        if index >= 2:
            for copy in tile_store(index - 2):
                copy.wait()
        active, slope = gelu_parts(mm(up_p_ref[...], up_ref[...]))
        active = active.astype(bf16)
        term = nt(active, down_ref[...])
        result_ref[...] = term if index == 0 else result_ref[...] + term
        gfeed_ref[2 * index % 4 + 1] = mm(cot_t_ref[...], active).astype(bf16)
        grad_up = (mm(cot_p_ref[...], down_ref[...]) * slope).astype(bf16)
        gfeed_ref[2 * index % 4] = mm(up_t_ref[...], grad_up).astype(bf16)
        for copy in tile_store(index):
            copy.start()
        term = nt(grad_up, up_ref[...])
        back_ref[...] = term if index == 0 else back_ref[...] + term
        if index + 2 < len(order):
            for copy in tile_load(index + 2):
                copy.start()

    out_ref[...] = (second_ref[...] + nt(result_ref[...].astype(bf16), perm_ref[...])).astype(bf16)
    upstream = nt(back_ref[...].astype(bf16), perm_ref[...])
    normed, recip = centre_scale(second_ref[...])
    back, gain, shift = norm_back(upstream, normed, recip, norms_ref[4:5, :])
    gsecond_ref[...] = cot_ref[...].astype(f32) + back
    gnorm_ref[0:1, :] = gain
    gnorm_ref[1:2, :] = shift
    for index in range(len(order) - 2, len(order)):
        for copy in tile_store(index):
            copy.wait()
    for copy in kept:
        copy.wait()
    send.finish()


def forward(lines, pairs, spans, neighbours, presence, w_shard, n_shard, inputs, perm, cot, near):
    unit_rows, unit_cols = w_shard.shape
    seqs, tokens, dim = inputs.shape
    count, length, width = seqs * tokens, 8 * tokens, pairs * LANES
    rows_near = near.shape[0]
    events = 2 * lines - 1
    any_space = pl.BlockSpec(memory_space=pl.ANY)
    vmem = pl.BlockSpec(memory_space=pltpu.VMEM)
    dma = pltpu.SemaphoreType.DMA
    packed = jax.ShapeDtypeStruct((unit_rows * lines, unit_cols * 8), bf16)
    kept = (
        ((length, dim), bf16),
        ((3 * pairs, length, LANES), bf16),
        ((length, width), bf16),
        ((pairs, 2, length), f32),
        ((count, dim), bf16),
        ((count, dim), f32),
        ((count, dim), bf16),
        ((count, dim), bf16),
        ((rows_near, dim), bf16),
        ((rows_near, 2 * dim), bf16),
        ((count, dim), bf16),
    )
    tile = unit_cols // 2
    return pl.pallas_call(
        partial(forward_kernel, lines, pairs, spans, neighbours),
        out_shape=(packed, packed)
        + tuple(jax.ShapeDtypeStruct(*entry) for entry in kept)
        + (
            jax.ShapeDtypeStruct((8, dim), f32),
            jax.ShapeDtypeStruct((count, dim), bf16),
            jax.ShapeDtypeStruct((count, dim), f32),
            jax.ShapeDtypeStruct((2, dim), f32),
        ),
        in_specs=[pl.BlockSpec(memory_space=pltpu.SMEM)] + [vmem] * 5 + [any_space],
        out_specs=(any_space,) * (2 + len(kept)) + (vmem,) * 4,
        scratch_shapes=[pltpu.VMEM(*entry) for entry in kept]
        + [
            pltpu.VMEM((count, dim), f32),
            pltpu.VMEM((unit_rows, unit_cols), bf16),
            pltpu.VMEM((lines,) + n_shard.shape, bf16),
            pltpu.VMEM((length, dim), bf16),
            pltpu.VMEM((dim, 3 * width), bf16),
            pltpu.VMEM((5, dim, dim), bf16),
            pltpu.VMEM((count, dim), bf16),
            pltpu.VMEM((count, dim), bf16),
            pltpu.VMEM((count, dim), bf16),
            pltpu.VMEM((dim, count), bf16),
            pltpu.VMEM((count, dim), bf16),
            pltpu.VMEM((dim, count), bf16),
            pltpu.VMEM((count, dim), f32),
            pltpu.VMEM((count, dim), f32),
            pltpu.VMEM((4, dim, tile), bf16),
            dma((11 * events + 7 + lines + 7 * pairs,)),
            dma((lines,)),
            dma((lines,)),
            dma((lines,)),
            dma((lines,)),
            dma((lines,)),
            dma((5, lines)),
            dma((lines,)),
            dma((8,)),
            dma((pairs, 8)),
            dma((3,)),
            dma((3,)),
            dma((5,)),
            dma((2, 4)),
            dma((len(kept),)),
        ],
        compiler_params=pltpu.CompilerParams(
            vmem_limit_bytes=VMEM_BYTES, collective_id=1, has_side_effects=True
        ),
        name="forward",
    )(presence, w_shard, n_shard, inputs, perm, cot, near)


def reduce_kernel(
    lines,
    grads_ref,
    small_ref,
    shard_ref,
    norms_ref,
    mine_ref,
    sib_ref,
    corner_a_ref,
    corner_b_ref,
    from_x_ref,
    from_y_ref,
    below_ref,
    above_ref,
    plane_ref,
    plane_sum_ref,
    line_ref,
    send_sems,
    load_sems,
    sib_sems,
    a_sems,
    b_sems,
    x_sems,
    y_sems,
    below_sems,
    above_sems,
    plane_sems,
    line_sems,
):
    place = Place(lines)
    z, me = place.z, place.me
    unit_rows, unit_cols = shard_ref.shape
    half = unit_rows // 2
    tile = 32
    place.meet()
    send = Sender(place, send_sems)
    chips = (place.dg, place.yn, place.xn, me)
    corner, over_y, over_x, here = range(4)

    unit = partial(unit_of, grads_ref, lines)

    def load(which, line):
        return pltpu.make_async_copy(
            unit(line, chips[which]), mine_ref.at[which, line], load_sems.at[which, line]
        )

    for other in place.plane():
        send.start(None, small_ref, plane_ref.at[me], plane_sems.at[me], seq=other)
    plane_ref[me] = small_ref[...]

    events = place.events()[::-1]
    for condition, line, _, _ in events:
        for which in range(4):
            theirs = chips[which] + 1 - 2 * place.core
            send.start(
                condition,
                unit(line, theirs),
                sib_ref.at[which, line],
                sib_sems.at[which, line],
                seq=place.sib,
            )
            when(condition, load(which, line).start)

    def add(target, *terms, begin=0, size=unit_rows):
        @pl.loop(0, size // tile)
        def _(step):
            rows = pl.ds(pl.multiple_of(begin + step * tile, tile), tile)
            if len(terms) == 1:
                ref, first = terms[0]
                at = pl.ds(pl.multiple_of(begin - first + step * tile, tile), tile)
                target[rows, :] = target[rows, :] + ref[at, :]
            else:
                total = target[rows, :].astype(f32)
                for ref, first in terms:
                    at = pl.ds(pl.multiple_of(begin - first + step * tile, tile), tile)
                    total = total + ref[at, :].astype(f32)
                target[rows, :] = total.astype(target.dtype)

    def own(which, index):
        condition, line, _, _ = events[index]
        send.arrived(condition, sib_ref.at[which, line], sib_sems.at[which, line])
        when(condition, load(which, line).wait)

    def first(index):
        condition, line, _, _ = events[index]
        own(corner, index)
        target = mine_ref.at[corner, line]
        when(condition, lambda: add(target, (sib_ref.at[corner, line], 0)))
        send.start(
            condition,
            target.at[pl.ds(0, half)],
            corner_a_ref.at[line],
            a_sems.at[line],
            seq=place.xn,
        )
        send.start(
            condition,
            target.at[pl.ds(half, half)],
            corner_b_ref.at[line],
            b_sems.at[line],
            seq=place.yn,
        )

    def second(index):
        condition, line, _, _ = events[index]
        for which, part, sems, begin, to, landing, landing_sems in (
            (over_y, corner_a_ref, a_sems, 0, place.yn, from_y_ref, y_sems),
            (over_x, corner_b_ref, b_sems, half, place.xn, from_x_ref, x_sems),
        ):
            own(which, index)
            send.arrived(condition, part.at[line], sems.at[line])
            target = mine_ref.at[which, line]

            def body(which=which, part=part, begin=begin, target=target):
                add(
                    target,
                    (sib_ref.at[which, line], 0),
                    (part.at[line], begin),
                    begin=begin,
                    size=half,
                )
                add(target, (sib_ref.at[which, line], 0), begin=half - begin, size=half)

            when(condition, body)
            send.start(condition, target, landing.at[line], landing_sems.at[line], seq=to)

    def third(index):
        condition, line, far, side = events[index]
        own(here, index)
        send.arrived(condition, from_x_ref.at[line], x_sems.at[line])
        send.arrived(condition, from_y_ref.at[line], y_sems.at[line])
        target = mine_ref.at[here, line]
        terms = [(ref.at[line], 0) for ref in (sib_ref.at[here], from_x_ref, from_y_ref)]
        if side == 0:
            has_below, has_above = z > 0, z < lines - 1
            add(target, *terms)
            send.arrived(has_below, below_ref.at[line], below_sems.at[line])
            send.arrived(has_above, above_ref.at[line], above_sems.at[line])

            @pl.loop(0, unit_rows // tile)
            def _(step):
                rows = rows_of(step, tile)
                shard_ref[rows, :] = target[rows, :].astype(f32)

            when(has_below, lambda: add(shard_ref, (below_ref.at[line], 0)))
            when(has_above, lambda: add(shard_ref, (above_ref.at[line], 0)))
            return
        landing, sems = (below_ref, below_sems) if side > 0 else (above_ref, above_sems)
        more = both(condition, z > 0) if side > 0 else both(condition, z < lines - 1)
        none = both(condition, z == 0) if side > 0 else both(condition, z == lines - 1)
        send.arrived(more, landing.at[line], sems.at[line])
        when(more, lambda: add(target, *terms, (landing.at[line], 0)))
        when(none, lambda: add(target, *terms))
        send.start(condition, target, landing.at[line], sems.at[line], z=z + side)

    count = len(events)
    first(0)
    first(1)
    for index in range(2, count + 4):
        if index < count:
            first(index)
        if 0 <= index - 2 < count:
            second(index - 2)
        if index == 3:
            for other in place.plane():
                send.arrived(None, plane_ref.at[other], plane_sems.at[other])
            total = plane_ref[0]
            for other in range(1, 8):
                total = total + plane_ref[other]
            plane_sum_ref[...] = total
            line_ref[z] = total
            for other in place.line():
                send.start(None, plane_sum_ref, line_ref.at[z], line_sems.at[z], z=other)
        if 0 <= index - 4 < count:
            third(index - 4)

    for other in place.line():
        send.arrived(None, line_ref.at[other], line_sems.at[other])
    total = line_ref[0]
    for other in range(1, lines):
        total = total + line_ref[other]
    norms_ref[...] = total
    send.finish()


def reduce_grads(lines, grads, small):
    rows, cols = grads.shape
    unit_rows, unit_cols = rows // lines, cols // 8
    half = unit_rows // 2
    any_space = pl.BlockSpec(memory_space=pl.ANY)
    vmem = pl.BlockSpec(memory_space=pltpu.VMEM)
    dma = pltpu.SemaphoreType.DMA
    return pl.pallas_call(
        partial(reduce_kernel, lines),
        out_shape=(
            jax.ShapeDtypeStruct((unit_rows, unit_cols), f32),
            jax.ShapeDtypeStruct(small.shape, f32),
        ),
        in_specs=[any_space, vmem],
        out_specs=(vmem, vmem),
        scratch_shapes=[
            pltpu.VMEM((4, lines, unit_rows, unit_cols), bf16),
            pltpu.VMEM((4, lines, unit_rows, unit_cols), bf16),
            pltpu.VMEM((lines, half, unit_cols), bf16),
            pltpu.VMEM((lines, half, unit_cols), bf16),
            pltpu.VMEM((lines, unit_rows, unit_cols), bf16),
            pltpu.VMEM((lines, unit_rows, unit_cols), bf16),
            pltpu.VMEM((lines, unit_rows, unit_cols), bf16),
            pltpu.VMEM((lines, unit_rows, unit_cols), bf16),
            pltpu.VMEM((8,) + small.shape, f32),
            pltpu.VMEM(small.shape, f32),
            pltpu.VMEM((lines,) + small.shape, f32),
            dma((9 * (2 * lines - 1) + 7 + lines,)),
            dma((4, lines)),
            dma((4, lines)),
            dma((lines,)),
            dma((lines,)),
            dma((lines,)),
            dma((lines,)),
            dma((lines,)),
            dma((lines,)),
            dma((8,)),
            dma((lines,)),
        ],
        compiler_params=pltpu.CompilerParams(
            vmem_limit_bytes=VMEM_BYTES, collective_id=4, has_side_effects=True
        ),
        name="reduce_grads",
    )(grads, small)


def adam_update(grad, weight, first, second, average, rate, decay):
    first = beta_first * first + (1.0 - beta_first) * grad
    second = beta_second * second + (1.0 - beta_second) * grad * grad
    stepped = (
        first / (1.0 - beta_first**STEP) / (jnp.sqrt(second / (1.0 - beta_second**STEP)) + adam_eps)
    )
    weight = weight - rate * (stepped + decay * weight)
    average = ema_decay * average + (1.0 - ema_decay) * weight
    return (first, second, weight, average)


def on_device(
    inputs,
    cotangent,
    neighbours,
    presence,
    row_order,
    w_master,
    w_first,
    w_second,
    w_average,
    n_master,
    n_first,
    n_second,
    n_average,
):
    seqs, tokens, dim = inputs.shape
    heads = dim // HEAD
    devices = lax.axis_size("seq")
    count = seqs * tokens
    length = devices * tokens
    me = lax.axis_index("seq")
    shares = devices // seqs
    held = heads // shares
    pairs = (held + 1) // 2
    width = pairs * LANES
    spare = width - held * HEAD
    sequence, share = me // shares, me % shares

    lines = lax.axis_size("dp")
    planar = devices == 8 and seqs == 4 and spare == 0
    perm = (jnp.arange(dim)[:, None] == row_order[None, :]).astype(bf16)
    perm_att = perm
    if spare:
        perm_att = jnp.pad(perm.reshape(shares, held * HEAD, dim), ((0, 0), (0, spare), (0, 0)))
        perm_att = perm_att.reshape(shares * width, dim)
    x = inputs.reshape(count, dim)
    spans = seqs * neighbours.shape[1]
    each = neighbours.shape[2]
    near = neighbours.reshape(-1, dim)
    live = presence.reshape(-1)
    part = n_master.shape[1]
    if planar:
        small = jnp.pad(n_master.astype(bf16), ((0, 16 - 6), (0, -part % LANES)))
        (
            weights,
            grads,
            hid,
            qkv,
            att,
            lse,
            att_p,
            first,
            hid_p,
            cross_q,
            near_p,
            near_kv,
            co_p,
            norms,
            outputs,
            gsecond,
            gnorm_e,
        ) = forward(
            lines,
            pairs,
            spans,
            each,
            live,
            w_master,
            small,
            inputs,
            perm,
            cotangent.reshape(count, dim),
            near,
        )
    else:
        weights = lax.all_gather(w_master.astype(bf16), "dp", axis=0, tiled=True)
        weights = lax.all_gather(weights, "seq", axis=1, tiled=True)
        norms = lax.all_gather(n_master.astype(bf16), "dp", axis=1, tiled=True).astype(f32)
        rows = lax.all_to_all(jnp.repeat(inputs, shares, axis=0), "seq", 0, 0)
        rows = rows.reshape(length, dim)
        w_qkv = weights[:, : 3 * dim].reshape(dim, 3, shares, held * HEAD)
        w_qkv = lax.dynamic_index_in_dim(w_qkv, share, axis=2, keepdims=False)
        w_qkv = jnp.pad(w_qkv, ((0, 0), (0, 0), (0, spare))).reshape(dim, 3 * width)
        hid, qkv, att, lse = self_forward(pairs, rows, norms, perm, w_qkv)
        att_tok = (
            lax.all_to_all(att.reshape(devices, tokens, width), "seq", 0, 0)
            .reshape(seqs, shares, tokens, width)
            .transpose(0, 2, 1, 3)
            .reshape(count, shares * width)
        )
        att_p, first, hid_p, cross_q, near_p, near_kv, co_p, second = cross_forward(
            spans, each, live, att_tok, x, norms, perm, perm_att, near, weights
        )
        outputs, gsecond, grads, gnorm_e = feed(
            second, cotangent.reshape(count, dim), norms, perm, weights
        )
    gfirst, gatt_tok, grads, gnorm_c = cross_backward(
        spans,
        each,
        lines if planar else 0,
        live,
        gsecond,
        first,
        norms,
        perm,
        perm_att,
        att_p,
        hid_p,
        cross_q,
        near_p,
        near_kv,
        co_p,
        weights,
        grads,
    )
    if planar:
        others = jnp.concatenate(
            [jnp.zeros((2, dim), f32), gnorm_c, gnorm_e, jnp.zeros((2, dim), f32)], axis=0
        )
        grads, grad_inputs, norm_grads = finish(
            pairs,
            lines,
            qkv,
            att,
            gatt_tok,
            lse,
            hid,
            x,
            gfirst,
            norms,
            perm,
            others,
            weights,
            grads,
        )
        grad_shard, norm_sums = reduce_grads(lines, grads, norm_grads)
        norm_shard = lax.dynamic_slice(norm_sums, (0, lax.axis_index("dp") * part), (6, part))
    else:
        gatt = lax.all_to_all(
            gatt_tok.reshape(seqs, tokens, shares, width)
            .transpose(0, 2, 1, 3)
            .reshape(devices, tokens, width),
            "seq",
            0,
            0,
        ).reshape(length, width)
        gqkv, ghid = self_backward(pairs, qkv, att, gatt, lse, hid, w_qkv)
        parts = (
            lax.all_to_all(ghid.reshape(devices, tokens, dim), "seq", 0, 0)
            .reshape(seqs, shares, tokens, dim)
            .transpose(1, 0, 2, 3)
            .reshape(shares, count, dim)
        )
        grad_inputs, gnorm_a = last_norm(parts, x, gfirst, norms, perm)
        gqkv = gqkv.reshape(dim, 3, 1, width)[..., : held * HEAD]
        gqkv = jnp.where(jnp.arange(shares)[:, None] == share, gqkv, jnp.zeros_like(gqkv))
        grads = lax.dynamic_update_slice(grads, gqkv.reshape(dim, 3 * dim), (0, 0))
        norm_grads = lax.psum(jnp.concatenate([gnorm_a, gnorm_c, gnorm_e], axis=0), "seq")
        partial_sum = lax.psum_scatter(grads, "seq", scatter_dimension=1, tiled=True)
        grad_shard = lax.psum_scatter(partial_sum, "dp", scatter_dimension=0, tiled=True)
        grad_shard = grad_shard.astype(f32)
        norm_shard = lax.psum_scatter(
            norm_grads.astype(bf16), "dp", scatter_dimension=1, tiled=True
        ).astype(f32)
    w_first_new, w_second_new, w_new, w_average_new = adam_update(
        grad_shard, w_master, w_first, w_second, w_average, learn_rate, weight_decay
    )
    n_first_new, n_second_new, n_new, n_average_new = adam_update(
        norm_shard, n_master, n_first, n_second, n_average, norm_rate, 0.0
    )
    return (
        outputs.reshape(seqs, tokens, dim),
        grad_inputs.reshape(seqs, tokens, dim),
        w_first_new,
        w_second_new,
        w_new,
        w_average_new,
        n_first_new,
        n_second_new,
        n_new,
        n_average_new,
    )


def solution(mesh):
    in_specs = (
        P("dp", "seq", None),
        P("dp", "seq", None),
        P("dp", "seq", None, None, None),
        P("dp", "seq", None),
        P(),
        P("dp", "seq"),
        P("dp", "seq"),
        P("dp", "seq"),
        P("dp", "seq"),
        P(None, "dp"),
        P(None, "dp"),
        P(None, "dp"),
        P(None, "dp"),
    )
    out_specs = (
        P("dp", "seq", None),
        P("dp", "seq", None),
        P("dp", "seq"),
        P("dp", "seq"),
        P("dp", "seq"),
        P("dp", "seq"),
        P(None, "dp"),
        P(None, "dp"),
        P(None, "dp"),
        P(None, "dp"),
    )
    return jax.shard_map(
        on_device, mesh=mesh, in_specs=in_specs, out_specs=out_specs, check_vma=False
    )
```

```python
from functools import partial

import jax
import jax.numpy as jnp
from jax import lax
from jax.experimental import pallas as pl
from jax.experimental.pallas import tpu as pltpu
from jax.sharding import PartitionSpec as P

HEAD = 64
STEP = 5
LANES = 128
SCALE = HEAD ** (-0.5)

beta_first = 0.9
beta_second = 0.95
adam_eps = 1e-08
learn_rate = 0.04
norm_rate = 0.6
weight_decay = 0.1
ema_decay = 0.5
norm_eps = 1e-05
masked_score = -1e30
VMEM_BYTES = 62 * 1024 * 1024
bf16 = jnp.bfloat16
f32 = jnp.float32


def mm(left, right):
    return lax.dot_general(left, right, (((1,), (0,)), ((), ())), preferred_element_type=f32)


def nt(left, right):
    return lax.dot_general(left, right, (((1,), (1,)), ((), ())), preferred_element_type=f32)


def tn(left, right):
    return lax.dot_general(left, right, (((0,), (0,)), ((), ())), preferred_element_type=f32)


def params():
    return pltpu.CompilerParams(vmem_limit_bytes=VMEM_BYTES)


def rows_of(index, size):
    return pl.ds(pl.multiple_of(index * size, size), size)


def centre_scale(values):
    centre = jnp.mean(values, axis=-1, keepdims=True)
    centred = values - centre
    spread = jnp.mean(centred * centred, axis=-1, keepdims=True)
    recip = lax.rsqrt(spread + norm_eps)
    return centred * recip, recip


def norm_back(upstream, normed, recip, gain):
    scaled = upstream * gain
    inner = (
        scaled
        - jnp.mean(scaled, axis=-1, keepdims=True)
        - normed * jnp.mean(scaled * normed, axis=-1, keepdims=True)
    )
    return (
        recip * inner,
        jnp.sum(upstream * normed, axis=0, keepdims=True),
        jnp.sum(upstream, axis=0, keepdims=True),
    )


def gelu_parts(value):
    const = 0.7978845608028654
    square = value * value
    bend = jnp.tanh(const * value * (1.0 + 0.044715 * square))
    half = 0.5 * (1.0 + bend)
    slope = half + 0.5 * value * (1.0 - bend * bend) * (const * (1.0 + 3 * 0.044715 * square))
    return value * half, slope


def head_mask(rows, half):
    lane = lax.broadcasted_iota(jnp.int32, (rows, LANES), 1)
    return (lane < HEAD) if half == 0 else (lane >= HEAD)


def pick(mask, value):
    return jnp.where(mask, value, jnp.zeros_like(value))


MESH = pl.DeviceIdType.MESH


class Place:
    def __init__(self, lines):
        self.lines = lines
        self.z = lax.axis_index("dp")
        self.me = lax.axis_index("seq")
        core, x, y = self.me % 2, (self.me // 2) % 2, self.me // 4
        self.core, self.x, self.y, self.chip = core, x, y, self.me // 2
        self.sib = self.me + 1 - 2 * core
        self.xn = self.me + 2 - 4 * x
        self.yn = self.me + 4 - 8 * y
        self.dg = self.xn + 4 - 8 * y

    def events(self):
        found = [(None, self.z, 0, 0)]
        for far in range(1, self.lines):
            found.append((self.z >= far, self.z - far, far, -1))
            found.append((self.z + far < self.lines, self.z + far, far, 1))
        return found

    def plane(self):
        return [lax.rem(self.me + step, 8) for step in range(1, 8)]

    def line(self):
        return [lax.rem(self.z + step, self.lines) for step in range(1, self.lines)]

    def meet(self):
        barrier = pltpu.get_barrier_semaphore()
        for other in self.plane():
            pl.semaphore_signal(
                barrier, inc=1, device_id={"dp": self.z, "seq": other}, device_id_type=MESH
            )
        for other in self.line():
            pl.semaphore_signal(
                barrier, inc=1, device_id={"dp": other, "seq": self.me}, device_id_type=MESH
            )
        pl.semaphore_wait(barrier, 7 + self.lines - 1)


def when(condition, body):
    if condition is None:
        body()
    else:
        pl.when(condition)(body)


def both(first, second):
    if first is None or second is None:
        return second if first is None else first
    return jnp.logical_and(first, second)


class Sender:
    def __init__(self, place, send_sems):
        self.place, self.sems, self.open, self.count = place, send_sems, [], 0

    def start(self, condition, src, dst, recv_sem, z=None, seq=None):
        place = self.place
        target = {"dp": place.z if z is None else z, "seq": place.me if seq is None else seq}
        copy = pltpu.make_async_remote_copy(
            src_ref=src,
            dst_ref=dst,
            send_sem=self.sems.at[self.count],
            recv_sem=recv_sem,
            device_id=target,
            device_id_type=MESH,
        )
        self.open.append((condition, copy))
        self.count += 1
        when(condition, copy.start)

    def arrived(self, condition, ref, recv_sem):
        copy = pltpu.make_async_remote_copy(
            src_ref=ref,
            dst_ref=ref,
            send_sem=self.sems.at[0],
            recv_sem=recv_sem,
            device_id={"dp": self.place.z, "seq": self.place.sib},
            device_id_type=MESH,
        )
        when(condition, copy.wait_recv)

    def finish(self):
        for condition, copy in self.open:
            when(condition, copy.wait_send)
        self.open = []


class Weave:
    def __init__(self, steps):
        self.steps = list(steps)

    def some(self, count):
        for _ in range(min(count, len(self.steps))):
            self.steps.pop(0)()

    def rest(self):
        self.some(len(self.steps))


def unit_of(ref, lines, line, seq, begin=0, size=None):
    rows, cols = ref.shape[0] // lines, ref.shape[1] // 8
    size = rows if size is None else size
    return ref.at[
        pl.ds(pl.multiple_of(line * rows + begin, 16), size),
        pl.ds(pl.multiple_of(seq * cols, cols), cols),
    ]


def weight_copies(pairs, dim, wts_ref, w_ref, sems):
    width = pairs * LANES
    first = lax.rem(lax.axis_index("seq"), dim // width) * width
    return [
        pltpu.make_async_copy(
            wts_ref.at[:, pl.ds(pl.multiple_of(first + part * dim, LANES), width)],
            w_ref.at[:, pl.ds(part * width, width)],
            sems.at[part],
        )
        for part in range(3)
    ]


def pair_forward(pair, pairs, qkv_ref, att_ref, lse_ref, between):
    length = att_ref.shape[0]
    tile = 256
    below = lax.broadcasted_iota(jnp.int32, (tile, tile), 1) <= lax.broadcasted_iota(
        jnp.int32, (tile, tile), 0
    )
    masks = [head_mask(tile, 0), head_mask(tile, 1)]
    lane = lax.broadcasted_iota(jnp.int32, (tile, LANES), 1)
    for step in range(length // tile):
        rows = slice(step * tile, (step + 1) * tile)
        query = qkv_ref[pair, rows, :] * SCALE
        keys_here = qkv_ref[pairs + pair, rows, :]
        values_here = qkv_ref[2 * pairs + pair, rows, :]
        outs, logs = [], []
        for half in range(2):
            mine = pick(masks[half], query)
            here = jnp.where(below, nt(mine, keys_here), masked_score)
            peak = jnp.max(here, axis=-1, keepdims=True)
            if step:
                past = nt(mine, qkv_ref[pairs + pair, : step * tile, :])
                peak = jnp.maximum(peak, jnp.max(past, axis=-1, keepdims=True))
                past = jnp.exp(past - peak)
            here = jnp.exp(here - peak)
            total = jnp.sum(here, axis=-1, keepdims=True)
            out = mm(here.astype(bf16), values_here)
            if step:
                total = total + jnp.sum(past, axis=-1, keepdims=True)
                out = out + mm(past.astype(bf16), qkv_ref[2 * pairs + pair, : step * tile, :])
            outs.append(out / total)
            logs.append(peak + jnp.log(total))
        lse_ref[pair, :, rows] = jnp.where(lane == 0, logs[0], logs[1]).T[0:2, :]
        att_ref[rows, pl.ds(pl.multiple_of(pair * LANES, LANES), LANES)] = jnp.where(
            masks[0], outs[0], outs[1]
        ).astype(bf16)
        between()


def norm_rows(x_ref, norms, perm_ref, hid_ref):
    tile = 256

    @pl.loop(0, x_ref.shape[0] // tile)
    def _(step):
        rows = rows_of(step, tile)
        normed, _ = centre_scale(x_ref[rows, :].astype(f32))
        hidden = (normed * norms[0:1, :] + norms[1:2, :]).astype(bf16)
        hid_ref[rows, :] = mm(hidden, perm_ref[...]).astype(bf16)


def triple_part(part, pairs, hid_ref, w_ref, qkv_ref):
    width = pairs * LANES
    triple = mm(hid_ref[...], w_ref[:, part * width : (part + 1) * width]).astype(bf16)
    for pair in range(pairs):
        qkv_ref[part * pairs + pair] = triple[:, pair * LANES : (pair + 1) * LANES]


def self_forward_kernel(
    pairs, x_ref, norms_ref, perm_ref, w_ref, hid_ref, qkv_ref, att_ref, lse_ref
):
    norm_rows(x_ref, norms_ref, perm_ref, hid_ref)
    for part in range(3):
        triple_part(part, pairs, hid_ref, w_ref, qkv_ref)

    @pl.loop(0, pairs)
    def _(pair):
        pair_forward(pair, pairs, qkv_ref, att_ref, lse_ref, lambda: None)


def self_forward(pairs, x, norms, perm, w):
    length, dim = x.shape
    return pl.pallas_call(
        partial(self_forward_kernel, pairs),
        out_shape=(
            jax.ShapeDtypeStruct((length, dim), bf16),
            jax.ShapeDtypeStruct((3 * pairs, length, LANES), bf16),
            jax.ShapeDtypeStruct((length, pairs * LANES), bf16),
            jax.ShapeDtypeStruct((pairs, 2, length), f32),
        ),
        compiler_params=params(),
        name="self_forward",
    )(x, norms, perm, w)


def pair_backward(pair, pairs, qkv_ref, att_ref, gatt_ref, lse_ref, grad_ref, acc_ref, between):
    length = att_ref.shape[0]
    width = pairs * LANES
    tile = 256
    above = lax.broadcasted_iota(jnp.int32, (tile, tile), 0) <= lax.broadcasted_iota(
        jnp.int32, (tile, tile), 1
    )
    masks = [head_mask(tile, 0), head_mask(tile, 1)]
    lanes = pl.ds(pl.multiple_of(pair * LANES, LANES), LANES)
    for step in range(length // tile):
        rows = slice(step * tile, (step + 1) * tile)
        query = qkv_ref[pair, rows, :] * SCALE
        grad_out = gatt_ref[rows, lanes]
        product = grad_out.astype(f32) * att_ref[rows, lanes].astype(f32)
        queries = [pick(masks[half], query) for half in range(2)]
        grads = [pick(masks[half], grad_out) for half in range(2)]
        deltas = [jnp.sum(pick(masks[half], product).T, axis=0, keepdims=True) for half in range(2)]
        grad_query = [None, None]
        for other in range(step + 1):
            cols = slice(other * tile, (other + 1) * tile)
            keys = qkv_ref[pairs + pair, cols, :]
            values = qkv_ref[2 * pairs + pair, cols, :]
            key_part = value_part = None
            for half in range(2):
                scores = nt(keys, queries[half])
                if other == step:
                    scores = jnp.where(above, scores, masked_score)
                probs = jnp.exp(scores - lse_ref[pair, half : half + 1, rows])
                grad_scores = (probs * (nt(values, grads[half]) - deltas[half])).astype(bf16)
                query_term = tn(grad_scores, keys)
                grad_query[half] = (
                    query_term if grad_query[half] is None else grad_query[half] + query_term
                )
                key_term = mm(grad_scores, queries[half])
                value_term = mm(probs.astype(bf16), grads[half])
                key_part = key_term if key_part is None else key_part + key_term
                value_part = value_term if value_part is None else value_part + value_term
            if other == step:
                acc_ref[0, cols, :] = key_part
                acc_ref[1, cols, :] = value_part
            else:
                acc_ref[0, cols, :] += key_part
                acc_ref[1, cols, :] += value_part
        grad_ref[rows, lanes] = (jnp.where(masks[0], grad_query[0], grad_query[1]) * SCALE).astype(
            bf16
        )
        between()
    for part in range(2):
        lanes_to = pl.ds(pl.multiple_of((part + 1) * width + pair * LANES, LANES), LANES)
        grad_ref[:, lanes_to] = acc_ref[part].astype(bf16)


def self_backward_kernel(
    pairs,
    qkv_ref,
    att_ref,
    gatt_ref,
    lse_ref,
    hid_ref,
    w_ref,
    gw_ref,
    ghid_ref,
    grad_ref,
    acc_ref,
):
    length = att_ref.shape[0]
    width = pairs * LANES
    attention = (qkv_ref, att_ref, gatt_ref, lse_ref, grad_ref, acc_ref)

    @pl.loop(0, pairs)
    def _(pair):
        pair_backward(pair, pairs, *attention, lambda: None)

    hidden_t = hid_ref[...].T
    for part in range(3):
        cols = slice(part * width, (part + 1) * width)
        gw_ref[:, cols] = mm(hidden_t, grad_ref[:, cols]).astype(bf16)
    for begin in range(0, length, 256):
        rows = slice(begin, begin + 256)
        ghid_ref[rows, :] = nt(grad_ref[rows, :], w_ref[...]).astype(bf16)


def self_backward(pairs, qkv, att, gatt, lse, hid, w):
    length, dim = hid.shape
    width = pairs * LANES
    return pl.pallas_call(
        partial(self_backward_kernel, pairs),
        out_shape=(
            jax.ShapeDtypeStruct((dim, 3 * width), bf16),
            jax.ShapeDtypeStruct((length, dim), bf16),
        ),
        scratch_shapes=[
            pltpu.VMEM((length, 3 * width), bf16),
            pltpu.VMEM((2, length, LANES), f32),
        ],
        compiler_params=params(),
        name="self_backward",
    )(qkv, att, gatt, lse, hid, w)


def spread_heads(block, rows, group):
    lane = lax.broadcasted_iota(jnp.int32, block.shape, 1) // HEAD
    return jnp.concatenate([pick(lane == head, block) for head in range(group)], axis=0)


def gather_heads(stacked, rows, group):
    lane = lax.broadcasted_iota(jnp.int32, (rows, stacked.shape[1]), 1) // HEAD
    out = None
    for head in range(group):
        part = pick(lane == head, stacked[head * rows : (head + 1) * rows])
        out = part if out is None else out + part
    return out


def live_keys(presence_ref, span, shape, axis, neighbours, each):
    index = lax.broadcasted_iota(jnp.int32, shape, axis) // each
    live = jnp.zeros(shape, f32)
    anyone = None
    for which in range(neighbours):
        here = presence_ref[span * neighbours + which]
        there = jnp.where(here > 0, 1.0, 0.0).astype(f32)
        live = jnp.where(index == which, there, live)
        anyone = here if anyone is None else jnp.maximum(anyone, here)
    return live, anyone.astype(f32)


def span_forward(span, spans, neighbours, presence_ref, cross_q_ref, near_kv_ref, cross_ref):
    count, dim = cross_q_ref.shape
    span_len = count // spans
    near = near_kv_ref.shape[0] // spans
    group = 256 // HEAD
    rows = rows_of(span, span_len)
    keys = rows_of(span, near)
    live, anyone = live_keys(presence_ref, span, (1, near), 1, neighbours, near // neighbours)
    for begin in range(0, dim, group * HEAD):
        lanes = slice(begin, begin + group * HEAD)
        lanes_v = slice(dim + begin, dim + begin + group * HEAD)
        query = spread_heads(cross_q_ref[rows, lanes] * SCALE, span_len, group)
        scores = jnp.where(live > 0, nt(query, near_kv_ref[keys, lanes]), masked_score)
        peak = jnp.max(scores, axis=-1, keepdims=True)
        expon = jnp.exp(scores - peak) * live
        total = jnp.sum(expon, axis=-1, keepdims=True) + 1.0 - anyone
        out = mm(expon.astype(bf16), near_kv_ref[keys, lanes_v]) / total
        cross_ref[rows, lanes] = gather_heads(out, span_len, group).astype(bf16)


def cross_forward_kernel(
    spans,
    neighbours,
    presence_ref,
    att_ref,
    x_ref,
    norms_ref,
    perm_ref,
    perm_att_ref,
    near_ref,
    w_out_ref,
    w_cq_ref,
    w_ck_ref,
    w_cv_ref,
    w_co_ref,
    att_p_ref,
    first_ref,
    hid_p_ref,
    cross_q_ref,
    near_p_ref,
    near_kv_ref,
    co_p_ref,
    second_ref,
    cross_ref,
):
    count, dim = x_ref.shape
    rows_near = near_ref.shape[0]
    tile = 512

    att_p_ref[...] = mm(att_ref[...], perm_att_ref[...]).astype(bf16)
    first_ref[...] = x_ref[...].astype(f32) + mm(att_p_ref[...], w_out_ref[...])

    normed, _ = centre_scale(first_ref[...])
    hidden = (normed * norms_ref[2:3, :] + norms_ref[3:4, :]).astype(bf16)
    hid_p_ref[...] = mm(hidden, perm_ref[...]).astype(bf16)
    cross_q_ref[...] = mm(hid_p_ref[...], w_cq_ref[...]).astype(bf16)

    @pl.loop(0, rows_near // tile)
    def _(step):
        rows = rows_of(step, tile)
        near_p_ref[rows, :] = mm(near_ref[rows, :], perm_ref[...]).astype(bf16)
        near_kv_ref[rows, :dim] = mm(near_p_ref[rows, :], w_ck_ref[...]).astype(bf16)
        near_kv_ref[rows, dim:] = mm(near_p_ref[rows, :], w_cv_ref[...]).astype(bf16)

    @pl.loop(0, spans)
    def _(span):
        span_forward(span, spans, neighbours, presence_ref, cross_q_ref, near_kv_ref, cross_ref)

    co_p_ref[...] = mm(cross_ref[...], perm_ref[...]).astype(bf16)
    second_ref[...] = first_ref[...] + mm(co_p_ref[...], w_co_ref[...])


def column_block(rows, width, index):
    return pl.BlockSpec((rows, width), lambda *_: (0, index), pipeline_mode=pl.Buffered(1))


def whole(array):
    return pl.BlockSpec(array.shape, lambda *_: (0,) * array.ndim, pipeline_mode=pl.Buffered(1))


def whole_shape(shape):
    return pl.BlockSpec(shape, lambda *_: (0,) * len(shape), pipeline_mode=pl.Buffered(1))


def cross_forward(spans, neighbours, presence, att, x, norms, perm, perm_att, near, weights):
    count, dim = x.shape
    rows_near = near.shape[0]
    out_shape = (
        jax.ShapeDtypeStruct((count, dim), bf16),
        jax.ShapeDtypeStruct((count, dim), f32),
        jax.ShapeDtypeStruct((count, dim), bf16),
        jax.ShapeDtypeStruct((count, dim), bf16),
        jax.ShapeDtypeStruct((rows_near, dim), bf16),
        jax.ShapeDtypeStruct((rows_near, 2 * dim), bf16),
        jax.ShapeDtypeStruct((count, dim), bf16),
        jax.ShapeDtypeStruct((count, dim), f32),
    )
    operands = (att, x, norms, perm, perm_att, near)
    return pl.pallas_call(
        partial(cross_forward_kernel, spans, neighbours),
        out_shape=out_shape,
        grid=(1,),
        in_specs=[pl.BlockSpec(memory_space=pltpu.SMEM)]
        + [whole(op) for op in operands]
        + [column_block(dim, dim, index) for index in (3, 4, 5, 6, 7)],
        out_specs=tuple(whole_shape(shape.shape) for shape in out_shape),
        scratch_shapes=[pltpu.VMEM((count, dim), bf16)],
        compiler_params=params(),
        name="cross_forward",
    )(presence, *operands, *([weights] * 5))


def feed_kernel(
    second_ref,
    cot_ref,
    norms_ref,
    perm_ref,
    w_up_ref,
    w_down_ref,
    out_ref,
    gsecond_ref,
    all_ref,
    gnorm_ref,
    hid_p_ref,
    hid_t_ref,
    cot_p_ref,
    cot_t_ref,
    result_ref,
    back_ref,
    gup_ref,
    gdown_ref,
    sems,
):
    step = pl.program_id(0)
    last = pl.num_programs(0) - 1
    slot = lax.rem(step, 2)
    dim, tile = w_up_ref.shape

    def copies(step, slot):
        up = pl.multiple_of(8 * dim + step * tile, tile)
        down = pl.multiple_of(8 * dim + (last + 1 + step) * tile, tile)
        return (
            pltpu.make_async_copy(gup_ref.at[slot], all_ref.at[:, pl.ds(up, tile)], sems.at[0, slot]),
            pltpu.make_async_copy(
                gdown_ref.at[slot], all_ref.at[:, pl.ds(down, tile)], sems.at[1, slot]
            ),
        )

    @pl.when(step >= 2)
    def _():
        for copy in copies(step - 2, slot):
            copy.wait()

    @pl.when(step == 0)
    def _():
        normed, _ = centre_scale(second_ref[...])
        hidden = (normed * norms_ref[4:5, :] + norms_ref[5:6, :]).astype(bf16)
        hid_p_ref[...] = mm(hidden, perm_ref[...]).astype(bf16)
        hid_t_ref[...] = hid_p_ref[...].T
        cot_p_ref[...] = mm(cot_ref[...], perm_ref[...]).astype(bf16)
        cot_t_ref[...] = cot_p_ref[...].T
        result_ref[...] = jnp.zeros_like(result_ref)
        back_ref[...] = jnp.zeros_like(back_ref)

    upward = mm(hid_p_ref[...], w_up_ref[...])
    active, slope = gelu_parts(upward)
    active = active.astype(bf16)
    result_ref[...] += nt(active, w_down_ref[...])
    gdown_ref[slot] = mm(cot_t_ref[...], active).astype(bf16)
    grad_up = (mm(cot_p_ref[...], w_down_ref[...]) * slope).astype(bf16)
    gup_ref[slot] = mm(hid_t_ref[...], grad_up).astype(bf16)
    for copy in copies(step, slot):
        copy.start()
    back_ref[...] += nt(grad_up, w_up_ref[...])

    @pl.when(step == last)
    def _():
        out_ref[...] = (
            second_ref[...] + nt(result_ref[...].astype(bf16), perm_ref[...])
        ).astype(bf16)
        upstream = nt(back_ref[...].astype(bf16), perm_ref[...])
        normed, recip = centre_scale(second_ref[...])
        back, gain, shift = norm_back(upstream, normed, recip, norms_ref[4:5, :])
        gsecond_ref[...] = cot_ref[...].astype(f32) + back
        gnorm_ref[0:1, :] = gain
        gnorm_ref[1:2, :] = shift
        for which in (step - 1, step):
            for copy in copies(which, lax.rem(which, 2)):
                copy.wait()


def feed(second, cot, norms, perm, weights):
    count, dim = second.shape
    ffw = (weights.shape[1] - 8 * dim) // 2
    tile = 512
    first_up = 8 * dim // tile
    first_down = (8 * dim + ffw) // tile
    out_shape = (
        jax.ShapeDtypeStruct((count, dim), bf16),
        jax.ShapeDtypeStruct((count, dim), f32),
        jax.ShapeDtypeStruct(weights.shape, bf16),
        jax.ShapeDtypeStruct((2, dim), f32),
    )
    operands = (second, cot, norms, perm)
    return pl.pallas_call(
        feed_kernel,
        out_shape=out_shape,
        grid=(ffw // tile,),
        in_specs=[whole(op) for op in operands]
        + [
            pl.BlockSpec((dim, tile), lambda i: (0, first_up + i)),
            pl.BlockSpec((dim, tile), lambda i: (0, first_down + i)),
        ],
        out_specs=(
            whole_shape((count, dim)),
            whole_shape((count, dim)),
            pl.BlockSpec(memory_space=pl.ANY),
            whole_shape((2, dim)),
        ),
        scratch_shapes=[
            pltpu.VMEM((count, dim), bf16),
            pltpu.VMEM((dim, count), bf16),
            pltpu.VMEM((count, dim), bf16),
            pltpu.VMEM((dim, count), bf16),
            pltpu.VMEM((count, dim), f32),
            pltpu.VMEM((count, dim), f32),
            pltpu.VMEM((2, dim, tile), bf16),
            pltpu.VMEM((2, dim, tile), bf16),
            pltpu.SemaphoreType.DMA((2, 2)),
        ],
        compiler_params=params(),
        name="feed",
    )(*operands, weights, weights)


def span_backward(
    span, spans, neighbours, presence_ref, cross_q_ref, gco_ref, near_kv_ref, gcq_ref, gnear_ref
):
    count, dim = cross_q_ref.shape
    span_len = count // spans
    near = near_kv_ref.shape[0] // spans
    group = 256 // HEAD
    rows = rows_of(span, span_len)
    keys = rows_of(span, near)
    live, anyone = live_keys(presence_ref, span, (near, 1), 0, neighbours, near // neighbours)
    for begin in range(0, dim, group * HEAD):
        lanes = slice(begin, begin + group * HEAD)
        lanes_v = slice(dim + begin, dim + begin + group * HEAD)
        query = spread_heads(cross_q_ref[rows, lanes] * SCALE, span_len, group)
        grad_out = spread_heads(gco_ref[rows, lanes], span_len, group)
        key = near_kv_ref[keys, lanes]
        scores = jnp.where(live > 0, nt(key, query), masked_score)
        peak = jnp.max(scores, axis=0, keepdims=True)
        expon = jnp.exp(scores - peak) * live
        total = jnp.sum(expon, axis=0, keepdims=True) + 1.0 - anyone
        probs = expon * (1.0 / total)
        grad_probs = nt(near_kv_ref[keys, lanes_v], grad_out)
        inner = jnp.sum(probs * grad_probs, axis=0, keepdims=True)
        grad_scores = (probs * (grad_probs - inner)).astype(bf16)
        gcq_ref[rows, lanes] = (
            gather_heads(tn(grad_scores, key), span_len, group) * SCALE
        ).astype(bf16)
        gnear_ref[keys, lanes] = mm(grad_scores, query).astype(bf16)
        gnear_ref[keys, lanes_v] = mm(probs.astype(bf16), grad_out).astype(bf16)


def cross_backward_kernel(
    spans,
    neighbours,
    presence_ref,
    gsecond_ref,
    first_ref,
    norms_ref,
    perm_ref,
    perm_att_ref,
    att_p_ref,
    hid_p_ref,
    cross_q_ref,
    near_p_ref,
    near_kv_ref,
    co_p_ref,
    w_out_ref,
    w_cq_ref,
    w_co_ref,
    _,
    gfirst_ref,
    gatt_ref,
    all_ref,
    gnorm_ref,
    gco_ref,
    gcq_ref,
    gnear_ref,
    gw_ref,
    sems,
):
    dim = first_ref.shape[1]
    outs = []

    def keep(index, value):
        gw_ref[index] = value.astype(bf16)
        outs.append(
            pltpu.make_async_copy(
                gw_ref.at[index], all_ref.at[:, pl.ds((3 + index) * dim, dim)], sems.at[index]
            )
        )
        outs[-1].start()

    upper = gsecond_ref[...].astype(bf16)
    gco_ref[...] = nt(nt(upper, w_co_ref[...]).astype(bf16), perm_ref[...]).astype(bf16)
    tables = (presence_ref, cross_q_ref, gco_ref, near_kv_ref, gcq_ref, gnear_ref)
    pl.loop(0, spans)(lambda span: span_backward(span, spans, neighbours, *tables))
    upstream = nt(nt(gcq_ref[...], w_cq_ref[...]).astype(bf16), perm_ref[...])
    normed, recip = centre_scale(first_ref[...])
    back, gain, shift = norm_back(upstream, normed, recip, norms_ref[2:3, :])
    gnorm_ref[0:1, :] = gain
    gnorm_ref[1:2, :] = shift
    gfirst_ref[...] = gsecond_ref[...] + back
    lower = gfirst_ref[...].astype(bf16)
    gatt_ref[...] = nt(nt(lower, w_out_ref[...]).astype(bf16), perm_att_ref[...]).astype(bf16)
    keep(4, mm(co_p_ref[...].T, upper))
    near_t = near_p_ref[...].T
    for part in range(2):
        keep(2 + part, mm(near_t, gnear_ref[:, part * dim : (part + 1) * dim]))
    keep(1, mm(hid_p_ref[...].T, gcq_ref[...]))
    keep(0, mm(att_p_ref[...].T, lower))
    for copy in outs:
        copy.wait()


def cross_backward(
    spans,
    neighbours,
    presence,
    gsecond,
    first,
    norms,
    perm,
    perm_att,
    att_p,
    hid_p,
    cross_q,
    near_p,
    near_kv,
    co_p,
    weights,
    grads,
):
    count, dim = first.shape
    rows_near = near_p.shape[0]
    out_shape = [
        jax.ShapeDtypeStruct((count, dim), f32),
        jax.ShapeDtypeStruct((count, perm_att.shape[0]), bf16),
        jax.ShapeDtypeStruct(grads.shape, bf16),
        jax.ShapeDtypeStruct((2, dim), f32),
    ]
    scratch = [
        pltpu.VMEM((count, dim), bf16),
        pltpu.VMEM((count, dim), bf16),
        pltpu.VMEM((rows_near, 2 * dim), bf16),
        pltpu.VMEM((5, dim, dim), bf16),
        pltpu.SemaphoreType.DMA((5,)),
    ]
    operands = (
        gsecond,
        first,
        norms,
        perm,
        perm_att,
        att_p,
        hid_p,
        cross_q,
        near_p,
        near_kv,
        co_p,
    )
    return pl.pallas_call(
        partial(cross_backward_kernel, spans, neighbours),
        out_shape=out_shape,
        grid=(1,),
        in_specs=[pl.BlockSpec(memory_space=pltpu.SMEM)]
        + [whole(op) for op in operands]
        + [column_block(dim, dim, index) for index in (3, 4, 7)]
        + [pl.BlockSpec(memory_space=pl.ANY)],
        out_specs=tuple(
            pl.BlockSpec(memory_space=pl.ANY) if index == 2 else whole_shape(shape.shape)
            for index, shape in enumerate(out_shape)
        ),
        scratch_shapes=scratch,
        input_output_aliases={len(operands) + 4: 2},
        compiler_params=params(),
        name="cross_backward",
    )(presence, *operands, *([weights] * 3), grads)


def last_norm_kernel(parts_ref, x_ref, gfirst_ref, norms_ref, perm_ref, out_ref, gnorm_ref):
    total = parts_ref[0].astype(f32)
    for part in range(1, parts_ref.shape[0]):
        total = total + parts_ref[part].astype(f32)
    upstream = nt(total.astype(bf16), perm_ref[...])
    normed, recip = centre_scale(x_ref[...].astype(f32))
    back, gain, shift = norm_back(upstream, normed, recip, norms_ref[0:1, :])
    out_ref[...] = gfirst_ref[...] + back
    gnorm_ref[0:1, :] = gain
    gnorm_ref[1:2, :] = shift


def last_norm(parts, x, gfirst, norms, perm):
    count, dim = x.shape
    return pl.pallas_call(
        last_norm_kernel,
        out_shape=(
            jax.ShapeDtypeStruct((count, dim), f32),
            jax.ShapeDtypeStruct((2, dim), f32),
        ),
        compiler_params=params(),
        name="last_norm",
    )(parts, x, gfirst, norms, perm)


def layer_kernel(
    lines,
    pairs,
    spans,
    neighbours,
    presence_ref,
    w_ref,
    norm_ref,
    x_ref,
    order_ref,
    cot_ref,
    near_ref,
    wts_ref,
    all_ref,
    out_ref,
    gin_ref,
    sums_ref,
    hid_ref,
    qkv_ref,
    att_ref,
    lse_ref,
    att_p_ref,
    first_ref,
    hid_p_ref,
    cross_q_ref,
    near_p_ref,
    near_kv_ref,
    co_p_ref,
    second_ref,
    own_ref,
    small_ref,
    rows_ref,
    w_qkv_ref,
    w_mid_ref,
    att_tok_ref,
    cross_ref,
    up_p_ref,
    up_t_ref,
    cot_p_ref,
    cot_t_ref,
    result_ref,
    back_ref,
    gfeed_ref,
    perm_ref,
    norms_ref,
    gatt_ref,
    acc_ref,
    gsib_ref,
    parts_ref,
    send_sems,
    z_sems,
    y_sems,
    x_sems,
    a_sems,
    b_sems,
    sib_sems,
    norm_sems,
    row_sems,
    att_sems,
    local_sems,
    qkv_sems,
    mid_sems,
    feed_sems,
    gatt_sems,
    gsib_sems,
    part_sems,
):
    place = Place(lines)
    z, me, core = place.z, place.me, place.core
    length, dim = hid_ref.shape
    width = pairs * LANES
    tokens = length // 8
    half = own_ref.shape[0] // 2
    near_load = pltpu.make_async_copy(near_ref, near_p_ref, local_sems.at[2])
    near_load.start()
    own_ref[...] = w_ref[...].astype(bf16)
    place.meet()
    send = Sender(place, send_sems)
    unit = partial(unit_of, wts_ref, lines)
    events = place.events()
    keep = pltpu.make_async_copy(own_ref, unit(z, me), local_sems.at[0])
    keep.start()

    def build_perm():
        row = lax.broadcasted_iota(jnp.int32, (dim, dim), 0)
        perm_ref[...] = jnp.where(row == order_ref[0:1, :], 1.0, 0.0).astype(bf16)

    def obtain(index):
        condition, line, far, side = events[index]
        mine = unit(line, me)
        src = own_ref if far == 0 else mine
        if far:
            send.arrived(condition, mine, z_sems.at[line])
        if side >= 0:
            send.start(both(condition, z > 0), src, mine, z_sems.at[line], z=z - 1)
        if side <= 0:
            send.start(both(condition, z < lines - 1), src, mine, z_sems.at[line], z=z + 1)
        send.start(condition, src, mine, x_sems.at[line], seq=place.xn)
        send.start(condition, src, mine, y_sems.at[line], seq=place.yn)
        send.start(condition, src, mine, sib_sems.at[0, line], seq=place.sib)

    def pass_on(index):
        condition, line, _, _ = events[index]
        from_x, from_y = unit(line, place.xn), unit(line, place.yn)
        send.arrived(condition, from_x, x_sems.at[line])
        part = unit(line, place.xn, half, half)
        send.start(condition, part, part, b_sems.at[line], seq=place.yn)
        send.start(condition, from_x, from_x, sib_sems.at[1, line], seq=place.sib)
        send.arrived(condition, from_y, y_sems.at[line])
        part = unit(line, place.yn, 0, half)
        send.start(condition, part, part, a_sems.at[line], seq=place.xn)
        send.start(condition, from_y, from_y, sib_sems.at[2, line], seq=place.sib)

    def corner(index):
        condition, line, _, _ = events[index]
        for group, begin, sems in ((3, 0, a_sems), (4, half, b_sems)):
            part = unit(line, place.dg, begin, half)
            send.arrived(condition, part, sems.at[line])
            send.start(condition, part, part, sib_sems.at[group, line], seq=place.sib)

    def row_block(seq):
        return rows_ref.at[pl.ds(pl.multiple_of(seq * tokens, tokens), tokens)]

    def middle(index):
        return pltpu.make_async_copy(
            wts_ref.at[:, pl.ds((3 + index) * dim, dim)], w_mid_ref.at[index], mid_sems.at[index]
        )

    obtain(0)
    own_rows = pltpu.make_async_copy(x_ref.at[place.chip], row_block(me), local_sems.at[1])
    own_rows.start()
    others = (place.xn, place.yn, place.dg)
    for other in place.line():
        send.start(None, norm_ref, small_ref.at[z], norm_sems.at[z], z=other)
    small_ref[z] = norm_ref[...]
    send.start(None, x_ref.at[place.chip], row_block(me), row_sems.at[me], seq=place.sib)
    for other in others:
        send.start(None, x_ref.at[other // 2], row_block(me), row_sems.at[me], seq=other)
    build_perm()
    near_load.wait()

    @pl.loop(0, near_p_ref.shape[0] // 512)
    def _(step):
        rows = rows_of(step, 512)
        near_p_ref[rows, :] = mm(near_p_ref[rows, :], perm_ref[...]).astype(bf16)

    obtain(1)
    obtain(2)
    pass_on(0)
    for other in others:
        send.arrived(None, row_block(other), row_sems.at[other])
        send.start(None, row_block(other), row_block(other), row_sems.at[other], seq=place.sib)
    obtain(3)
    obtain(4)
    cot_p_ref[...] = mm(cot_ref[...], perm_ref[...]).astype(bf16)
    cot_t_ref[...] = cot_p_ref[...].T
    pass_on(1)
    pass_on(2)
    corner(0)

    for other in place.line():
        send.arrived(None, small_ref.at[other], norm_sems.at[other])
    piece = small_ref.shape[2]
    total = None
    for line in range(lines):
        row = lax.broadcasted_iota(jnp.int32, (piece, dim), 0)
        column = lax.broadcasted_iota(jnp.int32, (piece, dim), 1)
        part = dim // lines
        place_of = jnp.logical_and(row < part, column == row + line * part).astype(bf16)
        term = mm(small_ref[line], place_of)
        total = term if total is None else total + term
    norms_ref[...] = total[: norms_ref.shape[0]]

    last = len(events)
    for index in range(5, last, 2):
        obtain(index)
        obtain(index + 1)
        if index == 5:
            for other in others:
                theirs = other + 1 - 2 * core
                send.arrived(None, row_block(theirs), row_sems.at[theirs])
            send.arrived(None, row_block(place.sib), row_sems.at[place.sib])
            own_rows.wait()
            norm_rows(rows_ref, norms_ref[...], perm_ref, hid_ref)
        pass_on(index - 2)
        pass_on(index - 1)
        corner(index - 4)
        corner(index - 3)
    for index in range(last - 2, last):
        pass_on(index)
    for index in range(last - 4, last):
        corner(index)
    keep.wait()
    for line in range(lines):
        for group, first in enumerate((me, place.xn, place.yn)):
            theirs = first + 1 - 2 * core
            send.arrived(None, unit(line, theirs), sib_sems.at[group, line])
        theirs = place.dg + 1 - 2 * core
        send.arrived(None, unit(line, theirs, 0, half), sib_sems.at[3, line])
        send.arrived(None, unit(line, theirs, half, half), sib_sems.at[4, line])
    copies = weight_copies(pairs, dim, wts_ref, w_qkv_ref, qkv_sems)
    for copy in copies + [middle(index) for index in (2, 3, 0, 1, 4)]:
        copy.start()
    for part in range(3):
        copies[part].wait()
        triple_part(part, pairs, hid_ref, w_qkv_ref, qkv_ref)

    share = lax.rem(me, dim // width)
    seq_rows = pl.ds(pl.multiple_of(place.chip * tokens, tokens), tokens)

    def landing(pair, chip_rows, share):
        lanes = pl.ds(pl.multiple_of(share * width + pair * LANES, LANES), LANES)
        return att_tok_ref.at[chip_rows, lanes]

    for pair in range(pairs):
        lanes = slice(pair * LANES, (pair + 1) * LANES)
        pair_forward(pair, pairs, qkv_ref, att_ref, lse_ref, lambda: None)
        for other in place.plane():
            block = att_ref.at[pl.ds(pl.multiple_of(other * tokens, tokens), tokens), lanes]
            to = landing(pair, seq_rows, share)
            send.start(None, block, to, att_sems.at[pair, me], seq=other)
        own_block = att_ref[pl.ds(pl.multiple_of(me * tokens, tokens), tokens), lanes]
        landing(pair, seq_rows, share)[...] = own_block

    for index in (2, 3, 0, 1, 4):
        middle(index).wait()
    for step in range(near_p_ref.shape[0] // 512):
        rows = slice(step * 512, (step + 1) * 512)
        near_kv_ref[rows, :dim] = mm(near_p_ref[rows, :], w_mid_ref[2]).astype(bf16)
        near_kv_ref[rows, dim:] = mm(near_p_ref[rows, :], w_mid_ref[3]).astype(bf16)
    w_out_ref, w_cq_ref, w_co_ref = (w_mid_ref.at[index] for index in (0, 1, 4))
    for pair in range(pairs):
        for other in place.plane():
            rows = pl.ds(pl.multiple_of(other // 2 * tokens, tokens), tokens)
            send.arrived(None, landing(pair, rows, lax.rem(other, 2)), att_sems.at[pair, other])
    att_p_ref[...] = mm(att_tok_ref[...], perm_ref[...]).astype(bf16)
    own_x = x_ref[...].reshape(first_ref.shape).astype(f32)
    first_ref[...] = own_x + mm(att_p_ref[...], w_out_ref[...])
    normed, _ = centre_scale(first_ref[...])
    hidden = (normed * norms_ref[2:3, :] + norms_ref[3:4, :]).astype(bf16)
    hid_p_ref[...] = mm(hidden, perm_ref[...]).astype(bf16)
    cross_q_ref[...] = mm(hid_p_ref[...], w_cq_ref[...]).astype(bf16)
    pl.loop(0, spans)(
        lambda span: span_forward(
            span, spans, neighbours, presence_ref, cross_q_ref, near_kv_ref, cross_ref
        )
    )

    ffw = (all_ref.shape[1] - 8 * dim) // 2
    tile = gfeed_ref.shape[2]
    order = range(0, ffw, tile)

    def tile_load(index):
        return [
            pltpu.make_async_copy(
                wts_ref.at[:, pl.ds(8 * dim + part * ffw + order[index], tile)],
                w_mid_ref.at[(2 * index + part) % 4],
                feed_sems.at[0, (2 * index + part) % 4],
            )
            for part in range(2)
        ]

    def tile_store(index):
        return [
            pltpu.make_async_copy(
                gfeed_ref.at[(2 * index + part) % 4],
                all_ref.at[:, pl.ds(8 * dim + part * ffw + order[index], tile)],
                feed_sems.at[1, (2 * index + part) % 4],
            )
            for part in range(2)
        ]

    for copy in tile_load(0) + tile_load(1):
        copy.start()
    co_p_ref[...] = mm(cross_ref[...], perm_ref[...]).astype(bf16)
    second_ref[...] = first_ref[...] + mm(co_p_ref[...], w_co_ref[...])
    normed, _ = centre_scale(second_ref[...])
    hidden = (normed * norms_ref[4:5, :] + norms_ref[5:6, :]).astype(bf16)
    up_p_ref[...] = mm(hidden, perm_ref[...]).astype(bf16)
    up_t_ref[...] = up_p_ref[...].T

    for index in range(len(order)):
        up_ref, down_ref = w_mid_ref.at[2 * index % 4], w_mid_ref.at[2 * index % 4 + 1]
        for copy in tile_load(index):
            copy.wait()
        if index >= 2:
            for copy in tile_store(index - 2):
                copy.wait()
        active, slope = gelu_parts(mm(up_p_ref[...], up_ref[...]))
        active = active.astype(bf16)
        term = nt(active, down_ref[...])
        result_ref[...] = term if index == 0 else result_ref[...] + term
        gfeed_ref[2 * index % 4 + 1] = mm(cot_t_ref[...], active).astype(bf16)
        grad_up = (mm(cot_p_ref[...], down_ref[...]) * slope).astype(bf16)
        gfeed_ref[2 * index % 4] = mm(up_t_ref[...], grad_up).astype(bf16)
        for copy in tile_store(index):
            copy.start()
        term = nt(grad_up, up_ref[...])
        back_ref[...] = term if index == 0 else back_ref[...] + term
        if index + 2 < len(order):
            for copy in tile_load(index + 2):
                copy.start()
        elif index + 2 == len(order):
            middle(0).start()
            middle(1).start()

    out_ref[...] = (second_ref[...] + nt(result_ref[...].astype(bf16), perm_ref[...])).astype(bf16)
    upstream = nt(back_ref[...].astype(bf16), perm_ref[...])
    normed, recip = centre_scale(second_ref[...])
    back, gain, shift = norm_back(upstream, normed, recip, norms_ref[4:5, :])
    gsecond_ref = second_ref
    gsecond_ref[...] = cot_ref[...].astype(f32) + back
    sums_ref[4:5, :] = gain
    sums_ref[5:6, :] = shift
    sums_ref[6:8, :] = jnp.zeros((2, dim), f32)
    for index in range(len(order) - 2, len(order)):
        for copy in tile_store(index):
            copy.wait()

    gco_ref, gcq_ref, gatt_tok_ref = up_p_ref, cot_p_ref, cross_ref
    outs = []

    def store(slot, part, first):
        copy = pltpu.make_async_copy(
            part, all_ref.at[:, pl.ds(first, part.shape[1])], feed_sems.at[1, slot]
        )
        outs.append(copy)
        copy.start()

    def keep_grad(index, value):
        slot = len(outs) % 4
        if len(outs) >= 4:
            outs[-4].wait()
        gfeed_ref[slot] = value.astype(bf16)
        store(slot, gfeed_ref.at[slot], (3 + index) * dim)

    upper = gsecond_ref[...].astype(bf16)
    gco_ref[...] = nt(nt(upper, w_co_ref[...]).astype(bf16), perm_ref[...]).astype(bf16)
    tables = (presence_ref, cross_q_ref, gco_ref, near_kv_ref, gcq_ref, near_kv_ref)
    pl.loop(0, spans)(lambda span: span_backward(span, spans, neighbours, *tables))
    for index in (0, 1):
        middle(index).wait()
    upstream = nt(nt(gcq_ref[...], w_cq_ref[...]).astype(bf16), perm_ref[...])
    normed, recip = centre_scale(first_ref[...])
    back, gain, shift = norm_back(upstream, normed, recip, norms_ref[2:3, :])
    sums_ref[2:3, :] = gain
    sums_ref[3:4, :] = shift
    gfirst_ref = gsecond_ref
    gfirst_ref[...] = gsecond_ref[...] + back
    lower = gfirst_ref[...].astype(bf16)
    gatt_tok_ref[...] = nt(nt(lower, w_out_ref[...]).astype(bf16), perm_ref[...]).astype(bf16)

    def gatt_block(device):
        return gatt_tok_ref.at[
            pl.ds(pl.multiple_of(device // 2 * tokens, tokens), tokens),
            pl.ds(pl.multiple_of(lax.rem(device, 2) * width, width), width),
        ]

    def gatt_rows(device):
        return gatt_ref.at[pl.ds(pl.multiple_of(device * tokens, tokens), tokens)]

    for other in place.plane():
        send.start(None, gatt_block(other), gatt_rows(me), gatt_sems.at[me], seq=other)
    own_gatt = pltpu.make_async_copy(gatt_block(me), gatt_rows(me), gatt_sems.at[me])
    own_gatt.start()
    keep_grad(4, mm(co_p_ref[...].T, upper))
    near_t = near_p_ref[...].T
    for part in range(2):
        keep_grad(2 + part, mm(near_t, near_kv_ref[:, part * dim : (part + 1) * dim]))
    keep_grad(1, mm(hid_p_ref[...].T, gcq_ref[...]))
    keep_grad(0, mm(att_p_ref[...].T, lower))
    for other in place.plane():
        send.arrived(None, gatt_rows(other), gatt_sems.at[other])
    own_gatt.wait()

    send.finish()
    grad_ref = near_kv_ref.at[pl.ds(0, length), pl.ds(0, 3 * width)]
    ghid_ref = rows_ref
    attention = (qkv_ref, att_ref, gatt_ref, lse_ref, grad_ref, acc_ref)
    pl.loop(0, pairs)(lambda pair: pair_backward(pair, pairs, *attention, lambda: None))
    for begin in range(0, length, 256):
        rows = slice(begin, begin + 256)
        ghid_ref[rows, :] = nt(grad_ref[rows, :], w_qkv_ref[...]).astype(bf16)
    chips = (place.xn // 2, place.yn // 2, place.dg // 2, place.chip)

    def token_rows(device):
        return pl.ds(pl.multiple_of(device * tokens, tokens), tokens)

    for chip in chips:
        theirs = ghid_ref.at[token_rows(chip * 2 + 1 - core)]
        send.start(None, theirs, gsib_ref.at[chip], gsib_sems.at[chip], seq=place.sib)

    for copy in outs[-4:]:
        copy.wait()
    outs.clear()
    gfeed_ref[3] = jnp.zeros_like(gfeed_ref[3])
    share_count = dim // width
    zeros = [
        pltpu.make_async_copy(
            gfeed_ref.at[3, :, pl.ds(0, width)],
            all_ref.at[
                :,
                pl.ds(
                    pl.multiple_of(part * dim + lax.rem(share + other, share_count) * width, LANES),
                    width,
                ),
            ],
            mid_sems.at[2 + part],
        )
        for part in range(3)
        for other in range(1, share_count)
    ]
    for copy in zeros:
        copy.start()
    hidden_t = hid_ref[...].T

    def triple_grad(part):
        columns = slice(part * width, (part + 1) * width)
        gfeed_ref[part, :, :width] = mm(hidden_t, grad_ref[:, columns]).astype(bf16)
        first = pl.multiple_of(part * dim + share * width, LANES)
        store(part, gfeed_ref.at[part, :, pl.ds(0, width)], first)

    triple_grad(0)
    triple_grad(1)
    for chip in chips:
        send.arrived(None, gsib_ref.at[chip], gsib_sems.at[chip])
        rows = token_rows(chip * 2 + core)
        total = (ghid_ref[rows, :].astype(f32) + gsib_ref[chip].astype(f32)).astype(bf16)
        if chip is place.chip:
            parts_ref[chip] = total
        else:
            ghid_ref[rows, :] = total
            landed, sem = parts_ref.at[place.chip], part_sems.at[place.chip]
            send.start(None, ghid_ref.at[rows], landed, sem, seq=chip * 2 + core)
    triple_grad(2)
    for chip in chips[:3]:
        send.arrived(None, parts_ref.at[chip], part_sems.at[chip])
    gain_sum = shift_sum = None
    for chip in range(4):
        rows = slice(chip * tokens, (chip + 1) * tokens)
        upstream = nt(parts_ref[chip], perm_ref[...])
        normed, recip = centre_scale(x_ref[chip].astype(f32))
        back, gain, shift = norm_back(upstream, normed, recip, norms_ref[0:1, :])
        gfirst_ref[rows, :] += back
        gain_sum = gain if gain_sum is None else gain_sum + gain
        shift_sum = shift if shift_sum is None else shift_sum + shift
    leave = pltpu.make_async_copy(gfirst_ref, gin_ref, local_sems.at[0])
    leave.start()
    sums_ref[0:1, :] = gain_sum
    sums_ref[1:2, :] = shift_sum
    for copy in outs + zeros:
        copy.wait()
    leave.wait()
    send.finish()


def layer(lines, pairs, spans, neighbours, presence, w_shard, n_shard, inputs, order, cot, near):
    unit_rows, unit_cols = w_shard.shape
    seqs, tokens, dim = inputs.shape
    count, length, width = seqs * tokens, 8 * tokens, pairs * LANES
    rows_near = near.shape[0]
    events = 2 * lines - 1
    any_space = pl.BlockSpec(memory_space=pl.ANY)
    vmem = pl.BlockSpec(memory_space=pltpu.VMEM)
    dma = pltpu.SemaphoreType.DMA
    packed = jax.ShapeDtypeStruct((unit_rows * lines, unit_cols * 8), bf16)
    tile = unit_cols // 2
    tokens_rows = (count, dim)
    scratch = [
        ((length, dim), bf16),
        ((3 * pairs, length, LANES), bf16),
        ((length, width), bf16),
        ((pairs, 2, length), f32),
        (tokens_rows, bf16),
        (tokens_rows, f32),
        (tokens_rows, bf16),
        (tokens_rows, bf16),
        ((rows_near, dim), bf16),
        ((rows_near, 2 * dim), bf16),
        (tokens_rows, bf16),
        (tokens_rows, f32),
        ((unit_rows, unit_cols), bf16),
        ((lines,) + n_shard.shape, bf16),
        ((length, dim), bf16),
        ((dim, 3 * width), bf16),
        ((5, dim, dim), bf16),
        (tokens_rows, bf16),
        (tokens_rows, bf16),
        (tokens_rows, bf16),
        ((dim, count), bf16),
        (tokens_rows, bf16),
        ((dim, count), bf16),
        (tokens_rows, f32),
        (tokens_rows, f32),
        ((4, dim, tile), bf16),
        ((dim, dim), bf16),
        ((8, dim), f32),
        ((length, width), bf16),
        ((2, length, LANES), f32),
        ((4, tokens, dim), bf16),
        ((4, tokens, dim), bf16),
    ]
    return pl.pallas_call(
        partial(layer_kernel, lines, pairs, spans, neighbours),
        out_shape=(
            packed,
            packed,
            jax.ShapeDtypeStruct(tokens_rows, bf16),
            jax.ShapeDtypeStruct(tokens_rows, f32),
            jax.ShapeDtypeStruct((8, dim), f32),
        ),
        in_specs=[pl.BlockSpec(memory_space=pltpu.SMEM)] + [vmem] * 5 + [any_space],
        out_specs=(any_space, any_space, vmem, any_space, vmem),
        scratch_shapes=[pltpu.VMEM(*entry) for entry in scratch]
        + [
            dma((11 * events + 7 + lines + 7 * pairs + 16,)),
            dma((lines,)),
            dma((lines,)),
            dma((lines,)),
            dma((lines,)),
            dma((lines,)),
            dma((5, lines)),
            dma((lines,)),
            dma((8,)),
            dma((pairs, 8)),
            dma((3,)),
            dma((3,)),
            dma((5,)),
            dma((2, 4)),
            dma((8,)),
            dma((4,)),
            dma((4,)),
        ],
        compiler_params=pltpu.CompilerParams(
            vmem_limit_bytes=VMEM_BYTES, collective_id=1, has_side_effects=True
        ),
        name="layer",
    )(presence, w_shard, n_shard, inputs, order, cot, near)


def reduce_kernel(
    lines,
    grads_ref,
    small_ref,
    shard_ref,
    norms_ref,
    mine_ref,
    sib_ref,
    corner_a_ref,
    corner_b_ref,
    from_x_ref,
    from_y_ref,
    below_ref,
    above_ref,
    plane_ref,
    plane_sum_ref,
    line_ref,
    send_sems,
    load_sems,
    sib_sems,
    a_sems,
    b_sems,
    x_sems,
    y_sems,
    below_sems,
    above_sems,
    plane_sems,
    line_sems,
):
    place = Place(lines)
    z, me = place.z, place.me
    unit_rows, unit_cols = shard_ref.shape
    half = unit_rows // 2
    tile = 32
    place.meet()
    send = Sender(place, send_sems)
    chips = (place.dg, place.yn, place.xn, me)
    corner, over_y, over_x, here = range(4)

    unit = partial(unit_of, grads_ref, lines)

    def load(which, line):
        return pltpu.make_async_copy(
            unit(line, chips[which]), mine_ref.at[which, line], load_sems.at[which, line]
        )

    for other in place.plane():
        send.start(None, small_ref, plane_ref.at[me], plane_sems.at[me], seq=other)
    plane_ref[me] = small_ref[...]

    events = place.events()[::-1]
    for condition, line, _, _ in events:
        for which in range(4):
            theirs = chips[which] + 1 - 2 * place.core
            send.start(
                condition,
                unit(line, theirs),
                sib_ref.at[which, line],
                sib_sems.at[which, line],
                seq=place.sib,
            )
            when(condition, load(which, line).start)

    def add(target, *terms, begin=0, size=unit_rows):
        @pl.loop(0, size // tile)
        def _(step):
            rows = pl.ds(pl.multiple_of(begin + step * tile, tile), tile)
            if len(terms) == 1:
                ref, first = terms[0]
                at = pl.ds(pl.multiple_of(begin - first + step * tile, tile), tile)
                target[rows, :] = target[rows, :] + ref[at, :]
            else:
                total = target[rows, :].astype(f32)
                for ref, first in terms:
                    at = pl.ds(pl.multiple_of(begin - first + step * tile, tile), tile)
                    total = total + ref[at, :].astype(f32)
                target[rows, :] = total.astype(target.dtype)

    def own(which, index):
        condition, line, _, _ = events[index]
        send.arrived(condition, sib_ref.at[which, line], sib_sems.at[which, line])
        when(condition, load(which, line).wait)

    def first(index):
        condition, line, _, _ = events[index]
        own(corner, index)
        target = mine_ref.at[corner, line]
        when(condition, lambda: add(target, (sib_ref.at[corner, line], 0)))
        send.start(
            condition,
            target.at[pl.ds(0, half)],
            corner_a_ref.at[line],
            a_sems.at[line],
            seq=place.xn,
        )
        send.start(
            condition,
            target.at[pl.ds(half, half)],
            corner_b_ref.at[line],
            b_sems.at[line],
            seq=place.yn,
        )

    def second(index):
        condition, line, _, _ = events[index]
        for which, part, sems, begin, to, landing, landing_sems in (
            (over_y, corner_a_ref, a_sems, 0, place.yn, from_y_ref, y_sems),
            (over_x, corner_b_ref, b_sems, half, place.xn, from_x_ref, x_sems),
        ):
            own(which, index)
            send.arrived(condition, part.at[line], sems.at[line])
            target = mine_ref.at[which, line]

            def body(which=which, part=part, begin=begin, target=target):
                add(
                    target,
                    (sib_ref.at[which, line], 0),
                    (part.at[line], begin),
                    begin=begin,
                    size=half,
                )
                add(target, (sib_ref.at[which, line], 0), begin=half - begin, size=half)

            when(condition, body)
            send.start(condition, target, landing.at[line], landing_sems.at[line], seq=to)

    def third(index):
        condition, line, far, side = events[index]
        own(here, index)
        send.arrived(condition, from_x_ref.at[line], x_sems.at[line])
        send.arrived(condition, from_y_ref.at[line], y_sems.at[line])
        target = mine_ref.at[here, line]
        terms = [(ref.at[line], 0) for ref in (sib_ref.at[here], from_x_ref, from_y_ref)]
        if side == 0:
            has_below, has_above = z > 0, z < lines - 1
            add(target, *terms)
            send.arrived(has_below, below_ref.at[line], below_sems.at[line])
            send.arrived(has_above, above_ref.at[line], above_sems.at[line])

            @pl.loop(0, unit_rows // tile)
            def _(step):
                rows = rows_of(step, tile)
                shard_ref[rows, :] = target[rows, :].astype(f32)

            when(has_below, lambda: add(shard_ref, (below_ref.at[line], 0)))
            when(has_above, lambda: add(shard_ref, (above_ref.at[line], 0)))
            return
        landing, sems = (below_ref, below_sems) if side > 0 else (above_ref, above_sems)
        more = both(condition, z > 0) if side > 0 else both(condition, z < lines - 1)
        none = both(condition, z == 0) if side > 0 else both(condition, z == lines - 1)
        send.arrived(more, landing.at[line], sems.at[line])
        when(more, lambda: add(target, *terms, (landing.at[line], 0)))
        when(none, lambda: add(target, *terms))
        send.start(condition, target, landing.at[line], sems.at[line], z=z + side)

    count = len(events)
    first(0)
    first(1)
    for index in range(2, count + 4):
        if index < count:
            first(index)
        if 0 <= index - 2 < count:
            second(index - 2)
        if index == 3:
            for other in place.plane():
                send.arrived(None, plane_ref.at[other], plane_sems.at[other])
            total = plane_ref[0]
            for other in range(1, 8):
                total = total + plane_ref[other]
            plane_sum_ref[...] = total
            line_ref[z] = total
            for other in place.line():
                send.start(None, plane_sum_ref, line_ref.at[z], line_sems.at[z], z=other)
        if 0 <= index - 4 < count:
            third(index - 4)

    for other in place.line():
        send.arrived(None, line_ref.at[other], line_sems.at[other])
    total = line_ref[0]
    for other in range(1, lines):
        total = total + line_ref[other]
    norms_ref[...] = total
    send.finish()


def reduce_grads(lines, grads, small):
    rows, cols = grads.shape
    unit_rows, unit_cols = rows // lines, cols // 8
    half = unit_rows // 2
    any_space = pl.BlockSpec(memory_space=pl.ANY)
    vmem = pl.BlockSpec(memory_space=pltpu.VMEM)
    dma = pltpu.SemaphoreType.DMA
    return pl.pallas_call(
        partial(reduce_kernel, lines),
        out_shape=(
            jax.ShapeDtypeStruct((unit_rows, unit_cols), f32),
            jax.ShapeDtypeStruct(small.shape, f32),
        ),
        in_specs=[any_space, vmem],
        out_specs=(vmem, vmem),
        scratch_shapes=[
            pltpu.VMEM((4, lines, unit_rows, unit_cols), bf16),
            pltpu.VMEM((4, lines, unit_rows, unit_cols), bf16),
            pltpu.VMEM((lines, half, unit_cols), bf16),
            pltpu.VMEM((lines, half, unit_cols), bf16),
            pltpu.VMEM((lines, unit_rows, unit_cols), bf16),
            pltpu.VMEM((lines, unit_rows, unit_cols), bf16),
            pltpu.VMEM((lines, unit_rows, unit_cols), bf16),
            pltpu.VMEM((lines, unit_rows, unit_cols), bf16),
            pltpu.VMEM((8,) + small.shape, f32),
            pltpu.VMEM(small.shape, f32),
            pltpu.VMEM((lines,) + small.shape, f32),
            dma((9 * (2 * lines - 1) + 7 + lines,)),
            dma((4, lines)),
            dma((4, lines)),
            dma((lines,)),
            dma((lines,)),
            dma((lines,)),
            dma((lines,)),
            dma((lines,)),
            dma((lines,)),
            dma((8,)),
            dma((lines,)),
        ],
        compiler_params=pltpu.CompilerParams(
            vmem_limit_bytes=VMEM_BYTES, collective_id=4, has_side_effects=True
        ),
        name="reduce_grads",
    )(grads, small)


def adam_update(grad, weight, first, second, average, rate, decay):
    first = beta_first * first + (1.0 - beta_first) * grad
    second = beta_second * second + (1.0 - beta_second) * grad * grad
    stepped = (
        first / (1.0 - beta_first**STEP) / (jnp.sqrt(second / (1.0 - beta_second**STEP)) + adam_eps)
    )
    weight = weight - rate * (stepped + decay * weight)
    average = ema_decay * average + (1.0 - ema_decay) * weight
    return (first, second, weight, average)


def on_device(
    inputs,
    cotangent,
    neighbours,
    presence,
    row_order,
    w_master,
    w_first,
    w_second,
    w_average,
    n_master,
    n_first,
    n_second,
    n_average,
):
    seqs, tokens, dim = inputs.shape
    heads = dim // HEAD
    devices = lax.axis_size("seq")
    count = seqs * tokens
    length = devices * tokens
    me = lax.axis_index("seq")
    shares = devices // seqs
    held = heads // shares
    pairs = (held + 1) // 2
    width = pairs * LANES
    spare = width - held * HEAD
    sequence, share = me // shares, me % shares

    lines = lax.axis_size("dp")
    planar = devices == 8 and seqs == 4 and spare == 0
    x = inputs.reshape(count, dim)
    cot = cotangent.reshape(count, dim)
    spans = seqs * neighbours.shape[1]
    each = neighbours.shape[2]
    near = neighbours.reshape(-1, dim)
    live = presence.reshape(-1)
    part = n_master.shape[1]
    if planar:
        small = jnp.pad(n_master.astype(bf16), ((0, 16 - 6), (0, -part % LANES)))
        order = row_order.reshape(1, dim)
        _, grads, outputs, grad_inputs, norm_grads = layer(
            lines, pairs, spans, each, live, w_master, small, inputs, order, cot, near
        )
        grad_shard, norm_sums = reduce_grads(lines, grads, norm_grads)
        norm_shard = lax.dynamic_slice(norm_sums, (0, lax.axis_index("dp") * part), (6, part))
    else:
        perm = (jnp.arange(dim)[:, None] == row_order[None, :]).astype(bf16)
        perm_att = jnp.pad(perm.reshape(shares, held * HEAD, dim), ((0, 0), (0, spare), (0, 0)))
        perm_att = perm_att.reshape(shares * width, dim)
        weights = lax.all_gather(w_master.astype(bf16), "dp", axis=0, tiled=True)
        weights = lax.all_gather(weights, "seq", axis=1, tiled=True)
        norms = lax.all_gather(n_master.astype(bf16), "dp", axis=1, tiled=True).astype(f32)
        rows = lax.all_to_all(jnp.repeat(inputs, shares, axis=0), "seq", 0, 0)
        rows = rows.reshape(length, dim)
        w_qkv = weights[:, : 3 * dim].reshape(dim, 3, shares, held * HEAD)
        w_qkv = lax.dynamic_index_in_dim(w_qkv, share, axis=2, keepdims=False)
        w_qkv = jnp.pad(w_qkv, ((0, 0), (0, 0), (0, spare))).reshape(dim, 3 * width)
        hid, qkv, att, lse = self_forward(pairs, rows, norms, perm, w_qkv)
        att_tok = (
            lax.all_to_all(att.reshape(devices, tokens, width), "seq", 0, 0)
            .reshape(seqs, shares, tokens, width)
            .transpose(0, 2, 1, 3)
            .reshape(count, shares * width)
        )
        att_p, first, hid_p, cross_q, near_p, near_kv, co_p, second = cross_forward(
            spans, each, live, att_tok, x, norms, perm, perm_att, near, weights
        )
        outputs, gsecond, grads, gnorm_e = feed(second, cot, norms, perm, weights)
        gfirst, gatt_tok, grads, gnorm_c = cross_backward(
            spans,
            each,
            live,
            gsecond,
            first,
            norms,
            perm,
            perm_att,
            att_p,
            hid_p,
            cross_q,
            near_p,
            near_kv,
            co_p,
            weights,
            grads,
        )
        gatt = lax.all_to_all(
            gatt_tok.reshape(seqs, tokens, shares, width)
            .transpose(0, 2, 1, 3)
            .reshape(devices, tokens, width),
            "seq",
            0,
            0,
        ).reshape(length, width)
        gqkv, ghid = self_backward(pairs, qkv, att, gatt, lse, hid, w_qkv)
        parts = (
            lax.all_to_all(ghid.reshape(devices, tokens, dim), "seq", 0, 0)
            .reshape(seqs, shares, tokens, dim)
            .transpose(1, 0, 2, 3)
            .reshape(shares, count, dim)
        )
        grad_inputs, gnorm_a = last_norm(parts, x, gfirst, norms, perm)
        gqkv = gqkv.reshape(dim, 3, 1, width)[..., : held * HEAD]
        gqkv = jnp.where(jnp.arange(shares)[:, None] == share, gqkv, jnp.zeros_like(gqkv))
        grads = lax.dynamic_update_slice(grads, gqkv.reshape(dim, 3 * dim), (0, 0))
        norm_grads = lax.psum(jnp.concatenate([gnorm_a, gnorm_c, gnorm_e], axis=0), "seq")
        partial_sum = lax.psum_scatter(grads, "seq", scatter_dimension=1, tiled=True)
        grad_shard = lax.psum_scatter(partial_sum, "dp", scatter_dimension=0, tiled=True)
        grad_shard = grad_shard.astype(f32)
        norm_shard = lax.psum_scatter(
            norm_grads.astype(bf16), "dp", scatter_dimension=1, tiled=True
        ).astype(f32)
    w_first_new, w_second_new, w_new, w_average_new = adam_update(
        grad_shard, w_master, w_first, w_second, w_average, learn_rate, weight_decay
    )
    n_first_new, n_second_new, n_new, n_average_new = adam_update(
        norm_shard, n_master, n_first, n_second, n_average, norm_rate, 0.0
    )
    return (
        outputs.reshape(seqs, tokens, dim),
        grad_inputs.reshape(seqs, tokens, dim),
        w_first_new,
        w_second_new,
        w_new,
        w_average_new,
        n_first_new,
        n_second_new,
        n_new,
        n_average_new,
    )


def solution(mesh):
    in_specs = (
        P("dp", "seq", None),
        P("dp", "seq", None),
        P("dp", "seq", None, None, None),
        P("dp", "seq", None),
        P(),
        P("dp", "seq"),
        P("dp", "seq"),
        P("dp", "seq"),
        P("dp", "seq"),
        P(None, "dp"),
        P(None, "dp"),
        P(None, "dp"),
        P(None, "dp"),
    )
    out_specs = (
        P("dp", "seq", None),
        P("dp", "seq", None),
        P("dp", "seq"),
        P("dp", "seq"),
        P("dp", "seq"),
        P("dp", "seq"),
        P(None, "dp"),
        P(None, "dp"),
        P(None, "dp"),
        P(None, "dp"),
    )
    return jax.shard_map(
        on_device, mesh=mesh, in_specs=in_specs, out_specs=out_specs, check_vma=False
    )
```

```python
from functools import partial

import jax
import jax.numpy as jnp
from jax import lax
from jax.experimental import pallas as pl
from jax.experimental.pallas import tpu as pltpu
from jax.sharding import PartitionSpec as P

HEAD = 64
STEP = 5
LANES = 128
SCALE = HEAD ** (-0.5)

beta_first = 0.9
beta_second = 0.95
adam_eps = 1e-08
learn_rate = 0.04
norm_rate = 0.6
weight_decay = 0.1
ema_decay = 0.5
norm_eps = 1e-05
masked_score = -1e30
VMEM_BYTES = 62 * 1024 * 1024
bf16 = jnp.bfloat16
f32 = jnp.float32


def mm(left, right):
    return lax.dot_general(left, right, (((1,), (0,)), ((), ())), preferred_element_type=f32)


def nt(left, right):
    return lax.dot_general(left, right, (((1,), (1,)), ((), ())), preferred_element_type=f32)


def tn(left, right):
    return lax.dot_general(left, right, (((0,), (0,)), ((), ())), preferred_element_type=f32)


def params():
    return pltpu.CompilerParams(vmem_limit_bytes=VMEM_BYTES)


def rows_of(index, size):
    return pl.ds(pl.multiple_of(index * size, size), size)


def centre_scale(values):
    centre = jnp.mean(values, axis=-1, keepdims=True)
    centred = values - centre
    spread = jnp.mean(centred * centred, axis=-1, keepdims=True)
    recip = lax.rsqrt(spread + norm_eps)
    return centred * recip, recip


def norm_back(upstream, normed, recip, gain):
    scaled = upstream * gain
    inner = (
        scaled
        - jnp.mean(scaled, axis=-1, keepdims=True)
        - normed * jnp.mean(scaled * normed, axis=-1, keepdims=True)
    )
    return (
        recip * inner,
        jnp.sum(upstream * normed, axis=0, keepdims=True),
        jnp.sum(upstream, axis=0, keepdims=True),
    )


def gelu_parts(value):
    const = 0.7978845608028654
    square = value * value
    bend = jnp.tanh(const * value * (1.0 + 0.044715 * square))
    half = 0.5 * (1.0 + bend)
    slope = half + 0.5 * value * (1.0 - bend * bend) * (const * (1.0 + 3 * 0.044715 * square))
    return value * half, slope


def head_mask(rows, half):
    lane = lax.broadcasted_iota(jnp.int32, (rows, LANES), 1)
    return (lane < HEAD) if half == 0 else (lane >= HEAD)


def pick(mask, value):
    return jnp.where(mask, value, jnp.zeros_like(value))


MESH = pl.DeviceIdType.MESH


class Place:
    def __init__(self, lines):
        self.lines = lines
        self.z = lax.axis_index("dp")
        self.me = lax.axis_index("seq")
        core, x, y = self.me % 2, (self.me // 2) % 2, self.me // 4
        self.core, self.x, self.y, self.chip = core, x, y, self.me // 2
        self.sib = self.me + 1 - 2 * core
        self.xn = self.me + 2 - 4 * x
        self.yn = self.me + 4 - 8 * y
        self.dg = self.xn + 4 - 8 * y

    def events(self):
        found = [(None, self.z, 0, 0)]
        for far in range(1, self.lines):
            found.append((self.z >= far, self.z - far, far, -1))
            found.append((self.z + far < self.lines, self.z + far, far, 1))
        return found

    def plane(self):
        return [lax.rem(self.me + step, 8) for step in range(1, 8)]

    def line(self):
        return [lax.rem(self.z + step, self.lines) for step in range(1, self.lines)]

    def meet(self):
        barrier = pltpu.get_barrier_semaphore()
        for other in self.plane():
            pl.semaphore_signal(
                barrier, inc=1, device_id={"dp": self.z, "seq": other}, device_id_type=MESH
            )
        for other in self.line():
            pl.semaphore_signal(
                barrier, inc=1, device_id={"dp": other, "seq": self.me}, device_id_type=MESH
            )
        pl.semaphore_wait(barrier, 7 + self.lines - 1)


def when(condition, body):
    if condition is None:
        body()
    else:
        pl.when(condition)(body)


def both(first, second):
    if first is None or second is None:
        return second if first is None else first
    return jnp.logical_and(first, second)


class Sender:
    def __init__(self, place, send_sems):
        self.place, self.sems, self.open, self.count = place, send_sems, [], 0

    def start(self, condition, src, dst, recv_sem, z=None, seq=None):
        place = self.place
        target = {"dp": place.z if z is None else z, "seq": place.me if seq is None else seq}
        copy = pltpu.make_async_remote_copy(
            src_ref=src,
            dst_ref=dst,
            send_sem=self.sems.at[self.count],
            recv_sem=recv_sem,
            device_id=target,
            device_id_type=MESH,
        )
        self.open.append((condition, copy))
        self.count += 1
        when(condition, copy.start)

    def arrived(self, condition, ref, recv_sem):
        copy = pltpu.make_async_remote_copy(
            src_ref=ref,
            dst_ref=ref,
            send_sem=self.sems.at[0],
            recv_sem=recv_sem,
            device_id={"dp": self.place.z, "seq": self.place.sib},
            device_id_type=MESH,
        )
        when(condition, copy.wait_recv)

    def finish(self):
        for condition, copy in self.open:
            when(condition, copy.wait_send)
        self.open = []


class Weave:
    def __init__(self, steps):
        self.steps = list(steps)

    def some(self, count):
        for _ in range(min(count, len(self.steps))):
            self.steps.pop(0)()

    def rest(self):
        self.some(len(self.steps))


def unit_of(ref, lines, line, seq, begin=0, size=None):
    rows, cols = ref.shape[0] // lines, ref.shape[1] // 8
    size = rows if size is None else size
    return ref.at[
        pl.ds(pl.multiple_of(line * rows + begin, 16), size),
        pl.ds(pl.multiple_of(seq * cols, cols), cols),
    ]


def weight_copies(pairs, dim, wts_ref, w_ref, sems):
    width = pairs * LANES
    first = lax.rem(lax.axis_index("seq"), dim // width) * width
    return [
        pltpu.make_async_copy(
            wts_ref.at[:, pl.ds(pl.multiple_of(first + part * dim, LANES), width)],
            w_ref.at[:, pl.ds(part * width, width)],
            sems.at[part],
        )
        for part in range(3)
    ]


def pair_forward(pair, pairs, qkv_ref, att_ref, lse_ref, between):
    length = att_ref.shape[0]
    tile = 256
    below = lax.broadcasted_iota(jnp.int32, (tile, tile), 1) <= lax.broadcasted_iota(
        jnp.int32, (tile, tile), 0
    )
    masks = [head_mask(tile, 0), head_mask(tile, 1)]
    lane = lax.broadcasted_iota(jnp.int32, (tile, LANES), 1)
    for step in range(length // tile):
        rows = slice(step * tile, (step + 1) * tile)
        query = qkv_ref[pair, rows, :] * SCALE
        keys_here = qkv_ref[pairs + pair, rows, :]
        values_here = qkv_ref[2 * pairs + pair, rows, :]
        outs, logs = [], []
        for half in range(2):
            mine = pick(masks[half], query)
            here = jnp.where(below, nt(mine, keys_here), masked_score)
            peak = jnp.max(here, axis=-1, keepdims=True)
            if step:
                past = nt(mine, qkv_ref[pairs + pair, : step * tile, :])
                peak = jnp.maximum(peak, jnp.max(past, axis=-1, keepdims=True))
                past = jnp.exp(past - peak)
            here = jnp.exp(here - peak)
            total = jnp.sum(here, axis=-1, keepdims=True)
            out = mm(here.astype(bf16), values_here)
            if step:
                total = total + jnp.sum(past, axis=-1, keepdims=True)
                out = out + mm(past.astype(bf16), qkv_ref[2 * pairs + pair, : step * tile, :])
            outs.append(out / total)
            logs.append(peak + jnp.log(total))
        lse_ref[pair, :, rows] = jnp.where(lane == 0, logs[0], logs[1]).T[0:2, :]
        att_ref[rows, pl.ds(pl.multiple_of(pair * LANES, LANES), LANES)] = jnp.where(
            masks[0], outs[0], outs[1]
        ).astype(bf16)
        between()


def norm_rows(x_ref, norms, perm_ref, hid_ref):
    tile = 256

    @pl.loop(0, x_ref.shape[0] // tile)
    def _(step):
        rows = rows_of(step, tile)
        normed, _ = centre_scale(x_ref[rows, :].astype(f32))
        hidden = (normed * norms[0:1, :] + norms[1:2, :]).astype(bf16)
        hid_ref[rows, :] = mm(hidden, perm_ref[...]).astype(bf16)


def triple_part(part, pairs, hid_ref, w_ref, qkv_ref):
    width = pairs * LANES
    triple = mm(hid_ref[...], w_ref[:, part * width : (part + 1) * width]).astype(bf16)
    for pair in range(pairs):
        qkv_ref[part * pairs + pair] = triple[:, pair * LANES : (pair + 1) * LANES]


def self_forward_kernel(
    pairs, x_ref, norms_ref, perm_ref, w_ref, hid_ref, qkv_ref, att_ref, lse_ref
):
    norm_rows(x_ref, norms_ref, perm_ref, hid_ref)
    for part in range(3):
        triple_part(part, pairs, hid_ref, w_ref, qkv_ref)

    @pl.loop(0, pairs)
    def _(pair):
        pair_forward(pair, pairs, qkv_ref, att_ref, lse_ref, lambda: None)


def self_forward(pairs, x, norms, perm, w):
    length, dim = x.shape
    return pl.pallas_call(
        partial(self_forward_kernel, pairs),
        out_shape=(
            jax.ShapeDtypeStruct((length, dim), bf16),
            jax.ShapeDtypeStruct((3 * pairs, length, LANES), bf16),
            jax.ShapeDtypeStruct((length, pairs * LANES), bf16),
            jax.ShapeDtypeStruct((pairs, 2, length), f32),
        ),
        compiler_params=params(),
        name="self_forward",
    )(x, norms, perm, w)


def pair_backward(pair, pairs, qkv_ref, att_ref, gatt_ref, lse_ref, grad_ref, acc_ref, between):
    length = att_ref.shape[0]
    width = pairs * LANES
    tile = 256
    above = lax.broadcasted_iota(jnp.int32, (tile, tile), 0) <= lax.broadcasted_iota(
        jnp.int32, (tile, tile), 1
    )
    masks = [head_mask(tile, 0), head_mask(tile, 1)]
    lanes = pl.ds(pl.multiple_of(pair * LANES, LANES), LANES)
    for step in range(length // tile):
        rows = slice(step * tile, (step + 1) * tile)
        query = qkv_ref[pair, rows, :] * SCALE
        grad_out = gatt_ref[rows, lanes]
        product = grad_out.astype(f32) * att_ref[rows, lanes].astype(f32)
        queries = [pick(masks[half], query) for half in range(2)]
        grads = [pick(masks[half], grad_out) for half in range(2)]
        deltas = [jnp.sum(pick(masks[half], product).T, axis=0, keepdims=True) for half in range(2)]
        grad_query = [None, None]
        for other in range(step + 1):
            cols = slice(other * tile, (other + 1) * tile)
            keys = qkv_ref[pairs + pair, cols, :]
            values = qkv_ref[2 * pairs + pair, cols, :]
            key_part = value_part = None
            for half in range(2):
                scores = nt(keys, queries[half])
                if other == step:
                    scores = jnp.where(above, scores, masked_score)
                probs = jnp.exp(scores - lse_ref[pair, half : half + 1, rows])
                grad_scores = (probs * (nt(values, grads[half]) - deltas[half])).astype(bf16)
                query_term = tn(grad_scores, keys)
                grad_query[half] = (
                    query_term if grad_query[half] is None else grad_query[half] + query_term
                )
                key_term = mm(grad_scores, queries[half])
                value_term = mm(probs.astype(bf16), grads[half])
                key_part = key_term if key_part is None else key_part + key_term
                value_part = value_term if value_part is None else value_part + value_term
            if other == step:
                acc_ref[0, cols, :] = key_part
                acc_ref[1, cols, :] = value_part
            else:
                acc_ref[0, cols, :] += key_part
                acc_ref[1, cols, :] += value_part
        grad_ref[rows, lanes] = (jnp.where(masks[0], grad_query[0], grad_query[1]) * SCALE).astype(
            bf16
        )
        between()
    for part in range(2):
        lanes_to = pl.ds(pl.multiple_of((part + 1) * width + pair * LANES, LANES), LANES)
        grad_ref[:, lanes_to] = acc_ref[part].astype(bf16)


def self_backward_kernel(
    pairs,
    qkv_ref,
    att_ref,
    gatt_ref,
    lse_ref,
    hid_ref,
    w_ref,
    gw_ref,
    ghid_ref,
    grad_ref,
    acc_ref,
):
    length = att_ref.shape[0]
    width = pairs * LANES
    attention = (qkv_ref, att_ref, gatt_ref, lse_ref, grad_ref, acc_ref)

    @pl.loop(0, pairs)
    def _(pair):
        pair_backward(pair, pairs, *attention, lambda: None)

    hidden_t = hid_ref[...].T
    for part in range(3):
        cols = slice(part * width, (part + 1) * width)
        gw_ref[:, cols] = mm(hidden_t, grad_ref[:, cols]).astype(bf16)
    for begin in range(0, length, 256):
        rows = slice(begin, begin + 256)
        ghid_ref[rows, :] = nt(grad_ref[rows, :], w_ref[...]).astype(bf16)


def self_backward(pairs, qkv, att, gatt, lse, hid, w):
    length, dim = hid.shape
    width = pairs * LANES
    return pl.pallas_call(
        partial(self_backward_kernel, pairs),
        out_shape=(
            jax.ShapeDtypeStruct((dim, 3 * width), bf16),
            jax.ShapeDtypeStruct((length, dim), bf16),
        ),
        scratch_shapes=[
            pltpu.VMEM((length, 3 * width), bf16),
            pltpu.VMEM((2, length, LANES), f32),
        ],
        compiler_params=params(),
        name="self_backward",
    )(qkv, att, gatt, lse, hid, w)


def spread_heads(block, rows, group):
    lane = lax.broadcasted_iota(jnp.int32, block.shape, 1) // HEAD
    return jnp.concatenate([pick(lane == head, block) for head in range(group)], axis=0)


def gather_heads(stacked, rows, group):
    lane = lax.broadcasted_iota(jnp.int32, (rows, stacked.shape[1]), 1) // HEAD
    out = None
    for head in range(group):
        part = pick(lane == head, stacked[head * rows : (head + 1) * rows])
        out = part if out is None else out + part
    return out


def live_keys(presence_ref, span, shape, axis, neighbours, each):
    index = lax.broadcasted_iota(jnp.int32, shape, axis) // each
    live = jnp.zeros(shape, f32)
    anyone = None
    for which in range(neighbours):
        here = presence_ref[span * neighbours + which]
        there = jnp.where(here > 0, 1.0, 0.0).astype(f32)
        live = jnp.where(index == which, there, live)
        anyone = here if anyone is None else jnp.maximum(anyone, here)
    return live, anyone.astype(f32)


def span_forward(span, spans, neighbours, presence_ref, cross_q_ref, near_kv_ref, cross_ref):
    count, dim = cross_q_ref.shape
    span_len = count // spans
    near = near_kv_ref.shape[0] // spans
    group = 256 // HEAD
    rows = rows_of(span, span_len)
    keys = rows_of(span, near)
    live, anyone = live_keys(presence_ref, span, (1, near), 1, neighbours, near // neighbours)
    for begin in range(0, dim, group * HEAD):
        lanes = slice(begin, begin + group * HEAD)
        lanes_v = slice(dim + begin, dim + begin + group * HEAD)
        query = spread_heads(cross_q_ref[rows, lanes] * SCALE, span_len, group)
        scores = jnp.where(live > 0, nt(query, near_kv_ref[keys, lanes]), masked_score)
        peak = jnp.max(scores, axis=-1, keepdims=True)
        expon = jnp.exp(scores - peak) * live
        total = jnp.sum(expon, axis=-1, keepdims=True) + 1.0 - anyone
        out = mm(expon.astype(bf16), near_kv_ref[keys, lanes_v]) / total
        cross_ref[rows, lanes] = gather_heads(out, span_len, group).astype(bf16)


def cross_forward_kernel(
    spans,
    neighbours,
    presence_ref,
    att_ref,
    x_ref,
    norms_ref,
    perm_ref,
    perm_att_ref,
    near_ref,
    w_out_ref,
    w_cq_ref,
    w_ck_ref,
    w_cv_ref,
    w_co_ref,
    att_p_ref,
    first_ref,
    hid_p_ref,
    cross_q_ref,
    near_p_ref,
    near_kv_ref,
    co_p_ref,
    second_ref,
    cross_ref,
):
    count, dim = x_ref.shape
    rows_near = near_ref.shape[0]
    tile = 512

    att_p_ref[...] = mm(att_ref[...], perm_att_ref[...]).astype(bf16)
    first_ref[...] = x_ref[...].astype(f32) + mm(att_p_ref[...], w_out_ref[...])

    normed, _ = centre_scale(first_ref[...])
    hidden = (normed * norms_ref[2:3, :] + norms_ref[3:4, :]).astype(bf16)
    hid_p_ref[...] = mm(hidden, perm_ref[...]).astype(bf16)
    cross_q_ref[...] = mm(hid_p_ref[...], w_cq_ref[...]).astype(bf16)

    @pl.loop(0, rows_near // tile)
    def _(step):
        rows = rows_of(step, tile)
        near_p_ref[rows, :] = mm(near_ref[rows, :], perm_ref[...]).astype(bf16)
        near_kv_ref[rows, :dim] = mm(near_p_ref[rows, :], w_ck_ref[...]).astype(bf16)
        near_kv_ref[rows, dim:] = mm(near_p_ref[rows, :], w_cv_ref[...]).astype(bf16)

    @pl.loop(0, spans)
    def _(span):
        span_forward(span, spans, neighbours, presence_ref, cross_q_ref, near_kv_ref, cross_ref)

    co_p_ref[...] = mm(cross_ref[...], perm_ref[...]).astype(bf16)
    second_ref[...] = first_ref[...] + mm(co_p_ref[...], w_co_ref[...])


def column_block(rows, width, index):
    return pl.BlockSpec((rows, width), lambda *_: (0, index), pipeline_mode=pl.Buffered(1))


def whole(array):
    return pl.BlockSpec(array.shape, lambda *_: (0,) * array.ndim, pipeline_mode=pl.Buffered(1))


def whole_shape(shape):
    return pl.BlockSpec(shape, lambda *_: (0,) * len(shape), pipeline_mode=pl.Buffered(1))


def cross_forward(spans, neighbours, presence, att, x, norms, perm, perm_att, near, weights):
    count, dim = x.shape
    rows_near = near.shape[0]
    out_shape = (
        jax.ShapeDtypeStruct((count, dim), bf16),
        jax.ShapeDtypeStruct((count, dim), f32),
        jax.ShapeDtypeStruct((count, dim), bf16),
        jax.ShapeDtypeStruct((count, dim), bf16),
        jax.ShapeDtypeStruct((rows_near, dim), bf16),
        jax.ShapeDtypeStruct((rows_near, 2 * dim), bf16),
        jax.ShapeDtypeStruct((count, dim), bf16),
        jax.ShapeDtypeStruct((count, dim), f32),
    )
    operands = (att, x, norms, perm, perm_att, near)
    return pl.pallas_call(
        partial(cross_forward_kernel, spans, neighbours),
        out_shape=out_shape,
        grid=(1,),
        in_specs=[pl.BlockSpec(memory_space=pltpu.SMEM)]
        + [whole(op) for op in operands]
        + [column_block(dim, dim, index) for index in (3, 4, 5, 6, 7)],
        out_specs=tuple(whole_shape(shape.shape) for shape in out_shape),
        scratch_shapes=[pltpu.VMEM((count, dim), bf16)],
        compiler_params=params(),
        name="cross_forward",
    )(presence, *operands, *([weights] * 5))


def feed_kernel(
    second_ref,
    cot_ref,
    norms_ref,
    perm_ref,
    w_up_ref,
    w_down_ref,
    out_ref,
    gsecond_ref,
    all_ref,
    gnorm_ref,
    hid_p_ref,
    hid_t_ref,
    cot_p_ref,
    cot_t_ref,
    result_ref,
    back_ref,
    gup_ref,
    gdown_ref,
    sems,
):
    step = pl.program_id(0)
    last = pl.num_programs(0) - 1
    slot = lax.rem(step, 2)
    dim, tile = w_up_ref.shape

    def copies(step, slot):
        up = pl.multiple_of(8 * dim + step * tile, tile)
        down = pl.multiple_of(8 * dim + (last + 1 + step) * tile, tile)
        return (
            pltpu.make_async_copy(gup_ref.at[slot], all_ref.at[:, pl.ds(up, tile)], sems.at[0, slot]),
            pltpu.make_async_copy(
                gdown_ref.at[slot], all_ref.at[:, pl.ds(down, tile)], sems.at[1, slot]
            ),
        )

    @pl.when(step >= 2)
    def _():
        for copy in copies(step - 2, slot):
            copy.wait()

    @pl.when(step == 0)
    def _():
        normed, _ = centre_scale(second_ref[...])
        hidden = (normed * norms_ref[4:5, :] + norms_ref[5:6, :]).astype(bf16)
        hid_p_ref[...] = mm(hidden, perm_ref[...]).astype(bf16)
        hid_t_ref[...] = hid_p_ref[...].T
        cot_p_ref[...] = mm(cot_ref[...], perm_ref[...]).astype(bf16)
        cot_t_ref[...] = cot_p_ref[...].T
        result_ref[...] = jnp.zeros_like(result_ref)
        back_ref[...] = jnp.zeros_like(back_ref)

    upward = mm(hid_p_ref[...], w_up_ref[...])
    active, slope = gelu_parts(upward)
    active = active.astype(bf16)
    result_ref[...] += nt(active, w_down_ref[...])
    gdown_ref[slot] = mm(cot_t_ref[...], active).astype(bf16)
    grad_up = (mm(cot_p_ref[...], w_down_ref[...]) * slope).astype(bf16)
    gup_ref[slot] = mm(hid_t_ref[...], grad_up).astype(bf16)
    for copy in copies(step, slot):
        copy.start()
    back_ref[...] += nt(grad_up, w_up_ref[...])

    @pl.when(step == last)
    def _():
        out_ref[...] = (
            second_ref[...] + nt(result_ref[...].astype(bf16), perm_ref[...])
        ).astype(bf16)
        upstream = nt(back_ref[...].astype(bf16), perm_ref[...])
        normed, recip = centre_scale(second_ref[...])
        back, gain, shift = norm_back(upstream, normed, recip, norms_ref[4:5, :])
        gsecond_ref[...] = cot_ref[...].astype(f32) + back
        gnorm_ref[0:1, :] = gain
        gnorm_ref[1:2, :] = shift
        for which in (step - 1, step):
            for copy in copies(which, lax.rem(which, 2)):
                copy.wait()


def feed(second, cot, norms, perm, weights):
    count, dim = second.shape
    ffw = (weights.shape[1] - 8 * dim) // 2
    tile = 512
    first_up = 8 * dim // tile
    first_down = (8 * dim + ffw) // tile
    out_shape = (
        jax.ShapeDtypeStruct((count, dim), bf16),
        jax.ShapeDtypeStruct((count, dim), f32),
        jax.ShapeDtypeStruct(weights.shape, bf16),
        jax.ShapeDtypeStruct((2, dim), f32),
    )
    operands = (second, cot, norms, perm)
    return pl.pallas_call(
        feed_kernel,
        out_shape=out_shape,
        grid=(ffw // tile,),
        in_specs=[whole(op) for op in operands]
        + [
            pl.BlockSpec((dim, tile), lambda i: (0, first_up + i)),
            pl.BlockSpec((dim, tile), lambda i: (0, first_down + i)),
        ],
        out_specs=(
            whole_shape((count, dim)),
            whole_shape((count, dim)),
            pl.BlockSpec(memory_space=pl.ANY),
            whole_shape((2, dim)),
        ),
        scratch_shapes=[
            pltpu.VMEM((count, dim), bf16),
            pltpu.VMEM((dim, count), bf16),
            pltpu.VMEM((count, dim), bf16),
            pltpu.VMEM((dim, count), bf16),
            pltpu.VMEM((count, dim), f32),
            pltpu.VMEM((count, dim), f32),
            pltpu.VMEM((2, dim, tile), bf16),
            pltpu.VMEM((2, dim, tile), bf16),
            pltpu.SemaphoreType.DMA((2, 2)),
        ],
        compiler_params=params(),
        name="feed",
    )(*operands, weights, weights)


def span_backward(
    span, spans, neighbours, presence_ref, cross_q_ref, gco_ref, near_kv_ref, gcq_ref, gnear_ref
):
    count, dim = cross_q_ref.shape
    span_len = count // spans
    near = near_kv_ref.shape[0] // spans
    group = 256 // HEAD
    rows = rows_of(span, span_len)
    keys = rows_of(span, near)
    live, anyone = live_keys(presence_ref, span, (near, 1), 0, neighbours, near // neighbours)
    for begin in range(0, dim, group * HEAD):
        lanes = slice(begin, begin + group * HEAD)
        lanes_v = slice(dim + begin, dim + begin + group * HEAD)
        query = spread_heads(cross_q_ref[rows, lanes] * SCALE, span_len, group)
        grad_out = spread_heads(gco_ref[rows, lanes], span_len, group)
        key = near_kv_ref[keys, lanes]
        scores = jnp.where(live > 0, nt(key, query), masked_score)
        peak = jnp.max(scores, axis=0, keepdims=True)
        expon = jnp.exp(scores - peak) * live
        total = jnp.sum(expon, axis=0, keepdims=True) + 1.0 - anyone
        probs = expon * (1.0 / total)
        grad_probs = nt(near_kv_ref[keys, lanes_v], grad_out)
        inner = jnp.sum(probs * grad_probs, axis=0, keepdims=True)
        grad_scores = (probs * (grad_probs - inner)).astype(bf16)
        gcq_ref[rows, lanes] = (
            gather_heads(tn(grad_scores, key), span_len, group) * SCALE
        ).astype(bf16)
        gnear_ref[keys, lanes] = mm(grad_scores, query).astype(bf16)
        gnear_ref[keys, lanes_v] = mm(probs.astype(bf16), grad_out).astype(bf16)


def cross_backward_kernel(
    spans,
    neighbours,
    presence_ref,
    gsecond_ref,
    first_ref,
    norms_ref,
    perm_ref,
    perm_att_ref,
    att_p_ref,
    hid_p_ref,
    cross_q_ref,
    near_p_ref,
    near_kv_ref,
    co_p_ref,
    w_out_ref,
    w_cq_ref,
    w_co_ref,
    _,
    gfirst_ref,
    gatt_ref,
    all_ref,
    gnorm_ref,
    gco_ref,
    gcq_ref,
    gnear_ref,
    gw_ref,
    sems,
):
    dim = first_ref.shape[1]
    outs = []

    def keep(index, value):
        gw_ref[index] = value.astype(bf16)
        outs.append(
            pltpu.make_async_copy(
                gw_ref.at[index], all_ref.at[:, pl.ds((3 + index) * dim, dim)], sems.at[index]
            )
        )
        outs[-1].start()

    upper = gsecond_ref[...].astype(bf16)
    gco_ref[...] = nt(nt(upper, w_co_ref[...]).astype(bf16), perm_ref[...]).astype(bf16)
    tables = (presence_ref, cross_q_ref, gco_ref, near_kv_ref, gcq_ref, gnear_ref)
    pl.loop(0, spans)(lambda span: span_backward(span, spans, neighbours, *tables))
    upstream = nt(nt(gcq_ref[...], w_cq_ref[...]).astype(bf16), perm_ref[...])
    normed, recip = centre_scale(first_ref[...])
    back, gain, shift = norm_back(upstream, normed, recip, norms_ref[2:3, :])
    gnorm_ref[0:1, :] = gain
    gnorm_ref[1:2, :] = shift
    gfirst_ref[...] = gsecond_ref[...] + back
    lower = gfirst_ref[...].astype(bf16)
    gatt_ref[...] = nt(nt(lower, w_out_ref[...]).astype(bf16), perm_att_ref[...]).astype(bf16)
    keep(4, mm(co_p_ref[...].T, upper))
    near_t = near_p_ref[...].T
    for part in range(2):
        keep(2 + part, mm(near_t, gnear_ref[:, part * dim : (part + 1) * dim]))
    keep(1, mm(hid_p_ref[...].T, gcq_ref[...]))
    keep(0, mm(att_p_ref[...].T, lower))
    for copy in outs:
        copy.wait()


def cross_backward(
    spans,
    neighbours,
    presence,
    gsecond,
    first,
    norms,
    perm,
    perm_att,
    att_p,
    hid_p,
    cross_q,
    near_p,
    near_kv,
    co_p,
    weights,
    grads,
):
    count, dim = first.shape
    rows_near = near_p.shape[0]
    out_shape = [
        jax.ShapeDtypeStruct((count, dim), f32),
        jax.ShapeDtypeStruct((count, perm_att.shape[0]), bf16),
        jax.ShapeDtypeStruct(grads.shape, bf16),
        jax.ShapeDtypeStruct((2, dim), f32),
    ]
    scratch = [
        pltpu.VMEM((count, dim), bf16),
        pltpu.VMEM((count, dim), bf16),
        pltpu.VMEM((rows_near, 2 * dim), bf16),
        pltpu.VMEM((5, dim, dim), bf16),
        pltpu.SemaphoreType.DMA((5,)),
    ]
    operands = (
        gsecond,
        first,
        norms,
        perm,
        perm_att,
        att_p,
        hid_p,
        cross_q,
        near_p,
        near_kv,
        co_p,
    )
    return pl.pallas_call(
        partial(cross_backward_kernel, spans, neighbours),
        out_shape=out_shape,
        grid=(1,),
        in_specs=[pl.BlockSpec(memory_space=pltpu.SMEM)]
        + [whole(op) for op in operands]
        + [column_block(dim, dim, index) for index in (3, 4, 7)]
        + [pl.BlockSpec(memory_space=pl.ANY)],
        out_specs=tuple(
            pl.BlockSpec(memory_space=pl.ANY) if index == 2 else whole_shape(shape.shape)
            for index, shape in enumerate(out_shape)
        ),
        scratch_shapes=scratch,
        input_output_aliases={len(operands) + 4: 2},
        compiler_params=params(),
        name="cross_backward",
    )(presence, *operands, *([weights] * 3), grads)


def last_norm_kernel(parts_ref, x_ref, gfirst_ref, norms_ref, perm_ref, out_ref, gnorm_ref):
    total = parts_ref[0].astype(f32)
    for part in range(1, parts_ref.shape[0]):
        total = total + parts_ref[part].astype(f32)
    upstream = nt(total.astype(bf16), perm_ref[...])
    normed, recip = centre_scale(x_ref[...].astype(f32))
    back, gain, shift = norm_back(upstream, normed, recip, norms_ref[0:1, :])
    out_ref[...] = gfirst_ref[...] + back
    gnorm_ref[0:1, :] = gain
    gnorm_ref[1:2, :] = shift


def last_norm(parts, x, gfirst, norms, perm):
    count, dim = x.shape
    return pl.pallas_call(
        last_norm_kernel,
        out_shape=(
            jax.ShapeDtypeStruct((count, dim), f32),
            jax.ShapeDtypeStruct((2, dim), f32),
        ),
        compiler_params=params(),
        name="last_norm",
    )(parts, x, gfirst, norms, perm)


def layer_kernel(
    lines,
    pairs,
    spans,
    neighbours,
    presence_ref,
    w_ref,
    norm_ref,
    x_ref,
    order_ref,
    cot_ref,
    near_ref,
    wts_ref,
    all_ref,
    out_ref,
    gin_ref,
    sums_ref,
    hid_ref,
    qkv_ref,
    att_ref,
    lse_ref,
    att_p_ref,
    first_ref,
    hid_p_ref,
    cross_q_ref,
    near_p_ref,
    near_kv_ref,
    co_p_ref,
    second_ref,
    own_ref,
    small_ref,
    rows_ref,
    w_qkv_ref,
    w_mid_ref,
    att_tok_ref,
    cross_ref,
    up_p_ref,
    up_t_ref,
    cot_p_ref,
    cot_t_ref,
    result_ref,
    back_ref,
    gfeed_ref,
    perm_ref,
    norms_ref,
    gatt_ref,
    acc_ref,
    gsib_ref,
    parts_ref,
    send_sems,
    z_sems,
    y_sems,
    x_sems,
    a_sems,
    b_sems,
    sib_sems,
    norm_sems,
    row_sems,
    att_sems,
    local_sems,
    qkv_sems,
    mid_sems,
    feed_sems,
    gatt_sems,
    gsib_sems,
    part_sems,
):
    place = Place(lines)
    z, me, core = place.z, place.me, place.core
    length, dim = hid_ref.shape
    width = pairs * LANES
    tokens = length // 8
    half = own_ref.shape[0] // 2
    near_load = pltpu.make_async_copy(near_ref, near_p_ref, local_sems.at[2])
    near_load.start()
    own_ref[...] = w_ref[...].astype(bf16)
    place.meet()
    send = Sender(place, send_sems)
    unit = partial(unit_of, wts_ref, lines)
    events = place.events()
    keep = pltpu.make_async_copy(own_ref, unit(z, me), local_sems.at[0])
    keep.start()

    def build_perm():
        row = lax.broadcasted_iota(jnp.int32, (dim, dim), 0)
        perm_ref[...] = jnp.where(row == order_ref[0:1, :], 1.0, 0.0).astype(bf16)

    def obtain(index):
        condition, line, far, side = events[index]
        mine = unit(line, me)
        src = own_ref if far == 0 else mine
        if far:
            send.arrived(condition, mine, z_sems.at[line])
        if side >= 0:
            send.start(both(condition, z > 0), src, mine, z_sems.at[line], z=z - 1)
        if side <= 0:
            send.start(both(condition, z < lines - 1), src, mine, z_sems.at[line], z=z + 1)
        send.start(condition, src, mine, x_sems.at[line], seq=place.xn)
        send.start(condition, src, mine, y_sems.at[line], seq=place.yn)
        send.start(condition, src, mine, sib_sems.at[0, line], seq=place.sib)

    def pass_on(index):
        condition, line, _, _ = events[index]
        from_x, from_y = unit(line, place.xn), unit(line, place.yn)
        send.arrived(condition, from_x, x_sems.at[line])
        part = unit(line, place.xn, half, half)
        send.start(condition, part, part, b_sems.at[line], seq=place.yn)
        send.start(condition, from_x, from_x, sib_sems.at[1, line], seq=place.sib)
        send.arrived(condition, from_y, y_sems.at[line])
        part = unit(line, place.yn, 0, half)
        send.start(condition, part, part, a_sems.at[line], seq=place.xn)
        send.start(condition, from_y, from_y, sib_sems.at[2, line], seq=place.sib)

    def corner(index):
        condition, line, _, _ = events[index]
        for group, begin, sems in ((3, 0, a_sems), (4, half, b_sems)):
            part = unit(line, place.dg, begin, half)
            send.arrived(condition, part, sems.at[line])
            send.start(condition, part, part, sib_sems.at[group, line], seq=place.sib)

    def row_block(seq):
        return rows_ref.at[pl.ds(pl.multiple_of(seq * tokens, tokens), tokens)]

    def middle(index):
        return pltpu.make_async_copy(
            wts_ref.at[:, pl.ds((3 + index) * dim, dim)], w_mid_ref.at[index], mid_sems.at[index]
        )

    obtain(0)
    own_rows = pltpu.make_async_copy(x_ref.at[place.chip], row_block(me), local_sems.at[1])
    own_rows.start()
    others = (place.xn, place.yn, place.dg)
    for other in place.line():
        send.start(None, norm_ref, small_ref.at[z], norm_sems.at[z], z=other)
    small_ref[z] = norm_ref[...]
    send.start(None, x_ref.at[place.chip], row_block(me), row_sems.at[me], seq=place.sib)
    for other in others:
        send.start(None, x_ref.at[other // 2], row_block(me), row_sems.at[me], seq=other)
    build_perm()
    near_load.wait()

    @pl.loop(0, near_p_ref.shape[0] // 512)
    def _(step):
        rows = rows_of(step, 512)
        near_p_ref[rows, :] = mm(near_p_ref[rows, :], perm_ref[...]).astype(bf16)

    obtain(1)
    obtain(2)
    pass_on(0)
    for other in others:
        send.arrived(None, row_block(other), row_sems.at[other])
        send.start(None, row_block(other), row_block(other), row_sems.at[other], seq=place.sib)
    obtain(3)
    obtain(4)
    cot_p_ref[...] = mm(cot_ref[...], perm_ref[...]).astype(bf16)
    cot_t_ref[...] = cot_p_ref[...].T
    pass_on(1)
    pass_on(2)
    corner(0)

    for other in place.line():
        send.arrived(None, small_ref.at[other], norm_sems.at[other])
    piece = small_ref.shape[2]
    total = None
    for line in range(lines):
        row = lax.broadcasted_iota(jnp.int32, (piece, dim), 0)
        column = lax.broadcasted_iota(jnp.int32, (piece, dim), 1)
        part = dim // lines
        place_of = jnp.logical_and(row < part, column == row + line * part).astype(bf16)
        term = mm(small_ref[line], place_of)
        total = term if total is None else total + term
    norms_ref[...] = total[: norms_ref.shape[0]]

    last = len(events)
    for index in range(5, last, 2):
        obtain(index)
        obtain(index + 1)
        if index == 5:
            for other in others:
                theirs = other + 1 - 2 * core
                send.arrived(None, row_block(theirs), row_sems.at[theirs])
            send.arrived(None, row_block(place.sib), row_sems.at[place.sib])
            own_rows.wait()
            norm_rows(rows_ref, norms_ref[...], perm_ref, hid_ref)
        pass_on(index - 2)
        pass_on(index - 1)
        corner(index - 4)
        corner(index - 3)
    for index in range(last - 2, last):
        pass_on(index)
    for index in range(last - 4, last):
        corner(index)
    keep.wait()
    for line in range(lines):
        for group, first in enumerate((me, place.xn, place.yn)):
            theirs = first + 1 - 2 * core
            send.arrived(None, unit(line, theirs), sib_sems.at[group, line])
        theirs = place.dg + 1 - 2 * core
        send.arrived(None, unit(line, theirs, 0, half), sib_sems.at[3, line])
        send.arrived(None, unit(line, theirs, half, half), sib_sems.at[4, line])
    copies = weight_copies(pairs, dim, wts_ref, w_qkv_ref, qkv_sems)
    for copy in copies + [middle(index) for index in (2, 3, 0, 1, 4)]:
        copy.start()
    for part in range(3):
        copies[part].wait()
        triple_part(part, pairs, hid_ref, w_qkv_ref, qkv_ref)

    share = lax.rem(me, dim // width)
    seq_rows = pl.ds(pl.multiple_of(place.chip * tokens, tokens), tokens)

    def landing(pair, chip_rows, share):
        lanes = pl.ds(pl.multiple_of(share * width + pair * LANES, LANES), LANES)
        return att_tok_ref.at[chip_rows, lanes]

    for pair in range(pairs):
        lanes = slice(pair * LANES, (pair + 1) * LANES)
        pair_forward(pair, pairs, qkv_ref, att_ref, lse_ref, lambda: None)
        for other in place.plane():
            block = att_ref.at[pl.ds(pl.multiple_of(other * tokens, tokens), tokens), lanes]
            to = landing(pair, seq_rows, share)
            send.start(None, block, to, att_sems.at[pair, me], seq=other)
        own_block = att_ref[pl.ds(pl.multiple_of(me * tokens, tokens), tokens), lanes]
        landing(pair, seq_rows, share)[...] = own_block

    for index in (2, 3, 0, 1, 4):
        middle(index).wait()
    for step in range(near_p_ref.shape[0] // 512):
        rows = slice(step * 512, (step + 1) * 512)
        near_kv_ref[rows, :dim] = mm(near_p_ref[rows, :], w_mid_ref[2]).astype(bf16)
        near_kv_ref[rows, dim:] = mm(near_p_ref[rows, :], w_mid_ref[3]).astype(bf16)
    w_out_ref, w_cq_ref, w_co_ref = (w_mid_ref.at[index] for index in (0, 1, 4))
    for pair in range(pairs):
        for other in place.plane():
            rows = pl.ds(pl.multiple_of(other // 2 * tokens, tokens), tokens)
            send.arrived(None, landing(pair, rows, lax.rem(other, 2)), att_sems.at[pair, other])
    att_p_ref[...] = mm(att_tok_ref[...], perm_ref[...]).astype(bf16)
    own_x = x_ref[...].reshape(first_ref.shape).astype(f32)
    first_ref[...] = own_x + mm(att_p_ref[...], w_out_ref[...])
    normed, _ = centre_scale(first_ref[...])
    hidden = (normed * norms_ref[2:3, :] + norms_ref[3:4, :]).astype(bf16)
    hid_p_ref[...] = mm(hidden, perm_ref[...]).astype(bf16)
    cross_q_ref[...] = mm(hid_p_ref[...], w_cq_ref[...]).astype(bf16)
    pl.loop(0, spans)(
        lambda span: span_forward(
            span, spans, neighbours, presence_ref, cross_q_ref, near_kv_ref, cross_ref
        )
    )

    ffw = (all_ref.shape[1] - 8 * dim) // 2
    tile = gfeed_ref.shape[2]
    order = range(0, ffw, tile)

    def tile_load(index):
        return [
            pltpu.make_async_copy(
                wts_ref.at[:, pl.ds(8 * dim + part * ffw + order[index], tile)],
                w_mid_ref.at[(2 * index + part) % 4],
                feed_sems.at[0, (2 * index + part) % 4],
            )
            for part in range(2)
        ]

    def tile_store(index):
        return [
            pltpu.make_async_copy(
                gfeed_ref.at[(2 * index + part) % 4],
                all_ref.at[:, pl.ds(8 * dim + part * ffw + order[index], tile)],
                feed_sems.at[1, (2 * index + part) % 4],
            )
            for part in range(2)
        ]

    for copy in tile_load(0) + tile_load(1):
        copy.start()
    co_p_ref[...] = mm(cross_ref[...], perm_ref[...]).astype(bf16)
    second_ref[...] = first_ref[...] + mm(co_p_ref[...], w_co_ref[...])
    normed, _ = centre_scale(second_ref[...])
    hidden = (normed * norms_ref[4:5, :] + norms_ref[5:6, :]).astype(bf16)
    up_p_ref[...] = mm(hidden, perm_ref[...]).astype(bf16)
    up_t_ref[...] = up_p_ref[...].T

    for index in range(len(order)):
        up_ref, down_ref = w_mid_ref.at[2 * index % 4], w_mid_ref.at[2 * index % 4 + 1]
        for copy in tile_load(index):
            copy.wait()
        if index >= 2:
            for copy in tile_store(index - 2):
                copy.wait()
        active, slope = gelu_parts(mm(up_p_ref[...], up_ref[...]))
        active = active.astype(bf16)
        term = nt(active, down_ref[...])
        result_ref[...] = term if index == 0 else result_ref[...] + term
        gfeed_ref[2 * index % 4 + 1] = mm(cot_t_ref[...], active).astype(bf16)
        grad_up = (mm(cot_p_ref[...], down_ref[...]) * slope).astype(bf16)
        gfeed_ref[2 * index % 4] = mm(up_t_ref[...], grad_up).astype(bf16)
        for copy in tile_store(index):
            copy.start()
        term = nt(grad_up, up_ref[...])
        back_ref[...] = term if index == 0 else back_ref[...] + term
        if index + 2 < len(order):
            for copy in tile_load(index + 2):
                copy.start()
        elif index + 2 == len(order):
            middle(0).start()
            middle(1).start()

    out_ref[...] = (second_ref[...] + nt(result_ref[...].astype(bf16), perm_ref[...])).astype(bf16)
    upstream = nt(back_ref[...].astype(bf16), perm_ref[...])
    normed, recip = centre_scale(second_ref[...])
    back, gain, shift = norm_back(upstream, normed, recip, norms_ref[4:5, :])
    gsecond_ref = second_ref
    gsecond_ref[...] = cot_ref[...].astype(f32) + back
    sums_ref[4:5, :] = gain
    sums_ref[5:6, :] = shift
    sums_ref[6:8, :] = jnp.zeros((2, dim), f32)
    for index in range(len(order) - 2, len(order)):
        for copy in tile_store(index):
            copy.wait()

    gco_ref, gcq_ref, gatt_tok_ref = up_p_ref, cot_p_ref, cross_ref
    outs = []

    def store(slot, part, first):
        copy = pltpu.make_async_copy(
            part, all_ref.at[:, pl.ds(first, part.shape[1])], feed_sems.at[1, slot]
        )
        outs.append(copy)
        copy.start()

    def keep_grad(index, value):
        slot = len(outs) % 4
        if len(outs) >= 4:
            outs[-4].wait()
        gfeed_ref[slot] = value.astype(bf16)
        store(slot, gfeed_ref.at[slot], (3 + index) * dim)

    upper = gsecond_ref[...].astype(bf16)
    gco_ref[...] = nt(nt(upper, w_co_ref[...]).astype(bf16), perm_ref[...]).astype(bf16)
    tables = (presence_ref, cross_q_ref, gco_ref, near_kv_ref, gcq_ref, near_kv_ref)
    pl.loop(0, spans)(lambda span: span_backward(span, spans, neighbours, *tables))
    for index in (0, 1):
        middle(index).wait()
    upstream = nt(nt(gcq_ref[...], w_cq_ref[...]).astype(bf16), perm_ref[...])
    normed, recip = centre_scale(first_ref[...])
    back, gain, shift = norm_back(upstream, normed, recip, norms_ref[2:3, :])
    sums_ref[2:3, :] = gain
    sums_ref[3:4, :] = shift
    gfirst_ref = gsecond_ref
    gfirst_ref[...] = gsecond_ref[...] + back
    lower = gfirst_ref[...].astype(bf16)
    gatt_tok_ref[...] = nt(nt(lower, w_out_ref[...]).astype(bf16), perm_ref[...]).astype(bf16)

    def gatt_block(device):
        return gatt_tok_ref.at[
            pl.ds(pl.multiple_of(device // 2 * tokens, tokens), tokens),
            pl.ds(pl.multiple_of(lax.rem(device, 2) * width, width), width),
        ]

    def gatt_rows(device):
        return gatt_ref.at[pl.ds(pl.multiple_of(device * tokens, tokens), tokens)]

    for other in place.plane():
        send.start(None, gatt_block(other), gatt_rows(me), gatt_sems.at[me], seq=other)
    own_gatt = pltpu.make_async_copy(gatt_block(me), gatt_rows(me), gatt_sems.at[me])
    own_gatt.start()
    keep_grad(4, mm(co_p_ref[...].T, upper))
    near_t = near_p_ref[...].T
    for part in range(2):
        keep_grad(2 + part, mm(near_t, near_kv_ref[:, part * dim : (part + 1) * dim]))
    keep_grad(1, mm(hid_p_ref[...].T, gcq_ref[...]))
    keep_grad(0, mm(att_p_ref[...].T, lower))
    for other in place.plane():
        send.arrived(None, gatt_rows(other), gatt_sems.at[other])
    own_gatt.wait()

    send.finish()
    grad_ref = near_kv_ref.at[pl.ds(0, length), pl.ds(0, 3 * width)]
    ghid_ref = rows_ref
    attention = (qkv_ref, att_ref, gatt_ref, lse_ref, grad_ref, acc_ref)
    pl.loop(0, pairs)(lambda pair: pair_backward(pair, pairs, *attention, lambda: None))
    for begin in range(0, length, 256):
        rows = slice(begin, begin + 256)
        ghid_ref[rows, :] = nt(grad_ref[rows, :], w_qkv_ref[...]).astype(bf16)
    chips = (place.xn // 2, place.yn // 2, place.dg // 2, place.chip)

    def token_rows(device):
        return pl.ds(pl.multiple_of(device * tokens, tokens), tokens)

    for chip in chips:
        theirs = ghid_ref.at[token_rows(chip * 2 + 1 - core)]
        send.start(None, theirs, gsib_ref.at[chip], gsib_sems.at[chip], seq=place.sib)

    for copy in outs[-4:]:
        copy.wait()
    outs.clear()
    gfeed_ref[3] = jnp.zeros_like(gfeed_ref[3])
    share_count = dim // width
    zeros = [
        pltpu.make_async_copy(
            gfeed_ref.at[3, :, pl.ds(0, width)],
            all_ref.at[
                :,
                pl.ds(
                    pl.multiple_of(part * dim + lax.rem(share + other, share_count) * width, LANES),
                    width,
                ),
            ],
            mid_sems.at[2 + part],
        )
        for part in range(3)
        for other in range(1, share_count)
    ]
    for copy in zeros:
        copy.start()
    hidden_t = hid_ref[...].T

    def triple_grad(part):
        columns = slice(part * width, (part + 1) * width)
        gfeed_ref[part, :, :width] = mm(hidden_t, grad_ref[:, columns]).astype(bf16)
        first = pl.multiple_of(part * dim + share * width, LANES)
        store(part, gfeed_ref.at[part, :, pl.ds(0, width)], first)

    triple_grad(0)
    triple_grad(1)
    for chip in chips:
        send.arrived(None, gsib_ref.at[chip], gsib_sems.at[chip])
        rows = token_rows(chip * 2 + core)
        total = (ghid_ref[rows, :].astype(f32) + gsib_ref[chip].astype(f32)).astype(bf16)
        if chip is place.chip:
            parts_ref[chip] = total
        else:
            ghid_ref[rows, :] = total
            landed, sem = parts_ref.at[place.chip], part_sems.at[place.chip]
            send.start(None, ghid_ref.at[rows], landed, sem, seq=chip * 2 + core)
    triple_grad(2)
    for chip in chips[:3]:
        send.arrived(None, parts_ref.at[chip], part_sems.at[chip])
    gain_sum = shift_sum = None
    for chip in range(4):
        rows = slice(chip * tokens, (chip + 1) * tokens)
        upstream = nt(parts_ref[chip], perm_ref[...])
        normed, recip = centre_scale(x_ref[chip].astype(f32))
        back, gain, shift = norm_back(upstream, normed, recip, norms_ref[0:1, :])
        gfirst_ref[rows, :] += back
        gain_sum = gain if gain_sum is None else gain_sum + gain
        shift_sum = shift if shift_sum is None else shift_sum + shift
    leave = pltpu.make_async_copy(gfirst_ref, gin_ref, local_sems.at[0])
    leave.start()
    sums_ref[0:1, :] = gain_sum
    sums_ref[1:2, :] = shift_sum
    for copy in outs + zeros:
        copy.wait()
    leave.wait()
    send.finish()


def layer(lines, pairs, spans, neighbours, presence, w_shard, n_shard, inputs, order, cot, near):
    unit_rows, unit_cols = w_shard.shape
    seqs, tokens, dim = inputs.shape
    count, length, width = seqs * tokens, 8 * tokens, pairs * LANES
    rows_near = near.shape[0]
    events = 2 * lines - 1
    any_space = pl.BlockSpec(memory_space=pl.ANY)
    vmem = pl.BlockSpec(memory_space=pltpu.VMEM)
    dma = pltpu.SemaphoreType.DMA
    packed = jax.ShapeDtypeStruct((unit_rows * lines, unit_cols * 8), bf16)
    tile = unit_cols // 2
    tokens_rows = (count, dim)
    scratch = [
        ((length, dim), bf16),
        ((3 * pairs, length, LANES), bf16),
        ((length, width), bf16),
        ((pairs, 2, length), f32),
        (tokens_rows, bf16),
        (tokens_rows, f32),
        (tokens_rows, bf16),
        (tokens_rows, bf16),
        ((rows_near, dim), bf16),
        ((rows_near, 2 * dim), bf16),
        (tokens_rows, bf16),
        (tokens_rows, f32),
        ((unit_rows, unit_cols), bf16),
        ((lines,) + n_shard.shape, bf16),
        ((length, dim), bf16),
        ((dim, 3 * width), bf16),
        ((5, dim, dim), bf16),
        (tokens_rows, bf16),
        (tokens_rows, bf16),
        (tokens_rows, bf16),
        ((dim, count), bf16),
        (tokens_rows, bf16),
        ((dim, count), bf16),
        (tokens_rows, f32),
        (tokens_rows, f32),
        ((4, dim, tile), bf16),
        ((dim, dim), bf16),
        ((8, dim), f32),
        ((length, width), bf16),
        ((2, length, LANES), f32),
        ((4, tokens, dim), bf16),
        ((4, tokens, dim), bf16),
    ]
    return pl.pallas_call(
        partial(layer_kernel, lines, pairs, spans, neighbours),
        out_shape=(
            packed,
            packed,
            jax.ShapeDtypeStruct(tokens_rows, bf16),
            jax.ShapeDtypeStruct(tokens_rows, f32),
            jax.ShapeDtypeStruct((8, dim), f32),
        ),
        in_specs=[pl.BlockSpec(memory_space=pltpu.SMEM)] + [vmem] * 5 + [any_space],
        out_specs=(any_space, any_space, vmem, any_space, vmem),
        scratch_shapes=[pltpu.VMEM(*entry) for entry in scratch]
        + [
            dma((11 * events + 7 + lines + 7 * pairs + 16,)),
            dma((lines,)),
            dma((lines,)),
            dma((lines,)),
            dma((lines,)),
            dma((lines,)),
            dma((5, lines)),
            dma((lines,)),
            dma((8,)),
            dma((pairs, 8)),
            dma((3,)),
            dma((3,)),
            dma((5,)),
            dma((2, 4)),
            dma((8,)),
            dma((4,)),
            dma((4,)),
        ],
        compiler_params=pltpu.CompilerParams(
            vmem_limit_bytes=VMEM_BYTES, collective_id=1, has_side_effects=True
        ),
        name="layer",
    )(presence, w_shard, n_shard, inputs, order, cot, near)


def reduce_kernel(
    lines,
    grads_ref,
    small_ref,
    shard_ref,
    norms_ref,
    mine_ref,
    sib_ref,
    corner_a_ref,
    corner_b_ref,
    from_x_ref,
    from_y_ref,
    below_ref,
    above_ref,
    early_below_ref,
    early_above_ref,
    plane_ref,
    plane_sum_ref,
    line_ref,
    send_sems,
    load_sems,
    sib_sems,
    a_sems,
    b_sems,
    x_sems,
    y_sems,
    below_sems,
    above_sems,
    early_below_sems,
    early_above_sems,
    plane_sems,
    line_sems,
):
    place = Place(lines)
    z, me = place.z, place.me
    unit_rows, unit_cols = shard_ref.shape
    tile = 16
    early = early_below_ref.shape[2]
    place.meet()
    send = Sender(place, send_sems)
    chips = (place.dg, place.yn, place.xn, me)
    corner, over_y, over_x, here = range(4)

    unit = partial(unit_of, grads_ref, lines)

    def load(which, line):
        return pltpu.make_async_copy(
            unit(line, chips[which]), mine_ref.at[which, line], load_sems.at[which, line]
        )

    for other in place.plane():
        send.start(None, small_ref, plane_ref.at[me], plane_sems.at[me], seq=other)
    plane_ref[me] = small_ref[...]

    events = place.events()[::-1]

    def begin(index):
        condition, line, _, _ = events[index]
        for which in range(4):
            theirs = chips[which] + 1 - 2 * place.core
            send.start(
                condition,
                unit(line, theirs),
                sib_ref.at[which, line],
                sib_sems.at[which, line],
                seq=place.sib,
            )
            when(condition, load(which, line).start)

    def parts(far):
        low = early if far else 0
        return low, (low + unit_rows) // 2

    def add(target, *terms, begin=0, end=unit_rows):
        @pl.loop(0, (end - begin) // tile)
        def _(step):
            rows = pl.ds(pl.multiple_of(begin + step * tile, tile), tile)
            if len(terms) == 1:
                ref, first = terms[0]
                at = pl.ds(pl.multiple_of(begin - first + step * tile, tile), tile)
                target[rows, :] = target[rows, :] + ref[at, :]
            else:
                total = target[rows, :].astype(f32)
                for ref, first in terms:
                    at = pl.ds(pl.multiple_of(begin - first + step * tile, tile), tile)
                    total = total + ref[at, :].astype(f32)
                target[rows, :] = total.astype(target.dtype)

    def early_rows(line):
        return mine_ref.at[:, line, pl.ds(0, early), :]

    def add_early(line, landing):
        for which in range(4):
            add(mine_ref.at[which, line], (landing.at[line, which], 0), end=early)

    def first(index):
        condition, line, far, side = events[index]
        low, middle = parts(far)
        for which in range(4):
            send.arrived(condition, sib_ref.at[which, line], sib_sems.at[which, line])
            when(condition, load(which, line).wait)

        def chip_sum():
            for which in range(4):
                add(mine_ref.at[which, line], (sib_ref.at[which, line], 0))

        when(condition, chip_sum)
        from_below, from_above = both(condition, z > 0), both(condition, z < lines - 1)
        sides = ((from_below, early_below_ref, early_below_sems),) if side >= 0 else ()
        if side <= 0:
            sides += ((from_above, early_above_ref, early_above_sems),)
        for on, landing, sems in sides:
            send.arrived(on, landing.at[line], sems.at[line])
            when(on, partial(add_early, line, landing))
        if far:
            landing, sems = sides[0][1:]
            send.start(condition, early_rows(line), landing.at[line], sems.at[line], z=z + side)
        target = mine_ref.at[corner, line]
        for begins, ends, landing, sems, to in (
            (low, middle, corner_a_ref, a_sems, place.xn),
            (middle, unit_rows, corner_b_ref, b_sems, place.yn),
        ):
            send.start(
                condition,
                target.at[pl.ds(begins, ends - begins)],
                landing.at[line, pl.ds(0, ends - begins)],
                sems.at[line],
                seq=to,
            )

    def second(index):
        condition, line, far, _ = events[index]
        low, middle = parts(far)
        size = unit_rows - low
        for which, part, sems, begins, ends, to, landing, landing_sems in (
            (over_y, corner_a_ref, a_sems, low, middle, place.yn, from_y_ref, y_sems),
            (over_x, corner_b_ref, b_sems, middle, unit_rows, place.xn, from_x_ref, x_sems),
        ):
            arrived = part.at[line, pl.ds(0, ends - begins)]
            send.arrived(condition, arrived, sems.at[line])
            target = mine_ref.at[which, line]
            when(
                condition,
                partial(add, target, (part.at[line], begins), begin=begins, end=ends),
            )
            send.start(
                condition,
                target.at[pl.ds(low, size)],
                landing.at[line, pl.ds(low, size)],
                landing_sems.at[line],
                seq=to,
            )

    def third(index):
        condition, line, far, side = events[index]
        low, _ = parts(far)
        late = pl.ds(low, unit_rows - low)
        send.arrived(condition, from_x_ref.at[line, late], x_sems.at[line])
        send.arrived(condition, from_y_ref.at[line, late], y_sems.at[line])
        target = mine_ref.at[here, line]
        terms = [(from_x_ref.at[line], 0), (from_y_ref.at[line], 0)]
        if side == 0:
            has_below, has_above = z > 0, z < lines - 1
            late = pl.ds(early, unit_rows - early)

            @pl.loop(0, unit_rows // tile)
            def _(step):
                rows = rows_of(step, tile)
                total = target[rows, :].astype(f32)
                for ref, _ in terms:
                    total = total + ref[rows, :].astype(f32)
                shard_ref[rows, :] = total

            for on, ref, sems in (
                (has_below, below_ref, below_sems),
                (has_above, above_ref, above_sems),
            ):
                send.arrived(on, ref.at[line, late], sems.at[line])
                when(on, partial(add, shard_ref, (ref.at[line], 0), begin=early))
            return
        landing, sems = (below_ref, below_sems) if side > 0 else (above_ref, above_sems)
        more = both(condition, z > 0) if side > 0 else both(condition, z < lines - 1)
        none = both(condition, z == 0) if side > 0 else both(condition, z == lines - 1)
        send.arrived(more, landing.at[line, late], sems.at[line])
        when(more, partial(add, target, *terms, (landing.at[line], 0), begin=low))
        when(none, partial(add, target, *terms, begin=low))
        send.start(
            condition, target.at[late], landing.at[line, late], sems.at[line], z=z + side
        )

    count = len(events)
    for index in range(min(4, count)):
        begin(index)
    first(0)
    first(1)
    for index in range(2, count + 4):
        if index + 2 < count:
            begin(index + 2)
        if index < count:
            first(index)
        if 0 <= index - 2 < count:
            second(index - 2)
        if index == 3:
            for other in place.plane():
                send.arrived(None, plane_ref.at[other], plane_sems.at[other])
            total = plane_ref[0]
            for other in range(1, 8):
                total = total + plane_ref[other]
            plane_sum_ref[...] = total
            line_ref[z] = total
            for other in place.line():
                send.start(None, plane_sum_ref, line_ref.at[z], line_sems.at[z], z=other)
        if 0 <= index - 4 < count:
            third(index - 4)

    for other in place.line():
        send.arrived(None, line_ref.at[other], line_sems.at[other])
    total = line_ref[0]
    for other in range(1, lines):
        total = total + line_ref[other]
    norms_ref[...] = total
    send.finish()


def reduce_grads(lines, grads, small):
    rows, cols = grads.shape
    unit_rows, unit_cols = rows // lines, cols // 8
    half = unit_rows // 2
    early = unit_rows // 96 * 16
    any_space = pl.BlockSpec(memory_space=pl.ANY)
    vmem = pl.BlockSpec(memory_space=pltpu.VMEM)
    dma = pltpu.SemaphoreType.DMA
    return pl.pallas_call(
        partial(reduce_kernel, lines),
        out_shape=(
            jax.ShapeDtypeStruct((unit_rows, unit_cols), f32),
            jax.ShapeDtypeStruct(small.shape, f32),
        ),
        in_specs=[any_space, vmem],
        out_specs=(vmem, vmem),
        scratch_shapes=[
            pltpu.VMEM((4, lines, unit_rows, unit_cols), bf16),
            pltpu.VMEM((4, lines, unit_rows, unit_cols), bf16),
            pltpu.VMEM((lines, half, unit_cols), bf16),
            pltpu.VMEM((lines, half, unit_cols), bf16),
            pltpu.VMEM((lines, unit_rows, unit_cols), bf16),
            pltpu.VMEM((lines, unit_rows, unit_cols), bf16),
            pltpu.VMEM((lines, unit_rows, unit_cols), bf16),
            pltpu.VMEM((lines, unit_rows, unit_cols), bf16),
            pltpu.VMEM((lines, 4, early, unit_cols), bf16),
            pltpu.VMEM((lines, 4, early, unit_cols), bf16),
            pltpu.VMEM((8,) + small.shape, f32),
            pltpu.VMEM(small.shape, f32),
            pltpu.VMEM((lines,) + small.shape, f32),
            dma((10 * (2 * lines - 1) + 7 + lines,)),
            dma((4, lines)),
            dma((4, lines)),
            dma((lines,)),
            dma((lines,)),
            dma((lines,)),
            dma((lines,)),
            dma((lines,)),
            dma((lines,)),
            dma((lines,)),
            dma((lines,)),
            dma((8,)),
            dma((lines,)),
        ],
        compiler_params=pltpu.CompilerParams(
            vmem_limit_bytes=VMEM_BYTES, collective_id=4, has_side_effects=True
        ),
        name="reduce_grads",
    )(grads, small)


def adam_update(grad, weight, first, second, average, rate, decay):
    first = beta_first * first + (1.0 - beta_first) * grad
    second = beta_second * second + (1.0 - beta_second) * grad * grad
    stepped = (
        first / (1.0 - beta_first**STEP) / (jnp.sqrt(second / (1.0 - beta_second**STEP)) + adam_eps)
    )
    weight = weight - rate * (stepped + decay * weight)
    average = ema_decay * average + (1.0 - ema_decay) * weight
    return (first, second, weight, average)


def on_device(
    inputs,
    cotangent,
    neighbours,
    presence,
    row_order,
    w_master,
    w_first,
    w_second,
    w_average,
    n_master,
    n_first,
    n_second,
    n_average,
):
    seqs, tokens, dim = inputs.shape
    heads = dim // HEAD
    devices = lax.axis_size("seq")
    count = seqs * tokens
    length = devices * tokens
    me = lax.axis_index("seq")
    shares = devices // seqs
    held = heads // shares
    pairs = (held + 1) // 2
    width = pairs * LANES
    spare = width - held * HEAD
    sequence, share = me // shares, me % shares

    lines = lax.axis_size("dp")
    planar = devices == 8 and seqs == 4 and spare == 0
    x = inputs.reshape(count, dim)
    cot = cotangent.reshape(count, dim)
    spans = seqs * neighbours.shape[1]
    each = neighbours.shape[2]
    near = neighbours.reshape(-1, dim)
    live = presence.reshape(-1)
    part = n_master.shape[1]
    if planar:
        small = jnp.pad(n_master.astype(bf16), ((0, 16 - 6), (0, -part % LANES)))
        order = row_order.reshape(1, dim)
        _, grads, outputs, grad_inputs, norm_grads = layer(
            lines, pairs, spans, each, live, w_master, small, inputs, order, cot, near
        )
        grad_shard, norm_sums = reduce_grads(lines, grads, norm_grads)
        norm_shard = lax.dynamic_slice(norm_sums, (0, lax.axis_index("dp") * part), (6, part))
    else:
        perm = (jnp.arange(dim)[:, None] == row_order[None, :]).astype(bf16)
        perm_att = jnp.pad(perm.reshape(shares, held * HEAD, dim), ((0, 0), (0, spare), (0, 0)))
        perm_att = perm_att.reshape(shares * width, dim)
        weights = lax.all_gather(w_master.astype(bf16), "dp", axis=0, tiled=True)
        weights = lax.all_gather(weights, "seq", axis=1, tiled=True)
        norms = lax.all_gather(n_master.astype(bf16), "dp", axis=1, tiled=True).astype(f32)
        rows = lax.all_to_all(jnp.repeat(inputs, shares, axis=0), "seq", 0, 0)
        rows = rows.reshape(length, dim)
        w_qkv = weights[:, : 3 * dim].reshape(dim, 3, shares, held * HEAD)
        w_qkv = lax.dynamic_index_in_dim(w_qkv, share, axis=2, keepdims=False)
        w_qkv = jnp.pad(w_qkv, ((0, 0), (0, 0), (0, spare))).reshape(dim, 3 * width)
        hid, qkv, att, lse = self_forward(pairs, rows, norms, perm, w_qkv)
        att_tok = (
            lax.all_to_all(att.reshape(devices, tokens, width), "seq", 0, 0)
            .reshape(seqs, shares, tokens, width)
            .transpose(0, 2, 1, 3)
            .reshape(count, shares * width)
        )
        att_p, first, hid_p, cross_q, near_p, near_kv, co_p, second = cross_forward(
            spans, each, live, att_tok, x, norms, perm, perm_att, near, weights
        )
        outputs, gsecond, grads, gnorm_e = feed(second, cot, norms, perm, weights)
        gfirst, gatt_tok, grads, gnorm_c = cross_backward(
            spans,
            each,
            live,
            gsecond,
            first,
            norms,
            perm,
            perm_att,
            att_p,
            hid_p,
            cross_q,
            near_p,
            near_kv,
            co_p,
            weights,
            grads,
        )
        gatt = lax.all_to_all(
            gatt_tok.reshape(seqs, tokens, shares, width)
            .transpose(0, 2, 1, 3)
            .reshape(devices, tokens, width),
            "seq",
            0,
            0,
        ).reshape(length, width)
        gqkv, ghid = self_backward(pairs, qkv, att, gatt, lse, hid, w_qkv)
        parts = (
            lax.all_to_all(ghid.reshape(devices, tokens, dim), "seq", 0, 0)
            .reshape(seqs, shares, tokens, dim)
            .transpose(1, 0, 2, 3)
            .reshape(shares, count, dim)
        )
        grad_inputs, gnorm_a = last_norm(parts, x, gfirst, norms, perm)
        gqkv = gqkv.reshape(dim, 3, 1, width)[..., : held * HEAD]
        gqkv = jnp.where(jnp.arange(shares)[:, None] == share, gqkv, jnp.zeros_like(gqkv))
        grads = lax.dynamic_update_slice(grads, gqkv.reshape(dim, 3 * dim), (0, 0))
        norm_grads = lax.psum(jnp.concatenate([gnorm_a, gnorm_c, gnorm_e], axis=0), "seq")
        partial_sum = lax.psum_scatter(grads, "seq", scatter_dimension=1, tiled=True)
        grad_shard = lax.psum_scatter(partial_sum, "dp", scatter_dimension=0, tiled=True)
        grad_shard = grad_shard.astype(f32)
        norm_shard = lax.psum_scatter(
            norm_grads.astype(bf16), "dp", scatter_dimension=1, tiled=True
        ).astype(f32)
    w_first_new, w_second_new, w_new, w_average_new = adam_update(
        grad_shard, w_master, w_first, w_second, w_average, learn_rate, weight_decay
    )
    n_first_new, n_second_new, n_new, n_average_new = adam_update(
        norm_shard, n_master, n_first, n_second, n_average, norm_rate, 0.0
    )
    return (
        outputs.reshape(seqs, tokens, dim),
        grad_inputs.reshape(seqs, tokens, dim),
        w_first_new,
        w_second_new,
        w_new,
        w_average_new,
        n_first_new,
        n_second_new,
        n_new,
        n_average_new,
    )


def solution(mesh):
    in_specs = (
        P("dp", "seq", None),
        P("dp", "seq", None),
        P("dp", "seq", None, None, None),
        P("dp", "seq", None),
        P(),
        P("dp", "seq"),
        P("dp", "seq"),
        P("dp", "seq"),
        P("dp", "seq"),
        P(None, "dp"),
        P(None, "dp"),
        P(None, "dp"),
        P(None, "dp"),
    )
    out_specs = (
        P("dp", "seq", None),
        P("dp", "seq", None),
        P("dp", "seq"),
        P("dp", "seq"),
        P("dp", "seq"),
        P("dp", "seq"),
        P(None, "dp"),
        P(None, "dp"),
        P(None, "dp"),
        P(None, "dp"),
    )
    return jax.shard_map(
        on_device, mesh=mesh, in_specs=in_specs, out_specs=out_specs, check_vma=False
    )
```

```python
from functools import partial

import jax
import jax.numpy as jnp
from jax import lax
from jax.experimental import pallas as pl
from jax.experimental.pallas import tpu as pltpu
from jax.sharding import PartitionSpec as P

HEAD = 64
STEP = 5
LANES = 128
SCALE = HEAD ** (-0.5)

beta_first = 0.9
beta_second = 0.95
adam_eps = 1e-08
learn_rate = 0.04
norm_rate = 0.6
weight_decay = 0.1
ema_decay = 0.5
norm_eps = 1e-05
masked_score = -1e30
VMEM_BYTES = 62 * 1024 * 1024
bf16 = jnp.bfloat16
f32 = jnp.float32


def mm(left, right):
    return lax.dot_general(left, right, (((1,), (0,)), ((), ())), preferred_element_type=f32)


def nt(left, right):
    return lax.dot_general(left, right, (((1,), (1,)), ((), ())), preferred_element_type=f32)


def tn(left, right):
    return lax.dot_general(left, right, (((0,), (0,)), ((), ())), preferred_element_type=f32)


def params():
    return pltpu.CompilerParams(vmem_limit_bytes=VMEM_BYTES)


def rows_of(index, size):
    return pl.ds(pl.multiple_of(index * size, size), size)


def centre_scale(values):
    centre = jnp.mean(values, axis=-1, keepdims=True)
    centred = values - centre
    spread = jnp.mean(centred * centred, axis=-1, keepdims=True)
    recip = lax.rsqrt(spread + norm_eps)
    return centred * recip, recip


def norm_back(upstream, normed, recip, gain):
    scaled = upstream * gain
    inner = (
        scaled
        - jnp.mean(scaled, axis=-1, keepdims=True)
        - normed * jnp.mean(scaled * normed, axis=-1, keepdims=True)
    )
    return (
        recip * inner,
        jnp.sum(upstream * normed, axis=0, keepdims=True),
        jnp.sum(upstream, axis=0, keepdims=True),
    )


def gelu_parts(value):
    const = 0.7978845608028654
    square = value * value
    bend = jnp.tanh(const * value * (1.0 + 0.044715 * square))
    half = 0.5 * (1.0 + bend)
    slope = half + 0.5 * value * (1.0 - bend * bend) * (const * (1.0 + 3 * 0.044715 * square))
    return value * half, slope


def head_mask(rows, half):
    lane = lax.broadcasted_iota(jnp.int32, (rows, LANES), 1)
    return (lane < HEAD) if half == 0 else (lane >= HEAD)


def pick(mask, value):
    return jnp.where(mask, value, jnp.zeros_like(value))


MESH = pl.DeviceIdType.MESH


class Place:
    def __init__(self, lines):
        self.lines = lines
        self.z = lax.axis_index("dp")
        self.me = lax.axis_index("seq")
        core, x, y = self.me % 2, (self.me // 2) % 2, self.me // 4
        self.core, self.x, self.y, self.chip = core, x, y, self.me // 2
        self.sib = self.me + 1 - 2 * core
        self.xn = self.me + 2 - 4 * x
        self.yn = self.me + 4 - 8 * y
        self.dg = self.xn + 4 - 8 * y

    def events(self):
        found = [(None, self.z, 0, 0)]
        for far in range(1, self.lines):
            found.append((self.z >= far, self.z - far, far, -1))
            found.append((self.z + far < self.lines, self.z + far, far, 1))
        return found

    def plane(self):
        return [lax.rem(self.me + step, 8) for step in range(1, 8)]

    def line(self):
        return [lax.rem(self.z + step, self.lines) for step in range(1, self.lines)]

    def meet(self):
        barrier = pltpu.get_barrier_semaphore()
        for other in self.plane():
            pl.semaphore_signal(
                barrier, inc=1, device_id={"dp": self.z, "seq": other}, device_id_type=MESH
            )
        for other in self.line():
            pl.semaphore_signal(
                barrier, inc=1, device_id={"dp": other, "seq": self.me}, device_id_type=MESH
            )
        pl.semaphore_wait(barrier, 7 + self.lines - 1)


def when(condition, body):
    if condition is None:
        body()
    else:
        pl.when(condition)(body)


def both(first, second):
    if first is None or second is None:
        return second if first is None else first
    return jnp.logical_and(first, second)


class Sender:
    def __init__(self, place, send_sems):
        self.place, self.sems, self.open, self.count = place, send_sems, [], 0

    def start(self, condition, src, dst, recv_sem, z=None, seq=None):
        place = self.place
        target = {"dp": place.z if z is None else z, "seq": place.me if seq is None else seq}
        copy = pltpu.make_async_remote_copy(
            src_ref=src,
            dst_ref=dst,
            send_sem=self.sems.at[self.count],
            recv_sem=recv_sem,
            device_id=target,
            device_id_type=MESH,
        )
        self.open.append((condition, copy))
        self.count += 1
        when(condition, copy.start)

    def arrived(self, condition, ref, recv_sem):
        copy = pltpu.make_async_remote_copy(
            src_ref=ref,
            dst_ref=ref,
            send_sem=self.sems.at[0],
            recv_sem=recv_sem,
            device_id={"dp": self.place.z, "seq": self.place.sib},
            device_id_type=MESH,
        )
        when(condition, copy.wait_recv)

    def finish(self):
        for condition, copy in self.open:
            when(condition, copy.wait_send)
        self.open = []


class Weave:
    def __init__(self, steps):
        self.steps = list(steps)

    def some(self, count):
        for _ in range(min(count, len(self.steps))):
            self.steps.pop(0)()

    def rest(self):
        self.some(len(self.steps))


def unit_of(ref, lines, line, seq, begin=0, size=None):
    rows, cols = ref.shape[0] // lines, ref.shape[1] // 8
    size = rows if size is None else size
    return ref.at[
        pl.ds(pl.multiple_of(line * rows + begin, 16), size),
        pl.ds(pl.multiple_of(seq * cols, cols), cols),
    ]


def weight_copies(pairs, dim, wts_ref, w_ref, sems):
    width = pairs * LANES
    first = lax.rem(lax.axis_index("seq"), dim // width) * width
    return [
        pltpu.make_async_copy(
            wts_ref.at[:, pl.ds(pl.multiple_of(first + part * dim, LANES), width)],
            w_ref.at[:, pl.ds(part * width, width)],
            sems.at[part],
        )
        for part in range(3)
    ]


def pair_forward(pair, pairs, qkv_ref, att_ref, lse_ref, between):
    length = att_ref.shape[0]
    tile = 256
    below = lax.broadcasted_iota(jnp.int32, (tile, tile), 1) <= lax.broadcasted_iota(
        jnp.int32, (tile, tile), 0
    )
    masks = [head_mask(tile, 0), head_mask(tile, 1)]
    lane = lax.broadcasted_iota(jnp.int32, (tile, LANES), 1)
    for step in range(length // tile):
        rows = slice(step * tile, (step + 1) * tile)
        query = qkv_ref[pair, rows, :] * SCALE
        keys_here = qkv_ref[pairs + pair, rows, :]
        values_here = qkv_ref[2 * pairs + pair, rows, :]
        outs, logs = [], []
        for half in range(2):
            mine = pick(masks[half], query)
            here = jnp.where(below, nt(mine, keys_here), masked_score)
            peak = jnp.max(here, axis=-1, keepdims=True)
            if step:
                past = nt(mine, qkv_ref[pairs + pair, : step * tile, :])
                peak = jnp.maximum(peak, jnp.max(past, axis=-1, keepdims=True))
                past = jnp.exp(past - peak)
            here = jnp.exp(here - peak)
            total = jnp.sum(here, axis=-1, keepdims=True)
            out = mm(here.astype(bf16), values_here)
            if step:
                total = total + jnp.sum(past, axis=-1, keepdims=True)
                out = out + mm(past.astype(bf16), qkv_ref[2 * pairs + pair, : step * tile, :])
            outs.append(out / total)
            logs.append(peak + jnp.log(total))
        lse_ref[pair, :, rows] = jnp.where(lane == 0, logs[0], logs[1]).T[0:2, :]
        att_ref[rows, pl.ds(pl.multiple_of(pair * LANES, LANES), LANES)] = jnp.where(
            masks[0], outs[0], outs[1]
        ).astype(bf16)
        between()


def norm_rows(x_ref, norms, perm_ref, hid_ref):
    tile = 256

    @pl.loop(0, x_ref.shape[0] // tile)
    def _(step):
        rows = rows_of(step, tile)
        normed, _ = centre_scale(x_ref[rows, :].astype(f32))
        hidden = (normed * norms[0:1, :] + norms[1:2, :]).astype(bf16)
        hid_ref[rows, :] = mm(hidden, perm_ref[...]).astype(bf16)


def triple_part(part, pairs, hid_ref, w_ref, qkv_ref):
    width = pairs * LANES
    triple = mm(hid_ref[...], w_ref[:, part * width : (part + 1) * width]).astype(bf16)
    for pair in range(pairs):
        qkv_ref[part * pairs + pair] = triple[:, pair * LANES : (pair + 1) * LANES]


def self_forward_kernel(
    pairs, x_ref, norms_ref, perm_ref, w_ref, hid_ref, qkv_ref, att_ref, lse_ref
):
    norm_rows(x_ref, norms_ref, perm_ref, hid_ref)
    for part in range(3):
        triple_part(part, pairs, hid_ref, w_ref, qkv_ref)

    @pl.loop(0, pairs)
    def _(pair):
        pair_forward(pair, pairs, qkv_ref, att_ref, lse_ref, lambda: None)


def self_forward(pairs, x, norms, perm, w):
    length, dim = x.shape
    return pl.pallas_call(
        partial(self_forward_kernel, pairs),
        out_shape=(
            jax.ShapeDtypeStruct((length, dim), bf16),
            jax.ShapeDtypeStruct((3 * pairs, length, LANES), bf16),
            jax.ShapeDtypeStruct((length, pairs * LANES), bf16),
            jax.ShapeDtypeStruct((pairs, 2, length), f32),
        ),
        compiler_params=params(),
        name="self_forward",
    )(x, norms, perm, w)


def pair_backward(pair, pairs, qkv_ref, att_ref, gatt_ref, lse_ref, grad_ref, acc_ref, between):
    length = att_ref.shape[0]
    width = pairs * LANES
    tile = 256
    above = lax.broadcasted_iota(jnp.int32, (tile, tile), 0) <= lax.broadcasted_iota(
        jnp.int32, (tile, tile), 1
    )
    masks = [head_mask(tile, 0), head_mask(tile, 1)]
    lanes = pl.ds(pl.multiple_of(pair * LANES, LANES), LANES)
    for step in range(length // tile):
        rows = slice(step * tile, (step + 1) * tile)
        query = qkv_ref[pair, rows, :] * SCALE
        grad_out = gatt_ref[rows, lanes]
        product = grad_out.astype(f32) * att_ref[rows, lanes].astype(f32)
        queries = [pick(masks[half], query) for half in range(2)]
        grads = [pick(masks[half], grad_out) for half in range(2)]
        deltas = [jnp.sum(pick(masks[half], product).T, axis=0, keepdims=True) for half in range(2)]
        grad_query = [None, None]
        for other in range(step + 1):
            cols = slice(other * tile, (other + 1) * tile)
            keys = qkv_ref[pairs + pair, cols, :]
            values = qkv_ref[2 * pairs + pair, cols, :]
            key_part = value_part = None
            for half in range(2):
                scores = nt(keys, queries[half])
                if other == step:
                    scores = jnp.where(above, scores, masked_score)
                probs = jnp.exp(scores - lse_ref[pair, half : half + 1, rows])
                grad_scores = (probs * (nt(values, grads[half]) - deltas[half])).astype(bf16)
                query_term = tn(grad_scores, keys)
                grad_query[half] = (
                    query_term if grad_query[half] is None else grad_query[half] + query_term
                )
                key_term = mm(grad_scores, queries[half])
                value_term = mm(probs.astype(bf16), grads[half])
                key_part = key_term if key_part is None else key_part + key_term
                value_part = value_term if value_part is None else value_part + value_term
            if other == step:
                acc_ref[0, cols, :] = key_part
                acc_ref[1, cols, :] = value_part
            else:
                acc_ref[0, cols, :] += key_part
                acc_ref[1, cols, :] += value_part
        grad_ref[rows, lanes] = (jnp.where(masks[0], grad_query[0], grad_query[1]) * SCALE).astype(
            bf16
        )
        between()
    for part in range(2):
        lanes_to = pl.ds(pl.multiple_of((part + 1) * width + pair * LANES, LANES), LANES)
        grad_ref[:, lanes_to] = acc_ref[part].astype(bf16)


def self_backward_kernel(
    pairs,
    qkv_ref,
    att_ref,
    gatt_ref,
    lse_ref,
    hid_ref,
    w_ref,
    gw_ref,
    ghid_ref,
    grad_ref,
    acc_ref,
):
    length = att_ref.shape[0]
    width = pairs * LANES
    attention = (qkv_ref, att_ref, gatt_ref, lse_ref, grad_ref, acc_ref)

    @pl.loop(0, pairs)
    def _(pair):
        pair_backward(pair, pairs, *attention, lambda: None)

    hidden_t = hid_ref[...].T
    for part in range(3):
        cols = slice(part * width, (part + 1) * width)
        gw_ref[:, cols] = mm(hidden_t, grad_ref[:, cols]).astype(bf16)
    for begin in range(0, length, 256):
        rows = slice(begin, begin + 256)
        ghid_ref[rows, :] = nt(grad_ref[rows, :], w_ref[...]).astype(bf16)


def self_backward(pairs, qkv, att, gatt, lse, hid, w):
    length, dim = hid.shape
    width = pairs * LANES
    return pl.pallas_call(
        partial(self_backward_kernel, pairs),
        out_shape=(
            jax.ShapeDtypeStruct((dim, 3 * width), bf16),
            jax.ShapeDtypeStruct((length, dim), bf16),
        ),
        scratch_shapes=[
            pltpu.VMEM((length, 3 * width), bf16),
            pltpu.VMEM((2, length, LANES), f32),
        ],
        compiler_params=params(),
        name="self_backward",
    )(qkv, att, gatt, lse, hid, w)


def spread_heads(block, rows, group):
    lane = lax.broadcasted_iota(jnp.int32, block.shape, 1) // HEAD
    return jnp.concatenate([pick(lane == head, block) for head in range(group)], axis=0)


def gather_heads(stacked, rows, group):
    lane = lax.broadcasted_iota(jnp.int32, (rows, stacked.shape[1]), 1) // HEAD
    out = None
    for head in range(group):
        part = pick(lane == head, stacked[head * rows : (head + 1) * rows])
        out = part if out is None else out + part
    return out


def live_keys(presence_ref, span, shape, axis, neighbours, each):
    index = lax.broadcasted_iota(jnp.int32, shape, axis) // each
    live = jnp.zeros(shape, f32)
    anyone = None
    for which in range(neighbours):
        here = presence_ref[span * neighbours + which]
        there = jnp.where(here > 0, 1.0, 0.0).astype(f32)
        live = jnp.where(index == which, there, live)
        anyone = here if anyone is None else jnp.maximum(anyone, here)
    return live, anyone.astype(f32)


def span_forward(span, spans, neighbours, presence_ref, cross_q_ref, near_kv_ref, cross_ref):
    count, dim = cross_q_ref.shape
    span_len = count // spans
    near = near_kv_ref.shape[0] // spans
    group = 256 // HEAD
    rows = rows_of(span, span_len)
    keys = rows_of(span, near)
    live, anyone = live_keys(presence_ref, span, (1, near), 1, neighbours, near // neighbours)
    for begin in range(0, dim, group * HEAD):
        lanes = slice(begin, begin + group * HEAD)
        lanes_v = slice(dim + begin, dim + begin + group * HEAD)
        query = spread_heads(cross_q_ref[rows, lanes] * SCALE, span_len, group)
        scores = jnp.where(live > 0, nt(query, near_kv_ref[keys, lanes]), masked_score)
        peak = jnp.max(scores, axis=-1, keepdims=True)
        expon = jnp.exp(scores - peak) * live
        total = jnp.sum(expon, axis=-1, keepdims=True) + 1.0 - anyone
        out = mm(expon.astype(bf16), near_kv_ref[keys, lanes_v]) / total
        cross_ref[rows, lanes] = gather_heads(out, span_len, group).astype(bf16)


def cross_forward_kernel(
    spans,
    neighbours,
    presence_ref,
    att_ref,
    x_ref,
    norms_ref,
    perm_ref,
    perm_att_ref,
    near_ref,
    w_out_ref,
    w_cq_ref,
    w_ck_ref,
    w_cv_ref,
    w_co_ref,
    att_p_ref,
    first_ref,
    hid_p_ref,
    cross_q_ref,
    near_p_ref,
    near_kv_ref,
    co_p_ref,
    second_ref,
    cross_ref,
):
    count, dim = x_ref.shape
    rows_near = near_ref.shape[0]
    tile = 512

    att_p_ref[...] = mm(att_ref[...], perm_att_ref[...]).astype(bf16)
    first_ref[...] = x_ref[...].astype(f32) + mm(att_p_ref[...], w_out_ref[...])

    normed, _ = centre_scale(first_ref[...])
    hidden = (normed * norms_ref[2:3, :] + norms_ref[3:4, :]).astype(bf16)
    hid_p_ref[...] = mm(hidden, perm_ref[...]).astype(bf16)
    cross_q_ref[...] = mm(hid_p_ref[...], w_cq_ref[...]).astype(bf16)

    @pl.loop(0, rows_near // tile)
    def _(step):
        rows = rows_of(step, tile)
        near_p_ref[rows, :] = mm(near_ref[rows, :], perm_ref[...]).astype(bf16)
        near_kv_ref[rows, :dim] = mm(near_p_ref[rows, :], w_ck_ref[...]).astype(bf16)
        near_kv_ref[rows, dim:] = mm(near_p_ref[rows, :], w_cv_ref[...]).astype(bf16)

    @pl.loop(0, spans)
    def _(span):
        span_forward(span, spans, neighbours, presence_ref, cross_q_ref, near_kv_ref, cross_ref)

    co_p_ref[...] = mm(cross_ref[...], perm_ref[...]).astype(bf16)
    second_ref[...] = first_ref[...] + mm(co_p_ref[...], w_co_ref[...])


def column_block(rows, width, index):
    return pl.BlockSpec((rows, width), lambda *_: (0, index), pipeline_mode=pl.Buffered(1))


def whole(array):
    return pl.BlockSpec(array.shape, lambda *_: (0,) * array.ndim, pipeline_mode=pl.Buffered(1))


def whole_shape(shape):
    return pl.BlockSpec(shape, lambda *_: (0,) * len(shape), pipeline_mode=pl.Buffered(1))


def cross_forward(spans, neighbours, presence, att, x, norms, perm, perm_att, near, weights):
    count, dim = x.shape
    rows_near = near.shape[0]
    out_shape = (
        jax.ShapeDtypeStruct((count, dim), bf16),
        jax.ShapeDtypeStruct((count, dim), f32),
        jax.ShapeDtypeStruct((count, dim), bf16),
        jax.ShapeDtypeStruct((count, dim), bf16),
        jax.ShapeDtypeStruct((rows_near, dim), bf16),
        jax.ShapeDtypeStruct((rows_near, 2 * dim), bf16),
        jax.ShapeDtypeStruct((count, dim), bf16),
        jax.ShapeDtypeStruct((count, dim), f32),
    )
    operands = (att, x, norms, perm, perm_att, near)
    return pl.pallas_call(
        partial(cross_forward_kernel, spans, neighbours),
        out_shape=out_shape,
        grid=(1,),
        in_specs=[pl.BlockSpec(memory_space=pltpu.SMEM)]
        + [whole(op) for op in operands]
        + [column_block(dim, dim, index) for index in (3, 4, 5, 6, 7)],
        out_specs=tuple(whole_shape(shape.shape) for shape in out_shape),
        scratch_shapes=[pltpu.VMEM((count, dim), bf16)],
        compiler_params=params(),
        name="cross_forward",
    )(presence, *operands, *([weights] * 5))


def feed_kernel(
    second_ref,
    cot_ref,
    norms_ref,
    perm_ref,
    w_up_ref,
    w_down_ref,
    out_ref,
    gsecond_ref,
    all_ref,
    gnorm_ref,
    hid_p_ref,
    hid_t_ref,
    cot_p_ref,
    cot_t_ref,
    result_ref,
    back_ref,
    gup_ref,
    gdown_ref,
    sems,
):
    step = pl.program_id(0)
    last = pl.num_programs(0) - 1
    slot = lax.rem(step, 2)
    dim, tile = w_up_ref.shape

    def copies(step, slot):
        up = pl.multiple_of(8 * dim + step * tile, tile)
        down = pl.multiple_of(8 * dim + (last + 1 + step) * tile, tile)
        return (
            pltpu.make_async_copy(gup_ref.at[slot], all_ref.at[:, pl.ds(up, tile)], sems.at[0, slot]),
            pltpu.make_async_copy(
                gdown_ref.at[slot], all_ref.at[:, pl.ds(down, tile)], sems.at[1, slot]
            ),
        )

    @pl.when(step >= 2)
    def _():
        for copy in copies(step - 2, slot):
            copy.wait()

    @pl.when(step == 0)
    def _():
        normed, _ = centre_scale(second_ref[...])
        hidden = (normed * norms_ref[4:5, :] + norms_ref[5:6, :]).astype(bf16)
        hid_p_ref[...] = mm(hidden, perm_ref[...]).astype(bf16)
        hid_t_ref[...] = hid_p_ref[...].T
        cot_p_ref[...] = mm(cot_ref[...], perm_ref[...]).astype(bf16)
        cot_t_ref[...] = cot_p_ref[...].T
        result_ref[...] = jnp.zeros_like(result_ref)
        back_ref[...] = jnp.zeros_like(back_ref)

    upward = mm(hid_p_ref[...], w_up_ref[...])
    active, slope = gelu_parts(upward)
    active = active.astype(bf16)
    result_ref[...] += nt(active, w_down_ref[...])
    gdown_ref[slot] = mm(cot_t_ref[...], active).astype(bf16)
    grad_up = (mm(cot_p_ref[...], w_down_ref[...]) * slope).astype(bf16)
    gup_ref[slot] = mm(hid_t_ref[...], grad_up).astype(bf16)
    for copy in copies(step, slot):
        copy.start()
    back_ref[...] += nt(grad_up, w_up_ref[...])

    @pl.when(step == last)
    def _():
        out_ref[...] = (
            second_ref[...] + nt(result_ref[...].astype(bf16), perm_ref[...])
        ).astype(bf16)
        upstream = nt(back_ref[...].astype(bf16), perm_ref[...])
        normed, recip = centre_scale(second_ref[...])
        back, gain, shift = norm_back(upstream, normed, recip, norms_ref[4:5, :])
        gsecond_ref[...] = cot_ref[...].astype(f32) + back
        gnorm_ref[0:1, :] = gain
        gnorm_ref[1:2, :] = shift
        for which in (step - 1, step):
            for copy in copies(which, lax.rem(which, 2)):
                copy.wait()


def feed(second, cot, norms, perm, weights):
    count, dim = second.shape
    ffw = (weights.shape[1] - 8 * dim) // 2
    tile = 512
    first_up = 8 * dim // tile
    first_down = (8 * dim + ffw) // tile
    out_shape = (
        jax.ShapeDtypeStruct((count, dim), bf16),
        jax.ShapeDtypeStruct((count, dim), f32),
        jax.ShapeDtypeStruct(weights.shape, bf16),
        jax.ShapeDtypeStruct((2, dim), f32),
    )
    operands = (second, cot, norms, perm)
    return pl.pallas_call(
        feed_kernel,
        out_shape=out_shape,
        grid=(ffw // tile,),
        in_specs=[whole(op) for op in operands]
        + [
            pl.BlockSpec((dim, tile), lambda i: (0, first_up + i)),
            pl.BlockSpec((dim, tile), lambda i: (0, first_down + i)),
        ],
        out_specs=(
            whole_shape((count, dim)),
            whole_shape((count, dim)),
            pl.BlockSpec(memory_space=pl.ANY),
            whole_shape((2, dim)),
        ),
        scratch_shapes=[
            pltpu.VMEM((count, dim), bf16),
            pltpu.VMEM((dim, count), bf16),
            pltpu.VMEM((count, dim), bf16),
            pltpu.VMEM((dim, count), bf16),
            pltpu.VMEM((count, dim), f32),
            pltpu.VMEM((count, dim), f32),
            pltpu.VMEM((2, dim, tile), bf16),
            pltpu.VMEM((2, dim, tile), bf16),
            pltpu.SemaphoreType.DMA((2, 2)),
        ],
        compiler_params=params(),
        name="feed",
    )(*operands, weights, weights)


def span_backward(
    span, spans, neighbours, presence_ref, cross_q_ref, gco_ref, near_kv_ref, gcq_ref, gnear_ref
):
    count, dim = cross_q_ref.shape
    span_len = count // spans
    near = near_kv_ref.shape[0] // spans
    group = 256 // HEAD
    rows = rows_of(span, span_len)
    keys = rows_of(span, near)
    live, anyone = live_keys(presence_ref, span, (near, 1), 0, neighbours, near // neighbours)
    for begin in range(0, dim, group * HEAD):
        lanes = slice(begin, begin + group * HEAD)
        lanes_v = slice(dim + begin, dim + begin + group * HEAD)
        query = spread_heads(cross_q_ref[rows, lanes] * SCALE, span_len, group)
        grad_out = spread_heads(gco_ref[rows, lanes], span_len, group)
        key = near_kv_ref[keys, lanes]
        scores = jnp.where(live > 0, nt(key, query), masked_score)
        peak = jnp.max(scores, axis=0, keepdims=True)
        expon = jnp.exp(scores - peak) * live
        total = jnp.sum(expon, axis=0, keepdims=True) + 1.0 - anyone
        probs = expon * (1.0 / total)
        grad_probs = nt(near_kv_ref[keys, lanes_v], grad_out)
        inner = jnp.sum(probs * grad_probs, axis=0, keepdims=True)
        grad_scores = (probs * (grad_probs - inner)).astype(bf16)
        gcq_ref[rows, lanes] = (
            gather_heads(tn(grad_scores, key), span_len, group) * SCALE
        ).astype(bf16)
        gnear_ref[keys, lanes] = mm(grad_scores, query).astype(bf16)
        gnear_ref[keys, lanes_v] = mm(probs.astype(bf16), grad_out).astype(bf16)


def cross_backward_kernel(
    spans,
    neighbours,
    presence_ref,
    gsecond_ref,
    first_ref,
    norms_ref,
    perm_ref,
    perm_att_ref,
    att_p_ref,
    hid_p_ref,
    cross_q_ref,
    near_p_ref,
    near_kv_ref,
    co_p_ref,
    w_out_ref,
    w_cq_ref,
    w_co_ref,
    _,
    gfirst_ref,
    gatt_ref,
    all_ref,
    gnorm_ref,
    gco_ref,
    gcq_ref,
    gnear_ref,
    gw_ref,
    sems,
):
    dim = first_ref.shape[1]
    outs = []

    def keep(index, value):
        gw_ref[index] = value.astype(bf16)
        outs.append(
            pltpu.make_async_copy(
                gw_ref.at[index], all_ref.at[:, pl.ds((3 + index) * dim, dim)], sems.at[index]
            )
        )
        outs[-1].start()

    upper = gsecond_ref[...].astype(bf16)
    gco_ref[...] = nt(nt(upper, w_co_ref[...]).astype(bf16), perm_ref[...]).astype(bf16)
    tables = (presence_ref, cross_q_ref, gco_ref, near_kv_ref, gcq_ref, gnear_ref)
    pl.loop(0, spans)(lambda span: span_backward(span, spans, neighbours, *tables))
    upstream = nt(nt(gcq_ref[...], w_cq_ref[...]).astype(bf16), perm_ref[...])
    normed, recip = centre_scale(first_ref[...])
    back, gain, shift = norm_back(upstream, normed, recip, norms_ref[2:3, :])
    gnorm_ref[0:1, :] = gain
    gnorm_ref[1:2, :] = shift
    gfirst_ref[...] = gsecond_ref[...] + back
    lower = gfirst_ref[...].astype(bf16)
    gatt_ref[...] = nt(nt(lower, w_out_ref[...]).astype(bf16), perm_att_ref[...]).astype(bf16)
    keep(4, mm(co_p_ref[...].T, upper))
    near_t = near_p_ref[...].T
    for part in range(2):
        keep(2 + part, mm(near_t, gnear_ref[:, part * dim : (part + 1) * dim]))
    keep(1, mm(hid_p_ref[...].T, gcq_ref[...]))
    keep(0, mm(att_p_ref[...].T, lower))
    for copy in outs:
        copy.wait()


def cross_backward(
    spans,
    neighbours,
    presence,
    gsecond,
    first,
    norms,
    perm,
    perm_att,
    att_p,
    hid_p,
    cross_q,
    near_p,
    near_kv,
    co_p,
    weights,
    grads,
):
    count, dim = first.shape
    rows_near = near_p.shape[0]
    out_shape = [
        jax.ShapeDtypeStruct((count, dim), f32),
        jax.ShapeDtypeStruct((count, perm_att.shape[0]), bf16),
        jax.ShapeDtypeStruct(grads.shape, bf16),
        jax.ShapeDtypeStruct((2, dim), f32),
    ]
    scratch = [
        pltpu.VMEM((count, dim), bf16),
        pltpu.VMEM((count, dim), bf16),
        pltpu.VMEM((rows_near, 2 * dim), bf16),
        pltpu.VMEM((5, dim, dim), bf16),
        pltpu.SemaphoreType.DMA((5,)),
    ]
    operands = (
        gsecond,
        first,
        norms,
        perm,
        perm_att,
        att_p,
        hid_p,
        cross_q,
        near_p,
        near_kv,
        co_p,
    )
    return pl.pallas_call(
        partial(cross_backward_kernel, spans, neighbours),
        out_shape=out_shape,
        grid=(1,),
        in_specs=[pl.BlockSpec(memory_space=pltpu.SMEM)]
        + [whole(op) for op in operands]
        + [column_block(dim, dim, index) for index in (3, 4, 7)]
        + [pl.BlockSpec(memory_space=pl.ANY)],
        out_specs=tuple(
            pl.BlockSpec(memory_space=pl.ANY) if index == 2 else whole_shape(shape.shape)
            for index, shape in enumerate(out_shape)
        ),
        scratch_shapes=scratch,
        input_output_aliases={len(operands) + 4: 2},
        compiler_params=params(),
        name="cross_backward",
    )(presence, *operands, *([weights] * 3), grads)


def last_norm_kernel(parts_ref, x_ref, gfirst_ref, norms_ref, perm_ref, out_ref, gnorm_ref):
    total = parts_ref[0].astype(f32)
    for part in range(1, parts_ref.shape[0]):
        total = total + parts_ref[part].astype(f32)
    upstream = nt(total.astype(bf16), perm_ref[...])
    normed, recip = centre_scale(x_ref[...].astype(f32))
    back, gain, shift = norm_back(upstream, normed, recip, norms_ref[0:1, :])
    out_ref[...] = gfirst_ref[...] + back
    gnorm_ref[0:1, :] = gain
    gnorm_ref[1:2, :] = shift


def last_norm(parts, x, gfirst, norms, perm):
    count, dim = x.shape
    return pl.pallas_call(
        last_norm_kernel,
        out_shape=(
            jax.ShapeDtypeStruct((count, dim), f32),
            jax.ShapeDtypeStruct((2, dim), f32),
        ),
        compiler_params=params(),
        name="last_norm",
    )(parts, x, gfirst, norms, perm)


def layer_kernel(
    lines,
    pairs,
    spans,
    neighbours,
    presence_ref,
    w_ref,
    norm_ref,
    x_ref,
    order_ref,
    cot_ref,
    near_ref,
    wts_ref,
    all_ref,
    out_ref,
    gin_ref,
    sums_ref,
    hid_ref,
    qkv_ref,
    att_ref,
    lse_ref,
    att_p_ref,
    first_ref,
    hid_p_ref,
    cross_q_ref,
    near_p_ref,
    near_kv_ref,
    co_p_ref,
    second_ref,
    own_ref,
    small_ref,
    rows_ref,
    w_qkv_ref,
    w_mid_ref,
    att_tok_ref,
    cross_ref,
    up_p_ref,
    up_t_ref,
    cot_p_ref,
    cot_t_ref,
    result_ref,
    back_ref,
    gfeed_ref,
    perm_ref,
    norms_ref,
    gatt_ref,
    acc_ref,
    gsib_ref,
    parts_ref,
    send_sems,
    z_sems,
    y_sems,
    x_sems,
    a_sems,
    b_sems,
    sib_sems,
    norm_sems,
    row_sems,
    att_sems,
    local_sems,
    qkv_sems,
    mid_sems,
    feed_sems,
    gatt_sems,
    gsib_sems,
    part_sems,
):
    place = Place(lines)
    z, me, core = place.z, place.me, place.core
    length, dim = hid_ref.shape
    width = pairs * LANES
    tokens = length // 8
    half = own_ref.shape[0] // 2
    near_load = pltpu.make_async_copy(near_ref, near_p_ref, local_sems.at[2])
    near_load.start()
    own_ref[...] = w_ref[...].astype(bf16)
    place.meet()
    send = Sender(place, send_sems)
    unit = partial(unit_of, wts_ref, lines)
    events = place.events()
    keep = pltpu.make_async_copy(own_ref, unit(z, me), local_sems.at[0])
    keep.start()

    def build_perm():
        row = lax.broadcasted_iota(jnp.int32, (dim, dim), 0)
        perm_ref[...] = jnp.where(row == order_ref[0:1, :], 1.0, 0.0).astype(bf16)

    def obtain(index):
        condition, line, far, side = events[index]
        mine = unit(line, me)
        src = own_ref if far == 0 else mine
        if far:
            send.arrived(condition, mine, z_sems.at[line])
        if side >= 0:
            send.start(both(condition, z > 0), src, mine, z_sems.at[line], z=z - 1)
        if side <= 0:
            send.start(both(condition, z < lines - 1), src, mine, z_sems.at[line], z=z + 1)
        send.start(condition, src, mine, x_sems.at[line], seq=place.xn)
        send.start(condition, src, mine, y_sems.at[line], seq=place.yn)
        send.start(condition, src, mine, sib_sems.at[0, line], seq=place.sib)

    def pass_on(index):
        condition, line, _, _ = events[index]
        from_x, from_y = unit(line, place.xn), unit(line, place.yn)
        send.arrived(condition, from_x, x_sems.at[line])
        part = unit(line, place.xn, half, half)
        send.start(condition, part, part, b_sems.at[line], seq=place.yn)
        send.start(condition, from_x, from_x, sib_sems.at[1, line], seq=place.sib)
        send.arrived(condition, from_y, y_sems.at[line])
        part = unit(line, place.yn, 0, half)
        send.start(condition, part, part, a_sems.at[line], seq=place.xn)
        send.start(condition, from_y, from_y, sib_sems.at[2, line], seq=place.sib)

    def corner(index):
        condition, line, _, _ = events[index]
        for group, begin, sems in ((3, 0, a_sems), (4, half, b_sems)):
            part = unit(line, place.dg, begin, half)
            send.arrived(condition, part, sems.at[line])
            send.start(condition, part, part, sib_sems.at[group, line], seq=place.sib)

    def row_block(seq):
        return rows_ref.at[pl.ds(pl.multiple_of(seq * tokens, tokens), tokens)]

    def middle(index):
        return pltpu.make_async_copy(
            wts_ref.at[:, pl.ds((3 + index) * dim, dim)], w_mid_ref.at[index], mid_sems.at[index]
        )

    obtain(0)
    own_rows = pltpu.make_async_copy(x_ref.at[place.chip], row_block(me), local_sems.at[1])
    own_rows.start()
    others = (place.xn, place.yn, place.dg)
    for other in place.line():
        send.start(None, norm_ref, small_ref.at[z], norm_sems.at[z], z=other)
    small_ref[z] = norm_ref[...]
    send.start(None, x_ref.at[place.chip], row_block(me), row_sems.at[me], seq=place.sib)
    for other in others:
        send.start(None, x_ref.at[other // 2], row_block(me), row_sems.at[me], seq=other)
    build_perm()
    near_load.wait()

    @pl.loop(0, near_p_ref.shape[0] // 512)
    def _(step):
        rows = rows_of(step, 512)
        near_p_ref[rows, :] = mm(near_p_ref[rows, :], perm_ref[...]).astype(bf16)

    obtain(1)
    obtain(2)
    pass_on(0)
    for other in others:
        send.arrived(None, row_block(other), row_sems.at[other])
        send.start(None, row_block(other), row_block(other), row_sems.at[other], seq=place.sib)
    obtain(3)
    obtain(4)
    cot_p_ref[...] = mm(cot_ref[...], perm_ref[...]).astype(bf16)
    cot_t_ref[...] = cot_p_ref[...].T
    pass_on(1)
    pass_on(2)
    corner(0)

    for other in place.line():
        send.arrived(None, small_ref.at[other], norm_sems.at[other])
    piece = small_ref.shape[2]
    total = None
    for line in range(lines):
        row = lax.broadcasted_iota(jnp.int32, (piece, dim), 0)
        column = lax.broadcasted_iota(jnp.int32, (piece, dim), 1)
        part = dim // lines
        place_of = jnp.logical_and(row < part, column == row + line * part).astype(bf16)
        term = mm(small_ref[line], place_of)
        total = term if total is None else total + term
    norms_ref[...] = total[: norms_ref.shape[0]]

    last = len(events)
    for index in range(5, last, 2):
        obtain(index)
        obtain(index + 1)
        if index == 5:
            for other in others:
                theirs = other + 1 - 2 * core
                send.arrived(None, row_block(theirs), row_sems.at[theirs])
            send.arrived(None, row_block(place.sib), row_sems.at[place.sib])
            own_rows.wait()
            norm_rows(rows_ref, norms_ref[...], perm_ref, hid_ref)
        pass_on(index - 2)
        pass_on(index - 1)
        corner(index - 4)
        corner(index - 3)
    for index in range(last - 2, last):
        pass_on(index)
    for index in range(last - 4, last):
        corner(index)
    keep.wait()
    for line in range(lines):
        for group, first in enumerate((me, place.xn, place.yn)):
            theirs = first + 1 - 2 * core
            send.arrived(None, unit(line, theirs), sib_sems.at[group, line])
        theirs = place.dg + 1 - 2 * core
        send.arrived(None, unit(line, theirs, 0, half), sib_sems.at[3, line])
        send.arrived(None, unit(line, theirs, half, half), sib_sems.at[4, line])
    copies = weight_copies(pairs, dim, wts_ref, w_qkv_ref, qkv_sems)
    for copy in copies + [middle(index) for index in (2, 3, 0, 1, 4)]:
        copy.start()
    for part in range(3):
        copies[part].wait()
        triple_part(part, pairs, hid_ref, w_qkv_ref, qkv_ref)

    share = lax.rem(me, dim // width)
    seq_rows = pl.ds(pl.multiple_of(place.chip * tokens, tokens), tokens)

    def landing(pair, chip_rows, share):
        lanes = pl.ds(pl.multiple_of(share * width + pair * LANES, LANES), LANES)
        return att_tok_ref.at[chip_rows, lanes]

    for pair in range(pairs):
        lanes = slice(pair * LANES, (pair + 1) * LANES)
        pair_forward(pair, pairs, qkv_ref, att_ref, lse_ref, lambda: None)
        for other in place.plane():
            block = att_ref.at[pl.ds(pl.multiple_of(other * tokens, tokens), tokens), lanes]
            to = landing(pair, seq_rows, share)
            send.start(None, block, to, att_sems.at[pair, me], seq=other)
        own_block = att_ref[pl.ds(pl.multiple_of(me * tokens, tokens), tokens), lanes]
        landing(pair, seq_rows, share)[...] = own_block

    for index in (2, 3, 0, 1, 4):
        middle(index).wait()
    for step in range(near_p_ref.shape[0] // 512):
        rows = slice(step * 512, (step + 1) * 512)
        near_kv_ref[rows, :dim] = mm(near_p_ref[rows, :], w_mid_ref[2]).astype(bf16)
        near_kv_ref[rows, dim:] = mm(near_p_ref[rows, :], w_mid_ref[3]).astype(bf16)
    w_out_ref, w_cq_ref, w_co_ref = (w_mid_ref.at[index] for index in (0, 1, 4))
    for pair in range(pairs):
        for other in place.plane():
            rows = pl.ds(pl.multiple_of(other // 2 * tokens, tokens), tokens)
            send.arrived(None, landing(pair, rows, lax.rem(other, 2)), att_sems.at[pair, other])
    att_p_ref[...] = mm(att_tok_ref[...], perm_ref[...]).astype(bf16)
    own_x = x_ref[...].reshape(first_ref.shape).astype(f32)
    first_ref[...] = own_x + mm(att_p_ref[...], w_out_ref[...])
    normed, _ = centre_scale(first_ref[...])
    hidden = (normed * norms_ref[2:3, :] + norms_ref[3:4, :]).astype(bf16)
    hid_p_ref[...] = mm(hidden, perm_ref[...]).astype(bf16)
    cross_q_ref[...] = mm(hid_p_ref[...], w_cq_ref[...]).astype(bf16)
    pl.loop(0, spans)(
        lambda span: span_forward(
            span, spans, neighbours, presence_ref, cross_q_ref, near_kv_ref, cross_ref
        )
    )

    ffw = (all_ref.shape[1] - 8 * dim) // 2
    tile = gfeed_ref.shape[2]
    order = range(0, ffw, tile)

    def tile_load(index):
        return [
            pltpu.make_async_copy(
                wts_ref.at[:, pl.ds(8 * dim + part * ffw + order[index], tile)],
                w_mid_ref.at[(2 * index + part) % 4],
                feed_sems.at[0, (2 * index + part) % 4],
            )
            for part in range(2)
        ]

    def tile_store(index):
        return [
            pltpu.make_async_copy(
                gfeed_ref.at[(2 * index + part) % 4],
                all_ref.at[:, pl.ds(8 * dim + part * ffw + order[index], tile)],
                feed_sems.at[1, (2 * index + part) % 4],
            )
            for part in range(2)
        ]

    for copy in tile_load(0) + tile_load(1):
        copy.start()
    co_p_ref[...] = mm(cross_ref[...], perm_ref[...]).astype(bf16)
    second_ref[...] = first_ref[...] + mm(co_p_ref[...], w_co_ref[...])
    normed, _ = centre_scale(second_ref[...])
    hidden = (normed * norms_ref[4:5, :] + norms_ref[5:6, :]).astype(bf16)
    up_p_ref[...] = mm(hidden, perm_ref[...]).astype(bf16)
    up_t_ref[...] = up_p_ref[...].T

    for index in range(len(order)):
        up_ref, down_ref = w_mid_ref.at[2 * index % 4], w_mid_ref.at[2 * index % 4 + 1]
        for copy in tile_load(index):
            copy.wait()
        if index >= 2:
            for copy in tile_store(index - 2):
                copy.wait()
        active, slope = gelu_parts(mm(up_p_ref[...], up_ref[...]))
        active = active.astype(bf16)
        term = nt(active, down_ref[...])
        result_ref[...] = term if index == 0 else result_ref[...] + term
        gfeed_ref[2 * index % 4 + 1] = mm(cot_t_ref[...], active).astype(bf16)
        grad_up = (mm(cot_p_ref[...], down_ref[...]) * slope).astype(bf16)
        gfeed_ref[2 * index % 4] = mm(up_t_ref[...], grad_up).astype(bf16)
        for copy in tile_store(index):
            copy.start()
        term = nt(grad_up, up_ref[...])
        back_ref[...] = term if index == 0 else back_ref[...] + term
        if index + 2 < len(order):
            for copy in tile_load(index + 2):
                copy.start()
        elif index + 2 == len(order):
            middle(0).start()
            middle(1).start()

    out_ref[...] = (second_ref[...] + nt(result_ref[...].astype(bf16), perm_ref[...])).astype(bf16)
    upstream = nt(back_ref[...].astype(bf16), perm_ref[...])
    normed, recip = centre_scale(second_ref[...])
    back, gain, shift = norm_back(upstream, normed, recip, norms_ref[4:5, :])
    gsecond_ref = second_ref
    gsecond_ref[...] = cot_ref[...].astype(f32) + back
    sums_ref[4:5, :] = gain
    sums_ref[5:6, :] = shift
    sums_ref[6:8, :] = jnp.zeros((2, dim), f32)
    for index in range(len(order) - 2, len(order)):
        for copy in tile_store(index):
            copy.wait()

    gco_ref, gcq_ref, gatt_tok_ref = up_p_ref, cot_p_ref, cross_ref
    outs = []

    def store(slot, part, first):
        copy = pltpu.make_async_copy(
            part, all_ref.at[:, pl.ds(first, part.shape[1])], feed_sems.at[1, slot]
        )
        outs.append(copy)
        copy.start()

    def keep_grad(index, value):
        slot = len(outs) % 4
        if len(outs) >= 4:
            outs[-4].wait()
        gfeed_ref[slot] = value.astype(bf16)
        store(slot, gfeed_ref.at[slot], (3 + index) * dim)

    upper = gsecond_ref[...].astype(bf16)
    gco_ref[...] = nt(nt(upper, w_co_ref[...]).astype(bf16), perm_ref[...]).astype(bf16)
    tables = (presence_ref, cross_q_ref, gco_ref, near_kv_ref, gcq_ref, near_kv_ref)
    pl.loop(0, spans)(lambda span: span_backward(span, spans, neighbours, *tables))
    for index in (0, 1):
        middle(index).wait()
    upstream = nt(nt(gcq_ref[...], w_cq_ref[...]).astype(bf16), perm_ref[...])
    normed, recip = centre_scale(first_ref[...])
    back, gain, shift = norm_back(upstream, normed, recip, norms_ref[2:3, :])
    sums_ref[2:3, :] = gain
    sums_ref[3:4, :] = shift
    gfirst_ref = gsecond_ref
    gfirst_ref[...] = gsecond_ref[...] + back
    lower = gfirst_ref[...].astype(bf16)
    gatt_tok_ref[...] = nt(nt(lower, w_out_ref[...]).astype(bf16), perm_ref[...]).astype(bf16)

    def gatt_block(device):
        return gatt_tok_ref.at[
            pl.ds(pl.multiple_of(device // 2 * tokens, tokens), tokens),
            pl.ds(pl.multiple_of(lax.rem(device, 2) * width, width), width),
        ]

    def gatt_rows(device):
        return gatt_ref.at[pl.ds(pl.multiple_of(device * tokens, tokens), tokens)]

    for other in place.plane():
        send.start(None, gatt_block(other), gatt_rows(me), gatt_sems.at[me], seq=other)
    own_gatt = pltpu.make_async_copy(gatt_block(me), gatt_rows(me), gatt_sems.at[me])
    own_gatt.start()
    keep_grad(4, mm(co_p_ref[...].T, upper))
    near_t = near_p_ref[...].T
    for part in range(2):
        keep_grad(2 + part, mm(near_t, near_kv_ref[:, part * dim : (part + 1) * dim]))
    keep_grad(1, mm(hid_p_ref[...].T, gcq_ref[...]))
    keep_grad(0, mm(att_p_ref[...].T, lower))
    for other in place.plane():
        send.arrived(None, gatt_rows(other), gatt_sems.at[other])
    own_gatt.wait()

    send.finish()
    grad_ref = near_kv_ref.at[pl.ds(0, length), pl.ds(0, 3 * width)]
    ghid_ref = rows_ref
    attention = (qkv_ref, att_ref, gatt_ref, lse_ref, grad_ref, acc_ref)
    pl.loop(0, pairs)(lambda pair: pair_backward(pair, pairs, *attention, lambda: None))
    for begin in range(0, length, 256):
        rows = slice(begin, begin + 256)
        ghid_ref[rows, :] = nt(grad_ref[rows, :], w_qkv_ref[...]).astype(bf16)
    chips = (place.xn // 2, place.yn // 2, place.dg // 2, place.chip)

    def token_rows(device):
        return pl.ds(pl.multiple_of(device * tokens, tokens), tokens)

    for chip in chips:
        theirs = ghid_ref.at[token_rows(chip * 2 + 1 - core)]
        send.start(None, theirs, gsib_ref.at[chip], gsib_sems.at[chip], seq=place.sib)

    for copy in outs[-4:]:
        copy.wait()
    outs.clear()
    gfeed_ref[3] = jnp.zeros_like(gfeed_ref[3])
    share_count = dim // width
    zeros = [
        pltpu.make_async_copy(
            gfeed_ref.at[3, :, pl.ds(0, width)],
            all_ref.at[
                :,
                pl.ds(
                    pl.multiple_of(part * dim + lax.rem(share + other, share_count) * width, LANES),
                    width,
                ),
            ],
            mid_sems.at[2 + part],
        )
        for part in range(3)
        for other in range(1, share_count)
    ]
    for copy in zeros:
        copy.start()
    hidden_t = hid_ref[...].T

    def triple_grad(part):
        columns = slice(part * width, (part + 1) * width)
        gfeed_ref[part, :, :width] = mm(hidden_t, grad_ref[:, columns]).astype(bf16)
        first = pl.multiple_of(part * dim + share * width, LANES)
        store(part, gfeed_ref.at[part, :, pl.ds(0, width)], first)

    triple_grad(0)
    triple_grad(1)
    for chip in chips:
        send.arrived(None, gsib_ref.at[chip], gsib_sems.at[chip])
        rows = token_rows(chip * 2 + core)
        total = (ghid_ref[rows, :].astype(f32) + gsib_ref[chip].astype(f32)).astype(bf16)
        if chip is place.chip:
            parts_ref[chip] = total
        else:
            ghid_ref[rows, :] = total
            landed, sem = parts_ref.at[place.chip], part_sems.at[place.chip]
            send.start(None, ghid_ref.at[rows], landed, sem, seq=chip * 2 + core)
    triple_grad(2)
    for chip in chips[:3]:
        send.arrived(None, parts_ref.at[chip], part_sems.at[chip])
    gain_sum = shift_sum = None
    for chip in range(4):
        rows = slice(chip * tokens, (chip + 1) * tokens)
        upstream = nt(parts_ref[chip], perm_ref[...])
        normed, recip = centre_scale(x_ref[chip].astype(f32))
        back, gain, shift = norm_back(upstream, normed, recip, norms_ref[0:1, :])
        gfirst_ref[rows, :] += back
        gain_sum = gain if gain_sum is None else gain_sum + gain
        shift_sum = shift if shift_sum is None else shift_sum + shift
    leave = pltpu.make_async_copy(gfirst_ref, gin_ref, local_sems.at[0])
    leave.start()
    sums_ref[0:1, :] = gain_sum
    sums_ref[1:2, :] = shift_sum
    for copy in outs + zeros:
        copy.wait()
    leave.wait()
    send.finish()


def layer(lines, pairs, spans, neighbours, presence, w_shard, n_shard, inputs, order, cot, near):
    unit_rows, unit_cols = w_shard.shape
    seqs, tokens, dim = inputs.shape
    count, length, width = seqs * tokens, 8 * tokens, pairs * LANES
    rows_near = near.shape[0]
    events = 2 * lines - 1
    any_space = pl.BlockSpec(memory_space=pl.ANY)
    vmem = pl.BlockSpec(memory_space=pltpu.VMEM)
    dma = pltpu.SemaphoreType.DMA
    packed = jax.ShapeDtypeStruct((unit_rows * lines, unit_cols * 8), bf16)
    tile = unit_cols // 2
    tokens_rows = (count, dim)
    scratch = [
        ((length, dim), bf16),
        ((3 * pairs, length, LANES), bf16),
        ((length, width), bf16),
        ((pairs, 2, length), f32),
        (tokens_rows, bf16),
        (tokens_rows, f32),
        (tokens_rows, bf16),
        (tokens_rows, bf16),
        ((rows_near, dim), bf16),
        ((rows_near, 2 * dim), bf16),
        (tokens_rows, bf16),
        (tokens_rows, f32),
        ((unit_rows, unit_cols), bf16),
        ((lines,) + n_shard.shape, bf16),
        ((length, dim), bf16),
        ((dim, 3 * width), bf16),
        ((5, dim, dim), bf16),
        (tokens_rows, bf16),
        (tokens_rows, bf16),
        (tokens_rows, bf16),
        ((dim, count), bf16),
        (tokens_rows, bf16),
        ((dim, count), bf16),
        (tokens_rows, f32),
        (tokens_rows, f32),
        ((4, dim, tile), bf16),
        ((dim, dim), bf16),
        ((8, dim), f32),
        ((length, width), bf16),
        ((2, length, LANES), f32),
        ((4, tokens, dim), bf16),
        ((4, tokens, dim), bf16),
    ]
    return pl.pallas_call(
        partial(layer_kernel, lines, pairs, spans, neighbours),
        out_shape=(
            packed,
            packed,
            jax.ShapeDtypeStruct(tokens_rows, bf16),
            jax.ShapeDtypeStruct(tokens_rows, f32),
            jax.ShapeDtypeStruct((8, dim), f32),
        ),
        in_specs=[pl.BlockSpec(memory_space=pltpu.SMEM)] + [vmem] * 5 + [any_space],
        out_specs=(any_space, any_space, vmem, any_space, vmem),
        scratch_shapes=[pltpu.VMEM(*entry) for entry in scratch]
        + [
            dma((11 * events + 7 + lines + 7 * pairs + 16,)),
            dma((lines,)),
            dma((lines,)),
            dma((lines,)),
            dma((lines,)),
            dma((lines,)),
            dma((5, lines)),
            dma((lines,)),
            dma((8,)),
            dma((pairs, 8)),
            dma((3,)),
            dma((3,)),
            dma((5,)),
            dma((2, 4)),
            dma((8,)),
            dma((4,)),
            dma((4,)),
        ],
        compiler_params=pltpu.CompilerParams(
            vmem_limit_bytes=VMEM_BYTES, collective_id=1, has_side_effects=True
        ),
        name="layer",
    )(presence, w_shard, n_shard, inputs, order, cot, near)


def reduce_kernel(
    lines,
    grads_ref,
    small_ref,
    shard_ref,
    norms_ref,
    mine_ref,
    sib_ref,
    corner_a_ref,
    corner_b_ref,
    from_x_ref,
    from_y_ref,
    below_ref,
    above_ref,
    early_below_ref,
    early_above_ref,
    plane_ref,
    plane_sum_ref,
    line_ref,
    send_sems,
    load_sems,
    sib_sems,
    a_sems,
    b_sems,
    x_sems,
    y_sems,
    below_sems,
    above_sems,
    early_below_sems,
    early_above_sems,
    plane_sems,
    line_sems,
):
    place = Place(lines)
    z, me = place.z, place.me
    unit_rows, unit_cols = shard_ref.shape
    early = early_below_ref.shape[2]
    place.meet()
    send = Sender(place, send_sems)
    chips = (place.dg, place.yn, place.xn, me)
    corner, over_y, over_x, here = range(4)

    unit = partial(unit_of, grads_ref, lines)

    def load(which, line):
        return pltpu.make_async_copy(
            unit(line, chips[which]), mine_ref.at[which, line], load_sems.at[which, line]
        )

    for other in place.plane():
        send.start(None, small_ref, plane_ref.at[me], plane_sems.at[me], seq=other)
    plane_ref[me] = small_ref[...]

    events = place.events()[::-1]
    count = len(events)

    def begin(index):
        condition, line, _, _ = events[index]
        for which in range(4):
            theirs = chips[which] + 1 - 2 * place.core
            send.start(
                condition,
                unit(line, theirs),
                sib_ref.at[which, line],
                sib_sems.at[which, line],
                seq=place.sib,
            )
            when(condition, load(which, line).start)

    def parts(index):
        if index == count:
            return 0, early // 2, early, (unit_rows - early) // 2, lines
        return early, (early + unit_rows) // 2, unit_rows, 0, events[index][1]

    def add(target, *terms, begin=0, end=unit_rows):
        tile = next(size for size in (96, 80, 64, 32, 16) if (end - begin) % size == 0)

        @pl.loop(0, (end - begin) // tile)
        def _(step):
            rows = pl.ds(pl.multiple_of(begin + step * tile, 16), tile)
            total = target[rows, :]
            if len(terms) > 1:
                total = total.astype(f32)
            for ref, first in terms:
                at = pl.ds(pl.multiple_of(begin - first + step * tile, 16), tile)
                term = ref[at, :]
                total = total + (term if len(terms) == 1 else term.astype(f32))
            target[rows, :] = total.astype(target.dtype)

    def early_rows(line):
        return mine_ref.at[:, line, pl.ds(0, early), :]

    def add_early(line, landing):
        for which in range(4):
            add(mine_ref.at[which, line], (landing.at[line, which], 0), end=early)

    def first(index):
        condition, line, far, side = events[min(index, count - 1)]
        low, middle, high, base, sem = parts(index)
        if index < count:
            for which in range(4):
                send.arrived(condition, sib_ref.at[which, line], sib_sems.at[which, line])
                when(condition, load(which, line).wait)

            def chip_sum():
                for which in range(4):
                    add(mine_ref.at[which, line], (sib_ref.at[which, line], 0))

            when(condition, chip_sum)
        if far or index == count:
            from_below, from_above = both(condition, z > 0), both(condition, z < lines - 1)
            sides = ((from_below, early_below_ref, early_below_sems),) if side >= 0 else ()
            if side <= 0:
                sides += ((from_above, early_above_ref, early_above_sems),)
            for on, landing, sems in sides:
                send.arrived(on, landing.at[line], sems.at[line])
                when(on, partial(add_early, line, landing))
        if far:
            landing, sems = sides[0][1:]
            send.start(condition, early_rows(line), landing.at[line], sems.at[line], z=z + side)
        target = mine_ref.at[corner, line]
        for begins, ends, landing, sems, to in (
            (low, middle, corner_a_ref, a_sems, place.xn),
            (middle, high, corner_b_ref, b_sems, place.yn),
        ):
            send.start(
                condition,
                target.at[pl.ds(begins, ends - begins)],
                landing.at[line, pl.ds(base, ends - begins)],
                sems.at[sem],
                seq=to,
            )

    def second(index):
        condition, line, _, _ = events[min(index, count - 1)]
        low, middle, high, base, sem = parts(index)
        for which, part, sems, begins, ends, to, landing, landing_sems in (
            (over_y, corner_a_ref, a_sems, low, middle, place.yn, from_y_ref, y_sems),
            (over_x, corner_b_ref, b_sems, middle, high, place.xn, from_x_ref, x_sems),
        ):
            send.arrived(condition, part.at[line, pl.ds(base, ends - begins)], sems.at[sem])
            target = mine_ref.at[which, line]
            term = (part.at[line], begins - base)
            when(condition, partial(add, target, term, begin=begins, end=ends))
            rows = pl.ds(low, high - low)
            landed = landing.at[line, rows]
            send.start(condition, target.at[rows], landed, landing_sems.at[sem], seq=to)

    def third(index):
        condition, line, far, side = events[min(index, count - 1)]
        low, _, high, _, sem = parts(index)
        rows = pl.ds(low, high - low)
        send.arrived(condition, from_x_ref.at[line, rows], x_sems.at[sem])
        send.arrived(condition, from_y_ref.at[line, rows], y_sems.at[sem])
        target = mine_ref.at[here, line]
        terms = [(from_x_ref.at[line], 0), (from_y_ref.at[line], 0)]
        if far == 0:
            tile = 32

            @pl.loop(low // tile, high // tile)
            def _(step):
                at = rows_of(step, tile)
                total = target[at, :].astype(f32)
                for ref, _ in terms:
                    total = total + ref[at, :].astype(f32)
                shard_ref[at, :] = total

            if index < count:
                for on, ref, sems in (
                    (z > 0, below_ref, below_sems),
                    (z < lines - 1, above_ref, above_sems),
                ):
                    send.arrived(on, ref.at[line, rows], sems.at[line])
                    when(on, partial(add, shard_ref, (ref.at[line], 0), begin=low))
            return
        landing, sems = (below_ref, below_sems) if side > 0 else (above_ref, above_sems)
        more = both(condition, z > 0) if side > 0 else both(condition, z < lines - 1)
        none = both(condition, z == 0) if side > 0 else both(condition, z == lines - 1)
        send.arrived(more, landing.at[line, rows], sems.at[line])
        when(more, partial(add, target, *terms, (landing.at[line], 0), begin=low))
        when(none, partial(add, target, *terms, begin=low))
        landed = landing.at[line, rows]
        send.start(condition, target.at[rows], landed, sems.at[line], z=z + side)

    for index in range(min(4, count)):
        begin(index)
    first(0)
    first(1)
    for index in range(2, count + 5):
        if index + 2 < count:
            begin(index + 2)
        if index <= count:
            first(index)
        if 0 <= index - 2 <= count:
            second(index - 2)
        if index == 3:
            for other in place.plane():
                send.arrived(None, plane_ref.at[other], plane_sems.at[other])
            total = plane_ref[0]
            for other in range(1, 8):
                total = total + plane_ref[other]
            plane_sum_ref[...] = total
            line_ref[z] = total
            for other in place.line():
                send.start(None, plane_sum_ref, line_ref.at[z], line_sems.at[z], z=other)
        if 0 <= index - 4 <= count:
            third(index - 4)

    for other in place.line():
        send.arrived(None, line_ref.at[other], line_sems.at[other])
    total = line_ref[0]
    for other in range(1, lines):
        total = total + line_ref[other]
    norms_ref[...] = total
    send.finish()


def reduce_grads(lines, grads, small):
    rows, cols = grads.shape
    unit_rows, unit_cols = rows // lines, cols // 8
    half = unit_rows // 2
    early = unit_rows // 96 * 16
    any_space = pl.BlockSpec(memory_space=pl.ANY)
    vmem = pl.BlockSpec(memory_space=pltpu.VMEM)
    dma = pltpu.SemaphoreType.DMA
    return pl.pallas_call(
        partial(reduce_kernel, lines),
        out_shape=(
            jax.ShapeDtypeStruct((unit_rows, unit_cols), f32),
            jax.ShapeDtypeStruct(small.shape, f32),
        ),
        in_specs=[any_space, vmem],
        out_specs=(vmem, vmem),
        scratch_shapes=[
            pltpu.VMEM((4, lines, unit_rows, unit_cols), bf16),
            pltpu.VMEM((4, lines, unit_rows, unit_cols), bf16),
            pltpu.VMEM((lines, half, unit_cols), bf16),
            pltpu.VMEM((lines, half, unit_cols), bf16),
            pltpu.VMEM((lines, unit_rows, unit_cols), bf16),
            pltpu.VMEM((lines, unit_rows, unit_cols), bf16),
            pltpu.VMEM((lines, unit_rows, unit_cols), bf16),
            pltpu.VMEM((lines, unit_rows, unit_cols), bf16),
            pltpu.VMEM((lines, 4, early, unit_cols), bf16),
            pltpu.VMEM((lines, 4, early, unit_cols), bf16),
            pltpu.VMEM((8,) + small.shape, f32),
            pltpu.VMEM(small.shape, f32),
            pltpu.VMEM((lines,) + small.shape, f32),
            dma((10 * (2 * lines - 1) + 4 + 7 + lines,)),
            dma((4, lines)),
            dma((4, lines)),
            dma((lines + 1,)),
            dma((lines + 1,)),
            dma((lines + 1,)),
            dma((lines + 1,)),
            dma((lines,)),
            dma((lines,)),
            dma((lines,)),
            dma((lines,)),
            dma((8,)),
            dma((lines,)),
        ],
        compiler_params=pltpu.CompilerParams(
            vmem_limit_bytes=VMEM_BYTES, collective_id=4, has_side_effects=True
        ),
        name="reduce_grads",
    )(grads, small)


def adam_update(grad, weight, first, second, average, rate, decay):
    first = beta_first * first + (1.0 - beta_first) * grad
    second = beta_second * second + (1.0 - beta_second) * grad * grad
    stepped = (
        first / (1.0 - beta_first**STEP) / (jnp.sqrt(second / (1.0 - beta_second**STEP)) + adam_eps)
    )
    weight = weight - rate * (stepped + decay * weight)
    average = ema_decay * average + (1.0 - ema_decay) * weight
    return (first, second, weight, average)


def on_device(
    inputs,
    cotangent,
    neighbours,
    presence,
    row_order,
    w_master,
    w_first,
    w_second,
    w_average,
    n_master,
    n_first,
    n_second,
    n_average,
):
    seqs, tokens, dim = inputs.shape
    heads = dim // HEAD
    devices = lax.axis_size("seq")
    count = seqs * tokens
    length = devices * tokens
    me = lax.axis_index("seq")
    shares = devices // seqs
    held = heads // shares
    pairs = (held + 1) // 2
    width = pairs * LANES
    spare = width - held * HEAD
    sequence, share = me // shares, me % shares

    lines = lax.axis_size("dp")
    planar = devices == 8 and seqs == 4 and spare == 0
    x = inputs.reshape(count, dim)
    cot = cotangent.reshape(count, dim)
    spans = seqs * neighbours.shape[1]
    each = neighbours.shape[2]
    near = neighbours.reshape(-1, dim)
    live = presence.reshape(-1)
    part = n_master.shape[1]
    if planar:
        small = jnp.pad(n_master.astype(bf16), ((0, 16 - 6), (0, -part % LANES)))
        order = row_order.reshape(1, dim)
        _, grads, outputs, grad_inputs, norm_grads = layer(
            lines, pairs, spans, each, live, w_master, small, inputs, order, cot, near
        )
        grad_shard, norm_sums = reduce_grads(lines, grads, norm_grads)
        norm_shard = lax.dynamic_slice(norm_sums, (0, lax.axis_index("dp") * part), (6, part))
    else:
        perm = (jnp.arange(dim)[:, None] == row_order[None, :]).astype(bf16)
        perm_att = jnp.pad(perm.reshape(shares, held * HEAD, dim), ((0, 0), (0, spare), (0, 0)))
        perm_att = perm_att.reshape(shares * width, dim)
        weights = lax.all_gather(w_master.astype(bf16), "dp", axis=0, tiled=True)
        weights = lax.all_gather(weights, "seq", axis=1, tiled=True)
        norms = lax.all_gather(n_master.astype(bf16), "dp", axis=1, tiled=True).astype(f32)
        rows = lax.all_to_all(jnp.repeat(inputs, shares, axis=0), "seq", 0, 0)
        rows = rows.reshape(length, dim)
        w_qkv = weights[:, : 3 * dim].reshape(dim, 3, shares, held * HEAD)
        w_qkv = lax.dynamic_index_in_dim(w_qkv, share, axis=2, keepdims=False)
        w_qkv = jnp.pad(w_qkv, ((0, 0), (0, 0), (0, spare))).reshape(dim, 3 * width)
        hid, qkv, att, lse = self_forward(pairs, rows, norms, perm, w_qkv)
        att_tok = (
            lax.all_to_all(att.reshape(devices, tokens, width), "seq", 0, 0)
            .reshape(seqs, shares, tokens, width)
            .transpose(0, 2, 1, 3)
            .reshape(count, shares * width)
        )
        att_p, first, hid_p, cross_q, near_p, near_kv, co_p, second = cross_forward(
            spans, each, live, att_tok, x, norms, perm, perm_att, near, weights
        )
        outputs, gsecond, grads, gnorm_e = feed(second, cot, norms, perm, weights)
        gfirst, gatt_tok, grads, gnorm_c = cross_backward(
            spans,
            each,
            live,
            gsecond,
            first,
            norms,
            perm,
            perm_att,
            att_p,
            hid_p,
            cross_q,
            near_p,
            near_kv,
            co_p,
            weights,
            grads,
        )
        gatt = lax.all_to_all(
            gatt_tok.reshape(seqs, tokens, shares, width)
            .transpose(0, 2, 1, 3)
            .reshape(devices, tokens, width),
            "seq",
            0,
            0,
        ).reshape(length, width)
        gqkv, ghid = self_backward(pairs, qkv, att, gatt, lse, hid, w_qkv)
        parts = (
            lax.all_to_all(ghid.reshape(devices, tokens, dim), "seq", 0, 0)
            .reshape(seqs, shares, tokens, dim)
            .transpose(1, 0, 2, 3)
            .reshape(shares, count, dim)
        )
        grad_inputs, gnorm_a = last_norm(parts, x, gfirst, norms, perm)
        gqkv = gqkv.reshape(dim, 3, 1, width)[..., : held * HEAD]
        gqkv = jnp.where(jnp.arange(shares)[:, None] == share, gqkv, jnp.zeros_like(gqkv))
        grads = lax.dynamic_update_slice(grads, gqkv.reshape(dim, 3 * dim), (0, 0))
        norm_grads = lax.psum(jnp.concatenate([gnorm_a, gnorm_c, gnorm_e], axis=0), "seq")
        partial_sum = lax.psum_scatter(grads, "seq", scatter_dimension=1, tiled=True)
        grad_shard = lax.psum_scatter(partial_sum, "dp", scatter_dimension=0, tiled=True)
        grad_shard = grad_shard.astype(f32)
        norm_shard = lax.psum_scatter(
            norm_grads.astype(bf16), "dp", scatter_dimension=1, tiled=True
        ).astype(f32)
    w_first_new, w_second_new, w_new, w_average_new = adam_update(
        grad_shard, w_master, w_first, w_second, w_average, learn_rate, weight_decay
    )
    n_first_new, n_second_new, n_new, n_average_new = adam_update(
        norm_shard, n_master, n_first, n_second, n_average, norm_rate, 0.0
    )
    return (
        outputs.reshape(seqs, tokens, dim),
        grad_inputs.reshape(seqs, tokens, dim),
        w_first_new,
        w_second_new,
        w_new,
        w_average_new,
        n_first_new,
        n_second_new,
        n_new,
        n_average_new,
    )


def solution(mesh):
    in_specs = (
        P("dp", "seq", None),
        P("dp", "seq", None),
        P("dp", "seq", None, None, None),
        P("dp", "seq", None),
        P(),
        P("dp", "seq"),
        P("dp", "seq"),
        P("dp", "seq"),
        P("dp", "seq"),
        P(None, "dp"),
        P(None, "dp"),
        P(None, "dp"),
        P(None, "dp"),
    )
    out_specs = (
        P("dp", "seq", None),
        P("dp", "seq", None),
        P("dp", "seq"),
        P("dp", "seq"),
        P("dp", "seq"),
        P("dp", "seq"),
        P(None, "dp"),
        P(None, "dp"),
        P(None, "dp"),
        P(None, "dp"),
    )
    return jax.shard_map(
        on_device, mesh=mesh, in_specs=in_specs, out_specs=out_specs, check_vma=False
    )
```

```python
from functools import partial

import jax
import jax.numpy as jnp
from jax import lax
from jax.experimental import pallas as pl
from jax.experimental.pallas import tpu as pltpu
from jax.sharding import PartitionSpec as P

HEAD = 64
STEP = 5
LANES = 128
SCALE = HEAD ** (-0.5)

beta_first = 0.9
beta_second = 0.95
adam_eps = 1e-08
learn_rate = 0.04
norm_rate = 0.6
weight_decay = 0.1
ema_decay = 0.5
norm_eps = 1e-05
masked_score = -1e30
VMEM_BYTES = 62 * 1024 * 1024
bf16 = jnp.bfloat16
f32 = jnp.float32


def mm(left, right):
    return lax.dot_general(left, right, (((1,), (0,)), ((), ())), preferred_element_type=f32)


def nt(left, right):
    return lax.dot_general(left, right, (((1,), (1,)), ((), ())), preferred_element_type=f32)


def tn(left, right):
    return lax.dot_general(left, right, (((0,), (0,)), ((), ())), preferred_element_type=f32)


def params():
    return pltpu.CompilerParams(vmem_limit_bytes=VMEM_BYTES)


def rows_of(index, size):
    return pl.ds(pl.multiple_of(index * size, size), size)


def centre_scale(values):
    centre = jnp.mean(values, axis=-1, keepdims=True)
    centred = values - centre
    spread = jnp.mean(centred * centred, axis=-1, keepdims=True)
    recip = lax.rsqrt(spread + norm_eps)
    return centred * recip, recip


def norm_back(upstream, normed, recip, gain):
    scaled = upstream * gain
    inner = (
        scaled
        - jnp.mean(scaled, axis=-1, keepdims=True)
        - normed * jnp.mean(scaled * normed, axis=-1, keepdims=True)
    )
    return (
        recip * inner,
        jnp.sum(upstream * normed, axis=0, keepdims=True),
        jnp.sum(upstream, axis=0, keepdims=True),
    )


def gelu_parts(value):
    const = 0.7978845608028654
    square = value * value
    bend = jnp.tanh(const * value * (1.0 + 0.044715 * square))
    half = 0.5 * (1.0 + bend)
    slope = half + 0.5 * value * (1.0 - bend * bend) * (const * (1.0 + 3 * 0.044715 * square))
    return value * half, slope


def head_mask(rows, half):
    lane = lax.broadcasted_iota(jnp.int32, (rows, LANES), 1)
    return (lane < HEAD) if half == 0 else (lane >= HEAD)


def pick(mask, value):
    return jnp.where(mask, value, jnp.zeros_like(value))


MESH = pl.DeviceIdType.MESH


class Place:
    def __init__(self, lines):
        self.lines = lines
        self.z = lax.axis_index("dp")
        self.me = lax.axis_index("seq")
        core, x, y = self.me % 2, (self.me // 2) % 2, self.me // 4
        self.core, self.x, self.y, self.chip = core, x, y, self.me // 2
        self.sib = self.me + 1 - 2 * core
        self.xn = self.me + 2 - 4 * x
        self.yn = self.me + 4 - 8 * y
        self.dg = self.xn + 4 - 8 * y

    def events(self):
        found = [(None, self.z, 0, 0)]
        for far in range(1, self.lines):
            found.append((self.z >= far, self.z - far, far, -1))
            found.append((self.z + far < self.lines, self.z + far, far, 1))
        return found

    def plane(self):
        return [lax.rem(self.me + step, 8) for step in range(1, 8)]

    def line(self):
        return [lax.rem(self.z + step, self.lines) for step in range(1, self.lines)]

    def meet(self):
        barrier = pltpu.get_barrier_semaphore()
        for other in self.plane():
            pl.semaphore_signal(
                barrier, inc=1, device_id={"dp": self.z, "seq": other}, device_id_type=MESH
            )
        for other in self.line():
            pl.semaphore_signal(
                barrier, inc=1, device_id={"dp": other, "seq": self.me}, device_id_type=MESH
            )
        pl.semaphore_wait(barrier, 7 + self.lines - 1)


def when(condition, body):
    if condition is None:
        body()
    else:
        pl.when(condition)(body)


def both(first, second):
    if first is None or second is None:
        return second if first is None else first
    return jnp.logical_and(first, second)


class Sender:
    def __init__(self, place, send_sems):
        self.place, self.sems, self.open, self.count = place, send_sems, [], 0

    def start(self, condition, src, dst, recv_sem, z=None, seq=None):
        place = self.place
        target = {"dp": place.z if z is None else z, "seq": place.me if seq is None else seq}
        copy = pltpu.make_async_remote_copy(
            src_ref=src,
            dst_ref=dst,
            send_sem=self.sems.at[self.count],
            recv_sem=recv_sem,
            device_id=target,
            device_id_type=MESH,
        )
        self.open.append((condition, copy))
        self.count += 1
        when(condition, copy.start)

    def arrived(self, condition, ref, recv_sem):
        copy = pltpu.make_async_remote_copy(
            src_ref=ref,
            dst_ref=ref,
            send_sem=self.sems.at[0],
            recv_sem=recv_sem,
            device_id={"dp": self.place.z, "seq": self.place.sib},
            device_id_type=MESH,
        )
        when(condition, copy.wait_recv)

    def finish(self):
        for condition, copy in self.open:
            when(condition, copy.wait_send)
        self.open = []


class Weave:
    def __init__(self, steps):
        self.steps = list(steps)

    def some(self, count):
        for _ in range(min(count, len(self.steps))):
            self.steps.pop(0)()

    def rest(self):
        self.some(len(self.steps))


def unit_of(ref, lines, line, seq, begin=0, size=None):
    rows, cols = ref.shape[0] // lines, ref.shape[1] // 8
    size = rows if size is None else size
    return ref.at[
        pl.ds(pl.multiple_of(line * rows + begin, 16), size),
        pl.ds(pl.multiple_of(seq * cols, cols), cols),
    ]


def weight_copies(pairs, dim, wts_ref, w_ref, sems):
    width = pairs * LANES
    first = lax.rem(lax.axis_index("seq"), dim // width) * width
    return [
        pltpu.make_async_copy(
            wts_ref.at[:, pl.ds(pl.multiple_of(first + part * dim, LANES), width)],
            w_ref.at[:, pl.ds(part * width, width)],
            sems.at[part],
        )
        for part in range(3)
    ]


def pair_forward(pair, pairs, qkv_ref, att_ref, lse_ref, between):
    length = att_ref.shape[0]
    tile = 256
    below = lax.broadcasted_iota(jnp.int32, (tile, tile), 1) <= lax.broadcasted_iota(
        jnp.int32, (tile, tile), 0
    )
    masks = [head_mask(tile, 0), head_mask(tile, 1)]
    lane = lax.broadcasted_iota(jnp.int32, (tile, LANES), 1)
    for step in range(length // tile):
        rows = slice(step * tile, (step + 1) * tile)
        query = qkv_ref[pair, rows, :] * SCALE
        keys_here = qkv_ref[pairs + pair, rows, :]
        values_here = qkv_ref[2 * pairs + pair, rows, :]
        outs, logs = [], []
        for half in range(2):
            mine = pick(masks[half], query)
            here = jnp.where(below, nt(mine, keys_here), masked_score)
            peak = jnp.max(here, axis=-1, keepdims=True)
            if step:
                past = nt(mine, qkv_ref[pairs + pair, : step * tile, :])
                peak = jnp.maximum(peak, jnp.max(past, axis=-1, keepdims=True))
                past = jnp.exp(past - peak)
            here = jnp.exp(here - peak)
            total = jnp.sum(here, axis=-1, keepdims=True)
            out = mm(here.astype(bf16), values_here)
            if step:
                total = total + jnp.sum(past, axis=-1, keepdims=True)
                out = out + mm(past.astype(bf16), qkv_ref[2 * pairs + pair, : step * tile, :])
            outs.append(out / total)
            logs.append(peak + jnp.log(total))
        lse_ref[pair, :, rows] = jnp.where(lane == 0, logs[0], logs[1]).T[0:2, :]
        att_ref[rows, pl.ds(pl.multiple_of(pair * LANES, LANES), LANES)] = jnp.where(
            masks[0], outs[0], outs[1]
        ).astype(bf16)
        between()


def norm_rows(x_ref, norms, perm_ref, hid_ref):
    tile = 256

    @pl.loop(0, x_ref.shape[0] // tile)
    def _(step):
        rows = rows_of(step, tile)
        normed, _ = centre_scale(x_ref[rows, :].astype(f32))
        hidden = (normed * norms[0:1, :] + norms[1:2, :]).astype(bf16)
        hid_ref[rows, :] = mm(hidden, perm_ref[...]).astype(bf16)


def triple_part(part, pairs, hid_ref, w_ref, qkv_ref):
    width = pairs * LANES
    triple = mm(hid_ref[...], w_ref[:, part * width : (part + 1) * width]).astype(bf16)
    for pair in range(pairs):
        qkv_ref[part * pairs + pair] = triple[:, pair * LANES : (pair + 1) * LANES]


def self_forward_kernel(
    pairs, x_ref, norms_ref, perm_ref, w_ref, hid_ref, qkv_ref, att_ref, lse_ref
):
    norm_rows(x_ref, norms_ref, perm_ref, hid_ref)
    for part in range(3):
        triple_part(part, pairs, hid_ref, w_ref, qkv_ref)

    @pl.loop(0, pairs)
    def _(pair):
        pair_forward(pair, pairs, qkv_ref, att_ref, lse_ref, lambda: None)


def self_forward(pairs, x, norms, perm, w):
    length, dim = x.shape
    return pl.pallas_call(
        partial(self_forward_kernel, pairs),
        out_shape=(
            jax.ShapeDtypeStruct((length, dim), bf16),
            jax.ShapeDtypeStruct((3 * pairs, length, LANES), bf16),
            jax.ShapeDtypeStruct((length, pairs * LANES), bf16),
            jax.ShapeDtypeStruct((pairs, 2, length), f32),
        ),
        compiler_params=params(),
        name="self_forward",
    )(x, norms, perm, w)


def pair_backward(pair, pairs, qkv_ref, att_ref, gatt_ref, lse_ref, grad_ref, acc_ref, between):
    length = att_ref.shape[0]
    width = pairs * LANES
    tile = 256
    above = lax.broadcasted_iota(jnp.int32, (tile, tile), 0) <= lax.broadcasted_iota(
        jnp.int32, (tile, tile), 1
    )
    masks = [head_mask(tile, 0), head_mask(tile, 1)]
    lanes = pl.ds(pl.multiple_of(pair * LANES, LANES), LANES)
    for step in range(length // tile):
        rows = slice(step * tile, (step + 1) * tile)
        query = qkv_ref[pair, rows, :] * SCALE
        grad_out = gatt_ref[rows, lanes]
        product = grad_out.astype(f32) * att_ref[rows, lanes].astype(f32)
        queries = [pick(masks[half], query) for half in range(2)]
        grads = [pick(masks[half], grad_out) for half in range(2)]
        deltas = [jnp.sum(pick(masks[half], product).T, axis=0, keepdims=True) for half in range(2)]
        grad_query = [None, None]
        for other in range(step + 1):
            cols = slice(other * tile, (other + 1) * tile)
            keys = qkv_ref[pairs + pair, cols, :]
            values = qkv_ref[2 * pairs + pair, cols, :]
            key_part = value_part = None
            for half in range(2):
                scores = nt(keys, queries[half])
                if other == step:
                    scores = jnp.where(above, scores, masked_score)
                probs = jnp.exp(scores - lse_ref[pair, half : half + 1, rows])
                grad_scores = (probs * (nt(values, grads[half]) - deltas[half])).astype(bf16)
                query_term = tn(grad_scores, keys)
                grad_query[half] = (
                    query_term if grad_query[half] is None else grad_query[half] + query_term
                )
                key_term = mm(grad_scores, queries[half])
                value_term = mm(probs.astype(bf16), grads[half])
                key_part = key_term if key_part is None else key_part + key_term
                value_part = value_term if value_part is None else value_part + value_term
            if other == step:
                acc_ref[0, cols, :] = key_part
                acc_ref[1, cols, :] = value_part
            else:
                acc_ref[0, cols, :] += key_part
                acc_ref[1, cols, :] += value_part
        grad_ref[rows, lanes] = (jnp.where(masks[0], grad_query[0], grad_query[1]) * SCALE).astype(
            bf16
        )
        between()
    for part in range(2):
        lanes_to = pl.ds(pl.multiple_of((part + 1) * width + pair * LANES, LANES), LANES)
        grad_ref[:, lanes_to] = acc_ref[part].astype(bf16)


def self_backward_kernel(
    pairs,
    qkv_ref,
    att_ref,
    gatt_ref,
    lse_ref,
    hid_ref,
    w_ref,
    gw_ref,
    ghid_ref,
    grad_ref,
    acc_ref,
):
    length = att_ref.shape[0]
    width = pairs * LANES
    attention = (qkv_ref, att_ref, gatt_ref, lse_ref, grad_ref, acc_ref)

    @pl.loop(0, pairs)
    def _(pair):
        pair_backward(pair, pairs, *attention, lambda: None)

    hidden_t = hid_ref[...].T
    for part in range(3):
        cols = slice(part * width, (part + 1) * width)
        gw_ref[:, cols] = mm(hidden_t, grad_ref[:, cols]).astype(bf16)
    for begin in range(0, length, 256):
        rows = slice(begin, begin + 256)
        ghid_ref[rows, :] = nt(grad_ref[rows, :], w_ref[...]).astype(bf16)


def self_backward(pairs, qkv, att, gatt, lse, hid, w):
    length, dim = hid.shape
    width = pairs * LANES
    return pl.pallas_call(
        partial(self_backward_kernel, pairs),
        out_shape=(
            jax.ShapeDtypeStruct((dim, 3 * width), bf16),
            jax.ShapeDtypeStruct((length, dim), bf16),
        ),
        scratch_shapes=[
            pltpu.VMEM((length, 3 * width), bf16),
            pltpu.VMEM((2, length, LANES), f32),
        ],
        compiler_params=params(),
        name="self_backward",
    )(qkv, att, gatt, lse, hid, w)


def spread_heads(block, rows, group):
    lane = lax.broadcasted_iota(jnp.int32, block.shape, 1) // HEAD
    return jnp.concatenate([pick(lane == head, block) for head in range(group)], axis=0)


def gather_heads(stacked, rows, group):
    lane = lax.broadcasted_iota(jnp.int32, (rows, stacked.shape[1]), 1) // HEAD
    out = None
    for head in range(group):
        part = pick(lane == head, stacked[head * rows : (head + 1) * rows])
        out = part if out is None else out + part
    return out


def live_keys(presence_ref, span, shape, axis, neighbours, each):
    index = lax.broadcasted_iota(jnp.int32, shape, axis) // each
    live = jnp.zeros(shape, f32)
    anyone = None
    for which in range(neighbours):
        here = presence_ref[span * neighbours + which]
        there = jnp.where(here > 0, 1.0, 0.0).astype(f32)
        live = jnp.where(index == which, there, live)
        anyone = here if anyone is None else jnp.maximum(anyone, here)
    return live, anyone.astype(f32)


def span_forward(span, spans, neighbours, presence_ref, cross_q_ref, near_kv_ref, cross_ref):
    count, dim = cross_q_ref.shape
    span_len = count // spans
    near = near_kv_ref.shape[0] // spans
    group = 256 // HEAD
    rows = rows_of(span, span_len)
    keys = rows_of(span, near)
    live, anyone = live_keys(presence_ref, span, (1, near), 1, neighbours, near // neighbours)
    for begin in range(0, dim, group * HEAD):
        lanes = slice(begin, begin + group * HEAD)
        lanes_v = slice(dim + begin, dim + begin + group * HEAD)
        query = spread_heads(cross_q_ref[rows, lanes] * SCALE, span_len, group)
        scores = jnp.where(live > 0, nt(query, near_kv_ref[keys, lanes]), masked_score)
        peak = jnp.max(scores, axis=-1, keepdims=True)
        expon = jnp.exp(scores - peak) * live
        total = jnp.sum(expon, axis=-1, keepdims=True) + 1.0 - anyone
        out = mm(expon.astype(bf16), near_kv_ref[keys, lanes_v]) / total
        cross_ref[rows, lanes] = gather_heads(out, span_len, group).astype(bf16)


def cross_forward_kernel(
    spans,
    neighbours,
    presence_ref,
    att_ref,
    x_ref,
    norms_ref,
    perm_ref,
    perm_att_ref,
    near_ref,
    w_out_ref,
    w_cq_ref,
    w_ck_ref,
    w_cv_ref,
    w_co_ref,
    att_p_ref,
    first_ref,
    hid_p_ref,
    cross_q_ref,
    near_p_ref,
    near_kv_ref,
    co_p_ref,
    second_ref,
    cross_ref,
):
    count, dim = x_ref.shape
    rows_near = near_ref.shape[0]
    tile = 512

    att_p_ref[...] = mm(att_ref[...], perm_att_ref[...]).astype(bf16)
    first_ref[...] = x_ref[...].astype(f32) + mm(att_p_ref[...], w_out_ref[...])

    normed, _ = centre_scale(first_ref[...])
    hidden = (normed * norms_ref[2:3, :] + norms_ref[3:4, :]).astype(bf16)
    hid_p_ref[...] = mm(hidden, perm_ref[...]).astype(bf16)
    cross_q_ref[...] = mm(hid_p_ref[...], w_cq_ref[...]).astype(bf16)

    @pl.loop(0, rows_near // tile)
    def _(step):
        rows = rows_of(step, tile)
        near_p_ref[rows, :] = mm(near_ref[rows, :], perm_ref[...]).astype(bf16)
        near_kv_ref[rows, :dim] = mm(near_p_ref[rows, :], w_ck_ref[...]).astype(bf16)
        near_kv_ref[rows, dim:] = mm(near_p_ref[rows, :], w_cv_ref[...]).astype(bf16)

    @pl.loop(0, spans)
    def _(span):
        span_forward(span, spans, neighbours, presence_ref, cross_q_ref, near_kv_ref, cross_ref)

    co_p_ref[...] = mm(cross_ref[...], perm_ref[...]).astype(bf16)
    second_ref[...] = first_ref[...] + mm(co_p_ref[...], w_co_ref[...])


def column_block(rows, width, index):
    return pl.BlockSpec((rows, width), lambda *_: (0, index), pipeline_mode=pl.Buffered(1))


def whole(array):
    return pl.BlockSpec(array.shape, lambda *_: (0,) * array.ndim, pipeline_mode=pl.Buffered(1))


def whole_shape(shape):
    return pl.BlockSpec(shape, lambda *_: (0,) * len(shape), pipeline_mode=pl.Buffered(1))


def cross_forward(spans, neighbours, presence, att, x, norms, perm, perm_att, near, weights):
    count, dim = x.shape
    rows_near = near.shape[0]
    out_shape = (
        jax.ShapeDtypeStruct((count, dim), bf16),
        jax.ShapeDtypeStruct((count, dim), f32),
        jax.ShapeDtypeStruct((count, dim), bf16),
        jax.ShapeDtypeStruct((count, dim), bf16),
        jax.ShapeDtypeStruct((rows_near, dim), bf16),
        jax.ShapeDtypeStruct((rows_near, 2 * dim), bf16),
        jax.ShapeDtypeStruct((count, dim), bf16),
        jax.ShapeDtypeStruct((count, dim), f32),
    )
    operands = (att, x, norms, perm, perm_att, near)
    return pl.pallas_call(
        partial(cross_forward_kernel, spans, neighbours),
        out_shape=out_shape,
        grid=(1,),
        in_specs=[pl.BlockSpec(memory_space=pltpu.SMEM)]
        + [whole(op) for op in operands]
        + [column_block(dim, dim, index) for index in (3, 4, 5, 6, 7)],
        out_specs=tuple(whole_shape(shape.shape) for shape in out_shape),
        scratch_shapes=[pltpu.VMEM((count, dim), bf16)],
        compiler_params=params(),
        name="cross_forward",
    )(presence, *operands, *([weights] * 5))


def feed_kernel(
    second_ref,
    cot_ref,
    norms_ref,
    perm_ref,
    w_up_ref,
    w_down_ref,
    out_ref,
    gsecond_ref,
    all_ref,
    gnorm_ref,
    hid_p_ref,
    hid_t_ref,
    cot_p_ref,
    cot_t_ref,
    result_ref,
    back_ref,
    gup_ref,
    gdown_ref,
    sems,
):
    step = pl.program_id(0)
    last = pl.num_programs(0) - 1
    slot = lax.rem(step, 2)
    dim, tile = w_up_ref.shape

    def copies(step, slot):
        up = pl.multiple_of(8 * dim + step * tile, tile)
        down = pl.multiple_of(8 * dim + (last + 1 + step) * tile, tile)
        return (
            pltpu.make_async_copy(gup_ref.at[slot], all_ref.at[:, pl.ds(up, tile)], sems.at[0, slot]),
            pltpu.make_async_copy(
                gdown_ref.at[slot], all_ref.at[:, pl.ds(down, tile)], sems.at[1, slot]
            ),
        )

    @pl.when(step >= 2)
    def _():
        for copy in copies(step - 2, slot):
            copy.wait()

    @pl.when(step == 0)
    def _():
        normed, _ = centre_scale(second_ref[...])
        hidden = (normed * norms_ref[4:5, :] + norms_ref[5:6, :]).astype(bf16)
        hid_p_ref[...] = mm(hidden, perm_ref[...]).astype(bf16)
        hid_t_ref[...] = hid_p_ref[...].T
        cot_p_ref[...] = mm(cot_ref[...], perm_ref[...]).astype(bf16)
        cot_t_ref[...] = cot_p_ref[...].T
        result_ref[...] = jnp.zeros_like(result_ref)
        back_ref[...] = jnp.zeros_like(back_ref)

    upward = mm(hid_p_ref[...], w_up_ref[...])
    active, slope = gelu_parts(upward)
    active = active.astype(bf16)
    result_ref[...] += nt(active, w_down_ref[...])
    gdown_ref[slot] = mm(cot_t_ref[...], active).astype(bf16)
    grad_up = (mm(cot_p_ref[...], w_down_ref[...]) * slope).astype(bf16)
    gup_ref[slot] = mm(hid_t_ref[...], grad_up).astype(bf16)
    for copy in copies(step, slot):
        copy.start()
    back_ref[...] += nt(grad_up, w_up_ref[...])

    @pl.when(step == last)
    def _():
        out_ref[...] = (
            second_ref[...] + nt(result_ref[...].astype(bf16), perm_ref[...])
        ).astype(bf16)
        upstream = nt(back_ref[...].astype(bf16), perm_ref[...])
        normed, recip = centre_scale(second_ref[...])
        back, gain, shift = norm_back(upstream, normed, recip, norms_ref[4:5, :])
        gsecond_ref[...] = cot_ref[...].astype(f32) + back
        gnorm_ref[0:1, :] = gain
        gnorm_ref[1:2, :] = shift
        for which in (step - 1, step):
            for copy in copies(which, lax.rem(which, 2)):
                copy.wait()


def feed(second, cot, norms, perm, weights):
    count, dim = second.shape
    ffw = (weights.shape[1] - 8 * dim) // 2
    tile = 512
    first_up = 8 * dim // tile
    first_down = (8 * dim + ffw) // tile
    out_shape = (
        jax.ShapeDtypeStruct((count, dim), bf16),
        jax.ShapeDtypeStruct((count, dim), f32),
        jax.ShapeDtypeStruct(weights.shape, bf16),
        jax.ShapeDtypeStruct((2, dim), f32),
    )
    operands = (second, cot, norms, perm)
    return pl.pallas_call(
        feed_kernel,
        out_shape=out_shape,
        grid=(ffw // tile,),
        in_specs=[whole(op) for op in operands]
        + [
            pl.BlockSpec((dim, tile), lambda i: (0, first_up + i)),
            pl.BlockSpec((dim, tile), lambda i: (0, first_down + i)),
        ],
        out_specs=(
            whole_shape((count, dim)),
            whole_shape((count, dim)),
            pl.BlockSpec(memory_space=pl.ANY),
            whole_shape((2, dim)),
        ),
        scratch_shapes=[
            pltpu.VMEM((count, dim), bf16),
            pltpu.VMEM((dim, count), bf16),
            pltpu.VMEM((count, dim), bf16),
            pltpu.VMEM((dim, count), bf16),
            pltpu.VMEM((count, dim), f32),
            pltpu.VMEM((count, dim), f32),
            pltpu.VMEM((2, dim, tile), bf16),
            pltpu.VMEM((2, dim, tile), bf16),
            pltpu.SemaphoreType.DMA((2, 2)),
        ],
        compiler_params=params(),
        name="feed",
    )(*operands, weights, weights)


def span_backward(
    span, spans, neighbours, presence_ref, cross_q_ref, gco_ref, near_kv_ref, gcq_ref, gnear_ref
):
    count, dim = cross_q_ref.shape
    span_len = count // spans
    near = near_kv_ref.shape[0] // spans
    group = 256 // HEAD
    rows = rows_of(span, span_len)
    keys = rows_of(span, near)
    live, anyone = live_keys(presence_ref, span, (near, 1), 0, neighbours, near // neighbours)
    for begin in range(0, dim, group * HEAD):
        lanes = slice(begin, begin + group * HEAD)
        lanes_v = slice(dim + begin, dim + begin + group * HEAD)
        query = spread_heads(cross_q_ref[rows, lanes] * SCALE, span_len, group)
        grad_out = spread_heads(gco_ref[rows, lanes], span_len, group)
        key = near_kv_ref[keys, lanes]
        scores = jnp.where(live > 0, nt(key, query), masked_score)
        peak = jnp.max(scores, axis=0, keepdims=True)
        expon = jnp.exp(scores - peak) * live
        total = jnp.sum(expon, axis=0, keepdims=True) + 1.0 - anyone
        probs = expon * (1.0 / total)
        grad_probs = nt(near_kv_ref[keys, lanes_v], grad_out)
        inner = jnp.sum(probs * grad_probs, axis=0, keepdims=True)
        grad_scores = (probs * (grad_probs - inner)).astype(bf16)
        gcq_ref[rows, lanes] = (
            gather_heads(tn(grad_scores, key), span_len, group) * SCALE
        ).astype(bf16)
        gnear_ref[keys, lanes] = mm(grad_scores, query).astype(bf16)
        gnear_ref[keys, lanes_v] = mm(probs.astype(bf16), grad_out).astype(bf16)


def cross_backward_kernel(
    spans,
    neighbours,
    presence_ref,
    gsecond_ref,
    first_ref,
    norms_ref,
    perm_ref,
    perm_att_ref,
    att_p_ref,
    hid_p_ref,
    cross_q_ref,
    near_p_ref,
    near_kv_ref,
    co_p_ref,
    w_out_ref,
    w_cq_ref,
    w_co_ref,
    _,
    gfirst_ref,
    gatt_ref,
    all_ref,
    gnorm_ref,
    gco_ref,
    gcq_ref,
    gnear_ref,
    gw_ref,
    sems,
):
    dim = first_ref.shape[1]
    outs = []

    def keep(index, value):
        gw_ref[index] = value.astype(bf16)
        outs.append(
            pltpu.make_async_copy(
                gw_ref.at[index], all_ref.at[:, pl.ds((3 + index) * dim, dim)], sems.at[index]
            )
        )
        outs[-1].start()

    upper = gsecond_ref[...].astype(bf16)
    gco_ref[...] = nt(nt(upper, w_co_ref[...]).astype(bf16), perm_ref[...]).astype(bf16)
    tables = (presence_ref, cross_q_ref, gco_ref, near_kv_ref, gcq_ref, gnear_ref)
    pl.loop(0, spans)(lambda span: span_backward(span, spans, neighbours, *tables))
    upstream = nt(nt(gcq_ref[...], w_cq_ref[...]).astype(bf16), perm_ref[...])
    normed, recip = centre_scale(first_ref[...])
    back, gain, shift = norm_back(upstream, normed, recip, norms_ref[2:3, :])
    gnorm_ref[0:1, :] = gain
    gnorm_ref[1:2, :] = shift
    gfirst_ref[...] = gsecond_ref[...] + back
    lower = gfirst_ref[...].astype(bf16)
    gatt_ref[...] = nt(nt(lower, w_out_ref[...]).astype(bf16), perm_att_ref[...]).astype(bf16)
    keep(4, mm(co_p_ref[...].T, upper))
    near_t = near_p_ref[...].T
    for part in range(2):
        keep(2 + part, mm(near_t, gnear_ref[:, part * dim : (part + 1) * dim]))
    keep(1, mm(hid_p_ref[...].T, gcq_ref[...]))
    keep(0, mm(att_p_ref[...].T, lower))
    for copy in outs:
        copy.wait()


def cross_backward(
    spans,
    neighbours,
    presence,
    gsecond,
    first,
    norms,
    perm,
    perm_att,
    att_p,
    hid_p,
    cross_q,
    near_p,
    near_kv,
    co_p,
    weights,
    grads,
):
    count, dim = first.shape
    rows_near = near_p.shape[0]
    out_shape = [
        jax.ShapeDtypeStruct((count, dim), f32),
        jax.ShapeDtypeStruct((count, perm_att.shape[0]), bf16),
        jax.ShapeDtypeStruct(grads.shape, bf16),
        jax.ShapeDtypeStruct((2, dim), f32),
    ]
    scratch = [
        pltpu.VMEM((count, dim), bf16),
        pltpu.VMEM((count, dim), bf16),
        pltpu.VMEM((rows_near, 2 * dim), bf16),
        pltpu.VMEM((5, dim, dim), bf16),
        pltpu.SemaphoreType.DMA((5,)),
    ]
    operands = (
        gsecond,
        first,
        norms,
        perm,
        perm_att,
        att_p,
        hid_p,
        cross_q,
        near_p,
        near_kv,
        co_p,
    )
    return pl.pallas_call(
        partial(cross_backward_kernel, spans, neighbours),
        out_shape=out_shape,
        grid=(1,),
        in_specs=[pl.BlockSpec(memory_space=pltpu.SMEM)]
        + [whole(op) for op in operands]
        + [column_block(dim, dim, index) for index in (3, 4, 7)]
        + [pl.BlockSpec(memory_space=pl.ANY)],
        out_specs=tuple(
            pl.BlockSpec(memory_space=pl.ANY) if index == 2 else whole_shape(shape.shape)
            for index, shape in enumerate(out_shape)
        ),
        scratch_shapes=scratch,
        input_output_aliases={len(operands) + 4: 2},
        compiler_params=params(),
        name="cross_backward",
    )(presence, *operands, *([weights] * 3), grads)


def last_norm_kernel(parts_ref, x_ref, gfirst_ref, norms_ref, perm_ref, out_ref, gnorm_ref):
    total = parts_ref[0].astype(f32)
    for part in range(1, parts_ref.shape[0]):
        total = total + parts_ref[part].astype(f32)
    upstream = nt(total.astype(bf16), perm_ref[...])
    normed, recip = centre_scale(x_ref[...].astype(f32))
    back, gain, shift = norm_back(upstream, normed, recip, norms_ref[0:1, :])
    out_ref[...] = gfirst_ref[...] + back
    gnorm_ref[0:1, :] = gain
    gnorm_ref[1:2, :] = shift


def last_norm(parts, x, gfirst, norms, perm):
    count, dim = x.shape
    return pl.pallas_call(
        last_norm_kernel,
        out_shape=(
            jax.ShapeDtypeStruct((count, dim), f32),
            jax.ShapeDtypeStruct((2, dim), f32),
        ),
        compiler_params=params(),
        name="last_norm",
    )(parts, x, gfirst, norms, perm)


def layer_kernel(
    lines,
    pairs,
    spans,
    neighbours,
    presence_ref,
    w_ref,
    norm_ref,
    x_ref,
    order_ref,
    cot_ref,
    near_ref,
    wts_ref,
    all_ref,
    out_ref,
    gin_ref,
    sums_ref,
    hid_ref,
    qkv_ref,
    att_ref,
    lse_ref,
    att_p_ref,
    first_ref,
    hid_p_ref,
    cross_q_ref,
    near_p_ref,
    near_kv_ref,
    co_p_ref,
    second_ref,
    own_ref,
    small_ref,
    rows_ref,
    w_qkv_ref,
    w_mid_ref,
    att_tok_ref,
    cross_ref,
    up_p_ref,
    up_t_ref,
    cot_p_ref,
    cot_t_ref,
    result_ref,
    back_ref,
    gfeed_ref,
    perm_ref,
    norms_ref,
    gatt_ref,
    acc_ref,
    gsib_ref,
    parts_ref,
    send_sems,
    z_sems,
    y_sems,
    x_sems,
    a_sems,
    b_sems,
    sib_sems,
    norm_sems,
    row_sems,
    att_sems,
    local_sems,
    qkv_sems,
    mid_sems,
    feed_sems,
    gatt_sems,
    gsib_sems,
    part_sems,
):
    place = Place(lines)
    z, me, core = place.z, place.me, place.core
    length, dim = hid_ref.shape
    width = pairs * LANES
    tokens = length // 8
    half = own_ref.shape[0] // 2
    near_load = pltpu.make_async_copy(near_ref, near_p_ref, local_sems.at[2])
    near_load.start()
    own_ref[...] = w_ref[...].astype(bf16)
    place.meet()
    send = Sender(place, send_sems)
    unit = partial(unit_of, wts_ref, lines)
    events = place.events()
    keep = pltpu.make_async_copy(own_ref, unit(z, me), local_sems.at[0])
    keep.start()

    def build_perm():
        row = lax.broadcasted_iota(jnp.int32, (dim, dim), 0)
        perm_ref[...] = jnp.where(row == order_ref[0:1, :], 1.0, 0.0).astype(bf16)

    def obtain(index):
        condition, line, far, side = events[index]
        mine = unit(line, me)
        src = own_ref if far == 0 else mine
        if far:
            send.arrived(condition, mine, z_sems.at[line])
        if side >= 0:
            send.start(both(condition, z > 0), src, mine, z_sems.at[line], z=z - 1)
        if side <= 0:
            send.start(both(condition, z < lines - 1), src, mine, z_sems.at[line], z=z + 1)
        send.start(condition, src, mine, x_sems.at[line], seq=place.xn)
        send.start(condition, src, mine, y_sems.at[line], seq=place.yn)
        send.start(condition, src, mine, sib_sems.at[0, line], seq=place.sib)

    def pass_on(index):
        condition, line, _, _ = events[index]
        from_x, from_y = unit(line, place.xn), unit(line, place.yn)
        send.arrived(condition, from_x, x_sems.at[line])
        part = unit(line, place.xn, half, half)
        send.start(condition, part, part, b_sems.at[line], seq=place.yn)
        send.start(condition, from_x, from_x, sib_sems.at[1, line], seq=place.sib)
        send.arrived(condition, from_y, y_sems.at[line])
        part = unit(line, place.yn, 0, half)
        send.start(condition, part, part, a_sems.at[line], seq=place.xn)
        send.start(condition, from_y, from_y, sib_sems.at[2, line], seq=place.sib)

    def corner(index):
        condition, line, _, _ = events[index]
        for group, begin, sems in ((3, 0, a_sems), (4, half, b_sems)):
            part = unit(line, place.dg, begin, half)
            send.arrived(condition, part, sems.at[line])
            send.start(condition, part, part, sib_sems.at[group, line], seq=place.sib)

    def row_block(seq):
        return rows_ref.at[pl.ds(pl.multiple_of(seq * tokens, tokens), tokens)]

    def middle(index):
        return pltpu.make_async_copy(
            wts_ref.at[:, pl.ds((3 + index) * dim, dim)], w_mid_ref.at[index], mid_sems.at[index]
        )

    obtain(0)
    own_rows = pltpu.make_async_copy(x_ref.at[place.chip], row_block(me), local_sems.at[1])
    own_rows.start()
    others = (place.xn, place.yn, place.dg)
    for other in place.line():
        send.start(None, norm_ref, small_ref.at[z], norm_sems.at[z], z=other)
    small_ref[z] = norm_ref[...]
    send.start(None, x_ref.at[place.chip], row_block(me), row_sems.at[me], seq=place.sib)
    for other in others:
        send.start(None, x_ref.at[other // 2], row_block(me), row_sems.at[me], seq=other)
    build_perm()
    near_load.wait()

    @pl.loop(0, near_p_ref.shape[0] // 512)
    def _(step):
        rows = rows_of(step, 512)
        near_p_ref[rows, :] = mm(near_p_ref[rows, :], perm_ref[...]).astype(bf16)

    obtain(1)
    obtain(2)
    pass_on(0)
    for other in others:
        send.arrived(None, row_block(other), row_sems.at[other])
        send.start(None, row_block(other), row_block(other), row_sems.at[other], seq=place.sib)
    obtain(3)
    obtain(4)
    cot_p_ref[...] = mm(cot_ref[...], perm_ref[...]).astype(bf16)
    cot_t_ref[...] = cot_p_ref[...].T
    pass_on(1)
    pass_on(2)
    corner(0)

    for other in place.line():
        send.arrived(None, small_ref.at[other], norm_sems.at[other])
    piece = small_ref.shape[2]
    total = None
    for line in range(lines):
        row = lax.broadcasted_iota(jnp.int32, (piece, dim), 0)
        column = lax.broadcasted_iota(jnp.int32, (piece, dim), 1)
        part = dim // lines
        place_of = jnp.logical_and(row < part, column == row + line * part).astype(bf16)
        term = mm(small_ref[line], place_of)
        total = term if total is None else total + term
    norms_ref[...] = total[: norms_ref.shape[0]]

    last = len(events)
    for index in range(5, last, 2):
        obtain(index)
        obtain(index + 1)
        if index == 5:
            for other in others:
                theirs = other + 1 - 2 * core
                send.arrived(None, row_block(theirs), row_sems.at[theirs])
            send.arrived(None, row_block(place.sib), row_sems.at[place.sib])
            own_rows.wait()
            norm_rows(rows_ref, norms_ref[...], perm_ref, hid_ref)
        pass_on(index - 2)
        pass_on(index - 1)
        corner(index - 4)
        corner(index - 3)
    for index in range(last - 2, last):
        pass_on(index)
    for index in range(last - 4, last):
        corner(index)
    keep.wait()
    for line in range(lines):
        for group, first in enumerate((me, place.xn, place.yn)):
            theirs = first + 1 - 2 * core
            send.arrived(None, unit(line, theirs), sib_sems.at[group, line])
        theirs = place.dg + 1 - 2 * core
        send.arrived(None, unit(line, theirs, 0, half), sib_sems.at[3, line])
        send.arrived(None, unit(line, theirs, half, half), sib_sems.at[4, line])
    copies = weight_copies(pairs, dim, wts_ref, w_qkv_ref, qkv_sems)
    for copy in copies + [middle(index) for index in (2, 3, 0, 1, 4)]:
        copy.start()
    for part in range(3):
        copies[part].wait()
        triple_part(part, pairs, hid_ref, w_qkv_ref, qkv_ref)

    share = lax.rem(me, dim // width)
    seq_rows = pl.ds(pl.multiple_of(place.chip * tokens, tokens), tokens)

    def landing(pair, chip_rows, share):
        lanes = pl.ds(pl.multiple_of(share * width + pair * LANES, LANES), LANES)
        return att_tok_ref.at[chip_rows, lanes]

    for pair in range(pairs):
        lanes = slice(pair * LANES, (pair + 1) * LANES)
        pair_forward(pair, pairs, qkv_ref, att_ref, lse_ref, lambda: None)
        for other in place.plane():
            block = att_ref.at[pl.ds(pl.multiple_of(other * tokens, tokens), tokens), lanes]
            to = landing(pair, seq_rows, share)
            send.start(None, block, to, att_sems.at[pair, me], seq=other)
        own_block = att_ref[pl.ds(pl.multiple_of(me * tokens, tokens), tokens), lanes]
        landing(pair, seq_rows, share)[...] = own_block

    for index in (2, 3, 0, 1, 4):
        middle(index).wait()
    for step in range(near_p_ref.shape[0] // 512):
        rows = slice(step * 512, (step + 1) * 512)
        near_kv_ref[rows, :dim] = mm(near_p_ref[rows, :], w_mid_ref[2]).astype(bf16)
        near_kv_ref[rows, dim:] = mm(near_p_ref[rows, :], w_mid_ref[3]).astype(bf16)
    w_out_ref, w_cq_ref, w_co_ref = (w_mid_ref.at[index] for index in (0, 1, 4))
    for pair in range(pairs):
        for other in place.plane():
            rows = pl.ds(pl.multiple_of(other // 2 * tokens, tokens), tokens)
            send.arrived(None, landing(pair, rows, lax.rem(other, 2)), att_sems.at[pair, other])
    att_p_ref[...] = mm(att_tok_ref[...], perm_ref[...]).astype(bf16)
    own_x = x_ref[...].reshape(first_ref.shape).astype(f32)
    first_ref[...] = own_x + mm(att_p_ref[...], w_out_ref[...])
    normed, _ = centre_scale(first_ref[...])
    hidden = (normed * norms_ref[2:3, :] + norms_ref[3:4, :]).astype(bf16)
    hid_p_ref[...] = mm(hidden, perm_ref[...]).astype(bf16)
    cross_q_ref[...] = mm(hid_p_ref[...], w_cq_ref[...]).astype(bf16)
    pl.loop(0, spans)(
        lambda span: span_forward(
            span, spans, neighbours, presence_ref, cross_q_ref, near_kv_ref, cross_ref
        )
    )

    ffw = (all_ref.shape[1] - 8 * dim) // 2
    tile = gfeed_ref.shape[2]
    order = range(0, ffw, tile)

    def tile_load(index):
        return [
            pltpu.make_async_copy(
                wts_ref.at[:, pl.ds(8 * dim + part * ffw + order[index], tile)],
                w_mid_ref.at[(2 * index + part) % 4],
                feed_sems.at[0, (2 * index + part) % 4],
            )
            for part in range(2)
        ]

    def tile_store(index):
        return [
            pltpu.make_async_copy(
                gfeed_ref.at[(2 * index + part) % 4],
                all_ref.at[:, pl.ds(8 * dim + part * ffw + order[index], tile)],
                feed_sems.at[1, (2 * index + part) % 4],
            )
            for part in range(2)
        ]

    for copy in tile_load(0) + tile_load(1):
        copy.start()
    co_p_ref[...] = mm(cross_ref[...], perm_ref[...]).astype(bf16)
    second_ref[...] = first_ref[...] + mm(co_p_ref[...], w_co_ref[...])
    normed, _ = centre_scale(second_ref[...])
    hidden = (normed * norms_ref[4:5, :] + norms_ref[5:6, :]).astype(bf16)
    up_p_ref[...] = mm(hidden, perm_ref[...]).astype(bf16)
    up_t_ref[...] = up_p_ref[...].T

    for index in range(len(order)):
        up_ref, down_ref = w_mid_ref.at[2 * index % 4], w_mid_ref.at[2 * index % 4 + 1]
        for copy in tile_load(index):
            copy.wait()
        if index >= 2:
            for copy in tile_store(index - 2):
                copy.wait()
        active, slope = gelu_parts(mm(up_p_ref[...], up_ref[...]))
        active = active.astype(bf16)
        term = nt(active, down_ref[...])
        result_ref[...] = term if index == 0 else result_ref[...] + term
        gfeed_ref[2 * index % 4 + 1] = mm(cot_t_ref[...], active).astype(bf16)
        grad_up = (mm(cot_p_ref[...], down_ref[...]) * slope).astype(bf16)
        gfeed_ref[2 * index % 4] = mm(up_t_ref[...], grad_up).astype(bf16)
        for copy in tile_store(index):
            copy.start()
        term = nt(grad_up, up_ref[...])
        back_ref[...] = term if index == 0 else back_ref[...] + term
        if index + 2 < len(order):
            for copy in tile_load(index + 2):
                copy.start()
        elif index + 2 == len(order):
            middle(0).start()
            middle(1).start()

    out_ref[...] = (second_ref[...] + nt(result_ref[...].astype(bf16), perm_ref[...])).astype(bf16)
    upstream = nt(back_ref[...].astype(bf16), perm_ref[...])
    normed, recip = centre_scale(second_ref[...])
    back, gain, shift = norm_back(upstream, normed, recip, norms_ref[4:5, :])
    gsecond_ref = second_ref
    gsecond_ref[...] = cot_ref[...].astype(f32) + back
    sums_ref[4:5, :] = gain
    sums_ref[5:6, :] = shift
    sums_ref[6:8, :] = jnp.zeros((2, dim), f32)
    for index in range(len(order) - 2, len(order)):
        for copy in tile_store(index):
            copy.wait()

    gco_ref, gcq_ref, gatt_tok_ref = up_p_ref, cot_p_ref, cross_ref
    outs = []

    def store(slot, part, first):
        copy = pltpu.make_async_copy(
            part, all_ref.at[:, pl.ds(first, part.shape[1])], feed_sems.at[1, slot]
        )
        outs.append(copy)
        copy.start()

    def keep_grad(index, value):
        slot = len(outs) % 4
        if len(outs) >= 4:
            outs[-4].wait()
        gfeed_ref[slot] = value.astype(bf16)
        store(slot, gfeed_ref.at[slot], (3 + index) * dim)

    upper = gsecond_ref[...].astype(bf16)
    gco_ref[...] = nt(nt(upper, w_co_ref[...]).astype(bf16), perm_ref[...]).astype(bf16)
    tables = (presence_ref, cross_q_ref, gco_ref, near_kv_ref, gcq_ref, near_kv_ref)
    pl.loop(0, spans)(lambda span: span_backward(span, spans, neighbours, *tables))
    for index in (0, 1):
        middle(index).wait()
    upstream = nt(nt(gcq_ref[...], w_cq_ref[...]).astype(bf16), perm_ref[...])
    normed, recip = centre_scale(first_ref[...])
    back, gain, shift = norm_back(upstream, normed, recip, norms_ref[2:3, :])
    sums_ref[2:3, :] = gain
    sums_ref[3:4, :] = shift
    gfirst_ref = gsecond_ref
    gfirst_ref[...] = gsecond_ref[...] + back
    lower = gfirst_ref[...].astype(bf16)
    gatt_tok_ref[...] = nt(nt(lower, w_out_ref[...]).astype(bf16), perm_ref[...]).astype(bf16)

    def gatt_block(device):
        return gatt_tok_ref.at[
            pl.ds(pl.multiple_of(device // 2 * tokens, tokens), tokens),
            pl.ds(pl.multiple_of(lax.rem(device, 2) * width, width), width),
        ]

    def gatt_rows(device):
        return gatt_ref.at[pl.ds(pl.multiple_of(device * tokens, tokens), tokens)]

    for other in place.plane():
        send.start(None, gatt_block(other), gatt_rows(me), gatt_sems.at[me], seq=other)
    own_gatt = pltpu.make_async_copy(gatt_block(me), gatt_rows(me), gatt_sems.at[me])
    own_gatt.start()
    keep_grad(4, mm(co_p_ref[...].T, upper))
    near_t = near_p_ref[...].T
    for part in range(2):
        keep_grad(2 + part, mm(near_t, near_kv_ref[:, part * dim : (part + 1) * dim]))
    keep_grad(1, mm(hid_p_ref[...].T, gcq_ref[...]))
    keep_grad(0, mm(att_p_ref[...].T, lower))
    for other in place.plane():
        send.arrived(None, gatt_rows(other), gatt_sems.at[other])
    own_gatt.wait()

    send.finish()
    grad_ref = near_kv_ref.at[pl.ds(0, length), pl.ds(0, 3 * width)]
    ghid_ref = rows_ref
    attention = (qkv_ref, att_ref, gatt_ref, lse_ref, grad_ref, acc_ref)
    pl.loop(0, pairs)(lambda pair: pair_backward(pair, pairs, *attention, lambda: None))
    for begin in range(0, length, 256):
        rows = slice(begin, begin + 256)
        ghid_ref[rows, :] = nt(grad_ref[rows, :], w_qkv_ref[...]).astype(bf16)
    chips = (place.xn // 2, place.yn // 2, place.dg // 2, place.chip)

    def token_rows(device):
        return pl.ds(pl.multiple_of(device * tokens, tokens), tokens)

    for chip in chips:
        theirs = ghid_ref.at[token_rows(chip * 2 + 1 - core)]
        send.start(None, theirs, gsib_ref.at[chip], gsib_sems.at[chip], seq=place.sib)

    for copy in outs[-4:]:
        copy.wait()
    outs.clear()
    gfeed_ref[3] = jnp.zeros_like(gfeed_ref[3])
    share_count = dim // width
    zeros = [
        pltpu.make_async_copy(
            gfeed_ref.at[3, :, pl.ds(0, width)],
            all_ref.at[
                :,
                pl.ds(
                    pl.multiple_of(part * dim + lax.rem(share + other, share_count) * width, LANES),
                    width,
                ),
            ],
            mid_sems.at[2 + part],
        )
        for part in range(3)
        for other in range(1, share_count)
    ]
    for copy in zeros:
        copy.start()
    hidden_t = hid_ref[...].T

    def triple_grad(part):
        columns = slice(part * width, (part + 1) * width)
        gfeed_ref[part, :, :width] = mm(hidden_t, grad_ref[:, columns]).astype(bf16)
        first = pl.multiple_of(part * dim + share * width, LANES)
        store(part, gfeed_ref.at[part, :, pl.ds(0, width)], first)

    triple_grad(0)
    triple_grad(1)
    for chip in chips:
        send.arrived(None, gsib_ref.at[chip], gsib_sems.at[chip])
        rows = token_rows(chip * 2 + core)
        total = (ghid_ref[rows, :].astype(f32) + gsib_ref[chip].astype(f32)).astype(bf16)
        if chip is place.chip:
            parts_ref[chip] = total
        else:
            ghid_ref[rows, :] = total
            landed, sem = parts_ref.at[place.chip], part_sems.at[place.chip]
            send.start(None, ghid_ref.at[rows], landed, sem, seq=chip * 2 + core)
    triple_grad(2)
    for chip in chips[:3]:
        send.arrived(None, parts_ref.at[chip], part_sems.at[chip])
    gain_sum = shift_sum = None
    for chip in range(4):
        rows = slice(chip * tokens, (chip + 1) * tokens)
        upstream = nt(parts_ref[chip], perm_ref[...])
        normed, recip = centre_scale(x_ref[chip].astype(f32))
        back, gain, shift = norm_back(upstream, normed, recip, norms_ref[0:1, :])
        gfirst_ref[rows, :] += back
        gain_sum = gain if gain_sum is None else gain_sum + gain
        shift_sum = shift if shift_sum is None else shift_sum + shift
    leave = pltpu.make_async_copy(gfirst_ref, gin_ref, local_sems.at[0])
    leave.start()
    sums_ref[0:1, :] = gain_sum
    sums_ref[1:2, :] = shift_sum
    for copy in outs + zeros:
        copy.wait()
    leave.wait()
    send.finish()


def layer(lines, pairs, spans, neighbours, presence, w_shard, n_shard, inputs, order, cot, near):
    unit_rows, unit_cols = w_shard.shape
    seqs, tokens, dim = inputs.shape
    count, length, width = seqs * tokens, 8 * tokens, pairs * LANES
    rows_near = near.shape[0]
    events = 2 * lines - 1
    any_space = pl.BlockSpec(memory_space=pl.ANY)
    vmem = pl.BlockSpec(memory_space=pltpu.VMEM)
    dma = pltpu.SemaphoreType.DMA
    packed = jax.ShapeDtypeStruct((unit_rows * lines, unit_cols * 8), bf16)
    tile = unit_cols // 2
    tokens_rows = (count, dim)
    scratch = [
        ((length, dim), bf16),
        ((3 * pairs, length, LANES), bf16),
        ((length, width), bf16),
        ((pairs, 2, length), f32),
        (tokens_rows, bf16),
        (tokens_rows, f32),
        (tokens_rows, bf16),
        (tokens_rows, bf16),
        ((rows_near, dim), bf16),
        ((rows_near, 2 * dim), bf16),
        (tokens_rows, bf16),
        (tokens_rows, f32),
        ((unit_rows, unit_cols), bf16),
        ((lines,) + n_shard.shape, bf16),
        ((length, dim), bf16),
        ((dim, 3 * width), bf16),
        ((5, dim, dim), bf16),
        (tokens_rows, bf16),
        (tokens_rows, bf16),
        (tokens_rows, bf16),
        ((dim, count), bf16),
        (tokens_rows, bf16),
        ((dim, count), bf16),
        (tokens_rows, f32),
        (tokens_rows, f32),
        ((4, dim, tile), bf16),
        ((dim, dim), bf16),
        ((8, dim), f32),
        ((length, width), bf16),
        ((2, length, LANES), f32),
        ((4, tokens, dim), bf16),
        ((4, tokens, dim), bf16),
    ]
    return pl.pallas_call(
        partial(layer_kernel, lines, pairs, spans, neighbours),
        out_shape=(
            packed,
            packed,
            jax.ShapeDtypeStruct(tokens_rows, bf16),
            jax.ShapeDtypeStruct(tokens_rows, f32),
            jax.ShapeDtypeStruct((8, dim), f32),
        ),
        in_specs=[pl.BlockSpec(memory_space=pltpu.SMEM)] + [vmem] * 5 + [any_space],
        out_specs=(any_space, any_space, vmem, any_space, vmem),
        scratch_shapes=[pltpu.VMEM(*entry) for entry in scratch]
        + [
            dma((11 * events + 7 + lines + 7 * pairs + 16,)),
            dma((lines,)),
            dma((lines,)),
            dma((lines,)),
            dma((lines,)),
            dma((lines,)),
            dma((5, lines)),
            dma((lines,)),
            dma((8,)),
            dma((pairs, 8)),
            dma((3,)),
            dma((3,)),
            dma((5,)),
            dma((2, 4)),
            dma((8,)),
            dma((4,)),
            dma((4,)),
        ],
        compiler_params=pltpu.CompilerParams(
            vmem_limit_bytes=VMEM_BYTES, collective_id=1, has_side_effects=True
        ),
        name="layer",
    )(presence, w_shard, n_shard, inputs, order, cot, near)


def reduce_kernel(
    lines,
    grads_ref,
    small_ref,
    shard_ref,
    norms_ref,
    mine_ref,
    sib_ref,
    corner_a_ref,
    corner_b_ref,
    from_x_ref,
    from_y_ref,
    below_ref,
    above_ref,
    early_below_ref,
    early_above_ref,
    plane_ref,
    plane_sum_ref,
    line_ref,
    send_sems,
    load_sems,
    sib_sems,
    a_sems,
    b_sems,
    x_sems,
    y_sems,
    below_sems,
    above_sems,
    early_below_sems,
    early_above_sems,
    plane_sems,
    line_sems,
):
    place = Place(lines)
    z, me = place.z, place.me
    unit_rows, unit_cols = shard_ref.shape
    early = early_below_ref.shape[2]
    place.meet()
    send = Sender(place, send_sems)
    chips = (place.dg, place.yn, place.xn, me)
    corner, over_y, over_x, here = range(4)

    unit = partial(unit_of, grads_ref, lines)

    def load(which, line):
        return pltpu.make_async_copy(
            unit(line, chips[which]), mine_ref.at[which, line], load_sems.at[which, line]
        )

    for other in place.plane():
        send.start(None, small_ref, plane_ref.at[me], plane_sems.at[me], seq=other)
    plane_ref[me] = small_ref[...]

    events = place.events()[::-1]
    count = len(events)

    def begin(index):
        condition, line, _, _ = events[index]
        for which in range(4):
            theirs = chips[which] + 1 - 2 * place.core
            send.start(
                condition,
                unit(line, theirs),
                sib_ref.at[which, line],
                sib_sems.at[which, line],
                seq=place.sib,
            )
            when(condition, load(which, line).start)

    def parts(index):
        if index == count:
            return 0, early // 2, early, (unit_rows - early) // 2, lines
        return early, (early + unit_rows) // 2, unit_rows, 0, events[index][1]

    def add(target, *terms, begin=0, end=unit_rows):
        tile = next(size for size in (96, 80, 64, 32, 16) if (end - begin) % size == 0)

        @pl.loop(0, (end - begin) // tile)
        def _(step):
            rows = pl.ds(pl.multiple_of(begin + step * tile, 16), tile)
            total = target[rows, :]
            if len(terms) > 1:
                total = total.astype(f32)
            for ref, first in terms:
                at = pl.ds(pl.multiple_of(begin - first + step * tile, 16), tile)
                term = ref[at, :]
                total = total + (term if len(terms) == 1 else term.astype(f32))
            target[rows, :] = total.astype(target.dtype)

    def early_rows(line):
        return mine_ref.at[:, line, pl.ds(0, early), :]

    def add_early(line, landing):
        for which in range(4):
            add(mine_ref.at[which, line], (landing.at[line, which], 0), end=early)

    def first(index):
        condition, line, far, side = events[min(index, count - 1)]
        low, middle, high, base, sem = parts(index)
        if index < count:
            for which in range(4):
                send.arrived(condition, sib_ref.at[which, line], sib_sems.at[which, line])
                when(condition, load(which, line).wait)

            def chip_sum():
                for which in range(4):
                    add(mine_ref.at[which, line], (sib_ref.at[which, line], 0))

            when(condition, chip_sum)
        if far or index == count:
            from_below, from_above = both(condition, z > 0), both(condition, z < lines - 1)
            sides = ((from_below, early_below_ref, early_below_sems),) if side >= 0 else ()
            if side <= 0:
                sides += ((from_above, early_above_ref, early_above_sems),)
            for on, landing, sems in sides:
                send.arrived(on, landing.at[line], sems.at[line])
                when(on, partial(add_early, line, landing))
        if far:
            landing, sems = sides[0][1:]
            send.start(condition, early_rows(line), landing.at[line], sems.at[line], z=z + side)
        target = mine_ref.at[corner, line]
        for begins, ends, landing, sems, to in (
            (low, middle, corner_a_ref, a_sems, place.xn),
            (middle, high, corner_b_ref, b_sems, place.yn),
        ):
            send.start(
                condition,
                target.at[pl.ds(begins, ends - begins)],
                landing.at[line, pl.ds(base, ends - begins)],
                sems.at[sem],
                seq=to,
            )

    def second(index):
        condition, line, _, _ = events[min(index, count - 1)]
        low, middle, high, base, sem = parts(index)
        for which, part, sems, begins, ends, to, landing, landing_sems in (
            (over_y, corner_a_ref, a_sems, low, middle, place.yn, from_y_ref, y_sems),
            (over_x, corner_b_ref, b_sems, middle, high, place.xn, from_x_ref, x_sems),
        ):
            send.arrived(condition, part.at[line, pl.ds(base, ends - begins)], sems.at[sem])
            target = mine_ref.at[which, line]
            term = (part.at[line], begins - base)
            when(condition, partial(add, target, term, begin=begins, end=ends))
            rows = pl.ds(low, high - low)
            landed = landing.at[line, rows]
            send.start(condition, target.at[rows], landed, landing_sems.at[sem], seq=to)

    def third(index):
        condition, line, far, side = events[min(index, count - 1)]
        low, _, high, _, sem = parts(index)
        rows = pl.ds(low, high - low)
        send.arrived(condition, from_x_ref.at[line, rows], x_sems.at[sem])
        send.arrived(condition, from_y_ref.at[line, rows], y_sems.at[sem])
        target = mine_ref.at[here, line]
        terms = [(from_x_ref.at[line], 0), (from_y_ref.at[line], 0)]
        if far == 0:
            tile = 32

            @pl.loop(low // tile, high // tile)
            def _(step):
                at = rows_of(step, tile)
                total = target[at, :].astype(f32)
                for ref, _ in terms:
                    total = total + ref[at, :].astype(f32)
                shard_ref[at, :] = total

            if index < count:
                for on, ref, sems in (
                    (z > 0, below_ref, below_sems),
                    (z < lines - 1, above_ref, above_sems),
                ):
                    send.arrived(on, ref.at[line, rows], sems.at[line])
                    when(on, partial(add, shard_ref, (ref.at[line], 0), begin=low))
            return
        landing, sems = (below_ref, below_sems) if side > 0 else (above_ref, above_sems)
        more = both(condition, z > 0) if side > 0 else both(condition, z < lines - 1)
        none = both(condition, z == 0) if side > 0 else both(condition, z == lines - 1)
        send.arrived(more, landing.at[line, rows], sems.at[line])
        when(more, partial(add, target, *terms, (landing.at[line], 0), begin=low))
        when(none, partial(add, target, *terms, begin=low))
        landed = landing.at[line, rows]
        send.start(condition, target.at[rows], landed, sems.at[line], z=z + side)

    for index in range(min(4, count)):
        begin(index)
    first(0)
    first(1)
    for index in range(2, count + 2):
        if index + 2 < count:
            begin(index + 2)
        if index < count:
            first(index)
        if 0 <= index - 2 < count:
            second(index - 2)
        if index == count:
            first(count)
        if index == 3:
            for other in place.plane():
                send.arrived(None, plane_ref.at[other], plane_sems.at[other])
            total = plane_ref[0]
            for other in range(1, 8):
                total = total + plane_ref[other]
            plane_sum_ref[...] = total
            line_ref[z] = total
            for other in place.line():
                send.start(None, plane_sum_ref, line_ref.at[z], line_sems.at[z], z=other)
        if 0 <= index - 4 <= count - 3:
            third(index - 4)
        if index == count + 1:
            third(count - 2)
            second(count)
            third(count - 1)
            third(count)

    for other in place.line():
        send.arrived(None, line_ref.at[other], line_sems.at[other])
    total = line_ref[0]
    for other in range(1, lines):
        total = total + line_ref[other]
    norms_ref[...] = total
    send.finish()


def reduce_grads(lines, grads, small):
    rows, cols = grads.shape
    unit_rows, unit_cols = rows // lines, cols // 8
    half = unit_rows // 2
    early = unit_rows // 96 * 16
    any_space = pl.BlockSpec(memory_space=pl.ANY)
    vmem = pl.BlockSpec(memory_space=pltpu.VMEM)
    dma = pltpu.SemaphoreType.DMA
    return pl.pallas_call(
        partial(reduce_kernel, lines),
        out_shape=(
            jax.ShapeDtypeStruct((unit_rows, unit_cols), f32),
            jax.ShapeDtypeStruct(small.shape, f32),
        ),
        in_specs=[any_space, vmem],
        out_specs=(vmem, vmem),
        scratch_shapes=[
            pltpu.VMEM((4, lines, unit_rows, unit_cols), bf16),
            pltpu.VMEM((4, lines, unit_rows, unit_cols), bf16),
            pltpu.VMEM((lines, half, unit_cols), bf16),
            pltpu.VMEM((lines, half, unit_cols), bf16),
            pltpu.VMEM((lines, unit_rows, unit_cols), bf16),
            pltpu.VMEM((lines, unit_rows, unit_cols), bf16),
            pltpu.VMEM((lines, unit_rows, unit_cols), bf16),
            pltpu.VMEM((lines, unit_rows, unit_cols), bf16),
            pltpu.VMEM((lines, 4, early, unit_cols), bf16),
            pltpu.VMEM((lines, 4, early, unit_cols), bf16),
            pltpu.VMEM((8,) + small.shape, f32),
            pltpu.VMEM(small.shape, f32),
            pltpu.VMEM((lines,) + small.shape, f32),
            dma((10 * (2 * lines - 1) + 4 + 7 + lines,)),
            dma((4, lines)),
            dma((4, lines)),
            dma((lines + 1,)),
            dma((lines + 1,)),
            dma((lines + 1,)),
            dma((lines + 1,)),
            dma((lines,)),
            dma((lines,)),
            dma((lines,)),
            dma((lines,)),
            dma((8,)),
            dma((lines,)),
        ],
        compiler_params=pltpu.CompilerParams(
            vmem_limit_bytes=VMEM_BYTES, collective_id=4, has_side_effects=True
        ),
        name="reduce_grads",
    )(grads, small)


def adam_update(grad, weight, first, second, average, rate, decay):
    first = beta_first * first + (1.0 - beta_first) * grad
    second = beta_second * second + (1.0 - beta_second) * grad * grad
    stepped = (
        first / (1.0 - beta_first**STEP) / (jnp.sqrt(second / (1.0 - beta_second**STEP)) + adam_eps)
    )
    weight = weight - rate * (stepped + decay * weight)
    average = ema_decay * average + (1.0 - ema_decay) * weight
    return (first, second, weight, average)


def on_device(
    inputs,
    cotangent,
    neighbours,
    presence,
    row_order,
    w_master,
    w_first,
    w_second,
    w_average,
    n_master,
    n_first,
    n_second,
    n_average,
):
    seqs, tokens, dim = inputs.shape
    heads = dim // HEAD
    devices = lax.axis_size("seq")
    count = seqs * tokens
    length = devices * tokens
    me = lax.axis_index("seq")
    shares = devices // seqs
    held = heads // shares
    pairs = (held + 1) // 2
    width = pairs * LANES
    spare = width - held * HEAD
    sequence, share = me // shares, me % shares

    lines = lax.axis_size("dp")
    planar = devices == 8 and seqs == 4 and spare == 0
    x = inputs.reshape(count, dim)
    cot = cotangent.reshape(count, dim)
    spans = seqs * neighbours.shape[1]
    each = neighbours.shape[2]
    near = neighbours.reshape(-1, dim)
    live = presence.reshape(-1)
    part = n_master.shape[1]
    if planar:
        small = jnp.pad(n_master.astype(bf16), ((0, 16 - 6), (0, -part % LANES)))
        order = row_order.reshape(1, dim)
        _, grads, outputs, grad_inputs, norm_grads = layer(
            lines, pairs, spans, each, live, w_master, small, inputs, order, cot, near
        )
        grad_shard, norm_sums = reduce_grads(lines, grads, norm_grads)
        norm_shard = lax.dynamic_slice(norm_sums, (0, lax.axis_index("dp") * part), (6, part))
    else:
        perm = (jnp.arange(dim)[:, None] == row_order[None, :]).astype(bf16)
        perm_att = jnp.pad(perm.reshape(shares, held * HEAD, dim), ((0, 0), (0, spare), (0, 0)))
        perm_att = perm_att.reshape(shares * width, dim)
        weights = lax.all_gather(w_master.astype(bf16), "dp", axis=0, tiled=True)
        weights = lax.all_gather(weights, "seq", axis=1, tiled=True)
        norms = lax.all_gather(n_master.astype(bf16), "dp", axis=1, tiled=True).astype(f32)
        rows = lax.all_to_all(jnp.repeat(inputs, shares, axis=0), "seq", 0, 0)
        rows = rows.reshape(length, dim)
        w_qkv = weights[:, : 3 * dim].reshape(dim, 3, shares, held * HEAD)
        w_qkv = lax.dynamic_index_in_dim(w_qkv, share, axis=2, keepdims=False)
        w_qkv = jnp.pad(w_qkv, ((0, 0), (0, 0), (0, spare))).reshape(dim, 3 * width)
        hid, qkv, att, lse = self_forward(pairs, rows, norms, perm, w_qkv)
        att_tok = (
            lax.all_to_all(att.reshape(devices, tokens, width), "seq", 0, 0)
            .reshape(seqs, shares, tokens, width)
            .transpose(0, 2, 1, 3)
            .reshape(count, shares * width)
        )
        att_p, first, hid_p, cross_q, near_p, near_kv, co_p, second = cross_forward(
            spans, each, live, att_tok, x, norms, perm, perm_att, near, weights
        )
        outputs, gsecond, grads, gnorm_e = feed(second, cot, norms, perm, weights)
        gfirst, gatt_tok, grads, gnorm_c = cross_backward(
            spans,
            each,
            live,
            gsecond,
            first,
            norms,
            perm,
            perm_att,
            att_p,
            hid_p,
            cross_q,
            near_p,
            near_kv,
            co_p,
            weights,
            grads,
        )
        gatt = lax.all_to_all(
            gatt_tok.reshape(seqs, tokens, shares, width)
            .transpose(0, 2, 1, 3)
            .reshape(devices, tokens, width),
            "seq",
            0,
            0,
        ).reshape(length, width)
        gqkv, ghid = self_backward(pairs, qkv, att, gatt, lse, hid, w_qkv)
        parts = (
            lax.all_to_all(ghid.reshape(devices, tokens, dim), "seq", 0, 0)
            .reshape(seqs, shares, tokens, dim)
            .transpose(1, 0, 2, 3)
            .reshape(shares, count, dim)
        )
        grad_inputs, gnorm_a = last_norm(parts, x, gfirst, norms, perm)
        gqkv = gqkv.reshape(dim, 3, 1, width)[..., : held * HEAD]
        gqkv = jnp.where(jnp.arange(shares)[:, None] == share, gqkv, jnp.zeros_like(gqkv))
        grads = lax.dynamic_update_slice(grads, gqkv.reshape(dim, 3 * dim), (0, 0))
        norm_grads = lax.psum(jnp.concatenate([gnorm_a, gnorm_c, gnorm_e], axis=0), "seq")
        partial_sum = lax.psum_scatter(grads, "seq", scatter_dimension=1, tiled=True)
        grad_shard = lax.psum_scatter(partial_sum, "dp", scatter_dimension=0, tiled=True)
        grad_shard = grad_shard.astype(f32)
        norm_shard = lax.psum_scatter(
            norm_grads.astype(bf16), "dp", scatter_dimension=1, tiled=True
        ).astype(f32)
    w_first_new, w_second_new, w_new, w_average_new = adam_update(
        grad_shard, w_master, w_first, w_second, w_average, learn_rate, weight_decay
    )
    n_first_new, n_second_new, n_new, n_average_new = adam_update(
        norm_shard, n_master, n_first, n_second, n_average, norm_rate, 0.0
    )
    return (
        outputs.reshape(seqs, tokens, dim),
        grad_inputs.reshape(seqs, tokens, dim),
        w_first_new,
        w_second_new,
        w_new,
        w_average_new,
        n_first_new,
        n_second_new,
        n_new,
        n_average_new,
    )


def solution(mesh):
    in_specs = (
        P("dp", "seq", None),
        P("dp", "seq", None),
        P("dp", "seq", None, None, None),
        P("dp", "seq", None),
        P(),
        P("dp", "seq"),
        P("dp", "seq"),
        P("dp", "seq"),
        P("dp", "seq"),
        P(None, "dp"),
        P(None, "dp"),
        P(None, "dp"),
        P(None, "dp"),
    )
    out_specs = (
        P("dp", "seq", None),
        P("dp", "seq", None),
        P("dp", "seq"),
        P("dp", "seq"),
        P("dp", "seq"),
        P("dp", "seq"),
        P(None, "dp"),
        P(None, "dp"),
        P(None, "dp"),
        P(None, "dp"),
    )
    return jax.shard_map(
        on_device, mesh=mesh, in_specs=in_specs, out_specs=out_specs, check_vma=False
    )
```

```python
from functools import partial

import jax
import jax.numpy as jnp
from jax import lax
from jax.experimental import pallas as pl
from jax.experimental.pallas import tpu as pltpu
from jax.sharding import PartitionSpec as P

HEAD = 64
STEP = 5
LANES = 128
SCALE = HEAD ** (-0.5)

beta_first = 0.9
beta_second = 0.95
adam_eps = 1e-08
learn_rate = 0.04
norm_rate = 0.6
weight_decay = 0.1
ema_decay = 0.5
norm_eps = 1e-05
masked_score = -1e30
VMEM_BYTES = 62 * 1024 * 1024
bf16 = jnp.bfloat16
f32 = jnp.float32


def mm(left, right):
    return lax.dot_general(left, right, (((1,), (0,)), ((), ())), preferred_element_type=f32)


def nt(left, right):
    return lax.dot_general(left, right, (((1,), (1,)), ((), ())), preferred_element_type=f32)


def tn(left, right):
    return lax.dot_general(left, right, (((0,), (0,)), ((), ())), preferred_element_type=f32)


def params():
    return pltpu.CompilerParams(vmem_limit_bytes=VMEM_BYTES)


def rows_of(index, size):
    return pl.ds(pl.multiple_of(index * size, size), size)


def centre_scale(values):
    centre = jnp.mean(values, axis=-1, keepdims=True)
    centred = values - centre
    spread = jnp.mean(centred * centred, axis=-1, keepdims=True)
    recip = lax.rsqrt(spread + norm_eps)
    return centred * recip, recip


def norm_back(upstream, normed, recip, gain):
    scaled = upstream * gain
    inner = (
        scaled
        - jnp.mean(scaled, axis=-1, keepdims=True)
        - normed * jnp.mean(scaled * normed, axis=-1, keepdims=True)
    )
    return (
        recip * inner,
        jnp.sum(upstream * normed, axis=0, keepdims=True),
        jnp.sum(upstream, axis=0, keepdims=True),
    )


def gelu_parts(value):
    const = 0.7978845608028654
    square = value * value
    bend = jnp.tanh(const * value * (1.0 + 0.044715 * square))
    half = 0.5 * (1.0 + bend)
    slope = half + 0.5 * value * (1.0 - bend * bend) * (const * (1.0 + 3 * 0.044715 * square))
    return value * half, slope


def head_mask(rows, half):
    lane = lax.broadcasted_iota(jnp.int32, (rows, LANES), 1)
    return (lane < HEAD) if half == 0 else (lane >= HEAD)


def pick(mask, value):
    return jnp.where(mask, value, jnp.zeros_like(value))


MESH = pl.DeviceIdType.MESH


class Place:
    def __init__(self, lines):
        self.lines = lines
        self.z = lax.axis_index("dp")
        self.me = lax.axis_index("seq")
        core, x, y = self.me % 2, (self.me // 2) % 2, self.me // 4
        self.core, self.x, self.y, self.chip = core, x, y, self.me // 2
        self.sib = self.me + 1 - 2 * core
        self.xn = self.me + 2 - 4 * x
        self.yn = self.me + 4 - 8 * y
        self.dg = self.xn + 4 - 8 * y

    def events(self):
        found = [(None, self.z, 0, 0)]
        for far in range(1, self.lines):
            found.append((self.z >= far, self.z - far, far, -1))
            found.append((self.z + far < self.lines, self.z + far, far, 1))
        return found

    def plane(self):
        return [lax.rem(self.me + step, 8) for step in range(1, 8)]

    def line(self):
        return [lax.rem(self.z + step, self.lines) for step in range(1, self.lines)]

    def meet(self):
        barrier = pltpu.get_barrier_semaphore()
        for other in self.plane():
            pl.semaphore_signal(
                barrier, inc=1, device_id={"dp": self.z, "seq": other}, device_id_type=MESH
            )
        for other in self.line():
            pl.semaphore_signal(
                barrier, inc=1, device_id={"dp": other, "seq": self.me}, device_id_type=MESH
            )
        pl.semaphore_wait(barrier, 7 + self.lines - 1)


def when(condition, body):
    if condition is None:
        body()
    else:
        pl.when(condition)(body)


def both(first, second):
    if first is None or second is None:
        return second if first is None else first
    return jnp.logical_and(first, second)


class Sender:
    def __init__(self, place, send_sems):
        self.place, self.sems, self.open, self.count = place, send_sems, [], 0

    def start(self, condition, src, dst, recv_sem, z=None, seq=None):
        place = self.place
        target = {"dp": place.z if z is None else z, "seq": place.me if seq is None else seq}
        copy = pltpu.make_async_remote_copy(
            src_ref=src,
            dst_ref=dst,
            send_sem=self.sems.at[self.count],
            recv_sem=recv_sem,
            device_id=target,
            device_id_type=MESH,
        )
        self.open.append((condition, copy))
        self.count += 1
        when(condition, copy.start)

    def arrived(self, condition, ref, recv_sem):
        copy = pltpu.make_async_remote_copy(
            src_ref=ref,
            dst_ref=ref,
            send_sem=self.sems.at[0],
            recv_sem=recv_sem,
            device_id={"dp": self.place.z, "seq": self.place.sib},
            device_id_type=MESH,
        )
        when(condition, copy.wait_recv)

    def finish(self):
        for condition, copy in self.open:
            when(condition, copy.wait_send)
        self.open = []


class Weave:
    def __init__(self, steps):
        self.steps = list(steps)

    def some(self, count):
        for _ in range(min(count, len(self.steps))):
            self.steps.pop(0)()

    def rest(self):
        self.some(len(self.steps))


def unit_of(ref, lines, line, seq, begin=0, size=None):
    rows, cols = ref.shape[0] // lines, ref.shape[1] // 8
    size = rows if size is None else size
    return ref.at[
        pl.ds(pl.multiple_of(line * rows + begin, 16), size),
        pl.ds(pl.multiple_of(seq * cols, cols), cols),
    ]


def weight_copies(pairs, dim, wts_ref, w_ref, sems):
    width = pairs * LANES
    first = lax.rem(lax.axis_index("seq"), dim // width) * width
    return [
        pltpu.make_async_copy(
            wts_ref.at[:, pl.ds(pl.multiple_of(first + part * dim, LANES), width)],
            w_ref.at[:, pl.ds(part * width, width)],
            sems.at[part],
        )
        for part in range(3)
    ]


def pair_forward(pair, pairs, qkv_ref, att_ref, lse_ref, between):
    length = att_ref.shape[0]
    tile = 256
    below = lax.broadcasted_iota(jnp.int32, (tile, tile), 1) <= lax.broadcasted_iota(
        jnp.int32, (tile, tile), 0
    )
    masks = [head_mask(tile, 0), head_mask(tile, 1)]
    lane = lax.broadcasted_iota(jnp.int32, (tile, LANES), 1)
    for step in range(length // tile):
        rows = slice(step * tile, (step + 1) * tile)
        query = qkv_ref[pair, rows, :] * SCALE
        keys_here = qkv_ref[pairs + pair, rows, :]
        values_here = qkv_ref[2 * pairs + pair, rows, :]
        outs, logs = [], []
        for half in range(2):
            mine = pick(masks[half], query)
            here = jnp.where(below, nt(mine, keys_here), masked_score)
            peak = jnp.max(here, axis=-1, keepdims=True)
            if step:
                past = nt(mine, qkv_ref[pairs + pair, : step * tile, :])
                peak = jnp.maximum(peak, jnp.max(past, axis=-1, keepdims=True))
                past = jnp.exp(past - peak)
            here = jnp.exp(here - peak)
            total = jnp.sum(here, axis=-1, keepdims=True)
            out = mm(here.astype(bf16), values_here)
            if step:
                total = total + jnp.sum(past, axis=-1, keepdims=True)
                out = out + mm(past.astype(bf16), qkv_ref[2 * pairs + pair, : step * tile, :])
            outs.append(out / total)
            logs.append(peak + jnp.log(total))
        lse_ref[pair, :, rows] = jnp.where(lane == 0, logs[0], logs[1]).T[0:2, :]
        att_ref[rows, pl.ds(pl.multiple_of(pair * LANES, LANES), LANES)] = jnp.where(
            masks[0], outs[0], outs[1]
        ).astype(bf16)
        between()


def norm_rows(x_ref, norms, perm_ref, hid_ref):
    tile = 256

    @pl.loop(0, x_ref.shape[0] // tile)
    def _(step):
        rows = rows_of(step, tile)
        normed, _ = centre_scale(x_ref[rows, :].astype(f32))
        hidden = (normed * norms[0:1, :] + norms[1:2, :]).astype(bf16)
        hid_ref[rows, :] = mm(hidden, perm_ref[...]).astype(bf16)


def triple_part(part, pairs, hid_ref, w_ref, qkv_ref):
    width = pairs * LANES
    triple = mm(hid_ref[...], w_ref[:, part * width : (part + 1) * width]).astype(bf16)
    for pair in range(pairs):
        qkv_ref[part * pairs + pair] = triple[:, pair * LANES : (pair + 1) * LANES]


def self_forward_kernel(
    pairs, x_ref, norms_ref, perm_ref, w_ref, hid_ref, qkv_ref, att_ref, lse_ref
):
    norm_rows(x_ref, norms_ref, perm_ref, hid_ref)
    for part in range(3):
        triple_part(part, pairs, hid_ref, w_ref, qkv_ref)

    @pl.loop(0, pairs)
    def _(pair):
        pair_forward(pair, pairs, qkv_ref, att_ref, lse_ref, lambda: None)


def self_forward(pairs, x, norms, perm, w):
    length, dim = x.shape
    return pl.pallas_call(
        partial(self_forward_kernel, pairs),
        out_shape=(
            jax.ShapeDtypeStruct((length, dim), bf16),
            jax.ShapeDtypeStruct((3 * pairs, length, LANES), bf16),
            jax.ShapeDtypeStruct((length, pairs * LANES), bf16),
            jax.ShapeDtypeStruct((pairs, 2, length), f32),
        ),
        compiler_params=params(),
        name="self_forward",
    )(x, norms, perm, w)


def pair_backward(pair, pairs, qkv_ref, att_ref, gatt_ref, lse_ref, grad_ref, acc_ref, between):
    length = att_ref.shape[0]
    width = pairs * LANES
    tile = 256
    above = lax.broadcasted_iota(jnp.int32, (tile, tile), 0) <= lax.broadcasted_iota(
        jnp.int32, (tile, tile), 1
    )
    masks = [head_mask(tile, 0), head_mask(tile, 1)]
    lanes = pl.ds(pl.multiple_of(pair * LANES, LANES), LANES)
    for step in range(length // tile):
        rows = slice(step * tile, (step + 1) * tile)
        query = qkv_ref[pair, rows, :] * SCALE
        grad_out = gatt_ref[rows, lanes]
        product = grad_out.astype(f32) * att_ref[rows, lanes].astype(f32)
        queries = [pick(masks[half], query) for half in range(2)]
        grads = [pick(masks[half], grad_out) for half in range(2)]
        deltas = [jnp.sum(pick(masks[half], product).T, axis=0, keepdims=True) for half in range(2)]
        grad_query = [None, None]
        for other in range(step + 1):
            cols = slice(other * tile, (other + 1) * tile)
            keys = qkv_ref[pairs + pair, cols, :]
            values = qkv_ref[2 * pairs + pair, cols, :]
            key_part = value_part = None
            for half in range(2):
                scores = nt(keys, queries[half])
                if other == step:
                    scores = jnp.where(above, scores, masked_score)
                probs = jnp.exp(scores - lse_ref[pair, half : half + 1, rows])
                grad_scores = (probs * (nt(values, grads[half]) - deltas[half])).astype(bf16)
                query_term = tn(grad_scores, keys)
                grad_query[half] = (
                    query_term if grad_query[half] is None else grad_query[half] + query_term
                )
                key_term = mm(grad_scores, queries[half])
                value_term = mm(probs.astype(bf16), grads[half])
                key_part = key_term if key_part is None else key_part + key_term
                value_part = value_term if value_part is None else value_part + value_term
            if other == step:
                acc_ref[0, cols, :] = key_part
                acc_ref[1, cols, :] = value_part
            else:
                acc_ref[0, cols, :] += key_part
                acc_ref[1, cols, :] += value_part
        grad_ref[rows, lanes] = (jnp.where(masks[0], grad_query[0], grad_query[1]) * SCALE).astype(
            bf16
        )
        between()
    for part in range(2):
        lanes_to = pl.ds(pl.multiple_of((part + 1) * width + pair * LANES, LANES), LANES)
        grad_ref[:, lanes_to] = acc_ref[part].astype(bf16)


def self_backward_kernel(
    pairs,
    qkv_ref,
    att_ref,
    gatt_ref,
    lse_ref,
    hid_ref,
    w_ref,
    gw_ref,
    ghid_ref,
    grad_ref,
    acc_ref,
):
    length = att_ref.shape[0]
    width = pairs * LANES
    attention = (qkv_ref, att_ref, gatt_ref, lse_ref, grad_ref, acc_ref)

    @pl.loop(0, pairs)
    def _(pair):
        pair_backward(pair, pairs, *attention, lambda: None)

    hidden_t = hid_ref[...].T
    for part in range(3):
        cols = slice(part * width, (part + 1) * width)
        gw_ref[:, cols] = mm(hidden_t, grad_ref[:, cols]).astype(bf16)
    for begin in range(0, length, 256):
        rows = slice(begin, begin + 256)
        ghid_ref[rows, :] = nt(grad_ref[rows, :], w_ref[...]).astype(bf16)


def self_backward(pairs, qkv, att, gatt, lse, hid, w):
    length, dim = hid.shape
    width = pairs * LANES
    return pl.pallas_call(
        partial(self_backward_kernel, pairs),
        out_shape=(
            jax.ShapeDtypeStruct((dim, 3 * width), bf16),
            jax.ShapeDtypeStruct((length, dim), bf16),
        ),
        scratch_shapes=[
            pltpu.VMEM((length, 3 * width), bf16),
            pltpu.VMEM((2, length, LANES), f32),
        ],
        compiler_params=params(),
        name="self_backward",
    )(qkv, att, gatt, lse, hid, w)


def spread_heads(block, rows, group):
    lane = lax.broadcasted_iota(jnp.int32, block.shape, 1) // HEAD
    return jnp.concatenate([pick(lane == head, block) for head in range(group)], axis=0)


def gather_heads(stacked, rows, group):
    lane = lax.broadcasted_iota(jnp.int32, (rows, stacked.shape[1]), 1) // HEAD
    out = None
    for head in range(group):
        part = pick(lane == head, stacked[head * rows : (head + 1) * rows])
        out = part if out is None else out + part
    return out


def live_keys(presence_ref, span, shape, axis, neighbours, each):
    index = lax.broadcasted_iota(jnp.int32, shape, axis) // each
    live = jnp.zeros(shape, f32)
    anyone = None
    for which in range(neighbours):
        here = presence_ref[span * neighbours + which]
        there = jnp.where(here > 0, 1.0, 0.0).astype(f32)
        live = jnp.where(index == which, there, live)
        anyone = here if anyone is None else jnp.maximum(anyone, here)
    return live, anyone.astype(f32)


def span_forward(span, spans, neighbours, presence_ref, cross_q_ref, near_kv_ref, cross_ref):
    count, dim = cross_q_ref.shape
    span_len = count // spans
    near = near_kv_ref.shape[0] // spans
    group = 256 // HEAD
    rows = rows_of(span, span_len)
    keys = rows_of(span, near)
    live, anyone = live_keys(presence_ref, span, (1, near), 1, neighbours, near // neighbours)
    for begin in range(0, dim, group * HEAD):
        lanes = slice(begin, begin + group * HEAD)
        lanes_v = slice(dim + begin, dim + begin + group * HEAD)
        query = spread_heads(cross_q_ref[rows, lanes] * SCALE, span_len, group)
        scores = jnp.where(live > 0, nt(query, near_kv_ref[keys, lanes]), masked_score)
        peak = jnp.max(scores, axis=-1, keepdims=True)
        expon = jnp.exp(scores - peak) * live
        total = jnp.sum(expon, axis=-1, keepdims=True) + 1.0 - anyone
        out = mm(expon.astype(bf16), near_kv_ref[keys, lanes_v]) / total
        cross_ref[rows, lanes] = gather_heads(out, span_len, group).astype(bf16)


def cross_forward_kernel(
    spans,
    neighbours,
    presence_ref,
    att_ref,
    x_ref,
    norms_ref,
    perm_ref,
    perm_att_ref,
    near_ref,
    w_out_ref,
    w_cq_ref,
    w_ck_ref,
    w_cv_ref,
    w_co_ref,
    att_p_ref,
    first_ref,
    hid_p_ref,
    cross_q_ref,
    near_p_ref,
    near_kv_ref,
    co_p_ref,
    second_ref,
    cross_ref,
):
    count, dim = x_ref.shape
    rows_near = near_ref.shape[0]
    tile = 512

    att_p_ref[...] = mm(att_ref[...], perm_att_ref[...]).astype(bf16)
    first_ref[...] = x_ref[...].astype(f32) + mm(att_p_ref[...], w_out_ref[...])

    normed, _ = centre_scale(first_ref[...])
    hidden = (normed * norms_ref[2:3, :] + norms_ref[3:4, :]).astype(bf16)
    hid_p_ref[...] = mm(hidden, perm_ref[...]).astype(bf16)
    cross_q_ref[...] = mm(hid_p_ref[...], w_cq_ref[...]).astype(bf16)

    @pl.loop(0, rows_near // tile)
    def _(step):
        rows = rows_of(step, tile)
        near_p_ref[rows, :] = mm(near_ref[rows, :], perm_ref[...]).astype(bf16)
        near_kv_ref[rows, :dim] = mm(near_p_ref[rows, :], w_ck_ref[...]).astype(bf16)
        near_kv_ref[rows, dim:] = mm(near_p_ref[rows, :], w_cv_ref[...]).astype(bf16)

    @pl.loop(0, spans)
    def _(span):
        span_forward(span, spans, neighbours, presence_ref, cross_q_ref, near_kv_ref, cross_ref)

    co_p_ref[...] = mm(cross_ref[...], perm_ref[...]).astype(bf16)
    second_ref[...] = first_ref[...] + mm(co_p_ref[...], w_co_ref[...])


def column_block(rows, width, index):
    return pl.BlockSpec((rows, width), lambda *_: (0, index), pipeline_mode=pl.Buffered(1))


def whole(array):
    return pl.BlockSpec(array.shape, lambda *_: (0,) * array.ndim, pipeline_mode=pl.Buffered(1))


def whole_shape(shape):
    return pl.BlockSpec(shape, lambda *_: (0,) * len(shape), pipeline_mode=pl.Buffered(1))


def cross_forward(spans, neighbours, presence, att, x, norms, perm, perm_att, near, weights):
    count, dim = x.shape
    rows_near = near.shape[0]
    out_shape = (
        jax.ShapeDtypeStruct((count, dim), bf16),
        jax.ShapeDtypeStruct((count, dim), f32),
        jax.ShapeDtypeStruct((count, dim), bf16),
        jax.ShapeDtypeStruct((count, dim), bf16),
        jax.ShapeDtypeStruct((rows_near, dim), bf16),
        jax.ShapeDtypeStruct((rows_near, 2 * dim), bf16),
        jax.ShapeDtypeStruct((count, dim), bf16),
        jax.ShapeDtypeStruct((count, dim), f32),
    )
    operands = (att, x, norms, perm, perm_att, near)
    return pl.pallas_call(
        partial(cross_forward_kernel, spans, neighbours),
        out_shape=out_shape,
        grid=(1,),
        in_specs=[pl.BlockSpec(memory_space=pltpu.SMEM)]
        + [whole(op) for op in operands]
        + [column_block(dim, dim, index) for index in (3, 4, 5, 6, 7)],
        out_specs=tuple(whole_shape(shape.shape) for shape in out_shape),
        scratch_shapes=[pltpu.VMEM((count, dim), bf16)],
        compiler_params=params(),
        name="cross_forward",
    )(presence, *operands, *([weights] * 5))


def feed_kernel(
    second_ref,
    cot_ref,
    norms_ref,
    perm_ref,
    w_up_ref,
    w_down_ref,
    out_ref,
    gsecond_ref,
    all_ref,
    gnorm_ref,
    hid_p_ref,
    hid_t_ref,
    cot_p_ref,
    cot_t_ref,
    result_ref,
    back_ref,
    gup_ref,
    gdown_ref,
    sems,
):
    step = pl.program_id(0)
    last = pl.num_programs(0) - 1
    slot = lax.rem(step, 2)
    dim, tile = w_up_ref.shape

    def copies(step, slot):
        up = pl.multiple_of(8 * dim + step * tile, tile)
        down = pl.multiple_of(8 * dim + (last + 1 + step) * tile, tile)
        return (
            pltpu.make_async_copy(gup_ref.at[slot], all_ref.at[:, pl.ds(up, tile)], sems.at[0, slot]),
            pltpu.make_async_copy(
                gdown_ref.at[slot], all_ref.at[:, pl.ds(down, tile)], sems.at[1, slot]
            ),
        )

    @pl.when(step >= 2)
    def _():
        for copy in copies(step - 2, slot):
            copy.wait()

    @pl.when(step == 0)
    def _():
        normed, _ = centre_scale(second_ref[...])
        hidden = (normed * norms_ref[4:5, :] + norms_ref[5:6, :]).astype(bf16)
        hid_p_ref[...] = mm(hidden, perm_ref[...]).astype(bf16)
        hid_t_ref[...] = hid_p_ref[...].T
        cot_p_ref[...] = mm(cot_ref[...], perm_ref[...]).astype(bf16)
        cot_t_ref[...] = cot_p_ref[...].T
        result_ref[...] = jnp.zeros_like(result_ref)
        back_ref[...] = jnp.zeros_like(back_ref)

    upward = mm(hid_p_ref[...], w_up_ref[...])
    active, slope = gelu_parts(upward)
    active = active.astype(bf16)
    result_ref[...] += nt(active, w_down_ref[...])
    gdown_ref[slot] = mm(cot_t_ref[...], active).astype(bf16)
    grad_up = (mm(cot_p_ref[...], w_down_ref[...]) * slope).astype(bf16)
    gup_ref[slot] = mm(hid_t_ref[...], grad_up).astype(bf16)
    for copy in copies(step, slot):
        copy.start()
    back_ref[...] += nt(grad_up, w_up_ref[...])

    @pl.when(step == last)
    def _():
        out_ref[...] = (
            second_ref[...] + nt(result_ref[...].astype(bf16), perm_ref[...])
        ).astype(bf16)
        upstream = nt(back_ref[...].astype(bf16), perm_ref[...])
        normed, recip = centre_scale(second_ref[...])
        back, gain, shift = norm_back(upstream, normed, recip, norms_ref[4:5, :])
        gsecond_ref[...] = cot_ref[...].astype(f32) + back
        gnorm_ref[0:1, :] = gain
        gnorm_ref[1:2, :] = shift
        for which in (step - 1, step):
            for copy in copies(which, lax.rem(which, 2)):
                copy.wait()


def feed(second, cot, norms, perm, weights):
    count, dim = second.shape
    ffw = (weights.shape[1] - 8 * dim) // 2
    tile = 512
    first_up = 8 * dim // tile
    first_down = (8 * dim + ffw) // tile
    out_shape = (
        jax.ShapeDtypeStruct((count, dim), bf16),
        jax.ShapeDtypeStruct((count, dim), f32),
        jax.ShapeDtypeStruct(weights.shape, bf16),
        jax.ShapeDtypeStruct((2, dim), f32),
    )
    operands = (second, cot, norms, perm)
    return pl.pallas_call(
        feed_kernel,
        out_shape=out_shape,
        grid=(ffw // tile,),
        in_specs=[whole(op) for op in operands]
        + [
            pl.BlockSpec((dim, tile), lambda i: (0, first_up + i)),
            pl.BlockSpec((dim, tile), lambda i: (0, first_down + i)),
        ],
        out_specs=(
            whole_shape((count, dim)),
            whole_shape((count, dim)),
            pl.BlockSpec(memory_space=pl.ANY),
            whole_shape((2, dim)),
        ),
        scratch_shapes=[
            pltpu.VMEM((count, dim), bf16),
            pltpu.VMEM((dim, count), bf16),
            pltpu.VMEM((count, dim), bf16),
            pltpu.VMEM((dim, count), bf16),
            pltpu.VMEM((count, dim), f32),
            pltpu.VMEM((count, dim), f32),
            pltpu.VMEM((2, dim, tile), bf16),
            pltpu.VMEM((2, dim, tile), bf16),
            pltpu.SemaphoreType.DMA((2, 2)),
        ],
        compiler_params=params(),
        name="feed",
    )(*operands, weights, weights)


def span_backward(
    span, spans, neighbours, presence_ref, cross_q_ref, gco_ref, near_kv_ref, gcq_ref, gnear_ref
):
    count, dim = cross_q_ref.shape
    span_len = count // spans
    near = near_kv_ref.shape[0] // spans
    group = 256 // HEAD
    rows = rows_of(span, span_len)
    keys = rows_of(span, near)
    live, anyone = live_keys(presence_ref, span, (near, 1), 0, neighbours, near // neighbours)
    for begin in range(0, dim, group * HEAD):
        lanes = slice(begin, begin + group * HEAD)
        lanes_v = slice(dim + begin, dim + begin + group * HEAD)
        query = spread_heads(cross_q_ref[rows, lanes] * SCALE, span_len, group)
        grad_out = spread_heads(gco_ref[rows, lanes], span_len, group)
        key = near_kv_ref[keys, lanes]
        scores = jnp.where(live > 0, nt(key, query), masked_score)
        peak = jnp.max(scores, axis=0, keepdims=True)
        expon = jnp.exp(scores - peak) * live
        total = jnp.sum(expon, axis=0, keepdims=True) + 1.0 - anyone
        probs = expon * (1.0 / total)
        grad_probs = nt(near_kv_ref[keys, lanes_v], grad_out)
        inner = jnp.sum(probs * grad_probs, axis=0, keepdims=True)
        grad_scores = (probs * (grad_probs - inner)).astype(bf16)
        gcq_ref[rows, lanes] = (
            gather_heads(tn(grad_scores, key), span_len, group) * SCALE
        ).astype(bf16)
        gnear_ref[keys, lanes] = mm(grad_scores, query).astype(bf16)
        gnear_ref[keys, lanes_v] = mm(probs.astype(bf16), grad_out).astype(bf16)


def cross_backward_kernel(
    spans,
    neighbours,
    presence_ref,
    gsecond_ref,
    first_ref,
    norms_ref,
    perm_ref,
    perm_att_ref,
    att_p_ref,
    hid_p_ref,
    cross_q_ref,
    near_p_ref,
    near_kv_ref,
    co_p_ref,
    w_out_ref,
    w_cq_ref,
    w_co_ref,
    _,
    gfirst_ref,
    gatt_ref,
    all_ref,
    gnorm_ref,
    gco_ref,
    gcq_ref,
    gnear_ref,
    gw_ref,
    sems,
):
    dim = first_ref.shape[1]
    outs = []

    def keep(index, value):
        gw_ref[index] = value.astype(bf16)
        outs.append(
            pltpu.make_async_copy(
                gw_ref.at[index], all_ref.at[:, pl.ds((3 + index) * dim, dim)], sems.at[index]
            )
        )
        outs[-1].start()

    upper = gsecond_ref[...].astype(bf16)
    gco_ref[...] = nt(nt(upper, w_co_ref[...]).astype(bf16), perm_ref[...]).astype(bf16)
    tables = (presence_ref, cross_q_ref, gco_ref, near_kv_ref, gcq_ref, gnear_ref)
    pl.loop(0, spans)(lambda span: span_backward(span, spans, neighbours, *tables))
    upstream = nt(nt(gcq_ref[...], w_cq_ref[...]).astype(bf16), perm_ref[...])
    normed, recip = centre_scale(first_ref[...])
    back, gain, shift = norm_back(upstream, normed, recip, norms_ref[2:3, :])
    gnorm_ref[0:1, :] = gain
    gnorm_ref[1:2, :] = shift
    gfirst_ref[...] = gsecond_ref[...] + back
    lower = gfirst_ref[...].astype(bf16)
    gatt_ref[...] = nt(nt(lower, w_out_ref[...]).astype(bf16), perm_att_ref[...]).astype(bf16)
    keep(4, mm(co_p_ref[...].T, upper))
    near_t = near_p_ref[...].T
    for part in range(2):
        keep(2 + part, mm(near_t, gnear_ref[:, part * dim : (part + 1) * dim]))
    keep(1, mm(hid_p_ref[...].T, gcq_ref[...]))
    keep(0, mm(att_p_ref[...].T, lower))
    for copy in outs:
        copy.wait()


def cross_backward(
    spans,
    neighbours,
    presence,
    gsecond,
    first,
    norms,
    perm,
    perm_att,
    att_p,
    hid_p,
    cross_q,
    near_p,
    near_kv,
    co_p,
    weights,
    grads,
):
    count, dim = first.shape
    rows_near = near_p.shape[0]
    out_shape = [
        jax.ShapeDtypeStruct((count, dim), f32),
        jax.ShapeDtypeStruct((count, perm_att.shape[0]), bf16),
        jax.ShapeDtypeStruct(grads.shape, bf16),
        jax.ShapeDtypeStruct((2, dim), f32),
    ]
    scratch = [
        pltpu.VMEM((count, dim), bf16),
        pltpu.VMEM((count, dim), bf16),
        pltpu.VMEM((rows_near, 2 * dim), bf16),
        pltpu.VMEM((5, dim, dim), bf16),
        pltpu.SemaphoreType.DMA((5,)),
    ]
    operands = (
        gsecond,
        first,
        norms,
        perm,
        perm_att,
        att_p,
        hid_p,
        cross_q,
        near_p,
        near_kv,
        co_p,
    )
    return pl.pallas_call(
        partial(cross_backward_kernel, spans, neighbours),
        out_shape=out_shape,
        grid=(1,),
        in_specs=[pl.BlockSpec(memory_space=pltpu.SMEM)]
        + [whole(op) for op in operands]
        + [column_block(dim, dim, index) for index in (3, 4, 7)]
        + [pl.BlockSpec(memory_space=pl.ANY)],
        out_specs=tuple(
            pl.BlockSpec(memory_space=pl.ANY) if index == 2 else whole_shape(shape.shape)
            for index, shape in enumerate(out_shape)
        ),
        scratch_shapes=scratch,
        input_output_aliases={len(operands) + 4: 2},
        compiler_params=params(),
        name="cross_backward",
    )(presence, *operands, *([weights] * 3), grads)


def last_norm_kernel(parts_ref, x_ref, gfirst_ref, norms_ref, perm_ref, out_ref, gnorm_ref):
    total = parts_ref[0].astype(f32)
    for part in range(1, parts_ref.shape[0]):
        total = total + parts_ref[part].astype(f32)
    upstream = nt(total.astype(bf16), perm_ref[...])
    normed, recip = centre_scale(x_ref[...].astype(f32))
    back, gain, shift = norm_back(upstream, normed, recip, norms_ref[0:1, :])
    out_ref[...] = gfirst_ref[...] + back
    gnorm_ref[0:1, :] = gain
    gnorm_ref[1:2, :] = shift


def last_norm(parts, x, gfirst, norms, perm):
    count, dim = x.shape
    return pl.pallas_call(
        last_norm_kernel,
        out_shape=(
            jax.ShapeDtypeStruct((count, dim), f32),
            jax.ShapeDtypeStruct((2, dim), f32),
        ),
        compiler_params=params(),
        name="last_norm",
    )(parts, x, gfirst, norms, perm)


def layer_kernel(
    lines,
    pairs,
    spans,
    neighbours,
    presence_ref,
    w_ref,
    norm_ref,
    x_ref,
    order_ref,
    cot_ref,
    near_ref,
    wts_ref,
    all_ref,
    out_ref,
    gin_ref,
    sums_ref,
    hid_ref,
    qkv_ref,
    att_ref,
    lse_ref,
    att_p_ref,
    first_ref,
    hid_p_ref,
    cross_q_ref,
    near_p_ref,
    near_kv_ref,
    co_p_ref,
    second_ref,
    own_ref,
    small_ref,
    rows_ref,
    w_qkv_ref,
    w_mid_ref,
    att_tok_ref,
    cross_ref,
    up_p_ref,
    up_t_ref,
    cot_p_ref,
    cot_t_ref,
    result_ref,
    back_ref,
    gfeed_ref,
    perm_ref,
    norms_ref,
    gatt_ref,
    acc_ref,
    gsib_ref,
    parts_ref,
    send_sems,
    z_sems,
    y_sems,
    x_sems,
    a_sems,
    b_sems,
    sib_sems,
    norm_sems,
    row_sems,
    att_sems,
    local_sems,
    qkv_sems,
    mid_sems,
    feed_sems,
    gatt_sems,
    gsib_sems,
    part_sems,
):
    place = Place(lines)
    z, me, core = place.z, place.me, place.core
    length, dim = hid_ref.shape
    width = pairs * LANES
    tokens = length // 8
    half = own_ref.shape[0] // 2
    near_load = pltpu.make_async_copy(near_ref, near_p_ref, local_sems.at[2])
    near_load.start()
    own_ref[...] = w_ref[...].astype(bf16)
    place.meet()
    send = Sender(place, send_sems)
    unit = partial(unit_of, wts_ref, lines)
    events = place.events()
    keep = pltpu.make_async_copy(own_ref, unit(z, me), local_sems.at[0])
    keep.start()

    def build_perm():
        row = lax.broadcasted_iota(jnp.int32, (dim, dim), 0)
        perm_ref[...] = jnp.where(row == order_ref[0:1, :], 1.0, 0.0).astype(bf16)

    def obtain(index):
        condition, line, far, side = events[index]
        mine = unit(line, me)
        src = own_ref if far == 0 else mine
        if far:
            send.arrived(condition, mine, z_sems.at[line])
        if side >= 0:
            send.start(both(condition, z > 0), src, mine, z_sems.at[line], z=z - 1)
        if side <= 0:
            send.start(both(condition, z < lines - 1), src, mine, z_sems.at[line], z=z + 1)
        send.start(condition, src, mine, x_sems.at[line], seq=place.xn)
        send.start(condition, src, mine, y_sems.at[line], seq=place.yn)
        send.start(condition, src, mine, sib_sems.at[0, line], seq=place.sib)

    def pass_on(index):
        condition, line, _, _ = events[index]
        from_x, from_y = unit(line, place.xn), unit(line, place.yn)
        send.arrived(condition, from_x, x_sems.at[line])
        part = unit(line, place.xn, half, half)
        send.start(condition, part, part, b_sems.at[line], seq=place.yn)
        send.start(condition, from_x, from_x, sib_sems.at[1, line], seq=place.sib)
        send.arrived(condition, from_y, y_sems.at[line])
        part = unit(line, place.yn, 0, half)
        send.start(condition, part, part, a_sems.at[line], seq=place.xn)
        send.start(condition, from_y, from_y, sib_sems.at[2, line], seq=place.sib)

    def corner(index):
        condition, line, _, _ = events[index]
        for group, begin, sems in ((3, 0, a_sems), (4, half, b_sems)):
            part = unit(line, place.dg, begin, half)
            send.arrived(condition, part, sems.at[line])
            send.start(condition, part, part, sib_sems.at[group, line], seq=place.sib)

    def row_block(seq):
        return rows_ref.at[pl.ds(pl.multiple_of(seq * tokens, tokens), tokens)]

    def middle(index):
        return pltpu.make_async_copy(
            wts_ref.at[:, pl.ds((3 + index) * dim, dim)], w_mid_ref.at[index], mid_sems.at[index]
        )

    obtain(0)
    own_rows = pltpu.make_async_copy(x_ref.at[place.chip], row_block(me), local_sems.at[1])
    own_rows.start()
    others = (place.xn, place.yn, place.dg)
    for other in place.line():
        send.start(None, norm_ref, small_ref.at[z], norm_sems.at[z], z=other)
    small_ref[z] = norm_ref[...]
    send.start(None, x_ref.at[place.chip], row_block(me), row_sems.at[me], seq=place.sib)
    for other in others:
        send.start(None, x_ref.at[other // 2], row_block(me), row_sems.at[me], seq=other)
    build_perm()
    near_load.wait()

    @pl.loop(0, near_p_ref.shape[0] // 512)
    def _(step):
        rows = rows_of(step, 512)
        near_p_ref[rows, :] = mm(near_p_ref[rows, :], perm_ref[...]).astype(bf16)

    obtain(1)
    obtain(2)
    pass_on(0)
    for other in others:
        send.arrived(None, row_block(other), row_sems.at[other])
        send.start(None, row_block(other), row_block(other), row_sems.at[other], seq=place.sib)
    obtain(3)
    obtain(4)
    cot_p_ref[...] = mm(cot_ref[...], perm_ref[...]).astype(bf16)
    cot_t_ref[...] = cot_p_ref[...].T
    pass_on(1)
    pass_on(2)
    corner(0)

    for other in place.line():
        send.arrived(None, small_ref.at[other], norm_sems.at[other])
    piece = small_ref.shape[2]
    total = None
    for line in range(lines):
        row = lax.broadcasted_iota(jnp.int32, (piece, dim), 0)
        column = lax.broadcasted_iota(jnp.int32, (piece, dim), 1)
        part = dim // lines
        place_of = jnp.logical_and(row < part, column == row + line * part).astype(bf16)
        term = mm(small_ref[line], place_of)
        total = term if total is None else total + term
    norms_ref[...] = total[: norms_ref.shape[0]]

    last = len(events)
    for index in range(5, last, 2):
        obtain(index)
        obtain(index + 1)
        if index == 5:
            for other in others:
                theirs = other + 1 - 2 * core
                send.arrived(None, row_block(theirs), row_sems.at[theirs])
            send.arrived(None, row_block(place.sib), row_sems.at[place.sib])
            own_rows.wait()
            norm_rows(rows_ref, norms_ref[...], perm_ref, hid_ref)
        pass_on(index - 2)
        pass_on(index - 1)
        corner(index - 4)
        corner(index - 3)
    for index in range(last - 2, last):
        pass_on(index)
    for index in range(last - 4, last):
        corner(index)
    keep.wait()
    for line in range(lines):
        for group, first in enumerate((me, place.xn, place.yn)):
            theirs = first + 1 - 2 * core
            send.arrived(None, unit(line, theirs), sib_sems.at[group, line])
        theirs = place.dg + 1 - 2 * core
        send.arrived(None, unit(line, theirs, 0, half), sib_sems.at[3, line])
        send.arrived(None, unit(line, theirs, half, half), sib_sems.at[4, line])
    copies = weight_copies(pairs, dim, wts_ref, w_qkv_ref, qkv_sems)
    for copy in copies + [middle(index) for index in (2, 3, 0, 1, 4)]:
        copy.start()
    for part in range(3):
        copies[part].wait()
        triple_part(part, pairs, hid_ref, w_qkv_ref, qkv_ref)

    share = lax.rem(me, dim // width)
    seq_rows = pl.ds(pl.multiple_of(place.chip * tokens, tokens), tokens)

    def landing(pair, chip_rows, share):
        lanes = pl.ds(pl.multiple_of(share * width + pair * LANES, LANES), LANES)
        return att_tok_ref.at[chip_rows, lanes]

    for pair in range(pairs):
        lanes = slice(pair * LANES, (pair + 1) * LANES)
        pair_forward(pair, pairs, qkv_ref, att_ref, lse_ref, lambda: None)
        for other in place.plane():
            block = att_ref.at[pl.ds(pl.multiple_of(other * tokens, tokens), tokens), lanes]
            to = landing(pair, seq_rows, share)
            send.start(None, block, to, att_sems.at[pair, me], seq=other)
        own_block = att_ref[pl.ds(pl.multiple_of(me * tokens, tokens), tokens), lanes]
        landing(pair, seq_rows, share)[...] = own_block

    for index in (2, 3, 0, 1, 4):
        middle(index).wait()
    for step in range(near_p_ref.shape[0] // 512):
        rows = slice(step * 512, (step + 1) * 512)
        near_kv_ref[rows, :dim] = mm(near_p_ref[rows, :], w_mid_ref[2]).astype(bf16)
        near_kv_ref[rows, dim:] = mm(near_p_ref[rows, :], w_mid_ref[3]).astype(bf16)
    w_out_ref, w_cq_ref, w_co_ref = (w_mid_ref.at[index] for index in (0, 1, 4))
    for pair in range(pairs):
        for other in place.plane():
            rows = pl.ds(pl.multiple_of(other // 2 * tokens, tokens), tokens)
            send.arrived(None, landing(pair, rows, lax.rem(other, 2)), att_sems.at[pair, other])
    att_p_ref[...] = mm(att_tok_ref[...], perm_ref[...]).astype(bf16)
    own_x = x_ref[...].reshape(first_ref.shape).astype(f32)
    first_ref[...] = own_x + mm(att_p_ref[...], w_out_ref[...])
    normed, _ = centre_scale(first_ref[...])
    hidden = (normed * norms_ref[2:3, :] + norms_ref[3:4, :]).astype(bf16)
    hid_p_ref[...] = mm(hidden, perm_ref[...]).astype(bf16)
    cross_q_ref[...] = mm(hid_p_ref[...], w_cq_ref[...]).astype(bf16)
    pl.loop(0, spans)(
        lambda span: span_forward(
            span, spans, neighbours, presence_ref, cross_q_ref, near_kv_ref, cross_ref
        )
    )

    ffw = (all_ref.shape[1] - 8 * dim) // 2
    tile = gfeed_ref.shape[2]
    order = range(0, ffw, tile)

    def tile_load(index):
        return [
            pltpu.make_async_copy(
                wts_ref.at[:, pl.ds(8 * dim + part * ffw + order[index], tile)],
                w_mid_ref.at[(2 * index + part) % 4],
                feed_sems.at[0, (2 * index + part) % 4],
            )
            for part in range(2)
        ]

    def tile_store(index):
        return [
            pltpu.make_async_copy(
                gfeed_ref.at[(2 * index + part) % 4],
                all_ref.at[:, pl.ds(8 * dim + part * ffw + order[index], tile)],
                feed_sems.at[1, (2 * index + part) % 4],
            )
            for part in range(2)
        ]

    for copy in tile_load(0) + tile_load(1):
        copy.start()
    co_p_ref[...] = mm(cross_ref[...], perm_ref[...]).astype(bf16)
    second_ref[...] = first_ref[...] + mm(co_p_ref[...], w_co_ref[...])
    normed, _ = centre_scale(second_ref[...])
    hidden = (normed * norms_ref[4:5, :] + norms_ref[5:6, :]).astype(bf16)
    up_p_ref[...] = mm(hidden, perm_ref[...]).astype(bf16)
    up_t_ref[...] = up_p_ref[...].T

    for index in range(len(order)):
        up_ref, down_ref = w_mid_ref.at[2 * index % 4], w_mid_ref.at[2 * index % 4 + 1]
        for copy in tile_load(index):
            copy.wait()
        if index >= 2:
            for copy in tile_store(index - 2):
                copy.wait()
        active, slope = gelu_parts(mm(up_p_ref[...], up_ref[...]))
        active = active.astype(bf16)
        term = nt(active, down_ref[...])
        result_ref[...] = term if index == 0 else result_ref[...] + term
        gfeed_ref[2 * index % 4 + 1] = mm(cot_t_ref[...], active).astype(bf16)
        grad_up = (mm(cot_p_ref[...], down_ref[...]) * slope).astype(bf16)
        gfeed_ref[2 * index % 4] = mm(up_t_ref[...], grad_up).astype(bf16)
        for copy in tile_store(index):
            copy.start()
        term = nt(grad_up, up_ref[...])
        back_ref[...] = term if index == 0 else back_ref[...] + term
        if index + 2 < len(order):
            for copy in tile_load(index + 2):
                copy.start()
        elif index + 2 == len(order):
            middle(0).start()
            middle(1).start()

    out_ref[...] = (second_ref[...] + nt(result_ref[...].astype(bf16), perm_ref[...])).astype(bf16)
    upstream = nt(back_ref[...].astype(bf16), perm_ref[...])
    normed, recip = centre_scale(second_ref[...])
    back, gain, shift = norm_back(upstream, normed, recip, norms_ref[4:5, :])
    gsecond_ref = second_ref
    gsecond_ref[...] = cot_ref[...].astype(f32) + back
    sums_ref[4:5, :] = gain
    sums_ref[5:6, :] = shift
    sums_ref[6:8, :] = jnp.zeros((2, dim), f32)
    for index in range(len(order) - 2, len(order)):
        for copy in tile_store(index):
            copy.wait()

    gco_ref, gcq_ref, gatt_tok_ref = up_p_ref, cot_p_ref, cross_ref
    outs = []

    def store(slot, part, first):
        copy = pltpu.make_async_copy(
            part, all_ref.at[:, pl.ds(first, part.shape[1])], feed_sems.at[1, slot]
        )
        outs.append(copy)
        copy.start()

    def keep_grad(index, value):
        slot = len(outs) % 4
        if len(outs) >= 4:
            outs[-4].wait()
        gfeed_ref[slot] = value.astype(bf16)
        store(slot, gfeed_ref.at[slot], (3 + index) * dim)

    upper = gsecond_ref[...].astype(bf16)
    gco_ref[...] = nt(nt(upper, w_co_ref[...]).astype(bf16), perm_ref[...]).astype(bf16)
    tables = (presence_ref, cross_q_ref, gco_ref, near_kv_ref, gcq_ref, near_kv_ref)
    pl.loop(0, spans)(lambda span: span_backward(span, spans, neighbours, *tables))
    for index in (0, 1):
        middle(index).wait()
    upstream = nt(nt(gcq_ref[...], w_cq_ref[...]).astype(bf16), perm_ref[...])
    normed, recip = centre_scale(first_ref[...])
    back, gain, shift = norm_back(upstream, normed, recip, norms_ref[2:3, :])
    sums_ref[2:3, :] = gain
    sums_ref[3:4, :] = shift
    gfirst_ref = gsecond_ref
    gfirst_ref[...] = gsecond_ref[...] + back
    lower = gfirst_ref[...].astype(bf16)
    gatt_tok_ref[...] = nt(nt(lower, w_out_ref[...]).astype(bf16), perm_ref[...]).astype(bf16)

    def gatt_block(device):
        return gatt_tok_ref.at[
            pl.ds(pl.multiple_of(device // 2 * tokens, tokens), tokens),
            pl.ds(pl.multiple_of(lax.rem(device, 2) * width, width), width),
        ]

    def gatt_rows(device):
        return gatt_ref.at[pl.ds(pl.multiple_of(device * tokens, tokens), tokens)]

    for other in place.plane():
        send.start(None, gatt_block(other), gatt_rows(me), gatt_sems.at[me], seq=other)
    own_gatt = pltpu.make_async_copy(gatt_block(me), gatt_rows(me), gatt_sems.at[me])
    own_gatt.start()
    keep_grad(4, mm(co_p_ref[...].T, upper))
    near_t = near_p_ref[...].T
    for part in range(2):
        keep_grad(2 + part, mm(near_t, near_kv_ref[:, part * dim : (part + 1) * dim]))
    keep_grad(1, mm(hid_p_ref[...].T, gcq_ref[...]))
    keep_grad(0, mm(att_p_ref[...].T, lower))
    for other in place.plane():
        send.arrived(None, gatt_rows(other), gatt_sems.at[other])
    own_gatt.wait()

    send.finish()
    grad_ref = near_kv_ref.at[pl.ds(0, length), pl.ds(0, 3 * width)]
    ghid_ref = rows_ref
    attention = (qkv_ref, att_ref, gatt_ref, lse_ref, grad_ref, acc_ref)
    pl.loop(0, pairs)(lambda pair: pair_backward(pair, pairs, *attention, lambda: None))
    for begin in range(0, length, 256):
        rows = slice(begin, begin + 256)
        ghid_ref[rows, :] = nt(grad_ref[rows, :], w_qkv_ref[...]).astype(bf16)
    chips = (place.xn // 2, place.yn // 2, place.dg // 2, place.chip)

    def token_rows(device):
        return pl.ds(pl.multiple_of(device * tokens, tokens), tokens)

    for chip in chips:
        theirs = ghid_ref.at[token_rows(chip * 2 + 1 - core)]
        send.start(None, theirs, gsib_ref.at[chip], gsib_sems.at[chip], seq=place.sib)

    for copy in outs[-4:]:
        copy.wait()
    outs.clear()
    gfeed_ref[3] = jnp.zeros_like(gfeed_ref[3])
    share_count = dim // width
    zeros = [
        pltpu.make_async_copy(
            gfeed_ref.at[3, :, pl.ds(0, width)],
            all_ref.at[
                :,
                pl.ds(
                    pl.multiple_of(part * dim + lax.rem(share + other, share_count) * width, LANES),
                    width,
                ),
            ],
            mid_sems.at[2 + part],
        )
        for part in range(3)
        for other in range(1, share_count)
    ]
    for copy in zeros:
        copy.start()
    hidden_t = hid_ref[...].T

    def triple_grad(part):
        columns = slice(part * width, (part + 1) * width)
        gfeed_ref[part, :, :width] = mm(hidden_t, grad_ref[:, columns]).astype(bf16)
        first = pl.multiple_of(part * dim + share * width, LANES)
        store(part, gfeed_ref.at[part, :, pl.ds(0, width)], first)

    triple_grad(0)
    triple_grad(1)
    for chip in chips:
        send.arrived(None, gsib_ref.at[chip], gsib_sems.at[chip])
        rows = token_rows(chip * 2 + core)
        total = (ghid_ref[rows, :].astype(f32) + gsib_ref[chip].astype(f32)).astype(bf16)
        if chip is place.chip:
            parts_ref[chip] = total
        else:
            ghid_ref[rows, :] = total
            landed, sem = parts_ref.at[place.chip], part_sems.at[place.chip]
            send.start(None, ghid_ref.at[rows], landed, sem, seq=chip * 2 + core)
    triple_grad(2)
    for chip in chips[:3]:
        send.arrived(None, parts_ref.at[chip], part_sems.at[chip])
    gain_sum = shift_sum = None
    for chip in range(4):
        rows = slice(chip * tokens, (chip + 1) * tokens)
        upstream = nt(parts_ref[chip], perm_ref[...])
        normed, recip = centre_scale(x_ref[chip].astype(f32))
        back, gain, shift = norm_back(upstream, normed, recip, norms_ref[0:1, :])
        gfirst_ref[rows, :] += back
        gain_sum = gain if gain_sum is None else gain_sum + gain
        shift_sum = shift if shift_sum is None else shift_sum + shift
    leave = pltpu.make_async_copy(gfirst_ref, gin_ref, local_sems.at[0])
    leave.start()
    sums_ref[0:1, :] = gain_sum
    sums_ref[1:2, :] = shift_sum
    for copy in outs + zeros:
        copy.wait()
    leave.wait()
    send.finish()


def layer(lines, pairs, spans, neighbours, presence, w_shard, n_shard, inputs, order, cot, near):
    unit_rows, unit_cols = w_shard.shape
    seqs, tokens, dim = inputs.shape
    count, length, width = seqs * tokens, 8 * tokens, pairs * LANES
    rows_near = near.shape[0]
    events = 2 * lines - 1
    any_space = pl.BlockSpec(memory_space=pl.ANY)
    vmem = pl.BlockSpec(memory_space=pltpu.VMEM)
    dma = pltpu.SemaphoreType.DMA
    packed = jax.ShapeDtypeStruct((unit_rows * lines, unit_cols * 8), bf16)
    tile = unit_cols // 2
    tokens_rows = (count, dim)
    scratch = [
        ((length, dim), bf16),
        ((3 * pairs, length, LANES), bf16),
        ((length, width), bf16),
        ((pairs, 2, length), f32),
        (tokens_rows, bf16),
        (tokens_rows, f32),
        (tokens_rows, bf16),
        (tokens_rows, bf16),
        ((rows_near, dim), bf16),
        ((rows_near, 2 * dim), bf16),
        (tokens_rows, bf16),
        (tokens_rows, f32),
        ((unit_rows, unit_cols), bf16),
        ((lines,) + n_shard.shape, bf16),
        ((length, dim), bf16),
        ((dim, 3 * width), bf16),
        ((5, dim, dim), bf16),
        (tokens_rows, bf16),
        (tokens_rows, bf16),
        (tokens_rows, bf16),
        ((dim, count), bf16),
        (tokens_rows, bf16),
        ((dim, count), bf16),
        (tokens_rows, f32),
        (tokens_rows, f32),
        ((4, dim, tile), bf16),
        ((dim, dim), bf16),
        ((8, dim), f32),
        ((length, width), bf16),
        ((2, length, LANES), f32),
        ((4, tokens, dim), bf16),
        ((4, tokens, dim), bf16),
    ]
    return pl.pallas_call(
        partial(layer_kernel, lines, pairs, spans, neighbours),
        out_shape=(
            packed,
            packed,
            jax.ShapeDtypeStruct(tokens_rows, bf16),
            jax.ShapeDtypeStruct(tokens_rows, f32),
            jax.ShapeDtypeStruct((8, dim), f32),
        ),
        in_specs=[pl.BlockSpec(memory_space=pltpu.SMEM)] + [vmem] * 5 + [any_space],
        out_specs=(any_space, any_space, vmem, any_space, vmem),
        scratch_shapes=[pltpu.VMEM(*entry) for entry in scratch]
        + [
            dma((11 * events + 7 + lines + 7 * pairs + 16,)),
            dma((lines,)),
            dma((lines,)),
            dma((lines,)),
            dma((lines,)),
            dma((lines,)),
            dma((5, lines)),
            dma((lines,)),
            dma((8,)),
            dma((pairs, 8)),
            dma((3,)),
            dma((3,)),
            dma((5,)),
            dma((2, 4)),
            dma((8,)),
            dma((4,)),
            dma((4,)),
        ],
        compiler_params=pltpu.CompilerParams(
            vmem_limit_bytes=VMEM_BYTES, collective_id=1, has_side_effects=True
        ),
        name="layer",
    )(presence, w_shard, n_shard, inputs, order, cot, near)


def reduce_kernel(
    lines,
    grads_ref,
    small_ref,
    shard_ref,
    norms_ref,
    mine_ref,
    sib_ref,
    corner_a_ref,
    corner_b_ref,
    from_x_ref,
    from_y_ref,
    below_ref,
    above_ref,
    early_below_ref,
    early_above_ref,
    plane_ref,
    plane_sum_ref,
    line_ref,
    send_sems,
    load_sems,
    sib_sems,
    a_sems,
    b_sems,
    x_sems,
    y_sems,
    below_sems,
    above_sems,
    early_below_sems,
    early_above_sems,
    plane_sems,
    line_sems,
):
    place = Place(lines)
    z, me = place.z, place.me
    unit_rows, unit_cols = shard_ref.shape
    early = early_below_ref.shape[2]
    place.meet()
    send = Sender(place, send_sems)
    chips = (place.dg, place.yn, place.xn, me)
    corner, over_y, over_x, here = range(4)

    unit = partial(unit_of, grads_ref, lines)

    def load(which, line):
        return pltpu.make_async_copy(
            unit(line, chips[which]), mine_ref.at[which, line], load_sems.at[which, line]
        )

    for other in place.plane():
        send.start(None, small_ref, plane_ref.at[me], plane_sems.at[me], seq=other)
    plane_ref[me] = small_ref[...]

    events = place.events()[::-1]
    count = len(events)

    def begin(index):
        condition, line, _, _ = events[index]
        for which in range(4):
            theirs = chips[which] + 1 - 2 * place.core
            send.start(
                condition,
                unit(line, theirs),
                sib_ref.at[which, line],
                sib_sems.at[which, line],
                seq=place.sib,
            )
            when(condition, load(which, line).start)

    def parts(index):
        if index == count:
            return 0, early // 2, early, (unit_rows - early) // 2, lines
        return early, (early + unit_rows) // 2, unit_rows, 0, events[index][1]

    def add(target, *terms, begin=0, end=unit_rows):
        tile = next(size for size in (96, 80, 64, 32, 16) if (end - begin) % size == 0)

        @pl.loop(0, (end - begin) // tile)
        def _(step):
            rows = pl.ds(pl.multiple_of(begin + step * tile, 16), tile)
            total = target[rows, :]
            if len(terms) > 1:
                total = total.astype(f32)
            for ref, first in terms:
                at = pl.ds(pl.multiple_of(begin - first + step * tile, 16), tile)
                term = ref[at, :]
                total = total + (term if len(terms) == 1 else term.astype(f32))
            target[rows, :] = total.astype(target.dtype)

    def early_rows(line):
        return mine_ref.at[:, line, pl.ds(0, early), :]

    def add_early(line, landing):
        for which in range(4):
            add(mine_ref.at[which, line], (landing.at[line, which], 0), end=early)

    def first(index):
        condition, line, far, side = events[min(index, count - 1)]
        low, middle, high, base, sem = parts(index)
        if index < count:
            for which in range(4):
                send.arrived(condition, sib_ref.at[which, line], sib_sems.at[which, line])
                when(condition, load(which, line).wait)

            def chip_sum():
                for which in range(4):
                    add(mine_ref.at[which, line], (sib_ref.at[which, line], 0))

            when(condition, chip_sum)
        def along_z():
            if far or index == count:
                from_below, from_above = both(condition, z > 0), both(condition, z < lines - 1)
                sides = ((from_below, early_below_ref, early_below_sems),) if side >= 0 else ()
                if side <= 0:
                    sides += ((from_above, early_above_ref, early_above_sems),)
                for on, landing, sems in sides:
                    send.arrived(on, landing.at[line], sems.at[line])
                    when(on, partial(add_early, line, landing))
            if far:
                landing, sems = sides[0][1:]
                send.start(condition, early_rows(line), landing.at[line], sems.at[line], z=z + side)

        def to_plane():
            target = mine_ref.at[corner, line]
            for begins, ends, landing, sems, to in (
                (low, middle, corner_a_ref, a_sems, place.xn),
                (middle, high, corner_b_ref, b_sems, place.yn),
            ):
                send.start(
                    condition,
                    target.at[pl.ds(begins, ends - begins)],
                    landing.at[line, pl.ds(base, ends - begins)],
                    sems.at[sem],
                    seq=to,
                )

        steps = (along_z, to_plane) if index == count else (to_plane, along_z)
        for step in steps:
            step()

    def second(index):
        condition, line, _, _ = events[min(index, count - 1)]
        low, middle, high, base, sem = parts(index)
        for which, part, sems, begins, ends, to, landing, landing_sems in (
            (over_y, corner_a_ref, a_sems, low, middle, place.yn, from_y_ref, y_sems),
            (over_x, corner_b_ref, b_sems, middle, high, place.xn, from_x_ref, x_sems),
        ):
            send.arrived(condition, part.at[line, pl.ds(base, ends - begins)], sems.at[sem])
            target = mine_ref.at[which, line]
            term = (part.at[line], begins - base)
            when(condition, partial(add, target, term, begin=begins, end=ends))
            rows = pl.ds(low, high - low)
            landed = landing.at[line, rows]
            send.start(condition, target.at[rows], landed, landing_sems.at[sem], seq=to)

    def third(index):
        condition, line, far, side = events[min(index, count - 1)]
        low, _, high, _, sem = parts(index)
        rows = pl.ds(low, high - low)
        send.arrived(condition, from_x_ref.at[line, rows], x_sems.at[sem])
        send.arrived(condition, from_y_ref.at[line, rows], y_sems.at[sem])
        target = mine_ref.at[here, line]
        terms = [(from_x_ref.at[line], 0), (from_y_ref.at[line], 0)]
        if far == 0:
            tile = 32

            @pl.loop(low // tile, high // tile)
            def _(step):
                at = rows_of(step, tile)
                total = target[at, :].astype(f32)
                for ref, _ in terms:
                    total = total + ref[at, :].astype(f32)
                shard_ref[at, :] = total

            if index < count:
                for on, ref, sems in (
                    (z > 0, below_ref, below_sems),
                    (z < lines - 1, above_ref, above_sems),
                ):
                    send.arrived(on, ref.at[line, rows], sems.at[line])
                    when(on, partial(add, shard_ref, (ref.at[line], 0), begin=low))
            return
        landing, sems = (below_ref, below_sems) if side > 0 else (above_ref, above_sems)
        more = both(condition, z > 0) if side > 0 else both(condition, z < lines - 1)
        none = both(condition, z == 0) if side > 0 else both(condition, z == lines - 1)
        send.arrived(more, landing.at[line, rows], sems.at[line])
        when(more, partial(add, target, *terms, (landing.at[line], 0), begin=low))
        when(none, partial(add, target, *terms, begin=low))
        landed = landing.at[line, rows]
        send.start(condition, target.at[rows], landed, sems.at[line], z=z + side)

    for index in range(min(4, count)):
        begin(index)
    first(0)
    first(1)
    for index in range(2, count + 2):
        if index + 2 < count:
            begin(index + 2)
        if index < count:
            first(index)
        if 0 <= index - 2 < count:
            second(index - 2)
        if index == count:
            first(count)
        if index == 3:
            for other in place.plane():
                send.arrived(None, plane_ref.at[other], plane_sems.at[other])
            total = plane_ref[0]
            for other in range(1, 8):
                total = total + plane_ref[other]
            plane_sum_ref[...] = total
            line_ref[z] = total
            for other in place.line():
                send.start(None, plane_sum_ref, line_ref.at[z], line_sems.at[z], z=other)
        if 0 <= index - 4 <= count - 3:
            third(index - 4)
        if index == count + 1:
            third(count - 2)
            second(count)
            third(count - 1)
            third(count)

    for other in place.line():
        send.arrived(None, line_ref.at[other], line_sems.at[other])
    total = line_ref[0]
    for other in range(1, lines):
        total = total + line_ref[other]
    norms_ref[...] = total
    send.finish()


def reduce_grads(lines, grads, small):
    rows, cols = grads.shape
    unit_rows, unit_cols = rows // lines, cols // 8
    half = unit_rows // 2
    early = unit_rows // 96 * 16
    any_space = pl.BlockSpec(memory_space=pl.ANY)
    vmem = pl.BlockSpec(memory_space=pltpu.VMEM)
    dma = pltpu.SemaphoreType.DMA
    return pl.pallas_call(
        partial(reduce_kernel, lines),
        out_shape=(
            jax.ShapeDtypeStruct((unit_rows, unit_cols), f32),
            jax.ShapeDtypeStruct(small.shape, f32),
        ),
        in_specs=[any_space, vmem],
        out_specs=(vmem, vmem),
        scratch_shapes=[
            pltpu.VMEM((4, lines, unit_rows, unit_cols), bf16),
            pltpu.VMEM((4, lines, unit_rows, unit_cols), bf16),
            pltpu.VMEM((lines, half, unit_cols), bf16),
            pltpu.VMEM((lines, half, unit_cols), bf16),
            pltpu.VMEM((lines, unit_rows, unit_cols), bf16),
            pltpu.VMEM((lines, unit_rows, unit_cols), bf16),
            pltpu.VMEM((lines, unit_rows, unit_cols), bf16),
            pltpu.VMEM((lines, unit_rows, unit_cols), bf16),
            pltpu.VMEM((lines, 4, early, unit_cols), bf16),
            pltpu.VMEM((lines, 4, early, unit_cols), bf16),
            pltpu.VMEM((8,) + small.shape, f32),
            pltpu.VMEM(small.shape, f32),
            pltpu.VMEM((lines,) + small.shape, f32),
            dma((10 * (2 * lines - 1) + 4 + 7 + lines,)),
            dma((4, lines)),
            dma((4, lines)),
            dma((lines + 1,)),
            dma((lines + 1,)),
            dma((lines + 1,)),
            dma((lines + 1,)),
            dma((lines,)),
            dma((lines,)),
            dma((lines,)),
            dma((lines,)),
            dma((8,)),
            dma((lines,)),
        ],
        compiler_params=pltpu.CompilerParams(
            vmem_limit_bytes=VMEM_BYTES, collective_id=4, has_side_effects=True
        ),
        name="reduce_grads",
    )(grads, small)


def adam_update(grad, weight, first, second, average, rate, decay):
    first = beta_first * first + (1.0 - beta_first) * grad
    second = beta_second * second + (1.0 - beta_second) * grad * grad
    stepped = (
        first / (1.0 - beta_first**STEP) / (jnp.sqrt(second / (1.0 - beta_second**STEP)) + adam_eps)
    )
    weight = weight - rate * (stepped + decay * weight)
    average = ema_decay * average + (1.0 - ema_decay) * weight
    return (first, second, weight, average)


def on_device(
    inputs,
    cotangent,
    neighbours,
    presence,
    row_order,
    w_master,
    w_first,
    w_second,
    w_average,
    n_master,
    n_first,
    n_second,
    n_average,
):
    seqs, tokens, dim = inputs.shape
    heads = dim // HEAD
    devices = lax.axis_size("seq")
    count = seqs * tokens
    length = devices * tokens
    me = lax.axis_index("seq")
    shares = devices // seqs
    held = heads // shares
    pairs = (held + 1) // 2
    width = pairs * LANES
    spare = width - held * HEAD
    sequence, share = me // shares, me % shares

    lines = lax.axis_size("dp")
    planar = devices == 8 and seqs == 4 and spare == 0
    x = inputs.reshape(count, dim)
    cot = cotangent.reshape(count, dim)
    spans = seqs * neighbours.shape[1]
    each = neighbours.shape[2]
    near = neighbours.reshape(-1, dim)
    live = presence.reshape(-1)
    part = n_master.shape[1]
    if planar:
        small = jnp.pad(n_master.astype(bf16), ((0, 16 - 6), (0, -part % LANES)))
        order = row_order.reshape(1, dim)
        _, grads, outputs, grad_inputs, norm_grads = layer(
            lines, pairs, spans, each, live, w_master, small, inputs, order, cot, near
        )
        grad_shard, norm_sums = reduce_grads(lines, grads, norm_grads)
        norm_shard = lax.dynamic_slice(norm_sums, (0, lax.axis_index("dp") * part), (6, part))
    else:
        perm = (jnp.arange(dim)[:, None] == row_order[None, :]).astype(bf16)
        perm_att = jnp.pad(perm.reshape(shares, held * HEAD, dim), ((0, 0), (0, spare), (0, 0)))
        perm_att = perm_att.reshape(shares * width, dim)
        weights = lax.all_gather(w_master.astype(bf16), "dp", axis=0, tiled=True)
        weights = lax.all_gather(weights, "seq", axis=1, tiled=True)
        norms = lax.all_gather(n_master.astype(bf16), "dp", axis=1, tiled=True).astype(f32)
        rows = lax.all_to_all(jnp.repeat(inputs, shares, axis=0), "seq", 0, 0)
        rows = rows.reshape(length, dim)
        w_qkv = weights[:, : 3 * dim].reshape(dim, 3, shares, held * HEAD)
        w_qkv = lax.dynamic_index_in_dim(w_qkv, share, axis=2, keepdims=False)
        w_qkv = jnp.pad(w_qkv, ((0, 0), (0, 0), (0, spare))).reshape(dim, 3 * width)
        hid, qkv, att, lse = self_forward(pairs, rows, norms, perm, w_qkv)
        att_tok = (
            lax.all_to_all(att.reshape(devices, tokens, width), "seq", 0, 0)
            .reshape(seqs, shares, tokens, width)
            .transpose(0, 2, 1, 3)
            .reshape(count, shares * width)
        )
        att_p, first, hid_p, cross_q, near_p, near_kv, co_p, second = cross_forward(
            spans, each, live, att_tok, x, norms, perm, perm_att, near, weights
        )
        outputs, gsecond, grads, gnorm_e = feed(second, cot, norms, perm, weights)
        gfirst, gatt_tok, grads, gnorm_c = cross_backward(
            spans,
            each,
            live,
            gsecond,
            first,
            norms,
            perm,
            perm_att,
            att_p,
            hid_p,
            cross_q,
            near_p,
            near_kv,
            co_p,
            weights,
            grads,
        )
        gatt = lax.all_to_all(
            gatt_tok.reshape(seqs, tokens, shares, width)
            .transpose(0, 2, 1, 3)
            .reshape(devices, tokens, width),
            "seq",
            0,
            0,
        ).reshape(length, width)
        gqkv, ghid = self_backward(pairs, qkv, att, gatt, lse, hid, w_qkv)
        parts = (
            lax.all_to_all(ghid.reshape(devices, tokens, dim), "seq", 0, 0)
            .reshape(seqs, shares, tokens, dim)
            .transpose(1, 0, 2, 3)
            .reshape(shares, count, dim)
        )
        grad_inputs, gnorm_a = last_norm(parts, x, gfirst, norms, perm)
        gqkv = gqkv.reshape(dim, 3, 1, width)[..., : held * HEAD]
        gqkv = jnp.where(jnp.arange(shares)[:, None] == share, gqkv, jnp.zeros_like(gqkv))
        grads = lax.dynamic_update_slice(grads, gqkv.reshape(dim, 3 * dim), (0, 0))
        norm_grads = lax.psum(jnp.concatenate([gnorm_a, gnorm_c, gnorm_e], axis=0), "seq")
        partial_sum = lax.psum_scatter(grads, "seq", scatter_dimension=1, tiled=True)
        grad_shard = lax.psum_scatter(partial_sum, "dp", scatter_dimension=0, tiled=True)
        grad_shard = grad_shard.astype(f32)
        norm_shard = lax.psum_scatter(
            norm_grads.astype(bf16), "dp", scatter_dimension=1, tiled=True
        ).astype(f32)
    w_first_new, w_second_new, w_new, w_average_new = adam_update(
        grad_shard, w_master, w_first, w_second, w_average, learn_rate, weight_decay
    )
    n_first_new, n_second_new, n_new, n_average_new = adam_update(
        norm_shard, n_master, n_first, n_second, n_average, norm_rate, 0.0
    )
    return (
        outputs.reshape(seqs, tokens, dim),
        grad_inputs.reshape(seqs, tokens, dim),
        w_first_new,
        w_second_new,
        w_new,
        w_average_new,
        n_first_new,
        n_second_new,
        n_new,
        n_average_new,
    )


def solution(mesh):
    in_specs = (
        P("dp", "seq", None),
        P("dp", "seq", None),
        P("dp", "seq", None, None, None),
        P("dp", "seq", None),
        P(),
        P("dp", "seq"),
        P("dp", "seq"),
        P("dp", "seq"),
        P("dp", "seq"),
        P(None, "dp"),
        P(None, "dp"),
        P(None, "dp"),
        P(None, "dp"),
    )
    out_specs = (
        P("dp", "seq", None),
        P("dp", "seq", None),
        P("dp", "seq"),
        P("dp", "seq"),
        P("dp", "seq"),
        P("dp", "seq"),
        P(None, "dp"),
        P(None, "dp"),
        P(None, "dp"),
        P(None, "dp"),
    )
    return jax.shard_map(
        on_device, mesh=mesh, in_specs=in_specs, out_specs=out_specs, check_vma=False
    )
```
